32 devices in a mesh: macro: 4 (over y, x), tile: 4 (over z), micro: 2 (over core).
Axes of the slice: x: 2, y: 2, z: 4, core: 2. Of those that a mesh axis runs over, the one named last changes fastest.
Arguments:
- velocity: float32 [3, 96, 32, 256], P(None, 'macro', 'tile', 'micro'), may hold values from -6 to 6
- viscosity: float32 [96, 32, 256], P('macro', 'tile', 'micro'), may hold values from 0.3 to 3
- flag_cell: int32 [1024], P(('macro', 'tile', 'micro')), may hold values from 1153 to 23422, as said below
- flag_owner: int32 [1024, 1], P(('macro', 'tile', 'micro')), may hold values from 0 to 7; in each aligned block of 32 rows (0 to 31, 32 to 63, ...) at most 8 rows name the same one
- conformations: float32 [3, 2048, 512], P(None, ('macro', 'tile', 'micro')), may hold values from -3.2 to 3.2
- increments: bfloat16 [16, 3, 2048, 512], P(None, None, ('macro', 'tile', 'micro')), may hold values from -4 to 4
Outputs:
- velocity_next: float32 [3, 96, 32, 256], P(None, 'macro', 'tile', 'micro')
- conformations_next: float32 [3, 2048, 512], P(None, ('macro', 'tile', 'micro'))
- flag_stress: float32 [6, 1024], P(None, ('macro', 'tile', 'micro'))
The draws below stay inside these ranges and needn't reach their ends.
Inputs may be any that keep to these rules, and one draw needn't show every extreme that they name: `flag_cell`: on each device 32 distinct cells of its own block, none of them on a face of the block. `flag_owner`: among the 32 entries of one device at most 8 name the same owner, and some device has an owner named 8 times.
All inputs are finite; a program needn't handle non-finite values.
Results may differ from the reference program's by a relative error of at most 0.0003.
Values sent between devices are 32-bit elements; how exact they have to be, the bound alone decides.
No kernel may reach another device: no remote copies, remote signals or barrier semaphores. Data moves between devices by JAX's collectives and lax.ppermute only.
A program may use at most 64 MiB of HBM per device.

```python
import math
import jax
import jax.numpy as jnp
import numpy as np
from jax import lax

CX = 24
CY = 8
CZ = 128
F_DEV = 32
DUMBBELLS = 512
SUBSTEPS = 16
OWNERS = 8
CAP = 8
SLOTS = 64
ENS = 2048
FLAGS = 1024
NX = 96
NY = 32
NZ = 256
N_TILE = 4
N_MICRO = 2


def draw_flag_cell(key, part):
    device_count = FLAGS // F_DEV
    inner_count = (CX - 2) * (CY - 2) * (CZ - 2)
    device_keys = jax.random.split(key, device_count)

    def one_device(device_key):
        chosen = jax.random.permutation(device_key, inner_count)[:F_DEV].astype(jnp.int32)
        inner_x = chosen // ((CY - 2) * (CZ - 2)) + 1
        inner_y = chosen // (CZ - 2) % (CY - 2) + 1
        inner_z = chosen % (CZ - 2) + 1
        return ((inner_x * CY + inner_y) * CZ + inner_z).astype(jnp.int32)
    return jax.vmap(one_device)(device_keys).reshape(FLAGS)


def block_levels(own_key, dims, shards, smallest, largest):
    gain, own = 1.0, jax.random.fold_in(own_key, 6)
    for dim, blocks in shards:
        heights = jnp.exp(jax.random.uniform(jax.random.fold_in(own, dim), (blocks,), jnp.float32, smallest / len(shards), largest / len(shards)))
        gain = gain * jnp.repeat(heights, dims[dim] // blocks).reshape([-1 if axis == dim else 1 for axis in range(len(dims))])
    return gain


def assign_block(own_key, own, number, rows, count, top, reach, skew):
    ranking = jax.random.permutation(own_key, count)
    crowded, common = load_shares(count, rows * top, reach, skew, True), load_shares(count, rows * top, reach, skew, False)
    places = jnp.arange(count)

    def named(lengths, rotation):
        used = int((lengths > 0).sum())
        fixed = max(1, used // 4)
        shifted = fixed + (places - fixed + rotation * (used - fixed)) % max(1, count - fixed)
        return jnp.zeros((count,), jnp.int32).at[ranking[jnp.where(places < fixed, places, shifted)]].set(jnp.asarray(lengths, jnp.int32))

    lengths = jnp.where(number % 4 == 0, named(crowded, number // 4), named(common, number - number // 4 - 1))
    mixed = jax.random.permutation(jax.random.fold_in(own, 3), count)
    source_of, taker = mixed[0:count // 2 * 2:2], mixed[1:count // 2 * 2:2]
    slack = jnp.minimum(lengths[source_of] - 1, reach - lengths[taker]) // 2
    slack = jnp.where((source_of == ranking[0]) | (taker == ranking[0]) | (lengths[taker] == 0), 0, jnp.maximum(slack, 0))
    shifted = jax.random.randint(jax.random.fold_in(own, 4), (count // 2,), 0, 1 << 20) % (slack + 1)
    lengths = lengths.at[source_of].add(-shifted).at[taker].add(shifted)
    labels = jnp.searchsorted(jnp.cumsum(lengths), jnp.arange(rows * top), side="right").astype(jnp.int32)
    listing = labels.reshape(top, rows).T
    listing = listing[jax.random.permutation(jax.random.fold_in(own, 1), rows)]
    rotation = jax.random.randint(jax.random.fold_in(own, 2), (rows, 1), 0, top)
    return jnp.take_along_axis(listing, (jnp.arange(top)[None, :] + rotation) % top, axis=1)


def load_shares(amount, total, limit, slope, full):
    loads = [(1 << 20) // math.isqrt(rank ** slope) + 1 for rank in range(1, amount + 1)]
    largest = limit if full else min(limit, max(-(-total // amount), total * loads[0] // sum(loads)))
    least = 1 if total - largest >= amount - 1 else 0
    given, rest = [largest] + [least] * (amount - 1), total - largest - least * (amount - 1)
    while rest > 0:
        candidates = [i for i in range(1, amount) if given[i] < largest] or [i for i in range(1, amount) if given[i] < limit]
        mass, left = sum([loads[i] for i in candidates]), rest
        for i in candidates:
            addition = min(limit - given[i], max(1, left * loads[i] // mass), rest)
            given[i] = given[i] + addition
            rest = rest - addition
    return np.array(given)


def normal_values(rng, shape, spread, reach, shards=(), kind=jnp.bfloat16):
    factor_of = block_levels(rng, shape, shards, -0.22, 0.18) if shards else 1.0
    array = jax.random.normal(rng, shape, jnp.float32) * spread * factor_of
    return jnp.minimum(jnp.maximum(array, -reach), reach).astype(kind)


def setup_inputs(seed: int = 0) -> dict:
    arg_keys = jax.random.split(jax.random.key(seed), 7)
    velocity = normal_values(arg_keys[0], (3, NX, NY, NZ), 1.0, 6.0, ((1, 4), (2, 4), (3, 2)), jnp.float32)
    viscosity = jnp.clip(jnp.exp(math.log(3.0) - 2.3025851 * jax.random.uniform(arg_keys[1], (NX, NY, NZ), jnp.float32) ** block_levels(arg_keys[1], (NX, NY, NZ), ((0, 4), (1, 4), (2, 2)), -0.2, 0.2)), 0.3, 3.0)
    flag_cell = draw_flag_cell(jax.random.fold_in(arg_keys[6], 71), 0)
    flag_owner_keys = jax.random.split(jax.random.fold_in(arg_keys[3], 1), FLAGS // F_DEV)
    flag_owner_turns = jax.random.permutation(jax.random.fold_in(arg_keys[3], 3), FLAGS // F_DEV)
    flag_owner = jax.vmap(lambda own, number: assign_block(jax.random.fold_in(arg_keys[3], 2), own, number, F_DEV, OWNERS, 1, CAP, 2))(flag_owner_keys, flag_owner_turns).reshape((FLAGS, 1))
    conformations = jnp.clip(jax.random.uniform(arg_keys[4], (3, ENS, DUMBBELLS), jnp.float32, -3.2, 3.2) * block_levels(arg_keys[4], (3, ENS, DUMBBELLS), ((1, 32),), -0.4, 0.0), -3.2, 3.2)
    increments = normal_values(arg_keys[5], (SUBSTEPS, 3, ENS, DUMBBELLS), 1.0, 4.0, ((2, 32),))
    return {"velocity": velocity, "viscosity": viscosity, "flag_cell": flag_cell, "flag_owner": flag_owner, "conformations": conformations, "increments": increments}


stress_pairs = ((0, 0), (1, 1), (2, 2), (0, 1), (0, 2), (1, 2))
macro_step = 0.1
micro_step = 0.01
noise_weight = 0.1
relax_rate = 0.5
fene_extent = 30.0
spring_floor = 0.1
polymer_weight = 0.25


def pair_index(left_axis, right_axis):
    return stress_pairs.index((min(left_axis, right_axis), max(left_axis, right_axis)))


def window(source, direction, offset):
    slicers = [slice(None)]
    for spatial in range(3):
        length = source.shape[spatial + 1] - 2
        if spatial == direction:
            slicers.append(slice(offset, offset + length))
        else:
            slicers.append(slice(1, 1 + length))
    return source[tuple(slicers)]


def stress_field(padded, viscous):
    slopes = [(window(padded, direction, 2) - window(padded, direction, 0)) * 0.5 for direction in range(3)]
    components = [viscous * (slopes[right_axis][left_axis] + slopes[left_axis][right_axis]) for left_axis, right_axis in stress_pairs]
    return jnp.stack(components, axis=0)


def divergence(padded_stress):
    result = []
    for left_axis in range(3):
        summed = None
        for right_axis in range(3):
            member = pair_index(left_axis, right_axis)
            column = padded_stress[member:member + 1]
            change = (window(column, right_axis, 2) - window(column, right_axis, 0))[0] * 0.5
            summed = change if summed is None else summed + change
        result.append(summed)
    return jnp.stack(result, axis=0)


def spring_of(current):
    return 1.0 / jnp.maximum(1.0 - (current[0] * current[0] + current[1] * current[1] + current[2] * current[2]) / fene_extent, spring_floor)


def advance(conform, gradient_in, noise):
    rate_table = gradient_in[:, :, None]

    def substep(substep_index, current):
        spring = spring_of(current)
        updated = []
        for left_axis in range(3):
            drift_term = rate_table[3 * left_axis] * current[0] + rate_table[3 * left_axis + 1] * current[1] + rate_table[3 * left_axis + 2] * current[2] - relax_rate * spring * current[left_axis]
            updated.append(current[left_axis] + micro_step * drift_term + noise_weight * noise[substep_index, left_axis].astype(jnp.float32))
        return jnp.stack(updated, axis=0)

    last_state = lax.fori_loop(0, noise.shape[0], substep, conform)
    spring = spring_of(last_state)
    stresses = []
    for left_axis, right_axis in stress_pairs:
        identity_part = 1.0 if left_axis == right_axis else 0.0
        stresses.append(polymer_weight * (jnp.mean(spring * last_state[left_axis] * last_state[right_axis], axis=-1) - identity_part))
    return last_state, jnp.stack(stresses, axis=0)


def reference(velocity, viscosity, flag_cell, flag_owner, conformations, increments):
    device_count = FLAGS // F_DEV
    device_of = jnp.arange(FLAGS, dtype=jnp.int32) // F_DEV
    macro_of = device_of // (N_TILE * N_MICRO)
    tile_of = (device_of // N_MICRO) % N_TILE
    micro_of = device_of % N_MICRO
    local_x = flag_cell // (CY * CZ)
    local_y = (flag_cell // CZ) % CY
    local_z = flag_cell % CZ
    global_x = macro_of * CX + local_x
    global_y = tile_of * CY + local_y
    global_z = micro_of * CZ + local_z
    slopes = []
    for shift_x, shift_y, shift_z in ((1, 0, 0), (0, 1, 0), (0, 0, 1)):
        upper_side = velocity[:, global_x + shift_x, global_y + shift_y, global_z + shift_z]
        lower_side = velocity[:, global_x - shift_x, global_y - shift_y, global_z - shift_z]
        slopes.append((upper_side - lower_side) * 0.5)
    gradient_rows = jnp.stack(slopes, axis=1).reshape(9, FLAGS)
    owner_index = flag_owner[:, 0]
    onehot = (owner_index[:, None] == jnp.arange(OWNERS, dtype=jnp.int32)[None, :]).astype(jnp.int32)
    onehot = onehot.reshape(device_count, F_DEV, OWNERS)
    earlier = jnp.cumsum(onehot, axis=1) - onehot
    slot_rank = jnp.sum(earlier * onehot, axis=2).reshape(FLAGS)
    sender = macro_of * N_MICRO + micro_of
    owner_device = ((owner_index // N_MICRO) * N_TILE + tile_of) * N_MICRO + owner_index % N_MICRO
    target = (owner_device * SLOTS + sender * CAP + slot_rank).astype(jnp.int32)
    gradient_in = jnp.zeros((9, ENS), jnp.float32).at[:, target].set(gradient_rows)
    last_state, polymer = advance(conformations, gradient_in, increments)
    polymer_rows = polymer[:, target]
    padded = jnp.pad(velocity, ((0, 0), (1, 1), (1, 1), (1, 1)))
    stress_all = stress_field(padded, viscosity)
    stress_all = stress_all.at[:, global_x, global_y, global_z].add(polymer_rows)
    flag_stress = stress_all[:, global_x, global_y, global_z]
    stress_pad = jnp.pad(stress_all, ((0, 0), (1, 1), (1, 1), (1, 1)))
    velocity_next = velocity + macro_step * divergence(stress_pad)
    return (velocity_next, last_state, flag_stress)
```

```python
import functools

import jax
import jax.numpy as jnp
from jax import lax
from jax.experimental import pallas as pl
from jax.experimental.pallas import tpu as pltpu
from jax.sharding import PartitionSpec as P

stress_pairs = ((0, 0), (1, 1), (2, 2), (0, 1), (0, 2), (1, 2))
macro_step = 0.1
micro_step = 0.01
noise_weight = 0.1
relax_rate = 0.5
fene_extent = 30.0
spring_floor = 0.1
polymer_weight = 0.25

SMEM = pl.BlockSpec(memory_space=pltpu.SMEM)
VMEM = pl.BlockSpec(memory_space=pltpu.VMEM)


def pair_index(left_axis, right_axis):
    return stress_pairs.index((min(left_axis, right_axis), max(left_axis, right_axis)))


def lanes_of(shape):
    return lax.broadcasted_iota(jnp.int32, shape, len(shape) - 1)


def gather_kernel(
    capacity, size_y, size_z, cell_ref, owner_ref, velocity_ref, viscosity_ref,
    slots_ref, position_ref, viscous_ref, masked, gradients, count,
):
    flags = cell_ref.shape[0]
    for owner in range(count.shape[0]):
        count[owner] = 0
    lane = lanes_of((1, size_z))
    for j in range(flags):
        cell = cell_ref[j]
        row = lax.div(cell, size_z)
        z = cell - row * size_z
        here = (lane == z).astype(jnp.float32)
        along_z = (lane == z + 1).astype(jnp.float32) - (lane == z - 1).astype(jnp.float32)
        for a in range(3):
            along_x = velocity_ref[a, pl.ds(row + size_y, 1), :] - velocity_ref[a, pl.ds(row - size_y, 1), :]
            along_y = velocity_ref[a, pl.ds(row + 1, 1), :] - velocity_ref[a, pl.ds(row - 1, 1), :]
            masked[3 * a, j : j + 1, :] = along_x * here
            masked[3 * a + 1, j : j + 1, :] = along_y * here
            masked[3 * a + 2, j : j + 1, :] = velocity_ref[a, pl.ds(row, 1), :] * along_z
        masked[9, j : j + 1, :] = viscosity_ref[pl.ds(row, 1), :] * here
        owner = owner_ref[j]
        rank = count[owner]
        count[owner] = rank + 1
        position_ref[j] = owner * capacity + rank
    columns = [0.5 * jnp.sum(masked[c], axis=1, keepdims=True) for c in range(9)]
    viscous = jnp.sum(masked[9], axis=1, keepdims=True)
    wide = lanes_of((flags, 128))
    packed = jnp.zeros((flags, 128), jnp.float32)
    for c in range(9):
        packed = jnp.where(wide == c, columns[c], packed)
    gradients[...] = packed
    stress = jnp.zeros((flags, 128), jnp.float32)
    for k, (a, b) in enumerate(stress_pairs):
        stress = jnp.where(wide == k, viscous * (columns[3 * a + b] + columns[3 * b + a]), stress)
    viscous_ref[...] = stress
    slots_ref[...] = jnp.zeros_like(slots_ref)
    for j in range(flags):
        slots_ref[pl.ds(position_ref[j], 1), :] = gradients[j : j + 1, :]


def gather_rows(flag_cell, owner, velocity, viscosity, slot_count, owner_count):
    size_x, size_y, size_z = viscosity.shape
    flags = flag_cell.shape[0]
    return pl.pallas_call(
        functools.partial(gather_kernel, slot_count // owner_count, size_y, size_z),
        out_shape=(
            jax.ShapeDtypeStruct((slot_count, 128), jnp.float32),
            jax.ShapeDtypeStruct((flags,), jnp.int32),
            jax.ShapeDtypeStruct((flags, 128), jnp.float32),
        ),
        in_specs=[SMEM, SMEM, VMEM, VMEM],
        out_specs=(VMEM, SMEM, VMEM),
        scratch_shapes=[
            pltpu.VMEM((10, flags, size_z), jnp.float32),
            pltpu.VMEM((flags, 128), jnp.float32),
            pltpu.SMEM((owner_count,), jnp.int32),
        ],
        cost_estimate=pl.CostEstimate(flops=400000, bytes_accessed=3000000, transcendentals=0),
        name="gather_rows",
    )(
        flag_cell,
        owner,
        velocity.reshape(3, size_x * size_y, size_z),
        viscosity.reshape(size_x * size_y, size_z),
    )


def roll_lanes(value, amount):
    return pltpu.roll(value, amount % value.shape[-1], value.ndim - 1)


def packed_lanes(values, layers, core):
    size = values[0].shape[-1]
    lane = lanes_of(values[0].shape)
    total = jnp.zeros_like(values[0])
    for i, (value, layer) in enumerate(zip(values, layers)):
        if core == 0:
            total = jnp.where(lane == 8 * i, roll_lanes(value, 1 + layer + 8 * i), total)
        else:
            total = jnp.where(lane == size - 1 - 8 * i, roll_lanes(value, -1 - layer - 8 * i), total)
    return total


def unpacked_lanes(packed, item, core):
    if item == 0:
        return packed
    return roll_lanes(packed, -8 * item if core == 0 else 8 * item)


def pack_kernel(
    size_x, size_y, size_z, place_ref, velocity_ref, viscosity_ref, face_y_ref, face_x_ref, face_z_ref, edge_ref
):
    def row_of(ref, a, y):
        if a is None:
            return ref[pl.ds(y, size_x, stride=size_y), :]
        return ref[a, pl.ds(y, size_x, stride=size_y), :]

    def plane_of(x):
        return pl.ds(x * size_y, size_y)

    near = []
    for side in range(2):
        ys = (0, 1) if side == 0 else (size_y - 1, size_y - 2)
        xs = (0, 1) if side == 0 else (size_x - 1, size_x - 2)
        for layer in range(2):
            for a in range(3):
                rows = row_of(velocity_ref, a, ys[layer])
                face_y_ref[7 * side + 3 * layer + a] = rows
                if layer == 0 and a > 0:
                    near.append(rows)
                face_x_ref[7 * side + 3 * layer + a] = velocity_ref[a, plane_of(xs[layer]), :]
        face_y_ref[7 * side + 6] = row_of(viscosity_ref, None, ys[0])
        face_x_ref[7 * side + 6] = viscosity_ref[plane_of(xs[0]), :]
        for other in range(2):
            y = 0 if other == 0 else size_y - 1
            for a in range(2):
                number = 4 * side + 2 * other + a
                edge_ref[number : number + 1, :] = velocity_ref[a, pl.ds(xs[0] * size_y + y, 1), :]
    core = place_ref[2]
    for option in range(2):

        @pl.when(core == option)
        def _(option=option):
            whole = [velocity_ref[a] for a in range(3)]
            face_z_ref[...] = packed_lanes(
                whole + [viscosity_ref[...]] + whole, (0, 0, 0, 0, 1, 1, 1), option
            )
            edge_ref[8:, :] = packed_lanes(near, (0, 0, 0, 0), option)


def pack_faces(place, velocity, viscosity):
    size_x, size_y, size_z = viscosity.shape
    return pl.pallas_call(
        functools.partial(pack_kernel, size_x, size_y, size_z),
        out_shape=(
            jax.ShapeDtypeStruct((14, size_x, size_z), jnp.float32),
            jax.ShapeDtypeStruct((14, size_y, size_z), jnp.float32),
            jax.ShapeDtypeStruct((size_x * size_y, size_z), jnp.float32),
            jax.ShapeDtypeStruct((8 + size_x, size_z), jnp.float32),
        ),
        in_specs=[SMEM, VMEM, VMEM],
        out_specs=(VMEM, VMEM, VMEM, VMEM),
        cost_estimate=pl.CostEstimate(flops=400000, bytes_accessed=3000000, transcendentals=0),
        name="pack_faces",
    )(
        place,
        velocity.reshape(3, size_x * size_y, size_z),
        viscosity.reshape(size_x * size_y, size_z),
    )


def reciprocal(value):
    first = pl.reciprocal(value, approx=True)
    return first * (2.0 - value * first)


def micro_kernel(parts, conform_ref, noise_ref, rate_ref, next_ref, polymer_ref):
    rows = conform_ref.shape[1]
    steps = noise_ref.shape[0]
    dumbbells = conform_ref.shape[2]
    width = dumbbells // parts
    scale = 1.0 / noise_weight
    extent = fene_extent * scale * scale
    rates = [
        [
            jnp.broadcast_to(
                micro_step * rate_ref[:, 3 * a + b : 3 * a + b + 1] + (1.0 if a == b else 0.0), (rows, width)
            )
            for b in range(3)
        ]
        for a in range(3)
    ]

    def inverse_of(q):
        return reciprocal(
            jnp.maximum(extent - (q[0] * q[0] + q[1] * q[1] + q[2] * q[2]), extent * spring_floor)
        )

    def substep(step, state):
        result = []
        for part in range(parts):
            q = state[3 * part : 3 * part + 3]
            spring = (micro_step * relax_rate * extent) * inverse_of(q)
            for a in range(3):
                noise = noise_ref[step, a, :, part * width : (part + 1) * width].astype(jnp.float32)
                terms = [(rates[a][b] - spring if a == b else rates[a][b]) * q[b] for b in range(3)]
                result.append(terms[0] + terms[1] + terms[2] + noise)
        return tuple(result)

    state = tuple(
        conform_ref[a, :, part * width : (part + 1) * width] * scale for part in range(parts) for a in range(3)
    )
    state = lax.fori_loop(0, steps, substep, state, unroll=True)
    lane = lanes_of((rows, 128))
    sums = [None] * 6
    for part in range(parts):
        q = state[3 * part : 3 * part + 3]
        for a in range(3):
            next_ref[a, :, part * width : (part + 1) * width] = q[a] * noise_weight
        inverse = inverse_of(q)
        for k, (a, b) in enumerate(stress_pairs):
            term = inverse * q[a] * q[b]
            sums[k] = term if sums[k] is None else sums[k] + term
    packed = jnp.zeros((rows, 128), jnp.float32)
    weight = extent * noise_weight * noise_weight / dumbbells
    for k, (a, b) in enumerate(stress_pairs):
        mean = jnp.sum(sums[k], axis=1, keepdims=True) * weight
        packed = jnp.where(lane == k, polymer_weight * (mean - (1.0 if a == b else 0.0)), packed)
    polymer_ref[...] = packed


def advance(conformations, increments, rates):
    slots, dumbbells = conformations.shape[1:]
    steps = increments.shape[0]
    rows = 16
    return pl.pallas_call(
        functools.partial(micro_kernel, 4),
        grid=(slots // rows,),
        out_shape=(
            jax.ShapeDtypeStruct(conformations.shape, jnp.float32),
            jax.ShapeDtypeStruct((slots, 128), jnp.float32),
        ),
        in_specs=[
            pl.BlockSpec((3, rows, dumbbells), lambda i: (0, i, 0)),
            pl.BlockSpec((steps, 3, rows, dumbbells), lambda i: (0, 0, i, 0)),
            pl.BlockSpec((rows, 128), lambda i: (i, 0)),
        ],
        out_specs=(
            pl.BlockSpec((3, rows, dumbbells), lambda i: (0, i, 0)),
            pl.BlockSpec((rows, 128), lambda i: (i, 0)),
        ),
        cost_estimate=pl.CostEstimate(flops=20000000, bytes_accessed=5000000, transcendentals=600000),
        name="advance",
    )(conformations, increments, rates)


def flow_kernel(
    size_x, size_y, size_z, place_ref,
    velocity_ref, viscosity_ref, y_low_ref, y_high_ref, x_low_ref, x_high_ref,
    xz_low_ref, xz_high_ref, z_ref, ll_ref, lh_ref, hl_ref, hh_ref, yz_low_ref, yz_high_ref,
    out_ref, stress_ref,
):
    m, t, core = place_ref[0], place_ref[1], place_ref[2]
    x_in = (m > 0, m < place_ref[3] - 1)
    y_in = (t > 0, t < place_ref[4] - 1)

    def kept(value, *conditions):
        weight = jnp.float32(1.0)
        for condition in conditions:
            weight = weight * jnp.where(condition, 1.0, 0.0)
        return value * weight

    def compute(core):
        block = (size_x, size_y, size_z)
        lane3 = lanes_of(block)
        row3 = lax.broadcasted_iota(jnp.int32, block, 1)
        end = size_z - 1 if core == 0 else 0
        sender = 1 - core

        x_face = [[kept(ref[0, i], x_in[s]) for i in range(7)] for s, ref in enumerate((x_low_ref, x_high_ref))]
        y_face = [[kept(ref[0, i], y_in[s]) for i in range(7)] for s, ref in enumerate((y_low_ref, y_high_ref))]
        packed = z_ref[0]
        z_face = [
            unpacked_lanes(packed, item, sender).reshape(block) for item in range(7)
        ]

        def shift_x(value, low, high):
            minus = jnp.concatenate([low[None], value[:-1]], axis=0)
            plus = jnp.concatenate([value[1:], high[None]], axis=0)
            return minus, plus

        def shift_y(value, low, high):
            minus = jnp.where(row3 == 0, low[:, None, :], pltpu.roll(value, 1, 1))
            plus = jnp.where(row3 == size_y - 1, high[:, None, :], pltpu.roll(value, size_y - 1, 1))
            return minus, plus

        def shift_z(value, ghost):
            lane = lanes_of(value.shape)
            minus, plus = roll_lanes(value, 1), roll_lanes(value, -1)
            if core == 0:
                return jnp.where(lane == 0, 0.0, minus), jnp.where(lane == size_z - 1, ghost, plus)
            return jnp.where(lane == 0, ghost, minus), jnp.where(lane == size_z - 1, 0.0, plus)

        velocity = [velocity_ref[a].reshape(block) for a in range(3)]
        viscosity = viscosity_ref[...].reshape(block)
        half = 0.5 * viscosity
        slopes = []
        for a in range(3):
            minus_x, plus_x = shift_x(velocity[a], x_face[0][a], x_face[1][a])
            minus_y, plus_y = shift_y(velocity[a], y_face[0][a], y_face[1][a])
            minus_z, plus_z = shift_z(velocity[a], z_face[a])
            slopes.append((plus_x - minus_x, plus_y - minus_y, plus_z - minus_z))
        for k, (a, b) in enumerate(stress_pairs):
            stress_ref[k] = half * (slopes[a][b] + slopes[b][a])

        corners = ((ll_ref, lh_ref), (hl_ref, hh_ref))
        xz_refs = (xz_low_ref, xz_high_ref)
        yz_refs = (yz_low_ref, yz_high_ref)

        x_ghost = []
        for s in range(2):
            v0, v1, weight = x_face[s][0:3], x_face[s][3:6], 0.5 * x_face[s][6]
            edge_plane = 0 if s == 0 else size_x - 1
            normal = [
                (velocity[a][edge_plane] - v1[a]) * (1.0 if s == 0 else -1.0) for a in range(3)
            ]
            row2 = lax.broadcasted_iota(jnp.int32, (size_y, size_z), 0)
            low = kept(corners[s][0][0, 4 * (1 - s) + 2 : 4 * (1 - s) + 3, :], x_in[s], y_in[0])
            high = kept(corners[s][1][0, 4 * (1 - s) : 4 * (1 - s) + 1, :], x_in[s], y_in[1])
            minus = jnp.where(row2 == 0, low, pltpu.roll(v0[0], 1, 0))
            plus = jnp.where(row2 == size_y - 1, high, pltpu.roll(v0[0], size_y - 1, 0))
            slope_y = plus - minus
            ghost = kept(roll_lanes(xz_refs[s][0, 0], 1 if core == 1 else -1), x_in[s])
            minus, plus = shift_z(v0[0], ghost)
            slope_z = plus - minus
            x_ghost.append(
                (weight * (2.0 * normal[0]), weight * (normal[1] + slope_y), weight * (normal[2] + slope_z))
            )

        y_ghost = []
        for s in range(2):
            v0, v1, weight = y_face[s][0:3], y_face[s][3:6], 0.5 * y_face[s][6]
            y = 0 if s == 0 else size_y - 1
            own = [velocity_ref[a, pl.ds(y, size_x, stride=size_y), :] for a in range(3)]
            normal = [(own[a] - v1[a]) * (1.0 if s == 0 else -1.0) for a in range(3)]
            row2 = lax.broadcasted_iota(jnp.int32, (size_x, size_z), 0)
            line = 2 * (1 - s) + 1
            low = kept(corners[0][s][0, 4 + line : 5 + line, :], x_in[0], y_in[s])
            high = kept(corners[1][s][0, line : 1 + line, :], x_in[1], y_in[s])
            minus = jnp.where(row2 == 0, low, pltpu.roll(v0[1], 1, 0))
            plus = jnp.where(row2 == size_x - 1, high, pltpu.roll(v0[1], size_x - 1, 0))
            slope_x = plus - minus
            packed_edge = yz_refs[s][0, 8:, :]
            ghost = kept(unpacked_lanes(packed_edge, 2 * (1 - s), sender), y_in[s])
            minus, plus = shift_z(v0[1], ghost)
            slope_z = plus - minus
            y_ghost.append(
                (weight * (normal[0] + slope_x), weight * (2.0 * normal[1]), weight * (normal[2] + slope_z))
            )

        v0, weight, v1 = z_face[0:3], 0.5 * z_face[3], z_face[4:7]
        sign = -1.0 if core == 0 else 1.0
        normal = [(velocity[a] - v1[a]) * sign for a in range(3)]
        low, high = [
            kept(roll_lanes(xz_refs[s][0, 2], 1 if core == 1 else -1), x_in[s]) for s in range(2)
        ]
        minus, plus = shift_x(v0[2], low, high)
        slope_x = plus - minus
        low, high = [
            kept(unpacked_lanes(yz_refs[s][0, 8:, :], 2 * (1 - s) + 1, sender), y_in[s]) for s in range(2)
        ]
        minus, plus = shift_y(v0[2], low, high)
        slope_y = plus - minus
        z_ghost = (weight * (normal[0] + slope_x), weight * (normal[1] + slope_y), weight * (2.0 * normal[2]))

        for a in range(3):
            column = stress_ref[pair_index(a, 0)]
            minus, plus = shift_x(column, x_ghost[0][a], x_ghost[1][a])
            total = plus - minus
            column = stress_ref[pair_index(a, 1)]
            minus, plus = shift_y(column, y_ghost[0][a], y_ghost[1][a])
            total = total + (plus - minus)
            column = stress_ref[pair_index(a, 2)]
            minus, plus = shift_z(column, z_ghost[a])
            total = total + (plus - minus)
            out_ref[a] = (velocity[a] + (0.5 * macro_step) * total).reshape(size_x * size_y, size_z)

    for option in range(2):

        @pl.when(core == option)
        def _(option=option):
            compute(option)


def flow_step(place, velocity, viscosity, faces_y, faces_x, faces_z, edges, counts):
    size_x, size_y, size_z = viscosity.shape
    macro_count, tile_count = counts

    def low(index):
        return jnp.maximum(index - 1, 0)

    def high(index, count):
        return jnp.minimum(index + 1, count - 1)

    def neighbour(index, side, count):
        return low(index) if side == 0 else high(index, count)

    def y_spec(side):
        return pl.BlockSpec(
            (1, 7, size_x, size_z), lambda i, p: (neighbour(p[1], side, tile_count), 1 - side, 0, 0)
        )

    def x_spec(side, other):
        return pl.BlockSpec(
            (1, 7, size_y, size_z),
            lambda i, p: (
                2 * neighbour(p[0], side, macro_count) + (1 - p[2] if other else p[2]), 1 - side, 0, 0
            ),
        )

    def device(m, t, c):
        return (m * tile_count + t) * 2 + c

    def corner_spec(x_side, y_side):
        return pl.BlockSpec(
            (1, 8, size_z),
            lambda i, p: (
                device(neighbour(p[0], x_side, macro_count), neighbour(p[1], y_side, tile_count), p[2]), 0, 0
            ),
        )

    def edge_spec(y_side):
        return pl.BlockSpec(
            (1, 8 + size_x, size_z),
            lambda i, p: (device(p[0], neighbour(p[1], y_side, tile_count), 1 - p[2]), 0, 0),
        )

    whole3 = pl.BlockSpec((3, size_x * size_y, size_z), lambda i, p: (0, 0, 0))
    return pl.pallas_call(
        functools.partial(flow_kernel, size_x, size_y, size_z),
        grid_spec=pltpu.PrefetchScalarGridSpec(
            num_scalar_prefetch=1,
            grid=(1,),
            in_specs=[
                whole3,
                pl.BlockSpec((size_x * size_y, size_z), lambda i, p: (0, 0)),
                y_spec(0), y_spec(1),
                x_spec(0, False), x_spec(1, False), x_spec(0, True), x_spec(1, True),
                pl.BlockSpec((1, size_x * size_y, size_z), lambda i, p: (1 - p[2], 0, 0)),
                corner_spec(0, 0), corner_spec(0, 1), corner_spec(1, 0), corner_spec(1, 1),
                edge_spec(0), edge_spec(1),
            ],
            out_specs=whole3,
            scratch_shapes=[pltpu.VMEM((6, size_x, size_y, size_z), jnp.float32)],
        ),
        out_shape=jax.ShapeDtypeStruct((3, size_x * size_y, size_z), jnp.float32),
        cost_estimate=pl.CostEstimate(flops=4000000, bytes_accessed=3000000, transcendentals=0),
        name="flow_step",
    )(
        place,
        velocity.reshape(3, size_x * size_y, size_z),
        viscosity.reshape(size_x * size_y, size_z),
        faces_y, faces_y, faces_x, faces_x, faces_x, faces_x, faces_z,
        edges, edges, edges, edges, edges, edges,
    )


def polymer_kernel(
    size_y, size_z, cell_ref, position_ref, slots_ref, viscous_ref, partial_ref,
    out_ref, flag_ref, polymer, lines, shifted,
):
    flags = cell_ref.shape[0]
    out_ref[...] = partial_ref[...]
    lane = lanes_of((1, size_z))
    for j in range(flags):
        polymer[j : j + 1, :] = slots_ref[pl.ds(position_ref[j], 1), :]
        cell = cell_ref[j]
        z = cell - lax.div(cell, size_z) * size_z
        lines[0, j : j + 1, :] = jnp.where(lane == z, 0.5 * macro_step, 0.0)
        lines[1, j : j + 1, :] = jnp.where(
            lane == z - 1, 0.5 * macro_step, jnp.where(lane == z + 1, -0.5 * macro_step, 0.0)
        )
    values = polymer[...]
    flag_ref[...] = (viscous_ref[...] + values).T[0:6, :]
    here, beside = lines[0], lines[1]
    for k in range(6):
        column = jnp.broadcast_to(values[:, k : k + 1], (flags, size_z))
        shifted[k] = column * here
        if stress_pairs[k][1] == 2:
            shifted[6 + stress_pairs[k][0]] = column * beside
    for j in range(flags):
        row = lax.div(cell_ref[j], size_z)
        targets = []
        for a in range(3):
            line_x = shifted[pair_index(a, 0), j : j + 1, :]
            line_y = shifted[pair_index(a, 1), j : j + 1, :]
            line_z = shifted[6 + a, j : j + 1, :]
            targets += [
                (a, row - size_y, line_x), (a, row + size_y, -line_x),
                (a, row - 1, line_y), (a, row + 1, -line_y), (a, row, line_z),
            ]
        updated = [out_ref[a, pl.ds(at, 1), :] + line for a, at, line in targets]
        for (a, at, _), line in zip(targets, updated):
            out_ref[a, pl.ds(at, 1), :] = line


def add_polymer(flag_cell, position, slots, viscous, partial, size_y):
    flags = flag_cell.shape[0]
    size_z = partial.shape[2]
    return pl.pallas_call(
        functools.partial(polymer_kernel, size_y, size_z),
        out_shape=(
            jax.ShapeDtypeStruct(partial.shape, jnp.float32),
            jax.ShapeDtypeStruct((6, flags), jnp.float32),
        ),
        in_specs=[SMEM, SMEM, VMEM, VMEM, VMEM],
        out_specs=(VMEM, VMEM),
        scratch_shapes=[
            pltpu.VMEM((flags, 128), jnp.float32),
            pltpu.VMEM((2, flags, size_z), jnp.float32),
            pltpu.VMEM((9, flags, size_z), jnp.float32),
        ],
        cost_estimate=pl.CostEstimate(flops=400000, bytes_accessed=3000000, transcendentals=0),
        name="add_polymer",
    )(flag_cell, position, slots, viscous, partial)


def shards(velocity, viscosity, flag_cell, flag_owner, conformations, increments):
    macro_count = lax.axis_size("macro")
    tile_count = lax.axis_size("tile")
    micro_count = lax.axis_size("micro")
    assert micro_count == 2
    owner_count = macro_count * micro_count
    slot_count = conformations.shape[1]
    capacity = slot_count // owner_count
    size_x, size_y, size_z = viscosity.shape
    place = jnp.stack(
        [
            lax.axis_index("macro"), lax.axis_index("tile"), lax.axis_index("micro"),
            jnp.int32(macro_count), jnp.int32(tile_count),
        ]
    ).astype(jnp.int32)
    slots, position, viscous = gather_rows(
        flag_cell, flag_owner.reshape(-1), velocity, viscosity, slot_count, owner_count
    )

    def exchange(rows):
        rows = rows.reshape(owner_count, capacity, 128)
        rows = lax.all_to_all(rows, ("macro", "micro"), split_axis=0, concat_axis=0, tiled=True)
        return rows.reshape(slot_count, 128)

    rates = exchange(slots)
    face_y, face_x, face_z, edge = pack_faces(place, velocity, viscosity)
    faces_y = lax.all_gather(face_y, "tile")
    faces_x = lax.all_gather(face_x, ("macro", "micro"))
    faces_z = lax.all_gather(face_z, "micro")
    edges = lax.all_gather(edge, ("macro", "tile", "micro"))
    last_state, polymer = advance(conformations, increments, rates)
    returned = exchange(polymer)
    partial = flow_step(
        place, velocity, viscosity, faces_y, faces_x, faces_z, edges, (macro_count, tile_count)
    )
    velocity_next, flag_stress = add_polymer(flag_cell, position, returned, viscous, partial, size_y)
    return (velocity_next.reshape(velocity.shape), last_state, flag_stress)


def solution(mesh):
    in_specs = (
        P(None, "macro", "tile", "micro"),
        P("macro", "tile", "micro"),
        P(("macro", "tile", "micro")),
        P(("macro", "tile", "micro"), None),
        P(None, ("macro", "tile", "micro"), None),
        P(None, None, ("macro", "tile", "micro"), None),
    )
    out_specs = (
        P(None, "macro", "tile", "micro"),
        P(None, ("macro", "tile", "micro"), None),
        P(None, ("macro", "tile", "micro")),
    )
    return jax.shard_map(shards, mesh=mesh, in_specs=in_specs, out_specs=out_specs, check_vma=False)
```

```python
import functools

import jax
import jax.numpy as jnp
from jax import lax
from jax.experimental import pallas as pl
from jax.experimental.pallas import tpu as pltpu
from jax.sharding import PartitionSpec as P

stress_pairs = ((0, 0), (1, 1), (2, 2), (0, 1), (0, 2), (1, 2))
macro_step = 0.1
micro_step = 0.01
noise_weight = 0.1
relax_rate = 0.5
fene_extent = 30.0
spring_floor = 0.1
polymer_weight = 0.25

SMEM = pl.BlockSpec(memory_space=pltpu.SMEM)
VMEM = pl.BlockSpec(memory_space=pltpu.VMEM)


def pair_index(left_axis, right_axis):
    return stress_pairs.index((min(left_axis, right_axis), max(left_axis, right_axis)))


def lanes_of(shape):
    return lax.broadcasted_iota(jnp.int32, shape, len(shape) - 1)


slot_rows = 8
item_count = 7
line_rows = 8


def limit(mebibytes):
    return pltpu.CompilerParams(vmem_limit_bytes=mebibytes * 1024 * 1024)


def place_of():
    return lax.axis_index("macro"), lax.axis_index("micro")


def rolled(value, amount):
    size = value.shape[-1]
    if isinstance(amount, int):
        return pltpu.roll(value, amount % size, value.ndim - 1)
    return pltpu.roll(value, lax.rem(amount + 2 * size, size), value.ndim - 1)


def gather_kernel(
    capacity, size_x, size_y, size_z, macro_count, cell_ref, owner_ref, velocity_ref, viscosity_ref,
    chunk_ref, position_ref, viscous_ref, y_low_ref, y_high_ref, masked, gradients, target, count,
):
    flags = cell_ref.shape[0]
    chunk_rows = slot_rows + item_count * size_y
    macro, core = place_of()
    lane = lanes_of((1, size_z))

    def clear(owner, carry):
        count[owner] = 0
        chunk_ref[pl.ds(pl.multiple_of(owner * chunk_rows, 8), slot_rows), :] = jnp.zeros(
            (slot_rows, 128), jnp.float32
        )
        return carry

    lax.fori_loop(0, count.shape[0], clear, 0, unroll=True)

    def read(j, carry):
        cell = cell_ref[j]
        row = lax.div(cell, size_z)
        z = cell - row * size_z
        here = (lane == z).astype(jnp.float32)
        along_z = (lane == z + 1).astype(jnp.float32) - (lane == z - 1).astype(jnp.float32)
        for a in range(3):
            along_x = velocity_ref[a, pl.ds(row + size_y, 1), :] - velocity_ref[a, pl.ds(row - size_y, 1), :]
            along_y = velocity_ref[a, pl.ds(row + 1, 1), :] - velocity_ref[a, pl.ds(row - 1, 1), :]
            masked[3 * a, pl.ds(j, 1), :] = along_x * here
            masked[3 * a + 1, pl.ds(j, 1), :] = along_y * here
            masked[3 * a + 2, pl.ds(j, 1), :] = velocity_ref[a, pl.ds(row, 1), :] * along_z
        masked[9, pl.ds(j, 1), :] = viscosity_ref[pl.ds(row, 1), :] * here
        owner = owner_ref[j]
        rank = count[owner]
        count[owner] = rank + 1
        target[j] = owner * chunk_rows + rank
        position_ref[j] = owner * (slot_rows + line_rows) + rank
        return carry

    lax.fori_loop(0, flags, read, 0, unroll=4)

    for side, ref in enumerate((y_low_ref, y_high_ref)):
        for layer in range(2):
            y = layer if side == 0 else size_y - 1 - layer
            for a in range(3):
                ref[3 * layer + a] = velocity_ref[a, pl.ds(y, size_x, stride=size_y), :]
        y = 0 if side == 0 else size_y - 1
        ref[6] = viscosity_ref[pl.ds(y, size_x, stride=size_y), :]

    for side in range(2):
        beside = macro - 1 if side == 0 else macro + 1

        @pl.when(beside >= 0 if side == 0 else beside < macro_count)
        def _(side=side, beside=beside):
            first = pl.multiple_of((2 * beside + core) * chunk_rows + slot_rows, 8)
            other = pl.multiple_of((2 * beside + 1 - core) * chunk_rows + slot_rows, 8)
            for layer in range(2):
                x = layer if side == 0 else size_x - 1 - layer
                for a in range(3):
                    chunk_ref[pl.ds(first + (3 * layer + a) * size_y, size_y), :] = velocity_ref[
                        a, x * size_y : (x + 1) * size_y, :
                    ]
            x = 0 if side == 0 else size_x - 1
            chunk_ref[pl.ds(first + 6 * size_y, size_y), :] = viscosity_ref[x * size_y : (x + 1) * size_y, :]
            for number, a in enumerate((0, 2)):
                chunk_ref[pl.ds(other + number * size_y, size_y), :] = velocity_ref[
                    a, x * size_y : (x + 1) * size_y, :
                ]

    group = size_z // 8
    lane2 = lanes_of((size_y, size_z))
    first = pl.multiple_of((2 * macro + 1 - core) * chunk_rows + slot_rows, 8)
    sources = [jnp.where(core == 0, size_z - 1 - layer, layer) for layer in range(2)]
    for block in range(-(-size_x // group)):

        def add_plane(x, total):
            rows = pl.ds(pl.multiple_of(x * size_y, 8), size_y)
            start = 8 * (x - block * group)
            for q in range(item_count):
                layer, a = (0, q) if q < 4 else (1, q - 4)
                value = viscosity_ref[rows, :] if q == 3 else velocity_ref[a, rows, :]
                total = jnp.where(lane2 == start + q, rolled(value, start + q - sources[layer]), total)
            return total

        total = lax.fori_loop(
            block * group, min(size_x, (block + 1) * group), add_plane,
            jnp.zeros((size_y, size_z), jnp.float32), unroll=4,
        )
        chunk_ref[pl.ds(first + block * size_y, size_y), :] = total

    columns = [0.5 * jnp.sum(masked[c], axis=1, keepdims=True) for c in range(9)]
    viscous = jnp.sum(masked[9], axis=1, keepdims=True)
    wide = lanes_of((flags, 128))
    packed = jnp.zeros((flags, 128), jnp.float32)
    for c in range(9):
        packed = jnp.where(wide == c, columns[c], packed)
    gradients[...] = packed
    stress = jnp.zeros((flags, 128), jnp.float32)
    for k, (a, b) in enumerate(stress_pairs):
        stress = jnp.where(wide == k, viscous * (columns[3 * a + b] + columns[3 * b + a]), stress)
    viscous_ref[...] = stress

    def place(j, carry):
        chunk_ref[pl.ds(target[j], 1), :] = gradients[pl.ds(j, 1), :]
        return carry

    lax.fori_loop(0, flags, place, 0, unroll=8)


def gather_rows(flag_cell, owner, velocity, viscosity, capacity, owner_count):
    size_x, size_y, size_z = viscosity.shape
    flags = flag_cell.shape[0]
    chunk_rows = slot_rows + item_count * size_y
    face = jax.ShapeDtypeStruct((item_count, size_x, size_z), jnp.float32)
    return pl.pallas_call(
        functools.partial(gather_kernel, capacity, size_x, size_y, size_z, owner_count // 2),
        out_shape=(
            jax.ShapeDtypeStruct((owner_count * chunk_rows, 128), jnp.float32),
            jax.ShapeDtypeStruct((flags,), jnp.int32),
            jax.ShapeDtypeStruct((flags, 128), jnp.float32),
            face,
            face,
        ),
        in_specs=[SMEM, SMEM, VMEM, VMEM],
        out_specs=(VMEM, SMEM, VMEM, VMEM, VMEM),
        scratch_shapes=[
            pltpu.VMEM((10, flags, size_z), jnp.float32),
            pltpu.VMEM((flags, 128), jnp.float32),
            pltpu.SMEM((flags,), jnp.int32),
            pltpu.SMEM((owner_count,), jnp.int32),
        ],
        compiler_params=limit(8),
        cost_estimate=pl.CostEstimate(flops=400000, bytes_accessed=3000000, transcendentals=0),
        name="gather_rows",
    )(
        flag_cell,
        owner,
        velocity.reshape(3, size_x * size_y, size_z),
        viscosity.reshape(size_x * size_y, size_z),
    )


def reciprocal(value):
    first = pl.reciprocal(value, approx=True)
    return first * (2.0 - value * first)


def micro_kernel(
    capacity, parts, rows, macro_count, conform_ref, noise_ref, rate_ref, y_low_ref, y_high_ref,
    next_ref, chunk_ref, conform, noise, result, rate, sums_ref, read_sem, noise_sem, write_sem,
):
    steps, _, slots, dumbbells = noise_ref.shape
    blocks = slots // rows
    width = dumbbells // parts
    owners = slots // capacity
    scale = 1.0 / noise_weight
    extent = fene_extent * scale * scale

    def block_rows(block):
        return pl.ds(pl.multiple_of(block * rows, rows), rows)

    def copies(block):
        at = block_rows(block)
        return (
            pltpu.make_async_copy(conform_ref.at[:, at, :], conform.at[:, at, :], read_sem.at[block]),
            pltpu.make_async_copy(noise_ref.at[:, :, at, :], noise.at[:, :, at, :], noise_sem.at[block]),
        )

    def write(block):
        at = block_rows(block)
        return pltpu.make_async_copy(result.at[:, at, :], next_ref.at[:, at, :], write_sem.at[block])

    for block in range(blocks):
        for copy in copies(block):
            copy.start()

    for owner in range(owners):
        rate[owner * capacity : (owner + 1) * capacity, :] = rate_ref[owner, 0:capacity, :]

    macro, core = place_of()
    size_x, size_z = y_low_ref.shape[1:]
    sides = (y_low_ref, y_high_ref)
    for side in range(2):
        beside = macro - 1 if side == 0 else macro + 1

        @pl.when(beside >= 0 if side == 0 else beside < macro_count)
        def _(side=side, beside=beside):
            x = 0 if side == 0 else size_x - 1
            for u in range(2):
                for a in range(2):
                    at = slot_rows + 2 * u + a
                    chunk_ref[2 * beside + core, at : at + 1, :] = sides[u][a, x : x + 1, :]

    lane = lanes_of((8, size_z))
    source = jnp.where(core == 0, size_z - 1, 0)
    total = jnp.zeros((8, size_z), jnp.float32)
    for i in range(size_x // 8):
        for u in range(2):
            for a in range(2):
                at = 4 * i + 2 * u + a
                total = jnp.where(
                    lane == at, rolled(sides[u][1 + a, 8 * i : 8 * i + 8, :], at - source), total
                )
    chunk_ref[2 * macro + 1 - core, slot_rows:, :] = total

    def inverse_of(q):
        return reciprocal(
            jnp.maximum(extent - (q[0] * q[0] + q[1] * q[1] + q[2] * q[2]), extent * spring_floor)
        )

    def advance_block(block, carry):
        at = block_rows(block)
        for copy in copies(block):
            copy.wait()
        table = rate[at, :]
        rates = [
            [
                jnp.broadcast_to(
                    micro_step * table[:, 3 * a + b : 3 * a + b + 1] + (1.0 if a == b else 0.0), (rows, width)
                )
                for b in range(3)
            ]
            for a in range(3)
        ]

        def substep(step, state):
            updated = []
            for part in range(parts):
                q = state[3 * part : 3 * part + 3]
                spring = (micro_step * relax_rate * extent) * inverse_of(q)
                for a in range(3):
                    kick = noise[step, a, at, part * width : (part + 1) * width].astype(jnp.float32)
                    terms = [(rates[a][b] - spring if a == b else rates[a][b]) * q[b] for b in range(3)]
                    updated.append(terms[0] + terms[1] + terms[2] + kick)
            return tuple(updated)

        state = tuple(
            conform[a, at, part * width : (part + 1) * width] * scale
            for part in range(parts)
            for a in range(3)
        )
        state = lax.fori_loop(0, steps, substep, state, unroll=4)
        sums = [None] * 6
        for part in range(parts):
            q = state[3 * part : 3 * part + 3]
            for a in range(3):
                result[a, at, part * width : (part + 1) * width] = q[a] * noise_weight
            inverse = inverse_of(q)
            for k, (a, b) in enumerate(stress_pairs):
                term = inverse * q[a] * q[b]
                sums[k] = term if sums[k] is None else sums[k] + term
        write(block).start()
        for k in range(6):
            sums_ref[k, at, :] = sums[k]
        return carry

    lax.fori_loop(0, blocks, advance_block, 0)
    lane = lanes_of((slots, 128))
    packed = jnp.zeros((slots, 128), jnp.float32)
    weight = extent * noise_weight * noise_weight / dumbbells
    for k, (a, b) in enumerate(stress_pairs):
        mean = jnp.sum(sums_ref[k], axis=1, keepdims=True) * weight
        packed = jnp.where(lane == k, polymer_weight * (mean - (1.0 if a == b else 0.0)), packed)
    for owner in range(owners):
        chunk_ref[owner, 0:capacity, :] = packed[owner * capacity : (owner + 1) * capacity]
    for block in range(blocks):
        write(block).wait()


def advance(conformations, increments, chunks, y_low, y_high, capacity):
    slots, dumbbells = conformations.shape[1:]
    steps = increments.shape[0]
    owners = slots // capacity
    rows, parts = 16, 4
    blocks = slots // rows
    whole = pl.BlockSpec(memory_space=pl.ANY)
    return pl.pallas_call(
        functools.partial(micro_kernel, capacity, parts, rows, owners // 2),
        out_shape=(
            jax.ShapeDtypeStruct(conformations.shape, jnp.float32),
            jax.ShapeDtypeStruct((owners, slot_rows + line_rows, 128), jnp.float32),
        ),
        in_specs=[
            pl.BlockSpec(memory_space=pltpu.HBM), pl.BlockSpec(memory_space=pltpu.HBM), VMEM, VMEM, VMEM
        ],
        out_specs=(pl.BlockSpec(memory_space=pltpu.HBM), VMEM),
        scratch_shapes=[
            pltpu.VMEM(conformations.shape, jnp.float32),
            pltpu.VMEM(increments.shape, jnp.bfloat16),
            pltpu.VMEM(conformations.shape, jnp.float32),
            pltpu.VMEM((slots, 128), jnp.float32),
            pltpu.VMEM((6, slots, dumbbells // parts), jnp.float32),
            pltpu.SemaphoreType.DMA((blocks,)),
            pltpu.SemaphoreType.DMA((blocks,)),
            pltpu.SemaphoreType.DMA((blocks,)),
        ],
        compiler_params=limit(12),
        cost_estimate=pl.CostEstimate(flops=20000000, bytes_accessed=5000000, transcendentals=600000),
        name="advance",
    )(conformations, increments, chunks, y_low, y_high)


def flow_kernel(
    size_x, size_y, size_z, macro_count, velocity_ref, viscosity_ref, chunk_ref, y_low_ref, y_high_ref,
    out_ref, corner_ref, edge_ref, padded, stress_x, stress_rest, faces, ghost_y, ghost_z,
):
    macro, core = place_of()
    inside = (macro > 0, macro < macro_count - 1)
    sign_z = jnp.where(core == 0, 1.0, -1.0)
    end = jnp.where(core == 0, size_z - 1, 0)
    shape = (size_y, size_z)
    lane, row = lanes_of(shape), lax.broadcasted_iota(jnp.int32, shape, 0)
    at_end = jnp.where(lane == end, sign_z, 0.0)

    def kept(value, condition):
        return jnp.where(condition, value, 0.0)

    def plane(x):
        return pl.ds(pl.multiple_of(x * size_y, 8), size_y)

    def difference_z(value):
        lane = lanes_of(value.shape)
        return jnp.where(lane == size_z - 1, 0.0, rolled(value, -1)) - jnp.where(
            lane == 0, 0.0, rolled(value, 1)
        )

    def difference_rows(value, low=0.0, high=0.0):
        count = value.shape[0]
        row = lax.broadcasted_iota(jnp.int32, value.shape, 0)
        return jnp.where(row == count - 1, high, pltpu.roll(value, count - 1, 0)) - jnp.where(
            row == 0, low, pltpu.roll(value, 1, 0)
        )

    x_faces, x_others = [], []
    for s in range(2):
        beside = jnp.maximum(macro - 1, 0) if s == 0 else jnp.minimum(macro + 1, macro_count - 1)
        x_faces.append(
            [
                kept(chunk_ref[2 * beside + core, slot_rows + i * size_y : slot_rows + (i + 1) * size_y, :], inside[s])
                for i in range(item_count)
            ]
        )
        x_others.append(
            [
                kept(
                    rolled(
                        chunk_ref[
                            2 * beside + 1 - core, slot_rows + i * size_y : slot_rows + (i + 1) * size_y, :
                        ],
                        2 * end + 1,
                    ),
                    inside[s],
                )
                for i in range(2)
            ]
        )

    group = size_z // 8
    packed = [
        chunk_ref[2 * macro + 1 - core, slot_rows + i * size_y : slot_rows + (i + 1) * size_y, :]
        for i in range(-(-size_x // group))
    ]
    for i, value in enumerate(packed):

        def unpack(x, carry):
            for q in range(item_count):
                faces[q, x + 1] = rolled(value, end - (8 * (x - i * group) + q))
            return carry

        lax.fori_loop(i * group, min(size_x, (i + 1) * group), unpack, 0, unroll=2)
    faces[2, 0] = x_others[0][1]
    faces[2, size_x + 1] = x_others[1][1]

    for a in range(3):
        padded[a, 0] = x_faces[0][a]
        padded[a, size_x + 1] = x_faces[1][a]

    def fill(x, carry):
        for a in range(3):
            padded[a, x + 1] = velocity_ref[a, plane(x), :]
        return carry

    lax.fori_loop(0, size_x, fill, 0, unroll=4)

    rest = {(1, 1): 0, (2, 2): 1, (1, 2): 2}

    def stress_plane(x, carry):
        along_x, along_y, along_z, centre = [], [], [], []
        for a in range(3):
            value = padded[a, x + 1]
            centre.append(value)
            along_x.append(padded[a, x + 2] - padded[a, x])
            along_y.append(
                difference_rows(value, y_low_ref[a, pl.ds(x, 1), :], y_high_ref[a, pl.ds(x, 1), :])
            )
            along_z.append(difference_z(value) + faces[a, x + 1] * at_end)
        slopes = (along_x, along_y, along_z)
        half = 0.5 * viscosity_ref[plane(x), :]
        for a, b in stress_pairs:
            value = half * (slopes[b][a] + slopes[a][b])
            if a == 0:
                stress_x[b, x + 1] = value
            else:
                stress_rest[rest[a, b], x] = value
        weight = (0.5 * faces[3, x + 1]) * at_end
        normal = [(faces[4 + a, x + 1] - centre[a]) * sign_z for a in range(3)]
        ghost_z[0, x] = weight * (normal[0] + (faces[2, x + 2] - faces[2, x]))
        ghost_z[1, x] = weight * (normal[1] + difference_rows(faces[2, x + 1]))
        ghost_z[2, x] = weight * (2.0 * normal[2])
        return carry

    lax.fori_loop(0, size_x, stress_plane, 0, unroll=2)

    for s in range(2):
        near, far, weight = x_faces[s][0:3], x_faces[s][3:6], 0.5 * x_faces[s][6]
        sign = -1.0 if s == 0 else 1.0
        normal = [(far[a] - padded[a, 1 if s == 0 else size_x]) * sign for a in range(3)]
        slope_y = difference_rows(near[0])
        slope_z = difference_z(near[0]) + x_others[s][0] * at_end
        at = 0 if s == 0 else size_x + 1
        stress_x[0, at] = weight * (2.0 * normal[0])
        stress_x[1, at] = weight * (normal[1] + slope_y)
        stress_x[2, at] = weight * (normal[2] + slope_z)
        for u in range(2):
            y, sign_y = (0, -1.0) if u == 0 else (size_y - 1, 1.0)
            number = 4 * s + 2 * u
            corner_ref[number : number + 1, :] = (0.5 * macro_step * sign * sign_y) * weight[y : y + 1, :]

    for u, ref in enumerate((y_low_ref, y_high_ref)):
        y, sign = (0, -1.0) if u == 0 else (size_y - 1, 1.0)
        weight = 0.5 * ref[6]
        normal = [
            (ref[3 + a] - velocity_ref[a, pl.ds(y, size_x, stride=size_y), :]) * sign for a in range(3)
        ]
        ghost_y[3 * u] = weight * (normal[0] + difference_rows(ref[1]))
        ghost_y[3 * u + 1] = weight * (2.0 * normal[1])
        ghost_y[3 * u + 2] = weight * (normal[2] + difference_z(ref[1]))
        for s in range(2):
            x, sign_x = (0, -1.0) if s == 0 else (size_x - 1, 1.0)
            number = 4 * s + 2 * u + 1
            corner_ref[number : number + 1, :] = (0.5 * macro_step * sign * sign_x) * weight[x : x + 1, :]
        wide = lanes_of((size_x, size_z))
        scale = jnp.where(wide == end, (0.5 * macro_step * sign) * sign_z, 0.0)
        edge_ref[2 * u] = scale * weight
        for x in range(size_x):
            edge_ref[2 * u + 1, x : x + 1, :] = scale[x : x + 1, :] * (0.5 * faces[3, x + 1, y : y + 1, :])

    columns = {(0, 1): (stress_x, 1, 1), (1, 1): (stress_rest, 0, 0), (2, 1): (stress_rest, 2, 0)}
    columns_z = {0: (stress_x, 2, 1), 1: (stress_rest, 2, 0), 2: (stress_rest, 1, 0)}

    def step_plane(x, carry):
        for a in range(3):
            total = stress_x[a, x + 2] - stress_x[a, x]
            ref, number, shift = columns[a, 1]
            total = total + difference_rows(
                ref[number, x + shift], ghost_y[a, pl.ds(x, 1), :], ghost_y[3 + a, pl.ds(x, 1), :]
            )
            ref, number, shift = columns_z[a]
            total = total + (difference_z(ref[number, x + shift]) + ghost_z[a, x])
            out_ref[a, plane(x), :] = padded[a, x + 1] + (0.5 * macro_step) * total
        return carry

    lax.fori_loop(0, size_x, step_plane, 0, unroll=2)


def flow_step(velocity, viscosity, chunks, y_low, y_high):
    size_x, size_y, size_z = viscosity.shape
    planes = (size_x, size_y, size_z)
    wide = (size_x + 2, size_y, size_z)
    return pl.pallas_call(
        functools.partial(flow_kernel, size_x, size_y, size_z, chunks.shape[0] // 2),
        out_shape=(
            jax.ShapeDtypeStruct((3, size_x * size_y, size_z), jnp.float32),
            jax.ShapeDtypeStruct((8, size_z), jnp.float32),
            jax.ShapeDtypeStruct((4, size_x, size_z), jnp.float32),
        ),
        in_specs=[VMEM] * 5,
        out_specs=(VMEM, VMEM, VMEM),
        scratch_shapes=[
            pltpu.VMEM((3, *wide), jnp.float32),
            pltpu.VMEM((3, *wide), jnp.float32),
            pltpu.VMEM((3, *planes), jnp.float32),
            pltpu.VMEM((item_count, *wide), jnp.float32),
            pltpu.VMEM((6, size_x, size_z), jnp.float32),
            pltpu.VMEM((3, *planes), jnp.float32),
        ],
        compiler_params=limit(12),
        cost_estimate=pl.CostEstimate(flops=4000000, bytes_accessed=3000000, transcendentals=0),
        name="flow_step",
    )(
        velocity.reshape(3, size_x * size_y, size_z),
        viscosity.reshape(size_x * size_y, size_z),
        chunks, y_low, y_high,
    )


def polymer_kernel(
    size_x, size_y, size_z, macro_count, cell_ref, position_ref, chunk_ref, viscous_ref, corner_ref,
    edge_ref, partial_ref, out_ref, flag_ref, polymer, lines, shifted,
):
    flags = cell_ref.shape[0]
    chunk_rows = slot_rows + line_rows
    macro, core = place_of()
    lane = lanes_of((1, size_z))
    weight = 0.5 * macro_step
    out_ref[...] = partial_ref[...]

    def read(j, carry):
        polymer[pl.ds(j, 1), :] = chunk_ref[pl.ds(position_ref[j], 1), :]
        cell = cell_ref[j]
        z = cell - lax.div(cell, size_z) * size_z
        lines[0, pl.ds(j, 1), :] = jnp.where(lane == z, weight, 0.0)
        lines[1, pl.ds(j, 1), :] = jnp.where(lane == z - 1, weight, jnp.where(lane == z + 1, -weight, 0.0))
        return carry

    lax.fori_loop(0, flags, read, 0, unroll=8)
    values = polymer[...]
    here, beside_z = lines[0], lines[1]
    for k in range(6):
        column = jnp.broadcast_to(values[:, k : k + 1], (flags, size_z))
        shifted[k] = column * here
        if stress_pairs[k][1] == 2:
            shifted[6 + stress_pairs[k][0]] = column * beside_z
    flag_ref[...] = (viscous_ref[...] + values).T[0:6, :]

    for s in range(2):
        inside = macro > 0 if s == 0 else macro < macro_count - 1
        beside = jnp.maximum(macro - 1, 0) if s == 0 else jnp.minimum(macro + 1, macro_count - 1)
        start = (2 * beside + core) * chunk_rows + slot_rows
        x = 0 if s == 0 else size_x - 1
        for u in range(2):
            at = x * size_y + (0 if u == 0 else size_y - 1)
            for a in range(2):
                number = 4 * s + 2 * u + a
                line = corner_ref[number : number + 1, :] * chunk_ref[pl.ds(start + 2 * u + a, 1), :]
                out_ref[1 - a, at : at + 1, :] += jnp.where(inside, line, 0.0)
    start = pl.multiple_of((2 * macro + 1 - core) * chunk_rows + slot_rows, 8)
    packed = chunk_ref[pl.ds(start, line_rows), :]
    end = jnp.where(core == 0, size_z - 1, 0)
    for u in range(2):
        y = 0 if u == 0 else size_y - 1
        for a in range(2):
            for i in range(size_x // 8):
                line = rolled(packed, end - (4 * i + 2 * u + a)) * edge_ref[2 * u + a, 8 * i : 8 * i + 8, :]
                at = pl.ds(8 * i * size_y + y, 8, stride=size_y)
                out_ref[2 - a, at, :] += line

    def add(j, carry):
        row = lax.div(cell_ref[j], size_z)
        targets = []
        for a in range(3):
            line_x = shifted[pair_index(a, 0), pl.ds(j, 1), :]
            line_y = shifted[pair_index(a, 1), pl.ds(j, 1), :]
            line_z = shifted[6 + a, pl.ds(j, 1), :]
            targets += [
                (a, row - size_y, line_x), (a, row + size_y, -line_x),
                (a, row - 1, line_y), (a, row + 1, -line_y), (a, row, line_z),
            ]
        updated = [out_ref[a, pl.ds(at, 1), :] + line for a, at, line in targets]
        for (a, at, _), line in zip(targets, updated):
            out_ref[a, pl.ds(at, 1), :] = line
        return carry

    lax.fori_loop(0, flags, add, 0, unroll=2)


def add_polymer(flag_cell, position, chunks, viscous, corners, edges, partial, shape):
    flags = flag_cell.shape[0]
    size_x, size_y, size_z = shape
    return pl.pallas_call(
        functools.partial(polymer_kernel, size_x, size_y, size_z, chunks.shape[0] // 2),
        out_shape=(
            jax.ShapeDtypeStruct(partial.shape, jnp.float32),
            jax.ShapeDtypeStruct((6, flags), jnp.float32),
        ),
        in_specs=[SMEM, SMEM, VMEM, VMEM, VMEM, VMEM, VMEM],
        out_specs=(VMEM, VMEM),
        scratch_shapes=[
            pltpu.VMEM((flags, 128), jnp.float32),
            pltpu.VMEM((2, flags, size_z), jnp.float32),
            pltpu.VMEM((9, flags, size_z), jnp.float32),
        ],
        compiler_params=limit(8),
        cost_estimate=pl.CostEstimate(flops=400000, bytes_accessed=3000000, transcendentals=0),
        name="add_polymer",
    )(flag_cell, position, chunks.reshape(-1, 128), viscous, corners, edges, partial)


def shards(velocity, viscosity, flag_cell, flag_owner, conformations, increments):
    macro_count = lax.axis_size("macro")
    tile_count = lax.axis_size("tile")
    assert lax.axis_size("micro") == 2
    owner_count = 2 * macro_count
    capacity = conformations.shape[1] // owner_count
    size_x, size_y, size_z = viscosity.shape
    assert capacity <= slot_rows and size_y == 8 and size_z == 128 and size_x % 8 == 0 and size_x <= 48
    chunks, position, viscous, y_first, y_last = gather_rows(
        flag_cell, flag_owner.reshape(-1), velocity, viscosity, capacity, owner_count
    )

    def exchange(rows):
        return lax.all_to_all(rows, ("macro", "micro"), split_axis=0, concat_axis=0, tiled=True)

    received = exchange(chunks.reshape(owner_count, -1, 128))
    up = [(i, i + 1) for i in range(tile_count - 1)]
    down = [(target, source) for source, target in up]
    y_low = lax.ppermute(y_last, "tile", up)
    y_high = lax.ppermute(y_first, "tile", down)
    last_state, polymer = advance(conformations, increments, received, y_low, y_high, capacity)
    returned = exchange(polymer)
    partial, corners, edges = flow_step(velocity, viscosity, received, y_low, y_high)
    velocity_next, flag_stress = add_polymer(
        flag_cell, position, returned, viscous, corners, edges, partial, viscosity.shape
    )
    return (velocity_next.reshape(velocity.shape), last_state, flag_stress)


def solution(mesh):
    in_specs = (
        P(None, "macro", "tile", "micro"),
        P("macro", "tile", "micro"),
        P(("macro", "tile", "micro")),
        P(("macro", "tile", "micro"), None),
        P(None, ("macro", "tile", "micro"), None),
        P(None, None, ("macro", "tile", "micro"), None),
    )
    out_specs = (
        P(None, "macro", "tile", "micro"),
        P(None, ("macro", "tile", "micro"), None),
        P(None, ("macro", "tile", "micro")),
    )
    return jax.shard_map(shards, mesh=mesh, in_specs=in_specs, out_specs=out_specs, check_vma=False)
```

```python
import functools

import jax
import jax.numpy as jnp
from jax import lax
from jax.experimental import pallas as pl
from jax.experimental.pallas import tpu as pltpu
from jax.sharding import PartitionSpec as P

stress_pairs = ((0, 0), (1, 1), (2, 2), (0, 1), (0, 2), (1, 2))
macro_step = 0.1
micro_step = 0.01
noise_weight = 0.1
relax_rate = 0.5
fene_extent = 30.0
spring_floor = 0.1
polymer_weight = 0.25

SMEM = pl.BlockSpec(memory_space=pltpu.SMEM)
VMEM = pl.BlockSpec(memory_space=pltpu.VMEM)


def pair_index(left_axis, right_axis):
    return stress_pairs.index((min(left_axis, right_axis), max(left_axis, right_axis)))


def lanes_of(shape):
    return lax.broadcasted_iota(jnp.int32, shape, len(shape) - 1)


slot_rows = 8
item_count = 7
line_rows = 8


def limit(mebibytes):
    return pltpu.CompilerParams(vmem_limit_bytes=mebibytes * 1024 * 1024)


def far(value):
    return pltpu.with_memory_space_constraint(value, pltpu.HBM)


def place_of():
    return lax.axis_index("macro"), lax.axis_index("micro")


def rolled(value, amount):
    size = value.shape[-1]
    if isinstance(amount, int):
        return pltpu.roll(value, amount % size, value.ndim - 1)
    return pltpu.roll(value, lax.rem(amount + 2 * size, size), value.ndim - 1)


def gather_kernel(
    capacity, size_x, size_y, size_z, macro_count, cell_ref, owner_ref, velocity_ref, viscosity_ref,
    chunk_ref, position_ref, viscous_ref, y_low_ref, y_high_ref, masked, gradients, target, count,
):
    flags = cell_ref.shape[0]
    chunk_rows = slot_rows + item_count * size_y
    macro, core = place_of()
    lane = lanes_of((1, size_z))

    for owner in range(count.shape[0]):
        count[owner] = 0
        chunk_ref[owner * chunk_rows : owner * chunk_rows + slot_rows, :] = jnp.zeros((slot_rows, 128), jnp.float32)
    for j in range(flags):
        cell = cell_ref[j]
        row = lax.div(cell, size_z)
        z = cell - row * size_z
        here = (lane == z).astype(jnp.float32)
        along_z = (lane == z + 1).astype(jnp.float32) - (lane == z - 1).astype(jnp.float32)
        for a in range(3):
            along_x = velocity_ref[a, pl.ds(row + size_y, 1), :] - velocity_ref[a, pl.ds(row - size_y, 1), :]
            along_y = velocity_ref[a, pl.ds(row + 1, 1), :] - velocity_ref[a, pl.ds(row - 1, 1), :]
            masked[3 * a, j : j + 1, :] = along_x * here
            masked[3 * a + 1, j : j + 1, :] = along_y * here
            masked[3 * a + 2, j : j + 1, :] = velocity_ref[a, pl.ds(row, 1), :] * along_z
        masked[9, j : j + 1, :] = viscosity_ref[pl.ds(row, 1), :] * here
        owner = owner_ref[j]
        rank = count[owner]
        count[owner] = rank + 1
        target[j] = owner * chunk_rows + rank
        position_ref[j] = owner * (slot_rows + line_rows) + rank

    for side, ref in enumerate((y_low_ref, y_high_ref)):
        for layer in range(2):
            y = layer if side == 0 else size_y - 1 - layer
            for a in range(3):
                ref[3 * layer + a] = velocity_ref[a, pl.ds(y, size_x, stride=size_y), :]
        y = 0 if side == 0 else size_y - 1
        ref[6] = viscosity_ref[pl.ds(y, size_x, stride=size_y), :]

    for side in range(2):
        beside = macro - 1 if side == 0 else macro + 1

        @pl.when(beside >= 0 if side == 0 else beside < macro_count)
        def _(side=side, beside=beside):
            first = pl.multiple_of((2 * beside + core) * chunk_rows + slot_rows, 8)
            other = pl.multiple_of((2 * beside + 1 - core) * chunk_rows + slot_rows, 8)
            for layer in range(2):
                x = layer if side == 0 else size_x - 1 - layer
                for a in range(3):
                    chunk_ref[pl.ds(first + (3 * layer + a) * size_y, size_y), :] = velocity_ref[
                        a, x * size_y : (x + 1) * size_y, :
                    ]
            x = 0 if side == 0 else size_x - 1
            chunk_ref[pl.ds(first + 6 * size_y, size_y), :] = viscosity_ref[x * size_y : (x + 1) * size_y, :]
            for number, a in enumerate((0, 2)):
                chunk_ref[pl.ds(other + number * size_y, size_y), :] = velocity_ref[
                    a, x * size_y : (x + 1) * size_y, :
                ]

    group = size_z // 8
    lane2 = lanes_of((size_y, size_z))
    first = pl.multiple_of((2 * macro + 1 - core) * chunk_rows + slot_rows, 8)
    source = jnp.where(core == 0, size_z - 2, 0)
    for block in range(-(-size_x // group)):
        total = jnp.zeros((size_y, size_z), jnp.float32)
        for x in range(block * group, min(size_x, (block + 1) * group)):
            rows = slice(x * size_y, (x + 1) * size_y)
            for a in range(4):
                at = 8 * (x - block * group) + 2 * a
                value = viscosity_ref[rows, :] if a == 3 else velocity_ref[a, rows, :]
                total = jnp.where((lane2 == at) | (lane2 == at + 1), rolled(value, at - source), total)
        chunk_ref[pl.ds(first + block * size_y, size_y), :] = total

    columns = [0.5 * jnp.sum(masked[c], axis=1, keepdims=True) for c in range(9)]
    viscous = jnp.sum(masked[9], axis=1, keepdims=True)
    wide = lanes_of((flags, 128))
    packed = jnp.zeros((flags, 128), jnp.float32)
    for c in range(9):
        packed = jnp.where(wide == c, columns[c], packed)
    gradients[...] = packed
    stress = jnp.zeros((flags, 128), jnp.float32)
    for k, (a, b) in enumerate(stress_pairs):
        stress = jnp.where(wide == k, viscous * (columns[3 * a + b] + columns[3 * b + a]), stress)
    viscous_ref[...] = stress

    for j in range(flags):
        chunk_ref[pl.ds(target[j], 1), :] = gradients[j : j + 1, :]


def gather_rows(flag_cell, owner, velocity, viscosity, capacity, owner_count):
    size_x, size_y, size_z = viscosity.shape
    flags = flag_cell.shape[0]
    chunk_rows = slot_rows + item_count * size_y
    face = jax.ShapeDtypeStruct((item_count, size_x, size_z), jnp.float32)
    return pl.pallas_call(
        functools.partial(gather_kernel, capacity, size_x, size_y, size_z, owner_count // 2),
        out_shape=(
            jax.ShapeDtypeStruct((owner_count * chunk_rows, 128), jnp.float32),
            jax.ShapeDtypeStruct((flags,), jnp.int32),
            jax.ShapeDtypeStruct((flags, 128), jnp.float32),
            face,
            face,
        ),
        in_specs=[SMEM, SMEM, VMEM, VMEM],
        out_specs=(VMEM, SMEM, VMEM, VMEM, VMEM),
        scratch_shapes=[
            pltpu.VMEM((10, flags, size_z), jnp.float32),
            pltpu.VMEM((flags, 128), jnp.float32),
            pltpu.SMEM((flags,), jnp.int32),
            pltpu.SMEM((owner_count,), jnp.int32),
        ],
        compiler_params=limit(8),
        cost_estimate=pl.CostEstimate(flops=400000, bytes_accessed=3000000, transcendentals=0),
        name="gather_rows",
    )(
        far(flag_cell),
        far(owner),
        far(velocity.reshape(3, size_x * size_y, size_z)),
        far(viscosity.reshape(size_x * size_y, size_z)),
    )


def micro_kernel(
    capacity, parts, rows, groups, conform_ref, noise_ref, rate_ref,
    next_ref, chunk_ref, conform, noise, result, rate, sums_ref, read_sem, noise_sem, write_sem,
):
    steps, _, slots, dumbbells = noise_ref.shape
    blocks = slots // rows
    span = steps // groups
    width = dumbbells // parts
    owners = slots // capacity
    scale = 1.0 / noise_weight
    extent = fene_extent * scale * scale

    def block_rows(block):
        return pl.ds(pl.multiple_of(block * rows, rows), rows)

    def read(block):
        at = block_rows(block)
        return pltpu.make_async_copy(conform_ref.at[:, at, :], conform.at[:, at, :], read_sem.at[block])

    def read_noise(block, group):
        at, when = block_rows(block), pl.ds(group * span, span)
        return pltpu.make_async_copy(
            noise_ref.at[when, :, at, :], noise.at[when, :, at, :], noise_sem.at[block, group]
        )

    def write(block):
        at = block_rows(block)
        return pltpu.make_async_copy(result.at[:, at, :], next_ref.at[:, at, :], write_sem.at[block])

    for block in range(blocks):
        read(block).start()
        for group in range(groups):
            read_noise(block, group).start()
    for owner in range(owners):
        rate[owner * capacity : (owner + 1) * capacity, :] = rate_ref[owner, 0:capacity, :]
        chunk_ref[owner, slot_rows:, :] = jnp.zeros((line_rows, 128), jnp.float32)

    def inverse_of(q):
        room = (extent - q[0] * q[0]) - (q[1] * q[1] + q[2] * q[2])
        return pl.reciprocal(jnp.maximum(room, extent * spring_floor), approx=True)

    def advance_block(block, carry):
        at = block_rows(block)
        table = rate[at, :]
        rates = [
            [
                jnp.broadcast_to(
                    micro_step * table[:, 3 * a + b : 3 * a + b + 1] + (1.0 if a == b else 0.0), (rows, width)
                )
                for b in range(3)
            ]
            for a in range(3)
        ]

        def substep(step, state):
            updated = []
            for part in range(parts):
                q = state[3 * part : 3 * part + 3]
                spring = (micro_step * relax_rate * extent) * inverse_of(q)
                for a in range(3):
                    b, c = [other for other in range(3) if other != a]
                    kick = noise[step, a, at, part * width : (part + 1) * width].astype(jnp.float32)
                    rest = (rates[a][b] * q[b] + rates[a][c] * q[c]) + kick
                    updated.append((rates[a][a] - spring) * q[a] + rest)
            return tuple(updated)

        def advance_group(group, state):
            read_noise(block, group).wait()
            for step in range(span):
                state = substep(group * span + step, state)
            return state

        read(block).wait()
        state = tuple(
            conform[a, at, part * width : (part + 1) * width] * scale
            for part in range(parts)
            for a in range(3)
        )
        state = lax.fori_loop(0, groups, advance_group, state)
        sums = [None] * 6
        for part in range(parts):
            q = state[3 * part : 3 * part + 3]
            for a in range(3):
                result[a, at, part * width : (part + 1) * width] = q[a] * noise_weight
            inverse = inverse_of(q)
            for k, (a, b) in enumerate(stress_pairs):
                term = (inverse * q[a]) * q[b]
                sums[k] = term if sums[k] is None else sums[k] + term
        write(block).start()
        for k in range(6):
            sums_ref[k, at, :] = sums[k]
        return carry

    lax.fori_loop(0, blocks, advance_block, 0)
    lane = lanes_of((slots, 128))
    packed = jnp.zeros((slots, 128), jnp.float32)
    weight = extent * noise_weight * noise_weight / dumbbells
    for k, (a, b) in enumerate(stress_pairs):
        mean = jnp.sum(sums_ref[k], axis=1, keepdims=True) * weight
        packed = jnp.where(lane == k, polymer_weight * (mean - (1.0 if a == b else 0.0)), packed)
    for owner in range(owners):
        chunk_ref[owner, 0:capacity, :] = packed[owner * capacity : (owner + 1) * capacity]
    for block in range(blocks):
        write(block).wait()


def advance(conformations, increments, chunks, capacity):
    slots, dumbbells = conformations.shape[1:]
    steps = increments.shape[0]
    owners = slots // capacity
    rows, parts, groups = 16, 4, 4
    blocks = slots // rows
    whole = pl.BlockSpec(memory_space=pltpu.HBM)
    return pl.pallas_call(
        functools.partial(micro_kernel, capacity, parts, rows, groups),
        out_shape=(
            jax.ShapeDtypeStruct(conformations.shape, jnp.float32),
            jax.ShapeDtypeStruct((owners, slot_rows + line_rows, 128), jnp.float32),
        ),
        in_specs=[whole, whole, VMEM],
        out_specs=(whole, VMEM),
        scratch_shapes=[
            pltpu.VMEM(conformations.shape, jnp.float32),
            pltpu.VMEM(increments.shape, jnp.bfloat16),
            pltpu.VMEM(conformations.shape, jnp.float32),
            pltpu.VMEM((slots, 128), jnp.float32),
            pltpu.VMEM((6, slots, dumbbells // parts), jnp.float32),
            pltpu.SemaphoreType.DMA((blocks,)),
            pltpu.SemaphoreType.DMA((blocks, groups)),
            pltpu.SemaphoreType.DMA((blocks,)),
        ],
        compiler_params=limit(12),
        cost_estimate=pl.CostEstimate(flops=20000000, bytes_accessed=5000000, transcendentals=600000),
        name="advance",
    )(far(conformations), far(increments), chunks)


def lines_kernel(macro_count, chunk_ref, y_low_ref, y_high_ref, out_ref):
    out_ref[...] = chunk_ref[...]
    macro, core = place_of()
    size_x, size_z = y_low_ref.shape[1:]
    sides = (y_low_ref, y_high_ref)
    for side in range(2):
        beside = macro - 1 if side == 0 else macro + 1

        @pl.when(beside >= 0 if side == 0 else beside < macro_count)
        def _(side=side, beside=beside):
            x = 0 if side == 0 else size_x - 1
            for u in range(2):
                for a in range(2):
                    at = slot_rows + 2 * u + a
                    out_ref[2 * beside + core, at : at + 1, :] = sides[u][a, x : x + 1, :]

    lane = lanes_of((8, size_z))
    source = jnp.where(core == 0, size_z - 1, 0)
    total = jnp.zeros((8, size_z), jnp.float32)
    for i in range(size_x // 8):
        for u in range(2):
            for a in range(2):
                at = 4 * i + 2 * u + a
                total = jnp.where(
                    lane == at, rolled(sides[u][1 + a, 8 * i : 8 * i + 8, :], at - source), total
                )
    out_ref[2 * macro + 1 - core, slot_rows:, :] = total


def add_lines(chunks, y_low, y_high):
    return pl.pallas_call(
        functools.partial(lines_kernel, chunks.shape[0] // 2),
        out_shape=jax.ShapeDtypeStruct(chunks.shape, jnp.float32),
        in_specs=[VMEM, VMEM, VMEM],
        out_specs=VMEM,
        compiler_params=limit(4),
        cost_estimate=pl.CostEstimate(flops=20000, bytes_accessed=400000, transcendentals=0),
        name="add_lines",
    )(chunks, y_low, y_high)


def flow_kernel(
    size_x, size_y, size_z, macro_count, velocity_ref, viscosity_ref, chunk_ref, y_low_ref, y_high_ref,
    out_ref, corner_ref, edge_ref, padded, stress_x, stress_rest, faces, ghost_y, ghost_z,
):
    macro, core = place_of()
    inside = (macro > 0, macro < macro_count - 1)
    sign_z = jnp.where(core == 0, 1.0, -1.0)
    end = jnp.where(core == 0, size_z - 1, 0)
    shape = (size_y, size_z)
    lane, row = lanes_of(shape), lax.broadcasted_iota(jnp.int32, shape, 0)
    at_end = jnp.where(lane == end, sign_z, 0.0)

    def kept(value, condition):
        return jnp.where(condition, value, 0.0)

    def plane(x):
        return pl.ds(pl.multiple_of(x * size_y, 8), size_y)

    def difference_z(value):
        lane = lanes_of(value.shape)
        return jnp.where(lane == size_z - 1, 0.0, rolled(value, -1)) - jnp.where(
            lane == 0, 0.0, rolled(value, 1)
        )

    def difference_rows(value, low=0.0, high=0.0):
        count = value.shape[0]
        row = lax.broadcasted_iota(jnp.int32, value.shape, 0)
        return jnp.where(row == count - 1, high, pltpu.roll(value, count - 1, 0)) - jnp.where(
            row == 0, low, pltpu.roll(value, 1, 0)
        )

    x_faces, x_others = [], []
    for s in range(2):
        beside = jnp.maximum(macro - 1, 0) if s == 0 else jnp.minimum(macro + 1, macro_count - 1)
        x_faces.append(
            [
                kept(chunk_ref[2 * beside + core, slot_rows + i * size_y : slot_rows + (i + 1) * size_y, :], inside[s])
                for i in range(item_count)
            ]
        )
        x_others.append(
            [
                kept(
                    rolled(
                        chunk_ref[
                            2 * beside + 1 - core, slot_rows + i * size_y : slot_rows + (i + 1) * size_y, :
                        ],
                        2 * end + 1,
                    ),
                    inside[s],
                )
                for i in range(2)
            ]
        )

    group = size_z // 8
    packed = [
        chunk_ref[2 * macro + 1 - core, slot_rows + i * size_y : slot_rows + (i + 1) * size_y, :]
        for i in range(-(-size_x // group))
    ]
    for i, value in enumerate(packed):

        def unpack(x, carry):
            for q in range(item_count):
                a, layer = (q, 0) if q < 4 else (q - 4, 1)
                at = 8 * (x - i * group) + 2 * a + (core if layer == 0 else 1 - core)
                faces[q, x + 1] = rolled(value, end - at)
            return carry

        lax.fori_loop(i * group, min(size_x, (i + 1) * group), unpack, 0, unroll=2)
    faces[2, 0] = x_others[0][1]
    faces[2, size_x + 1] = x_others[1][1]

    for a in range(3):
        padded[a, 0] = x_faces[0][a]
        padded[a, size_x + 1] = x_faces[1][a]

    def fill(x, carry):
        for a in range(3):
            padded[a, x + 1] = velocity_ref[a, plane(x), :]
        return carry

    lax.fori_loop(0, size_x, fill, 0, unroll=4)

    rest = {(1, 1): 0, (2, 2): 1, (1, 2): 2}

    def stress_plane(x, carry):
        along_x, along_y, along_z, centre = [], [], [], []
        for a in range(3):
            value = padded[a, x + 1]
            centre.append(value)
            along_x.append(padded[a, x + 2] - padded[a, x])
            along_y.append(
                difference_rows(value, y_low_ref[a, pl.ds(x, 1), :], y_high_ref[a, pl.ds(x, 1), :])
            )
            along_z.append(difference_z(value) + faces[a, x + 1] * at_end)
        slopes = (along_x, along_y, along_z)
        half = 0.5 * viscosity_ref[plane(x), :]
        for a, b in stress_pairs:
            value = half * (slopes[b][a] + slopes[a][b])
            if a == 0:
                stress_x[b, x + 1] = value
            else:
                stress_rest[rest[a, b], x] = value
        weight = (0.5 * faces[3, x + 1]) * at_end
        normal = [(faces[4 + a, x + 1] - centre[a]) * sign_z for a in range(3)]
        ghost_z[0, x] = weight * (normal[0] + (faces[2, x + 2] - faces[2, x]))
        ghost_z[1, x] = weight * (normal[1] + difference_rows(faces[2, x + 1]))
        ghost_z[2, x] = weight * (2.0 * normal[2])
        return carry

    lax.fori_loop(0, size_x, stress_plane, 0, unroll=2)

    for s in range(2):
        near, far, weight = x_faces[s][0:3], x_faces[s][3:6], 0.5 * x_faces[s][6]
        sign = -1.0 if s == 0 else 1.0
        normal = [(far[a] - padded[a, 1 if s == 0 else size_x]) * sign for a in range(3)]
        slope_y = difference_rows(near[0])
        slope_z = difference_z(near[0]) + x_others[s][0] * at_end
        at = 0 if s == 0 else size_x + 1
        stress_x[0, at] = weight * (2.0 * normal[0])
        stress_x[1, at] = weight * (normal[1] + slope_y)
        stress_x[2, at] = weight * (normal[2] + slope_z)
        for u in range(2):
            y, sign_y = (0, -1.0) if u == 0 else (size_y - 1, 1.0)
            number = 4 * s + 2 * u
            corner_ref[number : number + 1, :] = (0.5 * macro_step * sign * sign_y) * weight[y : y + 1, :]

    for u, ref in enumerate((y_low_ref, y_high_ref)):
        y, sign = (0, -1.0) if u == 0 else (size_y - 1, 1.0)
        weight = 0.5 * ref[6]
        normal = [
            (ref[3 + a] - velocity_ref[a, pl.ds(y, size_x, stride=size_y), :]) * sign for a in range(3)
        ]
        ghost_y[3 * u] = weight * (normal[0] + difference_rows(ref[1]))
        ghost_y[3 * u + 1] = weight * (2.0 * normal[1])
        ghost_y[3 * u + 2] = weight * (normal[2] + difference_z(ref[1]))
        for s in range(2):
            x, sign_x = (0, -1.0) if s == 0 else (size_x - 1, 1.0)
            number = 4 * s + 2 * u + 1
            corner_ref[number : number + 1, :] = (0.5 * macro_step * sign * sign_x) * weight[x : x + 1, :]
        wide = lanes_of((size_x, size_z))
        scale = jnp.where(wide == end, (0.5 * macro_step * sign) * sign_z, 0.0)
        edge_ref[2 * u] = scale * weight
        for x in range(size_x):
            edge_ref[2 * u + 1, x : x + 1, :] = scale[x : x + 1, :] * (0.5 * faces[3, x + 1, y : y + 1, :])

    columns = {(0, 1): (stress_x, 1, 1), (1, 1): (stress_rest, 0, 0), (2, 1): (stress_rest, 2, 0)}
    columns_z = {0: (stress_x, 2, 1), 1: (stress_rest, 2, 0), 2: (stress_rest, 1, 0)}

    def step_plane(x, carry):
        for a in range(3):
            total = stress_x[a, x + 2] - stress_x[a, x]
            ref, number, shift = columns[a, 1]
            total = total + difference_rows(
                ref[number, x + shift], ghost_y[a, pl.ds(x, 1), :], ghost_y[3 + a, pl.ds(x, 1), :]
            )
            ref, number, shift = columns_z[a]
            total = total + (difference_z(ref[number, x + shift]) + ghost_z[a, x])
            out_ref[a, plane(x), :] = padded[a, x + 1] + (0.5 * macro_step) * total
        return carry

    lax.fori_loop(0, size_x, step_plane, 0, unroll=2)


def flow_step(velocity, viscosity, chunks, y_low, y_high):
    size_x, size_y, size_z = viscosity.shape
    planes = (size_x, size_y, size_z)
    wide = (size_x + 2, size_y, size_z)
    return pl.pallas_call(
        functools.partial(flow_kernel, size_x, size_y, size_z, chunks.shape[0] // 2),
        out_shape=(
            jax.ShapeDtypeStruct((3, size_x * size_y, size_z), jnp.float32),
            jax.ShapeDtypeStruct((8, size_z), jnp.float32),
            jax.ShapeDtypeStruct((4, size_x, size_z), jnp.float32),
        ),
        in_specs=[VMEM] * 5,
        out_specs=(VMEM, VMEM, VMEM),
        scratch_shapes=[
            pltpu.VMEM((3, *wide), jnp.float32),
            pltpu.VMEM((3, *wide), jnp.float32),
            pltpu.VMEM((3, *planes), jnp.float32),
            pltpu.VMEM((item_count, *wide), jnp.float32),
            pltpu.VMEM((6, size_x, size_z), jnp.float32),
            pltpu.VMEM((3, *planes), jnp.float32),
        ],
        compiler_params=limit(12),
        cost_estimate=pl.CostEstimate(flops=4000000, bytes_accessed=3000000, transcendentals=0),
        name="flow_step",
    )(
        velocity.reshape(3, size_x * size_y, size_z),
        viscosity.reshape(size_x * size_y, size_z),
        chunks, y_low, y_high,
    )


def polymer_kernel(
    size_x, size_y, size_z, macro_count, cell_ref, position_ref, chunk_ref, viscous_ref, corner_ref,
    edge_ref, partial_ref, out_ref, flag_ref, polymer, lines, shifted, field_x, field_y, field_z, write_sem,
):
    flags = cell_ref.shape[0]
    chunk_rows = slot_rows + line_rows
    macro, core = place_of()
    lane = lanes_of((1, size_z))
    weight = 0.5 * macro_step
    fields = (field_x, field_y, field_z)
    for j in range(flags):
        polymer[j : j + 1, :] = chunk_ref[pl.ds(position_ref[j], 1), :]
        cell = cell_ref[j]
        z = cell - lax.div(cell, size_z) * size_z
        lines[0, j : j + 1, :] = jnp.where(lane == z, weight, 0.0)
        lines[1, j : j + 1, :] = jnp.where(lane == z - 1, weight, jnp.where(lane == z + 1, -weight, 0.0))
    for a in range(3):
        fields[a][...] = partial_ref[a]
    values = polymer[...]
    here, beside_z = lines[0], lines[1]
    for k in range(6):
        column = jnp.broadcast_to(values[:, k : k + 1], (flags, size_z))
        shifted[k] = column * here
        if stress_pairs[k][1] == 2:
            shifted[6 + stress_pairs[k][0]] = column * beside_z
    flag_ref[...] = (viscous_ref[...] + values).T[0:6, :]

    for s in range(2):
        inside = macro > 0 if s == 0 else macro < macro_count - 1
        beside = jnp.maximum(macro - 1, 0) if s == 0 else jnp.minimum(macro + 1, macro_count - 1)
        start = (2 * beside + core) * chunk_rows + slot_rows
        x = 0 if s == 0 else size_x - 1
        for u in range(2):
            at = x * size_y + (0 if u == 0 else size_y - 1)
            for a in range(2):
                number = 4 * s + 2 * u + a
                line = corner_ref[number : number + 1, :] * chunk_ref[pl.ds(start + 2 * u + a, 1), :]
                fields[1 - a][at : at + 1, :] += jnp.where(inside, line, 0.0)
    start = pl.multiple_of((2 * macro + 1 - core) * chunk_rows + slot_rows, 8)
    packed = chunk_ref[pl.ds(start, line_rows), :]
    end = jnp.where(core == 0, size_z - 1, 0)
    for u in range(2):
        y = 0 if u == 0 else size_y - 1
        for a in range(2):
            for i in range(size_x // 8):
                line = rolled(packed, end - (4 * i + 2 * u + a)) * edge_ref[2 * u + a, 8 * i : 8 * i + 8, :]
                at = pl.ds(8 * i * size_y + y, 8, stride=size_y)
                fields[2 - a][at, :] += line

    for j in range(flags):
        row = lax.div(cell_ref[j], size_z)
        targets = []
        for a in range(3):
            line_x = shifted[pair_index(a, 0), j : j + 1, :]
            line_y = shifted[pair_index(a, 1), j : j + 1, :]
            line_z = shifted[6 + a, j : j + 1, :]
            targets += [
                (a, row - size_y, line_x), (a, row + size_y, -line_x),
                (a, row - 1, line_y), (a, row + 1, -line_y), (a, row, line_z),
            ]
        updated = [fields[a][pl.ds(at, 1), :] + line for a, at, line in targets]
        for (a, at, _), line in zip(targets, updated):
            fields[a][pl.ds(at, 1), :] = line
    copies = [pltpu.make_async_copy(fields[a], out_ref.at[a], write_sem.at[a]) for a in range(3)]
    for copy in copies:
        copy.start()
    for copy in copies:
        copy.wait()


def add_polymer(flag_cell, position, chunks, viscous, corners, edges, partial, shape):
    flags = flag_cell.shape[0]
    size_x, size_y, size_z = shape
    return pl.pallas_call(
        functools.partial(polymer_kernel, size_x, size_y, size_z, chunks.shape[0] // 2),
        out_shape=(
            jax.ShapeDtypeStruct(partial.shape, jnp.float32),
            jax.ShapeDtypeStruct((6, flags), jnp.float32),
        ),
        in_specs=[SMEM, SMEM, VMEM, VMEM, VMEM, VMEM, VMEM],
        out_specs=(pl.BlockSpec(memory_space=pltpu.HBM), VMEM),
        scratch_shapes=[
            pltpu.VMEM((flags, 128), jnp.float32),
            pltpu.VMEM((2, flags, size_z), jnp.float32),
            pltpu.VMEM((9, flags, size_z), jnp.float32),
            pltpu.VMEM(partial.shape[1:], jnp.float32),
            pltpu.VMEM(partial.shape[1:], jnp.float32),
            pltpu.VMEM(partial.shape[1:], jnp.float32),
            pltpu.SemaphoreType.DMA((3,)),
        ],
        compiler_params=limit(8),
        cost_estimate=pl.CostEstimate(flops=400000, bytes_accessed=3000000, transcendentals=0),
        name="add_polymer",
    )(flag_cell, position, chunks.reshape(-1, 128), viscous, corners, edges, partial)


def shards(velocity, viscosity, flag_cell, flag_owner, conformations, increments):
    macro_count = lax.axis_size("macro")
    tile_count = lax.axis_size("tile")
    assert lax.axis_size("micro") == 2
    owner_count = 2 * macro_count
    capacity = conformations.shape[1] // owner_count
    size_x, size_y, size_z = viscosity.shape
    assert capacity <= slot_rows and size_y == 8 and size_z == 128 and size_x % 8 == 0 and size_x <= 48
    chunks, position, viscous, y_first, y_last = gather_rows(
        flag_cell, flag_owner.reshape(-1), velocity, viscosity, capacity, owner_count
    )

    def exchange(rows):
        return lax.all_to_all(rows, ("macro", "micro"), split_axis=0, concat_axis=0, tiled=True)

    received = exchange(chunks.reshape(owner_count, -1, 128))
    up = [(i, i + 1) for i in range(tile_count - 1)]
    down = [(target, source) for source, target in up]
    y_low = lax.ppermute(y_last, "tile", up)
    y_high = lax.ppermute(y_first, "tile", down)
    last_state, polymer = advance(conformations, increments, received, capacity)
    returned = exchange(add_lines(polymer, y_low, y_high))
    partial, corners, edges = flow_step(velocity, viscosity, received, y_low, y_high)
    velocity_next, flag_stress = add_polymer(
        flag_cell, position, returned, viscous, corners, edges, partial, viscosity.shape
    )
    return (velocity_next.reshape(velocity.shape), last_state, flag_stress)


def solution(mesh):
    in_specs = (
        P(None, "macro", "tile", "micro"),
        P("macro", "tile", "micro"),
        P(("macro", "tile", "micro")),
        P(("macro", "tile", "micro"), None),
        P(None, ("macro", "tile", "micro"), None),
        P(None, None, ("macro", "tile", "micro"), None),
    )
    out_specs = (
        P(None, "macro", "tile", "micro"),
        P(None, ("macro", "tile", "micro"), None),
        P(None, ("macro", "tile", "micro")),
    )
    return jax.shard_map(shards, mesh=mesh, in_specs=in_specs, out_specs=out_specs, check_vma=False)
```

```python
import functools

import jax
import jax.numpy as jnp
from jax import lax
from jax.experimental import pallas as pl
from jax.experimental.pallas import tpu as pltpu
from jax.sharding import PartitionSpec as P

stress_pairs = ((0, 0), (1, 1), (2, 2), (0, 1), (0, 2), (1, 2))
macro_step = 0.1
micro_step = 0.01
noise_weight = 0.1
relax_rate = 0.5
fene_extent = 30.0
spring_floor = 0.1
polymer_weight = 0.25

SMEM = pl.BlockSpec(memory_space=pltpu.SMEM)
VMEM = pl.BlockSpec(memory_space=pltpu.VMEM)


def pair_index(left_axis, right_axis):
    return stress_pairs.index((min(left_axis, right_axis), max(left_axis, right_axis)))


def lanes_of(shape):
    return lax.broadcasted_iota(jnp.int32, shape, len(shape) - 1)


slot_rows = 8
item_count = 7
line_rows = 8


def limit(mebibytes):
    return pltpu.CompilerParams(vmem_limit_bytes=mebibytes * 1024 * 1024)


def far(value):
    return pltpu.with_memory_space_constraint(value, pltpu.HBM)


def place_of():
    return lax.axis_index("macro"), lax.axis_index("micro")


def rolled(value, amount):
    size = value.shape[-1]
    if isinstance(amount, int):
        return pltpu.roll(value, amount % size, value.ndim - 1)
    return pltpu.roll(value, lax.rem(amount + 2 * size, size), value.ndim - 1)


def gather_kernel(
    capacity, size_x, size_y, size_z, macro_count, cell_ref, owner_ref, velocity_ref, viscosity_ref,
    chunk_ref, position_ref, viscous_ref, y_low_ref, y_high_ref, masked, gradients, target, count,
):
    flags = cell_ref.shape[0]
    chunk_rows = slot_rows + item_count * size_y
    macro, core = place_of()
    lane = lanes_of((1, size_z))

    for owner in range(count.shape[0]):
        count[owner] = 0
        chunk_ref[owner * chunk_rows : owner * chunk_rows + slot_rows, :] = jnp.zeros((slot_rows, 128), jnp.float32)
    for j in range(flags):
        cell = cell_ref[j]
        row = lax.div(cell, size_z)
        z = cell - row * size_z
        here = (lane == z).astype(jnp.float32)
        along_z = (lane == z + 1).astype(jnp.float32) - (lane == z - 1).astype(jnp.float32)
        for a in range(3):
            along_x = velocity_ref[a, pl.ds(row + size_y, 1), :] - velocity_ref[a, pl.ds(row - size_y, 1), :]
            along_y = velocity_ref[a, pl.ds(row + 1, 1), :] - velocity_ref[a, pl.ds(row - 1, 1), :]
            masked[3 * a, j : j + 1, :] = along_x * here
            masked[3 * a + 1, j : j + 1, :] = along_y * here
            masked[3 * a + 2, j : j + 1, :] = velocity_ref[a, pl.ds(row, 1), :] * along_z
        masked[9, j : j + 1, :] = viscosity_ref[pl.ds(row, 1), :] * here
        owner = owner_ref[j]
        rank = count[owner]
        count[owner] = rank + 1
        target[j] = owner * chunk_rows + rank
        position_ref[j] = owner * (slot_rows + line_rows) + rank

    for side, ref in enumerate((y_low_ref, y_high_ref)):
        for layer in range(2):
            y = layer if side == 0 else size_y - 1 - layer
            for a in range(3):
                ref[3 * layer + a] = velocity_ref[a, pl.ds(y, size_x, stride=size_y), :]
        y = 0 if side == 0 else size_y - 1
        ref[6] = viscosity_ref[pl.ds(y, size_x, stride=size_y), :]

    for side in range(2):
        beside = macro - 1 if side == 0 else macro + 1

        @pl.when(beside >= 0 if side == 0 else beside < macro_count)
        def _(side=side, beside=beside):
            first = pl.multiple_of((2 * beside + core) * chunk_rows + slot_rows, 8)
            other = pl.multiple_of((2 * beside + 1 - core) * chunk_rows + slot_rows, 8)
            for layer in range(2):
                x = layer if side == 0 else size_x - 1 - layer
                for a in range(3):
                    chunk_ref[pl.ds(first + (3 * layer + a) * size_y, size_y), :] = velocity_ref[
                        a, x * size_y : (x + 1) * size_y, :
                    ]
            x = 0 if side == 0 else size_x - 1
            chunk_ref[pl.ds(first + 6 * size_y, size_y), :] = viscosity_ref[x * size_y : (x + 1) * size_y, :]
            for number, a in enumerate((0, 2)):
                chunk_ref[pl.ds(other + number * size_y, size_y), :] = velocity_ref[
                    a, x * size_y : (x + 1) * size_y, :
                ]

    group = size_z // 8
    lane2 = lanes_of((size_y, size_z))
    first = pl.multiple_of((2 * macro + 1 - core) * chunk_rows + slot_rows, 8)
    source = jnp.where(core == 0, size_z - 2, 0)
    for block in range(-(-size_x // group)):
        total = jnp.zeros((size_y, size_z), jnp.float32)
        for x in range(block * group, min(size_x, (block + 1) * group)):
            rows = slice(x * size_y, (x + 1) * size_y)
            for a in range(4):
                at = 8 * (x - block * group) + 2 * a
                value = viscosity_ref[rows, :] if a == 3 else velocity_ref[a, rows, :]
                total = jnp.where((lane2 == at) | (lane2 == at + 1), rolled(value, at - source), total)
        chunk_ref[pl.ds(first + block * size_y, size_y), :] = total

    columns = [0.5 * jnp.sum(masked[c], axis=1, keepdims=True) for c in range(9)]
    viscous = jnp.sum(masked[9], axis=1, keepdims=True)
    wide = lanes_of((flags, 128))
    packed = jnp.zeros((flags, 128), jnp.float32)
    for c in range(9):
        packed = jnp.where(wide == c, columns[c], packed)
    gradients[...] = packed
    stress = jnp.zeros((flags, 128), jnp.float32)
    for k, (a, b) in enumerate(stress_pairs):
        stress = jnp.where(wide == k, viscous * (columns[3 * a + b] + columns[3 * b + a]), stress)
    viscous_ref[...] = stress

    for j in range(flags):
        chunk_ref[pl.ds(target[j], 1), :] = gradients[j : j + 1, :]


def gather_rows(flag_cell, owner, velocity, viscosity, capacity, owner_count):
    size_x, size_y, size_z = viscosity.shape
    flags = flag_cell.shape[0]
    chunk_rows = slot_rows + item_count * size_y
    face = jax.ShapeDtypeStruct((item_count, size_x, size_z), jnp.float32)
    return pl.pallas_call(
        functools.partial(gather_kernel, capacity, size_x, size_y, size_z, owner_count // 2),
        out_shape=(
            jax.ShapeDtypeStruct((owner_count * chunk_rows, 128), jnp.float32),
            jax.ShapeDtypeStruct((flags,), jnp.int32),
            jax.ShapeDtypeStruct((flags, 128), jnp.float32),
            face,
            face,
        ),
        in_specs=[SMEM, SMEM, VMEM, VMEM],
        out_specs=(VMEM, SMEM, VMEM, VMEM, VMEM),
        scratch_shapes=[
            pltpu.VMEM((10, flags, size_z), jnp.float32),
            pltpu.VMEM((flags, 128), jnp.float32),
            pltpu.SMEM((flags,), jnp.int32),
            pltpu.SMEM((owner_count,), jnp.int32),
        ],
        compiler_params=limit(8),
        cost_estimate=pl.CostEstimate(flops=400000, bytes_accessed=3000000, transcendentals=0),
        name="gather_rows",
    )(
        far(flag_cell),
        far(owner),
        far(velocity.reshape(3, size_x * size_y, size_z)),
        far(viscosity.reshape(size_x * size_y, size_z)),
    )


def micro_kernel(
    capacity, parts, rows, groups, conform_ref, noise_ref, rate_ref,
    next_ref, chunk_ref, conform, noise, result, rate, sums_ref, read_sem, noise_sem, write_sem,
):
    steps, _, slots, dumbbells = noise_ref.shape
    blocks = slots // rows
    span = steps // groups
    width = dumbbells // parts
    owners = slots // capacity
    scale = 1.0 / noise_weight
    extent = fene_extent * scale * scale

    def block_rows(block):
        return pl.ds(pl.multiple_of(block * rows, rows), rows)

    def read(block):
        at = block_rows(block)
        return pltpu.make_async_copy(conform_ref.at[:, at, :], conform.at[:, at, :], read_sem.at[block])

    def read_noise(block, group):
        at, when = block_rows(block), pl.ds(group * span, span)
        return pltpu.make_async_copy(
            noise_ref.at[when, :, at, :], noise.at[when, :, at, :], noise_sem.at[block, group]
        )

    def write(block):
        at = block_rows(block)
        return pltpu.make_async_copy(result.at[:, at, :], next_ref.at[:, at, :], write_sem.at[block])

    for block in range(blocks):
        read(block).start()
        for group in range(groups):
            read_noise(block, group).start()
    for owner in range(owners):
        rate[owner * capacity : (owner + 1) * capacity, :] = rate_ref[owner, 0:capacity, :]
        chunk_ref[owner, slot_rows:, :] = jnp.zeros((line_rows, 128), jnp.float32)

    def inverse_of(q):
        room = (extent - q[0] * q[0]) - (q[1] * q[1] + q[2] * q[2])
        return pl.reciprocal(jnp.maximum(room, extent * spring_floor), approx=True)

    def advance_block(block, carry):
        at = block_rows(block)
        table = rate[at, :]
        rates = [
            [
                jnp.broadcast_to(
                    micro_step * table[:, 3 * a + b : 3 * a + b + 1] + (1.0 if a == b else 0.0), (rows, width)
                )
                for b in range(3)
            ]
            for a in range(3)
        ]

        def substep(step, state):
            updated = []
            for part in range(parts):
                q = state[3 * part : 3 * part + 3]
                spring = (micro_step * relax_rate * extent) * inverse_of(q)
                for a in range(3):
                    b, c = [other for other in range(3) if other != a]
                    kick = noise[step, a, at, part * width : (part + 1) * width].astype(jnp.float32)
                    rest = (rates[a][b] * q[b] + rates[a][c] * q[c]) + kick
                    updated.append((rates[a][a] - spring) * q[a] + rest)
            return tuple(updated)

        def advance_group(group, state):
            read_noise(block, group).wait()
            for step in range(span):
                state = substep(group * span + step, state)
            return state

        read(block).wait()
        state = tuple(
            conform[a, at, part * width : (part + 1) * width] * scale
            for part in range(parts)
            for a in range(3)
        )
        state = lax.fori_loop(0, groups, advance_group, state, unroll=True)
        sums = [None] * 6
        for part in range(parts):
            q = state[3 * part : 3 * part + 3]
            for a in range(3):
                result[a, at, part * width : (part + 1) * width] = q[a] * noise_weight
            inverse = inverse_of(q)
            for k, (a, b) in enumerate(stress_pairs):
                term = (inverse * q[a]) * q[b]
                sums[k] = term if sums[k] is None else sums[k] + term
        write(block).start()
        for k in range(6):
            sums_ref[k, at, :] = sums[k]
        return carry

    lax.fori_loop(0, blocks, advance_block, 0)
    lane = lanes_of((slots, 128))
    packed = jnp.zeros((slots, 128), jnp.float32)
    weight = extent * noise_weight * noise_weight / dumbbells
    for k, (a, b) in enumerate(stress_pairs):
        mean = jnp.sum(sums_ref[k], axis=1, keepdims=True) * weight
        packed = jnp.where(lane == k, polymer_weight * (mean - (1.0 if a == b else 0.0)), packed)
    for owner in range(owners):
        chunk_ref[owner, 0:capacity, :] = packed[owner * capacity : (owner + 1) * capacity]
    for block in range(blocks):
        write(block).wait()


def advance(conformations, increments, chunks, capacity):
    slots, dumbbells = conformations.shape[1:]
    steps = increments.shape[0]
    owners = slots // capacity
    rows, parts, groups = 16, 4, 4
    blocks = slots // rows
    whole = pl.BlockSpec(memory_space=pltpu.HBM)
    return pl.pallas_call(
        functools.partial(micro_kernel, capacity, parts, rows, groups),
        out_shape=(
            jax.ShapeDtypeStruct(conformations.shape, jnp.float32),
            jax.ShapeDtypeStruct((owners, slot_rows + line_rows, 128), jnp.float32),
        ),
        in_specs=[whole, whole, VMEM],
        out_specs=(whole, VMEM),
        scratch_shapes=[
            pltpu.VMEM(conformations.shape, jnp.float32),
            pltpu.VMEM(increments.shape, jnp.bfloat16),
            pltpu.VMEM(conformations.shape, jnp.float32),
            pltpu.VMEM((slots, 128), jnp.float32),
            pltpu.VMEM((6, slots, dumbbells // parts), jnp.float32),
            pltpu.SemaphoreType.DMA((blocks,)),
            pltpu.SemaphoreType.DMA((blocks, groups)),
            pltpu.SemaphoreType.DMA((blocks,)),
        ],
        compiler_params=limit(12),
        cost_estimate=pl.CostEstimate(flops=20000000, bytes_accessed=5000000, transcendentals=600000),
        name="advance",
    )(far(conformations), far(increments), chunks)


def lines_kernel(macro_count, chunk_ref, y_low_ref, y_high_ref, out_ref):
    out_ref[...] = chunk_ref[...]
    macro, core = place_of()
    size_x, size_z = y_low_ref.shape[1:]
    sides = (y_low_ref, y_high_ref)
    for side in range(2):
        beside = macro - 1 if side == 0 else macro + 1

        @pl.when(beside >= 0 if side == 0 else beside < macro_count)
        def _(side=side, beside=beside):
            x = 0 if side == 0 else size_x - 1
            for u in range(2):
                for a in range(2):
                    at = slot_rows + 2 * u + a
                    out_ref[2 * beside + core, at : at + 1, :] = sides[u][a, x : x + 1, :]

    lane = lanes_of((8, size_z))
    source = jnp.where(core == 0, size_z - 1, 0)
    total = jnp.zeros((8, size_z), jnp.float32)
    for i in range(size_x // 8):
        for u in range(2):
            for a in range(2):
                at = 4 * i + 2 * u + a
                total = jnp.where(
                    lane == at, rolled(sides[u][1 + a, 8 * i : 8 * i + 8, :], at - source), total
                )
    out_ref[2 * macro + 1 - core, slot_rows:, :] = total


def add_lines(chunks, y_low, y_high):
    return pl.pallas_call(
        functools.partial(lines_kernel, chunks.shape[0] // 2),
        out_shape=jax.ShapeDtypeStruct(chunks.shape, jnp.float32),
        in_specs=[VMEM, VMEM, VMEM],
        out_specs=VMEM,
        compiler_params=limit(4),
        cost_estimate=pl.CostEstimate(flops=20000, bytes_accessed=400000, transcendentals=0),
        name="add_lines",
    )(chunks, y_low, y_high)


def flow_kernel(
    size_x, size_y, size_z, macro_count, velocity_ref, viscosity_ref, chunk_ref, y_low_ref, y_high_ref,
    out_ref, corner_ref, edge_ref, padded, stress_x, stress_rest, faces, ghost_y, ghost_z,
):
    macro, core = place_of()
    inside = (macro > 0, macro < macro_count - 1)
    sign_z = jnp.where(core == 0, 1.0, -1.0)
    end = jnp.where(core == 0, size_z - 1, 0)
    shape = (size_y, size_z)
    lane, row = lanes_of(shape), lax.broadcasted_iota(jnp.int32, shape, 0)
    at_end = jnp.where(lane == end, sign_z, 0.0)

    def kept(value, condition):
        return jnp.where(condition, value, 0.0)

    def plane(x):
        return pl.ds(pl.multiple_of(x * size_y, 8), size_y)

    def difference_z(value):
        lane = lanes_of(value.shape)
        return jnp.where(lane == size_z - 1, 0.0, rolled(value, -1)) - jnp.where(
            lane == 0, 0.0, rolled(value, 1)
        )

    def difference_rows(value, low=0.0, high=0.0):
        count = value.shape[0]
        row = lax.broadcasted_iota(jnp.int32, value.shape, 0)
        return jnp.where(row == count - 1, high, pltpu.roll(value, count - 1, 0)) - jnp.where(
            row == 0, low, pltpu.roll(value, 1, 0)
        )

    x_faces, x_others = [], []
    for s in range(2):
        beside = jnp.maximum(macro - 1, 0) if s == 0 else jnp.minimum(macro + 1, macro_count - 1)
        x_faces.append(
            [
                kept(chunk_ref[2 * beside + core, slot_rows + i * size_y : slot_rows + (i + 1) * size_y, :], inside[s])
                for i in range(item_count)
            ]
        )
        x_others.append(
            [
                kept(
                    rolled(
                        chunk_ref[
                            2 * beside + 1 - core, slot_rows + i * size_y : slot_rows + (i + 1) * size_y, :
                        ],
                        2 * end + 1,
                    ),
                    inside[s],
                )
                for i in range(2)
            ]
        )

    group = size_z // 8
    packed = [
        chunk_ref[2 * macro + 1 - core, slot_rows + i * size_y : slot_rows + (i + 1) * size_y, :]
        for i in range(-(-size_x // group))
    ]
    for i, value in enumerate(packed):

        def unpack(x, carry):
            for q in range(item_count):
                a, layer = (q, 0) if q < 4 else (q - 4, 1)
                at = 8 * (x - i * group) + 2 * a + (core if layer == 0 else 1 - core)
                faces[q, x + 1] = rolled(value, end - at)
            return carry

        lax.fori_loop(i * group, min(size_x, (i + 1) * group), unpack, 0, unroll=8)
    faces[2, 0] = x_others[0][1]
    faces[2, size_x + 1] = x_others[1][1]

    for a in range(3):
        padded[a, 0] = x_faces[0][a]
        padded[a, size_x + 1] = x_faces[1][a]

    def fill(x, carry):
        for a in range(3):
            padded[a, x + 1] = velocity_ref[a, plane(x), :]
        return carry

    lax.fori_loop(0, size_x, fill, 0, unroll=True)

    rest = {(1, 1): 0, (2, 2): 1, (1, 2): 2}

    def stress_plane(x, carry):
        along_x, along_y, along_z, centre = [], [], [], []
        for a in range(3):
            value = padded[a, x + 1]
            centre.append(value)
            along_x.append(padded[a, x + 2] - padded[a, x])
            along_y.append(
                difference_rows(value, y_low_ref[a, pl.ds(x, 1), :], y_high_ref[a, pl.ds(x, 1), :])
            )
            along_z.append(difference_z(value) + faces[a, x + 1] * at_end)
        slopes = (along_x, along_y, along_z)
        half = 0.5 * viscosity_ref[plane(x), :]
        for a, b in stress_pairs:
            value = half * (slopes[b][a] + slopes[a][b])
            if a == 0:
                stress_x[b, x + 1] = value
            else:
                stress_rest[rest[a, b], x] = value
        weight = (0.5 * faces[3, x + 1]) * at_end
        normal = [(faces[4 + a, x + 1] - centre[a]) * sign_z for a in range(3)]
        ghost_z[0, x] = weight * (normal[0] + (faces[2, x + 2] - faces[2, x]))
        ghost_z[1, x] = weight * (normal[1] + difference_rows(faces[2, x + 1]))
        ghost_z[2, x] = weight * (2.0 * normal[2])
        return carry

    lax.fori_loop(0, size_x, stress_plane, 0, unroll=6)

    for s in range(2):
        near, far, weight = x_faces[s][0:3], x_faces[s][3:6], 0.5 * x_faces[s][6]
        sign = -1.0 if s == 0 else 1.0
        normal = [(far[a] - padded[a, 1 if s == 0 else size_x]) * sign for a in range(3)]
        slope_y = difference_rows(near[0])
        slope_z = difference_z(near[0]) + x_others[s][0] * at_end
        at = 0 if s == 0 else size_x + 1
        stress_x[0, at] = weight * (2.0 * normal[0])
        stress_x[1, at] = weight * (normal[1] + slope_y)
        stress_x[2, at] = weight * (normal[2] + slope_z)
        for u in range(2):
            y, sign_y = (0, -1.0) if u == 0 else (size_y - 1, 1.0)
            number = 4 * s + 2 * u
            corner_ref[number : number + 1, :] = (0.5 * macro_step * sign * sign_y) * weight[y : y + 1, :]

    for u, ref in enumerate((y_low_ref, y_high_ref)):
        y, sign = (0, -1.0) if u == 0 else (size_y - 1, 1.0)
        weight = 0.5 * ref[6]
        normal = [
            (ref[3 + a] - velocity_ref[a, pl.ds(y, size_x, stride=size_y), :]) * sign for a in range(3)
        ]
        ghost_y[3 * u] = weight * (normal[0] + difference_rows(ref[1]))
        ghost_y[3 * u + 1] = weight * (2.0 * normal[1])
        ghost_y[3 * u + 2] = weight * (normal[2] + difference_z(ref[1]))
        for s in range(2):
            x, sign_x = (0, -1.0) if s == 0 else (size_x - 1, 1.0)
            number = 4 * s + 2 * u + 1
            corner_ref[number : number + 1, :] = (0.5 * macro_step * sign * sign_x) * weight[x : x + 1, :]
        wide = lanes_of((size_x, size_z))
        scale = jnp.where(wide == end, (0.5 * macro_step * sign) * sign_z, 0.0)
        edge_ref[2 * u] = scale * weight
        for x in range(size_x):
            edge_ref[2 * u + 1, x : x + 1, :] = scale[x : x + 1, :] * (0.5 * faces[3, x + 1, y : y + 1, :])

    columns = {(0, 1): (stress_x, 1, 1), (1, 1): (stress_rest, 0, 0), (2, 1): (stress_rest, 2, 0)}
    columns_z = {0: (stress_x, 2, 1), 1: (stress_rest, 2, 0), 2: (stress_rest, 1, 0)}

    def step_plane(x, carry):
        for a in range(3):
            total = stress_x[a, x + 2] - stress_x[a, x]
            ref, number, shift = columns[a, 1]
            total = total + difference_rows(
                ref[number, x + shift], ghost_y[a, pl.ds(x, 1), :], ghost_y[3 + a, pl.ds(x, 1), :]
            )
            ref, number, shift = columns_z[a]
            total = total + (difference_z(ref[number, x + shift]) + ghost_z[a, x])
            out_ref[a, plane(x), :] = padded[a, x + 1] + (0.5 * macro_step) * total
        return carry

    lax.fori_loop(0, size_x, step_plane, 0, unroll=6)


def flow_step(velocity, viscosity, chunks, y_low, y_high):
    size_x, size_y, size_z = viscosity.shape
    planes = (size_x, size_y, size_z)
    wide = (size_x + 2, size_y, size_z)
    return pl.pallas_call(
        functools.partial(flow_kernel, size_x, size_y, size_z, chunks.shape[0] // 2),
        out_shape=(
            jax.ShapeDtypeStruct((3, size_x * size_y, size_z), jnp.float32),
            jax.ShapeDtypeStruct((8, size_z), jnp.float32),
            jax.ShapeDtypeStruct((4, size_x, size_z), jnp.float32),
        ),
        in_specs=[VMEM] * 5,
        out_specs=(VMEM, VMEM, VMEM),
        scratch_shapes=[
            pltpu.VMEM((3, *wide), jnp.float32),
            pltpu.VMEM((3, *wide), jnp.float32),
            pltpu.VMEM((3, *planes), jnp.float32),
            pltpu.VMEM((item_count, *wide), jnp.float32),
            pltpu.VMEM((6, size_x, size_z), jnp.float32),
            pltpu.VMEM((3, *planes), jnp.float32),
        ],
        compiler_params=limit(12),
        cost_estimate=pl.CostEstimate(flops=4000000, bytes_accessed=3000000, transcendentals=0),
        name="flow_step",
    )(
        velocity.reshape(3, size_x * size_y, size_z),
        viscosity.reshape(size_x * size_y, size_z),
        chunks, y_low, y_high,
    )


def polymer_kernel(
    size_x, size_y, size_z, macro_count, cell_ref, position_ref, chunk_ref, viscous_ref, corner_ref,
    edge_ref, partial_ref, out_ref, flag_ref, polymer, lines, shifted, field_x, field_y, field_z, write_sem,
):
    flags = cell_ref.shape[0]
    chunk_rows = slot_rows + line_rows
    macro, core = place_of()
    lane = lanes_of((1, size_z))
    weight = 0.5 * macro_step
    fields = (field_x, field_y, field_z)
    for j in range(flags):
        polymer[j : j + 1, :] = chunk_ref[pl.ds(position_ref[j], 1), :]
        cell = cell_ref[j]
        z = cell - lax.div(cell, size_z) * size_z
        lines[0, j : j + 1, :] = jnp.where(lane == z, weight, 0.0)
        lines[1, j : j + 1, :] = jnp.where(lane == z - 1, weight, jnp.where(lane == z + 1, -weight, 0.0))
    for a in range(3):
        fields[a][...] = partial_ref[a]
    values = polymer[...]
    here, beside_z = lines[0], lines[1]
    for k in range(6):
        column = jnp.broadcast_to(values[:, k : k + 1], (flags, size_z))
        shifted[k] = column * here
        if stress_pairs[k][1] == 2:
            shifted[6 + stress_pairs[k][0]] = column * beside_z
    flag_ref[...] = (viscous_ref[...] + values).T[0:6, :]

    for s in range(2):
        inside = macro > 0 if s == 0 else macro < macro_count - 1
        beside = jnp.maximum(macro - 1, 0) if s == 0 else jnp.minimum(macro + 1, macro_count - 1)
        start = (2 * beside + core) * chunk_rows + slot_rows
        x = 0 if s == 0 else size_x - 1
        for u in range(2):
            at = x * size_y + (0 if u == 0 else size_y - 1)
            for a in range(2):
                number = 4 * s + 2 * u + a
                line = corner_ref[number : number + 1, :] * chunk_ref[pl.ds(start + 2 * u + a, 1), :]
                fields[1 - a][at : at + 1, :] += jnp.where(inside, line, 0.0)
    start = pl.multiple_of((2 * macro + 1 - core) * chunk_rows + slot_rows, 8)
    packed = chunk_ref[pl.ds(start, line_rows), :]
    end = jnp.where(core == 0, size_z - 1, 0)
    for u in range(2):
        y = 0 if u == 0 else size_y - 1
        for a in range(2):
            for i in range(size_x // 8):
                line = rolled(packed, end - (4 * i + 2 * u + a)) * edge_ref[2 * u + a, 8 * i : 8 * i + 8, :]
                at = pl.ds(8 * i * size_y + y, 8, stride=size_y)
                fields[2 - a][at, :] += line

    for j in range(flags):
        row = lax.div(cell_ref[j], size_z)
        targets = []
        for a in range(3):
            line_x = shifted[pair_index(a, 0), j : j + 1, :]
            line_y = shifted[pair_index(a, 1), j : j + 1, :]
            line_z = shifted[6 + a, j : j + 1, :]
            targets += [
                (a, row - size_y, line_x), (a, row + size_y, -line_x),
                (a, row - 1, line_y), (a, row + 1, -line_y), (a, row, line_z),
            ]
        updated = [fields[a][pl.ds(at, 1), :] + line for a, at, line in targets]
        for (a, at, _), line in zip(targets, updated):
            fields[a][pl.ds(at, 1), :] = line
    copies = [pltpu.make_async_copy(fields[a], out_ref.at[a], write_sem.at[a]) for a in range(3)]
    for copy in copies:
        copy.start()
    for copy in copies:
        copy.wait()


def add_polymer(flag_cell, position, chunks, viscous, corners, edges, partial, shape):
    flags = flag_cell.shape[0]
    size_x, size_y, size_z = shape
    return pl.pallas_call(
        functools.partial(polymer_kernel, size_x, size_y, size_z, chunks.shape[0] // 2),
        out_shape=(
            jax.ShapeDtypeStruct(partial.shape, jnp.float32),
            jax.ShapeDtypeStruct((6, flags), jnp.float32),
        ),
        in_specs=[SMEM, SMEM, VMEM, VMEM, VMEM, VMEM, VMEM],
        out_specs=(pl.BlockSpec(memory_space=pltpu.HBM), VMEM),
        scratch_shapes=[
            pltpu.VMEM((flags, 128), jnp.float32),
            pltpu.VMEM((2, flags, size_z), jnp.float32),
            pltpu.VMEM((9, flags, size_z), jnp.float32),
            pltpu.VMEM(partial.shape[1:], jnp.float32),
            pltpu.VMEM(partial.shape[1:], jnp.float32),
            pltpu.VMEM(partial.shape[1:], jnp.float32),
            pltpu.SemaphoreType.DMA((3,)),
        ],
        compiler_params=limit(8),
        cost_estimate=pl.CostEstimate(flops=400000, bytes_accessed=3000000, transcendentals=0),
        name="add_polymer",
    )(flag_cell, position, chunks.reshape(-1, 128), viscous, corners, edges, partial)


def shards(velocity, viscosity, flag_cell, flag_owner, conformations, increments):
    macro_count = lax.axis_size("macro")
    tile_count = lax.axis_size("tile")
    assert lax.axis_size("micro") == 2
    owner_count = 2 * macro_count
    capacity = conformations.shape[1] // owner_count
    size_x, size_y, size_z = viscosity.shape
    assert capacity <= slot_rows and size_y == 8 and size_z == 128 and size_x % 8 == 0 and size_x <= 48
    chunks, position, viscous, y_first, y_last = gather_rows(
        flag_cell, flag_owner.reshape(-1), velocity, viscosity, capacity, owner_count
    )

    def exchange(rows):
        return lax.all_to_all(rows, ("macro", "micro"), split_axis=0, concat_axis=0, tiled=True)

    received = exchange(chunks.reshape(owner_count, -1, 128))
    up = [(i, i + 1) for i in range(tile_count - 1)]
    down = [(target, source) for source, target in up]
    y_low = lax.ppermute(y_last, "tile", up)
    y_high = lax.ppermute(y_first, "tile", down)
    last_state, polymer = advance(conformations, increments, received, capacity)
    returned = exchange(add_lines(polymer, y_low, y_high))
    partial, corners, edges = flow_step(velocity, viscosity, received, y_low, y_high)
    velocity_next, flag_stress = add_polymer(
        flag_cell, position, returned, viscous, corners, edges, partial, viscosity.shape
    )
    return (velocity_next.reshape(velocity.shape), last_state, flag_stress)


def solution(mesh):
    in_specs = (
        P(None, "macro", "tile", "micro"),
        P("macro", "tile", "micro"),
        P(("macro", "tile", "micro")),
        P(("macro", "tile", "micro"), None),
        P(None, ("macro", "tile", "micro"), None),
        P(None, None, ("macro", "tile", "micro"), None),
    )
    out_specs = (
        P(None, "macro", "tile", "micro"),
        P(None, ("macro", "tile", "micro"), None),
        P(None, ("macro", "tile", "micro")),
    )
    return jax.shard_map(shards, mesh=mesh, in_specs=in_specs, out_specs=out_specs, check_vma=False)
```

```python
import functools

import jax
import jax.numpy as jnp
from jax import lax
from jax.experimental import pallas as pl
from jax.experimental.pallas import tpu as pltpu
from jax.sharding import PartitionSpec as P

stress_pairs = ((0, 0), (1, 1), (2, 2), (0, 1), (0, 2), (1, 2))
macro_step = 0.1
micro_step = 0.01
noise_weight = 0.1
relax_rate = 0.5
fene_extent = 30.0
spring_floor = 0.1
polymer_weight = 0.25

SMEM = pl.BlockSpec(memory_space=pltpu.SMEM)
VMEM = pl.BlockSpec(memory_space=pltpu.VMEM)


def pair_index(left_axis, right_axis):
    return stress_pairs.index((min(left_axis, right_axis), max(left_axis, right_axis)))


def lanes_of(shape):
    return lax.broadcasted_iota(jnp.int32, shape, len(shape) - 1)


slot_rows = 8
item_count = 7
line_rows = 8


def limit(mebibytes):
    return pltpu.CompilerParams(vmem_limit_bytes=mebibytes * 1024 * 1024)


def far(value):
    return pltpu.with_memory_space_constraint(value, pltpu.HBM)


def place_of():
    return lax.axis_index("macro"), lax.axis_index("micro")


def rolled(value, amount):
    size = value.shape[-1]
    if isinstance(amount, int):
        return pltpu.roll(value, amount % size, value.ndim - 1)
    return pltpu.roll(value, lax.rem(amount + 2 * size, size), value.ndim - 1)


def gather_kernel(
    capacity, size_x, size_y, size_z, macro_count, cell_in, owner_in, velocity_in, viscosity_in,
    chunk_ref, position_ref, viscous_ref, y_low_ref, y_high_ref,
    cell_ref, owner_ref, velocity_ref, viscosity_ref, masked, gradients, target, count, sems,
):
    flags = cell_ref.shape[0]
    copies = [
        pltpu.make_async_copy(source, into, sems.at[number])
        for number, (source, into) in enumerate(
            (
                (cell_in, cell_ref), (owner_in, owner_ref), (velocity_in, velocity_ref),
                (viscosity_in, viscosity_ref),
            )
        )
    ]
    for copy in copies:
        copy.start()
    chunk_rows = slot_rows + item_count * size_y
    macro, core = place_of()
    lane = lanes_of((1, size_z))

    for owner in range(count.shape[0]):
        count[owner] = 0
        chunk_ref[owner * chunk_rows : owner * chunk_rows + slot_rows, :] = jnp.zeros((slot_rows, 128), jnp.float32)
    for copy in copies[:2]:
        copy.wait()
    for j in range(flags):
        owner = owner_ref[j]
        rank = count[owner]
        count[owner] = rank + 1
        target[j] = owner * chunk_rows + rank
        position_ref[j] = owner * (slot_rows + line_rows) + rank
    for copy in copies[2:]:
        copy.wait()
    for j in range(flags):
        cell = cell_ref[j]
        row = lax.div(cell, size_z)
        z = cell - row * size_z
        here = (lane == z).astype(jnp.float32)
        along_z = (lane == z + 1).astype(jnp.float32) - (lane == z - 1).astype(jnp.float32)
        for a in range(3):
            along_x = velocity_ref[a, pl.ds(row + size_y, 1), :] - velocity_ref[a, pl.ds(row - size_y, 1), :]
            along_y = velocity_ref[a, pl.ds(row + 1, 1), :] - velocity_ref[a, pl.ds(row - 1, 1), :]
            masked[3 * a, j : j + 1, :] = along_x * here
            masked[3 * a + 1, j : j + 1, :] = along_y * here
            masked[3 * a + 2, j : j + 1, :] = velocity_ref[a, pl.ds(row, 1), :] * along_z
        masked[9, j : j + 1, :] = viscosity_ref[pl.ds(row, 1), :] * here

    for side, ref in enumerate((y_low_ref, y_high_ref)):
        for layer in range(2):
            y = layer if side == 0 else size_y - 1 - layer
            for a in range(3):
                ref[3 * layer + a] = velocity_ref[a, pl.ds(y, size_x, stride=size_y), :]
        y = 0 if side == 0 else size_y - 1
        ref[6] = viscosity_ref[pl.ds(y, size_x, stride=size_y), :]

    for side in range(2):
        beside = macro - 1 if side == 0 else macro + 1

        @pl.when(beside >= 0 if side == 0 else beside < macro_count)
        def _(side=side, beside=beside):
            first = pl.multiple_of((2 * beside + core) * chunk_rows + slot_rows, 8)
            other = pl.multiple_of((2 * beside + 1 - core) * chunk_rows + slot_rows, 8)
            for layer in range(2):
                x = layer if side == 0 else size_x - 1 - layer
                for a in range(3):
                    chunk_ref[pl.ds(first + (3 * layer + a) * size_y, size_y), :] = velocity_ref[
                        a, x * size_y : (x + 1) * size_y, :
                    ]
            x = 0 if side == 0 else size_x - 1
            chunk_ref[pl.ds(first + 6 * size_y, size_y), :] = viscosity_ref[x * size_y : (x + 1) * size_y, :]
            for number, a in enumerate((0, 2)):
                chunk_ref[pl.ds(other + number * size_y, size_y), :] = velocity_ref[
                    a, x * size_y : (x + 1) * size_y, :
                ]

    group = size_z // 8
    lane2 = lanes_of((size_y, size_z))
    first = pl.multiple_of((2 * macro + 1 - core) * chunk_rows + slot_rows, 8)
    source = jnp.where(core == 0, size_z - 2, 0)
    for block in range(-(-size_x // group)):
        total = jnp.zeros((size_y, size_z), jnp.float32)
        for x in range(block * group, min(size_x, (block + 1) * group)):
            rows = slice(x * size_y, (x + 1) * size_y)
            for a in range(4):
                at = 8 * (x - block * group) + 2 * a
                value = viscosity_ref[rows, :] if a == 3 else velocity_ref[a, rows, :]
                total = jnp.where((lane2 == at) | (lane2 == at + 1), rolled(value, at - source), total)
        chunk_ref[pl.ds(first + block * size_y, size_y), :] = total

    columns = [0.5 * jnp.sum(masked[c], axis=1, keepdims=True) for c in range(9)]
    viscous = jnp.sum(masked[9], axis=1, keepdims=True)
    wide = lanes_of((flags, 128))
    packed = jnp.zeros((flags, 128), jnp.float32)
    for c in range(9):
        packed = jnp.where(wide == c, columns[c], packed)
    gradients[...] = packed
    stress = jnp.zeros((flags, 128), jnp.float32)
    for k, (a, b) in enumerate(stress_pairs):
        stress = jnp.where(wide == k, viscous * (columns[3 * a + b] + columns[3 * b + a]), stress)
    viscous_ref[...] = stress

    for j in range(flags):
        chunk_ref[pl.ds(target[j], 1), :] = gradients[j : j + 1, :]


def gather_rows(flag_cell, owner, velocity, viscosity, capacity, owner_count):
    size_x, size_y, size_z = viscosity.shape
    flags = flag_cell.shape[0]
    chunk_rows = slot_rows + item_count * size_y
    face = jax.ShapeDtypeStruct((item_count, size_x, size_z), jnp.float32)
    return pl.pallas_call(
        functools.partial(gather_kernel, capacity, size_x, size_y, size_z, owner_count // 2),
        out_shape=(
            jax.ShapeDtypeStruct((owner_count * chunk_rows, 128), jnp.float32),
            jax.ShapeDtypeStruct((flags,), jnp.int32),
            jax.ShapeDtypeStruct((flags, 128), jnp.float32),
            face,
            face,
        ),
        in_specs=[pl.BlockSpec(memory_space=pltpu.HBM)] * 4,
        out_specs=(VMEM, SMEM, VMEM, VMEM, VMEM),
        scratch_shapes=[
            pltpu.SMEM((flags,), jnp.int32),
            pltpu.SMEM((flags,), jnp.int32),
            pltpu.VMEM((3, size_x * size_y, size_z), jnp.float32),
            pltpu.VMEM((size_x * size_y, size_z), jnp.float32),
            pltpu.VMEM((10, flags, size_z), jnp.float32),
            pltpu.VMEM((flags, 128), jnp.float32),
            pltpu.SMEM((flags,), jnp.int32),
            pltpu.SMEM((owner_count,), jnp.int32),
            pltpu.SemaphoreType.DMA((4,)),
        ],
        compiler_params=limit(8),
        cost_estimate=pl.CostEstimate(flops=400000, bytes_accessed=3000000, transcendentals=0),
        name="gather_rows",
    )(
        far(flag_cell),
        far(owner),
        far(velocity.reshape(3, size_x * size_y, size_z)),
        far(viscosity.reshape(size_x * size_y, size_z)),
    )


def micro_kernel(
    capacity, parts, rows, groups, conform_ref, noise_ref, rate_ref,
    next_ref, chunk_ref, conform, noise, rate, rate_wide, sums_ref, read_sem, noise_sem,
):
    steps, _, slots, dumbbells = noise_ref.shape
    blocks = slots // rows
    span = steps // groups
    width = dumbbells // parts
    owners = slots // capacity
    scale = 1.0 / noise_weight
    extent = fene_extent * scale * scale

    def block_rows(block):
        return pl.ds(pl.multiple_of(block * rows, rows), rows)

    def read(block):
        at = block_rows(block)
        return pltpu.make_async_copy(conform_ref.at[:, at, :], conform.at[:, at, :], read_sem.at[block])

    def read_noise(block, group):
        at, when = block_rows(block), pl.ds(group * span, span)
        return pltpu.make_async_copy(
            noise_ref.at[when, :, at, :], noise.at[when, :, at, :], noise_sem.at[block, group]
        )

    for block in range(blocks):
        read(block).start()
        for group in range(groups):
            read_noise(block, group).start()
    for owner in range(owners):
        rate[owner * capacity : (owner + 1) * capacity, :] = rate_ref[owner, 0:capacity, :]
        chunk_ref[owner] = jnp.zeros(chunk_ref.shape[1:], jnp.float32)
    for a in range(3):
        for b in range(3):
            column = micro_step * rate[:, 3 * a + b : 3 * a + b + 1] + (1.0 if a == b else 0.0)
            rate_wide[3 * a + b] = jnp.broadcast_to(column, (slots, width))

    def inverse_of(q):
        room = (extent - q[0] * q[0]) - (q[1] * q[1] + q[2] * q[2])
        return pl.reciprocal(jnp.maximum(room, extent * spring_floor), approx=True)

    def advance_block(block, carry):
        at = block_rows(block)
        rates = [[rate_wide.at[3 * a + b, at, :] for b in range(3)] for a in range(3)]

        def substep(step, state):
            updated = []
            for part in range(parts):
                q = state[3 * part : 3 * part + 3]
                spring = (micro_step * relax_rate * extent) * inverse_of(q)
                for a in range(3):
                    b, c = [other for other in range(3) if other != a]
                    kick = noise[step, a, at, part * width : (part + 1) * width].astype(jnp.float32)
                    rest = (rates[a][b][...] * q[b] + rates[a][c][...] * q[c]) + kick
                    updated.append((rates[a][a][...] - spring) * q[a] + rest)
            return tuple(updated)

        def advance_group(group, state):
            read_noise(block, group).wait()
            for step in range(span):
                state = substep(group * span + step, state)
            return state

        read(block).wait()
        state = tuple(
            conform[a, at, part * width : (part + 1) * width] * scale
            for part in range(parts)
            for a in range(3)
        )
        state = lax.fori_loop(0, groups, advance_group, state, unroll=True)
        sums = [None] * 6
        for part in range(parts):
            q = state[3 * part : 3 * part + 3]
            for a in range(3):
                next_ref[a, at, part * width : (part + 1) * width] = q[a] * noise_weight
            inverse = inverse_of(q)
            for k, (a, b) in enumerate(stress_pairs):
                term = (inverse * q[a]) * q[b]
                sums[k] = term if sums[k] is None else sums[k] + term
        for k in range(6):
            sums_ref[k, at, :] = sums[k]
        return carry

    lax.fori_loop(0, blocks, advance_block, 0)
    lane = lanes_of((slots, 128))
    packed = jnp.zeros((slots, 128), jnp.float32)
    weight = extent * noise_weight * noise_weight / dumbbells
    for k, (a, b) in enumerate(stress_pairs):
        mean = jnp.sum(sums_ref[k], axis=1, keepdims=True) * weight
        packed = jnp.where(lane == k, polymer_weight * (mean - (1.0 if a == b else 0.0)), packed)
    for owner in range(owners):
        chunk_ref[owner, 0:capacity, :] = packed[owner * capacity : (owner + 1) * capacity]


def advance(conformations, increments, chunks, capacity):
    slots, dumbbells = conformations.shape[1:]
    steps = increments.shape[0]
    owners = slots // capacity
    rows, parts, groups = 16, 4, 4
    blocks = slots // rows
    whole = pl.BlockSpec(memory_space=pltpu.HBM)
    return pl.pallas_call(
        functools.partial(micro_kernel, capacity, parts, rows, groups),
        out_shape=(
            pltpu.VMEM(conformations.shape, jnp.float32),
            jax.ShapeDtypeStruct((owners, slot_rows + line_rows, 128), jnp.float32),
        ),
        in_specs=[whole, whole, VMEM],
        out_specs=(VMEM, VMEM),
        scratch_shapes=[
            pltpu.VMEM(conformations.shape, jnp.float32),
            pltpu.VMEM(increments.shape, jnp.bfloat16),
            pltpu.VMEM((slots, 128), jnp.float32),
            pltpu.VMEM((9, slots, dumbbells // parts), jnp.float32),
            pltpu.VMEM((6, slots, dumbbells // parts), jnp.float32),
            pltpu.SemaphoreType.DMA((blocks,)),
            pltpu.SemaphoreType.DMA((blocks, groups)),
        ],
        compiler_params=limit(12),
        cost_estimate=pl.CostEstimate(flops=20000000, bytes_accessed=5000000, transcendentals=600000),
        name="advance",
    )(far(conformations), far(increments), chunks)


def lines_kernel(macro_count, chunk_ref, y_low_ref, y_high_ref, out_ref):
    out_ref[...] = chunk_ref[...]
    macro, core = place_of()
    size_x, size_z = y_low_ref.shape[1:]
    sides = (y_low_ref, y_high_ref)
    for side in range(2):
        beside = macro - 1 if side == 0 else macro + 1

        @pl.when(beside >= 0 if side == 0 else beside < macro_count)
        def _(side=side, beside=beside):
            x = 0 if side == 0 else size_x - 1
            for u in range(2):
                for a in range(2):
                    at = slot_rows + 2 * u + a
                    out_ref[2 * beside + core, at : at + 1, :] = sides[u][a, x : x + 1, :]

    lane = lanes_of((8, size_z))
    source = jnp.where(core == 0, size_z - 1, 0)
    total = jnp.zeros((8, size_z), jnp.float32)
    for i in range(size_x // 8):
        for u in range(2):
            for a in range(2):
                at = 4 * i + 2 * u + a
                total = jnp.where(
                    lane == at, rolled(sides[u][1 + a, 8 * i : 8 * i + 8, :], at - source), total
                )
    out_ref[2 * macro + 1 - core, slot_rows:, :] = total


def add_lines(chunks, y_low, y_high):
    return pl.pallas_call(
        functools.partial(lines_kernel, chunks.shape[0] // 2),
        out_shape=jax.ShapeDtypeStruct(chunks.shape, jnp.float32),
        in_specs=[VMEM, VMEM, VMEM],
        out_specs=VMEM,
        input_output_aliases={0: 0},
        compiler_params=limit(4),
        cost_estimate=pl.CostEstimate(flops=20000, bytes_accessed=400000, transcendentals=0),
        name="add_lines",
    )(chunks, y_low, y_high)


product_depth = 128


def one_hots(size_y, size_z, cell_ref, position_ref, lines_ref, pick_ref, spread_ref, rows):
    flags = cell_ref.shape[0]
    weight = 0.5 * macro_step
    row_count = spread_ref.shape[0]
    back_rows = pick_ref.shape[1] // 3
    lane = lanes_of((1, size_z))
    row_lane = lanes_of((1, rows.shape[1]))
    slot_lane = lanes_of((flags, back_rows))
    flag_row = lax.broadcasted_iota(jnp.int32, (flags, back_rows), 0)
    rows[3 * flags :, :] = jnp.zeros((product_depth - 3 * flags, rows.shape[1]), jnp.float32)
    slot = jnp.zeros((flags, back_rows), jnp.int32)
    for j in range(flags):
        cell = cell_ref[j]
        row = lax.div(cell, size_z)
        z = cell - row * size_z
        lines_ref[0, j : j + 1, :] = jnp.where(lane == z, weight, 0.0)
        lines_ref[1, j : j + 1, :] = jnp.where(
            lane == z - 1, weight, jnp.where(lane == z + 1, -weight, 0.0)
        )
        for number, shift in enumerate((size_y, 1)):
            rows[number * flags + j : number * flags + j + 1, :] = jnp.where(
                row_lane == row - shift, 1.0, jnp.where(row_lane == row + shift, -1.0, 0.0)
            )
        rows[2 * flags + j : 2 * flags + j + 1, :] = jnp.where(row_lane == row, 1.0, 0.0)
        slot = jnp.where(flag_row == j, position_ref[j], slot)
    spread = rows[...].T[:row_count].astype(jnp.bfloat16)
    pick = jnp.where(slot_lane == slot, 1.0, 0.0).astype(jnp.bfloat16)
    for piece in range(3):
        spread_ref[:, piece * product_depth : (piece + 1) * product_depth] = spread
        pick_ref[:, piece * back_rows : (piece + 1) * back_rows] = pick


def flow_kernel(
    size_x, size_y, size_z, macro_count, cell_ref, position_ref, velocity_ref, viscosity_ref, chunk_ref,
    y_low_ref, y_high_ref, out_ref, corner_ref, edge_ref, lines_ref, pick_ref, spread_ref,
    padded, stress_x, stress_rest, faces, ghost_y, ghost_z, rows,
):
    macro, core = place_of()
    one_hots(size_y, size_z, cell_ref, position_ref, lines_ref, pick_ref, spread_ref, rows)
    inside = (macro > 0, macro < macro_count - 1)
    sign_z = jnp.where(core == 0, 1.0, -1.0)
    end = jnp.where(core == 0, size_z - 1, 0)
    shape = (size_y, size_z)
    lane, row = lanes_of(shape), lax.broadcasted_iota(jnp.int32, shape, 0)
    at_end = jnp.where(lane == end, sign_z, 0.0)

    def kept(value, condition):
        return jnp.where(condition, value, 0.0)

    def plane(x):
        return pl.ds(pl.multiple_of(x * size_y, 8), size_y)

    def difference_z(value):
        lane = lanes_of(value.shape)
        return jnp.where(lane == size_z - 1, 0.0, rolled(value, -1)) - jnp.where(
            lane == 0, 0.0, rolled(value, 1)
        )

    def difference_rows(value, low=0.0, high=0.0):
        count = value.shape[0]
        row = lax.broadcasted_iota(jnp.int32, value.shape, 0)
        return jnp.where(row == count - 1, high, pltpu.roll(value, count - 1, 0)) - jnp.where(
            row == 0, low, pltpu.roll(value, 1, 0)
        )

    x_faces, x_others = [], []
    for s in range(2):
        beside = jnp.maximum(macro - 1, 0) if s == 0 else jnp.minimum(macro + 1, macro_count - 1)
        x_faces.append(
            [
                kept(chunk_ref[2 * beside + core, slot_rows + i * size_y : slot_rows + (i + 1) * size_y, :], inside[s])
                for i in range(item_count)
            ]
        )
        x_others.append(
            [
                kept(
                    rolled(
                        chunk_ref[
                            2 * beside + 1 - core, slot_rows + i * size_y : slot_rows + (i + 1) * size_y, :
                        ],
                        2 * end + 1,
                    ),
                    inside[s],
                )
                for i in range(2)
            ]
        )

    group = size_z // 8
    packed = [
        chunk_ref[2 * macro + 1 - core, slot_rows + i * size_y : slot_rows + (i + 1) * size_y, :]
        for i in range(-(-size_x // group))
    ]
    for i, value in enumerate(packed):

        def unpack(x, carry):
            for q in range(item_count):
                a, layer = (q, 0) if q < 4 else (q - 4, 1)
                at = 8 * (x - i * group) + 2 * a + (core if layer == 0 else 1 - core)
                faces[q, x + 1] = rolled(value, end - at)
            return carry

        lax.fori_loop(i * group, min(size_x, (i + 1) * group), unpack, 0, unroll=8)
    faces[2, 0] = x_others[0][1]
    faces[2, size_x + 1] = x_others[1][1]

    for a in range(3):
        padded[a, 0] = x_faces[0][a]
        padded[a, size_x + 1] = x_faces[1][a]

    def fill(x, carry):
        for a in range(3):
            padded[a, x + 1] = velocity_ref[a, plane(x), :]
        return carry

    lax.fori_loop(0, size_x, fill, 0, unroll=True)

    rest = {(1, 1): 0, (2, 2): 1, (1, 2): 2}

    def stress_plane(x, carry):
        along_x, along_y, along_z, centre = [], [], [], []
        for a in range(3):
            value = padded[a, x + 1]
            centre.append(value)
            along_x.append(padded[a, x + 2] - padded[a, x])
            along_y.append(
                difference_rows(value, y_low_ref[a, pl.ds(x, 1), :], y_high_ref[a, pl.ds(x, 1), :])
            )
            along_z.append(difference_z(value) + faces[a, x + 1] * at_end)
        slopes = (along_x, along_y, along_z)
        half = 0.5 * viscosity_ref[plane(x), :]
        for a, b in stress_pairs:
            value = half * (slopes[b][a] + slopes[a][b])
            if a == 0:
                stress_x[b, x + 1] = value
            else:
                stress_rest[rest[a, b], x] = value
        weight = (0.5 * faces[3, x + 1]) * at_end
        normal = [(faces[4 + a, x + 1] - centre[a]) * sign_z for a in range(3)]
        ghost_z[0, x] = weight * (normal[0] + (faces[2, x + 2] - faces[2, x]))
        ghost_z[1, x] = weight * (normal[1] + difference_rows(faces[2, x + 1]))
        ghost_z[2, x] = weight * (2.0 * normal[2])
        return carry

    lax.fori_loop(0, size_x, stress_plane, 0, unroll=6)

    for s in range(2):
        near, far, weight = x_faces[s][0:3], x_faces[s][3:6], 0.5 * x_faces[s][6]
        sign = -1.0 if s == 0 else 1.0
        normal = [(far[a] - padded[a, 1 if s == 0 else size_x]) * sign for a in range(3)]
        slope_y = difference_rows(near[0])
        slope_z = difference_z(near[0]) + x_others[s][0] * at_end
        at = 0 if s == 0 else size_x + 1
        stress_x[0, at] = weight * (2.0 * normal[0])
        stress_x[1, at] = weight * (normal[1] + slope_y)
        stress_x[2, at] = weight * (normal[2] + slope_z)
        for u in range(2):
            y, sign_y = (0, -1.0) if u == 0 else (size_y - 1, 1.0)
            number = 4 * s + 2 * u
            corner_ref[number : number + 1, :] = (0.5 * macro_step * sign * sign_y) * weight[y : y + 1, :]

    for u, ref in enumerate((y_low_ref, y_high_ref)):
        y, sign = (0, -1.0) if u == 0 else (size_y - 1, 1.0)
        weight = 0.5 * ref[6]
        normal = [
            (ref[3 + a] - velocity_ref[a, pl.ds(y, size_x, stride=size_y), :]) * sign for a in range(3)
        ]
        ghost_y[3 * u] = weight * (normal[0] + difference_rows(ref[1]))
        ghost_y[3 * u + 1] = weight * (2.0 * normal[1])
        ghost_y[3 * u + 2] = weight * (normal[2] + difference_z(ref[1]))
        for s in range(2):
            x, sign_x = (0, -1.0) if s == 0 else (size_x - 1, 1.0)
            number = 4 * s + 2 * u + 1
            corner_ref[number : number + 1, :] = (0.5 * macro_step * sign * sign_x) * weight[x : x + 1, :]
        wide = lanes_of((size_x, size_z))
        scale = jnp.where(wide == end, (0.5 * macro_step * sign) * sign_z, 0.0)
        edge_ref[2 * u] = scale * weight
        for x in range(size_x):
            edge_ref[2 * u + 1, x : x + 1, :] = scale[x : x + 1, :] * (0.5 * faces[3, x + 1, y : y + 1, :])

    columns = {(0, 1): (stress_x, 1, 1), (1, 1): (stress_rest, 0, 0), (2, 1): (stress_rest, 2, 0)}
    columns_z = {0: (stress_x, 2, 1), 1: (stress_rest, 2, 0), 2: (stress_rest, 1, 0)}

    def step_plane(x, carry):
        for a in range(3):
            total = stress_x[a, x + 2] - stress_x[a, x]
            ref, number, shift = columns[a, 1]
            total = total + difference_rows(
                ref[number, x + shift], ghost_y[a, pl.ds(x, 1), :], ghost_y[3 + a, pl.ds(x, 1), :]
            )
            ref, number, shift = columns_z[a]
            total = total + (difference_z(ref[number, x + shift]) + ghost_z[a, x])
            out_ref[a, plane(x), :] = padded[a, x + 1] + (0.5 * macro_step) * total
        return carry

    lax.fori_loop(0, size_x, step_plane, 0, unroll=6)


def flow_step(flag_cell, position, velocity, viscosity, chunks, y_low, y_high):
    size_x, size_y, size_z = viscosity.shape
    flags = flag_cell.shape[0]
    back_rows = chunks.shape[0] * (slot_rows + line_rows)
    row_count = size_x * size_y
    planes = (size_x, size_y, size_z)
    wide = (size_x + 2, size_y, size_z)
    return pl.pallas_call(
        functools.partial(flow_kernel, size_x, size_y, size_z, chunks.shape[0] // 2),
        out_shape=(
            jax.ShapeDtypeStruct((3, size_x * size_y, size_z), jnp.float32),
            jax.ShapeDtypeStruct((8, size_z), jnp.float32),
            jax.ShapeDtypeStruct((4, size_x, size_z), jnp.float32),
            jax.ShapeDtypeStruct((2, flags, size_z), jnp.float32),
            jax.ShapeDtypeStruct((flags, 3 * back_rows), jnp.bfloat16),
            jax.ShapeDtypeStruct((row_count, 3 * product_depth), jnp.bfloat16),
        ),
        in_specs=[SMEM] * 2 + [VMEM] * 5,
        out_specs=(VMEM,) * 6,
        scratch_shapes=[
            pltpu.VMEM((3, *wide), jnp.float32),
            pltpu.VMEM((3, *wide), jnp.float32),
            pltpu.VMEM((3, *planes), jnp.float32),
            pltpu.VMEM((item_count, *wide), jnp.float32),
            pltpu.VMEM((6, size_x, size_z), jnp.float32),
            pltpu.VMEM((3, *planes), jnp.float32),
            pltpu.VMEM((product_depth, -(-row_count // 128) * 128), jnp.float32),
        ],
        compiler_params=limit(12),
        cost_estimate=pl.CostEstimate(flops=4000000, bytes_accessed=3000000, transcendentals=0),
        name="flow_step",
    )(
        flag_cell, position,
        velocity.reshape(3, size_x * size_y, size_z),
        viscosity.reshape(size_x * size_y, size_z),
        chunks, y_low, y_high,
    )


def pieces(value):
    high = value.astype(jnp.bfloat16)
    rest = value - high.astype(jnp.float32)
    middle = rest.astype(jnp.bfloat16)
    return high, middle, (rest - middle.astype(jnp.float32)).astype(jnp.bfloat16)


def polymer_kernel(
    size_x, size_y, size_z, macro_count, chunk_ref, viscous_ref, corner_ref, edge_ref, lines_ref, pick_ref,
    spread_ref, partial_ref, out_ref, flag_ref, field, write_sem,
):
    flags = viscous_ref.shape[0]
    chunk_rows = slot_rows + line_rows
    macro, core = place_of()
    values = jnp.dot(
        pick_ref[...], jnp.concatenate(pieces(chunk_ref[...]), axis=0), preferred_element_type=jnp.float32
    )
    here, beside_z = lines_ref[0], lines_ref[1]
    columns = [jnp.broadcast_to(values[:, k : k + 1], (flags, size_z)) for k in range(6)]
    unused = jnp.zeros((product_depth - 3 * flags, size_z), jnp.float32)
    split = [
        pieces(
            jnp.concatenate(
                [
                    columns[pair_index(a, 0)] * here, columns[pair_index(a, 1)] * here,
                    columns[pair_index(a, 2)] * beside_z, unused,
                ],
                axis=0,
            )
        )
        for a in range(3)
    ]
    flag_ref[...] = (viscous_ref[...] + values).T[0:6, :]

    field[...] = partial_ref[...]
    for s in range(2):
        inside = macro > 0 if s == 0 else macro < macro_count - 1
        beside = jnp.maximum(macro - 1, 0) if s == 0 else jnp.minimum(macro + 1, macro_count - 1)
        start = (2 * beside + core) * chunk_rows + slot_rows
        x = 0 if s == 0 else size_x - 1
        for u in range(2):
            at = x * size_y + (0 if u == 0 else size_y - 1)
            for a in range(2):
                number = 4 * s + 2 * u + a
                line = corner_ref[number : number + 1, :] * chunk_ref[pl.ds(start + 2 * u + a, 1), :]
                field[1 - a, at : at + 1, :] += jnp.where(inside, line, 0.0)
    start = pl.multiple_of((2 * macro + 1 - core) * chunk_rows + slot_rows, 8)
    packed = chunk_ref[pl.ds(start, line_rows), :]
    end = jnp.where(core == 0, size_z - 1, 0)
    for u in range(2):
        y = 0 if u == 0 else size_y - 1
        for a in range(2):
            for i in range(size_x // 8):
                line = rolled(packed, end - (4 * i + 2 * u + a)) * edge_ref[2 * u + a, 8 * i : 8 * i + 8, :]
                at = pl.ds(8 * i * size_y + y, 8, stride=size_y)
                field[2 - a, at, :] += line
    copies = [pltpu.make_async_copy(field.at[a], out_ref.at[a], write_sem.at[a]) for a in range(3)]
    for a in range(3):
        field[a] += jnp.dot(
            spread_ref[...], jnp.concatenate(split[a], axis=0), preferred_element_type=jnp.float32
        )
        copies[a].start()
    for copy in copies:
        copy.wait()


def add_polymer(chunks, viscous, corners, edges, lines, pick, spread, partial, shape):
    flags = viscous.shape[0]
    size_x, size_y, size_z = shape
    return pl.pallas_call(
        functools.partial(polymer_kernel, size_x, size_y, size_z, chunks.shape[0] // 2),
        out_shape=(
            jax.ShapeDtypeStruct(partial.shape, jnp.float32),
            jax.ShapeDtypeStruct((6, flags), jnp.float32),
        ),
        in_specs=[VMEM] * 8,
        out_specs=(pl.BlockSpec(memory_space=pltpu.HBM), VMEM),
        scratch_shapes=[pltpu.VMEM(partial.shape, jnp.float32), pltpu.SemaphoreType.DMA((3,))],
        compiler_params=limit(8),
        cost_estimate=pl.CostEstimate(flops=400000, bytes_accessed=3000000, transcendentals=0),
        name="add_polymer",
    )(chunks.reshape(-1, 128), viscous, corners, edges, lines, pick, spread, partial)


def shards(velocity, viscosity, flag_cell, flag_owner, conformations, increments):
    macro_count = lax.axis_size("macro")
    tile_count = lax.axis_size("tile")
    assert lax.axis_size("micro") == 2
    owner_count = 2 * macro_count
    capacity = conformations.shape[1] // owner_count
    size_x, size_y, size_z = viscosity.shape
    assert capacity <= slot_rows and size_y == 8 and size_z == 128 and size_x % 8 == 0 and size_x <= 48
    chunks, position, viscous, y_first, y_last = gather_rows(
        flag_cell, flag_owner.reshape(-1), velocity, viscosity, capacity, owner_count
    )

    def exchange(rows):
        return lax.all_to_all(rows, ("macro", "micro"), split_axis=0, concat_axis=0, tiled=True)

    received = exchange(chunks.reshape(owner_count, -1, 128))
    up = [(i, i + 1) for i in range(tile_count - 1)]
    down = [(target, source) for source, target in up]
    y_low = lax.ppermute(y_last, "tile", up)
    y_high = lax.ppermute(y_first, "tile", down)
    last_state, polymer = advance(conformations, increments, received, capacity)
    returned = exchange(add_lines(polymer, y_low, y_high))
    partial, corners, edges, lines, pick, spread = flow_step(
        flag_cell, position, velocity, viscosity, received, y_low, y_high
    )
    velocity_next, flag_stress = add_polymer(
        returned, viscous, corners, edges, lines, pick, spread, partial, viscosity.shape
    )
    return (velocity_next.reshape(velocity.shape), last_state, flag_stress)


def solution(mesh):
    in_specs = (
        P(None, "macro", "tile", "micro"),
        P("macro", "tile", "micro"),
        P(("macro", "tile", "micro")),
        P(("macro", "tile", "micro"), None),
        P(None, ("macro", "tile", "micro"), None),
        P(None, None, ("macro", "tile", "micro"), None),
    )
    out_specs = (
        P(None, "macro", "tile", "micro"),
        P(None, ("macro", "tile", "micro"), None),
        P(None, ("macro", "tile", "micro")),
    )
    return jax.shard_map(shards, mesh=mesh, in_specs=in_specs, out_specs=out_specs, check_vma=False)
```

```python
import functools

import jax
import jax.numpy as jnp
from jax import lax
from jax.experimental import pallas as pl
from jax.experimental.pallas import tpu as pltpu
from jax.sharding import PartitionSpec as P

stress_pairs = ((0, 0), (1, 1), (2, 2), (0, 1), (0, 2), (1, 2))
macro_step = 0.1
micro_step = 0.01
noise_weight = 0.1
relax_rate = 0.5
fene_extent = 30.0
spring_floor = 0.1
polymer_weight = 0.25

SMEM = pl.BlockSpec(memory_space=pltpu.SMEM)
VMEM = pl.BlockSpec(memory_space=pltpu.VMEM)


def pair_index(left_axis, right_axis):
    return stress_pairs.index((min(left_axis, right_axis), max(left_axis, right_axis)))


def lanes_of(shape):
    return lax.broadcasted_iota(jnp.int32, shape, len(shape) - 1)


slot_rows = 8
item_count = 7
line_rows = 8


def limit(mebibytes):
    return pltpu.CompilerParams(vmem_limit_bytes=mebibytes * 1024 * 1024)


def far(value):
    return pltpu.with_memory_space_constraint(value, pltpu.HBM)


def place_of():
    return lax.axis_index("macro"), lax.axis_index("micro")


def rolled(value, amount):
    size = value.shape[-1]
    if isinstance(amount, int):
        return pltpu.roll(value, amount % size, value.ndim - 1)
    return pltpu.roll(value, lax.rem(amount + 2 * size, size), value.ndim - 1)


def gather_kernel(
    capacity, size_x, size_y, size_z, macro_count, cell_in, owner_in, velocity_in, viscosity_in,
    chunk_ref, position_ref, viscous_ref, y_low_ref, y_high_ref,
    cell_ref, owner_ref, velocity_ref, viscosity_ref, masked, gradients, target, count, sems,
):
    flags = cell_ref.shape[0]
    copies = [
        pltpu.make_async_copy(source, into, sems.at[number])
        for number, (source, into) in enumerate(
            (
                (cell_in, cell_ref), (owner_in, owner_ref), (velocity_in, velocity_ref),
                (viscosity_in, viscosity_ref),
            )
        )
    ]
    for copy in copies:
        copy.start()
    chunk_rows = slot_rows + item_count * size_y
    macro, core = place_of()
    lane = lanes_of((1, size_z))

    for owner in range(count.shape[0]):
        count[owner] = 0
        chunk_ref[owner * chunk_rows : owner * chunk_rows + slot_rows, :] = jnp.zeros((slot_rows, 128), jnp.float32)
    for copy in copies[:2]:
        copy.wait()
    for j in range(flags):
        owner = owner_ref[j]
        rank = count[owner]
        count[owner] = rank + 1
        target[j] = owner * chunk_rows + rank
        position_ref[j] = owner * (slot_rows + line_rows) + rank
    for copy in copies[2:]:
        copy.wait()
    for j in range(flags):
        cell = cell_ref[j]
        row = lax.div(cell, size_z)
        z = cell - row * size_z
        here = (lane == z).astype(jnp.float32)
        along_z = (lane == z + 1).astype(jnp.float32) - (lane == z - 1).astype(jnp.float32)
        for a in range(3):
            along_x = velocity_ref[a, pl.ds(row + size_y, 1), :] - velocity_ref[a, pl.ds(row - size_y, 1), :]
            along_y = velocity_ref[a, pl.ds(row + 1, 1), :] - velocity_ref[a, pl.ds(row - 1, 1), :]
            masked[3 * a, j : j + 1, :] = along_x * here
            masked[3 * a + 1, j : j + 1, :] = along_y * here
            masked[3 * a + 2, j : j + 1, :] = velocity_ref[a, pl.ds(row, 1), :] * along_z
        masked[9, j : j + 1, :] = viscosity_ref[pl.ds(row, 1), :] * here

    for side, ref in enumerate((y_low_ref, y_high_ref)):
        for layer in range(2):
            y = layer if side == 0 else size_y - 1 - layer
            for a in range(3):
                ref[3 * layer + a] = velocity_ref[a, pl.ds(y, size_x, stride=size_y), :]
        y = 0 if side == 0 else size_y - 1
        ref[6] = viscosity_ref[pl.ds(y, size_x, stride=size_y), :]

    for side in range(2):
        beside = macro - 1 if side == 0 else macro + 1

        @pl.when(beside >= 0 if side == 0 else beside < macro_count)
        def _(side=side, beside=beside):
            first = pl.multiple_of((2 * beside + core) * chunk_rows + slot_rows, 8)
            other = pl.multiple_of((2 * beside + 1 - core) * chunk_rows + slot_rows, 8)
            for layer in range(2):
                x = layer if side == 0 else size_x - 1 - layer
                for a in range(3):
                    chunk_ref[pl.ds(first + (3 * layer + a) * size_y, size_y), :] = velocity_ref[
                        a, x * size_y : (x + 1) * size_y, :
                    ]
            x = 0 if side == 0 else size_x - 1
            chunk_ref[pl.ds(first + 6 * size_y, size_y), :] = viscosity_ref[x * size_y : (x + 1) * size_y, :]
            for number, a in enumerate((0, 2)):
                chunk_ref[pl.ds(other + number * size_y, size_y), :] = velocity_ref[
                    a, x * size_y : (x + 1) * size_y, :
                ]

    group = size_z // 8
    lane2 = lanes_of((size_y, size_z))
    first = pl.multiple_of((2 * macro + 1 - core) * chunk_rows + slot_rows, 8)
    source = jnp.where(core == 0, size_z - 2, 0)
    for block in range(-(-size_x // group)):
        total = jnp.zeros((size_y, size_z), jnp.float32)
        for x in range(block * group, min(size_x, (block + 1) * group)):
            rows = slice(x * size_y, (x + 1) * size_y)
            for a in range(4):
                at = 8 * (x - block * group) + 2 * a
                value = viscosity_ref[rows, :] if a == 3 else velocity_ref[a, rows, :]
                total = jnp.where((lane2 == at) | (lane2 == at + 1), rolled(value, at - source), total)
        chunk_ref[pl.ds(first + block * size_y, size_y), :] = total

    columns = [0.5 * jnp.sum(masked[c], axis=1, keepdims=True) for c in range(9)]
    viscous = jnp.sum(masked[9], axis=1, keepdims=True)
    wide = lanes_of((flags, 128))
    packed = jnp.zeros((flags, 128), jnp.float32)
    for c in range(9):
        packed = jnp.where(wide == c, columns[c], packed)
    gradients[...] = packed
    stress = jnp.zeros((flags, 128), jnp.float32)
    for k, (a, b) in enumerate(stress_pairs):
        stress = jnp.where(wide == k, viscous * (columns[3 * a + b] + columns[3 * b + a]), stress)
    viscous_ref[...] = stress

    for j in range(flags):
        chunk_ref[pl.ds(target[j], 1), :] = gradients[j : j + 1, :]


def gather_rows(flag_cell, owner, velocity, viscosity, capacity, owner_count):
    size_x, size_y, size_z = viscosity.shape
    flags = flag_cell.shape[0]
    chunk_rows = slot_rows + item_count * size_y
    face = jax.ShapeDtypeStruct((item_count, size_x, size_z), jnp.float32)
    return pl.pallas_call(
        functools.partial(gather_kernel, capacity, size_x, size_y, size_z, owner_count // 2),
        out_shape=(
            jax.ShapeDtypeStruct((owner_count * chunk_rows, 128), jnp.float32),
            jax.ShapeDtypeStruct((flags,), jnp.int32),
            jax.ShapeDtypeStruct((flags, 128), jnp.float32),
            face,
            face,
        ),
        in_specs=[pl.BlockSpec(memory_space=pltpu.HBM)] * 4,
        out_specs=(VMEM, SMEM, VMEM, VMEM, VMEM),
        scratch_shapes=[
            pltpu.SMEM((flags,), jnp.int32),
            pltpu.SMEM((flags,), jnp.int32),
            pltpu.VMEM((3, size_x * size_y, size_z), jnp.float32),
            pltpu.VMEM((size_x * size_y, size_z), jnp.float32),
            pltpu.VMEM((10, flags, size_z), jnp.float32),
            pltpu.VMEM((flags, 128), jnp.float32),
            pltpu.SMEM((flags,), jnp.int32),
            pltpu.SMEM((owner_count,), jnp.int32),
            pltpu.SemaphoreType.DMA((4,)),
        ],
        compiler_params=limit(8),
        cost_estimate=pl.CostEstimate(flops=400000, bytes_accessed=3000000, transcendentals=0),
        name="gather_rows",
    )(
        far(flag_cell),
        far(owner),
        far(velocity.reshape(3, size_x * size_y, size_z)),
        far(viscosity.reshape(size_x * size_y, size_z)),
    )


def micro_kernel(
    capacity, parts, rows, groups, conform_ref, noise_ref, rate_ref,
    next_ref, chunk_ref, conform, noise, rate, rate_wide, sums_ref, read_sem, noise_sem,
):
    steps, _, slots, dumbbells = noise_ref.shape
    blocks = slots // rows
    span = steps // groups
    width = dumbbells // parts
    owners = slots // capacity
    scale = 1.0 / noise_weight
    extent = fene_extent * scale * scale

    def block_rows(block):
        return pl.ds(pl.multiple_of(block * rows, rows), rows)

    def read(block):
        at = block_rows(block)
        return pltpu.make_async_copy(conform_ref.at[:, at, :], conform.at[:, at, :], read_sem.at[block])

    def read_noise(block, group):
        at, when = block_rows(block), pl.ds(group * span, span)
        return pltpu.make_async_copy(
            noise_ref.at[when, :, at, :], noise.at[when, :, at, :], noise_sem.at[block, group]
        )

    for block in range(blocks):
        read(block).start()
        for group in range(groups):
            read_noise(block, group).start()
    for owner in range(owners):
        rate[owner * capacity : (owner + 1) * capacity, :] = rate_ref[owner, 0:capacity, :]
        chunk_ref[owner] = jnp.zeros(chunk_ref.shape[1:], jnp.float32)
    for a in range(3):
        for b in range(3):
            column = micro_step * rate[:, 3 * a + b : 3 * a + b + 1] + (1.0 if a == b else 0.0)
            rate_wide[3 * a + b] = jnp.broadcast_to(column, (slots, width))

    def inverses(state):
        rooms = []
        for part in range(parts):
            q = state[3 * part : 3 * part + 3]
            room = (extent - q[0] * q[0]) - (q[1] * q[1] + q[2] * q[2])
            rooms.append(jnp.maximum(room, extent * spring_floor))
        result = []
        for part in range(0, parts, 2):
            both = pl.reciprocal(rooms[part] * rooms[part + 1], approx=True)
            result += [both * rooms[part + 1], both * rooms[part]]
        return result

    def advance_block(block, carry):
        at = block_rows(block)
        rates = [[rate_wide.at[3 * a + b, at, :] for b in range(3)] for a in range(3)]

        def substep(step, state):
            updated = []
            inverse = inverses(state)
            for part in range(parts):
                q = state[3 * part : 3 * part + 3]
                spring = (micro_step * relax_rate * extent) * inverse[part]
                for a in range(3):
                    b, c = [other for other in range(3) if other != a]
                    kick = noise[step, a, at, part * width : (part + 1) * width].astype(jnp.float32)
                    rest = (rates[a][b][...] * q[b] + rates[a][c][...] * q[c]) + kick
                    updated.append((rates[a][a][...] - spring) * q[a] + rest)
            return tuple(updated)

        def advance_group(group, state):
            read_noise(block, group).wait()
            for step in range(span):
                state = substep(group * span + step, state)
            return state

        read(block).wait()
        state = tuple(
            conform[a, at, part * width : (part + 1) * width] * scale
            for part in range(parts)
            for a in range(3)
        )
        state = lax.fori_loop(0, groups, advance_group, state, unroll=True)
        sums = [None] * 6
        inverse = inverses(state)
        for part in range(parts):
            q = state[3 * part : 3 * part + 3]
            for a in range(3):
                next_ref[a, at, part * width : (part + 1) * width] = q[a] * noise_weight
            for k, (a, b) in enumerate(stress_pairs):
                term = (inverse[part] * q[a]) * q[b]
                sums[k] = term if sums[k] is None else sums[k] + term
        for k in range(6):
            sums_ref[k, at, :] = sums[k]
        return carry

    lax.fori_loop(0, blocks, advance_block, 0)
    lane = lanes_of((slots, 128))
    packed = jnp.zeros((slots, 128), jnp.float32)
    weight = extent * noise_weight * noise_weight / dumbbells
    for k, (a, b) in enumerate(stress_pairs):
        mean = jnp.sum(sums_ref[k], axis=1, keepdims=True) * weight
        packed = jnp.where(lane == k, polymer_weight * (mean - (1.0 if a == b else 0.0)), packed)
    for owner in range(owners):
        chunk_ref[owner, 0:capacity, :] = packed[owner * capacity : (owner + 1) * capacity]


def advance(conformations, increments, chunks, capacity):
    slots, dumbbells = conformations.shape[1:]
    steps = increments.shape[0]
    owners = slots // capacity
    rows, parts, groups = 16, 4, 4
    blocks = slots // rows
    whole = pl.BlockSpec(memory_space=pltpu.HBM)
    return pl.pallas_call(
        functools.partial(micro_kernel, capacity, parts, rows, groups),
        out_shape=(
            pltpu.VMEM(conformations.shape, jnp.float32),
            jax.ShapeDtypeStruct((owners, slot_rows + line_rows, 128), jnp.float32),
        ),
        in_specs=[whole, whole, VMEM],
        out_specs=(VMEM, VMEM),
        scratch_shapes=[
            pltpu.VMEM(conformations.shape, jnp.float32),
            pltpu.VMEM(increments.shape, jnp.bfloat16),
            pltpu.VMEM((slots, 128), jnp.float32),
            pltpu.VMEM((9, slots, dumbbells // parts), jnp.float32),
            pltpu.VMEM((6, slots, dumbbells // parts), jnp.float32),
            pltpu.SemaphoreType.DMA((blocks,)),
            pltpu.SemaphoreType.DMA((blocks, groups)),
        ],
        compiler_params=limit(12),
        cost_estimate=pl.CostEstimate(flops=20000000, bytes_accessed=5000000, transcendentals=600000),
        name="advance",
    )(far(conformations), far(increments), chunks)


def lines_kernel(macro_count, chunk_ref, y_low_ref, y_high_ref, out_ref):
    out_ref[...] = chunk_ref[...]
    macro, core = place_of()
    size_x, size_z = y_low_ref.shape[1:]
    sides = (y_low_ref, y_high_ref)
    for side in range(2):
        beside = macro - 1 if side == 0 else macro + 1

        @pl.when(beside >= 0 if side == 0 else beside < macro_count)
        def _(side=side, beside=beside):
            x = 0 if side == 0 else size_x - 1
            for u in range(2):
                for a in range(2):
                    at = slot_rows + 2 * u + a
                    out_ref[2 * beside + core, at : at + 1, :] = sides[u][a, x : x + 1, :]

    lane = lanes_of((8, size_z))
    source = jnp.where(core == 0, size_z - 1, 0)
    total = jnp.zeros((8, size_z), jnp.float32)
    for i in range(size_x // 8):
        for u in range(2):
            for a in range(2):
                at = 4 * i + 2 * u + a
                total = jnp.where(
                    lane == at, rolled(sides[u][1 + a, 8 * i : 8 * i + 8, :], at - source), total
                )
    out_ref[2 * macro + 1 - core, slot_rows:, :] = total


def add_lines(chunks, y_low, y_high):
    return pl.pallas_call(
        functools.partial(lines_kernel, chunks.shape[0] // 2),
        out_shape=jax.ShapeDtypeStruct(chunks.shape, jnp.float32),
        in_specs=[VMEM, VMEM, VMEM],
        out_specs=VMEM,
        compiler_params=limit(4),
        cost_estimate=pl.CostEstimate(flops=20000, bytes_accessed=400000, transcendentals=0),
        name="add_lines",
    )(chunks, y_low, y_high)


product_depth = 128


def one_hots(size_y, size_z, cell_ref, position_ref, lines_ref, pick_ref, spread_ref, rows):
    flags = cell_ref.shape[0]
    weight = 0.5 * macro_step
    row_count = spread_ref.shape[0]
    back_rows = pick_ref.shape[1] // 3
    lane = lanes_of((1, size_z))
    row_lane = lanes_of((1, rows.shape[1]))
    slot_lane = lanes_of((flags, back_rows))
    flag_row = lax.broadcasted_iota(jnp.int32, (flags, back_rows), 0)
    rows[3 * flags :, :] = jnp.zeros((product_depth - 3 * flags, rows.shape[1]), jnp.float32)
    slot = jnp.zeros((flags, back_rows), jnp.int32)
    for j in range(flags):
        cell = cell_ref[j]
        row = lax.div(cell, size_z)
        z = cell - row * size_z
        lines_ref[0, j : j + 1, :] = jnp.where(lane == z, weight, 0.0)
        lines_ref[1, j : j + 1, :] = jnp.where(
            lane == z - 1, weight, jnp.where(lane == z + 1, -weight, 0.0)
        )
        for number, shift in enumerate((size_y, 1)):
            rows[number * flags + j : number * flags + j + 1, :] = jnp.where(
                row_lane == row - shift, 1.0, jnp.where(row_lane == row + shift, -1.0, 0.0)
            )
        rows[2 * flags + j : 2 * flags + j + 1, :] = jnp.where(row_lane == row, 1.0, 0.0)
        slot = jnp.where(flag_row == j, position_ref[j], slot)
    spread = rows[...].T[:row_count].astype(jnp.bfloat16)
    pick = jnp.where(slot_lane == slot, 1.0, 0.0).astype(jnp.bfloat16)
    for piece in range(3):
        spread_ref[:, piece * product_depth : (piece + 1) * product_depth] = spread
        pick_ref[:, piece * back_rows : (piece + 1) * back_rows] = pick


def flow_kernel(
    size_x, size_y, size_z, macro_count, cell_ref, position_ref, velocity_ref, viscosity_ref, chunk_ref,
    y_low_ref, y_high_ref, out_ref, corner_ref, edge_ref, lines_ref, pick_ref, spread_ref,
    padded, stress_x, stress_rest, faces, ghost_y, ghost_z, rows,
):
    macro, core = place_of()
    one_hots(size_y, size_z, cell_ref, position_ref, lines_ref, pick_ref, spread_ref, rows)
    inside = (macro > 0, macro < macro_count - 1)
    sign_z = jnp.where(core == 0, 1.0, -1.0)
    end = jnp.where(core == 0, size_z - 1, 0)
    shape = (size_y, size_z)
    lane, row = lanes_of(shape), lax.broadcasted_iota(jnp.int32, shape, 0)
    at_end = jnp.where(lane == end, sign_z, 0.0)

    def kept(value, condition):
        return jnp.where(condition, value, 0.0)

    def plane(x):
        return pl.ds(pl.multiple_of(x * size_y, 8), size_y)

    def difference_z(value):
        lane = lanes_of(value.shape)
        return jnp.where(lane == size_z - 1, 0.0, rolled(value, -1)) - jnp.where(
            lane == 0, 0.0, rolled(value, 1)
        )

    def difference_rows(value, low=0.0, high=0.0):
        count = value.shape[0]
        row = lax.broadcasted_iota(jnp.int32, value.shape, 0)
        return jnp.where(row == count - 1, high, pltpu.roll(value, count - 1, 0)) - jnp.where(
            row == 0, low, pltpu.roll(value, 1, 0)
        )

    x_faces, x_others = [], []
    for s in range(2):
        beside = jnp.maximum(macro - 1, 0) if s == 0 else jnp.minimum(macro + 1, macro_count - 1)
        x_faces.append(
            [
                kept(chunk_ref[2 * beside + core, slot_rows + i * size_y : slot_rows + (i + 1) * size_y, :], inside[s])
                for i in range(item_count)
            ]
        )
        x_others.append(
            [
                kept(
                    rolled(
                        chunk_ref[
                            2 * beside + 1 - core, slot_rows + i * size_y : slot_rows + (i + 1) * size_y, :
                        ],
                        2 * end + 1,
                    ),
                    inside[s],
                )
                for i in range(2)
            ]
        )

    group = size_z // 8
    packed = [
        chunk_ref[2 * macro + 1 - core, slot_rows + i * size_y : slot_rows + (i + 1) * size_y, :]
        for i in range(-(-size_x // group))
    ]
    for i, value in enumerate(packed):

        def unpack(x, carry):
            for q in range(item_count):
                a, layer = (q, 0) if q < 4 else (q - 4, 1)
                at = 8 * (x - i * group) + 2 * a + (core if layer == 0 else 1 - core)
                faces[q, x + 1] = rolled(value, end - at)
            return carry

        lax.fori_loop(i * group, min(size_x, (i + 1) * group), unpack, 0, unroll=8)
    faces[2, 0] = x_others[0][1]
    faces[2, size_x + 1] = x_others[1][1]

    for a in range(3):
        padded[a, 0] = x_faces[0][a]
        padded[a, size_x + 1] = x_faces[1][a]

    def fill(x, carry):
        for a in range(3):
            padded[a, x + 1] = velocity_ref[a, plane(x), :]
        return carry

    lax.fori_loop(0, size_x, fill, 0, unroll=True)

    rest = {(1, 1): 0, (2, 2): 1, (1, 2): 2}

    def stress_plane(x, carry):
        along_x, along_y, along_z, centre = [], [], [], []
        for a in range(3):
            value = padded[a, x + 1]
            centre.append(value)
            along_x.append(padded[a, x + 2] - padded[a, x])
            along_y.append(
                difference_rows(value, y_low_ref[a, pl.ds(x, 1), :], y_high_ref[a, pl.ds(x, 1), :])
            )
            along_z.append(difference_z(value) + faces[a, x + 1] * at_end)
        slopes = (along_x, along_y, along_z)
        half = 0.5 * viscosity_ref[plane(x), :]
        for a, b in stress_pairs:
            value = half * (slopes[b][a] + slopes[a][b])
            if a == 0:
                stress_x[b, x + 1] = value
            else:
                stress_rest[rest[a, b], x] = value
        weight = (0.5 * faces[3, x + 1]) * at_end
        normal = [(faces[4 + a, x + 1] - centre[a]) * sign_z for a in range(3)]
        ghost_z[0, x] = weight * (normal[0] + (faces[2, x + 2] - faces[2, x]))
        ghost_z[1, x] = weight * (normal[1] + difference_rows(faces[2, x + 1]))
        ghost_z[2, x] = weight * (2.0 * normal[2])
        return carry

    lax.fori_loop(0, size_x, stress_plane, 0, unroll=6)

    for s in range(2):
        near, far, weight = x_faces[s][0:3], x_faces[s][3:6], 0.5 * x_faces[s][6]
        sign = -1.0 if s == 0 else 1.0
        normal = [(far[a] - padded[a, 1 if s == 0 else size_x]) * sign for a in range(3)]
        slope_y = difference_rows(near[0])
        slope_z = difference_z(near[0]) + x_others[s][0] * at_end
        at = 0 if s == 0 else size_x + 1
        stress_x[0, at] = weight * (2.0 * normal[0])
        stress_x[1, at] = weight * (normal[1] + slope_y)
        stress_x[2, at] = weight * (normal[2] + slope_z)
        for u in range(2):
            y, sign_y = (0, -1.0) if u == 0 else (size_y - 1, 1.0)
            number = 4 * s + 2 * u
            corner_ref[number : number + 1, :] = (0.5 * macro_step * sign * sign_y) * weight[y : y + 1, :]

    for u, ref in enumerate((y_low_ref, y_high_ref)):
        y, sign = (0, -1.0) if u == 0 else (size_y - 1, 1.0)
        weight = 0.5 * ref[6]
        normal = [
            (ref[3 + a] - velocity_ref[a, pl.ds(y, size_x, stride=size_y), :]) * sign for a in range(3)
        ]
        ghost_y[3 * u] = weight * (normal[0] + difference_rows(ref[1]))
        ghost_y[3 * u + 1] = weight * (2.0 * normal[1])
        ghost_y[3 * u + 2] = weight * (normal[2] + difference_z(ref[1]))
        for s in range(2):
            x, sign_x = (0, -1.0) if s == 0 else (size_x - 1, 1.0)
            number = 4 * s + 2 * u + 1
            corner_ref[number : number + 1, :] = (0.5 * macro_step * sign * sign_x) * weight[x : x + 1, :]
        wide = lanes_of((size_x, size_z))
        scale = jnp.where(wide == end, (0.5 * macro_step * sign) * sign_z, 0.0)
        edge_ref[2 * u] = scale * weight
        for x in range(size_x):
            edge_ref[2 * u + 1, x : x + 1, :] = scale[x : x + 1, :] * (0.5 * faces[3, x + 1, y : y + 1, :])

    columns = {(0, 1): (stress_x, 1, 1), (1, 1): (stress_rest, 0, 0), (2, 1): (stress_rest, 2, 0)}
    columns_z = {0: (stress_x, 2, 1), 1: (stress_rest, 2, 0), 2: (stress_rest, 1, 0)}

    def step_plane(x, carry):
        for a in range(3):
            total = stress_x[a, x + 2] - stress_x[a, x]
            ref, number, shift = columns[a, 1]
            total = total + difference_rows(
                ref[number, x + shift], ghost_y[a, pl.ds(x, 1), :], ghost_y[3 + a, pl.ds(x, 1), :]
            )
            ref, number, shift = columns_z[a]
            total = total + (difference_z(ref[number, x + shift]) + ghost_z[a, x])
            out_ref[a, plane(x), :] = padded[a, x + 1] + (0.5 * macro_step) * total
        return carry

    lax.fori_loop(0, size_x, step_plane, 0, unroll=6)


def flow_step(flag_cell, position, velocity, viscosity, chunks, y_low, y_high):
    size_x, size_y, size_z = viscosity.shape
    flags = flag_cell.shape[0]
    back_rows = chunks.shape[0] * (slot_rows + line_rows)
    row_count = size_x * size_y
    planes = (size_x, size_y, size_z)
    wide = (size_x + 2, size_y, size_z)
    return pl.pallas_call(
        functools.partial(flow_kernel, size_x, size_y, size_z, chunks.shape[0] // 2),
        out_shape=(
            jax.ShapeDtypeStruct((3, size_x * size_y, size_z), jnp.float32),
            jax.ShapeDtypeStruct((8, size_z), jnp.float32),
            jax.ShapeDtypeStruct((4, size_x, size_z), jnp.float32),
            jax.ShapeDtypeStruct((2, flags, size_z), jnp.float32),
            jax.ShapeDtypeStruct((flags, 3 * back_rows), jnp.bfloat16),
            jax.ShapeDtypeStruct((row_count, 3 * product_depth), jnp.bfloat16),
        ),
        in_specs=[SMEM] * 2 + [VMEM] * 5,
        out_specs=(VMEM,) * 6,
        scratch_shapes=[
            pltpu.VMEM((3, *wide), jnp.float32),
            pltpu.VMEM((3, *wide), jnp.float32),
            pltpu.VMEM((3, *planes), jnp.float32),
            pltpu.VMEM((item_count, *wide), jnp.float32),
            pltpu.VMEM((6, size_x, size_z), jnp.float32),
            pltpu.VMEM((3, *planes), jnp.float32),
            pltpu.VMEM((product_depth, -(-row_count // 128) * 128), jnp.float32),
        ],
        compiler_params=limit(12),
        cost_estimate=pl.CostEstimate(flops=4000000, bytes_accessed=3000000, transcendentals=0),
        name="flow_step",
    )(
        flag_cell, position,
        velocity.reshape(3, size_x * size_y, size_z),
        viscosity.reshape(size_x * size_y, size_z),
        chunks, y_low, y_high,
    )


def pieces(value):
    high = value.astype(jnp.bfloat16)
    rest = value - high.astype(jnp.float32)
    middle = rest.astype(jnp.bfloat16)
    return high, middle, (rest - middle.astype(jnp.float32)).astype(jnp.bfloat16)


def polymer_kernel(
    size_x, size_y, size_z, macro_count, chunk_ref, viscous_ref, corner_ref, edge_ref, lines_ref, pick_ref,
    spread_ref, partial_ref, out_ref, flag_ref, field, write_sem,
):
    flags = viscous_ref.shape[0]
    chunk_rows = slot_rows + line_rows
    macro, core = place_of()
    values = jnp.dot(
        pick_ref[...], jnp.concatenate(pieces(chunk_ref[...]), axis=0), preferred_element_type=jnp.float32
    )
    here, beside_z = lines_ref[0], lines_ref[1]
    columns = [jnp.broadcast_to(values[:, k : k + 1], (flags, size_z)) for k in range(6)]
    unused = jnp.zeros((product_depth - 3 * flags, size_z), jnp.float32)
    split = [
        pieces(
            jnp.concatenate(
                [
                    columns[pair_index(a, 0)] * here, columns[pair_index(a, 1)] * here,
                    columns[pair_index(a, 2)] * beside_z, unused,
                ],
                axis=0,
            )
        )
        for a in range(3)
    ]
    flag_ref[...] = (viscous_ref[...] + values).T[0:6, :]

    field[...] = partial_ref[...]
    for s in range(2):
        inside = macro > 0 if s == 0 else macro < macro_count - 1
        beside = jnp.maximum(macro - 1, 0) if s == 0 else jnp.minimum(macro + 1, macro_count - 1)
        start = (2 * beside + core) * chunk_rows + slot_rows
        x = 0 if s == 0 else size_x - 1
        for u in range(2):
            at = x * size_y + (0 if u == 0 else size_y - 1)
            for a in range(2):
                number = 4 * s + 2 * u + a
                line = corner_ref[number : number + 1, :] * chunk_ref[pl.ds(start + 2 * u + a, 1), :]
                field[1 - a, at : at + 1, :] += jnp.where(inside, line, 0.0)
    start = pl.multiple_of((2 * macro + 1 - core) * chunk_rows + slot_rows, 8)
    packed = chunk_ref[pl.ds(start, line_rows), :]
    end = jnp.where(core == 0, size_z - 1, 0)
    for u in range(2):
        y = 0 if u == 0 else size_y - 1
        for a in range(2):
            for i in range(size_x // 8):
                line = rolled(packed, end - (4 * i + 2 * u + a)) * edge_ref[2 * u + a, 8 * i : 8 * i + 8, :]
                at = pl.ds(8 * i * size_y + y, 8, stride=size_y)
                field[2 - a, at, :] += line
    copies = [pltpu.make_async_copy(field.at[a], out_ref.at[a], write_sem.at[a]) for a in range(3)]
    for a in range(3):
        field[a] += jnp.dot(
            spread_ref[...], jnp.concatenate(split[a], axis=0), preferred_element_type=jnp.float32
        )
        copies[a].start()
    for copy in copies:
        copy.wait()


def add_polymer(chunks, viscous, corners, edges, lines, pick, spread, partial, shape):
    flags = viscous.shape[0]
    size_x, size_y, size_z = shape
    return pl.pallas_call(
        functools.partial(polymer_kernel, size_x, size_y, size_z, chunks.shape[0] // 2),
        out_shape=(
            jax.ShapeDtypeStruct(partial.shape, jnp.float32),
            jax.ShapeDtypeStruct((6, flags), jnp.float32),
        ),
        in_specs=[VMEM] * 8,
        out_specs=(pl.BlockSpec(memory_space=pltpu.HBM), VMEM),
        scratch_shapes=[pltpu.VMEM(partial.shape, jnp.float32), pltpu.SemaphoreType.DMA((3,))],
        compiler_params=limit(8),
        cost_estimate=pl.CostEstimate(flops=400000, bytes_accessed=3000000, transcendentals=0),
        name="add_polymer",
    )(chunks.reshape(-1, 128), viscous, corners, edges, lines, pick, spread, partial)


def shards(velocity, viscosity, flag_cell, flag_owner, conformations, increments):
    macro_count = lax.axis_size("macro")
    tile_count = lax.axis_size("tile")
    assert lax.axis_size("micro") == 2
    owner_count = 2 * macro_count
    capacity = conformations.shape[1] // owner_count
    size_x, size_y, size_z = viscosity.shape
    assert capacity <= slot_rows and size_y == 8 and size_z == 128 and size_x % 8 == 0 and size_x <= 48
    chunks, position, viscous, y_first, y_last = gather_rows(
        flag_cell, flag_owner.reshape(-1), velocity, viscosity, capacity, owner_count
    )

    def exchange(rows):
        return lax.all_to_all(rows, ("macro", "micro"), split_axis=0, concat_axis=0, tiled=True)

    received = exchange(chunks.reshape(owner_count, -1, 128))
    up = [(i, i + 1) for i in range(tile_count - 1)]
    down = [(target, source) for source, target in up]
    y_low = lax.ppermute(y_last, "tile", up)
    y_high = lax.ppermute(y_first, "tile", down)
    last_state, polymer = advance(conformations, increments, received, capacity)
    returned = exchange(add_lines(polymer, y_low, y_high))
    partial, corners, edges, lines, pick, spread = flow_step(
        flag_cell, position, velocity, viscosity, received, y_low, y_high
    )
    velocity_next, flag_stress = add_polymer(
        returned, viscous, corners, edges, lines, pick, spread, partial, viscosity.shape
    )
    return (velocity_next.reshape(velocity.shape), last_state, flag_stress)


def solution(mesh):
    in_specs = (
        P(None, "macro", "tile", "micro"),
        P("macro", "tile", "micro"),
        P(("macro", "tile", "micro")),
        P(("macro", "tile", "micro"), None),
        P(None, ("macro", "tile", "micro"), None),
        P(None, None, ("macro", "tile", "micro"), None),
    )
    out_specs = (
        P(None, "macro", "tile", "micro"),
        P(None, ("macro", "tile", "micro"), None),
        P(None, ("macro", "tile", "micro")),
    )
    return jax.shard_map(shards, mesh=mesh, in_specs=in_specs, out_specs=out_specs, check_vma=False)
```

```python
import functools

import jax
import jax.numpy as jnp
from jax import lax
from jax.experimental import pallas as pl
from jax.experimental.pallas import tpu as pltpu
from jax.sharding import PartitionSpec as P

stress_pairs = ((0, 0), (1, 1), (2, 2), (0, 1), (0, 2), (1, 2))
macro_step = 0.1
micro_step = 0.01
noise_weight = 0.1
relax_rate = 0.5
fene_extent = 30.0
spring_floor = 0.1
polymer_weight = 0.25

SMEM = pl.BlockSpec(memory_space=pltpu.SMEM)
VMEM = pl.BlockSpec(memory_space=pltpu.VMEM)


def pair_index(left_axis, right_axis):
    return stress_pairs.index((min(left_axis, right_axis), max(left_axis, right_axis)))


def lanes_of(shape):
    return lax.broadcasted_iota(jnp.int32, shape, len(shape) - 1)


slot_rows = 8
item_count = 7
line_rows = 8


def limit(mebibytes):
    return pltpu.CompilerParams(vmem_limit_bytes=mebibytes * 1024 * 1024)


def far(value):
    return pltpu.with_memory_space_constraint(value, pltpu.HBM)


def place_of():
    return lax.axis_index("macro"), lax.axis_index("micro")


def rolled(value, amount):
    size = value.shape[-1]
    if isinstance(amount, int):
        return pltpu.roll(value, amount % size, value.ndim - 1)
    return pltpu.roll(value, lax.rem(amount + 2 * size, size), value.ndim - 1)


def gather_kernel(
    capacity, size_x, size_y, size_z, macro_count, cell_in, owner_in, velocity_in, viscosity_in,
    chunk_ref, position_ref, viscous_ref, y_low_ref, y_high_ref,
    cell_ref, owner_ref, velocity_ref, viscosity_ref, masked, gradients, target, count, sems,
):
    flags = cell_ref.shape[0]
    copies = [
        pltpu.make_async_copy(source, into, sems.at[number])
        for number, (source, into) in enumerate(
            (
                (cell_in, cell_ref), (owner_in, owner_ref), (velocity_in, velocity_ref),
                (viscosity_in, viscosity_ref),
            )
        )
    ]
    for copy in copies:
        copy.start()
    chunk_rows = slot_rows + item_count * size_y
    macro, core = place_of()
    lane = lanes_of((1, size_z))

    for owner in range(count.shape[0]):
        count[owner] = 0
        chunk_ref[owner * chunk_rows : owner * chunk_rows + slot_rows, :] = jnp.zeros((slot_rows, 128), jnp.float32)
    for copy in copies[:2]:
        copy.wait()
    for j in range(flags):
        owner = owner_ref[j]
        rank = count[owner]
        count[owner] = rank + 1
        target[j] = owner * chunk_rows + rank
        position_ref[j] = owner * (slot_rows + line_rows) + rank
    for copy in copies[2:]:
        copy.wait()
    for j in range(flags):
        cell = cell_ref[j]
        row = lax.div(cell, size_z)
        z = cell - row * size_z
        here = (lane == z).astype(jnp.float32)
        along_z = (lane == z + 1).astype(jnp.float32) - (lane == z - 1).astype(jnp.float32)
        for a in range(3):
            along_x = velocity_ref[a, pl.ds(row + size_y, 1), :] - velocity_ref[a, pl.ds(row - size_y, 1), :]
            along_y = velocity_ref[a, pl.ds(row + 1, 1), :] - velocity_ref[a, pl.ds(row - 1, 1), :]
            masked[3 * a, j : j + 1, :] = along_x * here
            masked[3 * a + 1, j : j + 1, :] = along_y * here
            masked[3 * a + 2, j : j + 1, :] = velocity_ref[a, pl.ds(row, 1), :] * along_z
        masked[9, j : j + 1, :] = viscosity_ref[pl.ds(row, 1), :] * here

    for side, ref in enumerate((y_low_ref, y_high_ref)):
        for layer in range(2):
            y = layer if side == 0 else size_y - 1 - layer
            for a in range(3):
                ref[3 * layer + a] = velocity_ref[a, pl.ds(y, size_x, stride=size_y), :]
        y = 0 if side == 0 else size_y - 1
        ref[6] = viscosity_ref[pl.ds(y, size_x, stride=size_y), :]

    for side in range(2):
        beside = macro - 1 if side == 0 else macro + 1

        @pl.when(beside >= 0 if side == 0 else beside < macro_count)
        def _(side=side, beside=beside):
            first = pl.multiple_of((2 * beside + core) * chunk_rows + slot_rows, 8)
            other = pl.multiple_of((2 * beside + 1 - core) * chunk_rows + slot_rows, 8)
            for layer in range(2):
                x = layer if side == 0 else size_x - 1 - layer
                for a in range(3):
                    chunk_ref[pl.ds(first + (3 * layer + a) * size_y, size_y), :] = velocity_ref[
                        a, x * size_y : (x + 1) * size_y, :
                    ]
            x = 0 if side == 0 else size_x - 1
            chunk_ref[pl.ds(first + 6 * size_y, size_y), :] = viscosity_ref[x * size_y : (x + 1) * size_y, :]
            for number, a in enumerate((0, 2)):
                chunk_ref[pl.ds(other + number * size_y, size_y), :] = velocity_ref[
                    a, x * size_y : (x + 1) * size_y, :
                ]

    group = size_z // 8
    lane2 = lanes_of((size_y, size_z))
    first = pl.multiple_of((2 * macro + 1 - core) * chunk_rows + slot_rows, 8)
    source = jnp.where(core == 0, size_z - 2, 0)
    for block in range(-(-size_x // group)):
        total = jnp.zeros((size_y, size_z), jnp.float32)
        for x in range(block * group, min(size_x, (block + 1) * group)):
            rows = slice(x * size_y, (x + 1) * size_y)
            for a in range(4):
                at = 8 * (x - block * group) + 2 * a
                value = viscosity_ref[rows, :] if a == 3 else velocity_ref[a, rows, :]
                total = jnp.where((lane2 == at) | (lane2 == at + 1), rolled(value, at - source), total)
        chunk_ref[pl.ds(first + block * size_y, size_y), :] = total

    columns = [0.5 * jnp.sum(masked[c], axis=1, keepdims=True) for c in range(9)]
    viscous = jnp.sum(masked[9], axis=1, keepdims=True)
    wide = lanes_of((flags, 128))
    packed = jnp.zeros((flags, 128), jnp.float32)
    for c in range(9):
        packed = jnp.where(wide == c, columns[c], packed)
    gradients[...] = packed
    stress = jnp.zeros((flags, 128), jnp.float32)
    for k, (a, b) in enumerate(stress_pairs):
        stress = jnp.where(wide == k, viscous * (columns[3 * a + b] + columns[3 * b + a]), stress)
    viscous_ref[...] = stress

    for j in range(flags):
        chunk_ref[pl.ds(target[j], 1), :] = gradients[j : j + 1, :]


def gather_rows(flag_cell, owner, velocity, viscosity, capacity, owner_count):
    size_x, size_y, size_z = viscosity.shape
    flags = flag_cell.shape[0]
    chunk_rows = slot_rows + item_count * size_y
    face = jax.ShapeDtypeStruct((item_count, size_x, size_z), jnp.float32)
    return pl.pallas_call(
        functools.partial(gather_kernel, capacity, size_x, size_y, size_z, owner_count // 2),
        out_shape=(
            jax.ShapeDtypeStruct((owner_count * chunk_rows, 128), jnp.float32),
            jax.ShapeDtypeStruct((flags,), jnp.int32),
            jax.ShapeDtypeStruct((flags, 128), jnp.float32),
            face,
            face,
        ),
        in_specs=[pl.BlockSpec(memory_space=pltpu.HBM)] * 4,
        out_specs=(VMEM, SMEM, VMEM, VMEM, VMEM),
        scratch_shapes=[
            pltpu.SMEM((flags,), jnp.int32),
            pltpu.SMEM((flags,), jnp.int32),
            pltpu.VMEM((3, size_x * size_y, size_z), jnp.float32),
            pltpu.VMEM((size_x * size_y, size_z), jnp.float32),
            pltpu.VMEM((10, flags, size_z), jnp.float32),
            pltpu.VMEM((flags, 128), jnp.float32),
            pltpu.SMEM((flags,), jnp.int32),
            pltpu.SMEM((owner_count,), jnp.int32),
            pltpu.SemaphoreType.DMA((4,)),
        ],
        compiler_params=limit(8),
        cost_estimate=pl.CostEstimate(flops=400000, bytes_accessed=3000000, transcendentals=0),
        name="gather_rows",
    )(
        far(flag_cell),
        far(owner),
        far(velocity.reshape(3, size_x * size_y, size_z)),
        far(viscosity.reshape(size_x * size_y, size_z)),
    )


def micro_kernel(
    capacity, parts, rows, groups, conform_ref, noise_ref, rate_ref, first_conform_ref, first_noise_ref,
    next_ref, chunk_ref, conform, noise, rate, rate_wide, sums_ref, read_sem, noise_sem,
):
    steps, _, slots, dumbbells = noise_ref.shape
    blocks = slots // rows
    span = steps // groups
    width = dumbbells // parts
    owners = slots // capacity
    scale = 1.0 / noise_weight
    extent = fene_extent * scale * scale

    def block_rows(block):
        return pl.ds(pl.multiple_of(block * rows, rows), rows)

    def read(block):
        at = block_rows(block)
        return pltpu.make_async_copy(conform_ref.at[:, at, :], conform.at[:, at, :], read_sem.at[block])

    def read_noise(block, group):
        at, when = block_rows(block), pl.ds(group * span, span)
        return pltpu.make_async_copy(
            noise_ref.at[when, :, at, :], noise.at[when, :, at, :], noise_sem.at[block, group]
        )

    assert parts == 4
    for block in range(1, blocks):
        read(block).start()
        for group in range(groups):
            read_noise(block, group).start()
    conform[:, 0:rows, :] = first_conform_ref[...]
    for step in range(steps):
        noise[step, :, 0:rows, :] = first_noise_ref[step]
    for owner in range(owners):
        rate[owner * capacity : (owner + 1) * capacity, :] = rate_ref[owner, 0:capacity, :]
        chunk_ref[owner] = jnp.zeros(chunk_ref.shape[1:], jnp.float32)
    for a in range(3):
        for b in range(3):
            column = micro_step * rate[:, 3 * a + b : 3 * a + b + 1] + (1.0 if a == b else 0.0)
            rate_wide[3 * a + b] = jnp.broadcast_to(column, (slots, width))

    def inverses(state, scale):
        rooms = []
        for part in range(parts):
            q = state[3 * part : 3 * part + 3]
            room = (extent - q[0] * q[0]) - (q[1] * q[1] + q[2] * q[2])
            rooms.append(jnp.maximum(room, extent * spring_floor))
        first, second = rooms[0] * rooms[1], rooms[2] * rooms[3]
        all_four = scale * pl.reciprocal(first * second)
        first, second = all_four * second, all_four * first
        return first * rooms[1], first * rooms[0], second * rooms[3], second * rooms[2]

    def advance_block(block, carry):
        at = block_rows(block)
        rates = [[rate_wide.at[3 * a + b, at, :] for b in range(3)] for a in range(3)]

        def substep(step, state):
            updated = []
            springs = inverses(state, micro_step * relax_rate * extent)
            for part in range(parts):
                q = state[3 * part : 3 * part + 3]
                spring = springs[part]
                for a in range(3):
                    b, c = [other for other in range(3) if other != a]
                    kick = noise[step, a, at, part * width : (part + 1) * width].astype(jnp.float32)
                    rest = (rates[a][b][...] * q[b] + rates[a][c][...] * q[c]) + kick
                    updated.append((rates[a][a][...] - spring) * q[a] + rest)
            return tuple(updated)

        def advance_group(group, state):
            @pl.when(block > 0)
            def _():
                read_noise(block, group).wait()

            for step in range(span):
                state = substep(group * span + step, state)
            return state

        @pl.when(block > 0)
        def _():
            read(block).wait()

        state = tuple(
            conform[a, at, part * width : (part + 1) * width] * scale
            for part in range(parts)
            for a in range(3)
        )
        state = lax.fori_loop(0, groups, advance_group, state, unroll=True)
        sums = [None] * 6
        inverse = inverses(state, 1.0)
        for part in range(parts):
            q = state[3 * part : 3 * part + 3]
            for a in range(3):
                next_ref[a, at, part * width : (part + 1) * width] = q[a] * noise_weight
            for k, (a, b) in enumerate(stress_pairs):
                term = (inverse[part] * q[a]) * q[b]
                sums[k] = term if sums[k] is None else sums[k] + term
        for k in range(6):
            sums_ref[k, at, :] = sums[k]
        return carry

    lax.fori_loop(0, blocks, advance_block, 0)
    lane = lanes_of((slots, 128))
    packed = jnp.zeros((slots, 128), jnp.float32)
    weight = extent * noise_weight * noise_weight / dumbbells
    for k, (a, b) in enumerate(stress_pairs):
        mean = jnp.sum(sums_ref[k], axis=1, keepdims=True) * weight
        packed = jnp.where(lane == k, polymer_weight * (mean - (1.0 if a == b else 0.0)), packed)
    for owner in range(owners):
        chunk_ref[owner, 0:capacity, :] = packed[owner * capacity : (owner + 1) * capacity]


block_slots = 16


def first_kernel(rows, after_ref, conform_ref, noise_ref, conform_out, noise_out, sems):
    copies = (
        pltpu.make_async_copy(conform_ref.at[:, 0:rows, :], conform_out, sems.at[0]),
        pltpu.make_async_copy(noise_ref.at[:, :, 0:rows, :], noise_out, sems.at[1]),
    )
    for copy in copies:
        copy.start()
    for copy in copies:
        copy.wait()


def first_block(after, conformations, increments):
    steps, _, _, dumbbells = increments.shape
    whole = pl.BlockSpec(memory_space=pltpu.HBM)
    return pl.pallas_call(
        functools.partial(first_kernel, block_slots),
        out_shape=(
            pltpu.VMEM((3, block_slots, dumbbells), jnp.float32),
            pltpu.VMEM((steps, 3, block_slots, dumbbells), jnp.bfloat16),
        ),
        in_specs=[pl.BlockSpec(memory_space=pl.ANY), whole, whole],
        out_specs=(VMEM, VMEM),
        scratch_shapes=[pltpu.SemaphoreType.DMA((2,))],
        compiler_params=limit(4),
        cost_estimate=pl.CostEstimate(flops=0, bytes_accessed=3000000, transcendentals=0),
        name="first_block",
    )(after, far(conformations), far(increments))


def advance(conformations, increments, chunks, first_conform, first_noise, capacity):
    slots, dumbbells = conformations.shape[1:]
    steps = increments.shape[0]
    owners = slots // capacity
    rows, parts, groups = block_slots, 4, 4
    blocks = slots // rows
    whole = pl.BlockSpec(memory_space=pltpu.HBM)
    return pl.pallas_call(
        functools.partial(micro_kernel, capacity, parts, rows, groups),
        out_shape=(
            pltpu.VMEM(conformations.shape, jnp.float32),
            jax.ShapeDtypeStruct((owners, slot_rows + line_rows, 128), jnp.float32),
        ),
        in_specs=[whole, whole, VMEM, VMEM, VMEM],
        out_specs=(VMEM, VMEM),
        scratch_shapes=[
            pltpu.VMEM(conformations.shape, jnp.float32),
            pltpu.VMEM(increments.shape, jnp.bfloat16),
            pltpu.VMEM((slots, 128), jnp.float32),
            pltpu.VMEM((9, slots, dumbbells // parts), jnp.float32),
            pltpu.VMEM((6, slots, dumbbells // parts), jnp.float32),
            pltpu.SemaphoreType.DMA((blocks,)),
            pltpu.SemaphoreType.DMA((blocks, groups)),
        ],
        compiler_params=limit(12),
        cost_estimate=pl.CostEstimate(flops=20000000, bytes_accessed=5000000, transcendentals=600000),
        name="advance",
    )(far(conformations), far(increments), chunks, first_conform, first_noise)


def lines_kernel(macro_count, chunk_ref, y_low_ref, y_high_ref, out_ref):
    out_ref[...] = chunk_ref[...]
    macro, core = place_of()
    size_x, size_z = y_low_ref.shape[1:]
    sides = (y_low_ref, y_high_ref)
    for side in range(2):
        beside = macro - 1 if side == 0 else macro + 1

        @pl.when(beside >= 0 if side == 0 else beside < macro_count)
        def _(side=side, beside=beside):
            x = 0 if side == 0 else size_x - 1
            for u in range(2):
                for a in range(2):
                    at = slot_rows + 2 * u + a
                    out_ref[2 * beside + core, at : at + 1, :] = sides[u][a, x : x + 1, :]

    lane = lanes_of((8, size_z))
    source = jnp.where(core == 0, size_z - 1, 0)
    total = jnp.zeros((8, size_z), jnp.float32)
    for i in range(size_x // 8):
        for u in range(2):
            for a in range(2):
                at = 4 * i + 2 * u + a
                total = jnp.where(
                    lane == at, rolled(sides[u][1 + a, 8 * i : 8 * i + 8, :], at - source), total
                )
    out_ref[2 * macro + 1 - core, slot_rows:, :] = total


def add_lines(chunks, y_low, y_high):
    return pl.pallas_call(
        functools.partial(lines_kernel, chunks.shape[0] // 2),
        out_shape=jax.ShapeDtypeStruct(chunks.shape, jnp.float32),
        in_specs=[VMEM, VMEM, VMEM],
        out_specs=VMEM,
        compiler_params=limit(4),
        cost_estimate=pl.CostEstimate(flops=20000, bytes_accessed=400000, transcendentals=0),
        name="add_lines",
    )(chunks, y_low, y_high)


product_depth = 128


def one_hots(size_y, size_z, cell_ref, position_ref, lines_ref, pick_ref, spread_ref, rows):
    flags = cell_ref.shape[0]
    weight = 0.5 * macro_step
    row_count = spread_ref.shape[0]
    back_rows = pick_ref.shape[1] // 3
    lane = lanes_of((1, size_z))
    row_lane = lanes_of((1, rows.shape[1]))
    slot_lane = lanes_of((flags, back_rows))
    flag_row = lax.broadcasted_iota(jnp.int32, (flags, back_rows), 0)
    rows[3 * flags :, :] = jnp.zeros((product_depth - 3 * flags, rows.shape[1]), jnp.float32)
    slot = jnp.zeros((flags, back_rows), jnp.int32)
    for j in range(flags):
        cell = cell_ref[j]
        row = lax.div(cell, size_z)
        z = cell - row * size_z
        lines_ref[0, j : j + 1, :] = jnp.where(lane == z, weight, 0.0)
        lines_ref[1, j : j + 1, :] = jnp.where(
            lane == z - 1, weight, jnp.where(lane == z + 1, -weight, 0.0)
        )
        for number, shift in enumerate((size_y, 1)):
            rows[number * flags + j : number * flags + j + 1, :] = jnp.where(
                row_lane == row - shift, 1.0, jnp.where(row_lane == row + shift, -1.0, 0.0)
            )
        rows[2 * flags + j : 2 * flags + j + 1, :] = jnp.where(row_lane == row, 1.0, 0.0)
        slot = jnp.where(flag_row == j, position_ref[j], slot)
    spread = rows[...].T[:row_count].astype(jnp.bfloat16)
    pick = jnp.where(slot_lane == slot, 1.0, 0.0).astype(jnp.bfloat16)
    for piece in range(3):
        spread_ref[:, piece * product_depth : (piece + 1) * product_depth] = spread
        pick_ref[:, piece * back_rows : (piece + 1) * back_rows] = pick


def flow_kernel(
    size_x, size_y, size_z, macro_count, cell_ref, position_ref, velocity_ref, viscosity_ref, chunk_ref,
    y_low_ref, y_high_ref, out_ref, corner_ref, edge_ref, lines_ref, pick_ref, spread_ref,
    padded, stress_x, stress_rest, faces, ghost_y, ghost_z, rows,
):
    macro, core = place_of()
    one_hots(size_y, size_z, cell_ref, position_ref, lines_ref, pick_ref, spread_ref, rows)
    inside = (macro > 0, macro < macro_count - 1)
    sign_z = jnp.where(core == 0, 1.0, -1.0)
    end = jnp.where(core == 0, size_z - 1, 0)
    shape = (size_y, size_z)
    lane, row = lanes_of(shape), lax.broadcasted_iota(jnp.int32, shape, 0)
    at_end = jnp.where(lane == end, sign_z, 0.0)

    def kept(value, condition):
        return jnp.where(condition, value, 0.0)

    def plane(x):
        return pl.ds(pl.multiple_of(x * size_y, 8), size_y)

    def difference_z(value):
        lane = lanes_of(value.shape)
        return jnp.where(lane == size_z - 1, 0.0, rolled(value, -1)) - jnp.where(
            lane == 0, 0.0, rolled(value, 1)
        )

    def difference_rows(value, low=0.0, high=0.0):
        count = value.shape[0]
        row = lax.broadcasted_iota(jnp.int32, value.shape, 0)
        return jnp.where(row == count - 1, high, pltpu.roll(value, count - 1, 0)) - jnp.where(
            row == 0, low, pltpu.roll(value, 1, 0)
        )

    x_faces, x_others = [], []
    for s in range(2):
        beside = jnp.maximum(macro - 1, 0) if s == 0 else jnp.minimum(macro + 1, macro_count - 1)
        x_faces.append(
            [
                kept(chunk_ref[2 * beside + core, slot_rows + i * size_y : slot_rows + (i + 1) * size_y, :], inside[s])
                for i in range(item_count)
            ]
        )
        x_others.append(
            [
                kept(
                    rolled(
                        chunk_ref[
                            2 * beside + 1 - core, slot_rows + i * size_y : slot_rows + (i + 1) * size_y, :
                        ],
                        2 * end + 1,
                    ),
                    inside[s],
                )
                for i in range(2)
            ]
        )

    group = size_z // 8
    packed = [
        chunk_ref[2 * macro + 1 - core, slot_rows + i * size_y : slot_rows + (i + 1) * size_y, :]
        for i in range(-(-size_x // group))
    ]
    for i, value in enumerate(packed):

        def unpack(x, carry):
            for q in range(item_count):
                a, layer = (q, 0) if q < 4 else (q - 4, 1)
                at = 8 * (x - i * group) + 2 * a + (core if layer == 0 else 1 - core)
                faces[q, x + 1] = rolled(value, end - at)
            return carry

        lax.fori_loop(i * group, min(size_x, (i + 1) * group), unpack, 0, unroll=8)
    faces[2, 0] = x_others[0][1]
    faces[2, size_x + 1] = x_others[1][1]

    for a in range(3):
        padded[a, 0] = x_faces[0][a]
        padded[a, size_x + 1] = x_faces[1][a]

    def fill(x, carry):
        for a in range(3):
            padded[a, x + 1] = velocity_ref[a, plane(x), :]
        return carry

    lax.fori_loop(0, size_x, fill, 0, unroll=True)

    rest = {(1, 1): 0, (2, 2): 1, (1, 2): 2}

    def stress_plane(x, carry):
        along_x, along_y, along_z, centre = [], [], [], []
        for a in range(3):
            value = padded[a, x + 1]
            centre.append(value)
            along_x.append(padded[a, x + 2] - padded[a, x])
            along_y.append(
                difference_rows(value, y_low_ref[a, pl.ds(x, 1), :], y_high_ref[a, pl.ds(x, 1), :])
            )
            along_z.append(difference_z(value) + faces[a, x + 1] * at_end)
        slopes = (along_x, along_y, along_z)
        half = 0.5 * viscosity_ref[plane(x), :]
        for a, b in stress_pairs:
            value = half * (slopes[b][a] + slopes[a][b])
            if a == 0:
                stress_x[b, x + 1] = value
            else:
                stress_rest[rest[a, b], x] = value
        weight = (0.5 * faces[3, x + 1]) * at_end
        normal = [(faces[4 + a, x + 1] - centre[a]) * sign_z for a in range(3)]
        ghost_z[0, x] = weight * (normal[0] + (faces[2, x + 2] - faces[2, x]))
        ghost_z[1, x] = weight * (normal[1] + difference_rows(faces[2, x + 1]))
        ghost_z[2, x] = weight * (2.0 * normal[2])
        return carry

    lax.fori_loop(0, size_x, stress_plane, 0, unroll=6)

    for s in range(2):
        near, far, weight = x_faces[s][0:3], x_faces[s][3:6], 0.5 * x_faces[s][6]
        sign = -1.0 if s == 0 else 1.0
        normal = [(far[a] - padded[a, 1 if s == 0 else size_x]) * sign for a in range(3)]
        slope_y = difference_rows(near[0])
        slope_z = difference_z(near[0]) + x_others[s][0] * at_end
        at = 0 if s == 0 else size_x + 1
        stress_x[0, at] = weight * (2.0 * normal[0])
        stress_x[1, at] = weight * (normal[1] + slope_y)
        stress_x[2, at] = weight * (normal[2] + slope_z)
        for u in range(2):
            y, sign_y = (0, -1.0) if u == 0 else (size_y - 1, 1.0)
            number = 4 * s + 2 * u
            corner_ref[number : number + 1, :] = (0.5 * macro_step * sign * sign_y) * weight[y : y + 1, :]

    for u, ref in enumerate((y_low_ref, y_high_ref)):
        y, sign = (0, -1.0) if u == 0 else (size_y - 1, 1.0)
        weight = 0.5 * ref[6]
        normal = [
            (ref[3 + a] - velocity_ref[a, pl.ds(y, size_x, stride=size_y), :]) * sign for a in range(3)
        ]
        ghost_y[3 * u] = weight * (normal[0] + difference_rows(ref[1]))
        ghost_y[3 * u + 1] = weight * (2.0 * normal[1])
        ghost_y[3 * u + 2] = weight * (normal[2] + difference_z(ref[1]))
        for s in range(2):
            x, sign_x = (0, -1.0) if s == 0 else (size_x - 1, 1.0)
            number = 4 * s + 2 * u + 1
            corner_ref[number : number + 1, :] = (0.5 * macro_step * sign * sign_x) * weight[x : x + 1, :]
        wide = lanes_of((size_x, size_z))
        scale = jnp.where(wide == end, (0.5 * macro_step * sign) * sign_z, 0.0)
        edge_ref[2 * u] = scale * weight
        for x in range(size_x):
            edge_ref[2 * u + 1, x : x + 1, :] = scale[x : x + 1, :] * (0.5 * faces[3, x + 1, y : y + 1, :])

    columns = {(0, 1): (stress_x, 1, 1), (1, 1): (stress_rest, 0, 0), (2, 1): (stress_rest, 2, 0)}
    columns_z = {0: (stress_x, 2, 1), 1: (stress_rest, 2, 0), 2: (stress_rest, 1, 0)}

    def step_plane(x, carry):
        for a in range(3):
            total = stress_x[a, x + 2] - stress_x[a, x]
            ref, number, shift = columns[a, 1]
            total = total + difference_rows(
                ref[number, x + shift], ghost_y[a, pl.ds(x, 1), :], ghost_y[3 + a, pl.ds(x, 1), :]
            )
            ref, number, shift = columns_z[a]
            total = total + (difference_z(ref[number, x + shift]) + ghost_z[a, x])
            out_ref[a, plane(x), :] = padded[a, x + 1] + (0.5 * macro_step) * total
        return carry

    lax.fori_loop(0, size_x, step_plane, 0, unroll=6)


def flow_step(flag_cell, position, velocity, viscosity, chunks, y_low, y_high):
    size_x, size_y, size_z = viscosity.shape
    flags = flag_cell.shape[0]
    back_rows = chunks.shape[0] * (slot_rows + line_rows)
    row_count = size_x * size_y
    planes = (size_x, size_y, size_z)
    wide = (size_x + 2, size_y, size_z)
    return pl.pallas_call(
        functools.partial(flow_kernel, size_x, size_y, size_z, chunks.shape[0] // 2),
        out_shape=(
            jax.ShapeDtypeStruct((3, size_x * size_y, size_z), jnp.float32),
            jax.ShapeDtypeStruct((8, size_z), jnp.float32),
            jax.ShapeDtypeStruct((4, size_x, size_z), jnp.float32),
            jax.ShapeDtypeStruct((2, flags, size_z), jnp.float32),
            jax.ShapeDtypeStruct((flags, 3 * back_rows), jnp.bfloat16),
            jax.ShapeDtypeStruct((row_count, 3 * product_depth), jnp.bfloat16),
        ),
        in_specs=[SMEM] * 2 + [VMEM] * 5,
        out_specs=(VMEM,) * 6,
        scratch_shapes=[
            pltpu.VMEM((3, *wide), jnp.float32),
            pltpu.VMEM((3, *wide), jnp.float32),
            pltpu.VMEM((3, *planes), jnp.float32),
            pltpu.VMEM((item_count, *wide), jnp.float32),
            pltpu.VMEM((6, size_x, size_z), jnp.float32),
            pltpu.VMEM((3, *planes), jnp.float32),
            pltpu.VMEM((product_depth, -(-row_count // 128) * 128), jnp.float32),
        ],
        compiler_params=limit(12),
        cost_estimate=pl.CostEstimate(flops=4000000, bytes_accessed=3000000, transcendentals=0),
        name="flow_step",
    )(
        flag_cell, position,
        velocity.reshape(3, size_x * size_y, size_z),
        viscosity.reshape(size_x * size_y, size_z),
        chunks, y_low, y_high,
    )


def pieces(value):
    high = value.astype(jnp.bfloat16)
    rest = value - high.astype(jnp.float32)
    middle = rest.astype(jnp.bfloat16)
    return high, middle, (rest - middle.astype(jnp.float32)).astype(jnp.bfloat16)


def polymer_kernel(
    size_x, size_y, size_z, macro_count, chunk_ref, viscous_ref, corner_ref, edge_ref, lines_ref, pick_ref,
    spread_ref, partial_ref, out_ref, flag_ref, field, write_sem,
):
    flags = viscous_ref.shape[0]
    chunk_rows = slot_rows + line_rows
    macro, core = place_of()
    values = jnp.dot(
        pick_ref[...], jnp.concatenate(pieces(chunk_ref[...]), axis=0), preferred_element_type=jnp.float32
    )
    here, beside_z = lines_ref[0], lines_ref[1]
    columns = [jnp.broadcast_to(values[:, k : k + 1], (flags, size_z)) for k in range(6)]
    unused = jnp.zeros((product_depth - 3 * flags, size_z), jnp.float32)
    split = [
        pieces(
            jnp.concatenate(
                [
                    columns[pair_index(a, 0)] * here, columns[pair_index(a, 1)] * here,
                    columns[pair_index(a, 2)] * beside_z, unused,
                ],
                axis=0,
            )
        )
        for a in range(3)
    ]
    flag_ref[...] = (viscous_ref[...] + values).T[0:6, :]

    field[...] = partial_ref[...]
    for s in range(2):
        inside = macro > 0 if s == 0 else macro < macro_count - 1
        beside = jnp.maximum(macro - 1, 0) if s == 0 else jnp.minimum(macro + 1, macro_count - 1)
        start = (2 * beside + core) * chunk_rows + slot_rows
        x = 0 if s == 0 else size_x - 1
        for u in range(2):
            at = x * size_y + (0 if u == 0 else size_y - 1)
            for a in range(2):
                number = 4 * s + 2 * u + a
                line = corner_ref[number : number + 1, :] * chunk_ref[pl.ds(start + 2 * u + a, 1), :]
                field[1 - a, at : at + 1, :] += jnp.where(inside, line, 0.0)
    start = pl.multiple_of((2 * macro + 1 - core) * chunk_rows + slot_rows, 8)
    packed = chunk_ref[pl.ds(start, line_rows), :]
    end = jnp.where(core == 0, size_z - 1, 0)
    for u in range(2):
        y = 0 if u == 0 else size_y - 1
        for a in range(2):
            for i in range(size_x // 8):
                line = rolled(packed, end - (4 * i + 2 * u + a)) * edge_ref[2 * u + a, 8 * i : 8 * i + 8, :]
                at = pl.ds(8 * i * size_y + y, 8, stride=size_y)
                field[2 - a, at, :] += line
    copies = [pltpu.make_async_copy(field.at[a], out_ref.at[a], write_sem.at[a]) for a in range(3)]
    for a in range(3):
        field[a] += jnp.dot(
            spread_ref[...], jnp.concatenate(split[a], axis=0), preferred_element_type=jnp.float32
        )
        copies[a].start()
    for copy in copies:
        copy.wait()


def add_polymer(chunks, viscous, corners, edges, lines, pick, spread, partial, shape):
    flags = viscous.shape[0]
    size_x, size_y, size_z = shape
    return pl.pallas_call(
        functools.partial(polymer_kernel, size_x, size_y, size_z, chunks.shape[0] // 2),
        out_shape=(
            jax.ShapeDtypeStruct(partial.shape, jnp.float32),
            jax.ShapeDtypeStruct((6, flags), jnp.float32),
        ),
        in_specs=[VMEM] * 8,
        out_specs=(pl.BlockSpec(memory_space=pltpu.HBM), VMEM),
        scratch_shapes=[pltpu.VMEM(partial.shape, jnp.float32), pltpu.SemaphoreType.DMA((3,))],
        compiler_params=limit(8),
        cost_estimate=pl.CostEstimate(flops=400000, bytes_accessed=3000000, transcendentals=0),
        name="add_polymer",
    )(chunks.reshape(-1, 128), viscous, corners, edges, lines, pick, spread, partial)


def shards(velocity, viscosity, flag_cell, flag_owner, conformations, increments):
    macro_count = lax.axis_size("macro")
    tile_count = lax.axis_size("tile")
    assert lax.axis_size("micro") == 2
    owner_count = 2 * macro_count
    capacity = conformations.shape[1] // owner_count
    size_x, size_y, size_z = viscosity.shape
    assert capacity <= slot_rows and size_y == 8 and size_z == 128 and size_x % 8 == 0 and size_x <= 48
    chunks, position, viscous, y_first, y_last = gather_rows(
        flag_cell, flag_owner.reshape(-1), velocity, viscosity, capacity, owner_count
    )

    def exchange(rows):
        return lax.all_to_all(rows, ("macro", "micro"), split_axis=0, concat_axis=0, tiled=True)

    received = exchange(chunks.reshape(owner_count, -1, 128))
    up = [(i, i + 1) for i in range(tile_count - 1)]
    down = [(target, source) for source, target in up]
    y_low = lax.ppermute(y_last, "tile", up)
    y_high = lax.ppermute(y_first, "tile", down)
    first_conform, first_noise = first_block(position, conformations, increments)
    last_state, polymer = advance(
        conformations, increments, received, first_conform, first_noise, capacity
    )
    returned = exchange(add_lines(polymer, y_low, y_high))
    partial, corners, edges, lines, pick, spread = flow_step(
        flag_cell, position, velocity, viscosity, received, y_low, y_high
    )
    velocity_next, flag_stress = add_polymer(
        returned, viscous, corners, edges, lines, pick, spread, partial, viscosity.shape
    )
    return (velocity_next.reshape(velocity.shape), last_state, flag_stress)


def solution(mesh):
    in_specs = (
        P(None, "macro", "tile", "micro"),
        P("macro", "tile", "micro"),
        P(("macro", "tile", "micro")),
        P(("macro", "tile", "micro"), None),
        P(None, ("macro", "tile", "micro"), None),
        P(None, None, ("macro", "tile", "micro"), None),
    )
    out_specs = (
        P(None, "macro", "tile", "micro"),
        P(None, ("macro", "tile", "micro"), None),
        P(None, ("macro", "tile", "micro")),
    )
    return jax.shard_map(shards, mesh=mesh, in_specs=in_specs, out_specs=out_specs, check_vma=False)
```

```python
import functools

import jax
import jax.numpy as jnp
from jax import lax
from jax.experimental import pallas as pl
from jax.experimental.pallas import tpu as pltpu
from jax.sharding import PartitionSpec as P

stress_pairs = ((0, 0), (1, 1), (2, 2), (0, 1), (0, 2), (1, 2))
macro_step = 0.1
micro_step = 0.01
noise_weight = 0.1
relax_rate = 0.5
fene_extent = 30.0
spring_floor = 0.1
polymer_weight = 0.25

SMEM = pl.BlockSpec(memory_space=pltpu.SMEM)
VMEM = pl.BlockSpec(memory_space=pltpu.VMEM)


def pair_index(left_axis, right_axis):
    return stress_pairs.index((min(left_axis, right_axis), max(left_axis, right_axis)))


def lanes_of(shape):
    return lax.broadcasted_iota(jnp.int32, shape, len(shape) - 1)


slot_rows = 8
item_count = 7
line_rows = 8


def limit(mebibytes):
    return pltpu.CompilerParams(vmem_limit_bytes=mebibytes * 1024 * 1024)


def far(value):
    return pltpu.with_memory_space_constraint(value, pltpu.HBM)


def place_of():
    return lax.axis_index("macro"), lax.axis_index("micro")


def rolled(value, amount):
    size = value.shape[-1]
    if isinstance(amount, int):
        return pltpu.roll(value, amount % size, value.ndim - 1)
    return pltpu.roll(value, lax.rem(amount + 2 * size, size), value.ndim - 1)


def gather_kernel(
    capacity, size_x, size_y, size_z, macro_count, cell_in, owner_in, velocity_in, viscosity_in,
    chunk_ref, position_ref, viscous_ref, y_low_ref, y_high_ref,
    cell_ref, owner_ref, velocity_ref, viscosity_ref, masked, gradients, target, count, sems,
):
    flags = cell_ref.shape[0]
    copies = [
        pltpu.make_async_copy(source, into, sems.at[number])
        for number, (source, into) in enumerate(
            (
                (cell_in, cell_ref), (owner_in, owner_ref), (velocity_in, velocity_ref),
                (viscosity_in, viscosity_ref),
            )
        )
    ]
    for copy in copies:
        copy.start()
    chunk_rows = slot_rows + item_count * size_y
    macro, core = place_of()
    lane = lanes_of((1, size_z))

    for owner in range(count.shape[0]):
        count[owner] = 0
        chunk_ref[owner * chunk_rows : owner * chunk_rows + slot_rows, :] = jnp.zeros((slot_rows, 128), jnp.float32)
    for copy in copies[:2]:
        copy.wait()
    for j in range(flags):
        owner = owner_ref[j]
        rank = count[owner]
        count[owner] = rank + 1
        target[j] = owner * chunk_rows + rank
        position_ref[j] = owner * (slot_rows + line_rows) + rank
    for copy in copies[2:]:
        copy.wait()
    planes = velocity_ref.reshape(3, size_x, size_y, size_z)
    layers = viscosity_ref.reshape(size_x, size_y, size_z)
    for j in range(flags):
        cell = cell_ref[j]
        x = lax.shift_right_logical(cell, 10)
        y = lax.shift_right_logical(cell, 7) & (size_y - 1)
        z = cell & (size_z - 1)
        here = (lane == z).astype(jnp.float32)
        along_z = (lane == z + 1).astype(jnp.float32) - (lane == z - 1).astype(jnp.float32)
        at = pl.ds(y, 1)
        for a in range(3):
            along_x = planes[a, x + 1, at, :] - planes[a, x - 1, at, :]
            along_y = planes[a, x, pl.ds(y + 1, 1), :] - planes[a, x, pl.ds(y - 1, 1), :]
            masked[3 * a, j : j + 1, :] = along_x * here
            masked[3 * a + 1, j : j + 1, :] = along_y * here
            masked[3 * a + 2, j : j + 1, :] = planes[a, x, at, :] * along_z
        masked[9, j : j + 1, :] = layers[x, at, :] * here

    for side, ref in enumerate((y_low_ref, y_high_ref)):
        for layer in range(2):
            y = layer if side == 0 else size_y - 1 - layer
            for a in range(3):
                ref[3 * layer + a] = velocity_ref[a, pl.ds(y, size_x, stride=size_y), :]
        y = 0 if side == 0 else size_y - 1
        ref[6] = viscosity_ref[pl.ds(y, size_x, stride=size_y), :]

    for side in range(2):
        beside = macro - 1 if side == 0 else macro + 1

        @pl.when(beside >= 0 if side == 0 else beside < macro_count)
        def _(side=side, beside=beside):
            first = pl.multiple_of((2 * beside + core) * chunk_rows + slot_rows, 8)
            other = pl.multiple_of((2 * beside + 1 - core) * chunk_rows + slot_rows, 8)
            for layer in range(2):
                x = layer if side == 0 else size_x - 1 - layer
                for a in range(3):
                    chunk_ref[pl.ds(first + (3 * layer + a) * size_y, size_y), :] = velocity_ref[
                        a, x * size_y : (x + 1) * size_y, :
                    ]
            x = 0 if side == 0 else size_x - 1
            chunk_ref[pl.ds(first + 6 * size_y, size_y), :] = viscosity_ref[x * size_y : (x + 1) * size_y, :]
            for number, a in enumerate((0, 2)):
                chunk_ref[pl.ds(other + number * size_y, size_y), :] = velocity_ref[
                    a, x * size_y : (x + 1) * size_y, :
                ]

    group = size_z // 8
    lane2 = lanes_of((size_y, size_z))
    first = pl.multiple_of((2 * macro + 1 - core) * chunk_rows + slot_rows, 8)
    source = jnp.where(core == 0, size_z - 2, 0)
    for block in range(-(-size_x // group)):
        total = jnp.zeros((size_y, size_z), jnp.float32)
        for x in range(block * group, min(size_x, (block + 1) * group)):
            rows = slice(x * size_y, (x + 1) * size_y)
            for a in range(4):
                at = 8 * (x - block * group) + 2 * a
                value = viscosity_ref[rows, :] if a == 3 else velocity_ref[a, rows, :]
                total = jnp.where((lane2 == at) | (lane2 == at + 1), rolled(value, at - source), total)
        chunk_ref[pl.ds(first + block * size_y, size_y), :] = total

    columns = [0.5 * jnp.sum(masked[c], axis=1, keepdims=True) for c in range(9)]
    viscous = jnp.sum(masked[9], axis=1, keepdims=True)
    wide = lanes_of((flags, 128))
    packed = jnp.zeros((flags, 128), jnp.float32)
    for c in range(9):
        packed = jnp.where(wide == c, columns[c], packed)
    gradients[...] = packed
    stress = jnp.zeros((flags, 128), jnp.float32)
    for k, (a, b) in enumerate(stress_pairs):
        stress = jnp.where(wide == k, viscous * (columns[3 * a + b] + columns[3 * b + a]), stress)
    viscous_ref[...] = stress

    for j in range(flags):
        chunk_ref[pl.ds(target[j], 1), :] = gradients[j : j + 1, :]


def gather_rows(flag_cell, owner, velocity, viscosity, capacity, owner_count):
    size_x, size_y, size_z = viscosity.shape
    flags = flag_cell.shape[0]
    chunk_rows = slot_rows + item_count * size_y
    face = jax.ShapeDtypeStruct((item_count, size_x, size_z), jnp.float32)
    return pl.pallas_call(
        functools.partial(gather_kernel, capacity, size_x, size_y, size_z, owner_count // 2),
        out_shape=(
            jax.ShapeDtypeStruct((owner_count * chunk_rows, 128), jnp.float32),
            jax.ShapeDtypeStruct((flags,), jnp.int32),
            jax.ShapeDtypeStruct((flags, 128), jnp.float32),
            face,
            face,
        ),
        in_specs=[pl.BlockSpec(memory_space=pltpu.HBM)] * 4,
        out_specs=(VMEM, SMEM, VMEM, VMEM, VMEM),
        scratch_shapes=[
            pltpu.SMEM((flags,), jnp.int32),
            pltpu.SMEM((flags,), jnp.int32),
            pltpu.VMEM((3, size_x * size_y, size_z), jnp.float32),
            pltpu.VMEM((size_x * size_y, size_z), jnp.float32),
            pltpu.VMEM((10, flags, size_z), jnp.float32),
            pltpu.VMEM((flags, 128), jnp.float32),
            pltpu.SMEM((flags,), jnp.int32),
            pltpu.SMEM((owner_count,), jnp.int32),
            pltpu.SemaphoreType.DMA((4,)),
        ],
        compiler_params=limit(8),
        cost_estimate=pl.CostEstimate(flops=400000, bytes_accessed=3000000, transcendentals=0),
        name="gather_rows",
    )(
        far(flag_cell),
        far(owner),
        far(velocity.reshape(3, size_x * size_y, size_z)),
        far(viscosity.reshape(size_x * size_y, size_z)),
    )


def micro_kernel(
    capacity, parts, rows, groups, conform_ref, noise_ref, rate_ref, first_conform_ref, first_noise_ref,
    next_ref, chunk_ref, conform, noise, rate, rate_wide, sums_ref, read_sem, noise_sem,
):
    steps, _, slots, dumbbells = noise_ref.shape
    blocks = slots // rows
    span = steps // groups
    width = dumbbells // parts
    owners = slots // capacity
    scale = 1.0 / noise_weight
    extent = fene_extent * scale * scale

    def block_rows(block):
        return pl.ds(pl.multiple_of(block * rows, rows), rows)

    def read(block):
        at = block_rows(block)
        return pltpu.make_async_copy(conform_ref.at[:, at, :], conform.at[:, at, :], read_sem.at[block])

    def read_noise(block, group):
        at, when = block_rows(block), pl.ds(group * span, span)
        return pltpu.make_async_copy(
            noise_ref.at[when, :, at, :], noise.at[when, :, at, :], noise_sem.at[block, group]
        )

    assert parts == 4
    early = groups // first_share
    for block in range(blocks):
        if block > 0:
            read(block).start()
        for group in range(early if block == 0 else 0, groups):
            read_noise(block, group).start()
    conform[:, 0:rows, :] = first_conform_ref[...]
    for step in range(steps // first_share):
        noise[step, :, 0:rows, :] = first_noise_ref[step]
    for owner in range(owners):
        rate[owner * capacity : (owner + 1) * capacity, :] = rate_ref[owner, 0:capacity, :]
        chunk_ref[owner] = jnp.zeros(chunk_ref.shape[1:], jnp.float32)
    for a in range(3):
        for b in range(3):
            column = micro_step * rate[:, 3 * a + b : 3 * a + b + 1] + (1.0 if a == b else 0.0)
            rate_wide[3 * a + b] = jnp.broadcast_to(column, (slots, width))

    def inverses(state, scale):
        rooms = []
        for part in range(parts):
            q = state[3 * part : 3 * part + 3]
            room = (extent - q[0] * q[0]) - (q[1] * q[1] + q[2] * q[2])
            rooms.append(jnp.maximum(room, extent * spring_floor))
        first, second = rooms[0] * rooms[1], rooms[2] * rooms[3]
        all_four = scale * pl.reciprocal(first * second)
        first, second = all_four * second, all_four * first
        return first * rooms[1], first * rooms[0], second * rooms[3], second * rooms[2]

    def advance_block(block, carry):
        at = block_rows(block)
        rates = [[rate_wide.at[3 * a + b, at, :] for b in range(3)] for a in range(3)]

        def substep(step, state):
            updated = []
            springs = inverses(state, micro_step * relax_rate * extent)
            for part in range(parts):
                q = state[3 * part : 3 * part + 3]
                spring = springs[part]
                for a in range(3):
                    b, c = [other for other in range(3) if other != a]
                    kick = noise[step, a, at, part * width : (part + 1) * width].astype(jnp.float32)
                    rest = (rates[a][b][...] * q[b] + rates[a][c][...] * q[c]) + kick
                    updated.append((rates[a][a][...] - spring) * q[a] + rest)
            return tuple(updated)

        def advance_group(group, state):
            if group < early:

                @pl.when(block > 0)
                def _():
                    read_noise(block, group).wait()

            else:
                read_noise(block, group).wait()
            for step in range(span):
                state = substep(group * span + step, state)
            return state

        @pl.when(block > 0)
        def _():
            read(block).wait()

        state = tuple(
            conform[a, at, part * width : (part + 1) * width] * scale
            for part in range(parts)
            for a in range(3)
        )
        for group in range(groups):
            state = advance_group(group, state)
        sums = [None] * 6
        inverse = inverses(state, 1.0)
        for part in range(parts):
            q = state[3 * part : 3 * part + 3]
            for a in range(3):
                next_ref[a, at, part * width : (part + 1) * width] = q[a] * noise_weight
            for k, (a, b) in enumerate(stress_pairs):
                term = (inverse[part] * q[a]) * q[b]
                sums[k] = term if sums[k] is None else sums[k] + term
        for k in range(6):
            sums_ref[k, at, :] = sums[k]
        return carry

    lax.fori_loop(0, blocks, advance_block, 0)
    lane = lanes_of((slots, 128))
    packed = jnp.zeros((slots, 128), jnp.float32)
    weight = extent * noise_weight * noise_weight / dumbbells
    for k, (a, b) in enumerate(stress_pairs):
        mean = jnp.sum(sums_ref[k], axis=1, keepdims=True) * weight
        packed = jnp.where(lane == k, polymer_weight * (mean - (1.0 if a == b else 0.0)), packed)
    for owner in range(owners):
        chunk_ref[owner, 0:capacity, :] = packed[owner * capacity : (owner + 1) * capacity]


block_slots = 32
first_share = 2


def first_kernel(rows, after_ref, conform_ref, noise_ref, conform_out, noise_out, sems):
    copies = (
        pltpu.make_async_copy(conform_ref.at[:, 0:rows, :], conform_out, sems.at[0]),
        pltpu.make_async_copy(noise_ref.at[0 : noise_out.shape[0], :, 0:rows, :], noise_out, sems.at[1]),
    )
    for copy in copies:
        copy.start()
    for copy in copies:
        copy.wait()


def first_block(after, conformations, increments):
    steps, _, _, dumbbells = increments.shape
    whole = pl.BlockSpec(memory_space=pltpu.HBM)
    return pl.pallas_call(
        functools.partial(first_kernel, block_slots),
        out_shape=(
            pltpu.VMEM((3, block_slots, dumbbells), jnp.float32),
            pltpu.VMEM((steps // first_share, 3, block_slots, dumbbells), jnp.bfloat16),
        ),
        in_specs=[pl.BlockSpec(memory_space=pl.ANY), whole, whole],
        out_specs=(VMEM, VMEM),
        scratch_shapes=[pltpu.SemaphoreType.DMA((2,))],
        compiler_params=limit(4),
        cost_estimate=pl.CostEstimate(flops=0, bytes_accessed=3000000, transcendentals=0),
        name="first_block",
    )(after, far(conformations), far(increments))


def advance(conformations, increments, chunks, first_conform, first_noise, capacity):
    slots, dumbbells = conformations.shape[1:]
    steps = increments.shape[0]
    owners = slots // capacity
    rows, parts, groups = block_slots, 4, 4
    blocks = slots // rows
    whole = pl.BlockSpec(memory_space=pltpu.HBM)
    return pl.pallas_call(
        functools.partial(micro_kernel, capacity, parts, rows, groups),
        out_shape=(
            pltpu.VMEM(conformations.shape, jnp.float32),
            jax.ShapeDtypeStruct((owners, slot_rows + line_rows, 128), jnp.float32),
        ),
        in_specs=[whole, whole, VMEM, VMEM, VMEM],
        out_specs=(VMEM, VMEM),
        scratch_shapes=[
            pltpu.VMEM(conformations.shape, jnp.float32),
            pltpu.VMEM(increments.shape, jnp.bfloat16),
            pltpu.VMEM((slots, 128), jnp.float32),
            pltpu.VMEM((9, slots, dumbbells // parts), jnp.float32),
            pltpu.VMEM((6, slots, dumbbells // parts), jnp.float32),
            pltpu.SemaphoreType.DMA((blocks,)),
            pltpu.SemaphoreType.DMA((blocks, groups)),
        ],
        compiler_params=limit(12),
        cost_estimate=pl.CostEstimate(flops=20000000, bytes_accessed=5000000, transcendentals=600000),
        name="advance",
    )(far(conformations), far(increments), chunks, first_conform, first_noise)


def lines_kernel(macro_count, chunk_ref, y_low_ref, y_high_ref, out_ref):
    out_ref[...] = chunk_ref[...]
    macro, core = place_of()
    size_x, size_z = y_low_ref.shape[1:]
    sides = (y_low_ref, y_high_ref)
    for side in range(2):
        beside = macro - 1 if side == 0 else macro + 1

        @pl.when(beside >= 0 if side == 0 else beside < macro_count)
        def _(side=side, beside=beside):
            x = 0 if side == 0 else size_x - 1
            for u in range(2):
                for a in range(2):
                    at = slot_rows + 2 * u + a
                    out_ref[2 * beside + core, at : at + 1, :] = sides[u][a, x : x + 1, :]

    lane = lanes_of((8, size_z))
    source = jnp.where(core == 0, size_z - 1, 0)
    total = jnp.zeros((8, size_z), jnp.float32)
    for i in range(size_x // 8):
        for u in range(2):
            for a in range(2):
                at = 4 * i + 2 * u + a
                total = jnp.where(
                    lane == at, rolled(sides[u][1 + a, 8 * i : 8 * i + 8, :], at - source), total
                )
    out_ref[2 * macro + 1 - core, slot_rows:, :] = total


def add_lines(chunks, y_low, y_high):
    return pl.pallas_call(
        functools.partial(lines_kernel, chunks.shape[0] // 2),
        out_shape=jax.ShapeDtypeStruct(chunks.shape, jnp.float32),
        in_specs=[VMEM, VMEM, VMEM],
        out_specs=VMEM,
        compiler_params=limit(4),
        cost_estimate=pl.CostEstimate(flops=20000, bytes_accessed=400000, transcendentals=0),
        name="add_lines",
    )(chunks, y_low, y_high)


product_depth = 128


def one_hots(size_y, size_z, cell_ref, position_ref, lines_ref, pick_ref, spread_ref, rows):
    flags = cell_ref.shape[0]
    weight = 0.5 * macro_step
    row_count = spread_ref.shape[0]
    back_rows = pick_ref.shape[1] // 3
    lane = lanes_of((1, size_z))
    row_lane = lanes_of((1, rows.shape[1]))
    slot_lane = lanes_of((flags, back_rows))
    flag_row = lax.broadcasted_iota(jnp.int32, (flags, back_rows), 0)
    rows[3 * flags :, :] = jnp.zeros((product_depth - 3 * flags, rows.shape[1]), jnp.float32)
    slot = jnp.zeros((flags, back_rows), jnp.int32)
    for j in range(flags):
        cell = cell_ref[j]
        row = lax.div(cell, size_z)
        z = cell - row * size_z
        lines_ref[0, j : j + 1, :] = jnp.where(lane == z, weight, 0.0)
        lines_ref[1, j : j + 1, :] = jnp.where(
            lane == z - 1, weight, jnp.where(lane == z + 1, -weight, 0.0)
        )
        for number, shift in enumerate((size_y, 1)):
            rows[number * flags + j : number * flags + j + 1, :] = jnp.where(
                row_lane == row - shift, 1.0, jnp.where(row_lane == row + shift, -1.0, 0.0)
            )
        rows[2 * flags + j : 2 * flags + j + 1, :] = jnp.where(row_lane == row, 1.0, 0.0)
        slot = jnp.where(flag_row == j, position_ref[j], slot)
    spread = rows[...].T[:row_count].astype(jnp.bfloat16)
    pick = jnp.where(slot_lane == slot, 1.0, 0.0).astype(jnp.bfloat16)
    for piece in range(3):
        spread_ref[:, piece * product_depth : (piece + 1) * product_depth] = spread
        pick_ref[:, piece * back_rows : (piece + 1) * back_rows] = pick


def flow_kernel(
    size_x, size_y, size_z, macro_count, cell_ref, position_ref, velocity_ref, viscosity_ref, chunk_ref,
    y_low_ref, y_high_ref, out_ref, corner_ref, edge_ref, lines_ref, pick_ref, spread_ref,
    padded, stress_x, stress_rest, faces, ghost_y, ghost_z, rows,
):
    macro, core = place_of()
    one_hots(size_y, size_z, cell_ref, position_ref, lines_ref, pick_ref, spread_ref, rows)
    inside = (macro > 0, macro < macro_count - 1)
    sign_z = jnp.where(core == 0, 1.0, -1.0)
    end = jnp.where(core == 0, size_z - 1, 0)
    shape = (size_y, size_z)
    lane, row = lanes_of(shape), lax.broadcasted_iota(jnp.int32, shape, 0)
    at_end = jnp.where(lane == end, sign_z, 0.0)

    def kept(value, condition):
        return jnp.where(condition, value, 0.0)

    def plane(x):
        return pl.ds(pl.multiple_of(x * size_y, 8), size_y)

    def difference_z(value):
        lane = lanes_of(value.shape)
        return jnp.where(lane == size_z - 1, 0.0, rolled(value, -1)) - jnp.where(
            lane == 0, 0.0, rolled(value, 1)
        )

    def difference_rows(value, low=0.0, high=0.0):
        count = value.shape[0]
        row = lax.broadcasted_iota(jnp.int32, value.shape, 0)
        return jnp.where(row == count - 1, high, pltpu.roll(value, count - 1, 0)) - jnp.where(
            row == 0, low, pltpu.roll(value, 1, 0)
        )

    x_faces, x_others = [], []
    for s in range(2):
        beside = jnp.maximum(macro - 1, 0) if s == 0 else jnp.minimum(macro + 1, macro_count - 1)
        x_faces.append(
            [
                kept(chunk_ref[2 * beside + core, slot_rows + i * size_y : slot_rows + (i + 1) * size_y, :], inside[s])
                for i in range(item_count)
            ]
        )
        x_others.append(
            [
                kept(
                    rolled(
                        chunk_ref[
                            2 * beside + 1 - core, slot_rows + i * size_y : slot_rows + (i + 1) * size_y, :
                        ],
                        2 * end + 1,
                    ),
                    inside[s],
                )
                for i in range(2)
            ]
        )

    group = size_z // 8
    packed = [
        chunk_ref[2 * macro + 1 - core, slot_rows + i * size_y : slot_rows + (i + 1) * size_y, :]
        for i in range(-(-size_x // group))
    ]
    for i, value in enumerate(packed):

        def unpack(x, carry):
            for q in range(item_count):
                a, layer = (q, 0) if q < 4 else (q - 4, 1)
                at = 8 * (x - i * group) + 2 * a + (core if layer == 0 else 1 - core)
                faces[q, x + 1] = rolled(value, end - at)
            return carry

        lax.fori_loop(i * group, min(size_x, (i + 1) * group), unpack, 0, unroll=8)
    faces[2, 0] = x_others[0][1]
    faces[2, size_x + 1] = x_others[1][1]

    for a in range(3):
        padded[a, 0] = x_faces[0][a]
        padded[a, size_x + 1] = x_faces[1][a]

    def fill(x, carry):
        for a in range(3):
            padded[a, x + 1] = velocity_ref[a, plane(x), :]
        return carry

    lax.fori_loop(0, size_x, fill, 0, unroll=True)

    rest = {(1, 1): 0, (2, 2): 1, (1, 2): 2}

    def stress_plane(x, carry):
        along_x, along_y, along_z, centre = [], [], [], []
        for a in range(3):
            value = padded[a, x + 1]
            centre.append(value)
            along_x.append(padded[a, x + 2] - padded[a, x])
            along_y.append(
                difference_rows(value, y_low_ref[a, pl.ds(x, 1), :], y_high_ref[a, pl.ds(x, 1), :])
            )
            along_z.append(difference_z(value) + faces[a, x + 1] * at_end)
        slopes = (along_x, along_y, along_z)
        half = 0.5 * viscosity_ref[plane(x), :]
        for a, b in stress_pairs:
            value = half * (slopes[b][a] + slopes[a][b])
            if a == 0:
                stress_x[b, x + 1] = value
            else:
                stress_rest[rest[a, b], x] = value
        weight = (0.5 * faces[3, x + 1]) * at_end
        normal = [(faces[4 + a, x + 1] - centre[a]) * sign_z for a in range(3)]
        ghost_z[0, x] = weight * (normal[0] + (faces[2, x + 2] - faces[2, x]))
        ghost_z[1, x] = weight * (normal[1] + difference_rows(faces[2, x + 1]))
        ghost_z[2, x] = weight * (2.0 * normal[2])
        return carry

    lax.fori_loop(0, size_x, stress_plane, 0, unroll=6)

    for s in range(2):
        near, far, weight = x_faces[s][0:3], x_faces[s][3:6], 0.5 * x_faces[s][6]
        sign = -1.0 if s == 0 else 1.0
        normal = [(far[a] - padded[a, 1 if s == 0 else size_x]) * sign for a in range(3)]
        slope_y = difference_rows(near[0])
        slope_z = difference_z(near[0]) + x_others[s][0] * at_end
        at = 0 if s == 0 else size_x + 1
        stress_x[0, at] = weight * (2.0 * normal[0])
        stress_x[1, at] = weight * (normal[1] + slope_y)
        stress_x[2, at] = weight * (normal[2] + slope_z)
        for u in range(2):
            y, sign_y = (0, -1.0) if u == 0 else (size_y - 1, 1.0)
            number = 4 * s + 2 * u
            corner_ref[number : number + 1, :] = (0.5 * macro_step * sign * sign_y) * weight[y : y + 1, :]

    for u, ref in enumerate((y_low_ref, y_high_ref)):
        y, sign = (0, -1.0) if u == 0 else (size_y - 1, 1.0)
        weight = 0.5 * ref[6]
        normal = [
            (ref[3 + a] - velocity_ref[a, pl.ds(y, size_x, stride=size_y), :]) * sign for a in range(3)
        ]
        ghost_y[3 * u] = weight * (normal[0] + difference_rows(ref[1]))
        ghost_y[3 * u + 1] = weight * (2.0 * normal[1])
        ghost_y[3 * u + 2] = weight * (normal[2] + difference_z(ref[1]))
        for s in range(2):
            x, sign_x = (0, -1.0) if s == 0 else (size_x - 1, 1.0)
            number = 4 * s + 2 * u + 1
            corner_ref[number : number + 1, :] = (0.5 * macro_step * sign * sign_x) * weight[x : x + 1, :]
        wide = lanes_of((size_x, size_z))
        scale = jnp.where(wide == end, (0.5 * macro_step * sign) * sign_z, 0.0)
        edge_ref[2 * u] = scale * weight
        for x in range(size_x):
            edge_ref[2 * u + 1, x : x + 1, :] = scale[x : x + 1, :] * (0.5 * faces[3, x + 1, y : y + 1, :])

    columns = {(0, 1): (stress_x, 1, 1), (1, 1): (stress_rest, 0, 0), (2, 1): (stress_rest, 2, 0)}
    columns_z = {0: (stress_x, 2, 1), 1: (stress_rest, 2, 0), 2: (stress_rest, 1, 0)}

    def step_plane(x, carry):
        for a in range(3):
            total = stress_x[a, x + 2] - stress_x[a, x]
            ref, number, shift = columns[a, 1]
            total = total + difference_rows(
                ref[number, x + shift], ghost_y[a, pl.ds(x, 1), :], ghost_y[3 + a, pl.ds(x, 1), :]
            )
            ref, number, shift = columns_z[a]
            total = total + (difference_z(ref[number, x + shift]) + ghost_z[a, x])
            out_ref[a, plane(x), :] = padded[a, x + 1] + (0.5 * macro_step) * total
        return carry

    lax.fori_loop(0, size_x, step_plane, 0, unroll=6)


def flow_step(flag_cell, position, velocity, viscosity, chunks, y_low, y_high):
    size_x, size_y, size_z = viscosity.shape
    flags = flag_cell.shape[0]
    back_rows = chunks.shape[0] * (slot_rows + line_rows)
    row_count = size_x * size_y
    planes = (size_x, size_y, size_z)
    wide = (size_x + 2, size_y, size_z)
    return pl.pallas_call(
        functools.partial(flow_kernel, size_x, size_y, size_z, chunks.shape[0] // 2),
        out_shape=(
            jax.ShapeDtypeStruct((3, size_x * size_y, size_z), jnp.float32),
            jax.ShapeDtypeStruct((8, size_z), jnp.float32),
            jax.ShapeDtypeStruct((4, size_x, size_z), jnp.float32),
            jax.ShapeDtypeStruct((2, flags, size_z), jnp.float32),
            jax.ShapeDtypeStruct((flags, 3 * back_rows), jnp.bfloat16),
            jax.ShapeDtypeStruct((row_count, 3 * product_depth), jnp.bfloat16),
        ),
        in_specs=[SMEM] * 2 + [VMEM] * 5,
        out_specs=(VMEM,) * 6,
        scratch_shapes=[
            pltpu.VMEM((3, *wide), jnp.float32),
            pltpu.VMEM((3, *wide), jnp.float32),
            pltpu.VMEM((3, *planes), jnp.float32),
            pltpu.VMEM((item_count, *wide), jnp.float32),
            pltpu.VMEM((6, size_x, size_z), jnp.float32),
            pltpu.VMEM((3, *planes), jnp.float32),
            pltpu.VMEM((product_depth, -(-row_count // 128) * 128), jnp.float32),
        ],
        compiler_params=limit(12),
        cost_estimate=pl.CostEstimate(flops=4000000, bytes_accessed=3000000, transcendentals=0),
        name="flow_step",
    )(
        flag_cell, position,
        velocity.reshape(3, size_x * size_y, size_z),
        viscosity.reshape(size_x * size_y, size_z),
        chunks, y_low, y_high,
    )


def pieces(value):
    high = value.astype(jnp.bfloat16)
    rest = value - high.astype(jnp.float32)
    middle = rest.astype(jnp.bfloat16)
    return high, middle, (rest - middle.astype(jnp.float32)).astype(jnp.bfloat16)


def polymer_kernel(
    size_x, size_y, size_z, macro_count, chunk_ref, viscous_ref, corner_ref, edge_ref, lines_ref, pick_ref,
    spread_ref, partial_ref, out_ref, flag_ref, field, write_sem,
):
    flags = viscous_ref.shape[0]
    chunk_rows = slot_rows + line_rows
    macro, core = place_of()
    values = jnp.dot(
        pick_ref[...], jnp.concatenate(pieces(chunk_ref[...]), axis=0), preferred_element_type=jnp.float32
    )
    here, beside_z = lines_ref[0], lines_ref[1]
    columns = [jnp.broadcast_to(values[:, k : k + 1], (flags, size_z)) for k in range(6)]
    unused = jnp.zeros((product_depth - 3 * flags, size_z), jnp.float32)
    split = [
        pieces(
            jnp.concatenate(
                [
                    columns[pair_index(a, 0)] * here, columns[pair_index(a, 1)] * here,
                    columns[pair_index(a, 2)] * beside_z, unused,
                ],
                axis=0,
            )
        )
        for a in range(3)
    ]
    flag_ref[...] = (viscous_ref[...] + values).T[0:6, :]

    field[...] = partial_ref[...]
    for s in range(2):
        inside = macro > 0 if s == 0 else macro < macro_count - 1
        beside = jnp.maximum(macro - 1, 0) if s == 0 else jnp.minimum(macro + 1, macro_count - 1)
        start = (2 * beside + core) * chunk_rows + slot_rows
        x = 0 if s == 0 else size_x - 1
        for u in range(2):
            at = x * size_y + (0 if u == 0 else size_y - 1)
            for a in range(2):
                number = 4 * s + 2 * u + a
                line = corner_ref[number : number + 1, :] * chunk_ref[pl.ds(start + 2 * u + a, 1), :]
                field[1 - a, at : at + 1, :] += jnp.where(inside, line, 0.0)
    start = pl.multiple_of((2 * macro + 1 - core) * chunk_rows + slot_rows, 8)
    packed = chunk_ref[pl.ds(start, line_rows), :]
    end = jnp.where(core == 0, size_z - 1, 0)
    for u in range(2):
        y = 0 if u == 0 else size_y - 1
        for a in range(2):
            for i in range(size_x // 8):
                line = rolled(packed, end - (4 * i + 2 * u + a)) * edge_ref[2 * u + a, 8 * i : 8 * i + 8, :]
                at = pl.ds(8 * i * size_y + y, 8, stride=size_y)
                field[2 - a, at, :] += line
    copies = [pltpu.make_async_copy(field.at[a], out_ref.at[a], write_sem.at[a]) for a in range(3)]
    for a in range(3):
        field[a] += jnp.dot(
            spread_ref[...], jnp.concatenate(split[a], axis=0), preferred_element_type=jnp.float32
        )
        copies[a].start()
    for copy in copies:
        copy.wait()


def add_polymer(chunks, viscous, corners, edges, lines, pick, spread, partial, shape):
    flags = viscous.shape[0]
    size_x, size_y, size_z = shape
    return pl.pallas_call(
        functools.partial(polymer_kernel, size_x, size_y, size_z, chunks.shape[0] // 2),
        out_shape=(
            jax.ShapeDtypeStruct(partial.shape, jnp.float32),
            jax.ShapeDtypeStruct((6, flags), jnp.float32),
        ),
        in_specs=[VMEM] * 8,
        out_specs=(pl.BlockSpec(memory_space=pltpu.HBM), VMEM),
        scratch_shapes=[pltpu.VMEM(partial.shape, jnp.float32), pltpu.SemaphoreType.DMA((3,))],
        compiler_params=limit(8),
        cost_estimate=pl.CostEstimate(flops=400000, bytes_accessed=3000000, transcendentals=0),
        name="add_polymer",
    )(chunks.reshape(-1, 128), viscous, corners, edges, lines, pick, spread, partial)


def shards(velocity, viscosity, flag_cell, flag_owner, conformations, increments):
    macro_count = lax.axis_size("macro")
    tile_count = lax.axis_size("tile")
    assert lax.axis_size("micro") == 2
    owner_count = 2 * macro_count
    capacity = conformations.shape[1] // owner_count
    size_x, size_y, size_z = viscosity.shape
    assert capacity <= slot_rows and size_y == 8 and size_z == 128 and size_x % 8 == 0 and size_x <= 48
    chunks, position, viscous, y_first, y_last = gather_rows(
        flag_cell, flag_owner.reshape(-1), velocity, viscosity, capacity, owner_count
    )

    def exchange(rows):
        return lax.all_to_all(rows, ("macro", "micro"), split_axis=0, concat_axis=0, tiled=True)

    received = exchange(chunks.reshape(owner_count, -1, 128))
    up = [(i, i + 1) for i in range(tile_count - 1)]
    down = [(target, source) for source, target in up]
    y_low = lax.ppermute(y_last, "tile", up)
    y_high = lax.ppermute(y_first, "tile", down)
    first_conform, first_noise = first_block(position, conformations, increments)
    last_state, polymer = advance(
        conformations, increments, received, first_conform, first_noise, capacity
    )
    returned = exchange(add_lines(polymer, y_low, y_high))
    partial, corners, edges, lines, pick, spread = flow_step(
        flag_cell, position, velocity, viscosity, received, y_low, y_high
    )
    velocity_next, flag_stress = add_polymer(
        returned, viscous, corners, edges, lines, pick, spread, partial, viscosity.shape
    )
    return (velocity_next.reshape(velocity.shape), last_state, flag_stress)


def solution(mesh):
    in_specs = (
        P(None, "macro", "tile", "micro"),
        P("macro", "tile", "micro"),
        P(("macro", "tile", "micro")),
        P(("macro", "tile", "micro"), None),
        P(None, ("macro", "tile", "micro"), None),
        P(None, None, ("macro", "tile", "micro"), None),
    )
    out_specs = (
        P(None, "macro", "tile", "micro"),
        P(None, ("macro", "tile", "micro"), None),
        P(None, ("macro", "tile", "micro")),
    )
    return jax.shard_map(shards, mesh=mesh, in_specs=in_specs, out_specs=out_specs, check_vma=False)
```

```python
import functools

import jax
import jax.numpy as jnp
from jax import lax
from jax.experimental import pallas as pl
from jax.experimental.pallas import tpu as pltpu
from jax.sharding import PartitionSpec as P

stress_pairs = ((0, 0), (1, 1), (2, 2), (0, 1), (0, 2), (1, 2))
macro_step = 0.1
micro_step = 0.01
noise_weight = 0.1
relax_rate = 0.5
fene_extent = 30.0
spring_floor = 0.1
polymer_weight = 0.25

SMEM = pl.BlockSpec(memory_space=pltpu.SMEM)
VMEM = pl.BlockSpec(memory_space=pltpu.VMEM)


def pair_index(left_axis, right_axis):
    return stress_pairs.index((min(left_axis, right_axis), max(left_axis, right_axis)))


def lanes_of(shape):
    return lax.broadcasted_iota(jnp.int32, shape, len(shape) - 1)


slot_rows = 8
item_count = 7
line_rows = 8


def limit(mebibytes):
    return pltpu.CompilerParams(vmem_limit_bytes=mebibytes * 1024 * 1024)


def far(value):
    return pltpu.with_memory_space_constraint(value, pltpu.HBM)


def place_of():
    return lax.axis_index("macro"), lax.axis_index("micro")


def neighbour(index, side, count):
    return jnp.maximum(index - 1, 0) if side == 0 else jnp.minimum(index + 1, count - 1)


def rolled(value, amount):
    size = value.shape[-1]
    if isinstance(amount, int):
        return pltpu.roll(value, amount % size, value.ndim - 1)
    return pltpu.roll(value, lax.rem(amount + 2 * size, size), value.ndim - 1)


def gather_kernel(
    capacity, size_x, size_y, size_z, macro_count, cell_in, owner_in, velocity_in, viscosity_in,
    chunk_ref, position_ref, viscous_ref, face_ref,
    cell_ref, owner_ref, velocity_ref, viscosity_ref, masked, gradients, target, count, sems,
):
    flags = cell_ref.shape[0]
    copies = [
        pltpu.make_async_copy(source, into, sems.at[number])
        for number, (source, into) in enumerate(
            (
                (cell_in, cell_ref), (owner_in, owner_ref), (velocity_in, velocity_ref),
                (viscosity_in, viscosity_ref),
            )
        )
    ]
    for copy in copies:
        copy.start()
    chunk_rows = slot_rows + item_count * size_y
    macro, core = place_of()
    lane = lanes_of((1, size_z))

    for owner in range(count.shape[0]):
        count[owner] = 0
        chunk_ref[owner * chunk_rows : owner * chunk_rows + slot_rows, :] = jnp.zeros((slot_rows, 128), jnp.float32)
    for copy in copies[:2]:
        copy.wait()
    for j in range(flags):
        owner = owner_ref[j]
        rank = count[owner]
        count[owner] = rank + 1
        target[j] = owner * chunk_rows + rank
        position_ref[j] = owner * (slot_rows + line_rows) + rank
    for copy in copies[2:]:
        copy.wait()
    planes = velocity_ref.reshape(3, size_x, size_y, size_z)
    layers = viscosity_ref.reshape(size_x, size_y, size_z)
    for j in range(flags):
        cell = cell_ref[j]
        x = lax.shift_right_logical(cell, 10)
        y = lax.shift_right_logical(cell, 7) & (size_y - 1)
        z = cell & (size_z - 1)
        here = (lane == z).astype(jnp.float32)
        along_z = (lane == z + 1).astype(jnp.float32) - (lane == z - 1).astype(jnp.float32)
        at = pl.ds(y, 1)
        for a in range(3):
            along_x = planes[a, x + 1, at, :] - planes[a, x - 1, at, :]
            along_y = planes[a, x, pl.ds(y + 1, 1), :] - planes[a, x, pl.ds(y - 1, 1), :]
            masked[3 * a, j : j + 1, :] = along_x * here
            masked[3 * a + 1, j : j + 1, :] = along_y * here
            masked[3 * a + 2, j : j + 1, :] = planes[a, x, at, :] * along_z
        masked[9, j : j + 1, :] = layers[x, at, :] * here

    tile, tile_count = lax.axis_index("tile"), face_ref.shape[0]
    for side in range(2):
        into = neighbour(tile, side, tile_count)
        for layer in range(2):
            y = layer if side == 0 else size_y - 1 - layer
            for a in range(3):
                face_ref[into, 3 * layer + a] = velocity_ref[a, pl.ds(y, size_x, stride=size_y), :]
        y = 0 if side == 0 else size_y - 1
        face_ref[into, 6] = viscosity_ref[pl.ds(y, size_x, stride=size_y), :]

    for side in range(2):
        beside = neighbour(macro, side, macro_count)
        first = pl.multiple_of((2 * beside + core) * chunk_rows + slot_rows, 8)
        other = pl.multiple_of((2 * beside + 1 - core) * chunk_rows + slot_rows, 8)
        for layer in range(2):
            x = layer if side == 0 else size_x - 1 - layer
            for a in range(3):
                chunk_ref[pl.ds(first + (3 * layer + a) * size_y, size_y), :] = velocity_ref[
                    a, x * size_y : (x + 1) * size_y, :
                ]
        x = 0 if side == 0 else size_x - 1
        chunk_ref[pl.ds(first + 6 * size_y, size_y), :] = viscosity_ref[x * size_y : (x + 1) * size_y, :]
        for number, a in enumerate((0, 2)):
            chunk_ref[pl.ds(other + number * size_y, size_y), :] = velocity_ref[
                a, x * size_y : (x + 1) * size_y, :
            ]

    group = size_z // 8
    lane2 = lanes_of((size_y, size_z))
    first = pl.multiple_of((2 * macro + 1 - core) * chunk_rows + slot_rows, 8)
    source = jnp.where(core == 0, size_z - 2, 0)
    for block in range(-(-size_x // group)):
        total = jnp.zeros((size_y, size_z), jnp.float32)
        for x in range(block * group, min(size_x, (block + 1) * group)):
            rows = slice(x * size_y, (x + 1) * size_y)
            for a in range(4):
                at = 8 * (x - block * group) + 2 * a
                value = viscosity_ref[rows, :] if a == 3 else velocity_ref[a, rows, :]
                total = jnp.where((lane2 == at) | (lane2 == at + 1), rolled(value, at - source), total)
        chunk_ref[pl.ds(first + block * size_y, size_y), :] = total

    columns = [0.5 * jnp.sum(masked[c], axis=1, keepdims=True) for c in range(9)]
    viscous = jnp.sum(masked[9], axis=1, keepdims=True)
    wide = lanes_of((flags, 128))
    packed = jnp.zeros((flags, 128), jnp.float32)
    for c in range(9):
        packed = jnp.where(wide == c, columns[c], packed)
    gradients[...] = packed
    stress = jnp.zeros((flags, 128), jnp.float32)
    for k, (a, b) in enumerate(stress_pairs):
        stress = jnp.where(wide == k, viscous * (columns[3 * a + b] + columns[3 * b + a]), stress)
    viscous_ref[...] = stress

    for j in range(flags):
        chunk_ref[pl.ds(target[j], 1), :] = gradients[j : j + 1, :]


def gather_rows(flag_cell, owner, velocity, viscosity, capacity, owner_count, tile_count):
    size_x, size_y, size_z = viscosity.shape
    flags = flag_cell.shape[0]
    chunk_rows = slot_rows + item_count * size_y
    return pl.pallas_call(
        functools.partial(gather_kernel, capacity, size_x, size_y, size_z, owner_count // 2),
        out_shape=(
            jax.ShapeDtypeStruct((owner_count * chunk_rows, 128), jnp.float32),
            jax.ShapeDtypeStruct((flags,), jnp.int32),
            jax.ShapeDtypeStruct((flags, 128), jnp.float32),
            jax.ShapeDtypeStruct((tile_count, item_count, size_x, size_z), jnp.float32),
        ),
        in_specs=[pl.BlockSpec(memory_space=pltpu.HBM)] * 4,
        out_specs=(VMEM, SMEM, VMEM, VMEM),
        scratch_shapes=[
            pltpu.SMEM((flags,), jnp.int32),
            pltpu.SMEM((flags,), jnp.int32),
            pltpu.VMEM((3, size_x * size_y, size_z), jnp.float32),
            pltpu.VMEM((size_x * size_y, size_z), jnp.float32),
            pltpu.VMEM((10, flags, size_z), jnp.float32),
            pltpu.VMEM((flags, 128), jnp.float32),
            pltpu.SMEM((flags,), jnp.int32),
            pltpu.SMEM((owner_count,), jnp.int32),
            pltpu.SemaphoreType.DMA((4,)),
        ],
        compiler_params=limit(8),
        cost_estimate=pl.CostEstimate(flops=400000, bytes_accessed=3000000, transcendentals=0),
        name="gather_rows",
    )(
        far(flag_cell),
        far(owner),
        far(velocity.reshape(3, size_x * size_y, size_z)),
        far(viscosity.reshape(size_x * size_y, size_z)),
    )


def micro_kernel(
    capacity, parts, rows, groups, conform_ref, noise_ref, rate_ref, first_conform_ref, first_noise_ref,
    next_ref, chunk_ref, conform, noise, rate, rate_wide, sums_ref, read_sem, noise_sem,
):
    steps, _, slots, dumbbells = noise_ref.shape
    blocks = slots // rows
    span = steps // groups
    width = dumbbells // parts
    owners = slots // capacity
    scale = 1.0 / noise_weight
    extent = fene_extent * scale * scale

    def block_rows(block):
        return pl.ds(pl.multiple_of(block * rows, rows), rows)

    def read(block):
        at = block_rows(block)
        return pltpu.make_async_copy(conform_ref.at[:, at, :], conform.at[:, at, :], read_sem.at[block])

    def read_noise(block, group):
        at, when = block_rows(block), pl.ds(group * span, span)
        return pltpu.make_async_copy(
            noise_ref.at[when, :, at, :], noise.at[when, :, at, :], noise_sem.at[block, group]
        )

    pieces = [
        (half, slice(part * width, (part + 1) * width)) for half in range(rows // 16) for part in range(parts)
    ]
    assert len(pieces) == 8
    early = groups // first_share
    for block in range(blocks):
        if block > 0:
            read(block).start()
        for group in range(early if block == 0 else 0, groups):
            read_noise(block, group).start()
    conform[:, 0:rows, :] = first_conform_ref[...]
    for step in range(steps // first_share):
        noise[step, :, 0:rows, :] = first_noise_ref[step]
    for owner in range(owners):
        rate[owner * capacity : (owner + 1) * capacity, :] = rate_ref[owner, 0:capacity, :]
        chunk_ref[owner] = jnp.zeros(chunk_ref.shape[1:], jnp.float32)
    for a in range(3):
        for b in range(3):
            column = micro_step * rate[:, 3 * a + b : 3 * a + b + 1] + (1.0 if a == b else 0.0)
            rate_wide[3 * a + b] = jnp.broadcast_to(column, (slots, width))

    def inverses(state, scale):
        rooms = []
        for piece in range(len(pieces)):
            q = state[3 * piece : 3 * piece + 3]
            room = (extent - q[0] * q[0]) - (q[1] * q[1] + q[2] * q[2])
            rooms.append(jnp.maximum(room, extent * spring_floor))
        levels = [rooms]
        while len(levels[-1]) > 1:
            levels.append([low * high for low, high in zip(levels[-1][0::2], levels[-1][1::2])])
        result = [scale * pl.reciprocal(levels[-1][0])]
        for level in reversed(levels[:-1]):
            result = [result[i // 2] * level[i ^ 1] for i in range(len(level))]
        return result

    def advance_block(block, carry):
        ats = [pl.ds(pl.multiple_of(block * rows + 16 * half, 16), 16) for half in range(rows // 16)]
        rates = [
            [[rate_wide.at[3 * a + b, at, :] for b in range(3)] for a in range(3)] for at in ats
        ]

        def substep(step, state):
            updated = []
            springs = inverses(state, micro_step * relax_rate * extent)
            for piece, (half, lanes) in enumerate(pieces):
                q = state[3 * piece : 3 * piece + 3]
                table = rates[half]
                for a in range(3):
                    b, c = [other for other in range(3) if other != a]
                    kick = noise[step, a, ats[half], lanes].astype(jnp.float32)
                    rest = (table[a][b][...] * q[b] + table[a][c][...] * q[c]) + kick
                    updated.append((table[a][a][...] - springs[piece]) * q[a] + rest)
            return tuple(updated)

        def advance_group(group, state):
            if group < early:

                @pl.when(block > 0)
                def _():
                    read_noise(block, group).wait()

            else:
                read_noise(block, group).wait()
            for step in range(span):
                state = substep(group * span + step, state)
            return state

        @pl.when(block > 0)
        def _():
            read(block).wait()

        state = tuple(conform[a, ats[half], lanes] * scale for half, lanes in pieces for a in range(3))
        for group in range(groups):
            state = advance_group(group, state)
        inverse = inverses(state, 1.0)
        for half, at in enumerate(ats):
            sums = [None] * 6
            for piece, (other, lanes) in enumerate(pieces):
                if other != half:
                    continue
                q = state[3 * piece : 3 * piece + 3]
                for a in range(3):
                    next_ref[a, at, lanes] = q[a] * noise_weight
                for k, (a, b) in enumerate(stress_pairs):
                    term = (inverse[piece] * q[a]) * q[b]
                    sums[k] = term if sums[k] is None else sums[k] + term
            for k in range(6):
                sums_ref[k, at, :] = sums[k]
        return carry

    lax.fori_loop(0, blocks, advance_block, 0)
    lane = lanes_of((slots, 128))
    packed = jnp.zeros((slots, 128), jnp.float32)
    weight = extent * noise_weight * noise_weight / dumbbells
    for k, (a, b) in enumerate(stress_pairs):
        mean = jnp.sum(sums_ref[k], axis=1, keepdims=True) * weight
        packed = jnp.where(lane == k, polymer_weight * (mean - (1.0 if a == b else 0.0)), packed)
    for owner in range(owners):
        chunk_ref[owner, 0:capacity, :] = packed[owner * capacity : (owner + 1) * capacity]


block_slots = 32
first_share = 2


def first_kernel(rows, after_ref, conform_ref, noise_ref, conform_out, noise_out, sems):
    copies = (
        pltpu.make_async_copy(conform_ref.at[:, 0:rows, :], conform_out, sems.at[0]),
        pltpu.make_async_copy(noise_ref.at[0 : noise_out.shape[0], :, 0:rows, :], noise_out, sems.at[1]),
    )
    for copy in copies:
        copy.start()
    for copy in copies:
        copy.wait()


def first_block(after, conformations, increments):
    steps, _, _, dumbbells = increments.shape
    whole = pl.BlockSpec(memory_space=pltpu.HBM)
    return pl.pallas_call(
        functools.partial(first_kernel, block_slots),
        out_shape=(
            pltpu.VMEM((3, block_slots, dumbbells), jnp.float32),
            pltpu.VMEM((steps // first_share, 3, block_slots, dumbbells), jnp.bfloat16),
        ),
        in_specs=[pl.BlockSpec(memory_space=pl.ANY), whole, whole],
        out_specs=(VMEM, VMEM),
        scratch_shapes=[pltpu.SemaphoreType.DMA((2,))],
        compiler_params=limit(4),
        cost_estimate=pl.CostEstimate(flops=0, bytes_accessed=3000000, transcendentals=0),
        name="first_block",
    )(after, far(conformations), far(increments))


def advance(conformations, increments, chunks, first_conform, first_noise, capacity):
    slots, dumbbells = conformations.shape[1:]
    steps = increments.shape[0]
    owners = slots // capacity
    rows, parts, groups = block_slots, 4, 4
    blocks = slots // rows
    whole = pl.BlockSpec(memory_space=pltpu.HBM)
    return pl.pallas_call(
        functools.partial(micro_kernel, capacity, parts, rows, groups),
        out_shape=(
            pltpu.VMEM(conformations.shape, jnp.float32),
            jax.ShapeDtypeStruct((owners, slot_rows + line_rows, 128), jnp.float32),
        ),
        in_specs=[whole, whole, VMEM, VMEM, VMEM],
        out_specs=(VMEM, VMEM),
        scratch_shapes=[
            pltpu.VMEM(conformations.shape, jnp.float32),
            pltpu.VMEM(increments.shape, jnp.bfloat16),
            pltpu.VMEM((slots, 128), jnp.float32),
            pltpu.VMEM((9, slots, dumbbells // parts), jnp.float32),
            pltpu.VMEM((6, slots, dumbbells // parts), jnp.float32),
            pltpu.SemaphoreType.DMA((blocks,)),
            pltpu.SemaphoreType.DMA((blocks, groups)),
        ],
        compiler_params=limit(12),
        cost_estimate=pl.CostEstimate(flops=20000000, bytes_accessed=5000000, transcendentals=600000),
        name="advance",
    )(far(conformations), far(increments), chunks, first_conform, first_noise)


def lines_kernel(macro_count, chunk_ref, face_ref, out_ref, y_low_ref, y_high_ref):
    out_ref[...] = chunk_ref[...]
    macro, core = place_of()
    tile, tile_count = lax.axis_index("tile"), face_ref.shape[0]
    inside = (tile > 0, tile < tile_count - 1)
    sides = (y_low_ref, y_high_ref)
    for u in range(2):
        at = neighbour(tile, u, tile_count)
        for i in range(item_count):
            sides[u][i] = jnp.where(inside[u], face_ref[at, i], 0.0)
    size_x, size_z = y_low_ref.shape[1:]
    for side in range(2):
        beside = neighbour(macro, side, macro_count)
        x = 0 if side == 0 else size_x - 1
        for u in range(2):
            for a in range(2):
                at = slot_rows + 2 * u + a
                out_ref[2 * beside + core, at : at + 1, :] = sides[u][a, x : x + 1, :]

    lane = lanes_of((8, size_z))
    source = jnp.where(core == 0, size_z - 1, 0)
    total = jnp.zeros((8, size_z), jnp.float32)
    for i in range(size_x // 8):
        for u in range(2):
            for a in range(2):
                at = 4 * i + 2 * u + a
                total = jnp.where(
                    lane == at, rolled(sides[u][1 + a, 8 * i : 8 * i + 8, :], at - source), total
                )
    out_ref[2 * macro + 1 - core, slot_rows:, :] = total


def add_lines(chunks, faces):
    face = jax.ShapeDtypeStruct(faces.shape[1:], jnp.float32)
    return pl.pallas_call(
        functools.partial(lines_kernel, chunks.shape[0] // 2),
        out_shape=(jax.ShapeDtypeStruct(chunks.shape, jnp.float32), face, face),
        in_specs=[VMEM, VMEM],
        out_specs=(VMEM, VMEM, VMEM),
        compiler_params=limit(4),
        cost_estimate=pl.CostEstimate(flops=20000, bytes_accessed=400000, transcendentals=0),
        name="add_lines",
    )(chunks, faces)


product_depth = 128


def one_hots(size_y, size_z, cell_ref, position_ref, lines_ref, pick_ref, spread_ref, rows):
    flags = cell_ref.shape[0]
    weight = 0.5 * macro_step
    row_count = spread_ref.shape[0]
    back_rows = pick_ref.shape[1] // 3
    lane = lanes_of((1, size_z))
    row_lane = lanes_of((1, rows.shape[1]))
    slot_lane = lanes_of((flags, back_rows))
    flag_row = lax.broadcasted_iota(jnp.int32, (flags, back_rows), 0)
    rows[3 * flags :, :] = jnp.zeros((product_depth - 3 * flags, rows.shape[1]), jnp.float32)
    slot = jnp.zeros((flags, back_rows), jnp.int32)
    for j in range(flags):
        cell = cell_ref[j]
        row = lax.div(cell, size_z)
        z = cell - row * size_z
        lines_ref[0, j : j + 1, :] = jnp.where(lane == z, weight, 0.0)
        lines_ref[1, j : j + 1, :] = jnp.where(
            lane == z - 1, weight, jnp.where(lane == z + 1, -weight, 0.0)
        )
        for number, shift in enumerate((size_y, 1)):
            rows[number * flags + j : number * flags + j + 1, :] = jnp.where(
                row_lane == row - shift, 1.0, jnp.where(row_lane == row + shift, -1.0, 0.0)
            )
        rows[2 * flags + j : 2 * flags + j + 1, :] = jnp.where(row_lane == row, 1.0, 0.0)
        slot = jnp.where(flag_row == j, position_ref[j], slot)
    spread = rows[...].T[:row_count].astype(jnp.bfloat16)
    pick = jnp.where(slot_lane == slot, 1.0, 0.0).astype(jnp.bfloat16)
    for piece in range(3):
        spread_ref[:, piece * product_depth : (piece + 1) * product_depth] = spread
        pick_ref[:, piece * back_rows : (piece + 1) * back_rows] = pick


def flow_kernel(
    size_x, size_y, size_z, macro_count, cell_ref, position_ref, velocity_ref, viscosity_ref, chunk_ref,
    y_low_ref, y_high_ref, out_ref, corner_ref, edge_ref, lines_ref, pick_ref, spread_ref,
    padded, stress_x, stress_rest, faces, ghost_y, ghost_z, rows,
):
    macro, core = place_of()
    one_hots(size_y, size_z, cell_ref, position_ref, lines_ref, pick_ref, spread_ref, rows)
    inside = (macro > 0, macro < macro_count - 1)
    sign_z = jnp.where(core == 0, 1.0, -1.0)
    end = jnp.where(core == 0, size_z - 1, 0)
    shape = (size_y, size_z)
    lane, row = lanes_of(shape), lax.broadcasted_iota(jnp.int32, shape, 0)
    at_end = jnp.where(lane == end, sign_z, 0.0)

    def kept(value, condition):
        return jnp.where(condition, value, 0.0)

    def plane(x):
        return pl.ds(pl.multiple_of(x * size_y, 8), size_y)

    def difference_z(value):
        lane = lanes_of(value.shape)
        return jnp.where(lane == size_z - 1, 0.0, rolled(value, -1)) - jnp.where(
            lane == 0, 0.0, rolled(value, 1)
        )

    def difference_rows(value, low=0.0, high=0.0):
        count = value.shape[0]
        row = lax.broadcasted_iota(jnp.int32, value.shape, 0)
        return jnp.where(row == count - 1, high, pltpu.roll(value, count - 1, 0)) - jnp.where(
            row == 0, low, pltpu.roll(value, 1, 0)
        )

    x_faces, x_others = [], []
    for s in range(2):
        beside = jnp.maximum(macro - 1, 0) if s == 0 else jnp.minimum(macro + 1, macro_count - 1)
        x_faces.append(
            [
                kept(chunk_ref[2 * beside + core, slot_rows + i * size_y : slot_rows + (i + 1) * size_y, :], inside[s])
                for i in range(item_count)
            ]
        )
        x_others.append(
            [
                kept(
                    rolled(
                        chunk_ref[
                            2 * beside + 1 - core, slot_rows + i * size_y : slot_rows + (i + 1) * size_y, :
                        ],
                        2 * end + 1,
                    ),
                    inside[s],
                )
                for i in range(2)
            ]
        )

    group = size_z // 8
    packed = [
        chunk_ref[2 * macro + 1 - core, slot_rows + i * size_y : slot_rows + (i + 1) * size_y, :]
        for i in range(-(-size_x // group))
    ]
    for i, value in enumerate(packed):

        def unpack(x, carry):
            for q in range(item_count):
                a, layer = (q, 0) if q < 4 else (q - 4, 1)
                at = 8 * (x - i * group) + 2 * a + (core if layer == 0 else 1 - core)
                faces[q, x + 1] = rolled(value, end - at)
            return carry

        lax.fori_loop(i * group, min(size_x, (i + 1) * group), unpack, 0, unroll=8)
    faces[2, 0] = x_others[0][1]
    faces[2, size_x + 1] = x_others[1][1]

    for a in range(3):
        padded[a, 0] = x_faces[0][a]
        padded[a, size_x + 1] = x_faces[1][a]

    def fill(x, carry):
        for a in range(3):
            padded[a, x + 1] = velocity_ref[a, plane(x), :]
        return carry

    lax.fori_loop(0, size_x, fill, 0, unroll=True)

    rest = {(1, 1): 0, (2, 2): 1, (1, 2): 2}

    def stress_plane(x, carry):
        along_x, along_y, along_z, centre = [], [], [], []
        for a in range(3):
            value = padded[a, x + 1]
            centre.append(value)
            along_x.append(padded[a, x + 2] - padded[a, x])
            along_y.append(
                difference_rows(value, y_low_ref[a, pl.ds(x, 1), :], y_high_ref[a, pl.ds(x, 1), :])
            )
            along_z.append(difference_z(value) + faces[a, x + 1] * at_end)
        slopes = (along_x, along_y, along_z)
        half = 0.5 * viscosity_ref[plane(x), :]
        for a, b in stress_pairs:
            value = half * (slopes[b][a] + slopes[a][b])
            if a == 0:
                stress_x[b, x + 1] = value
            else:
                stress_rest[rest[a, b], x] = value
        weight = (0.5 * faces[3, x + 1]) * at_end
        normal = [(faces[4 + a, x + 1] - centre[a]) * sign_z for a in range(3)]
        ghost_z[0, x] = weight * (normal[0] + (faces[2, x + 2] - faces[2, x]))
        ghost_z[1, x] = weight * (normal[1] + difference_rows(faces[2, x + 1]))
        ghost_z[2, x] = weight * (2.0 * normal[2])
        return carry

    lax.fori_loop(0, size_x, stress_plane, 0, unroll=6)

    for s in range(2):
        near, far, weight = x_faces[s][0:3], x_faces[s][3:6], 0.5 * x_faces[s][6]
        sign = -1.0 if s == 0 else 1.0
        normal = [(far[a] - padded[a, 1 if s == 0 else size_x]) * sign for a in range(3)]
        slope_y = difference_rows(near[0])
        slope_z = difference_z(near[0]) + x_others[s][0] * at_end
        at = 0 if s == 0 else size_x + 1
        stress_x[0, at] = weight * (2.0 * normal[0])
        stress_x[1, at] = weight * (normal[1] + slope_y)
        stress_x[2, at] = weight * (normal[2] + slope_z)
        for u in range(2):
            y, sign_y = (0, -1.0) if u == 0 else (size_y - 1, 1.0)
            number = 4 * s + 2 * u
            corner_ref[number : number + 1, :] = (0.5 * macro_step * sign * sign_y) * weight[y : y + 1, :]

    for u, ref in enumerate((y_low_ref, y_high_ref)):
        y, sign = (0, -1.0) if u == 0 else (size_y - 1, 1.0)
        weight = 0.5 * ref[6]
        normal = [
            (ref[3 + a] - velocity_ref[a, pl.ds(y, size_x, stride=size_y), :]) * sign for a in range(3)
        ]
        ghost_y[3 * u] = weight * (normal[0] + difference_rows(ref[1]))
        ghost_y[3 * u + 1] = weight * (2.0 * normal[1])
        ghost_y[3 * u + 2] = weight * (normal[2] + difference_z(ref[1]))
        for s in range(2):
            x, sign_x = (0, -1.0) if s == 0 else (size_x - 1, 1.0)
            number = 4 * s + 2 * u + 1
            corner_ref[number : number + 1, :] = (0.5 * macro_step * sign * sign_x) * weight[x : x + 1, :]
        wide = lanes_of((size_x, size_z))
        scale = jnp.where(wide == end, (0.5 * macro_step * sign) * sign_z, 0.0)
        edge_ref[2 * u] = scale * weight
        for x in range(size_x):
            edge_ref[2 * u + 1, x : x + 1, :] = scale[x : x + 1, :] * (0.5 * faces[3, x + 1, y : y + 1, :])

    columns = {(0, 1): (stress_x, 1, 1), (1, 1): (stress_rest, 0, 0), (2, 1): (stress_rest, 2, 0)}
    columns_z = {0: (stress_x, 2, 1), 1: (stress_rest, 2, 0), 2: (stress_rest, 1, 0)}

    def step_plane(x, carry):
        for a in range(3):
            total = stress_x[a, x + 2] - stress_x[a, x]
            ref, number, shift = columns[a, 1]
            total = total + difference_rows(
                ref[number, x + shift], ghost_y[a, pl.ds(x, 1), :], ghost_y[3 + a, pl.ds(x, 1), :]
            )
            ref, number, shift = columns_z[a]
            total = total + (difference_z(ref[number, x + shift]) + ghost_z[a, x])
            out_ref[a, plane(x), :] = padded[a, x + 1] + (0.5 * macro_step) * total
        return carry

    lax.fori_loop(0, size_x, step_plane, 0, unroll=6)


def flow_step(flag_cell, position, velocity, viscosity, chunks, y_low, y_high):
    size_x, size_y, size_z = viscosity.shape
    flags = flag_cell.shape[0]
    back_rows = chunks.shape[0] * (slot_rows + line_rows)
    row_count = size_x * size_y
    planes = (size_x, size_y, size_z)
    wide = (size_x + 2, size_y, size_z)
    return pl.pallas_call(
        functools.partial(flow_kernel, size_x, size_y, size_z, chunks.shape[0] // 2),
        out_shape=(
            jax.ShapeDtypeStruct((3, size_x * size_y, size_z), jnp.float32),
            jax.ShapeDtypeStruct((8, size_z), jnp.float32),
            jax.ShapeDtypeStruct((4, size_x, size_z), jnp.float32),
            jax.ShapeDtypeStruct((2, flags, size_z), jnp.float32),
            jax.ShapeDtypeStruct((flags, 3 * back_rows), jnp.bfloat16),
            jax.ShapeDtypeStruct((row_count, 3 * product_depth), jnp.bfloat16),
        ),
        in_specs=[SMEM] * 2 + [VMEM] * 5,
        out_specs=(VMEM,) * 6,
        scratch_shapes=[
            pltpu.VMEM((3, *wide), jnp.float32),
            pltpu.VMEM((3, *wide), jnp.float32),
            pltpu.VMEM((3, *planes), jnp.float32),
            pltpu.VMEM((item_count, *wide), jnp.float32),
            pltpu.VMEM((6, size_x, size_z), jnp.float32),
            pltpu.VMEM((3, *planes), jnp.float32),
            pltpu.VMEM((product_depth, -(-row_count // 128) * 128), jnp.float32),
        ],
        compiler_params=limit(12),
        cost_estimate=pl.CostEstimate(flops=4000000, bytes_accessed=3000000, transcendentals=0),
        name="flow_step",
    )(
        flag_cell, position,
        velocity.reshape(3, size_x * size_y, size_z),
        viscosity.reshape(size_x * size_y, size_z),
        chunks, y_low, y_high,
    )


def pieces(value):
    high = value.astype(jnp.bfloat16)
    rest = value - high.astype(jnp.float32)
    middle = rest.astype(jnp.bfloat16)
    return high, middle, (rest - middle.astype(jnp.float32)).astype(jnp.bfloat16)


def polymer_kernel(
    size_x, size_y, size_z, macro_count, chunk_ref, viscous_ref, corner_ref, edge_ref, lines_ref, pick_ref,
    spread_ref, partial_ref, out_ref, flag_ref, field, write_sem,
):
    flags = viscous_ref.shape[0]
    chunk_rows = slot_rows + line_rows
    macro, core = place_of()
    values = jnp.dot(
        pick_ref[...], jnp.concatenate(pieces(chunk_ref[...]), axis=0), preferred_element_type=jnp.float32
    )
    here, beside_z = lines_ref[0], lines_ref[1]
    columns = [jnp.broadcast_to(values[:, k : k + 1], (flags, size_z)) for k in range(6)]
    unused = jnp.zeros((product_depth - 3 * flags, size_z), jnp.float32)
    split = [
        pieces(
            jnp.concatenate(
                [
                    columns[pair_index(a, 0)] * here, columns[pair_index(a, 1)] * here,
                    columns[pair_index(a, 2)] * beside_z, unused,
                ],
                axis=0,
            )
        )
        for a in range(3)
    ]
    flag_ref[...] = (viscous_ref[...] + values).T[0:6, :]

    field[...] = partial_ref[...]
    for s in range(2):
        inside = macro > 0 if s == 0 else macro < macro_count - 1
        beside = jnp.maximum(macro - 1, 0) if s == 0 else jnp.minimum(macro + 1, macro_count - 1)
        start = (2 * beside + core) * chunk_rows + slot_rows
        x = 0 if s == 0 else size_x - 1
        for u in range(2):
            at = x * size_y + (0 if u == 0 else size_y - 1)
            for a in range(2):
                number = 4 * s + 2 * u + a
                line = corner_ref[number : number + 1, :] * chunk_ref[pl.ds(start + 2 * u + a, 1), :]
                field[1 - a, at : at + 1, :] += jnp.where(inside, line, 0.0)
    start = pl.multiple_of((2 * macro + 1 - core) * chunk_rows + slot_rows, 8)
    packed = chunk_ref[pl.ds(start, line_rows), :]
    end = jnp.where(core == 0, size_z - 1, 0)
    for u in range(2):
        y = 0 if u == 0 else size_y - 1
        for a in range(2):
            for i in range(size_x // 8):
                line = rolled(packed, end - (4 * i + 2 * u + a)) * edge_ref[2 * u + a, 8 * i : 8 * i + 8, :]
                at = pl.ds(8 * i * size_y + y, 8, stride=size_y)
                field[2 - a, at, :] += line
    copies = [pltpu.make_async_copy(field.at[a], out_ref.at[a], write_sem.at[a]) for a in range(3)]
    for a in range(3):
        field[a] += jnp.dot(
            spread_ref[...], jnp.concatenate(split[a], axis=0), preferred_element_type=jnp.float32
        )
        copies[a].start()
    for copy in copies:
        copy.wait()


def add_polymer(chunks, viscous, corners, edges, lines, pick, spread, partial, shape):
    flags = viscous.shape[0]
    size_x, size_y, size_z = shape
    return pl.pallas_call(
        functools.partial(polymer_kernel, size_x, size_y, size_z, chunks.shape[0] // 2),
        out_shape=(
            jax.ShapeDtypeStruct(partial.shape, jnp.float32),
            jax.ShapeDtypeStruct((6, flags), jnp.float32),
        ),
        in_specs=[VMEM] * 8,
        out_specs=(pl.BlockSpec(memory_space=pltpu.HBM), VMEM),
        scratch_shapes=[pltpu.VMEM(partial.shape, jnp.float32), pltpu.SemaphoreType.DMA((3,))],
        compiler_params=limit(8),
        cost_estimate=pl.CostEstimate(flops=400000, bytes_accessed=3000000, transcendentals=0),
        name="add_polymer",
    )(chunks.reshape(-1, 128), viscous, corners, edges, lines, pick, spread, partial)


def shards(velocity, viscosity, flag_cell, flag_owner, conformations, increments):
    macro_count = lax.axis_size("macro")
    tile_count = lax.axis_size("tile")
    assert lax.axis_size("micro") == 2
    owner_count = 2 * macro_count
    capacity = conformations.shape[1] // owner_count
    size_x, size_y, size_z = viscosity.shape
    assert capacity <= slot_rows and size_y == 8 and size_z == 128 and size_x % 8 == 0 and size_x <= 48
    chunks, position, viscous, faces = gather_rows(
        flag_cell, flag_owner.reshape(-1), velocity, viscosity, capacity, owner_count, tile_count
    )

    def exchange(rows, axes):
        return lax.all_to_all(rows, axes, split_axis=0, concat_axis=0, tiled=True)

    owners = ("macro", "micro")
    received = exchange(chunks.reshape(owner_count, -1, 128), owners)
    faces = exchange(faces, "tile")
    first_conform, first_noise = first_block(position, conformations, increments)
    last_state, polymer = advance(
        conformations, increments, received, first_conform, first_noise, capacity
    )
    polymer, y_low, y_high = add_lines(polymer, faces)
    returned = exchange(polymer, owners)
    partial, corners, edges, lines, pick, spread = flow_step(
        flag_cell, position, velocity, viscosity, received, y_low, y_high
    )
    velocity_next, flag_stress = add_polymer(
        returned, viscous, corners, edges, lines, pick, spread, partial, viscosity.shape
    )
    return (velocity_next.reshape(velocity.shape), last_state, flag_stress)


def solution(mesh):
    in_specs = (
        P(None, "macro", "tile", "micro"),
        P("macro", "tile", "micro"),
        P(("macro", "tile", "micro")),
        P(("macro", "tile", "micro"), None),
        P(None, ("macro", "tile", "micro"), None),
        P(None, None, ("macro", "tile", "micro"), None),
    )
    out_specs = (
        P(None, "macro", "tile", "micro"),
        P(None, ("macro", "tile", "micro"), None),
        P(None, ("macro", "tile", "micro")),
    )
    return jax.shard_map(shards, mesh=mesh, in_specs=in_specs, out_specs=out_specs, check_vma=False)
```

```python
import functools

import jax
import jax.numpy as jnp
from jax import lax
from jax.experimental import pallas as pl
from jax.experimental.pallas import tpu as pltpu
from jax.sharding import PartitionSpec as P

stress_pairs = ((0, 0), (1, 1), (2, 2), (0, 1), (0, 2), (1, 2))
macro_step = 0.1
micro_step = 0.01
noise_weight = 0.1
relax_rate = 0.5
fene_extent = 30.0
spring_floor = 0.1
polymer_weight = 0.25

SMEM = pl.BlockSpec(memory_space=pltpu.SMEM)
VMEM = pl.BlockSpec(memory_space=pltpu.VMEM)


def pair_index(left_axis, right_axis):
    return stress_pairs.index((min(left_axis, right_axis), max(left_axis, right_axis)))


def lanes_of(shape):
    return lax.broadcasted_iota(jnp.int32, shape, len(shape) - 1)


slot_rows = 8
item_count = 7
line_rows = 8


def limit(mebibytes):
    return pltpu.CompilerParams(vmem_limit_bytes=mebibytes * 1024 * 1024)


def far(value):
    return pltpu.with_memory_space_constraint(value, pltpu.HBM)


def place_of():
    return lax.axis_index("macro"), lax.axis_index("micro")


def neighbour(index, side, count):
    return jnp.maximum(index - 1, 0) if side == 0 else jnp.minimum(index + 1, count - 1)


def rolled(value, amount):
    size = value.shape[-1]
    if isinstance(amount, int):
        return pltpu.roll(value, amount % size, value.ndim - 1)
    return pltpu.roll(value, lax.rem(amount + 2 * size, size), value.ndim - 1)


def gather_kernel(
    capacity, size_x, size_y, size_z, macro_count, cell_in, owner_in, velocity_in, viscosity_in,
    chunk_ref, position_ref, viscous_ref, y_low_ref, y_high_ref,
    cell_ref, owner_ref, velocity_ref, viscosity_ref, masked, gradients, target, count, sems,
):
    flags = cell_ref.shape[0]
    copies = [
        pltpu.make_async_copy(source, into, sems.at[number])
        for number, (source, into) in enumerate(
            (
                (cell_in, cell_ref), (owner_in, owner_ref), (velocity_in, velocity_ref),
                (viscosity_in, viscosity_ref),
            )
        )
    ]
    for copy in copies:
        copy.start()
    chunk_rows = slot_rows + item_count * size_y
    macro, core = place_of()
    lane = lanes_of((1, size_z))

    for owner in range(count.shape[0]):
        count[owner] = 0
        chunk_ref[owner * chunk_rows : owner * chunk_rows + slot_rows, :] = jnp.zeros((slot_rows, 128), jnp.float32)
    for copy in copies[:2]:
        copy.wait()
    for j in range(flags):
        owner = owner_ref[j]
        rank = count[owner]
        count[owner] = rank + 1
        target[j] = owner * chunk_rows + rank
        position_ref[j] = owner * (slot_rows + line_rows) + rank
    for copy in copies[2:]:
        copy.wait()
    planes = velocity_ref.reshape(3, size_x, size_y, size_z)
    layers = viscosity_ref.reshape(size_x, size_y, size_z)
    for j in range(flags):
        cell = cell_ref[j]
        x = lax.shift_right_logical(cell, 10)
        y = lax.shift_right_logical(cell, 7) & (size_y - 1)
        z = cell & (size_z - 1)
        here = (lane == z).astype(jnp.float32)
        along_z = (lane == z + 1).astype(jnp.float32) - (lane == z - 1).astype(jnp.float32)
        at = pl.ds(y, 1)
        for a in range(3):
            along_x = planes[a, x + 1, at, :] - planes[a, x - 1, at, :]
            along_y = planes[a, x, pl.ds(y + 1, 1), :] - planes[a, x, pl.ds(y - 1, 1), :]
            masked[3 * a, j : j + 1, :] = along_x * here
            masked[3 * a + 1, j : j + 1, :] = along_y * here
            masked[3 * a + 2, j : j + 1, :] = planes[a, x, at, :] * along_z
        masked[9, j : j + 1, :] = layers[x, at, :] * here

    for side, ref in enumerate((y_low_ref, y_high_ref)):
        for layer in range(2):
            y = layer if side == 0 else size_y - 1 - layer
            for a in range(3):
                ref[3 * layer + a] = velocity_ref[a, pl.ds(y, size_x, stride=size_y), :]
        y = 0 if side == 0 else size_y - 1
        ref[6] = viscosity_ref[pl.ds(y, size_x, stride=size_y), :]

    for side in range(2):
        beside = neighbour(macro, side, macro_count)
        first = pl.multiple_of((2 * beside + core) * chunk_rows + slot_rows, 8)
        other = pl.multiple_of((2 * beside + 1 - core) * chunk_rows + slot_rows, 8)
        for layer in range(2):
            x = layer if side == 0 else size_x - 1 - layer
            for a in range(3):
                chunk_ref[pl.ds(first + (3 * layer + a) * size_y, size_y), :] = velocity_ref[
                    a, x * size_y : (x + 1) * size_y, :
                ]
        x = 0 if side == 0 else size_x - 1
        chunk_ref[pl.ds(first + 6 * size_y, size_y), :] = viscosity_ref[x * size_y : (x + 1) * size_y, :]
        for number, a in enumerate((0, 2)):
            chunk_ref[pl.ds(other + number * size_y, size_y), :] = velocity_ref[
                a, x * size_y : (x + 1) * size_y, :
            ]

    group = size_z // 8
    lane2 = lanes_of((size_y, size_z))
    first = pl.multiple_of((2 * macro + 1 - core) * chunk_rows + slot_rows, 8)
    source = jnp.where(core == 0, size_z - 2, 0)
    for block in range(-(-size_x // group)):
        total = jnp.zeros((size_y, size_z), jnp.float32)
        for x in range(block * group, min(size_x, (block + 1) * group)):
            rows = slice(x * size_y, (x + 1) * size_y)
            for a in range(4):
                at = 8 * (x - block * group) + 2 * a
                value = viscosity_ref[rows, :] if a == 3 else velocity_ref[a, rows, :]
                total = jnp.where((lane2 == at) | (lane2 == at + 1), rolled(value, at - source), total)
        chunk_ref[pl.ds(first + block * size_y, size_y), :] = total

    columns = [0.5 * jnp.sum(masked[c], axis=1, keepdims=True) for c in range(9)]
    viscous = jnp.sum(masked[9], axis=1, keepdims=True)
    wide = lanes_of((flags, 128))
    packed = jnp.zeros((flags, 128), jnp.float32)
    for c in range(9):
        packed = jnp.where(wide == c, columns[c], packed)
    gradients[...] = packed
    stress = jnp.zeros((flags, 128), jnp.float32)
    for k, (a, b) in enumerate(stress_pairs):
        stress = jnp.where(wide == k, viscous * (columns[3 * a + b] + columns[3 * b + a]), stress)
    viscous_ref[...] = stress

    for j in range(flags):
        chunk_ref[pl.ds(target[j], 1), :] = gradients[j : j + 1, :]


def gather_rows(flag_cell, owner, velocity, viscosity, capacity, owner_count):
    size_x, size_y, size_z = viscosity.shape
    flags = flag_cell.shape[0]
    chunk_rows = slot_rows + item_count * size_y
    face = jax.ShapeDtypeStruct((item_count, size_x, size_z), jnp.float32)
    return pl.pallas_call(
        functools.partial(gather_kernel, capacity, size_x, size_y, size_z, owner_count // 2),
        out_shape=(
            pltpu.VMEM((owner_count * chunk_rows, 128), jnp.float32),
            jax.ShapeDtypeStruct((flags,), jnp.int32),
            jax.ShapeDtypeStruct((flags, 128), jnp.float32),
            face,
            face,
        ),
        in_specs=[pl.BlockSpec(memory_space=pltpu.HBM)] * 4,
        out_specs=(VMEM, SMEM, VMEM, VMEM, VMEM),
        scratch_shapes=[
            pltpu.SMEM((flags,), jnp.int32),
            pltpu.SMEM((flags,), jnp.int32),
            pltpu.VMEM((3, size_x * size_y, size_z), jnp.float32),
            pltpu.VMEM((size_x * size_y, size_z), jnp.float32),
            pltpu.VMEM((10, flags, size_z), jnp.float32),
            pltpu.VMEM((flags, 128), jnp.float32),
            pltpu.SMEM((flags,), jnp.int32),
            pltpu.SMEM((owner_count,), jnp.int32),
            pltpu.SemaphoreType.DMA((4,)),
        ],
        compiler_params=limit(8),
        cost_estimate=pl.CostEstimate(flops=400000, bytes_accessed=3000000, transcendentals=0),
        name="gather_rows",
    )(
        far(flag_cell),
        far(owner),
        far(velocity.reshape(3, size_x * size_y, size_z)),
        far(viscosity.reshape(size_x * size_y, size_z)),
    )


def micro_kernel(
    capacity, parts, rows, groups, conform_ref, noise_ref, rate_ref, first_conform_ref, first_noise_ref,
    next_ref, chunk_ref, conform, noise, rate, rate_wide, sums_ref, read_sem, noise_sem,
):
    steps, _, slots, dumbbells = noise_ref.shape
    blocks = slots // rows
    span = steps // groups
    width = dumbbells // parts
    owners = slots // capacity
    scale = 1.0 / noise_weight
    extent = fene_extent * scale * scale

    def block_rows(block):
        return pl.ds(pl.multiple_of(block * rows, rows), rows)

    def read(block):
        at = block_rows(block)
        return pltpu.make_async_copy(conform_ref.at[:, at, :], conform.at[:, at, :], read_sem.at[block])

    def read_noise(block, group):
        at, when = block_rows(block), pl.ds(group * span, span)
        return pltpu.make_async_copy(
            noise_ref.at[when, :, at, :], noise.at[when, :, at, :], noise_sem.at[block, group]
        )

    pieces = [
        (half, slice(part * width, (part + 1) * width)) for half in range(rows // 16) for part in range(parts)
    ]
    assert len(pieces) == 8
    early = groups // first_share
    for block in range(blocks):
        if block > 0:
            read(block).start()
        for group in range(early if block == 0 else 0, groups):
            read_noise(block, group).start()
    conform[:, 0:rows, :] = first_conform_ref[...]
    for step in range(steps // first_share):
        noise[step, :, 0:rows, :] = first_noise_ref[step]
    for owner in range(owners):
        rate[owner * capacity : (owner + 1) * capacity, :] = rate_ref[owner, 0:capacity, :]
        chunk_ref[owner] = jnp.zeros(chunk_ref.shape[1:], jnp.float32)
    for a in range(3):
        for b in range(3):
            column = micro_step * rate[:, 3 * a + b : 3 * a + b + 1] + (1.0 if a == b else 0.0)
            rate_wide[3 * a + b] = jnp.broadcast_to(column, (slots, width))

    def inverses(state, scale):
        rooms = []
        for piece in range(len(pieces)):
            q = state[3 * piece : 3 * piece + 3]
            room = (extent - q[0] * q[0]) - (q[1] * q[1] + q[2] * q[2])
            rooms.append(jnp.maximum(room, extent * spring_floor))
        levels = [rooms]
        while len(levels[-1]) > 1:
            levels.append([low * high for low, high in zip(levels[-1][0::2], levels[-1][1::2])])
        result = [scale * pl.reciprocal(levels[-1][0])]
        for level in reversed(levels[:-1]):
            result = [result[i // 2] * level[i ^ 1] for i in range(len(level))]
        return result

    def advance_block(block, carry):
        ats = [pl.ds(pl.multiple_of(block * rows + 16 * half, 16), 16) for half in range(rows // 16)]
        rates = [
            [[rate_wide.at[3 * a + b, at, :] for b in range(3)] for a in range(3)] for at in ats
        ]

        def substep(step, state):
            updated = []
            springs = inverses(state, micro_step * relax_rate * extent)
            for piece, (half, lanes) in enumerate(pieces):
                q = state[3 * piece : 3 * piece + 3]
                table = rates[half]
                for a in range(3):
                    b, c = [other for other in range(3) if other != a]
                    kick = noise[step, a, ats[half], lanes].astype(jnp.float32)
                    rest = (table[a][b][...] * q[b] + table[a][c][...] * q[c]) + kick
                    updated.append((table[a][a][...] - springs[piece]) * q[a] + rest)
            return tuple(updated)

        def advance_group(group, state):
            if group < early:

                @pl.when(block > 0)
                def _():
                    read_noise(block, group).wait()

            else:
                read_noise(block, group).wait()
            for step in range(span):
                state = substep(group * span + step, state)
            return state

        @pl.when(block > 0)
        def _():
            read(block).wait()

        state = tuple(conform[a, ats[half], lanes] * scale for half, lanes in pieces for a in range(3))
        for group in range(groups):
            state = advance_group(group, state)
        inverse = inverses(state, 1.0)
        for half, at in enumerate(ats):
            sums = [None] * 6
            for piece, (other, lanes) in enumerate(pieces):
                if other != half:
                    continue
                q = state[3 * piece : 3 * piece + 3]
                for a in range(3):
                    next_ref[a, at, lanes] = q[a] * noise_weight
                for k, (a, b) in enumerate(stress_pairs):
                    term = (inverse[piece] * q[a]) * q[b]
                    sums[k] = term if sums[k] is None else sums[k] + term
            for k in range(6):
                sums_ref[k, at, :] = sums[k]
        return carry

    lax.fori_loop(0, blocks, advance_block, 0)
    lane = lanes_of((slots, 128))
    packed = jnp.zeros((slots, 128), jnp.float32)
    weight = extent * noise_weight * noise_weight / dumbbells
    for k, (a, b) in enumerate(stress_pairs):
        mean = jnp.sum(sums_ref[k], axis=1, keepdims=True) * weight
        packed = jnp.where(lane == k, polymer_weight * (mean - (1.0 if a == b else 0.0)), packed)
    for owner in range(owners):
        chunk_ref[owner, 0:capacity, :] = packed[owner * capacity : (owner + 1) * capacity]


block_slots = 32
first_share = 2


def first_kernel(rows, after_ref, conform_ref, noise_ref, conform_out, noise_out, sems):
    copies = (
        pltpu.make_async_copy(conform_ref.at[:, 0:rows, :], conform_out, sems.at[0]),
        pltpu.make_async_copy(noise_ref.at[0 : noise_out.shape[0], :, 0:rows, :], noise_out, sems.at[1]),
    )
    for copy in copies:
        copy.start()
    for copy in copies:
        copy.wait()


def first_block(after, conformations, increments):
    steps, _, _, dumbbells = increments.shape
    whole = pl.BlockSpec(memory_space=pltpu.HBM)
    return pl.pallas_call(
        functools.partial(first_kernel, block_slots),
        out_shape=(
            pltpu.VMEM((3, block_slots, dumbbells), jnp.float32),
            pltpu.VMEM((steps // first_share, 3, block_slots, dumbbells), jnp.bfloat16),
        ),
        in_specs=[pl.BlockSpec(memory_space=pl.ANY), whole, whole],
        out_specs=(VMEM, VMEM),
        scratch_shapes=[pltpu.SemaphoreType.DMA((2,))],
        compiler_params=limit(4),
        cost_estimate=pl.CostEstimate(flops=0, bytes_accessed=3000000, transcendentals=0),
        name="first_block",
    )(after, far(conformations), far(increments))


def advance(conformations, increments, chunks, first_conform, first_noise, capacity):
    slots, dumbbells = conformations.shape[1:]
    steps = increments.shape[0]
    owners = slots // capacity
    rows, parts, groups = block_slots, 4, 4
    blocks = slots // rows
    whole = pl.BlockSpec(memory_space=pltpu.HBM)
    return pl.pallas_call(
        functools.partial(micro_kernel, capacity, parts, rows, groups),
        out_shape=(
            pltpu.VMEM(conformations.shape, jnp.float32),
            jax.ShapeDtypeStruct((owners, slot_rows + line_rows, 128), jnp.float32),
        ),
        in_specs=[whole, whole, VMEM, VMEM, VMEM],
        out_specs=(VMEM, VMEM),
        scratch_shapes=[
            pltpu.VMEM(conformations.shape, jnp.float32),
            pltpu.VMEM(increments.shape, jnp.bfloat16),
            pltpu.VMEM((slots, 128), jnp.float32),
            pltpu.VMEM((9, slots, dumbbells // parts), jnp.float32),
            pltpu.VMEM((6, slots, dumbbells // parts), jnp.float32),
            pltpu.SemaphoreType.DMA((blocks,)),
            pltpu.SemaphoreType.DMA((blocks, groups)),
        ],
        compiler_params=limit(12),
        cost_estimate=pl.CostEstimate(flops=20000000, bytes_accessed=5000000, transcendentals=600000),
        name="advance",
    )(far(conformations), far(increments), chunks, first_conform, first_noise)


def lines_kernel(macro_count, chunk_ref, y_low_ref, y_high_ref, out_ref):
    out_ref[...] = chunk_ref[...]
    macro, core = place_of()
    sides = (y_low_ref, y_high_ref)
    size_x, size_z = y_low_ref.shape[1:]
    for side in range(2):
        beside = neighbour(macro, side, macro_count)
        x = 0 if side == 0 else size_x - 1
        for u in range(2):
            for a in range(2):
                at = slot_rows + 2 * u + a
                out_ref[2 * beside + core, at : at + 1, :] = sides[u][a, x : x + 1, :]

    lane = lanes_of((8, size_z))
    source = jnp.where(core == 0, size_z - 1, 0)
    total = jnp.zeros((8, size_z), jnp.float32)
    for i in range(size_x // 8):
        for u in range(2):
            for a in range(2):
                at = 4 * i + 2 * u + a
                total = jnp.where(
                    lane == at, rolled(sides[u][1 + a, 8 * i : 8 * i + 8, :], at - source), total
                )
    out_ref[2 * macro + 1 - core, slot_rows:, :] = total


def add_lines(chunks, y_low, y_high):
    return pl.pallas_call(
        functools.partial(lines_kernel, chunks.shape[0] // 2),
        out_shape=pltpu.VMEM(chunks.shape, jnp.float32),
        in_specs=[VMEM, VMEM, VMEM],
        out_specs=VMEM,
        compiler_params=limit(4),
        cost_estimate=pl.CostEstimate(flops=20000, bytes_accessed=400000, transcendentals=0),
        name="add_lines",
    )(chunks, y_low, y_high)


product_depth = 128


def one_hots(size_y, size_z, cell_ref, position_ref, lines_ref, pick_ref, spread_ref, rows):
    flags = cell_ref.shape[0]
    weight = 0.5 * macro_step
    row_count = spread_ref.shape[0]
    back_rows = pick_ref.shape[1] // 3
    lane = lanes_of((1, size_z))
    row_lane = lanes_of((1, rows.shape[1]))
    slot_lane = lanes_of((flags, back_rows))
    flag_row = lax.broadcasted_iota(jnp.int32, (flags, back_rows), 0)
    rows[3 * flags :, :] = jnp.zeros((product_depth - 3 * flags, rows.shape[1]), jnp.float32)
    slot = jnp.zeros((flags, back_rows), jnp.int32)
    for j in range(flags):
        cell = cell_ref[j]
        row = lax.div(cell, size_z)
        z = cell - row * size_z
        lines_ref[0, j : j + 1, :] = jnp.where(lane == z, weight, 0.0)
        lines_ref[1, j : j + 1, :] = jnp.where(
            lane == z - 1, weight, jnp.where(lane == z + 1, -weight, 0.0)
        )
        for number, shift in enumerate((size_y, 1)):
            rows[number * flags + j : number * flags + j + 1, :] = jnp.where(
                row_lane == row - shift, 1.0, jnp.where(row_lane == row + shift, -1.0, 0.0)
            )
        rows[2 * flags + j : 2 * flags + j + 1, :] = jnp.where(row_lane == row, 1.0, 0.0)
        slot = jnp.where(flag_row == j, position_ref[j], slot)
    spread = rows[...].T[:row_count].astype(jnp.bfloat16)
    pick = jnp.where(slot_lane == slot, 1.0, 0.0).astype(jnp.bfloat16)
    for piece in range(3):
        spread_ref[:, piece * product_depth : (piece + 1) * product_depth] = spread
        pick_ref[:, piece * back_rows : (piece + 1) * back_rows] = pick


def flow_kernel(
    size_x, size_y, size_z, macro_count, cell_ref, position_ref, velocity_ref, viscosity_ref, chunk_ref,
    y_low_ref, y_high_ref, out_ref, corner_ref, edge_ref, lines_ref, pick_ref, spread_ref,
    padded, stress_x, stress_rest, faces, ghost_y, ghost_z, rows,
):
    macro, core = place_of()
    one_hots(size_y, size_z, cell_ref, position_ref, lines_ref, pick_ref, spread_ref, rows)
    inside = (macro > 0, macro < macro_count - 1)
    sign_z = jnp.where(core == 0, 1.0, -1.0)
    end = jnp.where(core == 0, size_z - 1, 0)
    shape = (size_y, size_z)
    lane, row = lanes_of(shape), lax.broadcasted_iota(jnp.int32, shape, 0)
    at_end = jnp.where(lane == end, sign_z, 0.0)

    def kept(value, condition):
        return jnp.where(condition, value, 0.0)

    def plane(x):
        return pl.ds(pl.multiple_of(x * size_y, 8), size_y)

    def difference_z(value):
        lane = lanes_of(value.shape)
        return jnp.where(lane == size_z - 1, 0.0, rolled(value, -1)) - jnp.where(
            lane == 0, 0.0, rolled(value, 1)
        )

    def difference_rows(value, low=0.0, high=0.0):
        count = value.shape[0]
        row = lax.broadcasted_iota(jnp.int32, value.shape, 0)
        return jnp.where(row == count - 1, high, pltpu.roll(value, count - 1, 0)) - jnp.where(
            row == 0, low, pltpu.roll(value, 1, 0)
        )

    x_faces, x_others = [], []
    for s in range(2):
        beside = jnp.maximum(macro - 1, 0) if s == 0 else jnp.minimum(macro + 1, macro_count - 1)
        x_faces.append(
            [
                kept(chunk_ref[2 * beside + core, slot_rows + i * size_y : slot_rows + (i + 1) * size_y, :], inside[s])
                for i in range(item_count)
            ]
        )
        x_others.append(
            [
                kept(
                    rolled(
                        chunk_ref[
                            2 * beside + 1 - core, slot_rows + i * size_y : slot_rows + (i + 1) * size_y, :
                        ],
                        2 * end + 1,
                    ),
                    inside[s],
                )
                for i in range(2)
            ]
        )

    group = size_z // 8
    packed = [
        chunk_ref[2 * macro + 1 - core, slot_rows + i * size_y : slot_rows + (i + 1) * size_y, :]
        for i in range(-(-size_x // group))
    ]
    for i, value in enumerate(packed):

        def unpack(x, carry):
            for q in range(item_count):
                a, layer = (q, 0) if q < 4 else (q - 4, 1)
                at = 8 * (x - i * group) + 2 * a + (core if layer == 0 else 1 - core)
                faces[q, x + 1] = rolled(value, end - at)
            return carry

        lax.fori_loop(i * group, min(size_x, (i + 1) * group), unpack, 0, unroll=8)
    faces[2, 0] = x_others[0][1]
    faces[2, size_x + 1] = x_others[1][1]

    for a in range(3):
        padded[a, 0] = x_faces[0][a]
        padded[a, size_x + 1] = x_faces[1][a]

    def fill(x, carry):
        for a in range(3):
            padded[a, x + 1] = velocity_ref[a, plane(x), :]
        return carry

    lax.fori_loop(0, size_x, fill, 0, unroll=True)

    rest = {(1, 1): 0, (2, 2): 1, (1, 2): 2}

    def stress_plane(x, carry):
        along_x, along_y, along_z, centre = [], [], [], []
        for a in range(3):
            value = padded[a, x + 1]
            centre.append(value)
            along_x.append(padded[a, x + 2] - padded[a, x])
            along_y.append(
                difference_rows(value, y_low_ref[a, pl.ds(x, 1), :], y_high_ref[a, pl.ds(x, 1), :])
            )
            along_z.append(difference_z(value) + faces[a, x + 1] * at_end)
        slopes = (along_x, along_y, along_z)
        half = 0.5 * viscosity_ref[plane(x), :]
        for a, b in stress_pairs:
            value = half * (slopes[b][a] + slopes[a][b])
            if a == 0:
                stress_x[b, x + 1] = value
            else:
                stress_rest[rest[a, b], x] = value
        weight = (0.5 * faces[3, x + 1]) * at_end
        normal = [(faces[4 + a, x + 1] - centre[a]) * sign_z for a in range(3)]
        ghost_z[0, x] = weight * (normal[0] + (faces[2, x + 2] - faces[2, x]))
        ghost_z[1, x] = weight * (normal[1] + difference_rows(faces[2, x + 1]))
        ghost_z[2, x] = weight * (2.0 * normal[2])
        return carry

    lax.fori_loop(0, size_x, stress_plane, 0, unroll=6)

    for s in range(2):
        near, far, weight = x_faces[s][0:3], x_faces[s][3:6], 0.5 * x_faces[s][6]
        sign = -1.0 if s == 0 else 1.0
        normal = [(far[a] - padded[a, 1 if s == 0 else size_x]) * sign for a in range(3)]
        slope_y = difference_rows(near[0])
        slope_z = difference_z(near[0]) + x_others[s][0] * at_end
        at = 0 if s == 0 else size_x + 1
        stress_x[0, at] = weight * (2.0 * normal[0])
        stress_x[1, at] = weight * (normal[1] + slope_y)
        stress_x[2, at] = weight * (normal[2] + slope_z)
        for u in range(2):
            y, sign_y = (0, -1.0) if u == 0 else (size_y - 1, 1.0)
            number = 4 * s + 2 * u
            corner_ref[number : number + 1, :] = (0.5 * macro_step * sign * sign_y) * weight[y : y + 1, :]

    for u, ref in enumerate((y_low_ref, y_high_ref)):
        y, sign = (0, -1.0) if u == 0 else (size_y - 1, 1.0)
        weight = 0.5 * ref[6]
        normal = [
            (ref[3 + a] - velocity_ref[a, pl.ds(y, size_x, stride=size_y), :]) * sign for a in range(3)
        ]
        ghost_y[3 * u] = weight * (normal[0] + difference_rows(ref[1]))
        ghost_y[3 * u + 1] = weight * (2.0 * normal[1])
        ghost_y[3 * u + 2] = weight * (normal[2] + difference_z(ref[1]))
        for s in range(2):
            x, sign_x = (0, -1.0) if s == 0 else (size_x - 1, 1.0)
            number = 4 * s + 2 * u + 1
            corner_ref[number : number + 1, :] = (0.5 * macro_step * sign * sign_x) * weight[x : x + 1, :]
        wide = lanes_of((size_x, size_z))
        scale = jnp.where(wide == end, (0.5 * macro_step * sign) * sign_z, 0.0)
        edge_ref[2 * u] = scale * weight
        for x in range(size_x):
            edge_ref[2 * u + 1, x : x + 1, :] = scale[x : x + 1, :] * (0.5 * faces[3, x + 1, y : y + 1, :])

    columns = {(0, 1): (stress_x, 1, 1), (1, 1): (stress_rest, 0, 0), (2, 1): (stress_rest, 2, 0)}
    columns_z = {0: (stress_x, 2, 1), 1: (stress_rest, 2, 0), 2: (stress_rest, 1, 0)}

    def step_plane(x, carry):
        for a in range(3):
            total = stress_x[a, x + 2] - stress_x[a, x]
            ref, number, shift = columns[a, 1]
            total = total + difference_rows(
                ref[number, x + shift], ghost_y[a, pl.ds(x, 1), :], ghost_y[3 + a, pl.ds(x, 1), :]
            )
            ref, number, shift = columns_z[a]
            total = total + (difference_z(ref[number, x + shift]) + ghost_z[a, x])
            out_ref[a, plane(x), :] = padded[a, x + 1] + (0.5 * macro_step) * total
        return carry

    lax.fori_loop(0, size_x, step_plane, 0, unroll=6)


def flow_step(flag_cell, position, velocity, viscosity, chunks, y_low, y_high):
    size_x, size_y, size_z = viscosity.shape
    flags = flag_cell.shape[0]
    back_rows = chunks.shape[0] * (slot_rows + line_rows)
    row_count = size_x * size_y
    planes = (size_x, size_y, size_z)
    wide = (size_x + 2, size_y, size_z)
    return pl.pallas_call(
        functools.partial(flow_kernel, size_x, size_y, size_z, chunks.shape[0] // 2),
        out_shape=(
            jax.ShapeDtypeStruct((3, size_x * size_y, size_z), jnp.float32),
            jax.ShapeDtypeStruct((8, size_z), jnp.float32),
            jax.ShapeDtypeStruct((4, size_x, size_z), jnp.float32),
            jax.ShapeDtypeStruct((2, flags, size_z), jnp.float32),
            jax.ShapeDtypeStruct((flags, 3 * back_rows), jnp.bfloat16),
            jax.ShapeDtypeStruct((row_count, 3 * product_depth), jnp.bfloat16),
        ),
        in_specs=[SMEM] * 2 + [VMEM] * 5,
        out_specs=(VMEM,) * 6,
        scratch_shapes=[
            pltpu.VMEM((3, *wide), jnp.float32),
            pltpu.VMEM((3, *wide), jnp.float32),
            pltpu.VMEM((3, *planes), jnp.float32),
            pltpu.VMEM((item_count, *wide), jnp.float32),
            pltpu.VMEM((6, size_x, size_z), jnp.float32),
            pltpu.VMEM((3, *planes), jnp.float32),
            pltpu.VMEM((product_depth, -(-row_count // 128) * 128), jnp.float32),
        ],
        compiler_params=limit(12),
        cost_estimate=pl.CostEstimate(flops=4000000, bytes_accessed=3000000, transcendentals=0),
        name="flow_step",
    )(
        flag_cell, position,
        velocity.reshape(3, size_x * size_y, size_z),
        viscosity.reshape(size_x * size_y, size_z),
        chunks, y_low, y_high,
    )


def pieces(value):
    high = value.astype(jnp.bfloat16)
    rest = value - high.astype(jnp.float32)
    middle = rest.astype(jnp.bfloat16)
    return high, middle, (rest - middle.astype(jnp.float32)).astype(jnp.bfloat16)


def polymer_kernel(
    size_x, size_y, size_z, macro_count, chunk_ref, viscous_ref, corner_ref, edge_ref, lines_ref, pick_ref,
    spread_ref, partial_ref, out_ref, flag_ref, field, write_sem,
):
    flags = viscous_ref.shape[0]
    chunk_rows = slot_rows + line_rows
    macro, core = place_of()
    values = jnp.dot(
        pick_ref[...], jnp.concatenate(pieces(chunk_ref[...]), axis=0), preferred_element_type=jnp.float32
    )
    here, beside_z = lines_ref[0], lines_ref[1]
    columns = [jnp.broadcast_to(values[:, k : k + 1], (flags, size_z)) for k in range(6)]
    unused = jnp.zeros((product_depth - 3 * flags, size_z), jnp.float32)
    split = [
        pieces(
            jnp.concatenate(
                [
                    columns[pair_index(a, 0)] * here, columns[pair_index(a, 1)] * here,
                    columns[pair_index(a, 2)] * beside_z, unused,
                ],
                axis=0,
            )
        )
        for a in range(3)
    ]
    flag_ref[...] = (viscous_ref[...] + values).T[0:6, :]

    field[...] = partial_ref[...]
    for s in range(2):
        inside = macro > 0 if s == 0 else macro < macro_count - 1
        beside = jnp.maximum(macro - 1, 0) if s == 0 else jnp.minimum(macro + 1, macro_count - 1)
        start = (2 * beside + core) * chunk_rows + slot_rows
        x = 0 if s == 0 else size_x - 1
        for u in range(2):
            at = x * size_y + (0 if u == 0 else size_y - 1)
            for a in range(2):
                number = 4 * s + 2 * u + a
                line = corner_ref[number : number + 1, :] * chunk_ref[pl.ds(start + 2 * u + a, 1), :]
                field[1 - a, at : at + 1, :] += jnp.where(inside, line, 0.0)
    start = pl.multiple_of((2 * macro + 1 - core) * chunk_rows + slot_rows, 8)
    packed = chunk_ref[pl.ds(start, line_rows), :]
    end = jnp.where(core == 0, size_z - 1, 0)
    for u in range(2):
        y = 0 if u == 0 else size_y - 1
        for a in range(2):
            for i in range(size_x // 8):
                line = rolled(packed, end - (4 * i + 2 * u + a)) * edge_ref[2 * u + a, 8 * i : 8 * i + 8, :]
                at = pl.ds(8 * i * size_y + y, 8, stride=size_y)
                field[2 - a, at, :] += line
    copies = [pltpu.make_async_copy(field.at[a], out_ref.at[a], write_sem.at[a]) for a in range(3)]
    for a in range(3):
        field[a] += jnp.dot(
            spread_ref[...], jnp.concatenate(split[a], axis=0), preferred_element_type=jnp.float32
        )
        copies[a].start()
    for copy in copies:
        copy.wait()


def add_polymer(chunks, viscous, corners, edges, lines, pick, spread, partial, shape):
    flags = viscous.shape[0]
    size_x, size_y, size_z = shape
    return pl.pallas_call(
        functools.partial(polymer_kernel, size_x, size_y, size_z, chunks.shape[0] // 2),
        out_shape=(
            jax.ShapeDtypeStruct(partial.shape, jnp.float32),
            jax.ShapeDtypeStruct((6, flags), jnp.float32),
        ),
        in_specs=[VMEM] * 8,
        out_specs=(pl.BlockSpec(memory_space=pltpu.HBM), VMEM),
        scratch_shapes=[pltpu.VMEM(partial.shape, jnp.float32), pltpu.SemaphoreType.DMA((3,))],
        compiler_params=limit(8),
        cost_estimate=pl.CostEstimate(flops=400000, bytes_accessed=3000000, transcendentals=0),
        name="add_polymer",
    )(chunks.reshape(-1, 128), viscous, corners, edges, lines, pick, spread, partial)


def shards(velocity, viscosity, flag_cell, flag_owner, conformations, increments):
    macro_count = lax.axis_size("macro")
    tile_count = lax.axis_size("tile")
    assert lax.axis_size("micro") == 2
    owner_count = 2 * macro_count
    capacity = conformations.shape[1] // owner_count
    size_x, size_y, size_z = viscosity.shape
    assert capacity <= slot_rows and size_y == 8 and size_z == 128 and size_x % 8 == 0 and size_x <= 48
    chunks, position, viscous, y_first, y_last = gather_rows(
        flag_cell, flag_owner.reshape(-1), velocity, viscosity, capacity, owner_count
    )

    def exchange(rows):
        return lax.all_to_all(rows, ("macro", "micro"), split_axis=0, concat_axis=0, tiled=True)

    received = exchange(chunks.reshape(owner_count, -1, 128))
    up = [(i, i + 1) for i in range(tile_count - 1)]
    down = [(target, source) for source, target in up]
    y_low = lax.ppermute(y_last, "tile", up)
    y_high = lax.ppermute(y_first, "tile", down)
    first_conform, first_noise = first_block(position, conformations, increments)
    last_state, polymer = advance(
        conformations, increments, received, first_conform, first_noise, capacity
    )
    returned = exchange(add_lines(polymer, y_low, y_high))
    partial, corners, edges, lines, pick, spread = flow_step(
        flag_cell, position, velocity, viscosity, received, y_low, y_high
    )
    velocity_next, flag_stress = add_polymer(
        returned, viscous, corners, edges, lines, pick, spread, partial, viscosity.shape
    )
    return (velocity_next.reshape(velocity.shape), last_state, flag_stress)


def solution(mesh):
    in_specs = (
        P(None, "macro", "tile", "micro"),
        P("macro", "tile", "micro"),
        P(("macro", "tile", "micro")),
        P(("macro", "tile", "micro"), None),
        P(None, ("macro", "tile", "micro"), None),
        P(None, None, ("macro", "tile", "micro"), None),
    )
    out_specs = (
        P(None, "macro", "tile", "micro"),
        P(None, ("macro", "tile", "micro"), None),
        P(None, ("macro", "tile", "micro")),
    )
    return jax.shard_map(shards, mesh=mesh, in_specs=in_specs, out_specs=out_specs, check_vma=False)
```

```python
import functools

import jax
import jax.numpy as jnp
from jax import lax
from jax.experimental import pallas as pl
from jax.experimental.pallas import tpu as pltpu
from jax.sharding import PartitionSpec as P

stress_pairs = ((0, 0), (1, 1), (2, 2), (0, 1), (0, 2), (1, 2))
macro_step = 0.1
micro_step = 0.01
noise_weight = 0.1
relax_rate = 0.5
fene_extent = 30.0
spring_floor = 0.1
polymer_weight = 0.25

SMEM = pl.BlockSpec(memory_space=pltpu.SMEM)
VMEM = pl.BlockSpec(memory_space=pltpu.VMEM)


def pair_index(left_axis, right_axis):
    return stress_pairs.index((min(left_axis, right_axis), max(left_axis, right_axis)))


def lanes_of(shape):
    return lax.broadcasted_iota(jnp.int32, shape, len(shape) - 1)


slot_rows = 8
item_count = 7
line_rows = 8


block_slots = 32
first_share = 2


def limit(mebibytes):
    return pltpu.CompilerParams(vmem_limit_bytes=mebibytes * 1024 * 1024)


def far(value):
    return pltpu.with_memory_space_constraint(value, pltpu.HBM)


def place_of():
    return lax.axis_index("macro"), lax.axis_index("micro")


def neighbour(index, side, count):
    return jnp.maximum(index - 1, 0) if side == 0 else jnp.minimum(index + 1, count - 1)


def rolled(value, amount):
    size = value.shape[-1]
    if isinstance(amount, int):
        return pltpu.roll(value, amount % size, value.ndim - 1)
    return pltpu.roll(value, lax.rem(amount + 2 * size, size), value.ndim - 1)


def gather_kernel(
    capacity, size_x, size_y, size_z, macro_count, cell_in, owner_in, velocity_in, viscosity_in,
    conform_in, noise_in, chunk_ref, position_ref, viscous_ref, y_low_ref, y_high_ref, conform_ref, noise_ref,
    cell_ref, owner_ref, velocity_ref, viscosity_ref, masked, gradients, target, count, sems,
):
    flags = cell_ref.shape[0]
    copies = [
        pltpu.make_async_copy(source, into, sems.at[number])
        for number, (source, into) in enumerate(
            (
                (cell_in, cell_ref), (owner_in, owner_ref), (velocity_in, velocity_ref),
                (viscosity_in, viscosity_ref), (conform_in.at[:, 0:block_slots, :], conform_ref),
                (noise_in.at[0 : noise_ref.shape[0], :, 0:block_slots, :], noise_ref),
            )
        )
    ]
    for copy in copies:
        copy.start()
    chunk_rows = slot_rows + item_count * size_y
    macro, core = place_of()
    lane = lanes_of((1, size_z))

    for owner in range(count.shape[0]):
        count[owner] = 0
        chunk_ref[owner * chunk_rows : owner * chunk_rows + slot_rows, :] = jnp.zeros((slot_rows, 128), jnp.float32)
    for copy in copies[:2]:
        copy.wait()
    for j in range(flags):
        owner = owner_ref[j]
        rank = count[owner]
        count[owner] = rank + 1
        target[j] = owner * chunk_rows + rank
        position_ref[j] = owner * (slot_rows + line_rows) + rank
    for copy in copies[2:4]:
        copy.wait()
    planes = velocity_ref.reshape(3, size_x, size_y, size_z)
    layers = viscosity_ref.reshape(size_x, size_y, size_z)
    for j in range(flags):
        cell = cell_ref[j]
        x = lax.shift_right_logical(cell, 10)
        y = lax.shift_right_logical(cell, 7) & (size_y - 1)
        z = cell & (size_z - 1)
        here = (lane == z).astype(jnp.float32)
        along_z = (lane == z + 1).astype(jnp.float32) - (lane == z - 1).astype(jnp.float32)
        at = pl.ds(y, 1)
        for a in range(3):
            along_x = planes[a, x + 1, at, :] - planes[a, x - 1, at, :]
            along_y = planes[a, x, pl.ds(y + 1, 1), :] - planes[a, x, pl.ds(y - 1, 1), :]
            masked[3 * a, j : j + 1, :] = along_x * here
            masked[3 * a + 1, j : j + 1, :] = along_y * here
            masked[3 * a + 2, j : j + 1, :] = planes[a, x, at, :] * along_z
        masked[9, j : j + 1, :] = layers[x, at, :] * here

    for side, ref in enumerate((y_low_ref, y_high_ref)):
        for layer in range(2):
            y = layer if side == 0 else size_y - 1 - layer
            for a in range(3):
                ref[3 * layer + a] = velocity_ref[a, pl.ds(y, size_x, stride=size_y), :]
        y = 0 if side == 0 else size_y - 1
        ref[6] = viscosity_ref[pl.ds(y, size_x, stride=size_y), :]

    for side in range(2):
        beside = neighbour(macro, side, macro_count)
        first = pl.multiple_of((2 * beside + core) * chunk_rows + slot_rows, 8)
        other = pl.multiple_of((2 * beside + 1 - core) * chunk_rows + slot_rows, 8)
        for layer in range(2):
            x = layer if side == 0 else size_x - 1 - layer
            for a in range(3):
                chunk_ref[pl.ds(first + (3 * layer + a) * size_y, size_y), :] = velocity_ref[
                    a, x * size_y : (x + 1) * size_y, :
                ]
        x = 0 if side == 0 else size_x - 1
        chunk_ref[pl.ds(first + 6 * size_y, size_y), :] = viscosity_ref[x * size_y : (x + 1) * size_y, :]
        for number, a in enumerate((0, 2)):
            chunk_ref[pl.ds(other + number * size_y, size_y), :] = velocity_ref[
                a, x * size_y : (x + 1) * size_y, :
            ]

    group = size_z // 8
    lane2 = lanes_of((size_y, size_z))
    first = pl.multiple_of((2 * macro + 1 - core) * chunk_rows + slot_rows, 8)
    source = jnp.where(core == 0, size_z - 2, 0)
    for block in range(-(-size_x // group)):
        total = jnp.zeros((size_y, size_z), jnp.float32)
        for x in range(block * group, min(size_x, (block + 1) * group)):
            rows = slice(x * size_y, (x + 1) * size_y)
            for a in range(4):
                at = 8 * (x - block * group) + 2 * a
                value = viscosity_ref[rows, :] if a == 3 else velocity_ref[a, rows, :]
                total = jnp.where((lane2 == at) | (lane2 == at + 1), rolled(value, at - source), total)
        chunk_ref[pl.ds(first + block * size_y, size_y), :] = total

    columns = [0.5 * jnp.sum(masked[c], axis=1, keepdims=True) for c in range(9)]
    viscous = jnp.sum(masked[9], axis=1, keepdims=True)
    wide = lanes_of((flags, 128))
    packed = jnp.zeros((flags, 128), jnp.float32)
    for c in range(9):
        packed = jnp.where(wide == c, columns[c], packed)
    gradients[...] = packed
    stress = jnp.zeros((flags, 128), jnp.float32)
    for k, (a, b) in enumerate(stress_pairs):
        stress = jnp.where(wide == k, viscous * (columns[3 * a + b] + columns[3 * b + a]), stress)
    viscous_ref[...] = stress

    for j in range(flags):
        chunk_ref[pl.ds(target[j], 1), :] = gradients[j : j + 1, :]
    for copy in copies[4:]:
        copy.wait()


def gather_rows(flag_cell, owner, velocity, viscosity, conformations, increments, capacity, owner_count):
    size_x, size_y, size_z = viscosity.shape
    flags = flag_cell.shape[0]
    chunk_rows = slot_rows + item_count * size_y
    face = jax.ShapeDtypeStruct((item_count, size_x, size_z), jnp.float32)
    steps, _, _, dumbbells = increments.shape
    return pl.pallas_call(
        functools.partial(gather_kernel, capacity, size_x, size_y, size_z, owner_count // 2),
        out_shape=(
            jax.ShapeDtypeStruct((owner_count * chunk_rows, 128), jnp.float32),
            jax.ShapeDtypeStruct((flags,), jnp.int32),
            jax.ShapeDtypeStruct((flags, 128), jnp.float32),
            face,
            face,
            pltpu.VMEM((3, block_slots, dumbbells), jnp.float32),
            pltpu.VMEM((steps // first_share, 3, block_slots, dumbbells), jnp.bfloat16),
        ),
        in_specs=[pl.BlockSpec(memory_space=pltpu.HBM)] * 6,
        out_specs=(VMEM, SMEM, VMEM, VMEM, VMEM, VMEM, VMEM),
        scratch_shapes=[
            pltpu.SMEM((flags,), jnp.int32),
            pltpu.SMEM((flags,), jnp.int32),
            pltpu.VMEM((3, size_x * size_y, size_z), jnp.float32),
            pltpu.VMEM((size_x * size_y, size_z), jnp.float32),
            pltpu.VMEM((10, flags, size_z), jnp.float32),
            pltpu.VMEM((flags, 128), jnp.float32),
            pltpu.SMEM((flags,), jnp.int32),
            pltpu.SMEM((owner_count,), jnp.int32),
            pltpu.SemaphoreType.DMA((6,)),
        ],
        compiler_params=limit(8),
        cost_estimate=pl.CostEstimate(flops=400000, bytes_accessed=3000000, transcendentals=0),
        name="gather_rows",
    )(
        far(flag_cell),
        far(owner),
        far(velocity.reshape(3, size_x * size_y, size_z)),
        far(viscosity.reshape(size_x * size_y, size_z)),
        far(conformations),
        far(increments),
    )


def micro_kernel(
    capacity, parts, rows, groups, conform_ref, noise_ref, rate_ref, first_conform_ref, first_noise_ref,
    next_ref, chunk_ref, conform, noise, rate, rate_wide, sums_ref, read_sem, noise_sem,
):
    steps, _, slots, dumbbells = noise_ref.shape
    blocks = slots // rows
    span = steps // groups
    width = dumbbells // parts
    owners = slots // capacity
    scale = 1.0 / noise_weight
    extent = fene_extent * scale * scale

    def block_rows(block):
        return pl.ds(pl.multiple_of(block * rows, rows), rows)

    def read(block):
        at = block_rows(block)
        return pltpu.make_async_copy(conform_ref.at[:, at, :], conform.at[:, at, :], read_sem.at[block])

    def read_noise(block, group):
        at, when = block_rows(block), pl.ds(group * span, span)
        return pltpu.make_async_copy(
            noise_ref.at[when, :, at, :], noise.at[when, :, at, :], noise_sem.at[block, group]
        )

    pieces = [
        (half, slice(part * width, (part + 1) * width)) for half in range(rows // 16) for part in range(parts)
    ]
    assert len(pieces) == 8
    early = groups // first_share
    for block in range(blocks):
        if block > 0:
            read(block).start()
        for group in range(early if block == 0 else 0, groups):
            read_noise(block, group).start()
    conform[:, 0:rows, :] = first_conform_ref[...]
    for step in range(steps // first_share):
        noise[step, :, 0:rows, :] = first_noise_ref[step]
    for owner in range(owners):
        rate[owner * capacity : (owner + 1) * capacity, :] = rate_ref[owner, 0:capacity, :]
        chunk_ref[owner] = jnp.zeros(chunk_ref.shape[1:], jnp.float32)
    for a in range(3):
        for b in range(3):
            column = micro_step * rate[:, 3 * a + b : 3 * a + b + 1] + (1.0 if a == b else 0.0)
            rate_wide[3 * a + b] = jnp.broadcast_to(column, (slots, width))

    def inverses(state, scale):
        rooms = []
        for piece in range(len(pieces)):
            q = state[3 * piece : 3 * piece + 3]
            room = (extent - q[0] * q[0]) - (q[1] * q[1] + q[2] * q[2])
            rooms.append(jnp.maximum(room, extent * spring_floor))
        levels = [rooms]
        while len(levels[-1]) > 1:
            levels.append([low * high for low, high in zip(levels[-1][0::2], levels[-1][1::2])])
        result = [scale * pl.reciprocal(levels[-1][0])]
        for level in reversed(levels[:-1]):
            result = [result[i // 2] * level[i ^ 1] for i in range(len(level))]
        return result

    def advance_block(block, carry):
        ats = [pl.ds(pl.multiple_of(block * rows + 16 * half, 16), 16) for half in range(rows // 16)]
        rates = [
            [[rate_wide.at[3 * a + b, at, :] for b in range(3)] for a in range(3)] for at in ats
        ]

        def substep(step, state):
            updated = []
            springs = inverses(state, micro_step * relax_rate * extent)
            for piece, (half, lanes) in enumerate(pieces):
                q = state[3 * piece : 3 * piece + 3]
                table = rates[half]
                for a in range(3):
                    b, c = [other for other in range(3) if other != a]
                    kick = noise[step, a, ats[half], lanes].astype(jnp.float32)
                    rest = (table[a][b][...] * q[b] + table[a][c][...] * q[c]) + kick
                    updated.append((table[a][a][...] - springs[piece]) * q[a] + rest)
            return tuple(updated)

        def advance_group(group, state):
            if group < early:

                @pl.when(block > 0)
                def _():
                    read_noise(block, group).wait()

            else:
                read_noise(block, group).wait()
            for step in range(span):
                state = substep(group * span + step, state)
            return state

        @pl.when(block > 0)
        def _():
            read(block).wait()

        state = tuple(conform[a, ats[half], lanes] * scale for half, lanes in pieces for a in range(3))
        for group in range(groups):
            state = advance_group(group, state)
        inverse = inverses(state, 1.0)
        for half, at in enumerate(ats):
            sums = [None] * 6
            for piece, (other, lanes) in enumerate(pieces):
                if other != half:
                    continue
                q = state[3 * piece : 3 * piece + 3]
                for a in range(3):
                    next_ref[a, at, lanes] = q[a] * noise_weight
                for k, (a, b) in enumerate(stress_pairs):
                    term = (inverse[piece] * q[a]) * q[b]
                    sums[k] = term if sums[k] is None else sums[k] + term
            for k in range(6):
                sums_ref[k, at, :] = sums[k]
        return carry

    lax.fori_loop(0, blocks, advance_block, 0)
    lane = lanes_of((slots, 128))
    packed = jnp.zeros((slots, 128), jnp.float32)
    weight = extent * noise_weight * noise_weight / dumbbells
    for k, (a, b) in enumerate(stress_pairs):
        mean = jnp.sum(sums_ref[k], axis=1, keepdims=True) * weight
        packed = jnp.where(lane == k, polymer_weight * (mean - (1.0 if a == b else 0.0)), packed)
    for owner in range(owners):
        chunk_ref[owner, 0:capacity, :] = packed[owner * capacity : (owner + 1) * capacity]


def advance(conformations, increments, chunks, first_conform, first_noise, capacity):
    slots, dumbbells = conformations.shape[1:]
    steps = increments.shape[0]
    owners = slots // capacity
    rows, parts, groups = block_slots, 4, 4
    blocks = slots // rows
    whole = pl.BlockSpec(memory_space=pltpu.HBM)
    return pl.pallas_call(
        functools.partial(micro_kernel, capacity, parts, rows, groups),
        out_shape=(
            pltpu.VMEM(conformations.shape, jnp.float32),
            jax.ShapeDtypeStruct((owners, slot_rows + line_rows, 128), jnp.float32),
        ),
        in_specs=[whole, whole, VMEM, VMEM, VMEM],
        out_specs=(VMEM, VMEM),
        scratch_shapes=[
            pltpu.VMEM(conformations.shape, jnp.float32),
            pltpu.VMEM(increments.shape, jnp.bfloat16),
            pltpu.VMEM((slots, 128), jnp.float32),
            pltpu.VMEM((9, slots, dumbbells // parts), jnp.float32),
            pltpu.VMEM((6, slots, dumbbells // parts), jnp.float32),
            pltpu.SemaphoreType.DMA((blocks,)),
            pltpu.SemaphoreType.DMA((blocks, groups)),
        ],
        compiler_params=limit(12),
        cost_estimate=pl.CostEstimate(flops=20000000, bytes_accessed=5000000, transcendentals=600000),
        name="advance",
    )(far(conformations), far(increments), chunks, first_conform, first_noise)


def lines_kernel(macro_count, chunk_ref, y_low_ref, y_high_ref, out_ref):
    out_ref[...] = chunk_ref[...]
    macro, core = place_of()
    sides = (y_low_ref, y_high_ref)
    size_x, size_z = y_low_ref.shape[1:]
    for side in range(2):
        beside = neighbour(macro, side, macro_count)
        x = 0 if side == 0 else size_x - 1
        for u in range(2):
            for a in range(2):
                at = slot_rows + 2 * u + a
                out_ref[2 * beside + core, at : at + 1, :] = sides[u][a, x : x + 1, :]

    lane = lanes_of((8, size_z))
    source = jnp.where(core == 0, size_z - 1, 0)
    total = jnp.zeros((8, size_z), jnp.float32)
    for i in range(size_x // 8):
        for u in range(2):
            for a in range(2):
                at = 4 * i + 2 * u + a
                total = jnp.where(
                    lane == at, rolled(sides[u][1 + a, 8 * i : 8 * i + 8, :], at - source), total
                )
    out_ref[2 * macro + 1 - core, slot_rows:, :] = total


def add_lines(chunks, y_low, y_high):
    return pl.pallas_call(
        functools.partial(lines_kernel, chunks.shape[0] // 2),
        out_shape=jax.ShapeDtypeStruct(chunks.shape, jnp.float32),
        in_specs=[VMEM, VMEM, VMEM],
        out_specs=VMEM,
        compiler_params=limit(4),
        cost_estimate=pl.CostEstimate(flops=20000, bytes_accessed=400000, transcendentals=0),
        name="add_lines",
    )(chunks, y_low, y_high)


product_depth = 128


def one_hots(size_y, size_z, cell_ref, position_ref, lines_ref, pick_ref, spread_ref, rows):
    flags = cell_ref.shape[0]
    weight = 0.5 * macro_step
    row_count = spread_ref.shape[0]
    back_rows = pick_ref.shape[1] // 3
    lane = lanes_of((1, size_z))
    row_lane = lanes_of((1, rows.shape[1]))
    slot_lane = lanes_of((flags, back_rows))
    flag_row = lax.broadcasted_iota(jnp.int32, (flags, back_rows), 0)
    rows[3 * flags :, :] = jnp.zeros((product_depth - 3 * flags, rows.shape[1]), jnp.float32)
    slot = jnp.zeros((flags, back_rows), jnp.int32)
    for j in range(flags):
        cell = cell_ref[j]
        row = lax.div(cell, size_z)
        z = cell - row * size_z
        lines_ref[0, j : j + 1, :] = jnp.where(lane == z, weight, 0.0)
        lines_ref[1, j : j + 1, :] = jnp.where(
            lane == z - 1, weight, jnp.where(lane == z + 1, -weight, 0.0)
        )
        for number, shift in enumerate((size_y, 1)):
            rows[number * flags + j : number * flags + j + 1, :] = jnp.where(
                row_lane == row - shift, 1.0, jnp.where(row_lane == row + shift, -1.0, 0.0)
            )
        rows[2 * flags + j : 2 * flags + j + 1, :] = jnp.where(row_lane == row, 1.0, 0.0)
        slot = jnp.where(flag_row == j, position_ref[j], slot)
    spread = rows[...].T[:row_count].astype(jnp.bfloat16)
    pick = jnp.where(slot_lane == slot, 1.0, 0.0).astype(jnp.bfloat16)
    for piece in range(3):
        spread_ref[:, piece * product_depth : (piece + 1) * product_depth] = spread
        pick_ref[:, piece * back_rows : (piece + 1) * back_rows] = pick


def flow_kernel(
    size_x, size_y, size_z, macro_count, cell_ref, position_ref, velocity_ref, viscosity_ref, chunk_ref,
    y_low_ref, y_high_ref, out_ref, corner_ref, edge_ref, lines_ref, pick_ref, spread_ref,
    padded, stress_x, stress_rest, faces, ghost_y, ghost_z, rows,
):
    macro, core = place_of()
    one_hots(size_y, size_z, cell_ref, position_ref, lines_ref, pick_ref, spread_ref, rows)
    inside = (macro > 0, macro < macro_count - 1)
    sign_z = jnp.where(core == 0, 1.0, -1.0)
    end = jnp.where(core == 0, size_z - 1, 0)
    shape = (size_y, size_z)
    lane, row = lanes_of(shape), lax.broadcasted_iota(jnp.int32, shape, 0)
    at_end = jnp.where(lane == end, sign_z, 0.0)

    def kept(value, condition):
        return jnp.where(condition, value, 0.0)

    def plane(x):
        return pl.ds(pl.multiple_of(x * size_y, 8), size_y)

    def difference_z(value):
        lane = lanes_of(value.shape)
        return jnp.where(lane == size_z - 1, 0.0, rolled(value, -1)) - jnp.where(
            lane == 0, 0.0, rolled(value, 1)
        )

    def difference_rows(value, low=0.0, high=0.0):
        count = value.shape[0]
        row = lax.broadcasted_iota(jnp.int32, value.shape, 0)
        return jnp.where(row == count - 1, high, pltpu.roll(value, count - 1, 0)) - jnp.where(
            row == 0, low, pltpu.roll(value, 1, 0)
        )

    x_faces, x_others = [], []
    for s in range(2):
        beside = jnp.maximum(macro - 1, 0) if s == 0 else jnp.minimum(macro + 1, macro_count - 1)
        x_faces.append(
            [
                kept(chunk_ref[2 * beside + core, slot_rows + i * size_y : slot_rows + (i + 1) * size_y, :], inside[s])
                for i in range(item_count)
            ]
        )
        x_others.append(
            [
                kept(
                    rolled(
                        chunk_ref[
                            2 * beside + 1 - core, slot_rows + i * size_y : slot_rows + (i + 1) * size_y, :
                        ],
                        2 * end + 1,
                    ),
                    inside[s],
                )
                for i in range(2)
            ]
        )

    group = size_z // 8
    packed = [
        chunk_ref[2 * macro + 1 - core, slot_rows + i * size_y : slot_rows + (i + 1) * size_y, :]
        for i in range(-(-size_x // group))
    ]
    for i, value in enumerate(packed):

        def unpack(x, carry):
            for q in range(item_count):
                a, layer = (q, 0) if q < 4 else (q - 4, 1)
                at = 8 * (x - i * group) + 2 * a + (core if layer == 0 else 1 - core)
                faces[q, x + 1] = rolled(value, end - at)
            return carry

        lax.fori_loop(i * group, min(size_x, (i + 1) * group), unpack, 0, unroll=8)
    faces[2, 0] = x_others[0][1]
    faces[2, size_x + 1] = x_others[1][1]

    for a in range(3):
        padded[a, 0] = x_faces[0][a]
        padded[a, size_x + 1] = x_faces[1][a]

    def fill(x, carry):
        for a in range(3):
            padded[a, x + 1] = velocity_ref[a, plane(x), :]
        return carry

    lax.fori_loop(0, size_x, fill, 0, unroll=True)

    rest = {(1, 1): 0, (2, 2): 1, (1, 2): 2}

    def stress_plane(x, carry):
        along_x, along_y, along_z, centre = [], [], [], []
        for a in range(3):
            value = padded[a, x + 1]
            centre.append(value)
            along_x.append(padded[a, x + 2] - padded[a, x])
            along_y.append(
                difference_rows(value, y_low_ref[a, pl.ds(x, 1), :], y_high_ref[a, pl.ds(x, 1), :])
            )
            along_z.append(difference_z(value) + faces[a, x + 1] * at_end)
        slopes = (along_x, along_y, along_z)
        half = 0.5 * viscosity_ref[plane(x), :]
        for a, b in stress_pairs:
            value = half * (slopes[b][a] + slopes[a][b])
            if a == 0:
                stress_x[b, x + 1] = value
            else:
                stress_rest[rest[a, b], x] = value
        weight = (0.5 * faces[3, x + 1]) * at_end
        normal = [(faces[4 + a, x + 1] - centre[a]) * sign_z for a in range(3)]
        ghost_z[0, x] = weight * (normal[0] + (faces[2, x + 2] - faces[2, x]))
        ghost_z[1, x] = weight * (normal[1] + difference_rows(faces[2, x + 1]))
        ghost_z[2, x] = weight * (2.0 * normal[2])
        return carry

    lax.fori_loop(0, size_x, stress_plane, 0, unroll=6)

    for s in range(2):
        near, far, weight = x_faces[s][0:3], x_faces[s][3:6], 0.5 * x_faces[s][6]
        sign = -1.0 if s == 0 else 1.0
        normal = [(far[a] - padded[a, 1 if s == 0 else size_x]) * sign for a in range(3)]
        slope_y = difference_rows(near[0])
        slope_z = difference_z(near[0]) + x_others[s][0] * at_end
        at = 0 if s == 0 else size_x + 1
        stress_x[0, at] = weight * (2.0 * normal[0])
        stress_x[1, at] = weight * (normal[1] + slope_y)
        stress_x[2, at] = weight * (normal[2] + slope_z)
        for u in range(2):
            y, sign_y = (0, -1.0) if u == 0 else (size_y - 1, 1.0)
            number = 4 * s + 2 * u
            corner_ref[number : number + 1, :] = (0.5 * macro_step * sign * sign_y) * weight[y : y + 1, :]

    for u, ref in enumerate((y_low_ref, y_high_ref)):
        y, sign = (0, -1.0) if u == 0 else (size_y - 1, 1.0)
        weight = 0.5 * ref[6]
        normal = [
            (ref[3 + a] - velocity_ref[a, pl.ds(y, size_x, stride=size_y), :]) * sign for a in range(3)
        ]
        ghost_y[3 * u] = weight * (normal[0] + difference_rows(ref[1]))
        ghost_y[3 * u + 1] = weight * (2.0 * normal[1])
        ghost_y[3 * u + 2] = weight * (normal[2] + difference_z(ref[1]))
        for s in range(2):
            x, sign_x = (0, -1.0) if s == 0 else (size_x - 1, 1.0)
            number = 4 * s + 2 * u + 1
            corner_ref[number : number + 1, :] = (0.5 * macro_step * sign * sign_x) * weight[x : x + 1, :]
        wide = lanes_of((size_x, size_z))
        scale = jnp.where(wide == end, (0.5 * macro_step * sign) * sign_z, 0.0)
        edge_ref[2 * u] = scale * weight
        for x in range(size_x):
            edge_ref[2 * u + 1, x : x + 1, :] = scale[x : x + 1, :] * (0.5 * faces[3, x + 1, y : y + 1, :])

    columns = {(0, 1): (stress_x, 1, 1), (1, 1): (stress_rest, 0, 0), (2, 1): (stress_rest, 2, 0)}
    columns_z = {0: (stress_x, 2, 1), 1: (stress_rest, 2, 0), 2: (stress_rest, 1, 0)}

    def step_plane(x, carry):
        for a in range(3):
            total = stress_x[a, x + 2] - stress_x[a, x]
            ref, number, shift = columns[a, 1]
            total = total + difference_rows(
                ref[number, x + shift], ghost_y[a, pl.ds(x, 1), :], ghost_y[3 + a, pl.ds(x, 1), :]
            )
            ref, number, shift = columns_z[a]
            total = total + (difference_z(ref[number, x + shift]) + ghost_z[a, x])
            out_ref[a, plane(x), :] = padded[a, x + 1] + (0.5 * macro_step) * total
        return carry

    lax.fori_loop(0, size_x, step_plane, 0, unroll=6)


def flow_step(flag_cell, position, velocity, viscosity, chunks, y_low, y_high):
    size_x, size_y, size_z = viscosity.shape
    flags = flag_cell.shape[0]
    back_rows = chunks.shape[0] * (slot_rows + line_rows)
    row_count = size_x * size_y
    planes = (size_x, size_y, size_z)
    wide = (size_x + 2, size_y, size_z)
    return pl.pallas_call(
        functools.partial(flow_kernel, size_x, size_y, size_z, chunks.shape[0] // 2),
        out_shape=(
            jax.ShapeDtypeStruct((3, size_x * size_y, size_z), jnp.float32),
            jax.ShapeDtypeStruct((8, size_z), jnp.float32),
            jax.ShapeDtypeStruct((4, size_x, size_z), jnp.float32),
            jax.ShapeDtypeStruct((2, flags, size_z), jnp.float32),
            jax.ShapeDtypeStruct((flags, 3 * back_rows), jnp.bfloat16),
            jax.ShapeDtypeStruct((row_count, 3 * product_depth), jnp.bfloat16),
        ),
        in_specs=[SMEM] * 2 + [VMEM] * 5,
        out_specs=(VMEM,) * 6,
        scratch_shapes=[
            pltpu.VMEM((3, *wide), jnp.float32),
            pltpu.VMEM((3, *wide), jnp.float32),
            pltpu.VMEM((3, *planes), jnp.float32),
            pltpu.VMEM((item_count, *wide), jnp.float32),
            pltpu.VMEM((6, size_x, size_z), jnp.float32),
            pltpu.VMEM((3, *planes), jnp.float32),
            pltpu.VMEM((product_depth, -(-row_count // 128) * 128), jnp.float32),
        ],
        compiler_params=limit(12),
        cost_estimate=pl.CostEstimate(flops=4000000, bytes_accessed=3000000, transcendentals=0),
        name="flow_step",
    )(
        flag_cell, position,
        velocity.reshape(3, size_x * size_y, size_z),
        viscosity.reshape(size_x * size_y, size_z),
        chunks, y_low, y_high,
    )


def pieces(value):
    high = value.astype(jnp.bfloat16)
    rest = value - high.astype(jnp.float32)
    middle = rest.astype(jnp.bfloat16)
    return high, middle, (rest - middle.astype(jnp.float32)).astype(jnp.bfloat16)


def polymer_kernel(
    size_x, size_y, size_z, macro_count, chunk_ref, viscous_ref, corner_ref, edge_ref, lines_ref, pick_ref,
    spread_ref, partial_ref, out_ref, flag_ref, field, write_sem,
):
    flags = viscous_ref.shape[0]
    chunk_rows = slot_rows + line_rows
    macro, core = place_of()
    values = jnp.dot(
        pick_ref[...], jnp.concatenate(pieces(chunk_ref[...]), axis=0), preferred_element_type=jnp.float32
    )
    here, beside_z = lines_ref[0], lines_ref[1]
    columns = [jnp.broadcast_to(values[:, k : k + 1], (flags, size_z)) for k in range(6)]
    unused = jnp.zeros((product_depth - 3 * flags, size_z), jnp.float32)
    split = [
        pieces(
            jnp.concatenate(
                [
                    columns[pair_index(a, 0)] * here, columns[pair_index(a, 1)] * here,
                    columns[pair_index(a, 2)] * beside_z, unused,
                ],
                axis=0,
            )
        )
        for a in range(3)
    ]
    flag_ref[...] = (viscous_ref[...] + values).T[0:6, :]

    field[...] = partial_ref[...]
    for s in range(2):
        inside = macro > 0 if s == 0 else macro < macro_count - 1
        beside = jnp.maximum(macro - 1, 0) if s == 0 else jnp.minimum(macro + 1, macro_count - 1)
        start = (2 * beside + core) * chunk_rows + slot_rows
        x = 0 if s == 0 else size_x - 1
        for u in range(2):
            at = x * size_y + (0 if u == 0 else size_y - 1)
            for a in range(2):
                number = 4 * s + 2 * u + a
                line = corner_ref[number : number + 1, :] * chunk_ref[pl.ds(start + 2 * u + a, 1), :]
                field[1 - a, at : at + 1, :] += jnp.where(inside, line, 0.0)
    start = pl.multiple_of((2 * macro + 1 - core) * chunk_rows + slot_rows, 8)
    packed = chunk_ref[pl.ds(start, line_rows), :]
    end = jnp.where(core == 0, size_z - 1, 0)
    for u in range(2):
        y = 0 if u == 0 else size_y - 1
        for a in range(2):
            for i in range(size_x // 8):
                line = rolled(packed, end - (4 * i + 2 * u + a)) * edge_ref[2 * u + a, 8 * i : 8 * i + 8, :]
                at = pl.ds(8 * i * size_y + y, 8, stride=size_y)
                field[2 - a, at, :] += line
    copies = [pltpu.make_async_copy(field.at[a], out_ref.at[a], write_sem.at[a]) for a in range(3)]
    for a in range(3):
        field[a] += jnp.dot(
            spread_ref[...], jnp.concatenate(split[a], axis=0), preferred_element_type=jnp.float32
        )
        copies[a].start()
    for copy in copies:
        copy.wait()


def add_polymer(chunks, viscous, corners, edges, lines, pick, spread, partial, shape):
    flags = viscous.shape[0]
    size_x, size_y, size_z = shape
    return pl.pallas_call(
        functools.partial(polymer_kernel, size_x, size_y, size_z, chunks.shape[0] // 2),
        out_shape=(
            jax.ShapeDtypeStruct(partial.shape, jnp.float32),
            jax.ShapeDtypeStruct((6, flags), jnp.float32),
        ),
        in_specs=[VMEM] * 8,
        out_specs=(pl.BlockSpec(memory_space=pltpu.HBM), VMEM),
        scratch_shapes=[pltpu.VMEM(partial.shape, jnp.float32), pltpu.SemaphoreType.DMA((3,))],
        compiler_params=limit(8),
        cost_estimate=pl.CostEstimate(flops=400000, bytes_accessed=3000000, transcendentals=0),
        name="add_polymer",
    )(chunks.reshape(-1, 128), viscous, corners, edges, lines, pick, spread, partial)


def shards(velocity, viscosity, flag_cell, flag_owner, conformations, increments):
    macro_count = lax.axis_size("macro")
    tile_count = lax.axis_size("tile")
    assert lax.axis_size("micro") == 2
    owner_count = 2 * macro_count
    capacity = conformations.shape[1] // owner_count
    size_x, size_y, size_z = viscosity.shape
    assert capacity <= slot_rows and size_y == 8 and size_z == 128 and size_x % 8 == 0 and size_x <= 48
    chunks, position, viscous, y_first, y_last, first_conform, first_noise = gather_rows(
        flag_cell, flag_owner.reshape(-1), velocity, viscosity, conformations, increments, capacity, owner_count
    )

    def exchange(rows):
        return lax.all_to_all(rows, ("macro", "micro"), split_axis=0, concat_axis=0, tiled=True)

    received = exchange(chunks.reshape(owner_count, -1, 128))
    up = [(i, i + 1) for i in range(tile_count - 1)]
    down = [(target, source) for source, target in up]
    y_low = lax.ppermute(y_last, "tile", up)
    y_high = lax.ppermute(y_first, "tile", down)
    last_state, polymer = advance(
        conformations, increments, received, first_conform, first_noise, capacity
    )
    returned = exchange(add_lines(polymer, y_low, y_high))
    partial, corners, edges, lines, pick, spread = flow_step(
        flag_cell, position, velocity, viscosity, received, y_low, y_high
    )
    velocity_next, flag_stress = add_polymer(
        returned, viscous, corners, edges, lines, pick, spread, partial, viscosity.shape
    )
    return (velocity_next.reshape(velocity.shape), last_state, flag_stress)


def solution(mesh):
    in_specs = (
        P(None, "macro", "tile", "micro"),
        P("macro", "tile", "micro"),
        P(("macro", "tile", "micro")),
        P(("macro", "tile", "micro"), None),
        P(None, ("macro", "tile", "micro"), None),
        P(None, None, ("macro", "tile", "micro"), None),
    )
    out_specs = (
        P(None, "macro", "tile", "micro"),
        P(None, ("macro", "tile", "micro"), None),
        P(None, ("macro", "tile", "micro")),
    )
    return jax.shard_map(shards, mesh=mesh, in_specs=in_specs, out_specs=out_specs, check_vma=False)
```

```python
import functools

import jax
import jax.numpy as jnp
from jax import lax
from jax.experimental import pallas as pl
from jax.experimental.pallas import tpu as pltpu
from jax.sharding import PartitionSpec as P

stress_pairs = ((0, 0), (1, 1), (2, 2), (0, 1), (0, 2), (1, 2))
macro_step = 0.1
micro_step = 0.01
noise_weight = 0.1
relax_rate = 0.5
fene_extent = 30.0
spring_floor = 0.1
polymer_weight = 0.25

SMEM = pl.BlockSpec(memory_space=pltpu.SMEM)
VMEM = pl.BlockSpec(memory_space=pltpu.VMEM)


def pair_index(left_axis, right_axis):
    return stress_pairs.index((min(left_axis, right_axis), max(left_axis, right_axis)))


def lanes_of(shape):
    return lax.broadcasted_iota(jnp.int32, shape, len(shape) - 1)


slot_rows = 8
item_count = 7
back_rows = 8
polymer_row = 4
line_lane = 64


block_slots = 32
first_share = 2


def limit(mebibytes):
    return pltpu.CompilerParams(vmem_limit_bytes=mebibytes * 1024 * 1024)


def far(value):
    return pltpu.with_memory_space_constraint(value, pltpu.HBM)


def place_of():
    return lax.axis_index("macro"), lax.axis_index("micro")


def neighbour(index, side, count):
    return jnp.maximum(index - 1, 0) if side == 0 else jnp.minimum(index + 1, count - 1)


def rolled(value, amount):
    size = value.shape[-1]
    if isinstance(amount, int):
        return pltpu.roll(value, amount % size, value.ndim - 1)
    return pltpu.roll(value, lax.rem(amount + 2 * size, size), value.ndim - 1)


def gather_kernel(
    capacity, size_x, size_y, size_z, macro_count, cell_in, owner_in, velocity_in, viscosity_in,
    conform_in, noise_in, chunk_ref, position_ref, viscous_ref, y_low_ref, y_high_ref, conform_ref, noise_ref,
    cell_ref, owner_ref, velocity_ref, viscosity_ref, masked, gradients, target, count, sems,
):
    flags = cell_ref.shape[0]
    copies = [
        pltpu.make_async_copy(source, into, sems.at[number])
        for number, (source, into) in enumerate(
            (
                (cell_in, cell_ref), (owner_in, owner_ref), (velocity_in, velocity_ref),
                (viscosity_in, viscosity_ref), (conform_in.at[:, 0:block_slots, :], conform_ref),
                (noise_in.at[0 : noise_ref.shape[0], :, 0:block_slots, :], noise_ref),
            )
        )
    ]
    for copy in copies:
        copy.start()
    chunk_rows = slot_rows + item_count * size_y
    macro, core = place_of()
    lane = lanes_of((1, size_z))

    for owner in range(count.shape[0]):
        count[owner] = 0
        chunk_ref[owner * chunk_rows : owner * chunk_rows + slot_rows, :] = jnp.zeros((slot_rows, 128), jnp.float32)
    for copy in copies[:2]:
        copy.wait()
    for j in range(flags):
        owner = owner_ref[j]
        rank = count[owner]
        count[owner] = rank + 1
        target[j] = owner * chunk_rows + rank
        position_ref[j] = owner * slot_rows + rank
    for copy in copies[2:4]:
        copy.wait()
    planes = velocity_ref.reshape(3, size_x, size_y, size_z)
    layers = viscosity_ref.reshape(size_x, size_y, size_z)
    for j in range(flags):
        cell = cell_ref[j]
        x = lax.shift_right_logical(cell, 10)
        y = lax.shift_right_logical(cell, 7) & (size_y - 1)
        z = cell & (size_z - 1)
        here = (lane == z).astype(jnp.float32)
        along_z = (lane == z + 1).astype(jnp.float32) - (lane == z - 1).astype(jnp.float32)
        at = pl.ds(y, 1)
        for a in range(3):
            along_x = planes[a, x + 1, at, :] - planes[a, x - 1, at, :]
            along_y = planes[a, x, pl.ds(y + 1, 1), :] - planes[a, x, pl.ds(y - 1, 1), :]
            masked[3 * a, j : j + 1, :] = along_x * here
            masked[3 * a + 1, j : j + 1, :] = along_y * here
            masked[3 * a + 2, j : j + 1, :] = planes[a, x, at, :] * along_z
        masked[9, j : j + 1, :] = layers[x, at, :] * here

    for side, ref in enumerate((y_low_ref, y_high_ref)):
        for layer in range(2):
            y = layer if side == 0 else size_y - 1 - layer
            for a in range(3):
                ref[3 * layer + a] = velocity_ref[a, pl.ds(y, size_x, stride=size_y), :]
        y = 0 if side == 0 else size_y - 1
        ref[6] = viscosity_ref[pl.ds(y, size_x, stride=size_y), :]

    for side in range(2):
        beside = neighbour(macro, side, macro_count)
        first = pl.multiple_of((2 * beside + core) * chunk_rows + slot_rows, 8)
        other = pl.multiple_of((2 * beside + 1 - core) * chunk_rows + slot_rows, 8)
        for layer in range(2):
            x = layer if side == 0 else size_x - 1 - layer
            for a in range(3):
                chunk_ref[pl.ds(first + (3 * layer + a) * size_y, size_y), :] = velocity_ref[
                    a, x * size_y : (x + 1) * size_y, :
                ]
        x = 0 if side == 0 else size_x - 1
        chunk_ref[pl.ds(first + 6 * size_y, size_y), :] = viscosity_ref[x * size_y : (x + 1) * size_y, :]
        for number, a in enumerate((0, 2)):
            chunk_ref[pl.ds(other + number * size_y, size_y), :] = velocity_ref[
                a, x * size_y : (x + 1) * size_y, :
            ]

    group = size_z // 8
    lane2 = lanes_of((size_y, size_z))
    first = pl.multiple_of((2 * macro + 1 - core) * chunk_rows + slot_rows, 8)
    source = jnp.where(core == 0, size_z - 2, 0)
    for block in range(-(-size_x // group)):
        total = jnp.zeros((size_y, size_z), jnp.float32)
        for x in range(block * group, min(size_x, (block + 1) * group)):
            rows = slice(x * size_y, (x + 1) * size_y)
            for a in range(4):
                at = 8 * (x - block * group) + 2 * a
                value = viscosity_ref[rows, :] if a == 3 else velocity_ref[a, rows, :]
                total = jnp.where((lane2 == at) | (lane2 == at + 1), rolled(value, at - source), total)
        chunk_ref[pl.ds(first + block * size_y, size_y), :] = total

    columns = [0.5 * jnp.sum(masked[c], axis=1, keepdims=True) for c in range(9)]
    viscous = jnp.sum(masked[9], axis=1, keepdims=True)
    wide = lanes_of((flags, 128))
    packed = jnp.zeros((flags, 128), jnp.float32)
    for c in range(9):
        packed = jnp.where(wide == c, columns[c], packed)
    gradients[...] = packed
    stress = jnp.zeros((flags, 128), jnp.float32)
    for k, (a, b) in enumerate(stress_pairs):
        stress = jnp.where(wide == k, viscous * (columns[3 * a + b] + columns[3 * b + a]), stress)
    viscous_ref[...] = stress

    for j in range(flags):
        chunk_ref[pl.ds(target[j], 1), :] = gradients[j : j + 1, :]
    for copy in copies[4:]:
        copy.wait()


def gather_rows(flag_cell, owner, velocity, viscosity, conformations, increments, capacity, owner_count):
    size_x, size_y, size_z = viscosity.shape
    flags = flag_cell.shape[0]
    chunk_rows = slot_rows + item_count * size_y
    face = pltpu.HBM((item_count, size_x, size_z), jnp.float32)
    steps, _, _, dumbbells = increments.shape
    return pl.pallas_call(
        functools.partial(gather_kernel, capacity, size_x, size_y, size_z, owner_count // 2),
        out_shape=(
            jax.ShapeDtypeStruct((owner_count * chunk_rows, 128), jnp.float32),
            jax.ShapeDtypeStruct((flags,), jnp.int32),
            jax.ShapeDtypeStruct((flags, 128), jnp.float32),
            face,
            face,
            pltpu.VMEM((3, block_slots, dumbbells), jnp.float32),
            pltpu.VMEM((steps // first_share, 3, block_slots, dumbbells), jnp.bfloat16),
        ),
        in_specs=[pl.BlockSpec(memory_space=pltpu.HBM)] * 6,
        out_specs=(VMEM, SMEM, VMEM, VMEM, VMEM, VMEM, VMEM),
        scratch_shapes=[
            pltpu.SMEM((flags,), jnp.int32),
            pltpu.SMEM((flags,), jnp.int32),
            pltpu.VMEM((3, size_x * size_y, size_z), jnp.float32),
            pltpu.VMEM((size_x * size_y, size_z), jnp.float32),
            pltpu.VMEM((10, flags, size_z), jnp.float32),
            pltpu.VMEM((flags, 128), jnp.float32),
            pltpu.SMEM((flags,), jnp.int32),
            pltpu.SMEM((owner_count,), jnp.int32),
            pltpu.SemaphoreType.DMA((6,)),
        ],
        compiler_params=limit(8),
        cost_estimate=pl.CostEstimate(flops=400000, bytes_accessed=3000000, transcendentals=0),
        name="gather_rows",
    )(
        far(flag_cell),
        far(owner),
        far(velocity.reshape(3, size_x * size_y, size_z)),
        far(viscosity.reshape(size_x * size_y, size_z)),
        far(conformations),
        far(increments),
    )


def micro_kernel(
    capacity, parts, rows, groups, conform_ref, noise_ref, rate_ref, first_conform_ref, first_noise_ref,
    next_ref, chunk_ref, conform, noise, rate, rate_wide, sums_ref, read_sem, noise_sem,
):
    steps, _, slots, dumbbells = noise_ref.shape
    blocks = slots // rows
    span = steps // groups
    width = dumbbells // parts
    owners = slots // capacity
    scale = 1.0 / noise_weight
    extent = fene_extent * scale * scale

    def block_rows(block):
        return pl.ds(pl.multiple_of(block * rows, rows), rows)

    def read(block):
        at = block_rows(block)
        return pltpu.make_async_copy(conform_ref.at[:, at, :], conform.at[:, at, :], read_sem.at[block])

    def read_noise(block, group):
        at, when = block_rows(block), pl.ds(group * span, span)
        return pltpu.make_async_copy(
            noise_ref.at[when, :, at, :], noise.at[when, :, at, :], noise_sem.at[block, group]
        )

    pieces = [
        (half, slice(part * width, (part + 1) * width)) for half in range(rows // 16) for part in range(parts)
    ]
    assert len(pieces) == 8
    early = groups // first_share
    for block in range(blocks):
        if block > 0:
            read(block).start()
        for group in range(early if block == 0 else 0, groups):
            read_noise(block, group).start()
    conform[:, 0:rows, :] = first_conform_ref[...]
    for step in range(steps // first_share):
        noise[step, :, 0:rows, :] = first_noise_ref[step]
    for owner in range(owners):
        rate[owner * capacity : (owner + 1) * capacity, :] = rate_ref[owner, 0:capacity, :]
        chunk_ref[owner] = jnp.zeros(chunk_ref.shape[1:], jnp.float32)
    for a in range(3):
        for b in range(3):
            column = micro_step * rate[:, 3 * a + b : 3 * a + b + 1] + (1.0 if a == b else 0.0)
            rate_wide[3 * a + b] = jnp.broadcast_to(column, (slots, width))

    def inverses(state, scale):
        rooms = []
        for piece in range(len(pieces)):
            q = state[3 * piece : 3 * piece + 3]
            room = (extent - q[0] * q[0]) - (q[1] * q[1] + q[2] * q[2])
            rooms.append(jnp.maximum(room, extent * spring_floor))
        levels = [rooms]
        while len(levels[-1]) > 1:
            levels.append([low * high for low, high in zip(levels[-1][0::2], levels[-1][1::2])])
        result = [scale * pl.reciprocal(levels[-1][0])]
        for level in reversed(levels[:-1]):
            result = [result[i // 2] * level[i ^ 1] for i in range(len(level))]
        return result

    def advance_block(block, carry):
        ats = [pl.ds(pl.multiple_of(block * rows + 16 * half, 16), 16) for half in range(rows // 16)]
        rates = [
            [[rate_wide.at[3 * a + b, at, :] for b in range(3)] for a in range(3)] for at in ats
        ]

        def substep(step, state):
            updated = []
            springs = inverses(state, micro_step * relax_rate * extent)
            for piece, (half, lanes) in enumerate(pieces):
                q = state[3 * piece : 3 * piece + 3]
                table = rates[half]
                for a in range(3):
                    b, c = [other for other in range(3) if other != a]
                    kick = noise[step, a, ats[half], lanes].astype(jnp.float32)
                    rest = (table[a][b][...] * q[b] + table[a][c][...] * q[c]) + kick
                    updated.append((table[a][a][...] - springs[piece]) * q[a] + rest)
            return tuple(updated)

        def advance_group(group, state):
            if group < early:

                @pl.when(block > 0)
                def _():
                    read_noise(block, group).wait()

            else:
                read_noise(block, group).wait()
            for step in range(span):
                state = substep(group * span + step, state)
            return state

        @pl.when(block > 0)
        def _():
            read(block).wait()

        state = tuple(conform[a, ats[half], lanes] * scale for half, lanes in pieces for a in range(3))
        for group in range(groups):
            state = advance_group(group, state)
        inverse = inverses(state, 1.0)
        for half, at in enumerate(ats):
            sums = [None] * 6
            for piece, (other, lanes) in enumerate(pieces):
                if other != half:
                    continue
                q = state[3 * piece : 3 * piece + 3]
                for a in range(3):
                    next_ref[a, at, lanes] = q[a] * noise_weight
                for k, (a, b) in enumerate(stress_pairs):
                    term = (inverse[piece] * q[a]) * q[b]
                    sums[k] = term if sums[k] is None else sums[k] + term
            for k in range(6):
                sums_ref[k, at, :] = sums[k]
        return carry

    lax.fori_loop(0, blocks, advance_block, 0)
    lane = lanes_of((slots, 128))
    rank = lax.broadcasted_iota(jnp.int32, (slots, 128), 0) & (capacity - 1)
    packed = jnp.zeros((slots, 128), jnp.float32)
    weight = extent * noise_weight * noise_weight / dumbbells
    for k, (a, b) in enumerate(stress_pairs):
        mean = jnp.sum(sums_ref[k], axis=1, keepdims=True) * weight
        packed = jnp.where(lane == 8 * rank + k, polymer_weight * (mean - (1.0 if a == b else 0.0)), packed)
    for owner in range(owners):
        chunk_ref[owner, polymer_row : polymer_row + 1, :] = jnp.sum(
            packed[owner * capacity : (owner + 1) * capacity], axis=0, keepdims=True
        )


def advance(conformations, increments, chunks, first_conform, first_noise, capacity):
    slots, dumbbells = conformations.shape[1:]
    steps = increments.shape[0]
    owners = slots // capacity
    rows, parts, groups = block_slots, 4, 4
    blocks = slots // rows
    whole = pl.BlockSpec(memory_space=pltpu.HBM)
    return pl.pallas_call(
        functools.partial(micro_kernel, capacity, parts, rows, groups),
        out_shape=(
            pltpu.VMEM(conformations.shape, jnp.float32),
            jax.ShapeDtypeStruct((owners, back_rows, 128), jnp.float32),
        ),
        in_specs=[whole, whole, VMEM, VMEM, VMEM],
        out_specs=(VMEM, VMEM),
        scratch_shapes=[
            pltpu.VMEM(conformations.shape, jnp.float32),
            pltpu.VMEM(increments.shape, jnp.bfloat16),
            pltpu.VMEM((slots, 128), jnp.float32),
            pltpu.VMEM((9, slots, dumbbells // parts), jnp.float32),
            pltpu.VMEM((6, slots, dumbbells // parts), jnp.float32),
            pltpu.SemaphoreType.DMA((blocks,)),
            pltpu.SemaphoreType.DMA((blocks, groups)),
        ],
        compiler_params=limit(12),
        cost_estimate=pl.CostEstimate(flops=20000000, bytes_accessed=5000000, transcendentals=600000),
        name="advance",
    )(far(conformations), far(increments), chunks, first_conform, first_noise)


def lines_kernel(macro_count, chunk_ref, y_low_ref, y_high_ref, out_ref):
    out_ref[...] = chunk_ref[...]
    macro, core = place_of()
    sides = (y_low_ref, y_high_ref)
    size_x, size_z = y_low_ref.shape[1:]
    for side in range(2):
        beside = neighbour(macro, side, macro_count)
        x = 0 if side == 0 else size_x - 1
        for u in range(2):
            for a in range(2):
                at = 2 * u + a
                out_ref[2 * beside + core, at : at + 1, :] = sides[u][a, x : x + 1, :]

    lane = lanes_of((8, size_z))
    source = jnp.where(core == 0, size_z - 1, 0)
    other = 2 * macro + 1 - core
    total = chunk_ref[other]
    for i in range(size_x // 8):
        for u in range(2):
            for a in range(2):
                at = line_lane + 4 * i + 2 * u + a
                total = jnp.where(
                    lane == at, rolled(sides[u][1 + a, 8 * i : 8 * i + 8, :], at - source), total
                )
    out_ref[other] = total


def add_lines(chunks, y_low, y_high):
    return pl.pallas_call(
        functools.partial(lines_kernel, chunks.shape[0] // 2),
        out_shape=jax.ShapeDtypeStruct(chunks.shape, jnp.float32),
        in_specs=[VMEM, VMEM, VMEM],
        out_specs=VMEM,
        compiler_params=limit(4),
        cost_estimate=pl.CostEstimate(flops=20000, bytes_accessed=400000, transcendentals=0),
        name="add_lines",
    )(chunks, y_low, y_high)


product_depth = 128


def one_hots(size_y, size_z, cell_ref, position_ref, lines_ref, pick_ref, spread_ref, rows):
    flags = cell_ref.shape[0]
    weight = 0.5 * macro_step
    row_count = spread_ref.shape[0]
    returned = pick_ref.shape[1] // 4
    lane = lanes_of((1, size_z))
    row_lane = lanes_of((1, rows.shape[1]))
    slot_lane = lanes_of((flags, returned))
    flag_row = lax.broadcasted_iota(jnp.int32, (flags, returned), 0)
    rows[3 * flags :, :] = jnp.zeros((product_depth - 3 * flags, rows.shape[1]), jnp.float32)
    slot = jnp.zeros((flags, returned), jnp.int32)
    group = lax.shift_right_logical(lane, 3)
    for j in range(flags):
        cell = cell_ref[j]
        row = lax.div(cell, size_z)
        z = cell - row * size_z
        lines_ref[0, j : j + 1, :] = jnp.where(lane == z, weight, 0.0)
        lines_ref[1, j : j + 1, :] = jnp.where(
            lane == z - 1, weight, jnp.where(lane == z + 1, -weight, 0.0)
        )
        for number, shift in enumerate((size_y, 1)):
            rows[number * flags + j : number * flags + j + 1, :] = jnp.where(
                row_lane == row - shift, 1.0, jnp.where(row_lane == row + shift, -1.0, 0.0)
            )
        rows[2 * flags + j : 2 * flags + j + 1, :] = jnp.where(row_lane == row, 1.0, 0.0)
        owner = lax.div(position_ref[j], slot_rows)
        rank = position_ref[j] - owner * slot_rows
        lines_ref[2, j : j + 1, :] = jnp.where(group == rank, 1.0, 0.0)
        slot = jnp.where(flag_row == j, owner * back_rows + polymer_row, slot)
    spread = rows[...].T[:row_count].astype(jnp.bfloat16)
    pick = jnp.where(slot_lane == slot, 1.0, 0.0).astype(jnp.bfloat16)
    for piece in range(3):
        spread_ref[:, piece * product_depth : (piece + 1) * product_depth] = spread
        pick_ref[:, piece * returned : (piece + 1) * returned] = pick
    pick_ref[:, 3 * returned :] = jnp.zeros((flags, returned), jnp.bfloat16)


def flow_kernel(
    size_x, size_y, size_z, macro_count, cell_ref, position_ref, velocity_ref, viscosity_ref, chunk_ref,
    y_low_ref, y_high_ref, out_ref, corner_ref, edge_ref, lines_ref, pick_ref, spread_ref,
    padded, stress_x, stress_rest, faces, ghost_y, ghost_z, rows,
):
    macro, core = place_of()
    one_hots(size_y, size_z, cell_ref, position_ref, lines_ref, pick_ref, spread_ref, rows)
    inside = (macro > 0, macro < macro_count - 1)
    sign_z = jnp.where(core == 0, 1.0, -1.0)
    end = jnp.where(core == 0, size_z - 1, 0)
    shape = (size_y, size_z)
    lane, row = lanes_of(shape), lax.broadcasted_iota(jnp.int32, shape, 0)
    at_end = jnp.where(lane == end, sign_z, 0.0)

    def kept(value, condition):
        return jnp.where(condition, value, 0.0)

    def plane(x):
        return pl.ds(pl.multiple_of(x * size_y, 8), size_y)

    def difference_z(value):
        lane = lanes_of(value.shape)
        return jnp.where(lane == size_z - 1, 0.0, rolled(value, -1)) - jnp.where(
            lane == 0, 0.0, rolled(value, 1)
        )

    def difference_rows(value, low=0.0, high=0.0):
        count = value.shape[0]
        row = lax.broadcasted_iota(jnp.int32, value.shape, 0)
        return jnp.where(row == count - 1, high, pltpu.roll(value, count - 1, 0)) - jnp.where(
            row == 0, low, pltpu.roll(value, 1, 0)
        )

    x_faces, x_others = [], []
    for s in range(2):
        beside = jnp.maximum(macro - 1, 0) if s == 0 else jnp.minimum(macro + 1, macro_count - 1)
        x_faces.append(
            [
                kept(chunk_ref[2 * beside + core, slot_rows + i * size_y : slot_rows + (i + 1) * size_y, :], inside[s])
                for i in range(item_count)
            ]
        )
        x_others.append(
            [
                kept(
                    rolled(
                        chunk_ref[
                            2 * beside + 1 - core, slot_rows + i * size_y : slot_rows + (i + 1) * size_y, :
                        ],
                        2 * end + 1,
                    ),
                    inside[s],
                )
                for i in range(2)
            ]
        )

    group = size_z // 8
    packed = [
        chunk_ref[2 * macro + 1 - core, slot_rows + i * size_y : slot_rows + (i + 1) * size_y, :]
        for i in range(-(-size_x // group))
    ]
    for i, value in enumerate(packed):

        def unpack(x, carry):
            for q in range(item_count):
                a, layer = (q, 0) if q < 4 else (q - 4, 1)
                at = 8 * (x - i * group) + 2 * a + (core if layer == 0 else 1 - core)
                faces[q, x + 1] = rolled(value, end - at)
            return carry

        lax.fori_loop(i * group, min(size_x, (i + 1) * group), unpack, 0, unroll=8)
    faces[2, 0] = x_others[0][1]
    faces[2, size_x + 1] = x_others[1][1]

    for a in range(3):
        padded[a, 0] = x_faces[0][a]
        padded[a, size_x + 1] = x_faces[1][a]

    def fill(x, carry):
        for a in range(3):
            padded[a, x + 1] = velocity_ref[a, plane(x), :]
        return carry

    lax.fori_loop(0, size_x, fill, 0, unroll=True)

    rest = {(1, 1): 0, (2, 2): 1, (1, 2): 2}

    def stress_plane(x, carry):
        along_x, along_y, along_z, centre = [], [], [], []
        for a in range(3):
            value = padded[a, x + 1]
            centre.append(value)
            along_x.append(padded[a, x + 2] - padded[a, x])
            along_y.append(
                difference_rows(value, y_low_ref[a, pl.ds(x, 1), :], y_high_ref[a, pl.ds(x, 1), :])
            )
            along_z.append(difference_z(value) + faces[a, x + 1] * at_end)
        slopes = (along_x, along_y, along_z)
        half = 0.5 * viscosity_ref[plane(x), :]
        for a, b in stress_pairs:
            value = half * (slopes[b][a] + slopes[a][b])
            if a == 0:
                stress_x[b, x + 1] = value
            else:
                stress_rest[rest[a, b], x] = value
        weight = (0.5 * faces[3, x + 1]) * at_end
        normal = [(faces[4 + a, x + 1] - centre[a]) * sign_z for a in range(3)]
        ghost_z[0, x] = weight * (normal[0] + (faces[2, x + 2] - faces[2, x]))
        ghost_z[1, x] = weight * (normal[1] + difference_rows(faces[2, x + 1]))
        ghost_z[2, x] = weight * (2.0 * normal[2])
        return carry

    lax.fori_loop(0, size_x, stress_plane, 0, unroll=6)

    for s in range(2):
        near, far, weight = x_faces[s][0:3], x_faces[s][3:6], 0.5 * x_faces[s][6]
        sign = -1.0 if s == 0 else 1.0
        normal = [(far[a] - padded[a, 1 if s == 0 else size_x]) * sign for a in range(3)]
        slope_y = difference_rows(near[0])
        slope_z = difference_z(near[0]) + x_others[s][0] * at_end
        at = 0 if s == 0 else size_x + 1
        stress_x[0, at] = weight * (2.0 * normal[0])
        stress_x[1, at] = weight * (normal[1] + slope_y)
        stress_x[2, at] = weight * (normal[2] + slope_z)
        for u in range(2):
            y, sign_y = (0, -1.0) if u == 0 else (size_y - 1, 1.0)
            number = 4 * s + 2 * u
            corner_ref[number : number + 1, :] = (0.5 * macro_step * sign * sign_y) * weight[y : y + 1, :]

    for u, ref in enumerate((y_low_ref, y_high_ref)):
        y, sign = (0, -1.0) if u == 0 else (size_y - 1, 1.0)
        weight = 0.5 * ref[6]
        normal = [
            (ref[3 + a] - velocity_ref[a, pl.ds(y, size_x, stride=size_y), :]) * sign for a in range(3)
        ]
        ghost_y[3 * u] = weight * (normal[0] + difference_rows(ref[1]))
        ghost_y[3 * u + 1] = weight * (2.0 * normal[1])
        ghost_y[3 * u + 2] = weight * (normal[2] + difference_z(ref[1]))
        for s in range(2):
            x, sign_x = (0, -1.0) if s == 0 else (size_x - 1, 1.0)
            number = 4 * s + 2 * u + 1
            corner_ref[number : number + 1, :] = (0.5 * macro_step * sign * sign_x) * weight[x : x + 1, :]
        wide = lanes_of((size_x, size_z))
        scale = jnp.where(wide == end, (0.5 * macro_step * sign) * sign_z, 0.0)
        edge_ref[2 * u] = scale * weight
        for x in range(size_x):
            edge_ref[2 * u + 1, x : x + 1, :] = scale[x : x + 1, :] * (0.5 * faces[3, x + 1, y : y + 1, :])

    columns = {(0, 1): (stress_x, 1, 1), (1, 1): (stress_rest, 0, 0), (2, 1): (stress_rest, 2, 0)}
    columns_z = {0: (stress_x, 2, 1), 1: (stress_rest, 2, 0), 2: (stress_rest, 1, 0)}

    def step_plane(x, carry):
        for a in range(3):
            total = stress_x[a, x + 2] - stress_x[a, x]
            ref, number, shift = columns[a, 1]
            total = total + difference_rows(
                ref[number, x + shift], ghost_y[a, pl.ds(x, 1), :], ghost_y[3 + a, pl.ds(x, 1), :]
            )
            ref, number, shift = columns_z[a]
            total = total + (difference_z(ref[number, x + shift]) + ghost_z[a, x])
            out_ref[a, plane(x), :] = padded[a, x + 1] + (0.5 * macro_step) * total
        return carry

    lax.fori_loop(0, size_x, step_plane, 0, unroll=6)


def flow_step(flag_cell, position, velocity, viscosity, chunks, y_low, y_high):
    size_x, size_y, size_z = viscosity.shape
    flags = flag_cell.shape[0]
    returned = chunks.shape[0] * back_rows
    row_count = size_x * size_y
    planes = (size_x, size_y, size_z)
    wide = (size_x + 2, size_y, size_z)
    return pl.pallas_call(
        functools.partial(flow_kernel, size_x, size_y, size_z, chunks.shape[0] // 2),
        out_shape=(
            jax.ShapeDtypeStruct((3, size_x * size_y, size_z), jnp.float32),
            jax.ShapeDtypeStruct((8, size_z), jnp.float32),
            jax.ShapeDtypeStruct((4, size_x, size_z), jnp.float32),
            jax.ShapeDtypeStruct((3, flags, size_z), jnp.float32),
            jax.ShapeDtypeStruct((flags, 4 * returned), jnp.bfloat16),
            jax.ShapeDtypeStruct((row_count, 3 * product_depth), jnp.bfloat16),
        ),
        in_specs=[SMEM] * 2 + [VMEM] * 5,
        out_specs=(VMEM,) * 6,
        scratch_shapes=[
            pltpu.VMEM((3, *wide), jnp.float32),
            pltpu.VMEM((3, *wide), jnp.float32),
            pltpu.VMEM((3, *planes), jnp.float32),
            pltpu.VMEM((item_count, *wide), jnp.float32),
            pltpu.VMEM((6, size_x, size_z), jnp.float32),
            pltpu.VMEM((3, *planes), jnp.float32),
            pltpu.VMEM((product_depth, -(-row_count // 128) * 128), jnp.float32),
        ],
        compiler_params=limit(12),
        cost_estimate=pl.CostEstimate(flops=4000000, bytes_accessed=3000000, transcendentals=0),
        name="flow_step",
    )(
        flag_cell, position,
        velocity.reshape(3, size_x * size_y, size_z),
        viscosity.reshape(size_x * size_y, size_z),
        chunks, y_low, y_high,
    )


def pieces(value):
    high = value.astype(jnp.bfloat16)
    rest = value - high.astype(jnp.float32)
    middle = rest.astype(jnp.bfloat16)
    return high, middle, (rest - middle.astype(jnp.float32)).astype(jnp.bfloat16)


def polymer_kernel(
    size_x, size_y, size_z, macro_count, chunk_ref, viscous_ref, corner_ref, edge_ref, lines_ref, pick_ref,
    spread_ref, partial_ref, out_ref, flag_ref, field, write_sem,
):
    flags = viscous_ref.shape[0]
    macro, core = place_of()
    chunks = chunk_ref[...]
    split = jnp.concatenate((*pieces(chunks), jnp.zeros(chunks.shape, jnp.bfloat16)), axis=0)
    values = jnp.dot(pick_ref[...], split, preferred_element_type=jnp.float32) * lines_ref[2]
    here, beside_z = lines_ref[0], lines_ref[1]
    lane = lanes_of((flags, 128))
    columns = [
        jnp.broadcast_to(
            jnp.sum(jnp.where((lane & 7) == k, values, 0.0), axis=1, keepdims=True), (flags, size_z)
        )
        for k in range(6)
    ]
    stress = viscous_ref[...]
    for k in range(6):
        stress = jnp.where(lane == k, stress + columns[k], stress)
    unused = jnp.zeros((product_depth - 3 * flags, size_z), jnp.float32)
    split = [
        pieces(
            jnp.concatenate(
                [
                    columns[pair_index(a, 0)] * here, columns[pair_index(a, 1)] * here,
                    columns[pair_index(a, 2)] * beside_z, unused,
                ],
                axis=0,
            )
        )
        for a in range(3)
    ]
    flag_ref[...] = stress.T[0:6, :]

    field[...] = partial_ref[...]
    for s in range(2):
        inside = macro > 0 if s == 0 else macro < macro_count - 1
        beside = jnp.maximum(macro - 1, 0) if s == 0 else jnp.minimum(macro + 1, macro_count - 1)
        start = (2 * beside + core) * back_rows
        x = 0 if s == 0 else size_x - 1
        for u in range(2):
            at = x * size_y + (0 if u == 0 else size_y - 1)
            for a in range(2):
                number = 4 * s + 2 * u + a
                line = corner_ref[number : number + 1, :] * chunk_ref[pl.ds(start + 2 * u + a, 1), :]
                field[1 - a, at : at + 1, :] += jnp.where(inside, line, 0.0)
    start = pl.multiple_of((2 * macro + 1 - core) * back_rows, 8)
    packed = chunk_ref[pl.ds(start, back_rows), :]
    end = jnp.where(core == 0, size_z - 1, 0)
    for u in range(2):
        y = 0 if u == 0 else size_y - 1
        for a in range(2):
            for i in range(size_x // 8):
                line = rolled(packed, end - (line_lane + 4 * i + 2 * u + a)) * edge_ref[2 * u + a, 8 * i : 8 * i + 8, :]
                at = pl.ds(8 * i * size_y + y, 8, stride=size_y)
                field[2 - a, at, :] += line
    copies = [pltpu.make_async_copy(field.at[a], out_ref.at[a], write_sem.at[a]) for a in range(3)]
    for a in range(3):
        field[a] += jnp.dot(
            spread_ref[...], jnp.concatenate(split[a], axis=0), preferred_element_type=jnp.float32
        )
        copies[a].start()
    for copy in copies:
        copy.wait()


def add_polymer(chunks, viscous, corners, edges, lines, pick, spread, partial, shape):
    flags = viscous.shape[0]
    size_x, size_y, size_z = shape
    return pl.pallas_call(
        functools.partial(polymer_kernel, size_x, size_y, size_z, chunks.shape[0] // 2),
        out_shape=(
            jax.ShapeDtypeStruct(partial.shape, jnp.float32),
            jax.ShapeDtypeStruct((6, flags), jnp.float32),
        ),
        in_specs=[VMEM] * 8,
        out_specs=(pl.BlockSpec(memory_space=pltpu.HBM), VMEM),
        scratch_shapes=[pltpu.VMEM(partial.shape, jnp.float32), pltpu.SemaphoreType.DMA((3,))],
        compiler_params=limit(8),
        cost_estimate=pl.CostEstimate(flops=400000, bytes_accessed=3000000, transcendentals=0),
        name="add_polymer",
    )(chunks.reshape(-1, 128), viscous, corners, edges, lines, pick, spread, partial)


def shards(velocity, viscosity, flag_cell, flag_owner, conformations, increments):
    macro_count = lax.axis_size("macro")
    tile_count = lax.axis_size("tile")
    assert lax.axis_size("micro") == 2
    owner_count = 2 * macro_count
    capacity = conformations.shape[1] // owner_count
    size_x, size_y, size_z = viscosity.shape
    assert capacity <= slot_rows and size_y == 8 and size_z == 128 and size_x % 8 == 0 and size_x <= 48
    chunks, position, viscous, y_first, y_last, first_conform, first_noise = gather_rows(
        flag_cell, flag_owner.reshape(-1), velocity, viscosity, conformations, increments, capacity, owner_count
    )

    def exchange(rows):
        return lax.all_to_all(rows, ("macro", "micro"), split_axis=0, concat_axis=0, tiled=True)

    received = exchange(chunks.reshape(owner_count, -1, 128))
    up = [(i, i + 1) for i in range(tile_count - 1)]
    down = [(target, source) for source, target in up]
    y_low = lax.ppermute(y_last, "tile", up)
    y_high = lax.ppermute(y_first, "tile", down)
    last_state, polymer = advance(
        conformations, increments, received, first_conform, first_noise, capacity
    )
    returned = exchange(add_lines(polymer, y_low, y_high))
    partial, corners, edges, lines, pick, spread = flow_step(
        flag_cell, position, velocity, viscosity, received, y_low, y_high
    )
    velocity_next, flag_stress = add_polymer(
        returned, viscous, corners, edges, lines, pick, spread, partial, viscosity.shape
    )
    return (velocity_next.reshape(velocity.shape), last_state, flag_stress)


def solution(mesh):
    in_specs = (
        P(None, "macro", "tile", "micro"),
        P("macro", "tile", "micro"),
        P(("macro", "tile", "micro")),
        P(("macro", "tile", "micro"), None),
        P(None, ("macro", "tile", "micro"), None),
        P(None, None, ("macro", "tile", "micro"), None),
    )
    out_specs = (
        P(None, "macro", "tile", "micro"),
        P(None, ("macro", "tile", "micro"), None),
        P(None, ("macro", "tile", "micro")),
    )
    return jax.shard_map(shards, mesh=mesh, in_specs=in_specs, out_specs=out_specs, check_vma=False)
```

```python
import functools

import jax
import jax.numpy as jnp
from jax import lax
from jax.experimental import pallas as pl
from jax.experimental.pallas import tpu as pltpu
from jax.sharding import PartitionSpec as P

stress_pairs = ((0, 0), (1, 1), (2, 2), (0, 1), (0, 2), (1, 2))
macro_step = 0.1
micro_step = 0.01
noise_weight = 0.1
relax_rate = 0.5
fene_extent = 30.0
spring_floor = 0.1
polymer_weight = 0.25

SMEM = pl.BlockSpec(memory_space=pltpu.SMEM)
VMEM = pl.BlockSpec(memory_space=pltpu.VMEM)


def pair_index(left_axis, right_axis):
    return stress_pairs.index((min(left_axis, right_axis), max(left_axis, right_axis)))


def lanes_of(shape):
    return lax.broadcasted_iota(jnp.int32, shape, len(shape) - 1)


slot_rows = 8
item_count = 7
back_rows = 8
polymer_row = 4
line_lane = 64


block_slots = 32
first_share = 2


def limit(mebibytes):
    return pltpu.CompilerParams(vmem_limit_bytes=mebibytes * 1024 * 1024)


def far(value):
    return pltpu.with_memory_space_constraint(value, pltpu.HBM)


def place_of():
    return lax.axis_index("macro"), lax.axis_index("micro")


def neighbour(index, side, count):
    return jnp.maximum(index - 1, 0) if side == 0 else jnp.minimum(index + 1, count - 1)


def rolled(value, amount):
    size = value.shape[-1]
    if isinstance(amount, int):
        return pltpu.roll(value, amount % size, value.ndim - 1)
    return pltpu.roll(value, lax.rem(amount + 2 * size, size), value.ndim - 1)


def gather_kernel(
    capacity, size_x, size_y, size_z, macro_count, cell_in, owner_in, velocity_in, viscosity_in,
    conform_in, noise_in, chunk_ref, position_ref, viscous_ref, first_ref, second_ref, conform_ref, noise_ref,
    cell_ref, owner_ref, velocity_ref, viscosity_ref, masked, gradients, target, count, sems,
):
    flags = cell_ref.shape[0]
    copies = [
        pltpu.make_async_copy(source, into, sems.at[number])
        for number, (source, into) in enumerate(
            (
                (cell_in, cell_ref), (owner_in, owner_ref), (velocity_in, velocity_ref),
                (viscosity_in, viscosity_ref), (conform_in.at[:, 0:block_slots, :], conform_ref),
                (noise_in.at[0 : noise_ref.shape[0], :, 0:block_slots, :], noise_ref),
            )
        )
    ]
    for copy in copies:
        copy.start()
    chunk_rows = slot_rows + item_count * size_y
    macro, core = place_of()
    lane = lanes_of((1, size_z))

    for owner in range(count.shape[0]):
        count[owner] = 0
        chunk_ref[owner * chunk_rows : owner * chunk_rows + slot_rows, :] = jnp.zeros((slot_rows, 128), jnp.float32)
    for copy in copies[:2]:
        copy.wait()
    for j in range(flags):
        owner = owner_ref[j]
        rank = count[owner]
        count[owner] = rank + 1
        target[j] = owner * chunk_rows + rank
        position_ref[j] = owner * slot_rows + rank
    for copy in copies[2:4]:
        copy.wait()
    planes = velocity_ref.reshape(3, size_x, size_y, size_z)
    layers = viscosity_ref.reshape(size_x, size_y, size_z)
    for j in range(flags):
        cell = cell_ref[j]
        x = lax.shift_right_logical(cell, 10)
        y = lax.shift_right_logical(cell, 7) & (size_y - 1)
        z = cell & (size_z - 1)
        here = (lane == z).astype(jnp.float32)
        along_z = (lane == z + 1).astype(jnp.float32) - (lane == z - 1).astype(jnp.float32)
        at = pl.ds(y, 1)
        for a in range(3):
            along_x = planes[a, x + 1, at, :] - planes[a, x - 1, at, :]
            along_y = planes[a, x, pl.ds(y + 1, 1), :] - planes[a, x, pl.ds(y - 1, 1), :]
            masked[3 * a, j : j + 1, :] = along_x * here
            masked[3 * a + 1, j : j + 1, :] = along_y * here
            masked[3 * a + 2, j : j + 1, :] = planes[a, x, at, :] * along_z
        masked[9, j : j + 1, :] = layers[x, at, :] * here

    even = lax.axis_index("tile") & 1 == 0

    def put(number, ref, low, high):
        rows = [ref[pl.ds(y, size_x, stride=size_y), :] for y in (low, high)]
        first_ref[number] = jnp.where(even, rows[1], rows[0])
        second_ref[number] = jnp.where(even, rows[0], rows[1])

    for layer in range(2):
        for a in range(3):
            put(3 * layer + a, velocity_ref.at[a], layer, size_y - 1 - layer)
    put(6, viscosity_ref, 0, size_y - 1)

    for side in range(2):
        beside = neighbour(macro, side, macro_count)
        first = pl.multiple_of((2 * beside + core) * chunk_rows + slot_rows, 8)
        other = pl.multiple_of((2 * beside + 1 - core) * chunk_rows + slot_rows, 8)
        for layer in range(2):
            x = layer if side == 0 else size_x - 1 - layer
            for a in range(3):
                chunk_ref[pl.ds(first + (3 * layer + a) * size_y, size_y), :] = velocity_ref[
                    a, x * size_y : (x + 1) * size_y, :
                ]
        x = 0 if side == 0 else size_x - 1
        chunk_ref[pl.ds(first + 6 * size_y, size_y), :] = viscosity_ref[x * size_y : (x + 1) * size_y, :]
        for number, a in enumerate((0, 2)):
            chunk_ref[pl.ds(other + number * size_y, size_y), :] = velocity_ref[
                a, x * size_y : (x + 1) * size_y, :
            ]

    group = size_z // 8
    lane2 = lanes_of((size_y, size_z))
    first = pl.multiple_of((2 * macro + 1 - core) * chunk_rows + slot_rows, 8)
    source = jnp.where(core == 0, size_z - 2, 0)
    for block in range(-(-size_x // group)):
        total = jnp.zeros((size_y, size_z), jnp.float32)
        for x in range(block * group, min(size_x, (block + 1) * group)):
            rows = slice(x * size_y, (x + 1) * size_y)
            for a in range(4):
                at = 8 * (x - block * group) + 2 * a
                value = viscosity_ref[rows, :] if a == 3 else velocity_ref[a, rows, :]
                total = jnp.where((lane2 == at) | (lane2 == at + 1), rolled(value, at - source), total)
        chunk_ref[pl.ds(first + block * size_y, size_y), :] = total

    columns = [0.5 * jnp.sum(masked[c], axis=1, keepdims=True) for c in range(9)]
    viscous = jnp.sum(masked[9], axis=1, keepdims=True)
    wide = lanes_of((flags, 128))
    packed = jnp.zeros((flags, 128), jnp.float32)
    for c in range(9):
        packed = jnp.where(wide == c, columns[c], packed)
    gradients[...] = packed
    stress = jnp.zeros((flags, 128), jnp.float32)
    for k, (a, b) in enumerate(stress_pairs):
        stress = jnp.where(wide == k, viscous * (columns[3 * a + b] + columns[3 * b + a]), stress)
    viscous_ref[...] = stress

    for j in range(flags):
        chunk_ref[pl.ds(target[j], 1), :] = gradients[j : j + 1, :]
    for copy in copies[4:]:
        copy.wait()


def gather_rows(flag_cell, owner, velocity, viscosity, conformations, increments, capacity, owner_count):
    size_x, size_y, size_z = viscosity.shape
    flags = flag_cell.shape[0]
    chunk_rows = slot_rows + item_count * size_y
    face = jax.ShapeDtypeStruct((item_count, size_x, size_z), jnp.float32)
    steps, _, _, dumbbells = increments.shape
    return pl.pallas_call(
        functools.partial(gather_kernel, capacity, size_x, size_y, size_z, owner_count // 2),
        out_shape=(
            jax.ShapeDtypeStruct((owner_count * chunk_rows, 128), jnp.float32),
            jax.ShapeDtypeStruct((flags,), jnp.int32),
            jax.ShapeDtypeStruct((flags, 128), jnp.float32),
            face,
            face,
            pltpu.VMEM((3, block_slots, dumbbells), jnp.float32),
            pltpu.VMEM((steps // first_share, 3, block_slots, dumbbells), jnp.bfloat16),
        ),
        in_specs=[pl.BlockSpec(memory_space=pltpu.HBM)] * 6,
        out_specs=(VMEM, SMEM, VMEM, VMEM, VMEM, VMEM, VMEM),
        scratch_shapes=[
            pltpu.SMEM((flags,), jnp.int32),
            pltpu.SMEM((flags,), jnp.int32),
            pltpu.VMEM((3, size_x * size_y, size_z), jnp.float32),
            pltpu.VMEM((size_x * size_y, size_z), jnp.float32),
            pltpu.VMEM((10, flags, size_z), jnp.float32),
            pltpu.VMEM((flags, 128), jnp.float32),
            pltpu.SMEM((flags,), jnp.int32),
            pltpu.SMEM((owner_count,), jnp.int32),
            pltpu.SemaphoreType.DMA((6,)),
        ],
        compiler_params=limit(8),
        cost_estimate=pl.CostEstimate(flops=400000, bytes_accessed=3000000, transcendentals=0),
        name="gather_rows",
    )(
        far(flag_cell),
        far(owner),
        far(velocity.reshape(3, size_x * size_y, size_z)),
        far(viscosity.reshape(size_x * size_y, size_z)),
        far(conformations),
        far(increments),
    )


def micro_kernel(
    capacity, parts, rows, groups, conform_ref, noise_ref, rate_ref, first_conform_ref, first_noise_ref,
    next_ref, chunk_ref, conform, noise, rate, rate_wide, sums_ref, read_sem, noise_sem,
):
    steps, _, slots, dumbbells = noise_ref.shape
    blocks = slots // rows
    span = steps // groups
    width = dumbbells // parts
    owners = slots // capacity
    scale = 1.0 / noise_weight
    extent = fene_extent * scale * scale

    def block_rows(block):
        return pl.ds(pl.multiple_of(block * rows, rows), rows)

    def read(block):
        at = block_rows(block)
        return pltpu.make_async_copy(conform_ref.at[:, at, :], conform.at[:, at, :], read_sem.at[block])

    def read_noise(block, group):
        at, when = block_rows(block), pl.ds(group * span, span)
        return pltpu.make_async_copy(
            noise_ref.at[when, :, at, :], noise.at[when, :, at, :], noise_sem.at[block, group]
        )

    pieces = [
        (half, slice(part * width, (part + 1) * width)) for half in range(rows // 16) for part in range(parts)
    ]
    assert len(pieces) == 8
    early = groups // first_share
    for block in range(blocks):
        if block > 0:
            read(block).start()
        for group in range(early if block == 0 else 0, groups):
            read_noise(block, group).start()
    conform[:, 0:rows, :] = first_conform_ref[...]
    for step in range(steps // first_share):
        noise[step, :, 0:rows, :] = first_noise_ref[step]
    for owner in range(owners):
        rate[owner * capacity : (owner + 1) * capacity, :] = rate_ref[owner, 0:capacity, :]
        chunk_ref[owner] = jnp.zeros(chunk_ref.shape[1:], jnp.float32)
    for a in range(3):
        for b in range(3):
            column = micro_step * rate[:, 3 * a + b : 3 * a + b + 1] + (1.0 if a == b else 0.0)
            rate_wide[3 * a + b] = jnp.broadcast_to(column, (slots, width))

    def inverses(state, scale):
        rooms = []
        for piece in range(len(pieces)):
            q = state[3 * piece : 3 * piece + 3]
            room = (extent - q[0] * q[0]) - (q[1] * q[1] + q[2] * q[2])
            rooms.append(jnp.maximum(room, extent * spring_floor))
        levels = [rooms]
        while len(levels[-1]) > 1:
            levels.append([low * high for low, high in zip(levels[-1][0::2], levels[-1][1::2])])
        result = [scale * pl.reciprocal(levels[-1][0])]
        for level in reversed(levels[:-1]):
            result = [result[i // 2] * level[i ^ 1] for i in range(len(level))]
        return result

    def advance_block(block, carry):
        ats = [pl.ds(pl.multiple_of(block * rows + 16 * half, 16), 16) for half in range(rows // 16)]
        rates = [
            [[rate_wide.at[3 * a + b, at, :] for b in range(3)] for a in range(3)] for at in ats
        ]

        def substep(step, state):
            updated = []
            springs = inverses(state, micro_step * relax_rate * extent)
            for piece, (half, lanes) in enumerate(pieces):
                q = state[3 * piece : 3 * piece + 3]
                table = rates[half]
                for a in range(3):
                    b, c = [other for other in range(3) if other != a]
                    kick = noise[step, a, ats[half], lanes].astype(jnp.float32)
                    rest = (table[a][b][...] * q[b] + table[a][c][...] * q[c]) + kick
                    updated.append((table[a][a][...] - springs[piece]) * q[a] + rest)
            return tuple(updated)

        def advance_group(group, state):
            if group < early:

                @pl.when(block > 0)
                def _():
                    read_noise(block, group).wait()

            else:
                read_noise(block, group).wait()
            for step in range(span):
                state = substep(group * span + step, state)
            return state

        @pl.when(block > 0)
        def _():
            read(block).wait()

        state = tuple(conform[a, ats[half], lanes] * scale for half, lanes in pieces for a in range(3))
        for group in range(groups):
            state = advance_group(group, state)
        inverse = inverses(state, 1.0)
        for half, at in enumerate(ats):
            sums = [None] * 6
            for piece, (other, lanes) in enumerate(pieces):
                if other != half:
                    continue
                q = state[3 * piece : 3 * piece + 3]
                for a in range(3):
                    next_ref[a, at, lanes] = q[a] * noise_weight
                for k, (a, b) in enumerate(stress_pairs):
                    term = (inverse[piece] * q[a]) * q[b]
                    sums[k] = term if sums[k] is None else sums[k] + term
            for k in range(6):
                sums_ref[k, at, :] = sums[k]
        return carry

    lax.fori_loop(0, blocks, advance_block, 0)
    lane = lanes_of((slots, 128))
    rank = lax.broadcasted_iota(jnp.int32, (slots, 128), 0) & (capacity - 1)
    packed = jnp.zeros((slots, 128), jnp.float32)
    weight = extent * noise_weight * noise_weight / dumbbells
    for k, (a, b) in enumerate(stress_pairs):
        mean = jnp.sum(sums_ref[k], axis=1, keepdims=True) * weight
        packed = jnp.where(lane == 8 * rank + k, polymer_weight * (mean - (1.0 if a == b else 0.0)), packed)
    for owner in range(owners):
        chunk_ref[owner, polymer_row : polymer_row + 1, :] = jnp.sum(
            packed[owner * capacity : (owner + 1) * capacity], axis=0, keepdims=True
        )


def advance(conformations, increments, chunks, first_conform, first_noise, capacity):
    slots, dumbbells = conformations.shape[1:]
    steps = increments.shape[0]
    owners = slots // capacity
    rows, parts, groups = block_slots, 4, 4
    blocks = slots // rows
    whole = pl.BlockSpec(memory_space=pltpu.HBM)
    return pl.pallas_call(
        functools.partial(micro_kernel, capacity, parts, rows, groups),
        out_shape=(
            pltpu.VMEM(conformations.shape, jnp.float32),
            jax.ShapeDtypeStruct((owners, back_rows, 128), jnp.float32),
        ),
        in_specs=[whole, whole, VMEM, VMEM, VMEM],
        out_specs=(VMEM, VMEM),
        scratch_shapes=[
            pltpu.VMEM(conformations.shape, jnp.float32),
            pltpu.VMEM(increments.shape, jnp.bfloat16),
            pltpu.VMEM((slots, 128), jnp.float32),
            pltpu.VMEM((9, slots, dumbbells // parts), jnp.float32),
            pltpu.VMEM((6, slots, dumbbells // parts), jnp.float32),
            pltpu.SemaphoreType.DMA((blocks,)),
            pltpu.SemaphoreType.DMA((blocks, groups)),
        ],
        compiler_params=limit(12),
        cost_estimate=pl.CostEstimate(flops=20000000, bytes_accessed=5000000, transcendentals=600000),
        name="advance",
    )(far(conformations), far(increments), chunks, first_conform, first_noise)


def lines_kernel(macro_count, chunk_ref, first_ref, second_ref, out_ref, y_low_ref, y_high_ref):
    out_ref[...] = chunk_ref[...]
    macro, core = place_of()
    even = lax.axis_index("tile") & 1 == 0
    y_low_ref[...] = jnp.where(even, second_ref[...], first_ref[...])
    y_high_ref[...] = jnp.where(even, first_ref[...], second_ref[...])
    sides = (y_low_ref, y_high_ref)
    size_x, size_z = y_low_ref.shape[1:]
    for side in range(2):
        beside = neighbour(macro, side, macro_count)
        x = 0 if side == 0 else size_x - 1
        for u in range(2):
            for a in range(2):
                at = 2 * u + a
                out_ref[2 * beside + core, at : at + 1, :] = sides[u][a, x : x + 1, :]

    lane = lanes_of((8, size_z))
    source = jnp.where(core == 0, size_z - 1, 0)
    other = 2 * macro + 1 - core
    total = chunk_ref[other]
    for i in range(size_x // 8):
        for u in range(2):
            for a in range(2):
                at = line_lane + 4 * i + 2 * u + a
                total = jnp.where(
                    lane == at, rolled(sides[u][1 + a, 8 * i : 8 * i + 8, :], at - source), total
                )
    out_ref[other] = total


def add_lines(chunks, first, second):
    face = jax.ShapeDtypeStruct(first.shape, jnp.float32)
    return pl.pallas_call(
        functools.partial(lines_kernel, chunks.shape[0] // 2),
        out_shape=(jax.ShapeDtypeStruct(chunks.shape, jnp.float32), face, face),
        in_specs=[VMEM, VMEM, VMEM],
        out_specs=(VMEM, VMEM, VMEM),
        compiler_params=limit(4),
        cost_estimate=pl.CostEstimate(flops=20000, bytes_accessed=400000, transcendentals=0),
        name="add_lines",
    )(chunks, first, second)


product_depth = 128


def one_hots(size_y, size_z, cell_ref, position_ref, lines_ref, pick_ref, spread_ref, rows):
    flags = cell_ref.shape[0]
    weight = 0.5 * macro_step
    row_count = spread_ref.shape[0]
    returned = pick_ref.shape[1] // 4
    lane = lanes_of((1, size_z))
    row_lane = lanes_of((1, rows.shape[1]))
    slot_lane = lanes_of((flags, returned))
    flag_row = lax.broadcasted_iota(jnp.int32, (flags, returned), 0)
    rows[3 * flags :, :] = jnp.zeros((product_depth - 3 * flags, rows.shape[1]), jnp.float32)
    slot = jnp.zeros((flags, returned), jnp.int32)
    group = lax.shift_right_logical(lane, 3)
    for j in range(flags):
        cell = cell_ref[j]
        row = lax.div(cell, size_z)
        z = cell - row * size_z
        lines_ref[0, j : j + 1, :] = jnp.where(lane == z, weight, 0.0)
        lines_ref[1, j : j + 1, :] = jnp.where(
            lane == z - 1, weight, jnp.where(lane == z + 1, -weight, 0.0)
        )
        for number, shift in enumerate((size_y, 1)):
            rows[number * flags + j : number * flags + j + 1, :] = jnp.where(
                row_lane == row - shift, 1.0, jnp.where(row_lane == row + shift, -1.0, 0.0)
            )
        rows[2 * flags + j : 2 * flags + j + 1, :] = jnp.where(row_lane == row, 1.0, 0.0)
        owner = lax.div(position_ref[j], slot_rows)
        rank = position_ref[j] - owner * slot_rows
        lines_ref[2, j : j + 1, :] = jnp.where(group == rank, 1.0, 0.0)
        slot = jnp.where(flag_row == j, owner * back_rows + polymer_row, slot)
    spread = rows[...].T[:row_count].astype(jnp.bfloat16)
    pick = jnp.where(slot_lane == slot, 1.0, 0.0).astype(jnp.bfloat16)
    for piece in range(3):
        spread_ref[:, piece * product_depth : (piece + 1) * product_depth] = spread
        pick_ref[:, piece * returned : (piece + 1) * returned] = pick
    pick_ref[:, 3 * returned :] = jnp.zeros((flags, returned), jnp.bfloat16)


def flow_kernel(
    size_x, size_y, size_z, macro_count, cell_ref, position_ref, velocity_ref, viscosity_ref, chunk_ref,
    y_low_ref, y_high_ref, out_ref, corner_ref, edge_ref, lines_ref, pick_ref, spread_ref,
    padded, stress_x, stress_rest, faces, ghost_y, ghost_z, rows,
):
    macro, core = place_of()
    one_hots(size_y, size_z, cell_ref, position_ref, lines_ref, pick_ref, spread_ref, rows)
    inside = (macro > 0, macro < macro_count - 1)
    sign_z = jnp.where(core == 0, 1.0, -1.0)
    end = jnp.where(core == 0, size_z - 1, 0)
    shape = (size_y, size_z)
    lane, row = lanes_of(shape), lax.broadcasted_iota(jnp.int32, shape, 0)
    at_end = jnp.where(lane == end, sign_z, 0.0)

    def kept(value, condition):
        return jnp.where(condition, value, 0.0)

    def plane(x):
        return pl.ds(pl.multiple_of(x * size_y, 8), size_y)

    def difference_z(value):
        lane = lanes_of(value.shape)
        return jnp.where(lane == size_z - 1, 0.0, rolled(value, -1)) - jnp.where(
            lane == 0, 0.0, rolled(value, 1)
        )

    def difference_rows(value, low=0.0, high=0.0):
        count = value.shape[0]
        row = lax.broadcasted_iota(jnp.int32, value.shape, 0)
        return jnp.where(row == count - 1, high, pltpu.roll(value, count - 1, 0)) - jnp.where(
            row == 0, low, pltpu.roll(value, 1, 0)
        )

    x_faces, x_others = [], []
    for s in range(2):
        beside = jnp.maximum(macro - 1, 0) if s == 0 else jnp.minimum(macro + 1, macro_count - 1)
        x_faces.append(
            [
                kept(chunk_ref[2 * beside + core, slot_rows + i * size_y : slot_rows + (i + 1) * size_y, :], inside[s])
                for i in range(item_count)
            ]
        )
        x_others.append(
            [
                kept(
                    rolled(
                        chunk_ref[
                            2 * beside + 1 - core, slot_rows + i * size_y : slot_rows + (i + 1) * size_y, :
                        ],
                        2 * end + 1,
                    ),
                    inside[s],
                )
                for i in range(2)
            ]
        )

    group = size_z // 8
    packed = [
        chunk_ref[2 * macro + 1 - core, slot_rows + i * size_y : slot_rows + (i + 1) * size_y, :]
        for i in range(-(-size_x // group))
    ]
    for i, value in enumerate(packed):

        def unpack(x, carry):
            for q in range(item_count):
                a, layer = (q, 0) if q < 4 else (q - 4, 1)
                at = 8 * (x - i * group) + 2 * a + (core if layer == 0 else 1 - core)
                faces[q, x + 1] = rolled(value, end - at)
            return carry

        lax.fori_loop(i * group, min(size_x, (i + 1) * group), unpack, 0, unroll=8)
    faces[2, 0] = x_others[0][1]
    faces[2, size_x + 1] = x_others[1][1]

    for a in range(3):
        padded[a, 0] = x_faces[0][a]
        padded[a, size_x + 1] = x_faces[1][a]

    def fill(x, carry):
        for a in range(3):
            padded[a, x + 1] = velocity_ref[a, plane(x), :]
        return carry

    lax.fori_loop(0, size_x, fill, 0, unroll=True)

    rest = {(1, 1): 0, (2, 2): 1, (1, 2): 2}

    def stress_plane(x, carry):
        along_x, along_y, along_z, centre = [], [], [], []
        for a in range(3):
            value = padded[a, x + 1]
            centre.append(value)
            along_x.append(padded[a, x + 2] - padded[a, x])
            along_y.append(
                difference_rows(value, y_low_ref[a, pl.ds(x, 1), :], y_high_ref[a, pl.ds(x, 1), :])
            )
            along_z.append(difference_z(value) + faces[a, x + 1] * at_end)
        slopes = (along_x, along_y, along_z)
        half = 0.5 * viscosity_ref[plane(x), :]
        for a, b in stress_pairs:
            value = half * (slopes[b][a] + slopes[a][b])
            if a == 0:
                stress_x[b, x + 1] = value
            else:
                stress_rest[rest[a, b], x] = value
        weight = (0.5 * faces[3, x + 1]) * at_end
        normal = [(faces[4 + a, x + 1] - centre[a]) * sign_z for a in range(3)]
        ghost_z[0, x] = weight * (normal[0] + (faces[2, x + 2] - faces[2, x]))
        ghost_z[1, x] = weight * (normal[1] + difference_rows(faces[2, x + 1]))
        ghost_z[2, x] = weight * (2.0 * normal[2])
        return carry

    lax.fori_loop(0, size_x, stress_plane, 0, unroll=6)

    for s in range(2):
        near, far, weight = x_faces[s][0:3], x_faces[s][3:6], 0.5 * x_faces[s][6]
        sign = -1.0 if s == 0 else 1.0
        normal = [(far[a] - padded[a, 1 if s == 0 else size_x]) * sign for a in range(3)]
        slope_y = difference_rows(near[0])
        slope_z = difference_z(near[0]) + x_others[s][0] * at_end
        at = 0 if s == 0 else size_x + 1
        stress_x[0, at] = weight * (2.0 * normal[0])
        stress_x[1, at] = weight * (normal[1] + slope_y)
        stress_x[2, at] = weight * (normal[2] + slope_z)
        for u in range(2):
            y, sign_y = (0, -1.0) if u == 0 else (size_y - 1, 1.0)
            number = 4 * s + 2 * u
            corner_ref[number : number + 1, :] = (0.5 * macro_step * sign * sign_y) * weight[y : y + 1, :]

    for u, ref in enumerate((y_low_ref, y_high_ref)):
        y, sign = (0, -1.0) if u == 0 else (size_y - 1, 1.0)
        weight = 0.5 * ref[6]
        normal = [
            (ref[3 + a] - velocity_ref[a, pl.ds(y, size_x, stride=size_y), :]) * sign for a in range(3)
        ]
        ghost_y[3 * u] = weight * (normal[0] + difference_rows(ref[1]))
        ghost_y[3 * u + 1] = weight * (2.0 * normal[1])
        ghost_y[3 * u + 2] = weight * (normal[2] + difference_z(ref[1]))
        for s in range(2):
            x, sign_x = (0, -1.0) if s == 0 else (size_x - 1, 1.0)
            number = 4 * s + 2 * u + 1
            corner_ref[number : number + 1, :] = (0.5 * macro_step * sign * sign_x) * weight[x : x + 1, :]
        wide = lanes_of((size_x, size_z))
        scale = jnp.where(wide == end, (0.5 * macro_step * sign) * sign_z, 0.0)
        edge_ref[2 * u] = scale * weight
        for x in range(size_x):
            edge_ref[2 * u + 1, x : x + 1, :] = scale[x : x + 1, :] * (0.5 * faces[3, x + 1, y : y + 1, :])

    columns = {(0, 1): (stress_x, 1, 1), (1, 1): (stress_rest, 0, 0), (2, 1): (stress_rest, 2, 0)}
    columns_z = {0: (stress_x, 2, 1), 1: (stress_rest, 2, 0), 2: (stress_rest, 1, 0)}

    def step_plane(x, carry):
        for a in range(3):
            total = stress_x[a, x + 2] - stress_x[a, x]
            ref, number, shift = columns[a, 1]
            total = total + difference_rows(
                ref[number, x + shift], ghost_y[a, pl.ds(x, 1), :], ghost_y[3 + a, pl.ds(x, 1), :]
            )
            ref, number, shift = columns_z[a]
            total = total + (difference_z(ref[number, x + shift]) + ghost_z[a, x])
            out_ref[a, plane(x), :] = padded[a, x + 1] + (0.5 * macro_step) * total
        return carry

    lax.fori_loop(0, size_x, step_plane, 0, unroll=6)


def flow_step(flag_cell, position, velocity, viscosity, chunks, y_low, y_high):
    size_x, size_y, size_z = viscosity.shape
    flags = flag_cell.shape[0]
    returned = chunks.shape[0] * back_rows
    row_count = size_x * size_y
    planes = (size_x, size_y, size_z)
    wide = (size_x + 2, size_y, size_z)
    return pl.pallas_call(
        functools.partial(flow_kernel, size_x, size_y, size_z, chunks.shape[0] // 2),
        out_shape=(
            jax.ShapeDtypeStruct((3, size_x * size_y, size_z), jnp.float32),
            jax.ShapeDtypeStruct((8, size_z), jnp.float32),
            jax.ShapeDtypeStruct((4, size_x, size_z), jnp.float32),
            jax.ShapeDtypeStruct((3, flags, size_z), jnp.float32),
            jax.ShapeDtypeStruct((flags, 4 * returned), jnp.bfloat16),
            jax.ShapeDtypeStruct((row_count, 3 * product_depth), jnp.bfloat16),
        ),
        in_specs=[SMEM] * 2 + [VMEM] * 5,
        out_specs=(VMEM,) * 6,
        scratch_shapes=[
            pltpu.VMEM((3, *wide), jnp.float32),
            pltpu.VMEM((3, *wide), jnp.float32),
            pltpu.VMEM((3, *planes), jnp.float32),
            pltpu.VMEM((item_count, *wide), jnp.float32),
            pltpu.VMEM((6, size_x, size_z), jnp.float32),
            pltpu.VMEM((3, *planes), jnp.float32),
            pltpu.VMEM((product_depth, -(-row_count // 128) * 128), jnp.float32),
        ],
        compiler_params=limit(12),
        cost_estimate=pl.CostEstimate(flops=4000000, bytes_accessed=3000000, transcendentals=0),
        name="flow_step",
    )(
        flag_cell, position,
        velocity.reshape(3, size_x * size_y, size_z),
        viscosity.reshape(size_x * size_y, size_z),
        chunks, y_low, y_high,
    )


def pieces(value):
    high = value.astype(jnp.bfloat16)
    rest = value - high.astype(jnp.float32)
    middle = rest.astype(jnp.bfloat16)
    return high, middle, (rest - middle.astype(jnp.float32)).astype(jnp.bfloat16)


def polymer_kernel(
    size_x, size_y, size_z, macro_count, chunk_ref, viscous_ref, corner_ref, edge_ref, lines_ref, pick_ref,
    spread_ref, partial_ref, out_ref, flag_ref, field, write_sem,
):
    flags = viscous_ref.shape[0]
    macro, core = place_of()
    chunks = chunk_ref[...]
    split = jnp.concatenate((*pieces(chunks), jnp.zeros(chunks.shape, jnp.bfloat16)), axis=0)
    values = jnp.dot(pick_ref[...], split, preferred_element_type=jnp.float32) * lines_ref[2]
    here, beside_z = lines_ref[0], lines_ref[1]
    lane = lanes_of((flags, 128))
    columns = [
        jnp.broadcast_to(
            jnp.sum(jnp.where((lane & 7) == k, values, 0.0), axis=1, keepdims=True), (flags, size_z)
        )
        for k in range(6)
    ]
    stress = viscous_ref[...]
    for k in range(6):
        stress = jnp.where(lane == k, stress + columns[k], stress)
    unused = jnp.zeros((product_depth - 3 * flags, size_z), jnp.float32)
    split = [
        pieces(
            jnp.concatenate(
                [
                    columns[pair_index(a, 0)] * here, columns[pair_index(a, 1)] * here,
                    columns[pair_index(a, 2)] * beside_z, unused,
                ],
                axis=0,
            )
        )
        for a in range(3)
    ]
    flag_ref[...] = stress.T[0:6, :]

    field[...] = partial_ref[...]
    for s in range(2):
        inside = macro > 0 if s == 0 else macro < macro_count - 1
        beside = jnp.maximum(macro - 1, 0) if s == 0 else jnp.minimum(macro + 1, macro_count - 1)
        start = (2 * beside + core) * back_rows
        x = 0 if s == 0 else size_x - 1
        for u in range(2):
            at = x * size_y + (0 if u == 0 else size_y - 1)
            for a in range(2):
                number = 4 * s + 2 * u + a
                line = corner_ref[number : number + 1, :] * chunk_ref[pl.ds(start + 2 * u + a, 1), :]
                field[1 - a, at : at + 1, :] += jnp.where(inside, line, 0.0)
    start = pl.multiple_of((2 * macro + 1 - core) * back_rows, 8)
    packed = chunk_ref[pl.ds(start, back_rows), :]
    end = jnp.where(core == 0, size_z - 1, 0)
    for u in range(2):
        y = 0 if u == 0 else size_y - 1
        for a in range(2):
            for i in range(size_x // 8):
                line = rolled(packed, end - (line_lane + 4 * i + 2 * u + a)) * edge_ref[2 * u + a, 8 * i : 8 * i + 8, :]
                at = pl.ds(8 * i * size_y + y, 8, stride=size_y)
                field[2 - a, at, :] += line
    copies = [pltpu.make_async_copy(field.at[a], out_ref.at[a], write_sem.at[a]) for a in range(3)]
    for a in range(3):
        field[a] += jnp.dot(
            spread_ref[...], jnp.concatenate(split[a], axis=0), preferred_element_type=jnp.float32
        )
        copies[a].start()
    for copy in copies:
        copy.wait()


def add_polymer(chunks, viscous, corners, edges, lines, pick, spread, partial, shape):
    flags = viscous.shape[0]
    size_x, size_y, size_z = shape
    return pl.pallas_call(
        functools.partial(polymer_kernel, size_x, size_y, size_z, chunks.shape[0] // 2),
        out_shape=(
            jax.ShapeDtypeStruct(partial.shape, jnp.float32),
            jax.ShapeDtypeStruct((6, flags), jnp.float32),
        ),
        in_specs=[VMEM] * 8,
        out_specs=(pl.BlockSpec(memory_space=pltpu.HBM), VMEM),
        scratch_shapes=[pltpu.VMEM(partial.shape, jnp.float32), pltpu.SemaphoreType.DMA((3,))],
        compiler_params=limit(8),
        cost_estimate=pl.CostEstimate(flops=400000, bytes_accessed=3000000, transcendentals=0),
        name="add_polymer",
    )(chunks.reshape(-1, 128), viscous, corners, edges, lines, pick, spread, partial)


def shards(velocity, viscosity, flag_cell, flag_owner, conformations, increments):
    macro_count = lax.axis_size("macro")
    tile_count = lax.axis_size("tile")
    assert lax.axis_size("micro") == 2
    owner_count = 2 * macro_count
    capacity = conformations.shape[1] // owner_count
    size_x, size_y, size_z = viscosity.shape
    assert capacity <= slot_rows and size_y == 8 and size_z == 128 and size_x % 8 == 0 and size_x <= 48
    chunks, position, viscous, first, second, first_conform, first_noise = gather_rows(
        flag_cell, flag_owner.reshape(-1), velocity, viscosity, conformations, increments, capacity, owner_count
    )

    def exchange(rows):
        return lax.all_to_all(rows, ("macro", "micro"), split_axis=0, concat_axis=0, tiled=True)

    received = exchange(chunks.reshape(owner_count, -1, 128))
    swaps = []
    for start in range(2):
        pairs = [(i, i + 1) for i in range(start, tile_count - 1, 2)]
        swaps.append(pairs + [(high, low) for low, high in pairs])
    first = lax.ppermute(first, "tile", swaps[0])
    second = lax.ppermute(second, "tile", swaps[1])
    last_state, polymer = advance(
        conformations, increments, received, first_conform, first_noise, capacity
    )
    polymer, y_low, y_high = add_lines(polymer, first, second)
    returned = exchange(polymer)
    partial, corners, edges, lines, pick, spread = flow_step(
        flag_cell, position, velocity, viscosity, received, y_low, y_high
    )
    velocity_next, flag_stress = add_polymer(
        returned, viscous, corners, edges, lines, pick, spread, partial, viscosity.shape
    )
    return (velocity_next.reshape(velocity.shape), last_state, flag_stress)


def solution(mesh):
    in_specs = (
        P(None, "macro", "tile", "micro"),
        P("macro", "tile", "micro"),
        P(("macro", "tile", "micro")),
        P(("macro", "tile", "micro"), None),
        P(None, ("macro", "tile", "micro"), None),
        P(None, None, ("macro", "tile", "micro"), None),
    )
    out_specs = (
        P(None, "macro", "tile", "micro"),
        P(None, ("macro", "tile", "micro"), None),
        P(None, ("macro", "tile", "micro")),
    )
    return jax.shard_map(shards, mesh=mesh, in_specs=in_specs, out_specs=out_specs, check_vma=False)
```

```python
import functools

import jax
import jax.numpy as jnp
from jax import lax
from jax.experimental import pallas as pl
from jax.experimental.pallas import tpu as pltpu
from jax.sharding import PartitionSpec as P

stress_pairs = ((0, 0), (1, 1), (2, 2), (0, 1), (0, 2), (1, 2))
macro_step = 0.1
micro_step = 0.01
noise_weight = 0.1
relax_rate = 0.5
fene_extent = 30.0
spring_floor = 0.1
polymer_weight = 0.25

SMEM = pl.BlockSpec(memory_space=pltpu.SMEM)
VMEM = pl.BlockSpec(memory_space=pltpu.VMEM)


def pair_index(left_axis, right_axis):
    return stress_pairs.index((min(left_axis, right_axis), max(left_axis, right_axis)))


def lanes_of(shape):
    return lax.broadcasted_iota(jnp.int32, shape, len(shape) - 1)


slot_rows = 8
face_rows = 16
corner_lane = 64
item_count = 7
back_rows = 8
polymer_row = 4
line_lane = 64


block_slots = 32
first_share = 2


def limit(mebibytes):
    return pltpu.CompilerParams(vmem_limit_bytes=mebibytes * 1024 * 1024)


def far(value):
    return pltpu.with_memory_space_constraint(value, pltpu.HBM)


def place_of():
    return lax.axis_index("macro"), lax.axis_index("micro")


def neighbour(index, side, count):
    return jnp.maximum(index - 1, 0) if side == 0 else jnp.minimum(index + 1, count - 1)


def rolled(value, amount):
    size = value.shape[-1]
    if isinstance(amount, int):
        return pltpu.roll(value, amount % size, value.ndim - 1)
    return pltpu.roll(value, lax.rem(amount + 2 * size, size), value.ndim - 1)


def gather_kernel(
    capacity, size_x, size_y, size_z, macro_count, cell_in, owner_in, velocity_in, viscosity_in,
    conform_in, noise_in, chunk_ref, position_ref, viscous_ref, first_ref, second_ref, first_x_ref, second_x_ref, conform_ref, noise_ref,
    cell_ref, owner_ref, velocity_ref, viscosity_ref, masked, gradients, target, count, sems,
):
    flags = cell_ref.shape[0]
    copies = [
        pltpu.make_async_copy(source, into, sems.at[number])
        for number, (source, into) in enumerate(
            (
                (cell_in, cell_ref), (owner_in, owner_ref), (velocity_in, velocity_ref),
                (viscosity_in, viscosity_ref), (conform_in.at[:, 0:block_slots, :], conform_ref),
                (noise_in.at[0 : noise_ref.shape[0], :, 0:block_slots, :], noise_ref),
            )
        )
    ]
    for copy in copies:
        copy.start()
    chunk_rows = slot_rows + face_rows
    macro, core = place_of()
    lane = lanes_of((1, size_z))

    for owner in range(count.shape[0]):
        count[owner] = 0
        chunk_ref[owner * chunk_rows : owner * chunk_rows + slot_rows, :] = jnp.zeros((slot_rows, 128), jnp.float32)
    for copy in copies[:2]:
        copy.wait()
    for j in range(flags):
        owner = owner_ref[j]
        rank = count[owner]
        count[owner] = rank + 1
        target[j] = owner * chunk_rows + rank
        position_ref[j] = owner * slot_rows + rank
    for copy in copies[2:4]:
        copy.wait()
    planes = velocity_ref.reshape(3, size_x, size_y, size_z)
    layers = viscosity_ref.reshape(size_x, size_y, size_z)
    for j in range(flags):
        cell = cell_ref[j]
        x = lax.shift_right_logical(cell, 10)
        y = lax.shift_right_logical(cell, 7) & (size_y - 1)
        z = cell & (size_z - 1)
        here = (lane == z).astype(jnp.float32)
        along_z = (lane == z + 1).astype(jnp.float32) - (lane == z - 1).astype(jnp.float32)
        at = pl.ds(y, 1)
        for a in range(3):
            along_x = planes[a, x + 1, at, :] - planes[a, x - 1, at, :]
            along_y = planes[a, x, pl.ds(y + 1, 1), :] - planes[a, x, pl.ds(y - 1, 1), :]
            masked[3 * a, j : j + 1, :] = along_x * here
            masked[3 * a + 1, j : j + 1, :] = along_y * here
            masked[3 * a + 2, j : j + 1, :] = planes[a, x, at, :] * along_z
        masked[9, j : j + 1, :] = layers[x, at, :] * here

    even = lax.axis_index("tile") & 1 == 0

    def put(number, ref, low, high):
        rows = [ref[pl.ds(y, size_x, stride=size_y), :] for y in (low, high)]
        first_ref[number] = jnp.where(even, rows[1], rows[0])
        second_ref[number] = jnp.where(even, rows[0], rows[1])

    for layer in range(2):
        for a in range(3):
            put(3 * layer + a, velocity_ref.at[a], layer, size_y - 1 - layer)
    put(6, viscosity_ref, 0, size_y - 1)

    even_x = macro & 1 == 0

    def put_x(number, ref, low, high):
        planes = [ref[x * size_y : (x + 1) * size_y, :] for x in (low, high)]
        first_x_ref[number] = jnp.where(even_x, planes[1], planes[0])
        second_x_ref[number] = jnp.where(even_x, planes[0], planes[1])

    for layer in range(2):
        for a in range(3):
            put_x(3 * layer + a, velocity_ref.at[a], layer, size_x - 1 - layer)
    put_x(6, viscosity_ref, 0, size_x - 1)

    group = size_z // 8
    lane2 = lanes_of((size_y, size_z))
    first = pl.multiple_of((2 * macro + 1 - core) * chunk_rows + slot_rows, 8)
    source = jnp.where(core == 0, size_z - 2, 0)
    for block in range(-(-size_x // group)):
        total = jnp.zeros((size_y, size_z), jnp.float32)
        for x in range(block * group, min(size_x, (block + 1) * group)):
            rows = slice(x * size_y, (x + 1) * size_y)
            for a in range(4):
                at = 8 * (x - block * group) + 2 * a
                value = viscosity_ref[rows, :] if a == 3 else velocity_ref[a, rows, :]
                total = jnp.where((lane2 == at) | (lane2 == at + 1), rolled(value, at - source), total)
        chunk_ref[pl.ds(first + block * size_y, size_y), :] = total

    columns = [0.5 * jnp.sum(masked[c], axis=1, keepdims=True) for c in range(9)]
    viscous = jnp.sum(masked[9], axis=1, keepdims=True)
    wide = lanes_of((flags, 128))
    packed = jnp.zeros((flags, 128), jnp.float32)
    for c in range(9):
        packed = jnp.where(wide == c, columns[c], packed)
    gradients[...] = packed
    stress = jnp.zeros((flags, 128), jnp.float32)
    for k, (a, b) in enumerate(stress_pairs):
        stress = jnp.where(wide == k, viscous * (columns[3 * a + b] + columns[3 * b + a]), stress)
    viscous_ref[...] = stress

    for j in range(flags):
        chunk_ref[pl.ds(target[j], 1), :] = gradients[j : j + 1, :]

    edge = jnp.where(core == 0, size_z - 1, 0)
    for side in range(2):
        beside = neighbour(macro, side, macro_count)
        rows = pl.ds(pl.multiple_of((2 * beside + 1 - core) * chunk_rows, 8), slot_rows)
        x = 0 if side == 0 else size_x - 1
        value = chunk_ref[rows, :]
        for number, a in enumerate((0, 2)):
            plane = velocity_ref[a, x * size_y : (x + 1) * size_y, :]
            at = corner_lane + number
            value = jnp.where(lane2 == at, rolled(plane, at - edge), value)
        chunk_ref[rows, :] = value
    for copy in copies[4:]:
        copy.wait()


def gather_rows(flag_cell, owner, velocity, viscosity, conformations, increments, capacity, owner_count):
    size_x, size_y, size_z = viscosity.shape
    flags = flag_cell.shape[0]
    chunk_rows = slot_rows + face_rows
    face = jax.ShapeDtypeStruct((item_count, size_x, size_z), jnp.float32)
    face_x = jax.ShapeDtypeStruct((item_count, size_y, size_z), jnp.float32)
    steps, _, _, dumbbells = increments.shape
    return pl.pallas_call(
        functools.partial(gather_kernel, capacity, size_x, size_y, size_z, owner_count // 2),
        out_shape=(
            jax.ShapeDtypeStruct((owner_count * chunk_rows, 128), jnp.float32),
            jax.ShapeDtypeStruct((flags,), jnp.int32),
            jax.ShapeDtypeStruct((flags, 128), jnp.float32),
            face,
            face,
            face_x,
            face_x,
            pltpu.VMEM((3, block_slots, dumbbells), jnp.float32),
            pltpu.VMEM((steps // first_share, 3, block_slots, dumbbells), jnp.bfloat16),
        ),
        in_specs=[pl.BlockSpec(memory_space=pltpu.HBM)] * 6,
        out_specs=(VMEM, SMEM) + (VMEM,) * 7,
        scratch_shapes=[
            pltpu.SMEM((flags,), jnp.int32),
            pltpu.SMEM((flags,), jnp.int32),
            pltpu.VMEM((3, size_x * size_y, size_z), jnp.float32),
            pltpu.VMEM((size_x * size_y, size_z), jnp.float32),
            pltpu.VMEM((10, flags, size_z), jnp.float32),
            pltpu.VMEM((flags, 128), jnp.float32),
            pltpu.SMEM((flags,), jnp.int32),
            pltpu.SMEM((owner_count,), jnp.int32),
            pltpu.SemaphoreType.DMA((6,)),
        ],
        compiler_params=limit(8),
        cost_estimate=pl.CostEstimate(flops=400000, bytes_accessed=3000000, transcendentals=0),
        name="gather_rows",
    )(
        far(flag_cell),
        far(owner),
        far(velocity.reshape(3, size_x * size_y, size_z)),
        far(viscosity.reshape(size_x * size_y, size_z)),
        far(conformations),
        far(increments),
    )


def micro_kernel(
    capacity, parts, rows, groups, conform_ref, noise_ref, rate_ref, first_conform_ref, first_noise_ref,
    next_ref, chunk_ref, conform, noise, rate, rate_wide, sums_ref, read_sem, noise_sem,
):
    steps, _, slots, dumbbells = noise_ref.shape
    blocks = slots // rows
    span = steps // groups
    width = dumbbells // parts
    owners = slots // capacity
    scale = 1.0 / noise_weight
    extent = fene_extent * scale * scale

    def block_rows(block):
        return pl.ds(pl.multiple_of(block * rows, rows), rows)

    def read(block):
        at = block_rows(block)
        return pltpu.make_async_copy(conform_ref.at[:, at, :], conform.at[:, at, :], read_sem.at[block])

    def read_noise(block, group):
        at, when = block_rows(block), pl.ds(group * span, span)
        return pltpu.make_async_copy(
            noise_ref.at[when, :, at, :], noise.at[when, :, at, :], noise_sem.at[block, group]
        )

    pieces = [
        (half, slice(part * width, (part + 1) * width)) for half in range(rows // 16) for part in range(parts)
    ]
    assert len(pieces) == 8
    early = groups // first_share
    for block in range(blocks):
        if block > 0:
            read(block).start()
        for group in range(early if block == 0 else 0, groups):
            read_noise(block, group).start()
    conform[:, 0:rows, :] = first_conform_ref[...]
    for step in range(steps // first_share):
        noise[step, :, 0:rows, :] = first_noise_ref[step]
    for owner in range(owners):
        rate[owner * capacity : (owner + 1) * capacity, :] = rate_ref[owner, 0:capacity, :]
        chunk_ref[owner] = jnp.zeros(chunk_ref.shape[1:], jnp.float32)
    for a in range(3):
        for b in range(3):
            column = micro_step * rate[:, 3 * a + b : 3 * a + b + 1] + (1.0 if a == b else 0.0)
            rate_wide[3 * a + b] = jnp.broadcast_to(column, (slots, width))

    def inverses(state, scale):
        rooms = []
        for piece in range(len(pieces)):
            q = state[3 * piece : 3 * piece + 3]
            room = (extent - q[0] * q[0]) - (q[1] * q[1] + q[2] * q[2])
            rooms.append(jnp.maximum(room, extent * spring_floor))
        levels = [rooms]
        while len(levels[-1]) > 1:
            levels.append([low * high for low, high in zip(levels[-1][0::2], levels[-1][1::2])])
        result = [scale * pl.reciprocal(levels[-1][0])]
        for level in reversed(levels[:-1]):
            result = [result[i // 2] * level[i ^ 1] for i in range(len(level))]
        return result

    def advance_block(block, carry):
        ats = [pl.ds(pl.multiple_of(block * rows + 16 * half, 16), 16) for half in range(rows // 16)]
        rates = [
            [[rate_wide.at[3 * a + b, at, :] for b in range(3)] for a in range(3)] for at in ats
        ]

        def substep(step, state):
            updated = []
            springs = inverses(state, micro_step * relax_rate * extent)
            for piece, (half, lanes) in enumerate(pieces):
                q = state[3 * piece : 3 * piece + 3]
                table = rates[half]
                for a in range(3):
                    b, c = [other for other in range(3) if other != a]
                    kick = noise[step, a, ats[half], lanes].astype(jnp.float32)
                    rest = (table[a][b][...] * q[b] + table[a][c][...] * q[c]) + kick
                    updated.append((table[a][a][...] - springs[piece]) * q[a] + rest)
            return tuple(updated)

        def advance_group(group, state):
            if group < early:

                @pl.when(block > 0)
                def _():
                    read_noise(block, group).wait()

            else:
                read_noise(block, group).wait()
            for step in range(span):
                state = substep(group * span + step, state)
            return state

        @pl.when(block > 0)
        def _():
            read(block).wait()

        state = tuple(conform[a, ats[half], lanes] * scale for half, lanes in pieces for a in range(3))
        for group in range(groups):
            state = advance_group(group, state)
        inverse = inverses(state, 1.0)
        for half, at in enumerate(ats):
            sums = [None] * 6
            for piece, (other, lanes) in enumerate(pieces):
                if other != half:
                    continue
                q = state[3 * piece : 3 * piece + 3]
                for a in range(3):
                    next_ref[a, at, lanes] = q[a] * noise_weight
                for k, (a, b) in enumerate(stress_pairs):
                    term = (inverse[piece] * q[a]) * q[b]
                    sums[k] = term if sums[k] is None else sums[k] + term
            for k in range(6):
                sums_ref[k, at, :] = sums[k]
        return carry

    lax.fori_loop(0, blocks, advance_block, 0)
    lane = lanes_of((slots, 128))
    rank = lax.broadcasted_iota(jnp.int32, (slots, 128), 0) & (capacity - 1)
    packed = jnp.zeros((slots, 128), jnp.float32)
    weight = extent * noise_weight * noise_weight / dumbbells
    for k, (a, b) in enumerate(stress_pairs):
        mean = jnp.sum(sums_ref[k], axis=1, keepdims=True) * weight
        packed = jnp.where(lane == 8 * rank + k, polymer_weight * (mean - (1.0 if a == b else 0.0)), packed)
    for owner in range(owners):
        chunk_ref[owner, polymer_row : polymer_row + 1, :] = jnp.sum(
            packed[owner * capacity : (owner + 1) * capacity], axis=0, keepdims=True
        )


def advance(conformations, increments, chunks, first_conform, first_noise, capacity):
    slots, dumbbells = conformations.shape[1:]
    steps = increments.shape[0]
    owners = slots // capacity
    rows, parts, groups = block_slots, 4, 4
    blocks = slots // rows
    whole = pl.BlockSpec(memory_space=pltpu.HBM)
    return pl.pallas_call(
        functools.partial(micro_kernel, capacity, parts, rows, groups),
        out_shape=(
            pltpu.VMEM(conformations.shape, jnp.float32),
            jax.ShapeDtypeStruct((owners, back_rows, 128), jnp.float32),
        ),
        in_specs=[whole, whole, VMEM, VMEM, VMEM],
        out_specs=(VMEM, VMEM),
        scratch_shapes=[
            pltpu.VMEM(conformations.shape, jnp.float32),
            pltpu.VMEM(increments.shape, jnp.bfloat16),
            pltpu.VMEM((slots, 128), jnp.float32),
            pltpu.VMEM((9, slots, dumbbells // parts), jnp.float32),
            pltpu.VMEM((6, slots, dumbbells // parts), jnp.float32),
            pltpu.SemaphoreType.DMA((blocks,)),
            pltpu.SemaphoreType.DMA((blocks, groups)),
        ],
        compiler_params=limit(12),
        cost_estimate=pl.CostEstimate(flops=20000000, bytes_accessed=5000000, transcendentals=600000),
        name="advance",
    )(far(conformations), far(increments), chunks, first_conform, first_noise)


def lines_kernel(macro_count, chunk_ref, first_ref, second_ref, out_ref, y_low_ref, y_high_ref):
    out_ref[...] = chunk_ref[...]
    macro, core = place_of()
    even = lax.axis_index("tile") & 1 == 0
    y_low_ref[...] = jnp.where(even, second_ref[...], first_ref[...])
    y_high_ref[...] = jnp.where(even, first_ref[...], second_ref[...])
    sides = (y_low_ref, y_high_ref)
    size_x, size_z = y_low_ref.shape[1:]
    for side in range(2):
        beside = neighbour(macro, side, macro_count)
        x = 0 if side == 0 else size_x - 1
        for u in range(2):
            for a in range(2):
                at = 2 * u + a
                out_ref[2 * beside + core, at : at + 1, :] = sides[u][a, x : x + 1, :]

    lane = lanes_of((8, size_z))
    source = jnp.where(core == 0, size_z - 1, 0)
    other = 2 * macro + 1 - core
    total = chunk_ref[other]
    for i in range(size_x // 8):
        for u in range(2):
            for a in range(2):
                at = line_lane + 4 * i + 2 * u + a
                total = jnp.where(
                    lane == at, rolled(sides[u][1 + a, 8 * i : 8 * i + 8, :], at - source), total
                )
    out_ref[other] = total


def add_lines(chunks, first, second):
    face = jax.ShapeDtypeStruct(first.shape, jnp.float32)
    return pl.pallas_call(
        functools.partial(lines_kernel, chunks.shape[0] // 2),
        out_shape=(jax.ShapeDtypeStruct(chunks.shape, jnp.float32), face, face),
        in_specs=[VMEM, VMEM, VMEM],
        out_specs=(VMEM, VMEM, VMEM),
        compiler_params=limit(4),
        cost_estimate=pl.CostEstimate(flops=20000, bytes_accessed=400000, transcendentals=0),
        name="add_lines",
    )(chunks, first, second)


product_depth = 128


def one_hots(size_y, size_z, cell_ref, position_ref, lines_ref, pick_ref, spread_ref, rows):
    flags = cell_ref.shape[0]
    weight = 0.5 * macro_step
    row_count = spread_ref.shape[0]
    returned = pick_ref.shape[1] // 4
    lane = lanes_of((1, size_z))
    row_lane = lanes_of((1, rows.shape[1]))
    slot_lane = lanes_of((flags, returned))
    flag_row = lax.broadcasted_iota(jnp.int32, (flags, returned), 0)
    rows[3 * flags :, :] = jnp.zeros((product_depth - 3 * flags, rows.shape[1]), jnp.float32)
    slot = jnp.zeros((flags, returned), jnp.int32)
    group = lax.shift_right_logical(lane, 3)
    for j in range(flags):
        cell = cell_ref[j]
        row = lax.div(cell, size_z)
        z = cell - row * size_z
        lines_ref[0, j : j + 1, :] = jnp.where(lane == z, weight, 0.0)
        lines_ref[1, j : j + 1, :] = jnp.where(
            lane == z - 1, weight, jnp.where(lane == z + 1, -weight, 0.0)
        )
        for number, shift in enumerate((size_y, 1)):
            rows[number * flags + j : number * flags + j + 1, :] = jnp.where(
                row_lane == row - shift, 1.0, jnp.where(row_lane == row + shift, -1.0, 0.0)
            )
        rows[2 * flags + j : 2 * flags + j + 1, :] = jnp.where(row_lane == row, 1.0, 0.0)
        owner = lax.div(position_ref[j], slot_rows)
        rank = position_ref[j] - owner * slot_rows
        lines_ref[2, j : j + 1, :] = jnp.where(group == rank, 1.0, 0.0)
        slot = jnp.where(flag_row == j, owner * back_rows + polymer_row, slot)
    spread = rows[...].T[:row_count].astype(jnp.bfloat16)
    pick = jnp.where(slot_lane == slot, 1.0, 0.0).astype(jnp.bfloat16)
    for piece in range(3):
        spread_ref[:, piece * product_depth : (piece + 1) * product_depth] = spread
        pick_ref[:, piece * returned : (piece + 1) * returned] = pick
    pick_ref[:, 3 * returned :] = jnp.zeros((flags, returned), jnp.bfloat16)


def flow_kernel(
    size_x, size_y, size_z, macro_count, cell_ref, position_ref, velocity_ref, viscosity_ref, chunk_ref,
    y_low_ref, y_high_ref, first_x_ref, second_x_ref, out_ref, corner_ref, edge_ref, lines_ref, pick_ref, spread_ref,
    padded, stress_x, stress_rest, faces, ghost_y, ghost_z, rows,
):
    macro, core = place_of()
    one_hots(size_y, size_z, cell_ref, position_ref, lines_ref, pick_ref, spread_ref, rows)
    inside = (macro > 0, macro < macro_count - 1)
    sign_z = jnp.where(core == 0, 1.0, -1.0)
    end = jnp.where(core == 0, size_z - 1, 0)
    shape = (size_y, size_z)
    lane, row = lanes_of(shape), lax.broadcasted_iota(jnp.int32, shape, 0)
    at_end = jnp.where(lane == end, sign_z, 0.0)

    def kept(value, condition):
        return jnp.where(condition, value, 0.0)

    def plane(x):
        return pl.ds(pl.multiple_of(x * size_y, 8), size_y)

    def difference_z(value):
        lane = lanes_of(value.shape)
        return jnp.where(lane == size_z - 1, 0.0, rolled(value, -1)) - jnp.where(
            lane == 0, 0.0, rolled(value, 1)
        )

    def difference_rows(value, low=0.0, high=0.0):
        count = value.shape[0]
        row = lax.broadcasted_iota(jnp.int32, value.shape, 0)
        return jnp.where(row == count - 1, high, pltpu.roll(value, count - 1, 0)) - jnp.where(
            row == 0, low, pltpu.roll(value, 1, 0)
        )

    even = macro & 1 == 0
    x_faces, x_others = [[], []], []
    for i in range(item_count):
        first, second = first_x_ref[i], second_x_ref[i]
        x_faces[0].append(jnp.where(even, second, first))
        x_faces[1].append(jnp.where(even, first, second))
    for s in range(2):
        beside = neighbour(macro, s, macro_count)
        corner = chunk_ref[2 * beside + 1 - core, 0:slot_rows, :]
        x_others.append([kept(rolled(corner, end - (corner_lane + i)), inside[s]) for i in range(2)])

    group = size_z // 8
    packed = [
        chunk_ref[2 * macro + 1 - core, slot_rows + i * size_y : slot_rows + (i + 1) * size_y, :]
        for i in range(-(-size_x // group))
    ]
    for i, value in enumerate(packed):

        def unpack(x, carry):
            for q in range(item_count):
                a, layer = (q, 0) if q < 4 else (q - 4, 1)
                at = 8 * (x - i * group) + 2 * a + (core if layer == 0 else 1 - core)
                faces[q, x + 1] = rolled(value, end - at)
            return carry

        lax.fori_loop(i * group, min(size_x, (i + 1) * group), unpack, 0, unroll=8)
    faces[2, 0] = x_others[0][1]
    faces[2, size_x + 1] = x_others[1][1]

    for a in range(3):
        padded[a, 0] = x_faces[0][a]
        padded[a, size_x + 1] = x_faces[1][a]

    def fill(x, carry):
        for a in range(3):
            padded[a, x + 1] = velocity_ref[a, plane(x), :]
        return carry

    lax.fori_loop(0, size_x, fill, 0, unroll=True)

    rest = {(1, 1): 0, (2, 2): 1, (1, 2): 2}

    def stress_plane(x, carry):
        along_x, along_y, along_z, centre = [], [], [], []
        for a in range(3):
            value = padded[a, x + 1]
            centre.append(value)
            along_x.append(padded[a, x + 2] - padded[a, x])
            along_y.append(
                difference_rows(value, y_low_ref[a, pl.ds(x, 1), :], y_high_ref[a, pl.ds(x, 1), :])
            )
            along_z.append(difference_z(value) + faces[a, x + 1] * at_end)
        slopes = (along_x, along_y, along_z)
        half = 0.5 * viscosity_ref[plane(x), :]
        for a, b in stress_pairs:
            value = half * (slopes[b][a] + slopes[a][b])
            if a == 0:
                stress_x[b, x + 1] = value
            else:
                stress_rest[rest[a, b], x] = value
        weight = (0.5 * faces[3, x + 1]) * at_end
        normal = [(faces[4 + a, x + 1] - centre[a]) * sign_z for a in range(3)]
        ghost_z[0, x] = weight * (normal[0] + (faces[2, x + 2] - faces[2, x]))
        ghost_z[1, x] = weight * (normal[1] + difference_rows(faces[2, x + 1]))
        ghost_z[2, x] = weight * (2.0 * normal[2])
        return carry

    lax.fori_loop(0, size_x, stress_plane, 0, unroll=6)

    for s in range(2):
        near, far, weight = x_faces[s][0:3], x_faces[s][3:6], 0.5 * x_faces[s][6]
        sign = -1.0 if s == 0 else 1.0
        normal = [(far[a] - padded[a, 1 if s == 0 else size_x]) * sign for a in range(3)]
        slope_y = difference_rows(near[0])
        slope_z = difference_z(near[0]) + x_others[s][0] * at_end
        at = 0 if s == 0 else size_x + 1
        stress_x[0, at] = weight * (2.0 * normal[0])
        stress_x[1, at] = weight * (normal[1] + slope_y)
        stress_x[2, at] = weight * (normal[2] + slope_z)
        for u in range(2):
            y, sign_y = (0, -1.0) if u == 0 else (size_y - 1, 1.0)
            number = 4 * s + 2 * u
            corner_ref[number : number + 1, :] = (0.5 * macro_step * sign * sign_y) * weight[y : y + 1, :]

    for u, ref in enumerate((y_low_ref, y_high_ref)):
        y, sign = (0, -1.0) if u == 0 else (size_y - 1, 1.0)
        weight = 0.5 * ref[6]
        normal = [
            (ref[3 + a] - velocity_ref[a, pl.ds(y, size_x, stride=size_y), :]) * sign for a in range(3)
        ]
        ghost_y[3 * u] = weight * (normal[0] + difference_rows(ref[1]))
        ghost_y[3 * u + 1] = weight * (2.0 * normal[1])
        ghost_y[3 * u + 2] = weight * (normal[2] + difference_z(ref[1]))
        for s in range(2):
            x, sign_x = (0, -1.0) if s == 0 else (size_x - 1, 1.0)
            number = 4 * s + 2 * u + 1
            corner_ref[number : number + 1, :] = (0.5 * macro_step * sign * sign_x) * weight[x : x + 1, :]
        wide = lanes_of((size_x, size_z))
        scale = jnp.where(wide == end, (0.5 * macro_step * sign) * sign_z, 0.0)
        edge_ref[2 * u] = scale * weight
        for x in range(size_x):
            edge_ref[2 * u + 1, x : x + 1, :] = scale[x : x + 1, :] * (0.5 * faces[3, x + 1, y : y + 1, :])

    columns = {(0, 1): (stress_x, 1, 1), (1, 1): (stress_rest, 0, 0), (2, 1): (stress_rest, 2, 0)}
    columns_z = {0: (stress_x, 2, 1), 1: (stress_rest, 2, 0), 2: (stress_rest, 1, 0)}

    def step_plane(x, carry):
        for a in range(3):
            total = stress_x[a, x + 2] - stress_x[a, x]
            ref, number, shift = columns[a, 1]
            total = total + difference_rows(
                ref[number, x + shift], ghost_y[a, pl.ds(x, 1), :], ghost_y[3 + a, pl.ds(x, 1), :]
            )
            ref, number, shift = columns_z[a]
            total = total + (difference_z(ref[number, x + shift]) + ghost_z[a, x])
            out_ref[a, plane(x), :] = padded[a, x + 1] + (0.5 * macro_step) * total
        return carry

    lax.fori_loop(0, size_x, step_plane, 0, unroll=6)


def flow_step(flag_cell, position, velocity, viscosity, chunks, y_low, y_high, first_x, second_x):
    size_x, size_y, size_z = viscosity.shape
    flags = flag_cell.shape[0]
    returned = chunks.shape[0] * back_rows
    row_count = size_x * size_y
    planes = (size_x, size_y, size_z)
    wide = (size_x + 2, size_y, size_z)
    return pl.pallas_call(
        functools.partial(flow_kernel, size_x, size_y, size_z, chunks.shape[0] // 2),
        out_shape=(
            jax.ShapeDtypeStruct((3, size_x * size_y, size_z), jnp.float32),
            jax.ShapeDtypeStruct((8, size_z), jnp.float32),
            jax.ShapeDtypeStruct((4, size_x, size_z), jnp.float32),
            jax.ShapeDtypeStruct((3, flags, size_z), jnp.float32),
            jax.ShapeDtypeStruct((flags, 4 * returned), jnp.bfloat16),
            jax.ShapeDtypeStruct((row_count, 3 * product_depth), jnp.bfloat16),
        ),
        in_specs=[SMEM] * 2 + [VMEM] * 7,
        out_specs=(VMEM,) * 6,
        scratch_shapes=[
            pltpu.VMEM((3, *wide), jnp.float32),
            pltpu.VMEM((3, *wide), jnp.float32),
            pltpu.VMEM((3, *planes), jnp.float32),
            pltpu.VMEM((item_count, *wide), jnp.float32),
            pltpu.VMEM((6, size_x, size_z), jnp.float32),
            pltpu.VMEM((3, *planes), jnp.float32),
            pltpu.VMEM((product_depth, -(-row_count // 128) * 128), jnp.float32),
        ],
        compiler_params=limit(12),
        cost_estimate=pl.CostEstimate(flops=4000000, bytes_accessed=3000000, transcendentals=0),
        name="flow_step",
    )(
        flag_cell, position,
        velocity.reshape(3, size_x * size_y, size_z),
        viscosity.reshape(size_x * size_y, size_z),
        chunks, y_low, y_high, first_x, second_x,
    )


def pieces(value):
    high = value.astype(jnp.bfloat16)
    rest = value - high.astype(jnp.float32)
    middle = rest.astype(jnp.bfloat16)
    return high, middle, (rest - middle.astype(jnp.float32)).astype(jnp.bfloat16)


def polymer_kernel(
    size_x, size_y, size_z, macro_count, chunk_ref, viscous_ref, corner_ref, edge_ref, lines_ref, pick_ref,
    spread_ref, partial_ref, out_ref, flag_ref, field, write_sem,
):
    flags = viscous_ref.shape[0]
    macro, core = place_of()
    chunks = chunk_ref[...]
    split = jnp.concatenate((*pieces(chunks), jnp.zeros(chunks.shape, jnp.bfloat16)), axis=0)
    values = jnp.dot(pick_ref[...], split, preferred_element_type=jnp.float32) * lines_ref[2]
    here, beside_z = lines_ref[0], lines_ref[1]
    lane = lanes_of((flags, 128))
    columns = [
        jnp.broadcast_to(
            jnp.sum(jnp.where((lane & 7) == k, values, 0.0), axis=1, keepdims=True), (flags, size_z)
        )
        for k in range(6)
    ]
    stress = viscous_ref[...]
    for k in range(6):
        stress = jnp.where(lane == k, stress + columns[k], stress)
    unused = jnp.zeros((product_depth - 3 * flags, size_z), jnp.float32)
    split = [
        pieces(
            jnp.concatenate(
                [
                    columns[pair_index(a, 0)] * here, columns[pair_index(a, 1)] * here,
                    columns[pair_index(a, 2)] * beside_z, unused,
                ],
                axis=0,
            )
        )
        for a in range(3)
    ]
    flag_ref[...] = stress.T[0:6, :]

    field[...] = partial_ref[...]
    for s in range(2):
        inside = macro > 0 if s == 0 else macro < macro_count - 1
        beside = jnp.maximum(macro - 1, 0) if s == 0 else jnp.minimum(macro + 1, macro_count - 1)
        start = (2 * beside + core) * back_rows
        x = 0 if s == 0 else size_x - 1
        for u in range(2):
            at = x * size_y + (0 if u == 0 else size_y - 1)
            for a in range(2):
                number = 4 * s + 2 * u + a
                line = corner_ref[number : number + 1, :] * chunk_ref[pl.ds(start + 2 * u + a, 1), :]
                field[1 - a, at : at + 1, :] += jnp.where(inside, line, 0.0)
    start = pl.multiple_of((2 * macro + 1 - core) * back_rows, 8)
    packed = chunk_ref[pl.ds(start, back_rows), :]
    end = jnp.where(core == 0, size_z - 1, 0)
    for u in range(2):
        y = 0 if u == 0 else size_y - 1
        for a in range(2):
            for i in range(size_x // 8):
                line = rolled(packed, end - (line_lane + 4 * i + 2 * u + a)) * edge_ref[2 * u + a, 8 * i : 8 * i + 8, :]
                at = pl.ds(8 * i * size_y + y, 8, stride=size_y)
                field[2 - a, at, :] += line
    copies = [pltpu.make_async_copy(field.at[a], out_ref.at[a], write_sem.at[a]) for a in range(3)]
    for a in range(3):
        field[a] += jnp.dot(
            spread_ref[...], jnp.concatenate(split[a], axis=0), preferred_element_type=jnp.float32
        )
        copies[a].start()
    for copy in copies:
        copy.wait()


def add_polymer(chunks, viscous, corners, edges, lines, pick, spread, partial, shape):
    flags = viscous.shape[0]
    size_x, size_y, size_z = shape
    return pl.pallas_call(
        functools.partial(polymer_kernel, size_x, size_y, size_z, chunks.shape[0] // 2),
        out_shape=(
            jax.ShapeDtypeStruct(partial.shape, jnp.float32),
            jax.ShapeDtypeStruct((6, flags), jnp.float32),
        ),
        in_specs=[VMEM] * 8,
        out_specs=(pl.BlockSpec(memory_space=pltpu.HBM), VMEM),
        scratch_shapes=[pltpu.VMEM(partial.shape, jnp.float32), pltpu.SemaphoreType.DMA((3,))],
        compiler_params=limit(8),
        cost_estimate=pl.CostEstimate(flops=400000, bytes_accessed=3000000, transcendentals=0),
        name="add_polymer",
    )(chunks.reshape(-1, 128), viscous, corners, edges, lines, pick, spread, partial)


def shards(velocity, viscosity, flag_cell, flag_owner, conformations, increments):
    macro_count = lax.axis_size("macro")
    assert lax.axis_size("micro") == 2
    owner_count = 2 * macro_count
    capacity = conformations.shape[1] // owner_count
    size_x, size_y, size_z = viscosity.shape
    assert capacity <= slot_rows and size_y == 8 and size_z == 128 and size_x % 8 == 0 and size_x <= 32
    chunks, position, viscous, first, second, first_x, second_x, first_conform, first_noise = gather_rows(
        flag_cell, flag_owner.reshape(-1), velocity, viscosity, conformations, increments, capacity, owner_count
    )

    def exchange(rows):
        return lax.all_to_all(rows, ("macro", "micro"), split_axis=0, concat_axis=0, tiled=True)

    received = exchange(chunks.reshape(owner_count, -1, 128))

    def swaps(axis):
        result = []
        for start in range(2):
            pairs = [(i, i + 1) for i in range(start, lax.axis_size(axis) - 1, 2)]
            result.append(pairs + [(high, low) for low, high in pairs])
        return result

    first, second = [lax.ppermute(face, "tile", pairs) for face, pairs in zip((first, second), swaps("tile"))]
    first_x, second_x = [
        lax.ppermute(face, "macro", pairs) for face, pairs in zip((first_x, second_x), swaps("macro"))
    ]
    last_state, polymer = advance(
        conformations, increments, received, first_conform, first_noise, capacity
    )
    polymer, y_low, y_high = add_lines(polymer, first, second)
    returned = exchange(polymer)
    partial, corners, edges, lines, pick, spread = flow_step(
        flag_cell, position, velocity, viscosity, received, y_low, y_high, first_x, second_x
    )
    velocity_next, flag_stress = add_polymer(
        returned, viscous, corners, edges, lines, pick, spread, partial, viscosity.shape
    )
    return (velocity_next.reshape(velocity.shape), last_state, flag_stress)


def solution(mesh):
    in_specs = (
        P(None, "macro", "tile", "micro"),
        P("macro", "tile", "micro"),
        P(("macro", "tile", "micro")),
        P(("macro", "tile", "micro"), None),
        P(None, ("macro", "tile", "micro"), None),
        P(None, None, ("macro", "tile", "micro"), None),
    )
    out_specs = (
        P(None, "macro", "tile", "micro"),
        P(None, ("macro", "tile", "micro"), None),
        P(None, ("macro", "tile", "micro")),
    )
    return jax.shard_map(shards, mesh=mesh, in_specs=in_specs, out_specs=out_specs, check_vma=False)
```

```python
import functools

import jax
import jax.numpy as jnp
from jax import lax
from jax.experimental import pallas as pl
from jax.experimental.pallas import tpu as pltpu
from jax.sharding import PartitionSpec as P

stress_pairs = ((0, 0), (1, 1), (2, 2), (0, 1), (0, 2), (1, 2))
macro_step = 0.1
micro_step = 0.01
noise_weight = 0.1
relax_rate = 0.5
fene_extent = 30.0
spring_floor = 0.1
polymer_weight = 0.25

SMEM = pl.BlockSpec(memory_space=pltpu.SMEM)
VMEM = pl.BlockSpec(memory_space=pltpu.VMEM)


def pair_index(left_axis, right_axis):
    return stress_pairs.index((min(left_axis, right_axis), max(left_axis, right_axis)))


def lanes_of(shape):
    return lax.broadcasted_iota(jnp.int32, shape, len(shape) - 1)


slot_rows = 8
face_rows = 32
corner_lane = 64
item_count = 7
back_rows = 8
polymer_row = 4
line_lane = 64


block_slots = 32
first_share = 2


def limit(mebibytes):
    return pltpu.CompilerParams(vmem_limit_bytes=mebibytes * 1024 * 1024)


def far(value):
    return pltpu.with_memory_space_constraint(value, pltpu.HBM)


def place_of():
    return lax.axis_index("macro"), lax.axis_index("micro")


def neighbour(index, side, count):
    return jnp.maximum(index - 1, 0) if side == 0 else jnp.minimum(index + 1, count - 1)


def rolled(value, amount):
    size = value.shape[-1]
    if isinstance(amount, int):
        return pltpu.roll(value, amount % size, value.ndim - 1)
    return pltpu.roll(value, lax.rem(amount + 2 * size, size), value.ndim - 1)


def gather_kernel(
    capacity, size_x, size_y, size_z, macro_count, cell_in, owner_in, velocity_in, viscosity_in,
    conform_in, noise_in, chunk_ref, position_ref, viscous_ref, first_ref, second_ref, conform_ref, noise_ref,
    cell_ref, owner_ref, velocity_ref, viscosity_ref, masked, gradients, target, count, sems,
):
    flags = cell_ref.shape[0]
    copies = [
        pltpu.make_async_copy(source, into, sems.at[number])
        for number, (source, into) in enumerate(
            (
                (cell_in, cell_ref), (owner_in, owner_ref), (velocity_in, velocity_ref),
                (viscosity_in, viscosity_ref), (conform_in.at[:, 0:block_slots, :], conform_ref),
                (noise_in.at[0 : noise_ref.shape[0], :, 0:block_slots, :], noise_ref),
            )
        )
    ]
    for copy in copies:
        copy.start()
    chunk_rows = slot_rows + face_rows
    macro, core = place_of()
    lane = lanes_of((1, size_z))

    for owner in range(count.shape[0]):
        count[owner] = 0
        chunk_ref[owner * chunk_rows : owner * chunk_rows + slot_rows, :] = jnp.zeros((slot_rows, 128), jnp.float32)
    for copy in copies[:2]:
        copy.wait()
    for j in range(flags):
        owner = owner_ref[j]
        rank = count[owner]
        count[owner] = rank + 1
        target[j] = owner * chunk_rows + rank
        position_ref[j] = owner * slot_rows + rank
    for copy in copies[2:4]:
        copy.wait()
    planes = velocity_ref.reshape(3, size_x, size_y, size_z)
    layers = viscosity_ref.reshape(size_x, size_y, size_z)
    for j in range(flags):
        cell = cell_ref[j]
        x = lax.shift_right_logical(cell, 10)
        y = lax.shift_right_logical(cell, 7) & (size_y - 1)
        z = cell & (size_z - 1)
        here = (lane == z).astype(jnp.float32)
        along_z = (lane == z + 1).astype(jnp.float32) - (lane == z - 1).astype(jnp.float32)
        at = pl.ds(y, 1)
        for a in range(3):
            along_x = planes[a, x + 1, at, :] - planes[a, x - 1, at, :]
            along_y = planes[a, x, pl.ds(y + 1, 1), :] - planes[a, x, pl.ds(y - 1, 1), :]
            masked[3 * a, j : j + 1, :] = along_x * here
            masked[3 * a + 1, j : j + 1, :] = along_y * here
            masked[3 * a + 2, j : j + 1, :] = planes[a, x, at, :] * along_z
        masked[9, j : j + 1, :] = layers[x, at, :] * here

    even = lax.axis_index("tile") & 1 == 0

    def put(number, ref, low, high):
        rows = [ref[pl.ds(y, size_x, stride=size_y), :] for y in (low, high)]
        first_ref[number] = jnp.where(even, rows[1], rows[0])
        second_ref[number] = jnp.where(even, rows[0], rows[1])

    for layer in range(2):
        for a in range(3):
            put(3 * layer + a, velocity_ref.at[a], layer, size_y - 1 - layer)
    put(6, viscosity_ref, 0, size_y - 1)

    for side in range(2):
        beside = neighbour(macro, side, macro_count)
        same = pl.multiple_of((2 * beside + core) * chunk_rows + slot_rows, 8)
        other = pl.multiple_of((2 * beside + 1 - core) * chunk_rows + slot_rows, 8)
        for layer, start in enumerate((same, other)):
            x = layer if side == 0 else size_x - 1 - layer
            for a in range(3):
                chunk_ref[pl.ds(start + a * size_y, size_y), :] = velocity_ref[a, x * size_y : (x + 1) * size_y, :]
        x = 0 if side == 0 else size_x - 1
        chunk_ref[pl.ds(other + 3 * size_y, size_y), :] = viscosity_ref[x * size_y : (x + 1) * size_y, :]

    group = size_z // 8
    lane2 = lanes_of((size_y, size_z))
    first = pl.multiple_of((2 * macro + 1 - core) * chunk_rows + slot_rows, 8)
    source = jnp.where(core == 0, size_z - 2, 0)
    for block in range(-(-size_x // group)):
        total = jnp.zeros((size_y, size_z), jnp.float32)
        for x in range(block * group, min(size_x, (block + 1) * group)):
            rows = slice(x * size_y, (x + 1) * size_y)
            for a in range(4):
                at = 8 * (x - block * group) + 2 * a
                value = viscosity_ref[rows, :] if a == 3 else velocity_ref[a, rows, :]
                total = jnp.where((lane2 == at) | (lane2 == at + 1), rolled(value, at - source), total)
        chunk_ref[pl.ds(first + block * size_y, size_y), :] = total

    columns = [0.5 * jnp.sum(masked[c], axis=1, keepdims=True) for c in range(9)]
    viscous = jnp.sum(masked[9], axis=1, keepdims=True)
    wide = lanes_of((flags, 128))
    packed = jnp.zeros((flags, 128), jnp.float32)
    for c in range(9):
        packed = jnp.where(wide == c, columns[c], packed)
    gradients[...] = packed
    stress = jnp.zeros((flags, 128), jnp.float32)
    for k, (a, b) in enumerate(stress_pairs):
        stress = jnp.where(wide == k, viscous * (columns[3 * a + b] + columns[3 * b + a]), stress)
    viscous_ref[...] = stress

    for j in range(flags):
        chunk_ref[pl.ds(target[j], 1), :] = gradients[j : j + 1, :]

    edge = jnp.where(core == 0, size_z - 1, 0)
    for side in range(2):
        beside = neighbour(macro, side, macro_count)
        rows = pl.ds(pl.multiple_of((2 * beside + 1 - core) * chunk_rows, 8), slot_rows)
        x = 0 if side == 0 else size_x - 1
        value = chunk_ref[rows, :]
        for number, a in enumerate((0, 2)):
            plane = velocity_ref[a, x * size_y : (x + 1) * size_y, :]
            at = corner_lane + number
            value = jnp.where(lane2 == at, rolled(plane, at - edge), value)
        chunk_ref[rows, :] = value
    for copy in copies[4:]:
        copy.wait()


def gather_rows(flag_cell, owner, velocity, viscosity, conformations, increments, capacity, owner_count):
    size_x, size_y, size_z = viscosity.shape
    flags = flag_cell.shape[0]
    chunk_rows = slot_rows + face_rows
    face = jax.ShapeDtypeStruct((item_count, size_x, size_z), jnp.float32)
    steps, _, _, dumbbells = increments.shape
    return pl.pallas_call(
        functools.partial(gather_kernel, capacity, size_x, size_y, size_z, owner_count // 2),
        out_shape=(
            jax.ShapeDtypeStruct((owner_count * chunk_rows, 128), jnp.float32),
            jax.ShapeDtypeStruct((flags,), jnp.int32),
            jax.ShapeDtypeStruct((flags, 128), jnp.float32),
            face,
            face,
            pltpu.VMEM((3, block_slots, dumbbells), jnp.float32),
            pltpu.VMEM((steps // first_share, 3, block_slots, dumbbells), jnp.bfloat16),
        ),
        in_specs=[pl.BlockSpec(memory_space=pltpu.HBM)] * 6,
        out_specs=(VMEM, SMEM, VMEM, VMEM, VMEM, VMEM, VMEM),
        scratch_shapes=[
            pltpu.SMEM((flags,), jnp.int32),
            pltpu.SMEM((flags,), jnp.int32),
            pltpu.VMEM((3, size_x * size_y, size_z), jnp.float32),
            pltpu.VMEM((size_x * size_y, size_z), jnp.float32),
            pltpu.VMEM((10, flags, size_z), jnp.float32),
            pltpu.VMEM((flags, 128), jnp.float32),
            pltpu.SMEM((flags,), jnp.int32),
            pltpu.SMEM((owner_count,), jnp.int32),
            pltpu.SemaphoreType.DMA((6,)),
        ],
        compiler_params=limit(8),
        cost_estimate=pl.CostEstimate(flops=400000, bytes_accessed=3000000, transcendentals=0),
        name="gather_rows",
    )(
        far(flag_cell),
        far(owner),
        far(velocity.reshape(3, size_x * size_y, size_z)),
        far(viscosity.reshape(size_x * size_y, size_z)),
        far(conformations),
        far(increments),
    )


def micro_kernel(
    capacity, parts, rows, groups, conform_ref, noise_ref, rate_ref, first_conform_ref, first_noise_ref,
    next_ref, chunk_ref, conform, noise, rate, rate_wide, sums_ref, read_sem, noise_sem,
):
    steps, _, slots, dumbbells = noise_ref.shape
    blocks = slots // rows
    span = steps // groups
    width = dumbbells // parts
    owners = slots // capacity
    scale = 1.0 / noise_weight
    extent = fene_extent * scale * scale

    def block_rows(block):
        return pl.ds(pl.multiple_of(block * rows, rows), rows)

    def read(block):
        at = block_rows(block)
        return pltpu.make_async_copy(conform_ref.at[:, at, :], conform.at[:, at, :], read_sem.at[block])

    def read_noise(block, group):
        at, when = block_rows(block), pl.ds(group * span, span)
        return pltpu.make_async_copy(
            noise_ref.at[when, :, at, :], noise.at[when, :, at, :], noise_sem.at[block, group]
        )

    pieces = [
        (half, slice(part * width, (part + 1) * width)) for half in range(rows // 16) for part in range(parts)
    ]
    assert len(pieces) == 8
    early = groups // first_share
    for block in range(blocks):
        if block > 0:
            read(block).start()
        for group in range(early if block == 0 else 0, groups):
            read_noise(block, group).start()
    conform[:, 0:rows, :] = first_conform_ref[...]
    for step in range(steps // first_share):
        noise[step, :, 0:rows, :] = first_noise_ref[step]
    for owner in range(owners):
        rate[owner * capacity : (owner + 1) * capacity, :] = rate_ref[owner, 0:capacity, :]
        chunk_ref[owner] = jnp.zeros(chunk_ref.shape[1:], jnp.float32)
    for a in range(3):
        for b in range(3):
            column = micro_step * rate[:, 3 * a + b : 3 * a + b + 1] + (1.0 if a == b else 0.0)
            rate_wide[3 * a + b] = jnp.broadcast_to(column, (slots, width))

    def inverses(state, scale):
        rooms = []
        for piece in range(len(pieces)):
            q = state[3 * piece : 3 * piece + 3]
            room = (extent - q[0] * q[0]) - (q[1] * q[1] + q[2] * q[2])
            rooms.append(jnp.maximum(room, extent * spring_floor))
        levels = [rooms]
        while len(levels[-1]) > 1:
            levels.append([low * high for low, high in zip(levels[-1][0::2], levels[-1][1::2])])
        result = [scale * pl.reciprocal(levels[-1][0])]
        for level in reversed(levels[:-1]):
            result = [result[i // 2] * level[i ^ 1] for i in range(len(level))]
        return result

    def advance_block(block, carry):
        ats = [pl.ds(pl.multiple_of(block * rows + 16 * half, 16), 16) for half in range(rows // 16)]
        rates = [
            [[rate_wide.at[3 * a + b, at, :] for b in range(3)] for a in range(3)] for at in ats
        ]

        def substep(step, state):
            updated = []
            springs = inverses(state, micro_step * relax_rate * extent)
            for piece, (half, lanes) in enumerate(pieces):
                q = state[3 * piece : 3 * piece + 3]
                table = rates[half]
                for a in range(3):
                    b, c = [other for other in range(3) if other != a]
                    kick = noise[step, a, ats[half], lanes].astype(jnp.float32)
                    rest = (table[a][b][...] * q[b] + table[a][c][...] * q[c]) + kick
                    updated.append((table[a][a][...] - springs[piece]) * q[a] + rest)
            return tuple(updated)

        def advance_group(group, state):
            if group < early:

                @pl.when(block > 0)
                def _():
                    read_noise(block, group).wait()

            else:
                read_noise(block, group).wait()
            for step in range(span):
                state = substep(group * span + step, state)
            return state

        @pl.when(block > 0)
        def _():
            read(block).wait()

        state = tuple(conform[a, ats[half], lanes] * scale for half, lanes in pieces for a in range(3))
        for group in range(groups):
            state = advance_group(group, state)
        inverse = inverses(state, 1.0)
        for half, at in enumerate(ats):
            sums = [None] * 6
            for piece, (other, lanes) in enumerate(pieces):
                if other != half:
                    continue
                q = state[3 * piece : 3 * piece + 3]
                for a in range(3):
                    next_ref[a, at, lanes] = q[a] * noise_weight
                for k, (a, b) in enumerate(stress_pairs):
                    term = (inverse[piece] * q[a]) * q[b]
                    sums[k] = term if sums[k] is None else sums[k] + term
            for k in range(6):
                sums_ref[k, at, :] = sums[k]
        return carry

    lax.fori_loop(0, blocks, advance_block, 0)
    lane = lanes_of((slots, 128))
    rank = lax.broadcasted_iota(jnp.int32, (slots, 128), 0) & (capacity - 1)
    packed = jnp.zeros((slots, 128), jnp.float32)
    weight = extent * noise_weight * noise_weight / dumbbells
    for k, (a, b) in enumerate(stress_pairs):
        mean = jnp.sum(sums_ref[k], axis=1, keepdims=True) * weight
        packed = jnp.where(lane == 8 * rank + k, polymer_weight * (mean - (1.0 if a == b else 0.0)), packed)
    for owner in range(owners):
        chunk_ref[owner, polymer_row : polymer_row + 1, :] = jnp.sum(
            packed[owner * capacity : (owner + 1) * capacity], axis=0, keepdims=True
        )


def advance(conformations, increments, chunks, first_conform, first_noise, capacity):
    slots, dumbbells = conformations.shape[1:]
    steps = increments.shape[0]
    owners = slots // capacity
    rows, parts, groups = block_slots, 4, 4
    blocks = slots // rows
    whole = pl.BlockSpec(memory_space=pltpu.HBM)
    return pl.pallas_call(
        functools.partial(micro_kernel, capacity, parts, rows, groups),
        out_shape=(
            pltpu.VMEM(conformations.shape, jnp.float32),
            jax.ShapeDtypeStruct((owners, back_rows, 128), jnp.float32),
        ),
        in_specs=[whole, whole, VMEM, VMEM, VMEM],
        out_specs=(VMEM, VMEM),
        scratch_shapes=[
            pltpu.VMEM(conformations.shape, jnp.float32),
            pltpu.VMEM(increments.shape, jnp.bfloat16),
            pltpu.VMEM((slots, 128), jnp.float32),
            pltpu.VMEM((9, slots, dumbbells // parts), jnp.float32),
            pltpu.VMEM((6, slots, dumbbells // parts), jnp.float32),
            pltpu.SemaphoreType.DMA((blocks,)),
            pltpu.SemaphoreType.DMA((blocks, groups)),
        ],
        compiler_params=limit(12),
        cost_estimate=pl.CostEstimate(flops=20000000, bytes_accessed=5000000, transcendentals=600000),
        name="advance",
    )(far(conformations), far(increments), chunks, first_conform, first_noise)


def lines_kernel(
    macro_count, chunk_ref, received_ref, first_ref, second_ref, out_ref, y_low_ref, y_high_ref, handed_ref
):
    out_ref[...] = chunk_ref[...]
    macro, core = place_of()
    for side in range(2):
        beside = neighbour(macro, side, macro_count)
        handed_ref[side] = received_ref[2 * beside + 1 - core, slot_rows:, :]
    even = lax.axis_index("tile") & 1 == 0
    y_low_ref[...] = jnp.where(even, second_ref[...], first_ref[...])
    y_high_ref[...] = jnp.where(even, first_ref[...], second_ref[...])
    sides = (y_low_ref, y_high_ref)
    size_x, size_z = y_low_ref.shape[1:]
    for side in range(2):
        beside = neighbour(macro, side, macro_count)
        x = 0 if side == 0 else size_x - 1
        for u in range(2):
            for a in range(2):
                at = 2 * u + a
                out_ref[2 * beside + core, at : at + 1, :] = sides[u][a, x : x + 1, :]

    lane = lanes_of((8, size_z))
    source = jnp.where(core == 0, size_z - 1, 0)
    other = 2 * macro + 1 - core
    total = chunk_ref[other]
    for i in range(size_x // 8):
        for u in range(2):
            for a in range(2):
                at = line_lane + 4 * i + 2 * u + a
                total = jnp.where(
                    lane == at, rolled(sides[u][1 + a, 8 * i : 8 * i + 8, :], at - source), total
                )
    out_ref[other] = total


def add_lines(chunks, received, first, second):
    face = jax.ShapeDtypeStruct(first.shape, jnp.float32)
    return pl.pallas_call(
        functools.partial(lines_kernel, chunks.shape[0] // 2),
        out_shape=(
            jax.ShapeDtypeStruct(chunks.shape, jnp.float32), face, face,
            jax.ShapeDtypeStruct((2, face_rows, 128), jnp.float32),
        ),
        in_specs=[VMEM] * 4,
        out_specs=(VMEM,) * 4,
        compiler_params=limit(4),
        cost_estimate=pl.CostEstimate(flops=20000, bytes_accessed=400000, transcendentals=0),
        name="add_lines",
    )(chunks, received, first, second)


product_depth = 128


def one_hots(size_y, size_z, cell_ref, position_ref, lines_ref, pick_ref, spread_ref, rows):
    flags = cell_ref.shape[0]
    weight = 0.5 * macro_step
    row_count = spread_ref.shape[0]
    returned = pick_ref.shape[1] // 4
    lane = lanes_of((1, size_z))
    row_lane = lanes_of((1, rows.shape[1]))
    slot_lane = lanes_of((flags, returned))
    flag_row = lax.broadcasted_iota(jnp.int32, (flags, returned), 0)
    rows[3 * flags :, :] = jnp.zeros((product_depth - 3 * flags, rows.shape[1]), jnp.float32)
    slot = jnp.zeros((flags, returned), jnp.int32)
    group = lax.shift_right_logical(lane, 3)
    for j in range(flags):
        cell = cell_ref[j]
        row = lax.div(cell, size_z)
        z = cell - row * size_z
        lines_ref[0, j : j + 1, :] = jnp.where(lane == z, weight, 0.0)
        lines_ref[1, j : j + 1, :] = jnp.where(
            lane == z - 1, weight, jnp.where(lane == z + 1, -weight, 0.0)
        )
        for number, shift in enumerate((size_y, 1)):
            rows[number * flags + j : number * flags + j + 1, :] = jnp.where(
                row_lane == row - shift, 1.0, jnp.where(row_lane == row + shift, -1.0, 0.0)
            )
        rows[2 * flags + j : 2 * flags + j + 1, :] = jnp.where(row_lane == row, 1.0, 0.0)
        owner = lax.div(position_ref[j], slot_rows)
        rank = position_ref[j] - owner * slot_rows
        lines_ref[2, j : j + 1, :] = jnp.where(group == rank, 1.0, 0.0)
        slot = jnp.where(flag_row == j, owner * back_rows + polymer_row, slot)
    spread = rows[...].T[:row_count].astype(jnp.bfloat16)
    pick = jnp.where(slot_lane == slot, 1.0, 0.0).astype(jnp.bfloat16)
    for piece in range(3):
        spread_ref[:, piece * product_depth : (piece + 1) * product_depth] = spread
        pick_ref[:, piece * returned : (piece + 1) * returned] = pick
    pick_ref[:, 3 * returned :] = jnp.zeros((flags, returned), jnp.bfloat16)


def flow_kernel(
    size_x, size_y, size_z, macro_count, cell_ref, position_ref, velocity_ref, viscosity_ref, chunk_ref,
    y_low_ref, y_high_ref, handed_ref, out_ref, corner_ref, edge_ref, lines_ref, pick_ref, spread_ref,
    padded, stress_x, stress_rest, faces, ghost_y, ghost_z, rows,
):
    macro, core = place_of()
    one_hots(size_y, size_z, cell_ref, position_ref, lines_ref, pick_ref, spread_ref, rows)
    inside = (macro > 0, macro < macro_count - 1)
    sign_z = jnp.where(core == 0, 1.0, -1.0)
    end = jnp.where(core == 0, size_z - 1, 0)
    shape = (size_y, size_z)
    lane, row = lanes_of(shape), lax.broadcasted_iota(jnp.int32, shape, 0)
    at_end = jnp.where(lane == end, sign_z, 0.0)

    def kept(value, condition):
        return jnp.where(condition, value, 0.0)

    def plane(x):
        return pl.ds(pl.multiple_of(x * size_y, 8), size_y)

    def difference_z(value):
        lane = lanes_of(value.shape)
        return jnp.where(lane == size_z - 1, 0.0, rolled(value, -1)) - jnp.where(
            lane == 0, 0.0, rolled(value, 1)
        )

    def difference_rows(value, low=0.0, high=0.0):
        count = value.shape[0]
        row = lax.broadcasted_iota(jnp.int32, value.shape, 0)
        return jnp.where(row == count - 1, high, pltpu.roll(value, count - 1, 0)) - jnp.where(
            row == 0, low, pltpu.roll(value, 1, 0)
        )

    x_faces, x_others = [], []
    for s in range(2):
        beside = neighbour(macro, s, macro_count)
        outer = chunk_ref[2 * beside + core, slot_rows : slot_rows + 3 * size_y, :]
        items = [outer[i * size_y : (i + 1) * size_y] for i in range(3)]
        items += [handed_ref[s, i * size_y : (i + 1) * size_y, :] for i in range(4)]
        x_faces.append([kept(item, inside[s]) for item in items])
        corner = chunk_ref[2 * beside + 1 - core, 0:slot_rows, :]
        x_others.append([kept(rolled(corner, end - (corner_lane + i)), inside[s]) for i in range(2)])

    group = size_z // 8
    packed = [
        chunk_ref[2 * macro + 1 - core, slot_rows + i * size_y : slot_rows + (i + 1) * size_y, :]
        for i in range(-(-size_x // group))
    ]
    for i, value in enumerate(packed):

        def unpack(x, carry):
            for q in range(item_count):
                a, layer = (q, 0) if q < 4 else (q - 4, 1)
                at = 8 * (x - i * group) + 2 * a + (core if layer == 0 else 1 - core)
                faces[q, x + 1] = rolled(value, end - at)
            return carry

        lax.fori_loop(i * group, min(size_x, (i + 1) * group), unpack, 0, unroll=8)
    faces[2, 0] = x_others[0][1]
    faces[2, size_x + 1] = x_others[1][1]

    for a in range(3):
        padded[a, 0] = x_faces[0][a]
        padded[a, size_x + 1] = x_faces[1][a]

    def fill(x, carry):
        for a in range(3):
            padded[a, x + 1] = velocity_ref[a, plane(x), :]
        return carry

    lax.fori_loop(0, size_x, fill, 0, unroll=True)

    rest = {(1, 1): 0, (2, 2): 1, (1, 2): 2}

    def stress_plane(x, carry):
        along_x, along_y, along_z, centre = [], [], [], []
        for a in range(3):
            value = padded[a, x + 1]
            centre.append(value)
            along_x.append(padded[a, x + 2] - padded[a, x])
            along_y.append(
                difference_rows(value, y_low_ref[a, pl.ds(x, 1), :], y_high_ref[a, pl.ds(x, 1), :])
            )
            along_z.append(difference_z(value) + faces[a, x + 1] * at_end)
        slopes = (along_x, along_y, along_z)
        half = 0.5 * viscosity_ref[plane(x), :]
        for a, b in stress_pairs:
            value = half * (slopes[b][a] + slopes[a][b])
            if a == 0:
                stress_x[b, x + 1] = value
            else:
                stress_rest[rest[a, b], x] = value
        weight = (0.5 * faces[3, x + 1]) * at_end
        normal = [(faces[4 + a, x + 1] - centre[a]) * sign_z for a in range(3)]
        ghost_z[0, x] = weight * (normal[0] + (faces[2, x + 2] - faces[2, x]))
        ghost_z[1, x] = weight * (normal[1] + difference_rows(faces[2, x + 1]))
        ghost_z[2, x] = weight * (2.0 * normal[2])
        return carry

    lax.fori_loop(0, size_x, stress_plane, 0, unroll=6)

    for s in range(2):
        near, far, weight = x_faces[s][0:3], x_faces[s][3:6], 0.5 * x_faces[s][6]
        sign = -1.0 if s == 0 else 1.0
        normal = [(far[a] - padded[a, 1 if s == 0 else size_x]) * sign for a in range(3)]
        slope_y = difference_rows(near[0])
        slope_z = difference_z(near[0]) + x_others[s][0] * at_end
        at = 0 if s == 0 else size_x + 1
        stress_x[0, at] = weight * (2.0 * normal[0])
        stress_x[1, at] = weight * (normal[1] + slope_y)
        stress_x[2, at] = weight * (normal[2] + slope_z)
        for u in range(2):
            y, sign_y = (0, -1.0) if u == 0 else (size_y - 1, 1.0)
            number = 4 * s + 2 * u
            corner_ref[number : number + 1, :] = (0.5 * macro_step * sign * sign_y) * weight[y : y + 1, :]

    for u, ref in enumerate((y_low_ref, y_high_ref)):
        y, sign = (0, -1.0) if u == 0 else (size_y - 1, 1.0)
        weight = 0.5 * ref[6]
        normal = [
            (ref[3 + a] - velocity_ref[a, pl.ds(y, size_x, stride=size_y), :]) * sign for a in range(3)
        ]
        ghost_y[3 * u] = weight * (normal[0] + difference_rows(ref[1]))
        ghost_y[3 * u + 1] = weight * (2.0 * normal[1])
        ghost_y[3 * u + 2] = weight * (normal[2] + difference_z(ref[1]))
        for s in range(2):
            x, sign_x = (0, -1.0) if s == 0 else (size_x - 1, 1.0)
            number = 4 * s + 2 * u + 1
            corner_ref[number : number + 1, :] = (0.5 * macro_step * sign * sign_x) * weight[x : x + 1, :]
        wide = lanes_of((size_x, size_z))
        scale = jnp.where(wide == end, (0.5 * macro_step * sign) * sign_z, 0.0)
        edge_ref[2 * u] = scale * weight
        for x in range(size_x):
            edge_ref[2 * u + 1, x : x + 1, :] = scale[x : x + 1, :] * (0.5 * faces[3, x + 1, y : y + 1, :])

    columns = {(0, 1): (stress_x, 1, 1), (1, 1): (stress_rest, 0, 0), (2, 1): (stress_rest, 2, 0)}
    columns_z = {0: (stress_x, 2, 1), 1: (stress_rest, 2, 0), 2: (stress_rest, 1, 0)}

    def step_plane(x, carry):
        for a in range(3):
            total = stress_x[a, x + 2] - stress_x[a, x]
            ref, number, shift = columns[a, 1]
            total = total + difference_rows(
                ref[number, x + shift], ghost_y[a, pl.ds(x, 1), :], ghost_y[3 + a, pl.ds(x, 1), :]
            )
            ref, number, shift = columns_z[a]
            total = total + (difference_z(ref[number, x + shift]) + ghost_z[a, x])
            out_ref[a, plane(x), :] = padded[a, x + 1] + (0.5 * macro_step) * total
        return carry

    lax.fori_loop(0, size_x, step_plane, 0, unroll=6)


def flow_step(flag_cell, position, velocity, viscosity, chunks, y_low, y_high, handed):
    size_x, size_y, size_z = viscosity.shape
    flags = flag_cell.shape[0]
    returned = chunks.shape[0] * back_rows
    row_count = size_x * size_y
    planes = (size_x, size_y, size_z)
    wide = (size_x + 2, size_y, size_z)
    return pl.pallas_call(
        functools.partial(flow_kernel, size_x, size_y, size_z, chunks.shape[0] // 2),
        out_shape=(
            jax.ShapeDtypeStruct((3, size_x * size_y, size_z), jnp.float32),
            jax.ShapeDtypeStruct((8, size_z), jnp.float32),
            jax.ShapeDtypeStruct((4, size_x, size_z), jnp.float32),
            jax.ShapeDtypeStruct((3, flags, size_z), jnp.float32),
            jax.ShapeDtypeStruct((flags, 4 * returned), jnp.bfloat16),
            jax.ShapeDtypeStruct((row_count, 3 * product_depth), jnp.bfloat16),
        ),
        in_specs=[SMEM] * 2 + [VMEM] * 6,
        out_specs=(VMEM,) * 6,
        scratch_shapes=[
            pltpu.VMEM((3, *wide), jnp.float32),
            pltpu.VMEM((3, *wide), jnp.float32),
            pltpu.VMEM((3, *planes), jnp.float32),
            pltpu.VMEM((item_count, *wide), jnp.float32),
            pltpu.VMEM((6, size_x, size_z), jnp.float32),
            pltpu.VMEM((3, *planes), jnp.float32),
            pltpu.VMEM((product_depth, -(-row_count // 128) * 128), jnp.float32),
        ],
        compiler_params=limit(12),
        cost_estimate=pl.CostEstimate(flops=4000000, bytes_accessed=3000000, transcendentals=0),
        name="flow_step",
    )(
        flag_cell, position,
        velocity.reshape(3, size_x * size_y, size_z),
        viscosity.reshape(size_x * size_y, size_z),
        chunks, y_low, y_high, handed,
    )


def pieces(value):
    high = value.astype(jnp.bfloat16)
    rest = value - high.astype(jnp.float32)
    middle = rest.astype(jnp.bfloat16)
    return high, middle, (rest - middle.astype(jnp.float32)).astype(jnp.bfloat16)


def polymer_kernel(
    size_x, size_y, size_z, macro_count, chunk_ref, viscous_ref, corner_ref, edge_ref, lines_ref, pick_ref,
    spread_ref, partial_ref, out_ref, flag_ref, field, write_sem,
):
    flags = viscous_ref.shape[0]
    macro, core = place_of()
    chunks = chunk_ref[...]
    split = jnp.concatenate((*pieces(chunks), jnp.zeros(chunks.shape, jnp.bfloat16)), axis=0)
    values = jnp.dot(pick_ref[...], split, preferred_element_type=jnp.float32) * lines_ref[2]
    here, beside_z = lines_ref[0], lines_ref[1]
    lane = lanes_of((flags, 128))
    columns = [
        jnp.broadcast_to(
            jnp.sum(jnp.where((lane & 7) == k, values, 0.0), axis=1, keepdims=True), (flags, size_z)
        )
        for k in range(6)
    ]
    stress = viscous_ref[...]
    for k in range(6):
        stress = jnp.where(lane == k, stress + columns[k], stress)
    unused = jnp.zeros((product_depth - 3 * flags, size_z), jnp.float32)
    split = [
        pieces(
            jnp.concatenate(
                [
                    columns[pair_index(a, 0)] * here, columns[pair_index(a, 1)] * here,
                    columns[pair_index(a, 2)] * beside_z, unused,
                ],
                axis=0,
            )
        )
        for a in range(3)
    ]
    flag_ref[...] = stress.T[0:6, :]

    field[...] = partial_ref[...]
    for s in range(2):
        inside = macro > 0 if s == 0 else macro < macro_count - 1
        beside = jnp.maximum(macro - 1, 0) if s == 0 else jnp.minimum(macro + 1, macro_count - 1)
        start = (2 * beside + core) * back_rows
        x = 0 if s == 0 else size_x - 1
        for u in range(2):
            at = x * size_y + (0 if u == 0 else size_y - 1)
            for a in range(2):
                number = 4 * s + 2 * u + a
                line = corner_ref[number : number + 1, :] * chunk_ref[pl.ds(start + 2 * u + a, 1), :]
                field[1 - a, at : at + 1, :] += jnp.where(inside, line, 0.0)
    start = pl.multiple_of((2 * macro + 1 - core) * back_rows, 8)
    packed = chunk_ref[pl.ds(start, back_rows), :]
    end = jnp.where(core == 0, size_z - 1, 0)
    for u in range(2):
        y = 0 if u == 0 else size_y - 1
        for a in range(2):
            for i in range(size_x // 8):
                line = rolled(packed, end - (line_lane + 4 * i + 2 * u + a)) * edge_ref[2 * u + a, 8 * i : 8 * i + 8, :]
                at = pl.ds(8 * i * size_y + y, 8, stride=size_y)
                field[2 - a, at, :] += line
    copies = [pltpu.make_async_copy(field.at[a], out_ref.at[a], write_sem.at[a]) for a in range(3)]
    for a in range(3):
        field[a] += jnp.dot(
            spread_ref[...], jnp.concatenate(split[a], axis=0), preferred_element_type=jnp.float32
        )
        copies[a].start()
    for copy in copies:
        copy.wait()


def add_polymer(chunks, viscous, corners, edges, lines, pick, spread, partial, shape):
    flags = viscous.shape[0]
    size_x, size_y, size_z = shape
    return pl.pallas_call(
        functools.partial(polymer_kernel, size_x, size_y, size_z, chunks.shape[0] // 2),
        out_shape=(
            jax.ShapeDtypeStruct(partial.shape, jnp.float32),
            jax.ShapeDtypeStruct((6, flags), jnp.float32),
        ),
        in_specs=[VMEM] * 8,
        out_specs=(pl.BlockSpec(memory_space=pltpu.HBM), VMEM),
        scratch_shapes=[pltpu.VMEM(partial.shape, jnp.float32), pltpu.SemaphoreType.DMA((3,))],
        compiler_params=limit(8),
        cost_estimate=pl.CostEstimate(flops=400000, bytes_accessed=3000000, transcendentals=0),
        name="add_polymer",
    )(chunks.reshape(-1, 128), viscous, corners, edges, lines, pick, spread, partial)


def shards(velocity, viscosity, flag_cell, flag_owner, conformations, increments):
    macro_count = lax.axis_size("macro")
    tile_count = lax.axis_size("tile")
    assert lax.axis_size("micro") == 2
    owner_count = 2 * macro_count
    capacity = conformations.shape[1] // owner_count
    size_x, size_y, size_z = viscosity.shape
    assert capacity <= slot_rows and size_y == 8 and size_z == 128 and size_x % 8 == 0 and size_x <= 48
    chunks, position, viscous, first, second, first_conform, first_noise = gather_rows(
        flag_cell, flag_owner.reshape(-1), velocity, viscosity, conformations, increments, capacity, owner_count
    )

    def exchange(rows):
        return lax.all_to_all(rows, ("macro", "micro"), split_axis=0, concat_axis=0, tiled=True)

    received = exchange(chunks.reshape(owner_count, -1, 128))
    swaps = []
    for start in range(2):
        pairs = [(i, i + 1) for i in range(start, tile_count - 1, 2)]
        swaps.append(pairs + [(high, low) for low, high in pairs])
    first = lax.ppermute(first, "tile", swaps[0])
    second = lax.ppermute(second, "tile", swaps[1])
    last_state, polymer = advance(
        conformations, increments, received, first_conform, first_noise, capacity
    )
    polymer, y_low, y_high, handed = add_lines(polymer, received, first, second)
    returned = exchange(polymer)
    handed = lax.ppermute(handed, "micro", [(0, 1), (1, 0)])
    partial, corners, edges, lines, pick, spread = flow_step(
        flag_cell, position, velocity, viscosity, received, y_low, y_high, handed
    )
    velocity_next, flag_stress = add_polymer(
        returned, viscous, corners, edges, lines, pick, spread, partial, viscosity.shape
    )
    return (velocity_next.reshape(velocity.shape), last_state, flag_stress)


def solution(mesh):
    in_specs = (
        P(None, "macro", "tile", "micro"),
        P("macro", "tile", "micro"),
        P(("macro", "tile", "micro")),
        P(("macro", "tile", "micro"), None),
        P(None, ("macro", "tile", "micro"), None),
        P(None, None, ("macro", "tile", "micro"), None),
    )
    out_specs = (
        P(None, "macro", "tile", "micro"),
        P(None, ("macro", "tile", "micro"), None),
        P(None, ("macro", "tile", "micro")),
    )
    return jax.shard_map(shards, mesh=mesh, in_specs=in_specs, out_specs=out_specs, check_vma=False)
```

```python
import functools

import jax
import jax.numpy as jnp
from jax import lax
from jax.experimental import pallas as pl
from jax.experimental.pallas import tpu as pltpu
from jax.sharding import PartitionSpec as P

stress_pairs = ((0, 0), (1, 1), (2, 2), (0, 1), (0, 2), (1, 2))
macro_step = 0.1
micro_step = 0.01
noise_weight = 0.1
relax_rate = 0.5
fene_extent = 30.0
spring_floor = 0.1
polymer_weight = 0.25

SMEM = pl.BlockSpec(memory_space=pltpu.SMEM)
VMEM = pl.BlockSpec(memory_space=pltpu.VMEM)


def pair_index(left_axis, right_axis):
    return stress_pairs.index((min(left_axis, right_axis), max(left_axis, right_axis)))


def lanes_of(shape):
    return lax.broadcasted_iota(jnp.int32, shape, len(shape) - 1)


slot_rows = 8
face_rows = 32
corner_lane = 64
item_count = 7
back_rows = 8
polymer_row = 4
line_lane = 64


block_slots = 32
first_share = 2


def limit(mebibytes):
    return pltpu.CompilerParams(vmem_limit_bytes=mebibytes * 1024 * 1024)


def far(value):
    return pltpu.with_memory_space_constraint(value, pltpu.HBM)


def place_of():
    return lax.axis_index("macro"), lax.axis_index("micro")


def neighbour(index, side, count):
    return jnp.maximum(index - 1, 0) if side == 0 else jnp.minimum(index + 1, count - 1)


def rolled(value, amount):
    size = value.shape[-1]
    if isinstance(amount, int):
        return pltpu.roll(value, amount % size, value.ndim - 1)
    return pltpu.roll(value, lax.rem(amount + 2 * size, size), value.ndim - 1)


def gather_kernel(
    capacity, size_x, size_y, size_z, macro_count, cell_in, owner_in, velocity_in, viscosity_in,
    conform_in, noise_in, chunk_ref, position_ref, viscous_ref, first_ref, second_ref, conform_ref, noise_ref,
    cell_ref, owner_ref, velocity_ref, viscosity_ref, masked, gradients, target, count, sems,
):
    flags = cell_ref.shape[0]
    copies = [
        pltpu.make_async_copy(source, into, sems.at[number])
        for number, (source, into) in enumerate(
            (
                (cell_in, cell_ref), (owner_in, owner_ref), (velocity_in, velocity_ref),
                (viscosity_in, viscosity_ref), (conform_in.at[:, 0:block_slots, :], conform_ref),
                (noise_in.at[0 : noise_ref.shape[0], :, 0:block_slots, :], noise_ref),
            )
        )
    ]
    for copy in copies:
        copy.start()
    chunk_rows = slot_rows + face_rows
    macro, core = place_of()
    lane = lanes_of((1, size_z))

    for owner in range(count.shape[0]):
        count[owner] = 0
        chunk_ref[owner * chunk_rows : owner * chunk_rows + slot_rows, :] = jnp.zeros((slot_rows, 128), jnp.float32)
    for copy in copies[:2]:
        copy.wait()
    for j in range(flags):
        owner = owner_ref[j]
        rank = count[owner]
        count[owner] = rank + 1
        target[j] = owner * chunk_rows + rank
        position_ref[j] = owner * slot_rows + rank
    for copy in copies[2:4]:
        copy.wait()
    planes = velocity_ref.reshape(3, size_x, size_y, size_z)
    layers = viscosity_ref.reshape(size_x, size_y, size_z)
    for j in range(flags):
        cell = cell_ref[j]
        x = lax.shift_right_logical(cell, 10)
        y = lax.shift_right_logical(cell, 7) & (size_y - 1)
        z = cell & (size_z - 1)
        here = (lane == z).astype(jnp.float32)
        along_z = (lane == z + 1).astype(jnp.float32) - (lane == z - 1).astype(jnp.float32)
        at = pl.ds(y, 1)
        for a in range(3):
            along_x = planes[a, x + 1, at, :] - planes[a, x - 1, at, :]
            along_y = planes[a, x, pl.ds(y + 1, 1), :] - planes[a, x, pl.ds(y - 1, 1), :]
            masked[3 * a, j : j + 1, :] = along_x * here
            masked[3 * a + 1, j : j + 1, :] = along_y * here
            masked[3 * a + 2, j : j + 1, :] = planes[a, x, at, :] * along_z
        masked[9, j : j + 1, :] = layers[x, at, :] * here

    even = lax.axis_index("tile") & 1 == 0

    def put(number, ref, low, high):
        rows = [ref[pl.ds(y, size_x, stride=size_y), :] for y in (low, high)]
        first_ref[number] = jnp.where(even, rows[1], rows[0])
        second_ref[number] = jnp.where(even, rows[0], rows[1])

    for layer in range(2):
        for a in range(3):
            put(3 * layer + a, velocity_ref.at[a], layer, size_y - 1 - layer)
    put(6, viscosity_ref, 0, size_y - 1)

    for side in range(2):
        beside = neighbour(macro, side, macro_count)
        same = pl.multiple_of((2 * beside + core) * chunk_rows + slot_rows, 8)
        other = pl.multiple_of((2 * beside + 1 - core) * chunk_rows + slot_rows, 8)
        for layer, start in enumerate((same, other)):
            x = layer if side == 0 else size_x - 1 - layer
            for a in range(3):
                chunk_ref[pl.ds(start + a * size_y, size_y), :] = velocity_ref[a, x * size_y : (x + 1) * size_y, :]
        x = 0 if side == 0 else size_x - 1
        chunk_ref[pl.ds(other + 3 * size_y, size_y), :] = viscosity_ref[x * size_y : (x + 1) * size_y, :]

    group = size_z // 8
    lane2 = lanes_of((size_y, size_z))
    first = pl.multiple_of((2 * macro + 1 - core) * chunk_rows + slot_rows, 8)
    source = jnp.where(core == 0, size_z - 2, 0)
    for block in range(-(-size_x // group)):
        total = jnp.zeros((size_y, size_z), jnp.float32)
        for x in range(block * group, min(size_x, (block + 1) * group)):
            rows = slice(x * size_y, (x + 1) * size_y)
            for a in range(4):
                at = 8 * (x - block * group) + 2 * a
                value = viscosity_ref[rows, :] if a == 3 else velocity_ref[a, rows, :]
                total = jnp.where((lane2 == at) | (lane2 == at + 1), rolled(value, at - source), total)
        chunk_ref[pl.ds(first + block * size_y, size_y), :] = total

    columns = [0.5 * jnp.sum(masked[c], axis=1, keepdims=True) for c in range(9)]
    viscous = jnp.sum(masked[9], axis=1, keepdims=True)
    wide = lanes_of((flags, 128))
    packed = jnp.zeros((flags, 128), jnp.float32)
    for c in range(9):
        packed = jnp.where(wide == c, columns[c], packed)
    gradients[...] = packed
    stress = jnp.zeros((flags, 128), jnp.float32)
    for k, (a, b) in enumerate(stress_pairs):
        stress = jnp.where(wide == k, viscous * (columns[3 * a + b] + columns[3 * b + a]), stress)
    viscous_ref[...] = stress

    for j in range(flags):
        chunk_ref[pl.ds(target[j], 1), :] = gradients[j : j + 1, :]

    edge = jnp.where(core == 0, size_z - 1, 0)
    for side in range(2):
        beside = neighbour(macro, side, macro_count)
        rows = pl.ds(pl.multiple_of((2 * beside + 1 - core) * chunk_rows, 8), slot_rows)
        x = 0 if side == 0 else size_x - 1
        value = chunk_ref[rows, :]
        for number, a in enumerate((0, 2)):
            plane = velocity_ref[a, x * size_y : (x + 1) * size_y, :]
            at = corner_lane + number
            value = jnp.where(lane2 == at, rolled(plane, at - edge), value)
        chunk_ref[rows, :] = value
    for copy in copies[4:]:
        copy.wait()


def gather_rows(flag_cell, owner, velocity, viscosity, conformations, increments, capacity, owner_count):
    size_x, size_y, size_z = viscosity.shape
    flags = flag_cell.shape[0]
    chunk_rows = slot_rows + face_rows
    face = jax.ShapeDtypeStruct((item_count, size_x, size_z), jnp.float32)
    steps, _, _, dumbbells = increments.shape
    return pl.pallas_call(
        functools.partial(gather_kernel, capacity, size_x, size_y, size_z, owner_count // 2),
        out_shape=(
            jax.ShapeDtypeStruct((owner_count * chunk_rows, 128), jnp.float32),
            jax.ShapeDtypeStruct((flags,), jnp.int32),
            jax.ShapeDtypeStruct((flags, 128), jnp.float32),
            face,
            face,
            pltpu.VMEM((3, block_slots, dumbbells), jnp.float32),
            pltpu.VMEM((steps // first_share, 3, block_slots, dumbbells), jnp.bfloat16),
        ),
        in_specs=[pl.BlockSpec(memory_space=pltpu.HBM)] * 6,
        out_specs=(VMEM, SMEM, VMEM, VMEM, VMEM, VMEM, VMEM),
        scratch_shapes=[
            pltpu.SMEM((flags,), jnp.int32),
            pltpu.SMEM((flags,), jnp.int32),
            pltpu.VMEM((3, size_x * size_y, size_z), jnp.float32),
            pltpu.VMEM((size_x * size_y, size_z), jnp.float32),
            pltpu.VMEM((10, flags, size_z), jnp.float32),
            pltpu.VMEM((flags, 128), jnp.float32),
            pltpu.SMEM((flags,), jnp.int32),
            pltpu.SMEM((owner_count,), jnp.int32),
            pltpu.SemaphoreType.DMA((6,)),
        ],
        compiler_params=limit(8),
        cost_estimate=pl.CostEstimate(flops=400000, bytes_accessed=3000000, transcendentals=0),
        name="gather_rows",
    )(
        far(flag_cell),
        far(owner),
        far(velocity.reshape(3, size_x * size_y, size_z)),
        far(viscosity.reshape(size_x * size_y, size_z)),
        far(conformations),
        far(increments),
    )


def micro_kernel(
    capacity, parts, rows, groups, conform_ref, noise_ref, rate_ref, first_conform_ref, first_noise_ref,
    next_ref, chunk_ref, conform, noise, rate, rate_wide, sums_ref, read_sem, noise_sem,
):
    steps, _, slots, dumbbells = noise_ref.shape
    blocks = slots // rows
    span = steps // groups
    width = dumbbells // parts
    owners = slots // capacity
    scale = 1.0 / noise_weight
    extent = fene_extent * scale * scale

    def block_rows(block):
        return pl.ds(pl.multiple_of(block * rows, rows), rows)

    def read(block):
        at = block_rows(block)
        return pltpu.make_async_copy(conform_ref.at[:, at, :], conform.at[:, at, :], read_sem.at[block])

    def read_noise(block, group):
        at, when = block_rows(block), pl.ds(group * span, span)
        return pltpu.make_async_copy(
            noise_ref.at[when, :, at, :], noise.at[when, :, at, :], noise_sem.at[block, group]
        )

    pieces = [
        (half, slice(part * width, (part + 1) * width)) for half in range(rows // 16) for part in range(parts)
    ]
    assert len(pieces) == 8
    early = groups // first_share
    for block in range(blocks):
        if block > 0:
            read(block).start()
        for group in range(early if block == 0 else 0, groups):
            read_noise(block, group).start()
    conform[:, 0:rows, :] = first_conform_ref[...]
    for step in range(steps // first_share):
        noise[step, :, 0:rows, :] = first_noise_ref[step]
    for owner in range(owners):
        rate[owner * capacity : (owner + 1) * capacity, :] = rate_ref[owner, 0:capacity, :]
        chunk_ref[owner] = jnp.zeros(chunk_ref.shape[1:], jnp.float32)
    for a in range(3):
        for b in range(3):
            column = micro_step * rate[:, 3 * a + b : 3 * a + b + 1] + (1.0 if a == b else 0.0)
            rate_wide[3 * a + b] = jnp.broadcast_to(column, (slots, width))

    def inverses(state, scale):
        rooms = []
        for piece in range(len(pieces)):
            q = state[3 * piece : 3 * piece + 3]
            room = (extent - q[0] * q[0]) - (q[1] * q[1] + q[2] * q[2])
            rooms.append(jnp.maximum(room, extent * spring_floor))
        levels = [rooms]
        while len(levels[-1]) > 1:
            levels.append([low * high for low, high in zip(levels[-1][0::2], levels[-1][1::2])])
        result = [scale * pl.reciprocal(levels[-1][0])]
        for level in reversed(levels[:-1]):
            result = [result[i // 2] * level[i ^ 1] for i in range(len(level))]
        return result

    def advance_block(block, carry):
        ats = [pl.ds(pl.multiple_of(block * rows + 16 * half, 16), 16) for half in range(rows // 16)]
        rates = [
            [[rate_wide.at[3 * a + b, at, :] for b in range(3)] for a in range(3)] for at in ats
        ]

        def substep(step, state):
            updated = []
            springs = inverses(state, micro_step * relax_rate * extent)
            for piece, (half, lanes) in enumerate(pieces):
                q = state[3 * piece : 3 * piece + 3]
                table = rates[half]
                for a in range(3):
                    b, c = [other for other in range(3) if other != a]
                    kick = noise[step, a, ats[half], lanes].astype(jnp.float32)
                    rest = (table[a][b][...] * q[b] + table[a][c][...] * q[c]) + kick
                    updated.append((table[a][a][...] - springs[piece]) * q[a] + rest)
            return tuple(updated)

        def advance_group(group, state):
            if group < early:

                @pl.when(block > 0)
                def _():
                    read_noise(block, group).wait()

            else:
                read_noise(block, group).wait()
            for step in range(span):
                state = substep(group * span + step, state)
            return state

        @pl.when(block > 0)
        def _():
            read(block).wait()

        state = tuple(conform[a, ats[half], lanes] * scale for half, lanes in pieces for a in range(3))
        for group in range(groups):
            state = advance_group(group, state)
        inverse = inverses(state, 1.0)
        for half, at in enumerate(ats):
            sums = [None] * 6
            for piece, (other, lanes) in enumerate(pieces):
                if other != half:
                    continue
                q = state[3 * piece : 3 * piece + 3]
                for a in range(3):
                    next_ref[a, at, lanes] = q[a] * noise_weight
                for k, (a, b) in enumerate(stress_pairs):
                    term = (inverse[piece] * q[a]) * q[b]
                    sums[k] = term if sums[k] is None else sums[k] + term
            for k in range(6):
                sums_ref[k, at, :] = sums[k]
        return carry

    lax.fori_loop(0, blocks, advance_block, 0)
    lane = lanes_of((slots, 128))
    rank = lax.broadcasted_iota(jnp.int32, (slots, 128), 0) & (capacity - 1)
    packed = jnp.zeros((slots, 128), jnp.float32)
    weight = extent * noise_weight * noise_weight / dumbbells
    for k, (a, b) in enumerate(stress_pairs):
        mean = jnp.sum(sums_ref[k], axis=1, keepdims=True) * weight
        packed = jnp.where(lane == 8 * rank + k, polymer_weight * (mean - (1.0 if a == b else 0.0)), packed)
    for owner in range(owners):
        chunk_ref[owner, polymer_row : polymer_row + 1, :] = jnp.sum(
            packed[owner * capacity : (owner + 1) * capacity], axis=0, keepdims=True
        )


def advance(conformations, increments, chunks, first_conform, first_noise, capacity):
    slots, dumbbells = conformations.shape[1:]
    steps = increments.shape[0]
    owners = slots // capacity
    rows, parts, groups = block_slots, 4, 4
    blocks = slots // rows
    whole = pl.BlockSpec(memory_space=pltpu.HBM)
    return pl.pallas_call(
        functools.partial(micro_kernel, capacity, parts, rows, groups),
        out_shape=(
            pltpu.VMEM(conformations.shape, jnp.float32),
            jax.ShapeDtypeStruct((owners, back_rows, 128), jnp.float32),
        ),
        in_specs=[whole, whole, VMEM, VMEM, VMEM],
        out_specs=(VMEM, VMEM),
        scratch_shapes=[
            pltpu.VMEM(conformations.shape, jnp.float32),
            pltpu.VMEM(increments.shape, jnp.bfloat16),
            pltpu.VMEM((slots, 128), jnp.float32),
            pltpu.VMEM((9, slots, dumbbells // parts), jnp.float32),
            pltpu.VMEM((6, slots, dumbbells // parts), jnp.float32),
            pltpu.SemaphoreType.DMA((blocks,)),
            pltpu.SemaphoreType.DMA((blocks, groups)),
        ],
        compiler_params=limit(12),
        cost_estimate=pl.CostEstimate(flops=20000000, bytes_accessed=5000000, transcendentals=600000),
        name="advance",
    )(far(conformations), far(increments), chunks, first_conform, first_noise)


def lines_kernel(
    macro_count, chunk_ref, received_ref, first_ref, second_ref, out_ref, y_low_ref, y_high_ref, handed_ref
):
    out_ref[...] = chunk_ref[...]
    macro, core = place_of()
    for side in range(2):
        beside = neighbour(macro, side, macro_count)
        handed_ref[side] = received_ref[2 * beside + 1 - core, slot_rows:, :]
    even = lax.axis_index("tile") & 1 == 0
    y_low_ref[...] = jnp.where(even, second_ref[...], first_ref[...])
    y_high_ref[...] = jnp.where(even, first_ref[...], second_ref[...])
    sides = (y_low_ref, y_high_ref)
    size_x, size_z = y_low_ref.shape[1:]
    for side in range(2):
        beside = neighbour(macro, side, macro_count)
        x = 0 if side == 0 else size_x - 1
        for u in range(2):
            for a in range(2):
                at = 2 * u + a
                out_ref[2 * beside + core, at : at + 1, :] = sides[u][a, x : x + 1, :]

    lane = lanes_of((8, size_z))
    source = jnp.where(core == 0, size_z - 1, 0)
    other = 2 * macro + 1 - core
    total = chunk_ref[other]
    for i in range(size_x // 8):
        for u in range(2):
            for a in range(2):
                at = line_lane + 4 * i + 2 * u + a
                total = jnp.where(
                    lane == at, rolled(sides[u][1 + a, 8 * i : 8 * i + 8, :], at - source), total
                )
    out_ref[other] = total


def add_lines(chunks, received, first, second):
    face = jax.ShapeDtypeStruct(first.shape, jnp.float32)
    return pl.pallas_call(
        functools.partial(lines_kernel, chunks.shape[0] // 2),
        out_shape=(
            jax.ShapeDtypeStruct(chunks.shape, jnp.float32), face, face,
            jax.ShapeDtypeStruct((2, face_rows, 128), jnp.float32),
        ),
        in_specs=[VMEM] * 4,
        out_specs=(VMEM,) * 4,
        compiler_params=limit(4),
        cost_estimate=pl.CostEstimate(flops=20000, bytes_accessed=400000, transcendentals=0),
        name="add_lines",
    )(chunks, received, first, second)


product_depth = 128


def one_hots(core, size_y, size_z, cell_ref, position_ref, lines_ref, pick_ref, spread_ref, rows):
    flags = cell_ref.shape[0]
    weight = 0.5 * macro_step
    row_count = spread_ref.shape[0]
    returned = pick_ref.shape[1] // 4
    lane = lanes_of((1, size_z))
    row_lane = lanes_of((1, rows.shape[1]))
    slot_lane = lanes_of((flags, returned))
    flag_row = lax.broadcasted_iota(jnp.int32, (flags, returned), 0)
    rows[3 * flags :, :] = jnp.zeros((product_depth - 3 * flags, rows.shape[1]), jnp.float32)
    slot = jnp.zeros((flags, returned), jnp.int32)
    group = lax.shift_right_logical(lane, 3)
    for j in range(flags):
        cell = cell_ref[j]
        row = lax.div(cell, size_z)
        z = cell - row * size_z
        lines_ref[0, j : j + 1, :] = jnp.where(lane == z, weight, 0.0)
        lines_ref[1, j : j + 1, :] = jnp.where(
            lane == z - 1, weight, jnp.where(lane == z + 1, -weight, 0.0)
        )
        for number, shift in enumerate((size_y, 1)):
            rows[number * flags + j : number * flags + j + 1, :] = jnp.where(
                row_lane == row - shift, 1.0, jnp.where(row_lane == row + shift, -1.0, 0.0)
            )
        rows[2 * flags + j : 2 * flags + j + 1, :] = jnp.where(row_lane == row, 1.0, 0.0)
        owner = lax.div(position_ref[j], slot_rows)
        rank = position_ref[j] - owner * slot_rows
        lines_ref[2, j : j + 1, :] = jnp.where(group == rank, 1.0, 0.0)
        chip, sender = lax.div(owner, 2), owner & 1
        row = jnp.where(sender == core, 0, returned // 2) + (2 * chip + core) * back_rows + polymer_row
        slot = jnp.where(flag_row == j, row, slot)
    spread = rows[...].T[:row_count].astype(jnp.bfloat16)
    pick = jnp.where(slot_lane == slot, 1.0, 0.0).astype(jnp.bfloat16)
    for piece in range(3):
        spread_ref[:, piece * product_depth : (piece + 1) * product_depth] = spread
        pick_ref[:, piece * returned : (piece + 1) * returned] = pick
    pick_ref[:, 3 * returned :] = jnp.zeros((flags, returned), jnp.bfloat16)


def flow_kernel(
    size_x, size_y, size_z, macro_count, cell_ref, position_ref, velocity_ref, viscosity_ref, chunk_ref,
    y_low_ref, y_high_ref, handed_ref, out_ref, corner_ref, edge_ref, lines_ref, pick_ref, spread_ref,
    padded, stress_x, stress_rest, faces, ghost_y, ghost_z, rows,
):
    macro, core = place_of()
    one_hots(core, size_y, size_z, cell_ref, position_ref, lines_ref, pick_ref, spread_ref, rows)
    inside = (macro > 0, macro < macro_count - 1)
    sign_z = jnp.where(core == 0, 1.0, -1.0)
    end = jnp.where(core == 0, size_z - 1, 0)
    shape = (size_y, size_z)
    lane, row = lanes_of(shape), lax.broadcasted_iota(jnp.int32, shape, 0)
    at_end = jnp.where(lane == end, sign_z, 0.0)

    def kept(value, condition):
        return jnp.where(condition, value, 0.0)

    def plane(x):
        return pl.ds(pl.multiple_of(x * size_y, 8), size_y)

    def difference_z(value):
        lane = lanes_of(value.shape)
        return jnp.where(lane == size_z - 1, 0.0, rolled(value, -1)) - jnp.where(
            lane == 0, 0.0, rolled(value, 1)
        )

    def difference_rows(value, low=0.0, high=0.0):
        count = value.shape[0]
        row = lax.broadcasted_iota(jnp.int32, value.shape, 0)
        return jnp.where(row == count - 1, high, pltpu.roll(value, count - 1, 0)) - jnp.where(
            row == 0, low, pltpu.roll(value, 1, 0)
        )

    x_faces, x_others = [], []
    for s in range(2):
        beside = neighbour(macro, s, macro_count)
        outer = chunk_ref[2 * beside + core, slot_rows : slot_rows + 3 * size_y, :]
        items = [outer[i * size_y : (i + 1) * size_y] for i in range(3)]
        items += [handed_ref[s, i * size_y : (i + 1) * size_y, :] for i in range(4)]
        x_faces.append([kept(item, inside[s]) for item in items])
        corner = chunk_ref[2 * beside + 1 - core, 0:slot_rows, :]
        x_others.append([kept(rolled(corner, end - (corner_lane + i)), inside[s]) for i in range(2)])

    group = size_z // 8
    packed = [
        chunk_ref[2 * macro + 1 - core, slot_rows + i * size_y : slot_rows + (i + 1) * size_y, :]
        for i in range(-(-size_x // group))
    ]
    for i, value in enumerate(packed):

        def unpack(x, carry):
            for q in range(item_count):
                a, layer = (q, 0) if q < 4 else (q - 4, 1)
                at = 8 * (x - i * group) + 2 * a + (core if layer == 0 else 1 - core)
                faces[q, x + 1] = rolled(value, end - at)
            return carry

        lax.fori_loop(i * group, min(size_x, (i + 1) * group), unpack, 0, unroll=8)
    faces[2, 0] = x_others[0][1]
    faces[2, size_x + 1] = x_others[1][1]

    for a in range(3):
        padded[a, 0] = x_faces[0][a]
        padded[a, size_x + 1] = x_faces[1][a]

    def fill(x, carry):
        for a in range(3):
            padded[a, x + 1] = velocity_ref[a, plane(x), :]
        return carry

    lax.fori_loop(0, size_x, fill, 0, unroll=True)

    rest = {(1, 1): 0, (2, 2): 1, (1, 2): 2}

    def stress_plane(x, carry):
        along_x, along_y, along_z, centre = [], [], [], []
        for a in range(3):
            value = padded[a, x + 1]
            centre.append(value)
            along_x.append(padded[a, x + 2] - padded[a, x])
            along_y.append(
                difference_rows(value, y_low_ref[a, pl.ds(x, 1), :], y_high_ref[a, pl.ds(x, 1), :])
            )
            along_z.append(difference_z(value) + faces[a, x + 1] * at_end)
        slopes = (along_x, along_y, along_z)
        half = 0.5 * viscosity_ref[plane(x), :]
        for a, b in stress_pairs:
            value = half * (slopes[b][a] + slopes[a][b])
            if a == 0:
                stress_x[b, x + 1] = value
            else:
                stress_rest[rest[a, b], x] = value
        weight = (0.5 * faces[3, x + 1]) * at_end
        normal = [(faces[4 + a, x + 1] - centre[a]) * sign_z for a in range(3)]
        ghost_z[0, x] = weight * (normal[0] + (faces[2, x + 2] - faces[2, x]))
        ghost_z[1, x] = weight * (normal[1] + difference_rows(faces[2, x + 1]))
        ghost_z[2, x] = weight * (2.0 * normal[2])
        return carry

    lax.fori_loop(0, size_x, stress_plane, 0, unroll=6)

    for s in range(2):
        near, far, weight = x_faces[s][0:3], x_faces[s][3:6], 0.5 * x_faces[s][6]
        sign = -1.0 if s == 0 else 1.0
        normal = [(far[a] - padded[a, 1 if s == 0 else size_x]) * sign for a in range(3)]
        slope_y = difference_rows(near[0])
        slope_z = difference_z(near[0]) + x_others[s][0] * at_end
        at = 0 if s == 0 else size_x + 1
        stress_x[0, at] = weight * (2.0 * normal[0])
        stress_x[1, at] = weight * (normal[1] + slope_y)
        stress_x[2, at] = weight * (normal[2] + slope_z)
        for u in range(2):
            y, sign_y = (0, -1.0) if u == 0 else (size_y - 1, 1.0)
            number = 4 * s + 2 * u
            corner_ref[number : number + 1, :] = (0.5 * macro_step * sign * sign_y) * weight[y : y + 1, :]

    for u, ref in enumerate((y_low_ref, y_high_ref)):
        y, sign = (0, -1.0) if u == 0 else (size_y - 1, 1.0)
        weight = 0.5 * ref[6]
        normal = [
            (ref[3 + a] - velocity_ref[a, pl.ds(y, size_x, stride=size_y), :]) * sign for a in range(3)
        ]
        ghost_y[3 * u] = weight * (normal[0] + difference_rows(ref[1]))
        ghost_y[3 * u + 1] = weight * (2.0 * normal[1])
        ghost_y[3 * u + 2] = weight * (normal[2] + difference_z(ref[1]))
        for s in range(2):
            x, sign_x = (0, -1.0) if s == 0 else (size_x - 1, 1.0)
            number = 4 * s + 2 * u + 1
            corner_ref[number : number + 1, :] = (0.5 * macro_step * sign * sign_x) * weight[x : x + 1, :]
        wide = lanes_of((size_x, size_z))
        scale = jnp.where(wide == end, (0.5 * macro_step * sign) * sign_z, 0.0)
        edge_ref[2 * u] = scale * weight
        for x in range(size_x):
            edge_ref[2 * u + 1, x : x + 1, :] = scale[x : x + 1, :] * (0.5 * faces[3, x + 1, y : y + 1, :])

    columns = {(0, 1): (stress_x, 1, 1), (1, 1): (stress_rest, 0, 0), (2, 1): (stress_rest, 2, 0)}
    columns_z = {0: (stress_x, 2, 1), 1: (stress_rest, 2, 0), 2: (stress_rest, 1, 0)}

    def step_plane(x, carry):
        for a in range(3):
            total = stress_x[a, x + 2] - stress_x[a, x]
            ref, number, shift = columns[a, 1]
            total = total + difference_rows(
                ref[number, x + shift], ghost_y[a, pl.ds(x, 1), :], ghost_y[3 + a, pl.ds(x, 1), :]
            )
            ref, number, shift = columns_z[a]
            total = total + (difference_z(ref[number, x + shift]) + ghost_z[a, x])
            out_ref[a, plane(x), :] = padded[a, x + 1] + (0.5 * macro_step) * total
        return carry

    lax.fori_loop(0, size_x, step_plane, 0, unroll=6)


def flow_step(flag_cell, position, velocity, viscosity, chunks, y_low, y_high, handed):
    size_x, size_y, size_z = viscosity.shape
    flags = flag_cell.shape[0]
    returned = 2 * chunks.shape[0] * back_rows
    row_count = size_x * size_y
    planes = (size_x, size_y, size_z)
    wide = (size_x + 2, size_y, size_z)
    return pl.pallas_call(
        functools.partial(flow_kernel, size_x, size_y, size_z, chunks.shape[0] // 2),
        out_shape=(
            jax.ShapeDtypeStruct((3, size_x * size_y, size_z), jnp.float32),
            jax.ShapeDtypeStruct((8, size_z), jnp.float32),
            jax.ShapeDtypeStruct((4, size_x, size_z), jnp.float32),
            jax.ShapeDtypeStruct((3, flags, size_z), jnp.float32),
            jax.ShapeDtypeStruct((flags, 4 * returned), jnp.bfloat16),
            jax.ShapeDtypeStruct((row_count, 3 * product_depth), jnp.bfloat16),
        ),
        in_specs=[SMEM] * 2 + [VMEM] * 6,
        out_specs=(VMEM,) * 6,
        scratch_shapes=[
            pltpu.VMEM((3, *wide), jnp.float32),
            pltpu.VMEM((3, *wide), jnp.float32),
            pltpu.VMEM((3, *planes), jnp.float32),
            pltpu.VMEM((item_count, *wide), jnp.float32),
            pltpu.VMEM((6, size_x, size_z), jnp.float32),
            pltpu.VMEM((3, *planes), jnp.float32),
            pltpu.VMEM((product_depth, -(-row_count // 128) * 128), jnp.float32),
        ],
        compiler_params=limit(12),
        cost_estimate=pl.CostEstimate(flops=4000000, bytes_accessed=3000000, transcendentals=0),
        name="flow_step",
    )(
        flag_cell, position,
        velocity.reshape(3, size_x * size_y, size_z),
        viscosity.reshape(size_x * size_y, size_z),
        chunks, y_low, y_high, handed,
    )


def pieces(value):
    high = value.astype(jnp.bfloat16)
    rest = value - high.astype(jnp.float32)
    middle = rest.astype(jnp.bfloat16)
    return high, middle, (rest - middle.astype(jnp.float32)).astype(jnp.bfloat16)


def polymer_kernel(
    size_x, size_y, size_z, macro_count, own_ref, other_ref, viscous_ref, corner_ref, edge_ref, lines_ref, pick_ref,
    spread_ref, partial_ref, out_ref, flag_ref, field, write_sem,
):
    flags = viscous_ref.shape[0]
    macro, core = place_of()
    chunks = jnp.concatenate([own_ref[...], other_ref[...]], axis=0)
    split = jnp.concatenate((*pieces(chunks), jnp.zeros(chunks.shape, jnp.bfloat16)), axis=0)
    values = jnp.dot(pick_ref[...], split, preferred_element_type=jnp.float32) * lines_ref[2]
    here, beside_z = lines_ref[0], lines_ref[1]
    lane = lanes_of((flags, 128))
    columns = [
        jnp.broadcast_to(
            jnp.sum(jnp.where((lane & 7) == k, values, 0.0), axis=1, keepdims=True), (flags, size_z)
        )
        for k in range(6)
    ]
    stress = viscous_ref[...]
    for k in range(6):
        stress = jnp.where(lane == k, stress + columns[k], stress)
    unused = jnp.zeros((product_depth - 3 * flags, size_z), jnp.float32)
    split = [
        pieces(
            jnp.concatenate(
                [
                    columns[pair_index(a, 0)] * here, columns[pair_index(a, 1)] * here,
                    columns[pair_index(a, 2)] * beside_z, unused,
                ],
                axis=0,
            )
        )
        for a in range(3)
    ]
    flag_ref[...] = stress.T[0:6, :]

    field[...] = partial_ref[...]
    for s in range(2):
        inside = macro > 0 if s == 0 else macro < macro_count - 1
        beside = jnp.maximum(macro - 1, 0) if s == 0 else jnp.minimum(macro + 1, macro_count - 1)
        start = (2 * beside + core) * back_rows
        x = 0 if s == 0 else size_x - 1
        for u in range(2):
            at = x * size_y + (0 if u == 0 else size_y - 1)
            for a in range(2):
                number = 4 * s + 2 * u + a
                line = corner_ref[number : number + 1, :] * own_ref[pl.ds(start + 2 * u + a, 1), :]
                field[1 - a, at : at + 1, :] += jnp.where(inside, line, 0.0)
    start = pl.multiple_of((2 * macro + core) * back_rows, 8)
    packed = other_ref[pl.ds(start, back_rows), :]
    end = jnp.where(core == 0, size_z - 1, 0)
    for u in range(2):
        y = 0 if u == 0 else size_y - 1
        for a in range(2):
            for i in range(size_x // 8):
                line = rolled(packed, end - (line_lane + 4 * i + 2 * u + a)) * edge_ref[2 * u + a, 8 * i : 8 * i + 8, :]
                at = pl.ds(8 * i * size_y + y, 8, stride=size_y)
                field[2 - a, at, :] += line
    copies = [pltpu.make_async_copy(field.at[a], out_ref.at[a], write_sem.at[a]) for a in range(3)]
    for a in range(3):
        field[a] += jnp.dot(
            spread_ref[...], jnp.concatenate(split[a], axis=0), preferred_element_type=jnp.float32
        )
        copies[a].start()
    for copy in copies:
        copy.wait()


def add_polymer(own, other, viscous, corners, edges, lines, pick, spread, partial, shape):
    flags = viscous.shape[0]
    size_x, size_y, size_z = shape
    return pl.pallas_call(
        functools.partial(polymer_kernel, size_x, size_y, size_z, own.shape[0]),
        out_shape=(
            jax.ShapeDtypeStruct(partial.shape, jnp.float32),
            jax.ShapeDtypeStruct((6, flags), jnp.float32),
        ),
        in_specs=[VMEM] * 9,
        out_specs=(pl.BlockSpec(memory_space=pltpu.HBM), VMEM),
        scratch_shapes=[pltpu.VMEM(partial.shape, jnp.float32), pltpu.SemaphoreType.DMA((3,))],
        compiler_params=limit(8),
        cost_estimate=pl.CostEstimate(flops=400000, bytes_accessed=3000000, transcendentals=0),
        name="add_polymer",
    )(own.reshape(-1, 128), other.reshape(-1, 128), viscous, corners, edges, lines, pick, spread, partial)


def shards(velocity, viscosity, flag_cell, flag_owner, conformations, increments):
    macro_count = lax.axis_size("macro")
    tile_count = lax.axis_size("tile")
    assert lax.axis_size("micro") == 2
    owner_count = 2 * macro_count
    capacity = conformations.shape[1] // owner_count
    size_x, size_y, size_z = viscosity.shape
    assert capacity <= slot_rows and size_y == 8 and size_z == 128 and size_x % 8 == 0 and size_x <= 48
    chunks, position, viscous, first, second, first_conform, first_noise = gather_rows(
        flag_cell, flag_owner.reshape(-1), velocity, viscosity, conformations, increments, capacity, owner_count
    )

    def exchange(rows):
        return lax.all_to_all(rows, ("macro", "micro"), split_axis=0, concat_axis=0, tiled=True)

    received = exchange(chunks.reshape(owner_count, -1, 128))
    swaps = []
    for start in range(2):
        pairs = [(i, i + 1) for i in range(start, tile_count - 1, 2)]
        swaps.append(pairs + [(high, low) for low, high in pairs])
    first = lax.ppermute(first, "tile", swaps[0])
    second = lax.ppermute(second, "tile", swaps[1])
    last_state, polymer = advance(
        conformations, increments, received, first_conform, first_noise, capacity
    )
    polymer, y_low, y_high, handed = add_lines(polymer, received, first, second)
    returned = lax.all_to_all(
        polymer.reshape(macro_count, 2 * back_rows, 128), "macro", split_axis=0, concat_axis=0, tiled=True
    )
    other = lax.ppermute(returned, "micro", [(0, 1), (1, 0)])
    handed = lax.ppermute(handed, "micro", [(0, 1), (1, 0)])
    partial, corners, edges, lines, pick, spread = flow_step(
        flag_cell, position, velocity, viscosity, received, y_low, y_high, handed
    )
    velocity_next, flag_stress = add_polymer(
        returned, other, viscous, corners, edges, lines, pick, spread, partial, viscosity.shape
    )
    return (velocity_next.reshape(velocity.shape), last_state, flag_stress)


def solution(mesh):
    in_specs = (
        P(None, "macro", "tile", "micro"),
        P("macro", "tile", "micro"),
        P(("macro", "tile", "micro")),
        P(("macro", "tile", "micro"), None),
        P(None, ("macro", "tile", "micro"), None),
        P(None, None, ("macro", "tile", "micro"), None),
    )
    out_specs = (
        P(None, "macro", "tile", "micro"),
        P(None, ("macro", "tile", "micro"), None),
        P(None, ("macro", "tile", "micro")),
    )
    return jax.shard_map(shards, mesh=mesh, in_specs=in_specs, out_specs=out_specs, check_vma=False)
```

```python
import functools

import jax
import jax.numpy as jnp
from jax import lax
from jax.experimental import pallas as pl
from jax.experimental.pallas import tpu as pltpu
from jax.sharding import PartitionSpec as P

stress_pairs = ((0, 0), (1, 1), (2, 2), (0, 1), (0, 2), (1, 2))
macro_step = 0.1
micro_step = 0.01
noise_weight = 0.1
relax_rate = 0.5
fene_extent = 30.0
spring_floor = 0.1
polymer_weight = 0.25

SMEM = pl.BlockSpec(memory_space=pltpu.SMEM)
VMEM = pl.BlockSpec(memory_space=pltpu.VMEM)


def pair_index(left_axis, right_axis):
    return stress_pairs.index((min(left_axis, right_axis), max(left_axis, right_axis)))


def lanes_of(shape):
    return lax.broadcasted_iota(jnp.int32, shape, len(shape) - 1)


slot_rows = 8
chunk_rows = 32
half_face = 28
handed_rows = 48
item_count = 7
back_rows = 8
polymer_row = 4
line_lane = 64


block_slots = 32
first_share = 2


def limit(mebibytes):
    return pltpu.CompilerParams(vmem_limit_bytes=mebibytes * 1024 * 1024)


def far(value):
    return pltpu.with_memory_space_constraint(value, pltpu.HBM)


def place_of():
    return lax.axis_index("macro"), lax.axis_index("micro")


def neighbour(index, side, count):
    return jnp.maximum(index - 1, 0) if side == 0 else jnp.minimum(index + 1, count - 1)


def rolled(value, amount):
    size = value.shape[-1]
    if isinstance(amount, int):
        return pltpu.roll(value, amount % size, value.ndim - 1)
    return pltpu.roll(value, lax.rem(amount + 2 * size, size), value.ndim - 1)


def gather_kernel(
    capacity, size_x, size_y, size_z, macro_count, cell_in, owner_in, velocity_in, viscosity_in,
    conform_in, noise_in, chunk_ref, position_ref, viscous_ref, first_ref, second_ref, conform_ref, noise_ref,
    cell_ref, owner_ref, velocity_ref, viscosity_ref, masked, gradients, paired, target, count, sems,
):
    flags = cell_ref.shape[0]
    copies = [
        pltpu.make_async_copy(source, into, sems.at[number])
        for number, (source, into) in enumerate(
            (
                (cell_in, cell_ref), (owner_in, owner_ref), (velocity_in, velocity_ref),
                (viscosity_in, viscosity_ref), (conform_in.at[:, 0:block_slots, :], conform_ref),
                (noise_in.at[0 : noise_ref.shape[0], :, 0:block_slots, :], noise_ref),
            )
        )
    ]
    for copy in copies:
        copy.start()
    paired_rows = paired.shape[0] // 2
    macro, core = place_of()
    lane = lanes_of((1, size_z))

    for owner in range(count.shape[0]):
        count[owner] = 0
    paired[...] = jnp.zeros_like(paired)
    for copy in copies[:2]:
        copy.wait()
    for j in range(flags):
        owner = owner_ref[j]
        rank = count[owner]
        count[owner] = rank + 1
        target[j] = (rank & 1) * paired_rows + owner * (slot_rows // 2) + lax.shift_right_logical(rank, 1)
        position_ref[j] = owner * slot_rows + rank
    for copy in copies[2:4]:
        copy.wait()
    planes = velocity_ref.reshape(3, size_x, size_y, size_z)
    layers = viscosity_ref.reshape(size_x, size_y, size_z)
    for j in range(flags):
        cell = cell_ref[j]
        x = lax.shift_right_logical(cell, 10)
        y = lax.shift_right_logical(cell, 7) & (size_y - 1)
        z = cell & (size_z - 1)
        here = (lane == z).astype(jnp.float32)
        along_z = (lane == z + 1).astype(jnp.float32) - (lane == z - 1).astype(jnp.float32)
        at = pl.ds(y, 1)
        for a in range(3):
            along_x = planes[a, x + 1, at, :] - planes[a, x - 1, at, :]
            along_y = planes[a, x, pl.ds(y + 1, 1), :] - planes[a, x, pl.ds(y - 1, 1), :]
            masked[3 * a, j : j + 1, :] = along_x * here
            masked[3 * a + 1, j : j + 1, :] = along_y * here
            masked[3 * a + 2, j : j + 1, :] = planes[a, x, at, :] * along_z
        masked[9, j : j + 1, :] = layers[x, at, :] * here

    even = lax.axis_index("tile") & 1 == 0

    def put(number, ref, low, high):
        rows = [ref[pl.ds(y, size_x, stride=size_y), :] for y in (low, high)]
        first_ref[number] = jnp.where(even, rows[1], rows[0])
        second_ref[number] = jnp.where(even, rows[0], rows[1])

    for layer in range(2):
        for a in range(3):
            put(3 * layer + a, velocity_ref.at[a], layer, size_y - 1 - layer)
    put(6, viscosity_ref, 0, size_y - 1)

    for side in range(2):
        beside = neighbour(macro, side, macro_count)
        for layer, owner in enumerate((2 * beside + core, 2 * beside + 1 - core)):
            start = pl.multiple_of(owner * chunk_rows, 8)
            x = layer if side == 0 else size_x - 1 - layer
            for a in range(3):
                chunk_ref[pl.ds(start + a * size_y, size_y), :] = velocity_ref[a, x * size_y : (x + 1) * size_y, :]
            x = 0 if side == 0 else size_x - 1
            half = x * size_y + layer * (size_y // 2)
            chunk_ref[pl.ds(start + 3 * size_y, size_y // 2), :] = viscosity_ref[half : half + size_y // 2, :]

    group = size_z // 8
    lane2 = lanes_of((size_y, size_z))
    first = pl.multiple_of((2 * macro + 1 - core) * chunk_rows, 8)
    source = jnp.where(core == 0, size_z - 2, 0)
    for block in range(-(-size_x // group)):
        total = jnp.zeros((size_y, size_z), jnp.float32)
        for x in range(block * group, min(size_x, (block + 1) * group)):
            rows = slice(x * size_y, (x + 1) * size_y)
            for a in range(4):
                at = 8 * (x - block * group) + 2 * a
                value = viscosity_ref[rows, :] if a == 3 else velocity_ref[a, rows, :]
                total = jnp.where((lane2 == at) | (lane2 == at + 1), rolled(value, at - source), total)
        chunk_ref[pl.ds(first + block * size_y, size_y), :] = total

    columns = [0.5 * jnp.sum(masked[c], axis=1, keepdims=True) for c in range(9)]
    viscous = jnp.sum(masked[9], axis=1, keepdims=True)
    wide = lanes_of((flags, 128))
    packed = jnp.zeros((flags, 128), jnp.float32)
    for c in range(9):
        packed = jnp.where(wide == c, columns[c], packed)
    gradients[...] = packed
    stress = jnp.zeros((flags, 128), jnp.float32)
    for k, (a, b) in enumerate(stress_pairs):
        stress = jnp.where(wide == k, viscous * (columns[3 * a + b] + columns[3 * b + a]), stress)
    viscous_ref[...] = stress

    for j in range(flags):
        paired[pl.ds(target[j], 1), :] = gradients[j : j + 1, :]
    rows = paired[0:paired_rows, :] + rolled(paired[paired_rows:, :], 64)
    for owner in range(count.shape[0]):
        chunk_ref[owner * chunk_rows + half_face : (owner + 1) * chunk_rows, :] = rows[
            owner * (slot_rows // 2) : (owner + 1) * (slot_rows // 2)
        ]
    for copy in copies[4:]:
        copy.wait()


def gather_rows(flag_cell, owner, velocity, viscosity, conformations, increments, capacity, owner_count):
    size_x, size_y, size_z = viscosity.shape
    flags = flag_cell.shape[0]
    face = jax.ShapeDtypeStruct((item_count, size_x, size_z), jnp.float32)
    steps, _, _, dumbbells = increments.shape
    return pl.pallas_call(
        functools.partial(gather_kernel, capacity, size_x, size_y, size_z, owner_count // 2),
        out_shape=(
            jax.ShapeDtypeStruct((owner_count * chunk_rows, 128), jnp.float32),
            jax.ShapeDtypeStruct((flags,), jnp.int32),
            jax.ShapeDtypeStruct((flags, 128), jnp.float32),
            face,
            face,
            pltpu.VMEM((3, block_slots, dumbbells), jnp.float32),
            pltpu.VMEM((steps // first_share, 3, block_slots, dumbbells), jnp.bfloat16),
        ),
        in_specs=[pl.BlockSpec(memory_space=pltpu.HBM)] * 6,
        out_specs=(VMEM, SMEM, VMEM, VMEM, VMEM, VMEM, VMEM),
        scratch_shapes=[
            pltpu.SMEM((flags,), jnp.int32),
            pltpu.SMEM((flags,), jnp.int32),
            pltpu.VMEM((3, size_x * size_y, size_z), jnp.float32),
            pltpu.VMEM((size_x * size_y, size_z), jnp.float32),
            pltpu.VMEM((10, flags, size_z), jnp.float32),
            pltpu.VMEM((flags, 128), jnp.float32),
            pltpu.VMEM((owner_count * slot_rows, 128), jnp.float32),
            pltpu.SMEM((flags,), jnp.int32),
            pltpu.SMEM((owner_count,), jnp.int32),
            pltpu.SemaphoreType.DMA((6,)),
        ],
        compiler_params=limit(8),
        cost_estimate=pl.CostEstimate(flops=400000, bytes_accessed=3000000, transcendentals=0),
        name="gather_rows",
    )(
        far(flag_cell),
        far(owner),
        far(velocity.reshape(3, size_x * size_y, size_z)),
        far(viscosity.reshape(size_x * size_y, size_z)),
        far(conformations),
        far(increments),
    )


def micro_kernel(
    capacity, parts, rows, groups, conform_ref, noise_ref, rate_ref, first_conform_ref, first_noise_ref,
    next_ref, chunk_ref, conform, noise, rate, rate_wide, sums_ref, read_sem, noise_sem,
):
    steps, _, slots, dumbbells = noise_ref.shape
    blocks = slots // rows
    span = steps // groups
    width = dumbbells // parts
    owners = slots // capacity
    scale = 1.0 / noise_weight
    extent = fene_extent * scale * scale

    def block_rows(block):
        return pl.ds(pl.multiple_of(block * rows, rows), rows)

    def read(block):
        at = block_rows(block)
        return pltpu.make_async_copy(conform_ref.at[:, at, :], conform.at[:, at, :], read_sem.at[block])

    def read_noise(block, group):
        at, when = block_rows(block), pl.ds(group * span, span)
        return pltpu.make_async_copy(
            noise_ref.at[when, :, at, :], noise.at[when, :, at, :], noise_sem.at[block, group]
        )

    pieces = [
        (half, slice(part * width, (part + 1) * width)) for half in range(rows // 16) for part in range(parts)
    ]
    assert len(pieces) == 8
    early = groups // first_share
    for block in range(blocks):
        if block > 0:
            read(block).start()
        for group in range(early if block == 0 else 0, groups):
            read_noise(block, group).start()
    conform[:, 0:rows, :] = first_conform_ref[...]
    for step in range(steps // first_share):
        noise[step, :, 0:rows, :] = first_noise_ref[step]
    for owner in range(owners):
        packed = rate_ref[owner, half_face : half_face + capacity // 2, :]
        rate[pl.ds(owner * capacity, capacity // 2, stride=2), :] = packed
        rate[pl.ds(owner * capacity + 1, capacity // 2, stride=2), :] = rolled(packed, 64)
        chunk_ref[owner] = jnp.zeros(chunk_ref.shape[1:], jnp.float32)
    for a in range(3):
        for b in range(3):
            column = micro_step * rate[:, 3 * a + b : 3 * a + b + 1] + (1.0 if a == b else 0.0)
            rate_wide[3 * a + b] = jnp.broadcast_to(column, (slots, width))

    def inverses(state, scale):
        rooms = []
        for piece in range(len(pieces)):
            q = state[3 * piece : 3 * piece + 3]
            room = (extent - q[0] * q[0]) - (q[1] * q[1] + q[2] * q[2])
            rooms.append(jnp.maximum(room, extent * spring_floor))
        levels = [rooms]
        while len(levels[-1]) > 1:
            levels.append([low * high for low, high in zip(levels[-1][0::2], levels[-1][1::2])])
        result = [scale * pl.reciprocal(levels[-1][0])]
        for level in reversed(levels[:-1]):
            result = [result[i // 2] * level[i ^ 1] for i in range(len(level))]
        return result

    def advance_block(block, carry):
        ats = [pl.ds(pl.multiple_of(block * rows + 16 * half, 16), 16) for half in range(rows // 16)]
        rates = [
            [[rate_wide.at[3 * a + b, at, :] for b in range(3)] for a in range(3)] for at in ats
        ]

        def substep(step, state):
            updated = []
            springs = inverses(state, micro_step * relax_rate * extent)
            for piece, (half, lanes) in enumerate(pieces):
                q = state[3 * piece : 3 * piece + 3]
                table = rates[half]
                for a in range(3):
                    b, c = [other for other in range(3) if other != a]
                    kick = noise[step, a, ats[half], lanes].astype(jnp.float32)
                    rest = (table[a][b][...] * q[b] + table[a][c][...] * q[c]) + kick
                    updated.append((table[a][a][...] - springs[piece]) * q[a] + rest)
            return tuple(updated)

        def advance_group(group, state):
            if group < early:

                @pl.when(block > 0)
                def _():
                    read_noise(block, group).wait()

            else:
                read_noise(block, group).wait()
            for step in range(span):
                state = substep(group * span + step, state)
            return state

        @pl.when(block > 0)
        def _():
            read(block).wait()

        state = tuple(conform[a, ats[half], lanes] * scale for half, lanes in pieces for a in range(3))
        for group in range(groups):
            state = advance_group(group, state)
        inverse = inverses(state, 1.0)
        for half, at in enumerate(ats):
            sums = [None] * 6
            for piece, (other, lanes) in enumerate(pieces):
                if other != half:
                    continue
                q = state[3 * piece : 3 * piece + 3]
                for a in range(3):
                    next_ref[a, at, lanes] = q[a] * noise_weight
                for k, (a, b) in enumerate(stress_pairs):
                    term = (inverse[piece] * q[a]) * q[b]
                    sums[k] = term if sums[k] is None else sums[k] + term
            for k in range(6):
                sums_ref[k, at, :] = sums[k]
        return carry

    lax.fori_loop(0, blocks, advance_block, 0)
    lane = lanes_of((slots, 128))
    rank = lax.broadcasted_iota(jnp.int32, (slots, 128), 0) & (capacity - 1)
    packed = jnp.zeros((slots, 128), jnp.float32)
    weight = extent * noise_weight * noise_weight / dumbbells
    for k, (a, b) in enumerate(stress_pairs):
        mean = jnp.sum(sums_ref[k], axis=1, keepdims=True) * weight
        packed = jnp.where(lane == 8 * rank + k, polymer_weight * (mean - (1.0 if a == b else 0.0)), packed)
    for owner in range(owners):
        chunk_ref[owner, polymer_row : polymer_row + 1, :] = jnp.sum(
            packed[owner * capacity : (owner + 1) * capacity], axis=0, keepdims=True
        )


def advance(conformations, increments, chunks, first_conform, first_noise, capacity):
    slots, dumbbells = conformations.shape[1:]
    steps = increments.shape[0]
    owners = slots // capacity
    rows, parts, groups = block_slots, 4, 4
    blocks = slots // rows
    whole = pl.BlockSpec(memory_space=pltpu.HBM)
    return pl.pallas_call(
        functools.partial(micro_kernel, capacity, parts, rows, groups),
        out_shape=(
            pltpu.VMEM(conformations.shape, jnp.float32),
            jax.ShapeDtypeStruct((owners, back_rows, 128), jnp.float32),
        ),
        in_specs=[whole, whole, VMEM, VMEM, VMEM],
        out_specs=(VMEM, VMEM),
        scratch_shapes=[
            pltpu.VMEM(conformations.shape, jnp.float32),
            pltpu.VMEM(increments.shape, jnp.bfloat16),
            pltpu.VMEM((slots, 128), jnp.float32),
            pltpu.VMEM((9, slots, dumbbells // parts), jnp.float32),
            pltpu.VMEM((6, slots, dumbbells // parts), jnp.float32),
            pltpu.SemaphoreType.DMA((blocks,)),
            pltpu.SemaphoreType.DMA((blocks, groups)),
        ],
        compiler_params=limit(12),
        cost_estimate=pl.CostEstimate(flops=20000000, bytes_accessed=5000000, transcendentals=600000),
        name="advance",
    )(far(conformations), far(increments), chunks, first_conform, first_noise)


def lines_kernel(
    macro_count, chunk_ref, received_ref, first_ref, second_ref, out_ref, y_low_ref, y_high_ref, handed_ref
):
    out_ref[...] = chunk_ref[...]
    macro, core = place_of()
    for side in range(2):
        beside = neighbour(macro, side, macro_count)
        handed_ref[side, 0:chunk_rows, :] = received_ref[2 * beside + 1 - core]
        for number, a in enumerate((0, 2)):
            handed_ref[side, chunk_rows + number * 8 : chunk_rows + (number + 1) * 8, :] = received_ref[
                2 * beside + core, a * 8 : (a + 1) * 8, :
            ]
    even = lax.axis_index("tile") & 1 == 0
    y_low_ref[...] = jnp.where(even, second_ref[...], first_ref[...])
    y_high_ref[...] = jnp.where(even, first_ref[...], second_ref[...])
    sides = (y_low_ref, y_high_ref)
    size_x, size_z = y_low_ref.shape[1:]
    for side in range(2):
        beside = neighbour(macro, side, macro_count)
        x = 0 if side == 0 else size_x - 1
        for u in range(2):
            for a in range(2):
                at = 2 * u + a
                out_ref[2 * beside + core, at : at + 1, :] = sides[u][a, x : x + 1, :]

    lane = lanes_of((8, size_z))
    source = jnp.where(core == 0, size_z - 1, 0)
    other = 2 * macro + 1 - core
    total = chunk_ref[other]
    for i in range(size_x // 8):
        for u in range(2):
            for a in range(2):
                at = line_lane + 4 * i + 2 * u + a
                total = jnp.where(
                    lane == at, rolled(sides[u][1 + a, 8 * i : 8 * i + 8, :], at - source), total
                )
    out_ref[other] = total


def add_lines(chunks, received, first, second):
    face = jax.ShapeDtypeStruct(first.shape, jnp.float32)
    return pl.pallas_call(
        functools.partial(lines_kernel, chunks.shape[0] // 2),
        out_shape=(
            jax.ShapeDtypeStruct(chunks.shape, jnp.float32), face, face,
            jax.ShapeDtypeStruct((2, handed_rows, 128), jnp.float32),
        ),
        in_specs=[VMEM] * 4,
        out_specs=(VMEM,) * 4,
        compiler_params=limit(4),
        cost_estimate=pl.CostEstimate(flops=20000, bytes_accessed=400000, transcendentals=0),
        name="add_lines",
    )(chunks, received, first, second)


product_depth = 128


def one_hots(size_y, size_z, cell_ref, position_ref, lines_ref, pick_ref, spread_ref, rows):
    flags = cell_ref.shape[0]
    weight = 0.5 * macro_step
    row_count = spread_ref.shape[0]
    returned = pick_ref.shape[1] // 4
    lane = lanes_of((1, size_z))
    row_lane = lanes_of((1, rows.shape[1]))
    slot_lane = lanes_of((flags, returned))
    flag_row = lax.broadcasted_iota(jnp.int32, (flags, returned), 0)
    rows[3 * flags :, :] = jnp.zeros((product_depth - 3 * flags, rows.shape[1]), jnp.float32)
    slot = jnp.zeros((flags, returned), jnp.int32)
    group = lax.shift_right_logical(lane, 3)
    for j in range(flags):
        cell = cell_ref[j]
        row = lax.div(cell, size_z)
        z = cell - row * size_z
        lines_ref[0, j : j + 1, :] = jnp.where(lane == z, weight, 0.0)
        lines_ref[1, j : j + 1, :] = jnp.where(
            lane == z - 1, weight, jnp.where(lane == z + 1, -weight, 0.0)
        )
        for number, shift in enumerate((size_y, 1)):
            rows[number * flags + j : number * flags + j + 1, :] = jnp.where(
                row_lane == row - shift, 1.0, jnp.where(row_lane == row + shift, -1.0, 0.0)
            )
        rows[2 * flags + j : 2 * flags + j + 1, :] = jnp.where(row_lane == row, 1.0, 0.0)
        owner = lax.div(position_ref[j], slot_rows)
        rank = position_ref[j] - owner * slot_rows
        lines_ref[2, j : j + 1, :] = jnp.where(group == rank, 1.0, 0.0)
        slot = jnp.where(flag_row == j, owner * back_rows + polymer_row, slot)
    spread = rows[...].T[:row_count].astype(jnp.bfloat16)
    pick = jnp.where(slot_lane == slot, 1.0, 0.0).astype(jnp.bfloat16)
    for piece in range(3):
        spread_ref[:, piece * product_depth : (piece + 1) * product_depth] = spread
        pick_ref[:, piece * returned : (piece + 1) * returned] = pick
    pick_ref[:, 3 * returned :] = jnp.zeros((flags, returned), jnp.bfloat16)


def flow_kernel(
    size_x, size_y, size_z, macro_count, cell_ref, position_ref, velocity_ref, viscosity_ref, chunk_ref,
    y_low_ref, y_high_ref, handed_ref, out_ref, corner_ref, edge_ref, lines_ref, pick_ref, spread_ref,
    padded, stress_x, stress_rest, faces, ghost_y, ghost_z, rows, halves,
):
    macro, core = place_of()
    one_hots(size_y, size_z, cell_ref, position_ref, lines_ref, pick_ref, spread_ref, rows)
    inside = (macro > 0, macro < macro_count - 1)
    sign_z = jnp.where(core == 0, 1.0, -1.0)
    end = jnp.where(core == 0, size_z - 1, 0)
    shape = (size_y, size_z)
    lane, row = lanes_of(shape), lax.broadcasted_iota(jnp.int32, shape, 0)
    at_end = jnp.where(lane == end, sign_z, 0.0)

    def kept(value, condition):
        return jnp.where(condition, value, 0.0)

    def plane(x):
        return pl.ds(pl.multiple_of(x * size_y, 8), size_y)

    def difference_z(value):
        lane = lanes_of(value.shape)
        return jnp.where(lane == size_z - 1, 0.0, rolled(value, -1)) - jnp.where(
            lane == 0, 0.0, rolled(value, 1)
        )

    def difference_rows(value, low=0.0, high=0.0):
        count = value.shape[0]
        row = lax.broadcasted_iota(jnp.int32, value.shape, 0)
        return jnp.where(row == count - 1, high, pltpu.roll(value, count - 1, 0)) - jnp.where(
            row == 0, low, pltpu.roll(value, 1, 0)
        )

    x_faces, x_others = [], []
    half = size_y // 2
    for s in range(2):
        beside = neighbour(macro, s, macro_count)
        outer = chunk_ref[2 * beside + core]
        items = [outer[i * size_y : (i + 1) * size_y] for i in range(3)]
        items += [handed_ref[s, i * size_y : (i + 1) * size_y, :] for i in range(3)]
        halves[s, 0:half, :] = chunk_ref[2 * beside + core, 3 * size_y : 3 * size_y + half, :]
        halves[s, half:, :] = handed_ref[s, 3 * size_y : 3 * size_y + half, :]
        items.append(halves[s])
        x_faces.append([kept(item, inside[s]) for item in items])
        corners = [handed_ref[s, chunk_rows + i * size_y : chunk_rows + (i + 1) * size_y, :] for i in range(2)]
        x_others.append([kept(rolled(corner, 2 * end + 1), inside[s]) for corner in corners])

    group = size_z // 8
    packed = [
        chunk_ref[2 * macro + 1 - core, i * size_y : (i + 1) * size_y, :]
        for i in range(-(-size_x // group))
    ]
    for i, value in enumerate(packed):

        def unpack(x, carry):
            for q in range(item_count):
                a, layer = (q, 0) if q < 4 else (q - 4, 1)
                at = 8 * (x - i * group) + 2 * a + (core if layer == 0 else 1 - core)
                faces[q, x + 1] = rolled(value, end - at)
            return carry

        lax.fori_loop(i * group, min(size_x, (i + 1) * group), unpack, 0, unroll=8)
    faces[2, 0] = x_others[0][1]
    faces[2, size_x + 1] = x_others[1][1]

    for a in range(3):
        padded[a, 0] = x_faces[0][a]
        padded[a, size_x + 1] = x_faces[1][a]

    def fill(x, carry):
        for a in range(3):
            padded[a, x + 1] = velocity_ref[a, plane(x), :]
        return carry

    lax.fori_loop(0, size_x, fill, 0, unroll=True)

    rest = {(1, 1): 0, (2, 2): 1, (1, 2): 2}

    def stress_plane(x, carry):
        along_x, along_y, along_z, centre = [], [], [], []
        for a in range(3):
            value = padded[a, x + 1]
            centre.append(value)
            along_x.append(padded[a, x + 2] - padded[a, x])
            along_y.append(
                difference_rows(value, y_low_ref[a, pl.ds(x, 1), :], y_high_ref[a, pl.ds(x, 1), :])
            )
            along_z.append(difference_z(value) + faces[a, x + 1] * at_end)
        slopes = (along_x, along_y, along_z)
        half = 0.5 * viscosity_ref[plane(x), :]
        for a, b in stress_pairs:
            value = half * (slopes[b][a] + slopes[a][b])
            if a == 0:
                stress_x[b, x + 1] = value
            else:
                stress_rest[rest[a, b], x] = value
        weight = (0.5 * faces[3, x + 1]) * at_end
        normal = [(faces[4 + a, x + 1] - centre[a]) * sign_z for a in range(3)]
        ghost_z[0, x] = weight * (normal[0] + (faces[2, x + 2] - faces[2, x]))
        ghost_z[1, x] = weight * (normal[1] + difference_rows(faces[2, x + 1]))
        ghost_z[2, x] = weight * (2.0 * normal[2])
        return carry

    lax.fori_loop(0, size_x, stress_plane, 0, unroll=6)

    for s in range(2):
        near, far, weight = x_faces[s][0:3], x_faces[s][3:6], 0.5 * x_faces[s][6]
        sign = -1.0 if s == 0 else 1.0
        normal = [(far[a] - padded[a, 1 if s == 0 else size_x]) * sign for a in range(3)]
        slope_y = difference_rows(near[0])
        slope_z = difference_z(near[0]) + x_others[s][0] * at_end
        at = 0 if s == 0 else size_x + 1
        stress_x[0, at] = weight * (2.0 * normal[0])
        stress_x[1, at] = weight * (normal[1] + slope_y)
        stress_x[2, at] = weight * (normal[2] + slope_z)
        for u in range(2):
            y, sign_y = (0, -1.0) if u == 0 else (size_y - 1, 1.0)
            number = 4 * s + 2 * u
            corner_ref[number : number + 1, :] = (0.5 * macro_step * sign * sign_y) * weight[y : y + 1, :]

    for u, ref in enumerate((y_low_ref, y_high_ref)):
        y, sign = (0, -1.0) if u == 0 else (size_y - 1, 1.0)
        weight = 0.5 * ref[6]
        normal = [
            (ref[3 + a] - velocity_ref[a, pl.ds(y, size_x, stride=size_y), :]) * sign for a in range(3)
        ]
        ghost_y[3 * u] = weight * (normal[0] + difference_rows(ref[1]))
        ghost_y[3 * u + 1] = weight * (2.0 * normal[1])
        ghost_y[3 * u + 2] = weight * (normal[2] + difference_z(ref[1]))
        for s in range(2):
            x, sign_x = (0, -1.0) if s == 0 else (size_x - 1, 1.0)
            number = 4 * s + 2 * u + 1
            corner_ref[number : number + 1, :] = (0.5 * macro_step * sign * sign_x) * weight[x : x + 1, :]
        wide = lanes_of((size_x, size_z))
        scale = jnp.where(wide == end, (0.5 * macro_step * sign) * sign_z, 0.0)
        edge_ref[2 * u] = scale * weight
        for x in range(size_x):
            edge_ref[2 * u + 1, x : x + 1, :] = scale[x : x + 1, :] * (0.5 * faces[3, x + 1, y : y + 1, :])

    columns = {(0, 1): (stress_x, 1, 1), (1, 1): (stress_rest, 0, 0), (2, 1): (stress_rest, 2, 0)}
    columns_z = {0: (stress_x, 2, 1), 1: (stress_rest, 2, 0), 2: (stress_rest, 1, 0)}

    def step_plane(x, carry):
        for a in range(3):
            total = stress_x[a, x + 2] - stress_x[a, x]
            ref, number, shift = columns[a, 1]
            total = total + difference_rows(
                ref[number, x + shift], ghost_y[a, pl.ds(x, 1), :], ghost_y[3 + a, pl.ds(x, 1), :]
            )
            ref, number, shift = columns_z[a]
            total = total + (difference_z(ref[number, x + shift]) + ghost_z[a, x])
            out_ref[a, plane(x), :] = padded[a, x + 1] + (0.5 * macro_step) * total
        return carry

    lax.fori_loop(0, size_x, step_plane, 0, unroll=6)


def flow_step(flag_cell, position, velocity, viscosity, chunks, y_low, y_high, handed):
    size_x, size_y, size_z = viscosity.shape
    flags = flag_cell.shape[0]
    returned = chunks.shape[0] * back_rows
    row_count = size_x * size_y
    planes = (size_x, size_y, size_z)
    wide = (size_x + 2, size_y, size_z)
    return pl.pallas_call(
        functools.partial(flow_kernel, size_x, size_y, size_z, chunks.shape[0] // 2),
        out_shape=(
            jax.ShapeDtypeStruct((3, size_x * size_y, size_z), jnp.float32),
            jax.ShapeDtypeStruct((8, size_z), jnp.float32),
            jax.ShapeDtypeStruct((4, size_x, size_z), jnp.float32),
            jax.ShapeDtypeStruct((3, flags, size_z), jnp.float32),
            jax.ShapeDtypeStruct((flags, 4 * returned), jnp.bfloat16),
            jax.ShapeDtypeStruct((row_count, 3 * product_depth), jnp.bfloat16),
        ),
        in_specs=[SMEM] * 2 + [VMEM] * 6,
        out_specs=(VMEM,) * 6,
        scratch_shapes=[
            pltpu.VMEM((3, *wide), jnp.float32),
            pltpu.VMEM((3, *wide), jnp.float32),
            pltpu.VMEM((3, *planes), jnp.float32),
            pltpu.VMEM((item_count, *wide), jnp.float32),
            pltpu.VMEM((6, size_x, size_z), jnp.float32),
            pltpu.VMEM((3, *planes), jnp.float32),
            pltpu.VMEM((product_depth, -(-row_count // 128) * 128), jnp.float32),
            pltpu.VMEM((2, size_y, size_z), jnp.float32),
        ],
        compiler_params=limit(12),
        cost_estimate=pl.CostEstimate(flops=4000000, bytes_accessed=3000000, transcendentals=0),
        name="flow_step",
    )(
        flag_cell, position,
        velocity.reshape(3, size_x * size_y, size_z),
        viscosity.reshape(size_x * size_y, size_z),
        chunks, y_low, y_high, handed,
    )


def pieces(value):
    high = value.astype(jnp.bfloat16)
    rest = value - high.astype(jnp.float32)
    middle = rest.astype(jnp.bfloat16)
    return high, middle, (rest - middle.astype(jnp.float32)).astype(jnp.bfloat16)


def polymer_kernel(
    size_x, size_y, size_z, macro_count, chunk_ref, viscous_ref, corner_ref, edge_ref, lines_ref, pick_ref,
    spread_ref, partial_ref, out_ref, flag_ref, field, write_sem,
):
    flags = viscous_ref.shape[0]
    macro, core = place_of()
    chunks = chunk_ref[...]
    split = jnp.concatenate((*pieces(chunks), jnp.zeros(chunks.shape, jnp.bfloat16)), axis=0)
    values = jnp.dot(pick_ref[...], split, preferred_element_type=jnp.float32) * lines_ref[2]
    here, beside_z = lines_ref[0], lines_ref[1]
    lane = lanes_of((flags, 128))
    columns = [
        jnp.broadcast_to(
            jnp.sum(jnp.where((lane & 7) == k, values, 0.0), axis=1, keepdims=True), (flags, size_z)
        )
        for k in range(6)
    ]
    stress = viscous_ref[...]
    for k in range(6):
        stress = jnp.where(lane == k, stress + columns[k], stress)
    unused = jnp.zeros((product_depth - 3 * flags, size_z), jnp.float32)
    split = [
        pieces(
            jnp.concatenate(
                [
                    columns[pair_index(a, 0)] * here, columns[pair_index(a, 1)] * here,
                    columns[pair_index(a, 2)] * beside_z, unused,
                ],
                axis=0,
            )
        )
        for a in range(3)
    ]
    flag_ref[...] = stress.T[0:6, :]

    field[...] = partial_ref[...]
    for s in range(2):
        inside = macro > 0 if s == 0 else macro < macro_count - 1
        beside = jnp.maximum(macro - 1, 0) if s == 0 else jnp.minimum(macro + 1, macro_count - 1)
        start = (2 * beside + core) * back_rows
        x = 0 if s == 0 else size_x - 1
        for u in range(2):
            at = x * size_y + (0 if u == 0 else size_y - 1)
            for a in range(2):
                number = 4 * s + 2 * u + a
                line = corner_ref[number : number + 1, :] * chunk_ref[pl.ds(start + 2 * u + a, 1), :]
                field[1 - a, at : at + 1, :] += jnp.where(inside, line, 0.0)
    start = pl.multiple_of((2 * macro + 1 - core) * back_rows, 8)
    packed = chunk_ref[pl.ds(start, back_rows), :]
    end = jnp.where(core == 0, size_z - 1, 0)
    for u in range(2):
        y = 0 if u == 0 else size_y - 1
        for a in range(2):
            for i in range(size_x // 8):
                line = rolled(packed, end - (line_lane + 4 * i + 2 * u + a)) * edge_ref[2 * u + a, 8 * i : 8 * i + 8, :]
                at = pl.ds(8 * i * size_y + y, 8, stride=size_y)
                field[2 - a, at, :] += line
    copies = [pltpu.make_async_copy(field.at[a], out_ref.at[a], write_sem.at[a]) for a in range(3)]
    for a in range(3):
        field[a] += jnp.dot(
            spread_ref[...], jnp.concatenate(split[a], axis=0), preferred_element_type=jnp.float32
        )
        copies[a].start()
    for copy in copies:
        copy.wait()


def add_polymer(chunks, viscous, corners, edges, lines, pick, spread, partial, shape):
    flags = viscous.shape[0]
    size_x, size_y, size_z = shape
    return pl.pallas_call(
        functools.partial(polymer_kernel, size_x, size_y, size_z, chunks.shape[0] // 2),
        out_shape=(
            jax.ShapeDtypeStruct(partial.shape, jnp.float32),
            jax.ShapeDtypeStruct((6, flags), jnp.float32),
        ),
        in_specs=[VMEM] * 8,
        out_specs=(pl.BlockSpec(memory_space=pltpu.HBM), VMEM),
        scratch_shapes=[pltpu.VMEM(partial.shape, jnp.float32), pltpu.SemaphoreType.DMA((3,))],
        compiler_params=limit(8),
        cost_estimate=pl.CostEstimate(flops=400000, bytes_accessed=3000000, transcendentals=0),
        name="add_polymer",
    )(chunks.reshape(-1, 128), viscous, corners, edges, lines, pick, spread, partial)


def shards(velocity, viscosity, flag_cell, flag_owner, conformations, increments):
    macro_count = lax.axis_size("macro")
    tile_count = lax.axis_size("tile")
    assert lax.axis_size("micro") == 2
    owner_count = 2 * macro_count
    capacity = conformations.shape[1] // owner_count
    size_x, size_y, size_z = viscosity.shape
    assert capacity <= slot_rows and capacity % 2 == 0 and size_y == 8 and size_z == 128 and size_x % 8 == 0 and size_x <= 48
    chunks, position, viscous, first, second, first_conform, first_noise = gather_rows(
        flag_cell, flag_owner.reshape(-1), velocity, viscosity, conformations, increments, capacity, owner_count
    )

    def exchange(rows):
        return lax.all_to_all(rows, ("macro", "micro"), split_axis=0, concat_axis=0, tiled=True)

    received = exchange(chunks.reshape(owner_count, -1, 128))
    swaps = []
    for start in range(2):
        pairs = [(i, i + 1) for i in range(start, tile_count - 1, 2)]
        swaps.append(pairs + [(high, low) for low, high in pairs])
    first = lax.ppermute(first, "tile", swaps[0])
    second = lax.ppermute(second, "tile", swaps[1])
    last_state, polymer = advance(
        conformations, increments, received, first_conform, first_noise, capacity
    )
    polymer, y_low, y_high, handed = add_lines(polymer, received, first, second)
    returned = exchange(polymer)
    handed = lax.ppermute(handed, "micro", [(0, 1), (1, 0)])
    partial, corners, edges, lines, pick, spread = flow_step(
        flag_cell, position, velocity, viscosity, received, y_low, y_high, handed
    )
    velocity_next, flag_stress = add_polymer(
        returned, viscous, corners, edges, lines, pick, spread, partial, viscosity.shape
    )
    return (velocity_next.reshape(velocity.shape), last_state, flag_stress)


def solution(mesh):
    in_specs = (
        P(None, "macro", "tile", "micro"),
        P("macro", "tile", "micro"),
        P(("macro", "tile", "micro")),
        P(("macro", "tile", "micro"), None),
        P(None, ("macro", "tile", "micro"), None),
        P(None, None, ("macro", "tile", "micro"), None),
    )
    out_specs = (
        P(None, "macro", "tile", "micro"),
        P(None, ("macro", "tile", "micro"), None),
        P(None, ("macro", "tile", "micro")),
    )
    return jax.shard_map(shards, mesh=mesh, in_specs=in_specs, out_specs=out_specs, check_vma=False)
```

```python
import functools

import jax
import jax.numpy as jnp
from jax import lax
from jax.experimental import pallas as pl
from jax.experimental.pallas import tpu as pltpu
from jax.sharding import PartitionSpec as P

stress_pairs = ((0, 0), (1, 1), (2, 2), (0, 1), (0, 2), (1, 2))
macro_step = 0.1
micro_step = 0.01
noise_weight = 0.1
relax_rate = 0.5
fene_extent = 30.0
spring_floor = 0.1
polymer_weight = 0.25

SMEM = pl.BlockSpec(memory_space=pltpu.SMEM)
VMEM = pl.BlockSpec(memory_space=pltpu.VMEM)


def pair_index(left_axis, right_axis):
    return stress_pairs.index((min(left_axis, right_axis), max(left_axis, right_axis)))


def lanes_of(shape):
    return lax.broadcasted_iota(jnp.int32, shape, len(shape) - 1)


slot_rows = 8
chunk_rows = 32
half_face = 28
handed_rows = 48
item_count = 7
back_rows = 8
polymer_row = 4
line_lane = 64


block_slots = 32
first_share = 2


def limit(mebibytes):
    return pltpu.CompilerParams(vmem_limit_bytes=mebibytes * 1024 * 1024)


def far(value):
    return pltpu.with_memory_space_constraint(value, pltpu.HBM)


def place_of():
    return lax.axis_index("macro"), lax.axis_index("micro")


def neighbour(index, side, count):
    return jnp.maximum(index - 1, 0) if side == 0 else jnp.minimum(index + 1, count - 1)


def rolled(value, amount):
    size = value.shape[-1]
    if isinstance(amount, int):
        return pltpu.roll(value, amount % size, value.ndim - 1)
    return pltpu.roll(value, lax.rem(amount + 2 * size, size), value.ndim - 1)


def gather_kernel(
    capacity, size_x, size_y, size_z, macro_count, cell_in, owner_in, velocity_in, viscosity_in,
    conform_in, noise_in, chunk_out, position_ref, viscous_ref, first_ref, second_ref, conform_ref, noise_ref,
    cell_ref, owner_ref, velocity_ref, viscosity_ref, masked, gradients, paired, chunk_ref, target, count, sems, write_sem,
):
    flags = cell_ref.shape[0]
    copies = [
        pltpu.make_async_copy(source, into, sems.at[number])
        for number, (source, into) in enumerate(
            (
                (cell_in, cell_ref), (owner_in, owner_ref), (velocity_in, velocity_ref),
                (viscosity_in, viscosity_ref), (conform_in.at[:, 0:block_slots, :], conform_ref),
                (noise_in.at[0 : noise_ref.shape[0], :, 0:block_slots, :], noise_ref),
            )
        )
    ]
    for copy in copies:
        copy.start()
    paired_rows = paired.shape[0] // 2
    macro, core = place_of()
    lane = lanes_of((1, size_z))

    for owner in range(count.shape[0]):
        count[owner] = 0
    paired[...] = jnp.zeros_like(paired)
    for copy in copies[:2]:
        copy.wait()
    for j in range(flags):
        owner = owner_ref[j]
        rank = count[owner]
        count[owner] = rank + 1
        target[j] = (rank & 1) * paired_rows + owner * (slot_rows // 2) + lax.shift_right_logical(rank, 1)
        position_ref[j] = owner * slot_rows + rank
    for copy in copies[2:4]:
        copy.wait()
    planes = velocity_ref.reshape(3, size_x, size_y, size_z)
    layers = viscosity_ref.reshape(size_x, size_y, size_z)
    for j in range(flags):
        cell = cell_ref[j]
        x = lax.shift_right_logical(cell, 10)
        y = lax.shift_right_logical(cell, 7) & (size_y - 1)
        z = cell & (size_z - 1)
        here = (lane == z).astype(jnp.float32)
        along_z = (lane == z + 1).astype(jnp.float32) - (lane == z - 1).astype(jnp.float32)
        at = pl.ds(y, 1)
        for a in range(3):
            along_x = planes[a, x + 1, at, :] - planes[a, x - 1, at, :]
            along_y = planes[a, x, pl.ds(y + 1, 1), :] - planes[a, x, pl.ds(y - 1, 1), :]
            masked[3 * a, j : j + 1, :] = along_x * here
            masked[3 * a + 1, j : j + 1, :] = along_y * here
            masked[3 * a + 2, j : j + 1, :] = planes[a, x, at, :] * along_z
        masked[9, j : j + 1, :] = layers[x, at, :] * here

    for side in range(2):
        beside = neighbour(macro, side, macro_count)
        for layer, owner in enumerate((2 * beside + core, 2 * beside + 1 - core)):
            start = pl.multiple_of(owner * chunk_rows, 8)
            x = layer if side == 0 else size_x - 1 - layer
            for a in range(3):
                chunk_ref[pl.ds(start + a * size_y, size_y), :] = velocity_ref[a, x * size_y : (x + 1) * size_y, :]
            x = 0 if side == 0 else size_x - 1
            half = x * size_y + layer * (size_y // 2)
            chunk_ref[pl.ds(start + 3 * size_y, size_y // 2), :] = viscosity_ref[half : half + size_y // 2, :]

    group = size_z // 8
    lane2 = lanes_of((size_y, size_z))
    first = pl.multiple_of((2 * macro + 1 - core) * chunk_rows, 8)
    source = jnp.where(core == 0, size_z - 2, 0)
    for block in range(-(-size_x // group)):
        total = jnp.zeros((size_y, size_z), jnp.float32)
        for x in range(block * group, min(size_x, (block + 1) * group)):
            rows = slice(x * size_y, (x + 1) * size_y)
            for a in range(4):
                at = 8 * (x - block * group) + 2 * a
                value = viscosity_ref[rows, :] if a == 3 else velocity_ref[a, rows, :]
                total = jnp.where((lane2 == at) | (lane2 == at + 1), rolled(value, at - source), total)
        chunk_ref[pl.ds(first + block * size_y, size_y), :] = total

    columns = [0.5 * jnp.sum(masked[c], axis=1, keepdims=True) for c in range(9)]
    viscous = jnp.sum(masked[9], axis=1, keepdims=True)
    wide = lanes_of((flags, 128))
    packed = jnp.zeros((flags, 128), jnp.float32)
    for c in range(9):
        packed = jnp.where(wide == c, columns[c], packed)
    gradients[...] = packed
    for j in range(flags):
        paired[pl.ds(target[j], 1), :] = gradients[j : j + 1, :]
    rows = paired[0:paired_rows, :] + rolled(paired[paired_rows:, :], 64)
    for owner in range(count.shape[0]):
        chunk_ref[owner * chunk_rows + half_face : (owner + 1) * chunk_rows, :] = rows[
            owner * (slot_rows // 2) : (owner + 1) * (slot_rows // 2)
        ]
    write = pltpu.make_async_copy(chunk_ref, chunk_out, write_sem)
    write.start()

    stress = jnp.zeros((flags, 128), jnp.float32)
    for k, (a, b) in enumerate(stress_pairs):
        stress = jnp.where(wide == k, viscous * (columns[3 * a + b] + columns[3 * b + a]), stress)
    viscous_ref[...] = stress

    even = lax.axis_index("tile") & 1 == 0

    def put(number, ref, low, high):
        rows = [ref[pl.ds(y, size_x, stride=size_y), :] for y in (low, high)]
        first_ref[number] = jnp.where(even, rows[1], rows[0])
        second_ref[number] = jnp.where(even, rows[0], rows[1])

    for layer in range(2):
        for a in range(3):
            put(3 * layer + a, velocity_ref.at[a], layer, size_y - 1 - layer)
    put(6, viscosity_ref, 0, size_y - 1)

    for copy in copies[4:]:
        copy.wait()
    write.wait()


def gather_rows(flag_cell, owner, velocity, viscosity, conformations, increments, capacity, owner_count):
    size_x, size_y, size_z = viscosity.shape
    flags = flag_cell.shape[0]
    face = jax.ShapeDtypeStruct((item_count, size_x, size_z), jnp.float32)
    steps, _, _, dumbbells = increments.shape
    return pl.pallas_call(
        functools.partial(gather_kernel, capacity, size_x, size_y, size_z, owner_count // 2),
        out_shape=(
            jax.ShapeDtypeStruct((owner_count * chunk_rows, 128), jnp.float32),
            jax.ShapeDtypeStruct((flags,), jnp.int32),
            jax.ShapeDtypeStruct((flags, 128), jnp.float32),
            face,
            face,
            pltpu.VMEM((3, block_slots, dumbbells), jnp.float32),
            pltpu.VMEM((steps // first_share, 3, block_slots, dumbbells), jnp.bfloat16),
        ),
        in_specs=[pl.BlockSpec(memory_space=pltpu.HBM)] * 6,
        out_specs=(pl.BlockSpec(memory_space=pltpu.HBM), SMEM) + (VMEM,) * 5,
        scratch_shapes=[
            pltpu.SMEM((flags,), jnp.int32),
            pltpu.SMEM((flags,), jnp.int32),
            pltpu.VMEM((3, size_x * size_y, size_z), jnp.float32),
            pltpu.VMEM((size_x * size_y, size_z), jnp.float32),
            pltpu.VMEM((10, flags, size_z), jnp.float32),
            pltpu.VMEM((flags, 128), jnp.float32),
            pltpu.VMEM((owner_count * slot_rows, 128), jnp.float32),
            pltpu.VMEM((owner_count * chunk_rows, 128), jnp.float32),
            pltpu.SMEM((flags,), jnp.int32),
            pltpu.SMEM((owner_count,), jnp.int32),
            pltpu.SemaphoreType.DMA((6,)),
            pltpu.SemaphoreType.DMA,
        ],
        compiler_params=limit(8),
        cost_estimate=pl.CostEstimate(flops=400000, bytes_accessed=3000000, transcendentals=0),
        name="gather_rows",
    )(
        far(flag_cell),
        far(owner),
        far(velocity.reshape(3, size_x * size_y, size_z)),
        far(viscosity.reshape(size_x * size_y, size_z)),
        far(conformations),
        far(increments),
    )


def micro_kernel(
    capacity, parts, rows, groups, conform_ref, noise_ref, rate_ref, first_conform_ref, first_noise_ref,
    next_ref, chunk_ref, conform, noise, rate, rate_wide, sums_ref, read_sem, noise_sem,
):
    steps, _, slots, dumbbells = noise_ref.shape
    blocks = slots // rows
    span = steps // groups
    width = dumbbells // parts
    owners = slots // capacity
    scale = 1.0 / noise_weight
    extent = fene_extent * scale * scale

    def block_rows(block):
        return pl.ds(pl.multiple_of(block * rows, rows), rows)

    def read(block):
        at = block_rows(block)
        return pltpu.make_async_copy(conform_ref.at[:, at, :], conform.at[:, at, :], read_sem.at[block])

    def read_noise(block, group):
        at, when = block_rows(block), pl.ds(group * span, span)
        return pltpu.make_async_copy(
            noise_ref.at[when, :, at, :], noise.at[when, :, at, :], noise_sem.at[block, group]
        )

    pieces = [
        (half, slice(part * width, (part + 1) * width)) for half in range(rows // 16) for part in range(parts)
    ]
    assert len(pieces) == 8
    early = groups // first_share
    for block in range(blocks):
        if block > 0:
            read(block).start()
        for group in range(early if block == 0 else 0, groups):
            read_noise(block, group).start()
    conform[:, 0:rows, :] = first_conform_ref[...]
    for step in range(steps // first_share):
        noise[step, :, 0:rows, :] = first_noise_ref[step]
    for owner in range(owners):
        packed = rate_ref[owner, half_face : half_face + capacity // 2, :]
        rate[pl.ds(owner * capacity, capacity // 2, stride=2), :] = packed
        rate[pl.ds(owner * capacity + 1, capacity // 2, stride=2), :] = rolled(packed, 64)
        chunk_ref[owner] = jnp.zeros(chunk_ref.shape[1:], jnp.float32)
    for a in range(3):
        for b in range(3):
            column = micro_step * rate[:, 3 * a + b : 3 * a + b + 1] + (1.0 if a == b else 0.0)
            rate_wide[3 * a + b] = jnp.broadcast_to(column, (slots, width))

    def inverses(state, scale):
        rooms = []
        for piece in range(len(pieces)):
            q = state[3 * piece : 3 * piece + 3]
            room = (extent - q[0] * q[0]) - (q[1] * q[1] + q[2] * q[2])
            rooms.append(jnp.maximum(room, extent * spring_floor))
        levels = [rooms]
        while len(levels[-1]) > 1:
            levels.append([low * high for low, high in zip(levels[-1][0::2], levels[-1][1::2])])
        result = [scale * pl.reciprocal(levels[-1][0])]
        for level in reversed(levels[:-1]):
            result = [result[i // 2] * level[i ^ 1] for i in range(len(level))]
        return result

    def advance_block(block, carry):
        ats = [pl.ds(pl.multiple_of(block * rows + 16 * half, 16), 16) for half in range(rows // 16)]
        rates = [
            [[rate_wide.at[3 * a + b, at, :] for b in range(3)] for a in range(3)] for at in ats
        ]

        def substep(step, state):
            updated = []
            springs = inverses(state, micro_step * relax_rate * extent)
            for piece, (half, lanes) in enumerate(pieces):
                q = state[3 * piece : 3 * piece + 3]
                table = rates[half]
                for a in range(3):
                    b, c = [other for other in range(3) if other != a]
                    kick = noise[step, a, ats[half], lanes].astype(jnp.float32)
                    rest = (table[a][b][...] * q[b] + table[a][c][...] * q[c]) + kick
                    updated.append((table[a][a][...] - springs[piece]) * q[a] + rest)
            return tuple(updated)

        def advance_group(group, state):
            if group < early:

                @pl.when(block > 0)
                def _():
                    read_noise(block, group).wait()

            else:
                read_noise(block, group).wait()
            for step in range(span):
                state = substep(group * span + step, state)
            return state

        @pl.when(block > 0)
        def _():
            read(block).wait()

        state = tuple(conform[a, ats[half], lanes] * scale for half, lanes in pieces for a in range(3))
        for group in range(groups):
            state = advance_group(group, state)
        inverse = inverses(state, 1.0)
        for half, at in enumerate(ats):
            sums = [None] * 6
            for piece, (other, lanes) in enumerate(pieces):
                if other != half:
                    continue
                q = state[3 * piece : 3 * piece + 3]
                for a in range(3):
                    next_ref[a, at, lanes] = q[a] * noise_weight
                for k, (a, b) in enumerate(stress_pairs):
                    term = (inverse[piece] * q[a]) * q[b]
                    sums[k] = term if sums[k] is None else sums[k] + term
            for k in range(6):
                sums_ref[k, at, :] = sums[k]
        return carry

    lax.fori_loop(0, blocks, advance_block, 0)
    lane = lanes_of((slots, 128))
    rank = lax.broadcasted_iota(jnp.int32, (slots, 128), 0) & (capacity - 1)
    packed = jnp.zeros((slots, 128), jnp.float32)
    weight = extent * noise_weight * noise_weight / dumbbells
    for k, (a, b) in enumerate(stress_pairs):
        mean = jnp.sum(sums_ref[k], axis=1, keepdims=True) * weight
        packed = jnp.where(lane == 8 * rank + k, polymer_weight * (mean - (1.0 if a == b else 0.0)), packed)
    for owner in range(owners):
        chunk_ref[owner, polymer_row : polymer_row + 1, :] = jnp.sum(
            packed[owner * capacity : (owner + 1) * capacity], axis=0, keepdims=True
        )


def advance(conformations, increments, chunks, first_conform, first_noise, capacity):
    slots, dumbbells = conformations.shape[1:]
    steps = increments.shape[0]
    owners = slots // capacity
    rows, parts, groups = block_slots, 4, 4
    blocks = slots // rows
    whole = pl.BlockSpec(memory_space=pltpu.HBM)
    return pl.pallas_call(
        functools.partial(micro_kernel, capacity, parts, rows, groups),
        out_shape=(
            pltpu.VMEM(conformations.shape, jnp.float32),
            jax.ShapeDtypeStruct((owners, back_rows, 128), jnp.float32),
        ),
        in_specs=[whole, whole, VMEM, VMEM, VMEM],
        out_specs=(VMEM, VMEM),
        scratch_shapes=[
            pltpu.VMEM(conformations.shape, jnp.float32),
            pltpu.VMEM(increments.shape, jnp.bfloat16),
            pltpu.VMEM((slots, 128), jnp.float32),
            pltpu.VMEM((9, slots, dumbbells // parts), jnp.float32),
            pltpu.VMEM((6, slots, dumbbells // parts), jnp.float32),
            pltpu.SemaphoreType.DMA((blocks,)),
            pltpu.SemaphoreType.DMA((blocks, groups)),
        ],
        compiler_params=limit(12),
        cost_estimate=pl.CostEstimate(flops=20000000, bytes_accessed=5000000, transcendentals=600000),
        name="advance",
    )(far(conformations), far(increments), chunks, first_conform, first_noise)


def lines_kernel(
    macro_count, chunk_ref, received_ref, first_ref, second_ref, chunk_out, y_low_ref, y_high_ref, handed_ref,
    out_ref, write_sem,
):
    macro, core = place_of()
    even = lax.axis_index("tile") & 1 == 0
    size_x, size_z = first_ref.shape[1:]
    out_ref[...] = chunk_ref[...]

    def side_of(u, item, at):
        first, second = first_ref[item, at, :], second_ref[item, at, :]
        return jnp.where(even, second, first) if u == 0 else jnp.where(even, first, second)

    for side in range(2):
        beside = neighbour(macro, side, macro_count)
        x = 0 if side == 0 else size_x - 1
        for u in range(2):
            for a in range(2):
                at = 2 * u + a
                out_ref[2 * beside + core, at : at + 1, :] = side_of(u, a, slice(x, x + 1))

    lane = lanes_of((8, size_z))
    source = jnp.where(core == 0, size_z - 1, 0)
    other = 2 * macro + 1 - core
    total = chunk_ref[other]
    for i in range(size_x // 8):
        for u in range(2):
            for a in range(2):
                at = line_lane + 4 * i + 2 * u + a
                value = side_of(u, 1 + a, slice(8 * i, 8 * i + 8))
                total = jnp.where(lane == at, rolled(value, at - source), total)
    out_ref[other] = total
    write = pltpu.make_async_copy(out_ref, chunk_out, write_sem)
    write.start()

    for side in range(2):
        beside = neighbour(macro, side, macro_count)
        handed_ref[side, 0:chunk_rows, :] = received_ref[2 * beside + 1 - core]
        for number, a in enumerate((0, 2)):
            handed_ref[side, chunk_rows + number * 8 : chunk_rows + (number + 1) * 8, :] = received_ref[
                2 * beside + core, a * 8 : (a + 1) * 8, :
            ]
    y_low_ref[...] = jnp.where(even, second_ref[...], first_ref[...])
    y_high_ref[...] = jnp.where(even, first_ref[...], second_ref[...])
    write.wait()


def add_lines(chunks, received, first, second):
    face = jax.ShapeDtypeStruct(first.shape, jnp.float32)
    return pl.pallas_call(
        functools.partial(lines_kernel, chunks.shape[0] // 2),
        out_shape=(
            jax.ShapeDtypeStruct(chunks.shape, jnp.float32), face, face,
            jax.ShapeDtypeStruct((2, handed_rows, 128), jnp.float32),
        ),
        in_specs=[VMEM] * 4,
        out_specs=(pl.BlockSpec(memory_space=pltpu.HBM),) + (VMEM,) * 3,
        scratch_shapes=[pltpu.VMEM(chunks.shape, jnp.float32), pltpu.SemaphoreType.DMA],
        compiler_params=limit(4),
        cost_estimate=pl.CostEstimate(flops=20000, bytes_accessed=400000, transcendentals=0),
        name="add_lines",
    )(chunks, received, first, second)


product_depth = 128


def one_hots(size_y, size_z, cell_ref, position_ref, lines_ref, pick_ref, spread_ref, rows):
    flags = cell_ref.shape[0]
    weight = 0.5 * macro_step
    row_count = spread_ref.shape[0]
    returned = pick_ref.shape[1] // 4
    lane = lanes_of((1, size_z))
    row_lane = lanes_of((1, rows.shape[1]))
    slot_lane = lanes_of((flags, returned))
    flag_row = lax.broadcasted_iota(jnp.int32, (flags, returned), 0)
    rows[3 * flags :, :] = jnp.zeros((product_depth - 3 * flags, rows.shape[1]), jnp.float32)
    slot = jnp.zeros((flags, returned), jnp.int32)
    group = lax.shift_right_logical(lane, 3)
    for j in range(flags):
        cell = cell_ref[j]
        row = lax.div(cell, size_z)
        z = cell - row * size_z
        lines_ref[0, j : j + 1, :] = jnp.where(lane == z, weight, 0.0)
        lines_ref[1, j : j + 1, :] = jnp.where(
            lane == z - 1, weight, jnp.where(lane == z + 1, -weight, 0.0)
        )
        for number, shift in enumerate((size_y, 1)):
            rows[number * flags + j : number * flags + j + 1, :] = jnp.where(
                row_lane == row - shift, 1.0, jnp.where(row_lane == row + shift, -1.0, 0.0)
            )
        rows[2 * flags + j : 2 * flags + j + 1, :] = jnp.where(row_lane == row, 1.0, 0.0)
        owner = lax.div(position_ref[j], slot_rows)
        rank = position_ref[j] - owner * slot_rows
        lines_ref[2, j : j + 1, :] = jnp.where(group == rank, 1.0, 0.0)
        slot = jnp.where(flag_row == j, owner * back_rows + polymer_row, slot)
    spread = rows[...].T[:row_count].astype(jnp.bfloat16)
    pick = jnp.where(slot_lane == slot, 1.0, 0.0).astype(jnp.bfloat16)
    for piece in range(3):
        spread_ref[:, piece * product_depth : (piece + 1) * product_depth] = spread
        pick_ref[:, piece * returned : (piece + 1) * returned] = pick
    pick_ref[:, 3 * returned :] = jnp.zeros((flags, returned), jnp.bfloat16)


def flow_kernel(
    size_x, size_y, size_z, macro_count, cell_ref, position_ref, velocity_ref, viscosity_ref, chunk_ref,
    y_low_ref, y_high_ref, handed_ref, out_ref, corner_ref, edge_ref, lines_ref, pick_ref, spread_ref,
    padded, stress_x, stress_rest, faces, ghost_y, ghost_z, rows, halves,
):
    macro, core = place_of()
    one_hots(size_y, size_z, cell_ref, position_ref, lines_ref, pick_ref, spread_ref, rows)
    inside = (macro > 0, macro < macro_count - 1)
    sign_z = jnp.where(core == 0, 1.0, -1.0)
    end = jnp.where(core == 0, size_z - 1, 0)
    shape = (size_y, size_z)
    lane, row = lanes_of(shape), lax.broadcasted_iota(jnp.int32, shape, 0)
    at_end = jnp.where(lane == end, sign_z, 0.0)

    def kept(value, condition):
        return jnp.where(condition, value, 0.0)

    def plane(x):
        return pl.ds(pl.multiple_of(x * size_y, 8), size_y)

    def difference_z(value):
        lane = lanes_of(value.shape)
        return jnp.where(lane == size_z - 1, 0.0, rolled(value, -1)) - jnp.where(
            lane == 0, 0.0, rolled(value, 1)
        )

    def difference_rows(value, low=0.0, high=0.0):
        count = value.shape[0]
        row = lax.broadcasted_iota(jnp.int32, value.shape, 0)
        return jnp.where(row == count - 1, high, pltpu.roll(value, count - 1, 0)) - jnp.where(
            row == 0, low, pltpu.roll(value, 1, 0)
        )

    x_faces, x_others = [], []
    half = size_y // 2
    for s in range(2):
        beside = neighbour(macro, s, macro_count)
        outer = chunk_ref[2 * beside + core]
        items = [outer[i * size_y : (i + 1) * size_y] for i in range(3)]
        items += [handed_ref[s, i * size_y : (i + 1) * size_y, :] for i in range(3)]
        halves[s, 0:half, :] = chunk_ref[2 * beside + core, 3 * size_y : 3 * size_y + half, :]
        halves[s, half:, :] = handed_ref[s, 3 * size_y : 3 * size_y + half, :]
        items.append(halves[s])
        x_faces.append([kept(item, inside[s]) for item in items])
        corners = [handed_ref[s, chunk_rows + i * size_y : chunk_rows + (i + 1) * size_y, :] for i in range(2)]
        x_others.append([kept(rolled(corner, 2 * end + 1), inside[s]) for corner in corners])

    group = size_z // 8
    packed = [
        chunk_ref[2 * macro + 1 - core, i * size_y : (i + 1) * size_y, :]
        for i in range(-(-size_x // group))
    ]
    for i, value in enumerate(packed):

        def unpack(x, carry):
            for q in range(item_count):
                a, layer = (q, 0) if q < 4 else (q - 4, 1)
                at = 8 * (x - i * group) + 2 * a + (core if layer == 0 else 1 - core)
                faces[q, x + 1] = rolled(value, end - at)
            return carry

        lax.fori_loop(i * group, min(size_x, (i + 1) * group), unpack, 0, unroll=8)
    faces[2, 0] = x_others[0][1]
    faces[2, size_x + 1] = x_others[1][1]

    for a in range(3):
        padded[a, 0] = x_faces[0][a]
        padded[a, size_x + 1] = x_faces[1][a]

    def fill(x, carry):
        for a in range(3):
            padded[a, x + 1] = velocity_ref[a, plane(x), :]
        return carry

    lax.fori_loop(0, size_x, fill, 0, unroll=True)

    rest = {(1, 1): 0, (2, 2): 1, (1, 2): 2}

    def stress_plane(x, carry):
        along_x, along_y, along_z, centre = [], [], [], []
        for a in range(3):
            value = padded[a, x + 1]
            centre.append(value)
            along_x.append(padded[a, x + 2] - padded[a, x])
            along_y.append(
                difference_rows(value, y_low_ref[a, pl.ds(x, 1), :], y_high_ref[a, pl.ds(x, 1), :])
            )
            along_z.append(difference_z(value) + faces[a, x + 1] * at_end)
        slopes = (along_x, along_y, along_z)
        half = 0.5 * viscosity_ref[plane(x), :]
        for a, b in stress_pairs:
            value = half * (slopes[b][a] + slopes[a][b])
            if a == 0:
                stress_x[b, x + 1] = value
            else:
                stress_rest[rest[a, b], x] = value
        weight = (0.5 * faces[3, x + 1]) * at_end
        normal = [(faces[4 + a, x + 1] - centre[a]) * sign_z for a in range(3)]
        ghost_z[0, x] = weight * (normal[0] + (faces[2, x + 2] - faces[2, x]))
        ghost_z[1, x] = weight * (normal[1] + difference_rows(faces[2, x + 1]))
        ghost_z[2, x] = weight * (2.0 * normal[2])
        return carry

    lax.fori_loop(0, size_x, stress_plane, 0, unroll=6)

    for s in range(2):
        near, far, weight = x_faces[s][0:3], x_faces[s][3:6], 0.5 * x_faces[s][6]
        sign = -1.0 if s == 0 else 1.0
        normal = [(far[a] - padded[a, 1 if s == 0 else size_x]) * sign for a in range(3)]
        slope_y = difference_rows(near[0])
        slope_z = difference_z(near[0]) + x_others[s][0] * at_end
        at = 0 if s == 0 else size_x + 1
        stress_x[0, at] = weight * (2.0 * normal[0])
        stress_x[1, at] = weight * (normal[1] + slope_y)
        stress_x[2, at] = weight * (normal[2] + slope_z)
        for u in range(2):
            y, sign_y = (0, -1.0) if u == 0 else (size_y - 1, 1.0)
            number = 4 * s + 2 * u
            corner_ref[number : number + 1, :] = (0.5 * macro_step * sign * sign_y) * weight[y : y + 1, :]

    for u, ref in enumerate((y_low_ref, y_high_ref)):
        y, sign = (0, -1.0) if u == 0 else (size_y - 1, 1.0)
        weight = 0.5 * ref[6]
        normal = [
            (ref[3 + a] - velocity_ref[a, pl.ds(y, size_x, stride=size_y), :]) * sign for a in range(3)
        ]
        ghost_y[3 * u] = weight * (normal[0] + difference_rows(ref[1]))
        ghost_y[3 * u + 1] = weight * (2.0 * normal[1])
        ghost_y[3 * u + 2] = weight * (normal[2] + difference_z(ref[1]))
        for s in range(2):
            x, sign_x = (0, -1.0) if s == 0 else (size_x - 1, 1.0)
            number = 4 * s + 2 * u + 1
            corner_ref[number : number + 1, :] = (0.5 * macro_step * sign * sign_x) * weight[x : x + 1, :]
        wide = lanes_of((size_x, size_z))
        scale = jnp.where(wide == end, (0.5 * macro_step * sign) * sign_z, 0.0)
        edge_ref[2 * u] = scale * weight
        for x in range(size_x):
            edge_ref[2 * u + 1, x : x + 1, :] = scale[x : x + 1, :] * (0.5 * faces[3, x + 1, y : y + 1, :])

    columns = {(0, 1): (stress_x, 1, 1), (1, 1): (stress_rest, 0, 0), (2, 1): (stress_rest, 2, 0)}
    columns_z = {0: (stress_x, 2, 1), 1: (stress_rest, 2, 0), 2: (stress_rest, 1, 0)}

    def step_plane(x, carry):
        for a in range(3):
            total = stress_x[a, x + 2] - stress_x[a, x]
            ref, number, shift = columns[a, 1]
            total = total + difference_rows(
                ref[number, x + shift], ghost_y[a, pl.ds(x, 1), :], ghost_y[3 + a, pl.ds(x, 1), :]
            )
            ref, number, shift = columns_z[a]
            total = total + (difference_z(ref[number, x + shift]) + ghost_z[a, x])
            out_ref[a, plane(x), :] = padded[a, x + 1] + (0.5 * macro_step) * total
        return carry

    lax.fori_loop(0, size_x, step_plane, 0, unroll=6)


def flow_step(flag_cell, position, velocity, viscosity, chunks, y_low, y_high, handed):
    size_x, size_y, size_z = viscosity.shape
    flags = flag_cell.shape[0]
    returned = chunks.shape[0] * back_rows
    row_count = size_x * size_y
    planes = (size_x, size_y, size_z)
    wide = (size_x + 2, size_y, size_z)
    return pl.pallas_call(
        functools.partial(flow_kernel, size_x, size_y, size_z, chunks.shape[0] // 2),
        out_shape=(
            jax.ShapeDtypeStruct((3, size_x * size_y, size_z), jnp.float32),
            jax.ShapeDtypeStruct((8, size_z), jnp.float32),
            jax.ShapeDtypeStruct((4, size_x, size_z), jnp.float32),
            jax.ShapeDtypeStruct((3, flags, size_z), jnp.float32),
            jax.ShapeDtypeStruct((flags, 4 * returned), jnp.bfloat16),
            jax.ShapeDtypeStruct((row_count, 3 * product_depth), jnp.bfloat16),
        ),
        in_specs=[SMEM] * 2 + [VMEM] * 6,
        out_specs=(VMEM,) * 6,
        scratch_shapes=[
            pltpu.VMEM((3, *wide), jnp.float32),
            pltpu.VMEM((3, *wide), jnp.float32),
            pltpu.VMEM((3, *planes), jnp.float32),
            pltpu.VMEM((item_count, *wide), jnp.float32),
            pltpu.VMEM((6, size_x, size_z), jnp.float32),
            pltpu.VMEM((3, *planes), jnp.float32),
            pltpu.VMEM((product_depth, -(-row_count // 128) * 128), jnp.float32),
            pltpu.VMEM((2, size_y, size_z), jnp.float32),
        ],
        compiler_params=limit(12),
        cost_estimate=pl.CostEstimate(flops=4000000, bytes_accessed=3000000, transcendentals=0),
        name="flow_step",
    )(
        flag_cell, position,
        velocity.reshape(3, size_x * size_y, size_z),
        viscosity.reshape(size_x * size_y, size_z),
        chunks, y_low, y_high, handed,
    )


def pieces(value):
    high = value.astype(jnp.bfloat16)
    rest = value - high.astype(jnp.float32)
    middle = rest.astype(jnp.bfloat16)
    return high, middle, (rest - middle.astype(jnp.float32)).astype(jnp.bfloat16)


def polymer_kernel(
    size_x, size_y, size_z, macro_count, chunk_ref, viscous_ref, corner_ref, edge_ref, lines_ref, pick_ref,
    spread_ref, partial_ref, out_ref, flag_ref, field, write_sem,
):
    flags = viscous_ref.shape[0]
    macro, core = place_of()
    chunks = chunk_ref[...]
    split = jnp.concatenate((*pieces(chunks), jnp.zeros(chunks.shape, jnp.bfloat16)), axis=0)
    values = jnp.dot(pick_ref[...], split, preferred_element_type=jnp.float32) * lines_ref[2]
    here, beside_z = lines_ref[0], lines_ref[1]
    lane = lanes_of((flags, 128))
    columns = [
        jnp.broadcast_to(
            jnp.sum(jnp.where((lane & 7) == k, values, 0.0), axis=1, keepdims=True), (flags, size_z)
        )
        for k in range(6)
    ]
    stress = viscous_ref[...]
    for k in range(6):
        stress = jnp.where(lane == k, stress + columns[k], stress)
    unused = jnp.zeros((product_depth - 3 * flags, size_z), jnp.float32)
    split = [
        pieces(
            jnp.concatenate(
                [
                    columns[pair_index(a, 0)] * here, columns[pair_index(a, 1)] * here,
                    columns[pair_index(a, 2)] * beside_z, unused,
                ],
                axis=0,
            )
        )
        for a in range(3)
    ]
    flag_ref[...] = stress.T[0:6, :]

    field[...] = partial_ref[...]
    for s in range(2):
        inside = macro > 0 if s == 0 else macro < macro_count - 1
        beside = jnp.maximum(macro - 1, 0) if s == 0 else jnp.minimum(macro + 1, macro_count - 1)
        start = (2 * beside + core) * back_rows
        x = 0 if s == 0 else size_x - 1
        for u in range(2):
            at = x * size_y + (0 if u == 0 else size_y - 1)
            for a in range(2):
                number = 4 * s + 2 * u + a
                line = corner_ref[number : number + 1, :] * chunk_ref[pl.ds(start + 2 * u + a, 1), :]
                field[1 - a, at : at + 1, :] += jnp.where(inside, line, 0.0)
    start = pl.multiple_of((2 * macro + 1 - core) * back_rows, 8)
    packed = chunk_ref[pl.ds(start, back_rows), :]
    end = jnp.where(core == 0, size_z - 1, 0)
    for u in range(2):
        y = 0 if u == 0 else size_y - 1
        for a in range(2):
            for i in range(size_x // 8):
                line = rolled(packed, end - (line_lane + 4 * i + 2 * u + a)) * edge_ref[2 * u + a, 8 * i : 8 * i + 8, :]
                at = pl.ds(8 * i * size_y + y, 8, stride=size_y)
                field[2 - a, at, :] += line
    copies = [pltpu.make_async_copy(field.at[a], out_ref.at[a], write_sem.at[a]) for a in range(3)]
    for a in range(3):
        field[a] += jnp.dot(
            spread_ref[...], jnp.concatenate(split[a], axis=0), preferred_element_type=jnp.float32
        )
        copies[a].start()
    for copy in copies:
        copy.wait()


def add_polymer(chunks, viscous, corners, edges, lines, pick, spread, partial, shape):
    flags = viscous.shape[0]
    size_x, size_y, size_z = shape
    return pl.pallas_call(
        functools.partial(polymer_kernel, size_x, size_y, size_z, chunks.shape[0] // 2),
        out_shape=(
            jax.ShapeDtypeStruct(partial.shape, jnp.float32),
            jax.ShapeDtypeStruct((6, flags), jnp.float32),
        ),
        in_specs=[VMEM] * 8,
        out_specs=(pl.BlockSpec(memory_space=pltpu.HBM), VMEM),
        scratch_shapes=[pltpu.VMEM(partial.shape, jnp.float32), pltpu.SemaphoreType.DMA((3,))],
        compiler_params=limit(8),
        cost_estimate=pl.CostEstimate(flops=400000, bytes_accessed=3000000, transcendentals=0),
        name="add_polymer",
    )(chunks.reshape(-1, 128), viscous, corners, edges, lines, pick, spread, partial)


def shards(velocity, viscosity, flag_cell, flag_owner, conformations, increments):
    macro_count = lax.axis_size("macro")
    tile_count = lax.axis_size("tile")
    assert lax.axis_size("micro") == 2
    owner_count = 2 * macro_count
    capacity = conformations.shape[1] // owner_count
    size_x, size_y, size_z = viscosity.shape
    assert capacity <= slot_rows and capacity % 2 == 0 and size_y == 8 and size_z == 128 and size_x % 8 == 0 and size_x <= 48
    chunks, position, viscous, first, second, first_conform, first_noise = gather_rows(
        flag_cell, flag_owner.reshape(-1), velocity, viscosity, conformations, increments, capacity, owner_count
    )

    def exchange(rows):
        return lax.all_to_all(rows, ("macro", "micro"), split_axis=0, concat_axis=0, tiled=True)

    received = exchange(chunks.reshape(owner_count, -1, 128))
    swaps = []
    for start in range(2):
        pairs = [(i, i + 1) for i in range(start, tile_count - 1, 2)]
        swaps.append(pairs + [(high, low) for low, high in pairs])
    first = lax.ppermute(first, "tile", swaps[0])
    second = lax.ppermute(second, "tile", swaps[1])
    last_state, polymer = advance(
        conformations, increments, received, first_conform, first_noise, capacity
    )
    polymer, y_low, y_high, handed = add_lines(polymer, received, first, second)
    returned = exchange(polymer)
    handed = lax.ppermute(handed, "micro", [(0, 1), (1, 0)])
    partial, corners, edges, lines, pick, spread = flow_step(
        flag_cell, position, velocity, viscosity, received, y_low, y_high, handed
    )
    velocity_next, flag_stress = add_polymer(
        returned, viscous, corners, edges, lines, pick, spread, partial, viscosity.shape
    )
    return (velocity_next.reshape(velocity.shape), last_state, flag_stress)


def solution(mesh):
    in_specs = (
        P(None, "macro", "tile", "micro"),
        P("macro", "tile", "micro"),
        P(("macro", "tile", "micro")),
        P(("macro", "tile", "micro"), None),
        P(None, ("macro", "tile", "micro"), None),
        P(None, None, ("macro", "tile", "micro"), None),
    )
    out_specs = (
        P(None, "macro", "tile", "micro"),
        P(None, ("macro", "tile", "micro"), None),
        P(None, ("macro", "tile", "micro")),
    )
    return jax.shard_map(shards, mesh=mesh, in_specs=in_specs, out_specs=out_specs, check_vma=False)
```

```python
import functools

import jax
import jax.numpy as jnp
from jax import lax
from jax.experimental import pallas as pl
from jax.experimental.pallas import tpu as pltpu
from jax.sharding import PartitionSpec as P

stress_pairs = ((0, 0), (1, 1), (2, 2), (0, 1), (0, 2), (1, 2))
macro_step = 0.1
micro_step = 0.01
noise_weight = 0.1
relax_rate = 0.5
fene_extent = 30.0
spring_floor = 0.1
polymer_weight = 0.25

SMEM = pl.BlockSpec(memory_space=pltpu.SMEM)
VMEM = pl.BlockSpec(memory_space=pltpu.VMEM)


def pair_index(left_axis, right_axis):
    return stress_pairs.index((min(left_axis, right_axis), max(left_axis, right_axis)))


def lanes_of(shape):
    return lax.broadcasted_iota(jnp.int32, shape, len(shape) - 1)


slot_rows = 8
chunk_rows = 32
half_face = 28
handed_rows = 48
item_count = 7
back_rows = 8
polymer_row = 4
line_lane = 64


block_slots = 32
first_share = 2


def limit(mebibytes):
    return pltpu.CompilerParams(vmem_limit_bytes=mebibytes * 1024 * 1024)


def far(value):
    return pltpu.with_memory_space_constraint(value, pltpu.HBM)


def place_of():
    return lax.axis_index("macro"), lax.axis_index("micro")


def neighbour(index, side, count):
    return jnp.maximum(index - 1, 0) if side == 0 else jnp.minimum(index + 1, count - 1)


def rolled(value, amount):
    size = value.shape[-1]
    if isinstance(amount, int):
        return pltpu.roll(value, amount % size, value.ndim - 1)
    return pltpu.roll(value, lax.rem(amount + 2 * size, size), value.ndim - 1)


def gather_kernel(
    capacity, size_x, size_y, size_z, macro_count, cell_in, owner_in, velocity_in, viscosity_in,
    conform_in, noise_in, chunk_ref, position_ref, viscous_ref, first_ref, second_ref, conform_ref, noise_ref,
    cell_ref, owner_ref, velocity_ref, viscosity_ref, masked, gradients, paired, target, count, sems,
):
    flags = cell_ref.shape[0]
    copies = [
        pltpu.make_async_copy(source, into, sems.at[number])
        for number, (source, into) in enumerate(
            (
                (cell_in, cell_ref), (owner_in, owner_ref), (velocity_in, velocity_ref),
                (viscosity_in, viscosity_ref), (conform_in.at[:, 0:block_slots, :], conform_ref),
                (noise_in.at[0 : noise_ref.shape[0], :, 0:block_slots, :], noise_ref),
            )
        )
    ]
    for copy in copies:
        copy.start()
    paired_rows = paired.shape[0] // 2
    macro, core = place_of()
    lane = lanes_of((1, size_z))

    for owner in range(count.shape[0]):
        count[owner] = 0
    paired[...] = jnp.zeros_like(paired)
    for copy in copies[:2]:
        copy.wait()
    for j in range(flags):
        owner = owner_ref[j]
        rank = count[owner]
        count[owner] = rank + 1
        target[j] = (rank & 1) * paired_rows + owner * (slot_rows // 2) + lax.shift_right_logical(rank, 1)
        position_ref[j] = owner * slot_rows + rank
    for copy in copies[2:4]:
        copy.wait()
    planes = velocity_ref.reshape(3, size_x, size_y, size_z)
    layers = viscosity_ref.reshape(size_x, size_y, size_z)
    for j in range(flags):
        cell = cell_ref[j]
        x = lax.shift_right_logical(cell, 10)
        y = lax.shift_right_logical(cell, 7) & (size_y - 1)
        z = cell & (size_z - 1)
        here = (lane == z).astype(jnp.float32)
        along_z = (lane == z + 1).astype(jnp.float32) - (lane == z - 1).astype(jnp.float32)
        at = pl.ds(y, 1)
        for a in range(3):
            along_x = planes[a, x + 1, at, :] - planes[a, x - 1, at, :]
            along_y = planes[a, x, pl.ds(y + 1, 1), :] - planes[a, x, pl.ds(y - 1, 1), :]
            masked[3 * a, j : j + 1, :] = along_x * here
            masked[3 * a + 1, j : j + 1, :] = along_y * here
            masked[3 * a + 2, j : j + 1, :] = planes[a, x, at, :] * along_z
        masked[9, j : j + 1, :] = layers[x, at, :] * here

    even = lax.axis_index("tile") & 1 == 0

    def put(number, ref, low, high):
        rows = [ref[pl.ds(y, size_x, stride=size_y), :] for y in (low, high)]
        first_ref[number] = jnp.where(even, rows[1], rows[0])
        second_ref[number] = jnp.where(even, rows[0], rows[1])

    for layer in range(2):
        for a in range(3):
            put(3 * layer + a, velocity_ref.at[a], layer, size_y - 1 - layer)
    put(6, viscosity_ref, 0, size_y - 1)

    for side in range(2):
        beside = neighbour(macro, side, macro_count)
        for layer, owner in enumerate((2 * beside + core, 2 * beside + 1 - core)):
            start = pl.multiple_of(owner * chunk_rows, 8)
            x = layer if side == 0 else size_x - 1 - layer
            for a in range(3):
                chunk_ref[pl.ds(start + a * size_y, size_y), :] = velocity_ref[a, x * size_y : (x + 1) * size_y, :]
            x = 0 if side == 0 else size_x - 1
            half = x * size_y + layer * (size_y // 2)
            chunk_ref[pl.ds(start + 3 * size_y, size_y // 2), :] = viscosity_ref[half : half + size_y // 2, :]

    group = size_z // 8
    lane2 = lanes_of((size_y, size_z))
    first = pl.multiple_of((2 * macro + 1 - core) * chunk_rows, 8)
    source = jnp.where(core == 0, size_z - 2, 0)
    for block in range(-(-size_x // group)):
        total = jnp.zeros((size_y, size_z), jnp.float32)
        for x in range(block * group, min(size_x, (block + 1) * group)):
            rows = slice(x * size_y, (x + 1) * size_y)
            for a in range(4):
                at = 8 * (x - block * group) + 2 * a
                value = viscosity_ref[rows, :] if a == 3 else velocity_ref[a, rows, :]
                total = jnp.where((lane2 == at) | (lane2 == at + 1), rolled(value, at - source), total)
        chunk_ref[pl.ds(first + block * size_y, size_y), :] = total

    columns = [0.5 * jnp.sum(masked[c], axis=1, keepdims=True) for c in range(9)]
    viscous = jnp.sum(masked[9], axis=1, keepdims=True)
    wide = lanes_of((flags, 128))
    packed = jnp.zeros((flags, 128), jnp.float32)
    for c in range(9):
        packed = jnp.where(wide == c, columns[c], packed)
    gradients[...] = packed
    stress = jnp.zeros((flags, 128), jnp.float32)
    for k, (a, b) in enumerate(stress_pairs):
        stress = jnp.where(wide == k, viscous * (columns[3 * a + b] + columns[3 * b + a]), stress)
    viscous_ref[...] = stress

    for j in range(flags):
        paired[pl.ds(target[j], 1), :] = gradients[j : j + 1, :]
    rows = paired[0:paired_rows, :] + rolled(paired[paired_rows:, :], 64)
    for owner in range(count.shape[0]):
        chunk_ref[owner * chunk_rows + half_face : (owner + 1) * chunk_rows, :] = rows[
            owner * (slot_rows // 2) : (owner + 1) * (slot_rows // 2)
        ]
    for copy in copies[4:]:
        copy.wait()


def gather_rows(flag_cell, owner, velocity, viscosity, conformations, increments, capacity, owner_count):
    size_x, size_y, size_z = viscosity.shape
    flags = flag_cell.shape[0]
    face = jax.ShapeDtypeStruct((item_count, size_x, size_z), jnp.float32)
    steps, _, _, dumbbells = increments.shape
    return pl.pallas_call(
        functools.partial(gather_kernel, capacity, size_x, size_y, size_z, owner_count // 2),
        out_shape=(
            jax.ShapeDtypeStruct((owner_count * chunk_rows, 128), jnp.float32),
            jax.ShapeDtypeStruct((flags,), jnp.int32),
            jax.ShapeDtypeStruct((flags, 128), jnp.float32),
            face,
            face,
            pltpu.VMEM((3, block_slots, dumbbells), jnp.float32),
            pltpu.VMEM((steps // first_share, 3, block_slots, dumbbells), jnp.bfloat16),
        ),
        in_specs=[pl.BlockSpec(memory_space=pltpu.HBM)] * 6,
        out_specs=(VMEM, SMEM, VMEM, VMEM, VMEM, VMEM, VMEM),
        scratch_shapes=[
            pltpu.SMEM((flags,), jnp.int32),
            pltpu.SMEM((flags,), jnp.int32),
            pltpu.VMEM((3, size_x * size_y, size_z), jnp.float32),
            pltpu.VMEM((size_x * size_y, size_z), jnp.float32),
            pltpu.VMEM((10, flags, size_z), jnp.float32),
            pltpu.VMEM((flags, 128), jnp.float32),
            pltpu.VMEM((owner_count * slot_rows, 128), jnp.float32),
            pltpu.SMEM((flags,), jnp.int32),
            pltpu.SMEM((owner_count,), jnp.int32),
            pltpu.SemaphoreType.DMA((6,)),
        ],
        compiler_params=limit(8),
        cost_estimate=pl.CostEstimate(flops=400000, bytes_accessed=3000000, transcendentals=0),
        name="gather_rows",
    )(
        far(flag_cell),
        far(owner),
        far(velocity.reshape(3, size_x * size_y, size_z)),
        far(viscosity.reshape(size_x * size_y, size_z)),
        far(conformations),
        far(increments),
    )


def micro_kernel(
    capacity, parts, rows, groups, conform_ref, noise_ref, rate_ref, first_conform_ref, first_noise_ref,
    next_ref, chunk_ref, conform, noise, rate, rate_wide, sums_ref, read_sem, noise_sem,
):
    steps, _, slots, dumbbells = noise_ref.shape
    blocks = slots // rows
    span = steps // groups
    width = dumbbells // parts
    owners = slots // capacity
    scale = 1.0 / noise_weight
    extent = fene_extent * scale * scale

    def block_rows(block):
        return pl.ds(pl.multiple_of(block * rows, rows), rows)

    def read(block):
        at = block_rows(block)
        return pltpu.make_async_copy(conform_ref.at[:, at, :], conform.at[:, at, :], read_sem.at[block])

    def read_noise(block, group):
        at, when = block_rows(block), pl.ds(group * span, span)
        return pltpu.make_async_copy(
            noise_ref.at[when, :, at, :], noise.at[when, :, at, :], noise_sem.at[block, group]
        )

    pieces = [
        (half, slice(part * width, (part + 1) * width)) for half in range(rows // 16) for part in range(parts)
    ]
    assert len(pieces) == 8
    early = groups // first_share
    for block in range(blocks):
        if block > 0:
            read(block).start()
        for group in range(early if block == 0 else 0, groups):
            read_noise(block, group).start()
    conform[:, 0:rows, :] = first_conform_ref[...]
    for step in range(steps // first_share):
        noise[step, :, 0:rows, :] = first_noise_ref[step]
    for owner in range(owners):
        packed = rate_ref[owner, half_face : half_face + capacity // 2, :]
        rate[pl.ds(owner * capacity, capacity // 2, stride=2), :] = packed
        rate[pl.ds(owner * capacity + 1, capacity // 2, stride=2), :] = rolled(packed, 64)
        chunk_ref[owner] = jnp.zeros(chunk_ref.shape[1:], jnp.float32)
    for a in range(3):
        for b in range(3):
            column = micro_step * rate[:, 3 * a + b : 3 * a + b + 1] + (1.0 if a == b else 0.0)
            rate_wide[3 * a + b] = jnp.broadcast_to(column, (slots, width))

    def inverses(state, scale):
        rooms = []
        for piece in range(len(pieces)):
            q = state[3 * piece : 3 * piece + 3]
            room = (extent - q[0] * q[0]) - (q[1] * q[1] + q[2] * q[2])
            rooms.append(jnp.maximum(room, extent * spring_floor))
        levels = [rooms]
        while len(levels[-1]) > 1:
            levels.append([low * high for low, high in zip(levels[-1][0::2], levels[-1][1::2])])
        result = [scale * pl.reciprocal(levels[-1][0])]
        for level in reversed(levels[:-1]):
            result = [result[i // 2] * level[i ^ 1] for i in range(len(level))]
        return result

    def advance_block(block, carry):
        ats = [pl.ds(pl.multiple_of(block * rows + 16 * half, 16), 16) for half in range(rows // 16)]
        rates = [
            [[rate_wide.at[3 * a + b, at, :] for b in range(3)] for a in range(3)] for at in ats
        ]

        def substep(step, state):
            updated = []
            springs = inverses(state, micro_step * relax_rate * extent)
            for piece, (half, lanes) in enumerate(pieces):
                q = state[3 * piece : 3 * piece + 3]
                table = rates[half]
                for a in range(3):
                    b, c = [other for other in range(3) if other != a]
                    kick = noise[step, a, ats[half], lanes].astype(jnp.float32)
                    rest = (table[a][b][...] * q[b] + table[a][c][...] * q[c]) + kick
                    updated.append((table[a][a][...] - springs[piece]) * q[a] + rest)
            return tuple(updated)

        def advance_group(group, state):
            if group < early:

                @pl.when(block > 0)
                def _():
                    read_noise(block, group).wait()

            else:
                read_noise(block, group).wait()
            for step in range(span):
                state = substep(group * span + step, state)
            return state

        @pl.when(block > 0)
        def _():
            read(block).wait()

        state = tuple(conform[a, ats[half], lanes] * scale for half, lanes in pieces for a in range(3))
        for group in range(groups):
            state = advance_group(group, state)
        inverse = inverses(state, 1.0)
        for half, at in enumerate(ats):
            sums = [None] * 6
            for piece, (other, lanes) in enumerate(pieces):
                if other != half:
                    continue
                q = state[3 * piece : 3 * piece + 3]
                for a in range(3):
                    next_ref[a, at, lanes] = q[a] * noise_weight
                for k, (a, b) in enumerate(stress_pairs):
                    term = (inverse[piece] * q[a]) * q[b]
                    sums[k] = term if sums[k] is None else sums[k] + term
            for k in range(6):
                sums_ref[k, at, :] = sums[k]
        return carry

    lax.fori_loop(0, blocks, advance_block, 0)
    lane = lanes_of((slots, 128))
    rank = lax.broadcasted_iota(jnp.int32, (slots, 128), 0) & (capacity - 1)
    packed = jnp.zeros((slots, 128), jnp.float32)
    weight = extent * noise_weight * noise_weight / dumbbells
    for k, (a, b) in enumerate(stress_pairs):
        mean = jnp.sum(sums_ref[k], axis=1, keepdims=True) * weight
        packed = jnp.where(lane == 8 * rank + k, polymer_weight * (mean - (1.0 if a == b else 0.0)), packed)
    for owner in range(owners):
        chunk_ref[owner, polymer_row : polymer_row + 1, :] = jnp.sum(
            packed[owner * capacity : (owner + 1) * capacity], axis=0, keepdims=True
        )


def advance(conformations, increments, chunks, first_conform, first_noise, capacity):
    slots, dumbbells = conformations.shape[1:]
    steps = increments.shape[0]
    owners = slots // capacity
    rows, parts, groups = block_slots, 4, 4
    blocks = slots // rows
    whole = pl.BlockSpec(memory_space=pltpu.HBM)
    return pl.pallas_call(
        functools.partial(micro_kernel, capacity, parts, rows, groups),
        out_shape=(
            pltpu.VMEM(conformations.shape, jnp.float32),
            jax.ShapeDtypeStruct((owners, back_rows, 128), jnp.float32),
        ),
        in_specs=[whole, whole, VMEM, VMEM, VMEM],
        out_specs=(VMEM, VMEM),
        scratch_shapes=[
            pltpu.VMEM(conformations.shape, jnp.float32),
            pltpu.VMEM(increments.shape, jnp.bfloat16),
            pltpu.VMEM((slots, 128), jnp.float32),
            pltpu.VMEM((9, slots, dumbbells // parts), jnp.float32),
            pltpu.VMEM((6, slots, dumbbells // parts), jnp.float32),
            pltpu.SemaphoreType.DMA((blocks,)),
            pltpu.SemaphoreType.DMA((blocks, groups)),
        ],
        compiler_params=limit(12),
        cost_estimate=pl.CostEstimate(flops=20000000, bytes_accessed=5000000, transcendentals=600000),
        name="advance",
    )(far(conformations), far(increments), chunks, first_conform, first_noise)


def lines_kernel(
    macro_count, chunk_ref, received_ref, first_ref, second_ref, out_ref, y_low_ref, y_high_ref, handed_ref
):
    out_ref[...] = chunk_ref[...]
    macro, core = place_of()
    for side in range(2):
        beside = neighbour(macro, side, macro_count)
        handed_ref[side, 0:chunk_rows, :] = received_ref[2 * beside + 1 - core]
        for number, a in enumerate((0, 2)):
            handed_ref[side, chunk_rows + number * 8 : chunk_rows + (number + 1) * 8, :] = received_ref[
                2 * beside + core, a * 8 : (a + 1) * 8, :
            ]
    even = lax.axis_index("tile") & 1 == 0
    y_low_ref[...] = jnp.where(even, second_ref[...], first_ref[...])
    y_high_ref[...] = jnp.where(even, first_ref[...], second_ref[...])
    sides = (y_low_ref, y_high_ref)
    size_x, size_z = y_low_ref.shape[1:]
    for side in range(2):
        beside = neighbour(macro, side, macro_count)
        x = 0 if side == 0 else size_x - 1
        for u in range(2):
            for a in range(2):
                at = 2 * u + a
                out_ref[2 * beside + core, at : at + 1, :] = sides[u][a, x : x + 1, :]

    lane = lanes_of((8, size_z))
    source = jnp.where(core == 0, size_z - 1, 0)
    other = 2 * macro + 1 - core
    total = chunk_ref[other]
    for i in range(size_x // 8):
        for u in range(2):
            for a in range(2):
                at = line_lane + 4 * i + 2 * u + a
                total = jnp.where(
                    lane == at, rolled(sides[u][1 + a, 8 * i : 8 * i + 8, :], at - source), total
                )
    out_ref[other] = total


def add_lines(chunks, received, first, second):
    face = jax.ShapeDtypeStruct(first.shape, jnp.float32)
    return pl.pallas_call(
        functools.partial(lines_kernel, chunks.shape[0] // 2),
        out_shape=(
            jax.ShapeDtypeStruct(chunks.shape, jnp.float32), face, face,
            jax.ShapeDtypeStruct((2, handed_rows, 128), jnp.float32),
        ),
        in_specs=[VMEM] * 4,
        out_specs=(VMEM,) * 4,
        compiler_params=limit(4),
        cost_estimate=pl.CostEstimate(flops=20000, bytes_accessed=400000, transcendentals=0),
        name="add_lines",
    )(chunks, received, first, second)


product_depth = 128


def one_hots(size_y, size_z, cell_ref, position_ref, lines_ref, pick_ref, spread_ref, rows):
    flags = cell_ref.shape[0]
    weight = 0.5 * macro_step
    row_count = spread_ref.shape[0]
    returned = pick_ref.shape[1] // 4
    lane = lanes_of((1, size_z))
    row_lane = lanes_of((1, rows.shape[1]))
    slot_lane = lanes_of((flags, returned))
    flag_row = lax.broadcasted_iota(jnp.int32, (flags, returned), 0)
    rows[3 * flags :, :] = jnp.zeros((product_depth - 3 * flags, rows.shape[1]), jnp.float32)
    slot = jnp.zeros((flags, returned), jnp.int32)
    group = lax.shift_right_logical(lane, 3)
    for j in range(flags):
        cell = cell_ref[j]
        row = lax.div(cell, size_z)
        z = cell - row * size_z
        lines_ref[0, j : j + 1, :] = jnp.where(lane == z, weight, 0.0)
        lines_ref[1, j : j + 1, :] = jnp.where(
            lane == z - 1, weight, jnp.where(lane == z + 1, -weight, 0.0)
        )
        for number, shift in enumerate((size_y, 1)):
            rows[number * flags + j : number * flags + j + 1, :] = jnp.where(
                row_lane == row - shift, 1.0, jnp.where(row_lane == row + shift, -1.0, 0.0)
            )
        rows[2 * flags + j : 2 * flags + j + 1, :] = jnp.where(row_lane == row, 1.0, 0.0)
        owner = lax.div(position_ref[j], slot_rows)
        rank = position_ref[j] - owner * slot_rows
        lines_ref[2, j : j + 1, :] = jnp.where(group == rank, 1.0, 0.0)
        slot = jnp.where(flag_row == j, owner * back_rows + polymer_row, slot)
    spread = rows[...].T[:row_count].astype(jnp.bfloat16)
    pick = jnp.where(slot_lane == slot, 1.0, 0.0).astype(jnp.bfloat16)
    for piece in range(3):
        spread_ref[:, piece * product_depth : (piece + 1) * product_depth] = spread
        pick_ref[:, piece * returned : (piece + 1) * returned] = pick
    pick_ref[:, 3 * returned :] = jnp.zeros((flags, returned), jnp.bfloat16)


def flow_kernel(
    size_x, size_y, size_z, macro_count, cell_ref, position_ref, velocity_ref, viscosity_ref, chunk_ref,
    y_low_ref, y_high_ref, handed_ref, out_ref, corner_ref, edge_ref, lines_ref, pick_ref, spread_ref,
    padded, stress_x, stress_rest, faces, ghost_y, ghost_z, rows, halves,
):
    macro, core = place_of()
    one_hots(size_y, size_z, cell_ref, position_ref, lines_ref, pick_ref, spread_ref, rows)
    inside = (macro > 0, macro < macro_count - 1)
    sign_z = jnp.where(core == 0, 1.0, -1.0)
    end = jnp.where(core == 0, size_z - 1, 0)
    shape = (size_y, size_z)
    lane, row = lanes_of(shape), lax.broadcasted_iota(jnp.int32, shape, 0)
    at_end = jnp.where(lane == end, sign_z, 0.0)

    def kept(value, condition):
        return jnp.where(condition, value, 0.0)

    def plane(x):
        return pl.ds(pl.multiple_of(x * size_y, 8), size_y)

    def difference_z(value):
        lane = lanes_of(value.shape)
        return jnp.where(lane == size_z - 1, 0.0, rolled(value, -1)) - jnp.where(
            lane == 0, 0.0, rolled(value, 1)
        )

    def difference_rows(value, low=0.0, high=0.0):
        count = value.shape[0]
        row = lax.broadcasted_iota(jnp.int32, value.shape, 0)
        return jnp.where(row == count - 1, high, pltpu.roll(value, count - 1, 0)) - jnp.where(
            row == 0, low, pltpu.roll(value, 1, 0)
        )

    x_faces, x_others = [], []
    half = size_y // 2
    for s in range(2):
        beside = neighbour(macro, s, macro_count)
        outer = chunk_ref[2 * beside + core]
        items = [outer[i * size_y : (i + 1) * size_y] for i in range(3)]
        items += [handed_ref[s, i * size_y : (i + 1) * size_y, :] for i in range(3)]
        halves[s, 0:half, :] = chunk_ref[2 * beside + core, 3 * size_y : 3 * size_y + half, :]
        halves[s, half:, :] = handed_ref[s, 3 * size_y : 3 * size_y + half, :]
        items.append(halves[s])
        x_faces.append([kept(item, inside[s]) for item in items])
        corners = [handed_ref[s, chunk_rows + i * size_y : chunk_rows + (i + 1) * size_y, :] for i in range(2)]
        x_others.append([kept(rolled(corner, 2 * end + 1), inside[s]) for corner in corners])

    group = size_z // 8
    packed = [
        chunk_ref[2 * macro + 1 - core, i * size_y : (i + 1) * size_y, :]
        for i in range(-(-size_x // group))
    ]
    for i, value in enumerate(packed):

        def unpack(x, carry):
            for q in range(item_count):
                a, layer = (q, 0) if q < 4 else (q - 4, 1)
                at = 8 * (x - i * group) + 2 * a + (core if layer == 0 else 1 - core)
                faces[q, x + 1] = rolled(value, end - at)
            return carry

        lax.fori_loop(i * group, min(size_x, (i + 1) * group), unpack, 0, unroll=8)
    faces[2, 0] = x_others[0][1]
    faces[2, size_x + 1] = x_others[1][1]

    for a in range(3):
        padded[a, 0] = x_faces[0][a]
        padded[a, size_x + 1] = x_faces[1][a]

    def fill(x, carry):
        for a in range(3):
            padded[a, x + 1] = velocity_ref[a, plane(x), :]
        return carry

    lax.fori_loop(0, size_x, fill, 0, unroll=True)

    rest = {(1, 1): 0, (2, 2): 1, (1, 2): 2}

    def stress_plane(x, carry):
        along_x, along_y, along_z, centre = [], [], [], []
        for a in range(3):
            value = padded[a, x + 1]
            centre.append(value)
            along_x.append(padded[a, x + 2] - padded[a, x])
            along_y.append(
                difference_rows(value, y_low_ref[a, pl.ds(x, 1), :], y_high_ref[a, pl.ds(x, 1), :])
            )
            along_z.append(difference_z(value) + faces[a, x + 1] * at_end)
        slopes = (along_x, along_y, along_z)
        half = 0.5 * viscosity_ref[plane(x), :]
        for a, b in stress_pairs:
            value = half * (slopes[b][a] + slopes[a][b])
            if a == 0:
                stress_x[b, x + 1] = value
            else:
                stress_rest[rest[a, b], x] = value
        weight = (0.5 * faces[3, x + 1]) * at_end
        normal = [(faces[4 + a, x + 1] - centre[a]) * sign_z for a in range(3)]
        ghost_z[0, x] = weight * (normal[0] + (faces[2, x + 2] - faces[2, x]))
        ghost_z[1, x] = weight * (normal[1] + difference_rows(faces[2, x + 1]))
        ghost_z[2, x] = weight * (2.0 * normal[2])
        return carry

    lax.fori_loop(0, size_x, stress_plane, 0, unroll=6)

    for s in range(2):
        near, far, weight = x_faces[s][0:3], x_faces[s][3:6], 0.5 * x_faces[s][6]
        sign = -1.0 if s == 0 else 1.0
        normal = [(far[a] - padded[a, 1 if s == 0 else size_x]) * sign for a in range(3)]
        slope_y = difference_rows(near[0])
        slope_z = difference_z(near[0]) + x_others[s][0] * at_end
        at = 0 if s == 0 else size_x + 1
        stress_x[0, at] = weight * (2.0 * normal[0])
        stress_x[1, at] = weight * (normal[1] + slope_y)
        stress_x[2, at] = weight * (normal[2] + slope_z)
        for u in range(2):
            y, sign_y = (0, -1.0) if u == 0 else (size_y - 1, 1.0)
            number = 4 * s + 2 * u
            corner_ref[number : number + 1, :] = (0.5 * macro_step * sign * sign_y) * weight[y : y + 1, :]

    for u, ref in enumerate((y_low_ref, y_high_ref)):
        y, sign = (0, -1.0) if u == 0 else (size_y - 1, 1.0)
        weight = 0.5 * ref[6]
        normal = [
            (ref[3 + a] - velocity_ref[a, pl.ds(y, size_x, stride=size_y), :]) * sign for a in range(3)
        ]
        ghost_y[3 * u] = weight * (normal[0] + difference_rows(ref[1]))
        ghost_y[3 * u + 1] = weight * (2.0 * normal[1])
        ghost_y[3 * u + 2] = weight * (normal[2] + difference_z(ref[1]))
        for s in range(2):
            x, sign_x = (0, -1.0) if s == 0 else (size_x - 1, 1.0)
            number = 4 * s + 2 * u + 1
            corner_ref[number : number + 1, :] = (0.5 * macro_step * sign * sign_x) * weight[x : x + 1, :]
        wide = lanes_of((size_x, size_z))
        scale = jnp.where(wide == end, (0.5 * macro_step * sign) * sign_z, 0.0)
        edge_ref[2 * u] = scale * weight
        for x in range(size_x):
            edge_ref[2 * u + 1, x : x + 1, :] = scale[x : x + 1, :] * (0.5 * faces[3, x + 1, y : y + 1, :])

    columns = {(0, 1): (stress_x, 1, 1), (1, 1): (stress_rest, 0, 0), (2, 1): (stress_rest, 2, 0)}
    columns_z = {0: (stress_x, 2, 1), 1: (stress_rest, 2, 0), 2: (stress_rest, 1, 0)}

    def step_plane(x, carry):
        for a in range(3):
            total = stress_x[a, x + 2] - stress_x[a, x]
            ref, number, shift = columns[a, 1]
            total = total + difference_rows(
                ref[number, x + shift], ghost_y[a, pl.ds(x, 1), :], ghost_y[3 + a, pl.ds(x, 1), :]
            )
            ref, number, shift = columns_z[a]
            total = total + (difference_z(ref[number, x + shift]) + ghost_z[a, x])
            out_ref[a, plane(x), :] = padded[a, x + 1] + (0.5 * macro_step) * total
        return carry

    lax.fori_loop(0, size_x, step_plane, 0, unroll=6)


def flow_step(flag_cell, position, velocity, viscosity, chunks, y_low, y_high, handed):
    size_x, size_y, size_z = viscosity.shape
    flags = flag_cell.shape[0]
    returned = chunks.shape[0] * back_rows
    row_count = size_x * size_y
    planes = (size_x, size_y, size_z)
    wide = (size_x + 2, size_y, size_z)
    return pl.pallas_call(
        functools.partial(flow_kernel, size_x, size_y, size_z, chunks.shape[0] // 2),
        out_shape=(
            jax.ShapeDtypeStruct((3, size_x * size_y, size_z), jnp.float32),
            jax.ShapeDtypeStruct((8, size_z), jnp.float32),
            jax.ShapeDtypeStruct((4, size_x, size_z), jnp.float32),
            jax.ShapeDtypeStruct((3, flags, size_z), jnp.float32),
            jax.ShapeDtypeStruct((flags, 4 * returned), jnp.bfloat16),
            jax.ShapeDtypeStruct((row_count, 3 * product_depth), jnp.bfloat16),
        ),
        in_specs=[SMEM] * 2 + [VMEM] * 6,
        out_specs=(VMEM,) * 6,
        scratch_shapes=[
            pltpu.VMEM((3, *wide), jnp.float32),
            pltpu.VMEM((3, *wide), jnp.float32),
            pltpu.VMEM((3, *planes), jnp.float32),
            pltpu.VMEM((item_count, *wide), jnp.float32),
            pltpu.VMEM((6, size_x, size_z), jnp.float32),
            pltpu.VMEM((3, *planes), jnp.float32),
            pltpu.VMEM((product_depth, -(-row_count // 128) * 128), jnp.float32),
            pltpu.VMEM((2, size_y, size_z), jnp.float32),
        ],
        compiler_params=limit(12),
        cost_estimate=pl.CostEstimate(flops=4000000, bytes_accessed=3000000, transcendentals=0),
        name="flow_step",
    )(
        flag_cell, position,
        velocity.reshape(3, size_x * size_y, size_z),
        viscosity.reshape(size_x * size_y, size_z),
        chunks, y_low, y_high, handed,
    )


def pieces(value):
    high = value.astype(jnp.bfloat16)
    rest = value - high.astype(jnp.float32)
    middle = rest.astype(jnp.bfloat16)
    return high, middle, (rest - middle.astype(jnp.float32)).astype(jnp.bfloat16)


def polymer_kernel(
    size_x, size_y, size_z, macro_count, chunk_ref, viscous_ref, corner_ref, edge_ref, lines_ref, pick_ref,
    spread_ref, partial_ref, out_ref, flag_ref,
):
    flags = viscous_ref.shape[0]
    macro, core = place_of()
    chunks = chunk_ref[...]
    split = jnp.concatenate((*pieces(chunks), jnp.zeros(chunks.shape, jnp.bfloat16)), axis=0)
    values = jnp.dot(pick_ref[...], split, preferred_element_type=jnp.float32) * lines_ref[2]
    here, beside_z = lines_ref[0], lines_ref[1]
    lane = lanes_of((flags, 128))
    columns = [
        jnp.broadcast_to(
            jnp.sum(jnp.where((lane & 7) == k, values, 0.0), axis=1, keepdims=True), (flags, size_z)
        )
        for k in range(6)
    ]
    stress = viscous_ref[...]
    for k in range(6):
        stress = jnp.where(lane == k, stress + columns[k], stress)
    unused = jnp.zeros((product_depth - 3 * flags, size_z), jnp.float32)
    split = [
        pieces(
            jnp.concatenate(
                [
                    columns[pair_index(a, 0)] * here, columns[pair_index(a, 1)] * here,
                    columns[pair_index(a, 2)] * beside_z, unused,
                ],
                axis=0,
            )
        )
        for a in range(3)
    ]
    flag_ref[...] = stress.T[0:6, :]

    out_ref[...] = partial_ref[...]
    for s in range(2):
        inside = macro > 0 if s == 0 else macro < macro_count - 1
        beside = jnp.maximum(macro - 1, 0) if s == 0 else jnp.minimum(macro + 1, macro_count - 1)
        start = (2 * beside + core) * back_rows
        x = 0 if s == 0 else size_x - 1
        for u in range(2):
            at = x * size_y + (0 if u == 0 else size_y - 1)
            for a in range(2):
                number = 4 * s + 2 * u + a
                line = corner_ref[number : number + 1, :] * chunk_ref[pl.ds(start + 2 * u + a, 1), :]
                out_ref[1 - a, at : at + 1, :] += jnp.where(inside, line, 0.0)
    start = pl.multiple_of((2 * macro + 1 - core) * back_rows, 8)
    packed = chunk_ref[pl.ds(start, back_rows), :]
    end = jnp.where(core == 0, size_z - 1, 0)
    for u in range(2):
        y = 0 if u == 0 else size_y - 1
        for a in range(2):
            for i in range(size_x // 8):
                line = rolled(packed, end - (line_lane + 4 * i + 2 * u + a)) * edge_ref[2 * u + a, 8 * i : 8 * i + 8, :]
                at = pl.ds(8 * i * size_y + y, 8, stride=size_y)
                out_ref[2 - a, at, :] += line
    for a in range(3):
        out_ref[a] += jnp.dot(
            spread_ref[...], jnp.concatenate(split[a], axis=0), preferred_element_type=jnp.float32
        )


def add_polymer(chunks, viscous, corners, edges, lines, pick, spread, partial, shape):
    flags = viscous.shape[0]
    size_x, size_y, size_z = shape
    return pl.pallas_call(
        functools.partial(polymer_kernel, size_x, size_y, size_z, chunks.shape[0] // 2),
        out_shape=(
            jax.ShapeDtypeStruct(partial.shape, jnp.float32),
            jax.ShapeDtypeStruct((6, flags), jnp.float32),
        ),
        in_specs=[VMEM] * 8,
        out_specs=(VMEM, VMEM),
        compiler_params=limit(8),
        cost_estimate=pl.CostEstimate(flops=400000, bytes_accessed=3000000, transcendentals=0),
        name="add_polymer",
    )(chunks.reshape(-1, 128), viscous, corners, edges, lines, pick, spread, partial)


def shards(velocity, viscosity, flag_cell, flag_owner, conformations, increments):
    macro_count = lax.axis_size("macro")
    tile_count = lax.axis_size("tile")
    assert lax.axis_size("micro") == 2
    owner_count = 2 * macro_count
    capacity = conformations.shape[1] // owner_count
    size_x, size_y, size_z = viscosity.shape
    assert capacity <= slot_rows and capacity % 2 == 0 and size_y == 8 and size_z == 128 and size_x % 8 == 0 and size_x <= 48
    chunks, position, viscous, first, second, first_conform, first_noise = gather_rows(
        flag_cell, flag_owner.reshape(-1), velocity, viscosity, conformations, increments, capacity, owner_count
    )

    def exchange(rows):
        return lax.all_to_all(rows, ("macro", "micro"), split_axis=0, concat_axis=0, tiled=True)

    received = exchange(chunks.reshape(owner_count, -1, 128))
    swaps = []
    for start in range(2):
        pairs = [(i, i + 1) for i in range(start, tile_count - 1, 2)]
        swaps.append(pairs + [(high, low) for low, high in pairs])
    first = lax.ppermute(first, "tile", swaps[0])
    second = lax.ppermute(second, "tile", swaps[1])
    last_state, polymer = advance(
        conformations, increments, received, first_conform, first_noise, capacity
    )
    polymer, y_low, y_high, handed = add_lines(polymer, received, first, second)
    returned = exchange(polymer)
    handed = lax.ppermute(handed, "micro", [(0, 1), (1, 0)])
    partial, corners, edges, lines, pick, spread = flow_step(
        flag_cell, position, velocity, viscosity, received, y_low, y_high, handed
    )
    velocity_next, flag_stress = add_polymer(
        returned, viscous, corners, edges, lines, pick, spread, partial, viscosity.shape
    )
    return (velocity_next.reshape(velocity.shape), last_state, flag_stress)


def solution(mesh):
    in_specs = (
        P(None, "macro", "tile", "micro"),
        P("macro", "tile", "micro"),
        P(("macro", "tile", "micro")),
        P(("macro", "tile", "micro"), None),
        P(None, ("macro", "tile", "micro"), None),
        P(None, None, ("macro", "tile", "micro"), None),
    )
    out_specs = (
        P(None, "macro", "tile", "micro"),
        P(None, ("macro", "tile", "micro"), None),
        P(None, ("macro", "tile", "micro")),
    )
    return jax.shard_map(shards, mesh=mesh, in_specs=in_specs, out_specs=out_specs, check_vma=False)
```

```python
import functools

import jax
import jax.numpy as jnp
from jax import lax
from jax.experimental import pallas as pl
from jax.experimental.pallas import tpu as pltpu
from jax.sharding import PartitionSpec as P

stress_pairs = ((0, 0), (1, 1), (2, 2), (0, 1), (0, 2), (1, 2))
macro_step = 0.1
micro_step = 0.01
noise_weight = 0.1
relax_rate = 0.5
fene_extent = 30.0
spring_floor = 0.1
polymer_weight = 0.25

SMEM = pl.BlockSpec(memory_space=pltpu.SMEM)
VMEM = pl.BlockSpec(memory_space=pltpu.VMEM)


def pair_index(left_axis, right_axis):
    return stress_pairs.index((min(left_axis, right_axis), max(left_axis, right_axis)))


def lanes_of(shape):
    return lax.broadcasted_iota(jnp.int32, shape, len(shape) - 1)


slot_rows = 8
chunk_rows = 32
half_face = 28
handed_rows = 48
item_count = 7
back_rows = 8
polymer_row = 4


block_slots = 32
first_share = 2


def limit(mebibytes):
    return pltpu.CompilerParams(vmem_limit_bytes=mebibytes * 1024 * 1024)


def far(value):
    return pltpu.with_memory_space_constraint(value, pltpu.HBM)


def place_of():
    return lax.axis_index("macro"), lax.axis_index("micro")


def neighbour(index, side, count):
    return jnp.maximum(index - 1, 0) if side == 0 else jnp.minimum(index + 1, count - 1)


def rolled(value, amount):
    size = value.shape[-1]
    if isinstance(amount, int):
        return pltpu.roll(value, amount % size, value.ndim - 1)
    return pltpu.roll(value, lax.rem(amount + 2 * size, size), value.ndim - 1)


def gather_kernel(
    capacity, size_x, size_y, size_z, macro_count, cell_in, owner_in, velocity_in, viscosity_in,
    conform_in, noise_in, chunk_ref, position_ref, viscous_ref, first_ref, second_ref, conform_ref, noise_ref,
    cell_ref, owner_ref, velocity_ref, viscosity_ref, masked, gradients, paired, target, count, sems,
):
    flags = cell_ref.shape[0]
    copies = [
        pltpu.make_async_copy(source, into, sems.at[number])
        for number, (source, into) in enumerate(
            (
                (cell_in, cell_ref), (owner_in, owner_ref), (velocity_in, velocity_ref),
                (viscosity_in, viscosity_ref), (conform_in.at[:, 0:block_slots, :], conform_ref),
                (noise_in.at[0 : noise_ref.shape[0], :, 0:block_slots, :], noise_ref),
            )
        )
    ]
    for copy in copies:
        copy.start()
    paired_rows = paired.shape[0] // 2
    macro, core = place_of()
    lane = lanes_of((1, size_z))

    for owner in range(count.shape[0]):
        count[owner] = 0
    paired[...] = jnp.zeros_like(paired)
    for copy in copies[:2]:
        copy.wait()
    for j in range(flags):
        owner = owner_ref[j]
        rank = count[owner]
        count[owner] = rank + 1
        target[j] = (rank & 1) * paired_rows + owner * (slot_rows // 2) + lax.shift_right_logical(rank, 1)
        position_ref[j] = owner * slot_rows + rank
    for copy in copies[2:4]:
        copy.wait()
    planes = velocity_ref.reshape(3, size_x, size_y, size_z)
    layers = viscosity_ref.reshape(size_x, size_y, size_z)
    for j in range(flags):
        cell = cell_ref[j]
        x = lax.shift_right_logical(cell, 10)
        y = lax.shift_right_logical(cell, 7) & (size_y - 1)
        z = cell & (size_z - 1)
        here = (lane == z).astype(jnp.float32)
        along_z = (lane == z + 1).astype(jnp.float32) - (lane == z - 1).astype(jnp.float32)
        at = pl.ds(y, 1)
        for a in range(3):
            along_x = planes[a, x + 1, at, :] - planes[a, x - 1, at, :]
            along_y = planes[a, x, pl.ds(y + 1, 1), :] - planes[a, x, pl.ds(y - 1, 1), :]
            masked[3 * a, j : j + 1, :] = along_x * here
            masked[3 * a + 1, j : j + 1, :] = along_y * here
            masked[3 * a + 2, j : j + 1, :] = planes[a, x, at, :] * along_z
        masked[9, j : j + 1, :] = layers[x, at, :] * here

    even = lax.axis_index("tile") & 1 == 0

    def put(number, ref, low, high):
        rows = [ref[pl.ds(y, size_x, stride=size_y), :] for y in (low, high)]
        first_ref[number] = jnp.where(even, rows[1], rows[0])
        second_ref[number] = jnp.where(even, rows[0], rows[1])

    for layer in range(2):
        for a in range(3):
            put(3 * layer + a, velocity_ref.at[a], layer, size_y - 1 - layer)
    put(6, viscosity_ref, 0, size_y - 1)

    for side in range(2):
        beside = neighbour(macro, side, macro_count)
        for layer, owner in enumerate((2 * beside + core, 2 * beside + 1 - core)):
            start = pl.multiple_of(owner * chunk_rows, 8)
            x = layer if side == 0 else size_x - 1 - layer
            for a in range(3):
                chunk_ref[pl.ds(start + a * size_y, size_y), :] = velocity_ref[a, x * size_y : (x + 1) * size_y, :]
            x = 0 if side == 0 else size_x - 1
            half = x * size_y + layer * (size_y // 2)
            chunk_ref[pl.ds(start + 3 * size_y, size_y // 2), :] = viscosity_ref[half : half + size_y // 2, :]

    group = size_z // 8
    lane2 = lanes_of((size_y, size_z))
    first = pl.multiple_of((2 * macro + 1 - core) * chunk_rows, 8)
    source = jnp.where(core == 0, size_z - 2, 0)
    for block in range(-(-size_x // group)):
        total = jnp.zeros((size_y, size_z), jnp.float32)
        for x in range(block * group, min(size_x, (block + 1) * group)):
            rows = slice(x * size_y, (x + 1) * size_y)
            for a in range(4):
                at = 8 * (x - block * group) + 2 * a
                value = viscosity_ref[rows, :] if a == 3 else velocity_ref[a, rows, :]
                total = jnp.where((lane2 == at) | (lane2 == at + 1), rolled(value, at - source), total)
        chunk_ref[pl.ds(first + block * size_y, size_y), :] = total

    columns = [0.5 * jnp.sum(masked[c], axis=1, keepdims=True) for c in range(9)]
    viscous = jnp.sum(masked[9], axis=1, keepdims=True)
    wide = lanes_of((flags, 128))
    packed = jnp.zeros((flags, 128), jnp.float32)
    for c in range(9):
        packed = jnp.where(wide == c, columns[c], packed)
    gradients[...] = packed
    stress = jnp.zeros((flags, 128), jnp.float32)
    for k, (a, b) in enumerate(stress_pairs):
        stress = jnp.where(wide == k, viscous * (columns[3 * a + b] + columns[3 * b + a]), stress)
    viscous_ref[...] = stress

    for j in range(flags):
        paired[pl.ds(target[j], 1), :] = gradients[j : j + 1, :]
    rows = paired[0:paired_rows, :] + rolled(paired[paired_rows:, :], 64)
    for owner in range(count.shape[0]):
        chunk_ref[owner * chunk_rows + half_face : (owner + 1) * chunk_rows, :] = rows[
            owner * (slot_rows // 2) : (owner + 1) * (slot_rows // 2)
        ]
    for copy in copies[4:]:
        copy.wait()


def gather_rows(flag_cell, owner, velocity, viscosity, conformations, increments, capacity, owner_count):
    size_x, size_y, size_z = viscosity.shape
    flags = flag_cell.shape[0]
    face = jax.ShapeDtypeStruct((item_count, size_x, size_z), jnp.float32)
    steps, _, _, dumbbells = increments.shape
    return pl.pallas_call(
        functools.partial(gather_kernel, capacity, size_x, size_y, size_z, owner_count // 2),
        out_shape=(
            jax.ShapeDtypeStruct((owner_count * chunk_rows, 128), jnp.float32),
            jax.ShapeDtypeStruct((flags,), jnp.int32),
            jax.ShapeDtypeStruct((flags, 128), jnp.float32),
            face,
            face,
            pltpu.VMEM((3, block_slots, dumbbells), jnp.float32),
            pltpu.VMEM((steps // first_share, 3, block_slots, dumbbells), jnp.bfloat16),
        ),
        in_specs=[pl.BlockSpec(memory_space=pltpu.HBM)] * 6,
        out_specs=(VMEM, SMEM, VMEM, VMEM, VMEM, VMEM, VMEM),
        scratch_shapes=[
            pltpu.SMEM((flags,), jnp.int32),
            pltpu.SMEM((flags,), jnp.int32),
            pltpu.VMEM((3, size_x * size_y, size_z), jnp.float32),
            pltpu.VMEM((size_x * size_y, size_z), jnp.float32),
            pltpu.VMEM((10, flags, size_z), jnp.float32),
            pltpu.VMEM((flags, 128), jnp.float32),
            pltpu.VMEM((owner_count * slot_rows, 128), jnp.float32),
            pltpu.SMEM((flags,), jnp.int32),
            pltpu.SMEM((owner_count,), jnp.int32),
            pltpu.SemaphoreType.DMA((6,)),
        ],
        compiler_params=limit(8),
        cost_estimate=pl.CostEstimate(flops=400000, bytes_accessed=3000000, transcendentals=0),
        name="gather_rows",
    )(
        far(flag_cell),
        far(owner),
        far(velocity.reshape(3, size_x * size_y, size_z)),
        far(viscosity.reshape(size_x * size_y, size_z)),
        far(conformations),
        far(increments),
    )


def micro_kernel(
    capacity, parts, rows, groups, conform_ref, noise_ref, rate_ref, first_conform_ref, first_noise_ref,
    next_ref, chunk_ref, conform, noise, rate, rate_wide, sums_ref, read_sem, noise_sem,
):
    steps, _, slots, dumbbells = noise_ref.shape
    blocks = slots // rows
    span = steps // groups
    width = dumbbells // parts
    owners = slots // capacity
    scale = 1.0 / noise_weight
    extent = fene_extent * scale * scale

    def block_rows(block):
        return pl.ds(pl.multiple_of(block * rows, rows), rows)

    def read(block):
        at = block_rows(block)
        return pltpu.make_async_copy(conform_ref.at[:, at, :], conform.at[:, at, :], read_sem.at[block])

    def read_noise(block, group):
        at, when = block_rows(block), pl.ds(group * span, span)
        return pltpu.make_async_copy(
            noise_ref.at[when, :, at, :], noise.at[when, :, at, :], noise_sem.at[block, group]
        )

    pieces = [
        (half, slice(part * width, (part + 1) * width)) for half in range(rows // 16) for part in range(parts)
    ]
    assert len(pieces) == 8
    early = groups // first_share
    for block in range(blocks):
        if block > 0:
            read(block).start()
        for group in range(early if block == 0 else 0, groups):
            read_noise(block, group).start()
    conform[:, 0:rows, :] = first_conform_ref[...]
    for step in range(steps // first_share):
        noise[step, :, 0:rows, :] = first_noise_ref[step]
    for owner in range(owners):
        packed = rate_ref[owner, half_face : half_face + capacity // 2, :]
        rate[pl.ds(owner * capacity, capacity // 2, stride=2), :] = packed
        rate[pl.ds(owner * capacity + 1, capacity // 2, stride=2), :] = rolled(packed, 64)
        chunk_ref[owner] = jnp.zeros(chunk_ref.shape[1:], jnp.float32)
    for a in range(3):
        for b in range(3):
            column = micro_step * rate[:, 3 * a + b : 3 * a + b + 1] + (1.0 if a == b else 0.0)
            rate_wide[3 * a + b] = jnp.broadcast_to(column, (slots, width))

    def inverses(state, scale):
        rooms = []
        for piece in range(len(pieces)):
            q = state[3 * piece : 3 * piece + 3]
            room = (extent - q[0] * q[0]) - (q[1] * q[1] + q[2] * q[2])
            rooms.append(jnp.maximum(room, extent * spring_floor))
        levels = [rooms]
        while len(levels[-1]) > 1:
            levels.append([low * high for low, high in zip(levels[-1][0::2], levels[-1][1::2])])
        result = [scale * pl.reciprocal(levels[-1][0])]
        for level in reversed(levels[:-1]):
            result = [result[i // 2] * level[i ^ 1] for i in range(len(level))]
        return result

    def advance_block(block, carry):
        ats = [pl.ds(pl.multiple_of(block * rows + 16 * half, 16), 16) for half in range(rows // 16)]
        rates = [
            [[rate_wide.at[3 * a + b, at, :] for b in range(3)] for a in range(3)] for at in ats
        ]

        def substep(step, state):
            updated = []
            springs = inverses(state, micro_step * relax_rate * extent)
            for piece, (half, lanes) in enumerate(pieces):
                q = state[3 * piece : 3 * piece + 3]
                table = rates[half]
                for a in range(3):
                    b, c = [other for other in range(3) if other != a]
                    kick = noise[step, a, ats[half], lanes].astype(jnp.float32)
                    rest = (table[a][b][...] * q[b] + table[a][c][...] * q[c]) + kick
                    updated.append((table[a][a][...] - springs[piece]) * q[a] + rest)
            return tuple(updated)

        def advance_group(group, state):
            if group < early:

                @pl.when(block > 0)
                def _():
                    read_noise(block, group).wait()

            else:
                read_noise(block, group).wait()
            for step in range(span):
                state = substep(group * span + step, state)
            return state

        @pl.when(block > 0)
        def _():
            read(block).wait()

        state = tuple(conform[a, ats[half], lanes] * scale for half, lanes in pieces for a in range(3))
        for group in range(groups):
            state = advance_group(group, state)
        inverse = inverses(state, 1.0)
        for half, at in enumerate(ats):
            sums = [None] * 6
            for piece, (other, lanes) in enumerate(pieces):
                if other != half:
                    continue
                q = state[3 * piece : 3 * piece + 3]
                for a in range(3):
                    next_ref[a, at, lanes] = q[a] * noise_weight
                for k, (a, b) in enumerate(stress_pairs):
                    term = (inverse[piece] * q[a]) * q[b]
                    sums[k] = term if sums[k] is None else sums[k] + term
            for k in range(6):
                sums_ref[k, at, :] = sums[k]
        return carry

    lax.fori_loop(0, blocks, advance_block, 0)
    lane = lanes_of((slots, 128))
    rank = lax.broadcasted_iota(jnp.int32, (slots, 128), 0) & (capacity - 1)
    packed = jnp.zeros((slots, 128), jnp.float32)
    weight = extent * noise_weight * noise_weight / dumbbells
    for k, (a, b) in enumerate(stress_pairs):
        mean = jnp.sum(sums_ref[k], axis=1, keepdims=True) * weight
        packed = jnp.where(lane == 8 * rank + k, polymer_weight * (mean - (1.0 if a == b else 0.0)), packed)
    for owner in range(owners):
        chunk_ref[owner, polymer_row : polymer_row + 1, :] = jnp.sum(
            packed[owner * capacity : (owner + 1) * capacity], axis=0, keepdims=True
        )


def advance(conformations, increments, chunks, first_conform, first_noise, capacity):
    slots, dumbbells = conformations.shape[1:]
    steps = increments.shape[0]
    owners = slots // capacity
    rows, parts, groups = block_slots, 4, 4
    blocks = slots // rows
    whole = pl.BlockSpec(memory_space=pltpu.HBM)
    return pl.pallas_call(
        functools.partial(micro_kernel, capacity, parts, rows, groups),
        out_shape=(
            pltpu.VMEM(conformations.shape, jnp.float32),
            jax.ShapeDtypeStruct((owners, back_rows, 128), jnp.float32),
        ),
        in_specs=[whole, whole, VMEM, VMEM, VMEM],
        out_specs=(VMEM, VMEM),
        scratch_shapes=[
            pltpu.VMEM(conformations.shape, jnp.float32),
            pltpu.VMEM(increments.shape, jnp.bfloat16),
            pltpu.VMEM((slots, 128), jnp.float32),
            pltpu.VMEM((9, slots, dumbbells // parts), jnp.float32),
            pltpu.VMEM((6, slots, dumbbells // parts), jnp.float32),
            pltpu.SemaphoreType.DMA((blocks,)),
            pltpu.SemaphoreType.DMA((blocks, groups)),
        ],
        compiler_params=limit(12),
        cost_estimate=pl.CostEstimate(flops=20000000, bytes_accessed=5000000, transcendentals=600000),
        name="advance",
    )(far(conformations), far(increments), chunks, first_conform, first_noise)


def lines_kernel(
    macro_count, chunk_ref, received_ref, first_ref, second_ref, out_ref, y_low_ref, y_high_ref, handed_ref
):
    out_ref[...] = chunk_ref[...]
    macro, core = place_of()
    for side in range(2):
        beside = neighbour(macro, side, macro_count)
        handed_ref[side, 0:chunk_rows, :] = received_ref[2 * beside + 1 - core]
        for number, a in enumerate((0, 2)):
            handed_ref[side, chunk_rows + number * 8 : chunk_rows + (number + 1) * 8, :] = received_ref[
                2 * beside + core, a * 8 : (a + 1) * 8, :
            ]
    even = lax.axis_index("tile") & 1 == 0
    y_low_ref[...] = jnp.where(even, second_ref[...], first_ref[...])
    y_high_ref[...] = jnp.where(even, first_ref[...], second_ref[...])
    sides = (y_low_ref, y_high_ref)
    size_x, size_z = y_low_ref.shape[1:]
    for side in range(2):
        beside = neighbour(macro, side, macro_count)
        x = 0 if side == 0 else size_x - 1
        for u in range(2):
            for a in range(2):
                at = 2 * u + a
                out_ref[2 * beside + core, at : at + 1, :] = sides[u][a, x : x + 1, :]

    for u in range(2):
        for number in range(2):
            start = handed_rows + number * size_x
            handed_ref[u, start : start + size_x, :] = sides[u][1 + number]


def add_lines(chunks, received, first, second):
    face = jax.ShapeDtypeStruct(first.shape, jnp.float32)
    return pl.pallas_call(
        functools.partial(lines_kernel, chunks.shape[0] // 2),
        out_shape=(
            jax.ShapeDtypeStruct(chunks.shape, jnp.float32), face, face,
            jax.ShapeDtypeStruct((2, handed_rows + 2 * first.shape[1], 128), jnp.float32),
        ),
        in_specs=[VMEM] * 4,
        out_specs=(VMEM,) * 4,
        compiler_params=limit(4),
        cost_estimate=pl.CostEstimate(flops=20000, bytes_accessed=400000, transcendentals=0),
        name="add_lines",
    )(chunks, received, first, second)


product_depth = 128


def one_hots(size_y, size_z, cell_ref, position_ref, lines_ref, pick_ref, spread_ref, rows):
    flags = cell_ref.shape[0]
    weight = 0.5 * macro_step
    row_count = spread_ref.shape[0]
    returned = pick_ref.shape[1] // 4
    lane = lanes_of((1, size_z))
    row_lane = lanes_of((1, rows.shape[1]))
    slot_lane = lanes_of((flags, returned))
    flag_row = lax.broadcasted_iota(jnp.int32, (flags, returned), 0)
    rows[3 * flags :, :] = jnp.zeros((product_depth - 3 * flags, rows.shape[1]), jnp.float32)
    slot = jnp.zeros((flags, returned), jnp.int32)
    group = lax.shift_right_logical(lane, 3)
    for j in range(flags):
        cell = cell_ref[j]
        row = lax.div(cell, size_z)
        z = cell - row * size_z
        lines_ref[0, j : j + 1, :] = jnp.where(lane == z, weight, 0.0)
        lines_ref[1, j : j + 1, :] = jnp.where(
            lane == z - 1, weight, jnp.where(lane == z + 1, -weight, 0.0)
        )
        for number, shift in enumerate((size_y, 1)):
            rows[number * flags + j : number * flags + j + 1, :] = jnp.where(
                row_lane == row - shift, 1.0, jnp.where(row_lane == row + shift, -1.0, 0.0)
            )
        rows[2 * flags + j : 2 * flags + j + 1, :] = jnp.where(row_lane == row, 1.0, 0.0)
        owner = lax.div(position_ref[j], slot_rows)
        rank = position_ref[j] - owner * slot_rows
        lines_ref[2, j : j + 1, :] = jnp.where(group == rank, 1.0, 0.0)
        slot = jnp.where(flag_row == j, owner * back_rows + polymer_row, slot)
    spread = rows[...].T[:row_count].astype(jnp.bfloat16)
    pick = jnp.where(slot_lane == slot, 1.0, 0.0).astype(jnp.bfloat16)
    for piece in range(3):
        spread_ref[:, piece * product_depth : (piece + 1) * product_depth] = spread
        pick_ref[:, piece * returned : (piece + 1) * returned] = pick
    pick_ref[:, 3 * returned :] = jnp.zeros((flags, returned), jnp.bfloat16)


def flow_kernel(
    size_x, size_y, size_z, macro_count, cell_ref, position_ref, velocity_ref, viscosity_ref, chunk_ref,
    y_low_ref, y_high_ref, handed_ref, out_ref, corner_ref, lines_ref, pick_ref, spread_ref,
    padded, stress_x, stress_rest, faces, ghost_y, ghost_z, rows, halves, beyond,
):
    macro, core = place_of()
    one_hots(size_y, size_z, cell_ref, position_ref, lines_ref, pick_ref, spread_ref, rows)
    inside = (macro > 0, macro < macro_count - 1)
    sign_z = jnp.where(core == 0, 1.0, -1.0)
    end = jnp.where(core == 0, size_z - 1, 0)
    shape = (size_y, size_z)
    lane, row = lanes_of(shape), lax.broadcasted_iota(jnp.int32, shape, 0)
    at_end = jnp.where(lane == end, sign_z, 0.0)

    def kept(value, condition):
        return jnp.where(condition, value, 0.0)

    def plane(x):
        return pl.ds(pl.multiple_of(x * size_y, 8), size_y)

    def difference_z(value):
        lane = lanes_of(value.shape)
        return jnp.where(lane == size_z - 1, 0.0, rolled(value, -1)) - jnp.where(
            lane == 0, 0.0, rolled(value, 1)
        )

    def difference_rows(value, low=0.0, high=0.0):
        count = value.shape[0]
        row = lax.broadcasted_iota(jnp.int32, value.shape, 0)
        return jnp.where(row == count - 1, high, pltpu.roll(value, count - 1, 0)) - jnp.where(
            row == 0, low, pltpu.roll(value, 1, 0)
        )

    x_faces, x_others = [], []
    half = size_y // 2
    for s in range(2):
        beside = neighbour(macro, s, macro_count)
        outer = chunk_ref[2 * beside + core]
        items = [outer[i * size_y : (i + 1) * size_y] for i in range(3)]
        items += [handed_ref[s, i * size_y : (i + 1) * size_y, :] for i in range(3)]
        halves[s, 0:half, :] = chunk_ref[2 * beside + core, 3 * size_y : 3 * size_y + half, :]
        halves[s, half:, :] = handed_ref[s, 3 * size_y : 3 * size_y + half, :]
        items.append(halves[s])
        x_faces.append([kept(item, inside[s]) for item in items])
        corners = [handed_ref[s, chunk_rows + i * size_y : chunk_rows + (i + 1) * size_y, :] for i in range(2)]
        x_others.append([kept(rolled(corner, 2 * end + 1), inside[s]) for corner in corners])

    y_others = []
    for u in range(2):
        start = handed_rows + size_x
        y_others.append(rolled(handed_ref[u, handed_rows:start, :], 2 * end + 1))
        beyond[u] = rolled(handed_ref[u, start : start + size_x, :], 2 * end + 1)

    group = size_z // 8
    packed = [
        chunk_ref[2 * macro + 1 - core, i * size_y : (i + 1) * size_y, :]
        for i in range(-(-size_x // group))
    ]
    for i, value in enumerate(packed):

        def unpack(x, carry):
            for q in range(item_count):
                a, layer = (q, 0) if q < 4 else (q - 4, 1)
                at = 8 * (x - i * group) + 2 * a + (core if layer == 0 else 1 - core)
                faces[q, x + 1] = rolled(value, end - at)
            return carry

        lax.fori_loop(i * group, min(size_x, (i + 1) * group), unpack, 0, unroll=8)
    faces[2, 0] = x_others[0][1]
    faces[2, size_x + 1] = x_others[1][1]

    for a in range(3):
        padded[a, 0] = x_faces[0][a]
        padded[a, size_x + 1] = x_faces[1][a]

    def fill(x, carry):
        for a in range(3):
            padded[a, x + 1] = velocity_ref[a, plane(x), :]
        return carry

    lax.fori_loop(0, size_x, fill, 0, unroll=True)

    rest = {(1, 1): 0, (2, 2): 1, (1, 2): 2}

    def stress_plane(x, carry):
        along_x, along_y, along_z, centre = [], [], [], []
        for a in range(3):
            value = padded[a, x + 1]
            centre.append(value)
            along_x.append(padded[a, x + 2] - padded[a, x])
            along_y.append(
                difference_rows(value, y_low_ref[a, pl.ds(x, 1), :], y_high_ref[a, pl.ds(x, 1), :])
            )
            along_z.append(difference_z(value) + faces[a, x + 1] * at_end)
        slopes = (along_x, along_y, along_z)
        half = 0.5 * viscosity_ref[plane(x), :]
        for a, b in stress_pairs:
            value = half * (slopes[b][a] + slopes[a][b])
            if a == 0:
                stress_x[b, x + 1] = value
            else:
                stress_rest[rest[a, b], x] = value
        weight = (0.5 * faces[3, x + 1]) * at_end
        normal = [(faces[4 + a, x + 1] - centre[a]) * sign_z for a in range(3)]
        ghost_z[0, x] = weight * (normal[0] + (faces[2, x + 2] - faces[2, x]))
        slope = difference_rows(faces[2, x + 1], beyond[0, pl.ds(x, 1), :], beyond[1, pl.ds(x, 1), :])
        ghost_z[1, x] = weight * (normal[1] + slope)
        ghost_z[2, x] = weight * (2.0 * normal[2])
        return carry

    lax.fori_loop(0, size_x, stress_plane, 0, unroll=6)

    for s in range(2):
        near, far, weight = x_faces[s][0:3], x_faces[s][3:6], 0.5 * x_faces[s][6]
        sign = -1.0 if s == 0 else 1.0
        normal = [(far[a] - padded[a, 1 if s == 0 else size_x]) * sign for a in range(3)]
        slope_y = difference_rows(near[0])
        slope_z = difference_z(near[0]) + x_others[s][0] * at_end
        at = 0 if s == 0 else size_x + 1
        stress_x[0, at] = weight * (2.0 * normal[0])
        stress_x[1, at] = weight * (normal[1] + slope_y)
        stress_x[2, at] = weight * (normal[2] + slope_z)
        for u in range(2):
            y, sign_y = (0, -1.0) if u == 0 else (size_y - 1, 1.0)
            number = 4 * s + 2 * u
            corner_ref[number : number + 1, :] = (0.5 * macro_step * sign * sign_y) * weight[y : y + 1, :]

    for u, ref in enumerate((y_low_ref, y_high_ref)):
        y, sign = (0, -1.0) if u == 0 else (size_y - 1, 1.0)
        weight = 0.5 * ref[6]
        normal = [
            (ref[3 + a] - velocity_ref[a, pl.ds(y, size_x, stride=size_y), :]) * sign for a in range(3)
        ]
        ghost_y[3 * u] = weight * (normal[0] + difference_rows(ref[1]))
        ghost_y[3 * u + 1] = weight * (2.0 * normal[1])
        wide = lanes_of((size_x, size_z))
        across = jnp.where(wide == end, y_others[u] * sign_z, 0.0)
        ghost_y[3 * u + 2] = weight * (normal[2] + (difference_z(ref[1]) + across))
        for s in range(2):
            x, sign_x = (0, -1.0) if s == 0 else (size_x - 1, 1.0)
            number = 4 * s + 2 * u + 1
            corner_ref[number : number + 1, :] = (0.5 * macro_step * sign * sign_x) * weight[x : x + 1, :]

    columns = {(0, 1): (stress_x, 1, 1), (1, 1): (stress_rest, 0, 0), (2, 1): (stress_rest, 2, 0)}
    columns_z = {0: (stress_x, 2, 1), 1: (stress_rest, 2, 0), 2: (stress_rest, 1, 0)}

    def step_plane(x, carry):
        for a in range(3):
            total = stress_x[a, x + 2] - stress_x[a, x]
            ref, number, shift = columns[a, 1]
            total = total + difference_rows(
                ref[number, x + shift], ghost_y[a, pl.ds(x, 1), :], ghost_y[3 + a, pl.ds(x, 1), :]
            )
            ref, number, shift = columns_z[a]
            total = total + (difference_z(ref[number, x + shift]) + ghost_z[a, x])
            out_ref[a, plane(x), :] = padded[a, x + 1] + (0.5 * macro_step) * total
        return carry

    lax.fori_loop(0, size_x, step_plane, 0, unroll=6)


def flow_step(flag_cell, position, velocity, viscosity, chunks, y_low, y_high, handed):
    size_x, size_y, size_z = viscosity.shape
    flags = flag_cell.shape[0]
    returned = chunks.shape[0] * back_rows
    row_count = size_x * size_y
    planes = (size_x, size_y, size_z)
    wide = (size_x + 2, size_y, size_z)
    return pl.pallas_call(
        functools.partial(flow_kernel, size_x, size_y, size_z, chunks.shape[0] // 2),
        out_shape=(
            jax.ShapeDtypeStruct((3, size_x * size_y, size_z), jnp.float32),
            jax.ShapeDtypeStruct((8, size_z), jnp.float32),
            jax.ShapeDtypeStruct((3, flags, size_z), jnp.float32),
            jax.ShapeDtypeStruct((flags, 4 * returned), jnp.bfloat16),
            jax.ShapeDtypeStruct((row_count, 3 * product_depth), jnp.bfloat16),
        ),
        in_specs=[SMEM] * 2 + [VMEM] * 6,
        out_specs=(VMEM,) * 5,
        scratch_shapes=[
            pltpu.VMEM((3, *wide), jnp.float32),
            pltpu.VMEM((3, *wide), jnp.float32),
            pltpu.VMEM((3, *planes), jnp.float32),
            pltpu.VMEM((item_count, *wide), jnp.float32),
            pltpu.VMEM((6, size_x, size_z), jnp.float32),
            pltpu.VMEM((3, *planes), jnp.float32),
            pltpu.VMEM((product_depth, -(-row_count // 128) * 128), jnp.float32),
            pltpu.VMEM((2, size_y, size_z), jnp.float32),
            pltpu.VMEM((2, size_x, size_z), jnp.float32),
        ],
        compiler_params=limit(12),
        cost_estimate=pl.CostEstimate(flops=4000000, bytes_accessed=3000000, transcendentals=0),
        name="flow_step",
    )(
        flag_cell, position,
        velocity.reshape(3, size_x * size_y, size_z),
        viscosity.reshape(size_x * size_y, size_z),
        chunks, y_low, y_high, handed,
    )


def pieces(value):
    high = value.astype(jnp.bfloat16)
    rest = value - high.astype(jnp.float32)
    middle = rest.astype(jnp.bfloat16)
    return high, middle, (rest - middle.astype(jnp.float32)).astype(jnp.bfloat16)


def polymer_kernel(
    size_x, size_y, size_z, macro_count, chunk_ref, viscous_ref, corner_ref, lines_ref, pick_ref,
    spread_ref, partial_ref, out_ref, flag_ref,
):
    flags = viscous_ref.shape[0]
    macro, core = place_of()
    chunks = chunk_ref[...]
    split = jnp.concatenate((*pieces(chunks), jnp.zeros(chunks.shape, jnp.bfloat16)), axis=0)
    values = jnp.dot(pick_ref[...], split, preferred_element_type=jnp.float32) * lines_ref[2]
    here, beside_z = lines_ref[0], lines_ref[1]
    lane = lanes_of((flags, 128))
    columns = [
        jnp.broadcast_to(
            jnp.sum(jnp.where((lane & 7) == k, values, 0.0), axis=1, keepdims=True), (flags, size_z)
        )
        for k in range(6)
    ]
    stress = viscous_ref[...]
    for k in range(6):
        stress = jnp.where(lane == k, stress + columns[k], stress)
    unused = jnp.zeros((product_depth - 3 * flags, size_z), jnp.float32)
    split = [
        pieces(
            jnp.concatenate(
                [
                    columns[pair_index(a, 0)] * here, columns[pair_index(a, 1)] * here,
                    columns[pair_index(a, 2)] * beside_z, unused,
                ],
                axis=0,
            )
        )
        for a in range(3)
    ]
    flag_ref[...] = stress.T[0:6, :]

    out_ref[...] = partial_ref[...]
    for s in range(2):
        inside = macro > 0 if s == 0 else macro < macro_count - 1
        beside = jnp.maximum(macro - 1, 0) if s == 0 else jnp.minimum(macro + 1, macro_count - 1)
        start = (2 * beside + core) * back_rows
        x = 0 if s == 0 else size_x - 1
        for u in range(2):
            at = x * size_y + (0 if u == 0 else size_y - 1)
            for a in range(2):
                number = 4 * s + 2 * u + a
                line = corner_ref[number : number + 1, :] * chunk_ref[pl.ds(start + 2 * u + a, 1), :]
                out_ref[1 - a, at : at + 1, :] += jnp.where(inside, line, 0.0)
    for a in range(3):
        out_ref[a] += jnp.dot(
            spread_ref[...], jnp.concatenate(split[a], axis=0), preferred_element_type=jnp.float32
        )


def add_polymer(chunks, viscous, corners, lines, pick, spread, partial, shape):
    flags = viscous.shape[0]
    size_x, size_y, size_z = shape
    return pl.pallas_call(
        functools.partial(polymer_kernel, size_x, size_y, size_z, chunks.shape[0] // 2),
        out_shape=(
            jax.ShapeDtypeStruct(partial.shape, jnp.float32),
            jax.ShapeDtypeStruct((6, flags), jnp.float32),
        ),
        in_specs=[VMEM] * 7,
        out_specs=(VMEM, VMEM),
        compiler_params=limit(8),
        cost_estimate=pl.CostEstimate(flops=400000, bytes_accessed=3000000, transcendentals=0),
        name="add_polymer",
    )(chunks.reshape(-1, 128), viscous, corners, lines, pick, spread, partial)


def shards(velocity, viscosity, flag_cell, flag_owner, conformations, increments):
    macro_count = lax.axis_size("macro")
    tile_count = lax.axis_size("tile")
    assert lax.axis_size("micro") == 2
    owner_count = 2 * macro_count
    capacity = conformations.shape[1] // owner_count
    size_x, size_y, size_z = viscosity.shape
    assert capacity <= slot_rows and capacity % 2 == 0 and size_y == 8 and size_z == 128 and size_x % 8 == 0 and size_x <= 48
    chunks, position, viscous, first, second, first_conform, first_noise = gather_rows(
        flag_cell, flag_owner.reshape(-1), velocity, viscosity, conformations, increments, capacity, owner_count
    )

    def exchange(rows):
        return lax.all_to_all(rows, ("macro", "micro"), split_axis=0, concat_axis=0, tiled=True)

    received = exchange(chunks.reshape(owner_count, -1, 128))
    swaps = []
    for start in range(2):
        pairs = [(i, i + 1) for i in range(start, tile_count - 1, 2)]
        swaps.append(pairs + [(high, low) for low, high in pairs])
    first = lax.ppermute(first, "tile", swaps[0])
    second = lax.ppermute(second, "tile", swaps[1])
    last_state, polymer = advance(
        conformations, increments, received, first_conform, first_noise, capacity
    )
    polymer, y_low, y_high, handed = add_lines(polymer, received, first, second)
    returned = exchange(polymer)
    handed = lax.ppermute(handed, "micro", [(0, 1), (1, 0)])
    partial, corners, lines, pick, spread = flow_step(
        flag_cell, position, velocity, viscosity, received, y_low, y_high, handed
    )
    velocity_next, flag_stress = add_polymer(
        returned, viscous, corners, lines, pick, spread, partial, viscosity.shape
    )
    return (velocity_next.reshape(velocity.shape), last_state, flag_stress)


def solution(mesh):
    in_specs = (
        P(None, "macro", "tile", "micro"),
        P("macro", "tile", "micro"),
        P(("macro", "tile", "micro")),
        P(("macro", "tile", "micro"), None),
        P(None, ("macro", "tile", "micro"), None),
        P(None, None, ("macro", "tile", "micro"), None),
    )
    out_specs = (
        P(None, "macro", "tile", "micro"),
        P(None, ("macro", "tile", "micro"), None),
        P(None, ("macro", "tile", "micro")),
    )
    return jax.shard_map(shards, mesh=mesh, in_specs=in_specs, out_specs=out_specs, check_vma=False)
```

```python
import functools

import jax
import jax.numpy as jnp
from jax import lax
from jax.experimental import pallas as pl
from jax.experimental.pallas import tpu as pltpu
from jax.sharding import PartitionSpec as P

stress_pairs = ((0, 0), (1, 1), (2, 2), (0, 1), (0, 2), (1, 2))
macro_step = 0.1
micro_step = 0.01
noise_weight = 0.1
relax_rate = 0.5
fene_extent = 30.0
spring_floor = 0.1
polymer_weight = 0.25

SMEM = pl.BlockSpec(memory_space=pltpu.SMEM)
VMEM = pl.BlockSpec(memory_space=pltpu.VMEM)


def pair_index(left_axis, right_axis):
    return stress_pairs.index((min(left_axis, right_axis), max(left_axis, right_axis)))


def lanes_of(shape):
    return lax.broadcasted_iota(jnp.int32, shape, len(shape) - 1)


slot_rows = 8
chunk_rows = 32
half_face = 28
handed_rows = 48
item_count = 7
back_rows = 8
polymer_row = 4


block_slots = 32
first_share = 2


def limit(mebibytes):
    return pltpu.CompilerParams(vmem_limit_bytes=mebibytes * 1024 * 1024)


def far(value):
    return pltpu.with_memory_space_constraint(value, pltpu.HBM)


def place_of():
    return lax.axis_index("macro"), lax.axis_index("micro")


def neighbour(index, side, count):
    return jnp.maximum(index - 1, 0) if side == 0 else jnp.minimum(index + 1, count - 1)


def rolled(value, amount):
    size = value.shape[-1]
    if isinstance(amount, int):
        return pltpu.roll(value, amount % size, value.ndim - 1)
    return pltpu.roll(value, lax.rem(amount + 2 * size, size), value.ndim - 1)


def gather_kernel(
    capacity, size_x, size_y, size_z, macro_count, cell_in, owner_in, velocity_in, viscosity_in,
    conform_in, noise_in, chunk_ref, position_ref, viscous_ref, first_ref, second_ref, conform_ref, noise_ref,
    cell_ref, owner_ref, velocity_ref, viscosity_ref, masked, gradients, paired, target, count, sems,
):
    flags = cell_ref.shape[0]
    copies = [
        pltpu.make_async_copy(source, into, sems.at[number])
        for number, (source, into) in enumerate(
            (
                (cell_in, cell_ref), (owner_in, owner_ref), (velocity_in, velocity_ref),
                (viscosity_in, viscosity_ref), (conform_in.at[:, 0:block_slots, :], conform_ref),
                (noise_in.at[0 : noise_ref.shape[0], :, 0:block_slots, :], noise_ref),
            )
        )
    ]
    for copy in copies:
        copy.start()
    paired_rows = paired.shape[0] // 2
    macro, core = place_of()
    lane = lanes_of((1, size_z))

    for owner in range(count.shape[0]):
        count[owner] = 0
    paired[...] = jnp.zeros_like(paired)
    for copy in copies[:2]:
        copy.wait()
    for j in range(flags):
        owner = owner_ref[j]
        rank = count[owner]
        count[owner] = rank + 1
        target[j] = (rank & 1) * paired_rows + owner * (slot_rows // 2) + lax.shift_right_logical(rank, 1)
        position_ref[j] = owner * slot_rows + rank
    for copy in copies[2:4]:
        copy.wait()
    planes = velocity_ref.reshape(3, size_x, size_y, size_z)
    layers = viscosity_ref.reshape(size_x, size_y, size_z)
    for j in range(flags):
        cell = cell_ref[j]
        x = lax.shift_right_logical(cell, 10)
        y = lax.shift_right_logical(cell, 7) & (size_y - 1)
        z = cell & (size_z - 1)
        here = (lane == z).astype(jnp.float32)
        along_z = (lane == z + 1).astype(jnp.float32) - (lane == z - 1).astype(jnp.float32)
        at = pl.ds(y, 1)
        for a in range(3):
            along_x = planes[a, x + 1, at, :] - planes[a, x - 1, at, :]
            along_y = planes[a, x, pl.ds(y + 1, 1), :] - planes[a, x, pl.ds(y - 1, 1), :]
            masked[3 * a, j : j + 1, :] = along_x * here
            masked[3 * a + 1, j : j + 1, :] = along_y * here
            masked[3 * a + 2, j : j + 1, :] = planes[a, x, at, :] * along_z
        masked[9, j : j + 1, :] = layers[x, at, :] * here

    even = lax.axis_index("tile") & 1 == 0

    def put(number, ref, low, high):
        rows = [ref[pl.ds(y, size_x, stride=size_y), :] for y in (low, high)]
        first_ref[number] = jnp.where(even, rows[1], rows[0])
        second_ref[number] = jnp.where(even, rows[0], rows[1])

    for layer in range(2):
        for a in range(3):
            put(3 * layer + a, velocity_ref.at[a], layer, size_y - 1 - layer)
    put(6, viscosity_ref, 0, size_y - 1)

    for side in range(2):
        beside = neighbour(macro, side, macro_count)
        for layer, owner in enumerate((2 * beside + core, 2 * beside + 1 - core)):
            start = pl.multiple_of(owner * chunk_rows, 8)
            x = layer if side == 0 else size_x - 1 - layer
            for a in range(3):
                chunk_ref[pl.ds(start + a * size_y, size_y), :] = velocity_ref[a, x * size_y : (x + 1) * size_y, :]
            x = 0 if side == 0 else size_x - 1
            half = x * size_y + layer * (size_y // 2)
            chunk_ref[pl.ds(start + 3 * size_y, size_y // 2), :] = viscosity_ref[half : half + size_y // 2, :]

    group = size_z // 8
    lane2 = lanes_of((size_y, size_z))
    first = pl.multiple_of((2 * macro + 1 - core) * chunk_rows, 8)
    source = jnp.where(core == 0, size_z - 2, 0)
    for block in range(-(-size_x // group)):
        total = jnp.zeros((size_y, size_z), jnp.float32)
        for x in range(block * group, min(size_x, (block + 1) * group)):
            rows = slice(x * size_y, (x + 1) * size_y)
            for a in range(4):
                at = 8 * (x - block * group) + 2 * a
                value = viscosity_ref[rows, :] if a == 3 else velocity_ref[a, rows, :]
                total = jnp.where((lane2 == at) | (lane2 == at + 1), rolled(value, at - source), total)
        chunk_ref[pl.ds(first + block * size_y, size_y), :] = total

    columns = [0.5 * jnp.sum(masked[c], axis=1, keepdims=True) for c in range(9)]
    viscous = jnp.sum(masked[9], axis=1, keepdims=True)
    wide = lanes_of((flags, 128))
    packed = jnp.zeros((flags, 128), jnp.float32)
    for c in range(9):
        packed = jnp.where(wide == c, columns[c], packed)
    gradients[...] = packed
    stress = jnp.zeros((flags, 128), jnp.float32)
    for k, (a, b) in enumerate(stress_pairs):
        stress = jnp.where(wide == k, viscous * (columns[3 * a + b] + columns[3 * b + a]), stress)
    viscous_ref[...] = stress

    for j in range(flags):
        paired[pl.ds(target[j], 1), :] = gradients[j : j + 1, :]
    rows = paired[0:paired_rows, :] + rolled(paired[paired_rows:, :], 64)
    for owner in range(count.shape[0]):
        chunk_ref[owner * chunk_rows + half_face : (owner + 1) * chunk_rows, :] = rows[
            owner * (slot_rows // 2) : (owner + 1) * (slot_rows // 2)
        ]
    for copy in copies[4:]:
        copy.wait()


def gather_rows(flag_cell, owner, velocity, viscosity, conformations, increments, capacity, owner_count):
    size_x, size_y, size_z = viscosity.shape
    flags = flag_cell.shape[0]
    face = jax.ShapeDtypeStruct((item_count, size_x, size_z), jnp.float32)
    steps, _, _, dumbbells = increments.shape
    return pl.pallas_call(
        functools.partial(gather_kernel, capacity, size_x, size_y, size_z, owner_count // 2),
        out_shape=(
            jax.ShapeDtypeStruct((owner_count * chunk_rows, 128), jnp.float32),
            jax.ShapeDtypeStruct((flags,), jnp.int32),
            jax.ShapeDtypeStruct((flags, 128), jnp.float32),
            face,
            face,
            pltpu.VMEM((3, block_slots, dumbbells), jnp.float32),
            pltpu.VMEM((steps // first_share, 3, block_slots, dumbbells), jnp.bfloat16),
        ),
        in_specs=[pl.BlockSpec(memory_space=pltpu.HBM)] * 6,
        out_specs=(VMEM, SMEM, VMEM, VMEM, VMEM, VMEM, VMEM),
        scratch_shapes=[
            pltpu.SMEM((flags,), jnp.int32),
            pltpu.SMEM((flags,), jnp.int32),
            pltpu.VMEM((3, size_x * size_y, size_z), jnp.float32),
            pltpu.VMEM((size_x * size_y, size_z), jnp.float32),
            pltpu.VMEM((10, flags, size_z), jnp.float32),
            pltpu.VMEM((flags, 128), jnp.float32),
            pltpu.VMEM((owner_count * slot_rows, 128), jnp.float32),
            pltpu.SMEM((flags,), jnp.int32),
            pltpu.SMEM((owner_count,), jnp.int32),
            pltpu.SemaphoreType.DMA((6,)),
        ],
        compiler_params=limit(8),
        cost_estimate=pl.CostEstimate(flops=400000, bytes_accessed=3000000, transcendentals=0),
        name="gather_rows",
    )(
        far(flag_cell),
        far(owner),
        far(velocity.reshape(3, size_x * size_y, size_z)),
        far(viscosity.reshape(size_x * size_y, size_z)),
        far(conformations),
        far(increments),
    )


def micro_kernel(
    capacity, parts, rows, groups, conform_ref, noise_ref, rate_ref, first_conform_ref, first_noise_ref,
    next_ref, chunk_ref, conform, noise, rate, rate_wide, sums_ref, read_sem, noise_sem,
):
    steps, _, slots, dumbbells = noise_ref.shape
    blocks = slots // rows
    span = steps // groups
    width = dumbbells // parts
    owners = slots // capacity
    scale = 1.0 / noise_weight
    extent = fene_extent * scale * scale

    def block_rows(block):
        return pl.ds(pl.multiple_of(block * rows, rows), rows)

    def read(block):
        at = block_rows(block)
        return pltpu.make_async_copy(conform_ref.at[:, at, :], conform.at[:, at, :], read_sem.at[block])

    def read_noise(block, group):
        at, when = block_rows(block), pl.ds(group * span, span)
        return pltpu.make_async_copy(
            noise_ref.at[when, :, at, :], noise.at[when, :, at, :], noise_sem.at[block, group]
        )

    pieces = [
        (half, slice(part * width, (part + 1) * width)) for half in range(rows // 16) for part in range(parts)
    ]
    assert len(pieces) == 8
    early = groups // first_share
    for block in range(blocks):
        if block > 0:
            read(block).start()
        for group in range(early if block == 0 else 0, groups):
            read_noise(block, group).start()
    conform[:, 0:rows, :] = first_conform_ref[...]
    for step in range(steps // first_share):
        noise[step, :, 0:rows, :] = first_noise_ref[step]
    for owner in range(owners):
        packed = rate_ref[owner, half_face : half_face + capacity // 2, :]
        rate[pl.ds(owner * capacity, capacity // 2, stride=2), :] = packed
        rate[pl.ds(owner * capacity + 1, capacity // 2, stride=2), :] = rolled(packed, 64)
        chunk_ref[owner] = jnp.zeros(chunk_ref.shape[1:], jnp.float32)
    for a in range(3):
        for b in range(3):
            column = micro_step * rate[:, 3 * a + b : 3 * a + b + 1] + (1.0 if a == b else 0.0)
            rate_wide[3 * a + b] = jnp.broadcast_to(column, (slots, width))

    def inverses(state, scale):
        rooms = []
        for piece in range(len(pieces)):
            q = state[3 * piece : 3 * piece + 3]
            room = (extent - q[0] * q[0]) - (q[1] * q[1] + q[2] * q[2])
            rooms.append(jnp.maximum(room, extent * spring_floor))
        levels = [rooms]
        while len(levels[-1]) > 1:
            levels.append([low * high for low, high in zip(levels[-1][0::2], levels[-1][1::2])])
        result = [scale * pl.reciprocal(levels[-1][0])]
        for level in reversed(levels[:-1]):
            result = [result[i // 2] * level[i ^ 1] for i in range(len(level))]
        return result

    def advance_block(block, carry):
        ats = [pl.ds(pl.multiple_of(block * rows + 16 * half, 16), 16) for half in range(rows // 16)]
        rates = [
            [[rate_wide.at[3 * a + b, at, :] for b in range(3)] for a in range(3)] for at in ats
        ]

        def substep(step, state):
            updated = []
            springs = inverses(state, micro_step * relax_rate * extent)
            for piece, (half, lanes) in enumerate(pieces):
                q = state[3 * piece : 3 * piece + 3]
                table = rates[half]
                for a in range(3):
                    b, c = [other for other in range(3) if other != a]
                    kick = noise[step, a, ats[half], lanes].astype(jnp.float32)
                    rest = (table[a][b][...] * q[b] + table[a][c][...] * q[c]) + kick
                    updated.append((table[a][a][...] - springs[piece]) * q[a] + rest)
            return tuple(updated)

        def advance_group(group, state):
            if group < early:

                @pl.when(block > 0)
                def _():
                    read_noise(block, group).wait()

            else:
                read_noise(block, group).wait()
            for step in range(span):
                state = substep(group * span + step, state)
            return state

        @pl.when(block > 0)
        def _():
            read(block).wait()

        state = tuple(conform[a, ats[half], lanes] * scale for half, lanes in pieces for a in range(3))
        for group in range(groups):
            state = advance_group(group, state)
        inverse = inverses(state, 1.0)
        for half, at in enumerate(ats):
            sums = [None] * 6
            for piece, (other, lanes) in enumerate(pieces):
                if other != half:
                    continue
                q = state[3 * piece : 3 * piece + 3]
                for a in range(3):
                    next_ref[a, at, lanes] = q[a] * noise_weight
                for k, (a, b) in enumerate(stress_pairs):
                    term = (inverse[piece] * q[a]) * q[b]
                    sums[k] = term if sums[k] is None else sums[k] + term
            for k in range(6):
                sums_ref[k, at, :] = sums[k]
        return carry

    lax.fori_loop(0, blocks, advance_block, 0)
    lane = lanes_of((slots, 128))
    rank = lax.broadcasted_iota(jnp.int32, (slots, 128), 0) & (capacity - 1)
    packed = jnp.zeros((slots, 128), jnp.float32)
    weight = extent * noise_weight * noise_weight / dumbbells
    for k, (a, b) in enumerate(stress_pairs):
        mean = jnp.sum(sums_ref[k], axis=1, keepdims=True) * weight
        packed = jnp.where(lane == 8 * rank + k, polymer_weight * (mean - (1.0 if a == b else 0.0)), packed)
    for owner in range(owners):
        chunk_ref[owner, polymer_row : polymer_row + 1, :] = jnp.sum(
            packed[owner * capacity : (owner + 1) * capacity], axis=0, keepdims=True
        )


def advance(conformations, increments, chunks, first_conform, first_noise, capacity):
    slots, dumbbells = conformations.shape[1:]
    steps = increments.shape[0]
    owners = slots // capacity
    rows, parts, groups = block_slots, 4, 4
    blocks = slots // rows
    whole = pl.BlockSpec(memory_space=pltpu.HBM)
    return pl.pallas_call(
        functools.partial(micro_kernel, capacity, parts, rows, groups),
        out_shape=(
            pltpu.VMEM(conformations.shape, jnp.float32),
            jax.ShapeDtypeStruct((owners, back_rows, 128), jnp.float32),
        ),
        in_specs=[whole, whole, VMEM, VMEM, VMEM],
        out_specs=(VMEM, VMEM),
        scratch_shapes=[
            pltpu.VMEM(conformations.shape, jnp.float32),
            pltpu.VMEM(increments.shape, jnp.bfloat16),
            pltpu.VMEM((slots, 128), jnp.float32),
            pltpu.VMEM((9, slots, dumbbells // parts), jnp.float32),
            pltpu.VMEM((6, slots, dumbbells // parts), jnp.float32),
            pltpu.SemaphoreType.DMA((blocks,)),
            pltpu.SemaphoreType.DMA((blocks, groups)),
        ],
        compiler_params=limit(12),
        cost_estimate=pl.CostEstimate(flops=20000000, bytes_accessed=5000000, transcendentals=600000),
        name="advance",
    )(far(conformations), far(increments), chunks, first_conform, first_noise)


def lines_kernel(macro_count, chunk_ref, received_ref, first_ref, second_ref, out_ref, handed_ref):
    out_ref[...] = chunk_ref[...]
    macro, core = place_of()
    even = lax.axis_index("tile") & 1 == 0
    size_x = first_ref.shape[1]

    def side_of(u, item, at):
        first, second = first_ref[item, at, :], second_ref[item, at, :]
        return jnp.where(even, second, first) if u == 0 else jnp.where(even, first, second)

    for side in range(2):
        beside = neighbour(macro, side, macro_count)
        handed_ref[side, 0:chunk_rows, :] = received_ref[2 * beside + 1 - core]
        for number, a in enumerate((0, 2)):
            handed_ref[side, chunk_rows + number * 8 : chunk_rows + (number + 1) * 8, :] = received_ref[
                2 * beside + core, a * 8 : (a + 1) * 8, :
            ]
        x = 0 if side == 0 else size_x - 1
        for u in range(2):
            for a in range(2):
                at = 2 * u + a
                out_ref[2 * beside + core, at : at + 1, :] = side_of(u, a, slice(x, x + 1))
    for u in range(2):
        for number in range(2):
            start = handed_rows + number * size_x
            handed_ref[u, start : start + size_x, :] = side_of(u, 1 + number, slice(0, size_x))


def add_lines(chunks, received, first, second):
    return pl.pallas_call(
        functools.partial(lines_kernel, chunks.shape[0] // 2),
        out_shape=(
            jax.ShapeDtypeStruct(chunks.shape, jnp.float32),
            jax.ShapeDtypeStruct((2, handed_rows + 2 * first.shape[1], 128), jnp.float32),
        ),
        in_specs=[VMEM] * 4,
        out_specs=(VMEM,) * 2,
        compiler_params=limit(4),
        cost_estimate=pl.CostEstimate(flops=20000, bytes_accessed=400000, transcendentals=0),
        name="add_lines",
    )(chunks, received, first, second)


product_depth = 128


def one_hots(size_y, size_z, cell_ref, position_ref, lines_ref, pick_ref, spread_ref, rows):
    flags = cell_ref.shape[0]
    weight = 0.5 * macro_step
    row_count = spread_ref.shape[0]
    returned = pick_ref.shape[1] // 4
    lane = lanes_of((1, size_z))
    row_lane = lanes_of((1, rows.shape[1]))
    slot_lane = lanes_of((flags, returned))
    flag_row = lax.broadcasted_iota(jnp.int32, (flags, returned), 0)
    rows[3 * flags :, :] = jnp.zeros((product_depth - 3 * flags, rows.shape[1]), jnp.float32)
    slot = jnp.zeros((flags, returned), jnp.int32)
    group = lax.shift_right_logical(lane, 3)
    for j in range(flags):
        cell = cell_ref[j]
        row = lax.div(cell, size_z)
        z = cell - row * size_z
        lines_ref[0, j : j + 1, :] = jnp.where(lane == z, weight, 0.0)
        lines_ref[1, j : j + 1, :] = jnp.where(
            lane == z - 1, weight, jnp.where(lane == z + 1, -weight, 0.0)
        )
        for number, shift in enumerate((size_y, 1)):
            rows[number * flags + j : number * flags + j + 1, :] = jnp.where(
                row_lane == row - shift, 1.0, jnp.where(row_lane == row + shift, -1.0, 0.0)
            )
        rows[2 * flags + j : 2 * flags + j + 1, :] = jnp.where(row_lane == row, 1.0, 0.0)
        owner = lax.div(position_ref[j], slot_rows)
        rank = position_ref[j] - owner * slot_rows
        lines_ref[2, j : j + 1, :] = jnp.where(group == rank, 1.0, 0.0)
        slot = jnp.where(flag_row == j, owner * back_rows + polymer_row, slot)
    spread = rows[...].T[:row_count].astype(jnp.bfloat16)
    pick = jnp.where(slot_lane == slot, 1.0, 0.0).astype(jnp.bfloat16)
    for piece in range(3):
        spread_ref[:, piece * product_depth : (piece + 1) * product_depth] = spread
        pick_ref[:, piece * returned : (piece + 1) * returned] = pick
    pick_ref[:, 3 * returned :] = jnp.zeros((flags, returned), jnp.bfloat16)


def flow_kernel(
    size_x, size_y, size_z, macro_count, cell_ref, position_ref, velocity_ref, viscosity_ref, chunk_ref,
    first_ref, second_ref, handed_ref, out_ref, corner_ref, lines_ref, pick_ref, spread_ref,
    padded, stress_x, stress_rest, faces, ghost_y, ghost_z, rows, halves, beyond,
    y_low_ref, y_high_ref,
):
    macro, core = place_of()
    even = lax.axis_index("tile") & 1 == 0
    y_low_ref[...] = jnp.where(even, second_ref[...], first_ref[...])
    y_high_ref[...] = jnp.where(even, first_ref[...], second_ref[...])
    one_hots(size_y, size_z, cell_ref, position_ref, lines_ref, pick_ref, spread_ref, rows)
    inside = (macro > 0, macro < macro_count - 1)
    sign_z = jnp.where(core == 0, 1.0, -1.0)
    end = jnp.where(core == 0, size_z - 1, 0)
    shape = (size_y, size_z)
    lane, row = lanes_of(shape), lax.broadcasted_iota(jnp.int32, shape, 0)
    at_end = jnp.where(lane == end, sign_z, 0.0)

    def kept(value, condition):
        return jnp.where(condition, value, 0.0)

    def plane(x):
        return pl.ds(pl.multiple_of(x * size_y, 8), size_y)

    def difference_z(value):
        lane = lanes_of(value.shape)
        return jnp.where(lane == size_z - 1, 0.0, rolled(value, -1)) - jnp.where(
            lane == 0, 0.0, rolled(value, 1)
        )

    def difference_rows(value, low=0.0, high=0.0):
        count = value.shape[0]
        row = lax.broadcasted_iota(jnp.int32, value.shape, 0)
        return jnp.where(row == count - 1, high, pltpu.roll(value, count - 1, 0)) - jnp.where(
            row == 0, low, pltpu.roll(value, 1, 0)
        )

    x_faces, x_others = [], []
    half = size_y // 2
    for s in range(2):
        beside = neighbour(macro, s, macro_count)
        outer = chunk_ref[2 * beside + core]
        items = [outer[i * size_y : (i + 1) * size_y] for i in range(3)]
        items += [handed_ref[s, i * size_y : (i + 1) * size_y, :] for i in range(3)]
        halves[s, 0:half, :] = chunk_ref[2 * beside + core, 3 * size_y : 3 * size_y + half, :]
        halves[s, half:, :] = handed_ref[s, 3 * size_y : 3 * size_y + half, :]
        items.append(halves[s])
        x_faces.append([kept(item, inside[s]) for item in items])
        corners = [handed_ref[s, chunk_rows + i * size_y : chunk_rows + (i + 1) * size_y, :] for i in range(2)]
        x_others.append([kept(rolled(corner, 2 * end + 1), inside[s]) for corner in corners])

    y_others = []
    for u in range(2):
        start = handed_rows + size_x
        y_others.append(rolled(handed_ref[u, handed_rows:start, :], 2 * end + 1))
        beyond[u] = rolled(handed_ref[u, start : start + size_x, :], 2 * end + 1)

    group = size_z // 8
    packed = [
        chunk_ref[2 * macro + 1 - core, i * size_y : (i + 1) * size_y, :]
        for i in range(-(-size_x // group))
    ]
    for i, value in enumerate(packed):

        def unpack(x, carry):
            for q in range(item_count):
                a, layer = (q, 0) if q < 4 else (q - 4, 1)
                at = 8 * (x - i * group) + 2 * a + (core if layer == 0 else 1 - core)
                faces[q, x + 1] = rolled(value, end - at)
            return carry

        lax.fori_loop(i * group, min(size_x, (i + 1) * group), unpack, 0, unroll=8)
    faces[2, 0] = x_others[0][1]
    faces[2, size_x + 1] = x_others[1][1]

    for a in range(3):
        padded[a, 0] = x_faces[0][a]
        padded[a, size_x + 1] = x_faces[1][a]

    def fill(x, carry):
        for a in range(3):
            padded[a, x + 1] = velocity_ref[a, plane(x), :]
        return carry

    lax.fori_loop(0, size_x, fill, 0, unroll=True)

    rest = {(1, 1): 0, (2, 2): 1, (1, 2): 2}

    def stress_plane(x, carry):
        along_x, along_y, along_z, centre = [], [], [], []
        for a in range(3):
            value = padded[a, x + 1]
            centre.append(value)
            along_x.append(padded[a, x + 2] - padded[a, x])
            along_y.append(
                difference_rows(value, y_low_ref[a, pl.ds(x, 1), :], y_high_ref[a, pl.ds(x, 1), :])
            )
            along_z.append(difference_z(value) + faces[a, x + 1] * at_end)
        slopes = (along_x, along_y, along_z)
        half = 0.5 * viscosity_ref[plane(x), :]
        for a, b in stress_pairs:
            value = half * (slopes[b][a] + slopes[a][b])
            if a == 0:
                stress_x[b, x + 1] = value
            else:
                stress_rest[rest[a, b], x] = value
        weight = (0.5 * faces[3, x + 1]) * at_end
        normal = [(faces[4 + a, x + 1] - centre[a]) * sign_z for a in range(3)]
        ghost_z[0, x] = weight * (normal[0] + (faces[2, x + 2] - faces[2, x]))
        slope = difference_rows(faces[2, x + 1], beyond[0, pl.ds(x, 1), :], beyond[1, pl.ds(x, 1), :])
        ghost_z[1, x] = weight * (normal[1] + slope)
        ghost_z[2, x] = weight * (2.0 * normal[2])
        return carry

    lax.fori_loop(0, size_x, stress_plane, 0, unroll=6)

    for s in range(2):
        near, far, weight = x_faces[s][0:3], x_faces[s][3:6], 0.5 * x_faces[s][6]
        sign = -1.0 if s == 0 else 1.0
        normal = [(far[a] - padded[a, 1 if s == 0 else size_x]) * sign for a in range(3)]
        slope_y = difference_rows(near[0])
        slope_z = difference_z(near[0]) + x_others[s][0] * at_end
        at = 0 if s == 0 else size_x + 1
        stress_x[0, at] = weight * (2.0 * normal[0])
        stress_x[1, at] = weight * (normal[1] + slope_y)
        stress_x[2, at] = weight * (normal[2] + slope_z)
        for u in range(2):
            y, sign_y = (0, -1.0) if u == 0 else (size_y - 1, 1.0)
            number = 4 * s + 2 * u
            corner_ref[number : number + 1, :] = (0.5 * macro_step * sign * sign_y) * weight[y : y + 1, :]

    for u, ref in enumerate((y_low_ref, y_high_ref)):
        y, sign = (0, -1.0) if u == 0 else (size_y - 1, 1.0)
        weight = 0.5 * ref[6]
        normal = [
            (ref[3 + a] - velocity_ref[a, pl.ds(y, size_x, stride=size_y), :]) * sign for a in range(3)
        ]
        ghost_y[3 * u] = weight * (normal[0] + difference_rows(ref[1]))
        ghost_y[3 * u + 1] = weight * (2.0 * normal[1])
        wide = lanes_of((size_x, size_z))
        across = jnp.where(wide == end, y_others[u] * sign_z, 0.0)
        ghost_y[3 * u + 2] = weight * (normal[2] + (difference_z(ref[1]) + across))
        for s in range(2):
            x, sign_x = (0, -1.0) if s == 0 else (size_x - 1, 1.0)
            number = 4 * s + 2 * u + 1
            corner_ref[number : number + 1, :] = (0.5 * macro_step * sign * sign_x) * weight[x : x + 1, :]

    columns = {(0, 1): (stress_x, 1, 1), (1, 1): (stress_rest, 0, 0), (2, 1): (stress_rest, 2, 0)}
    columns_z = {0: (stress_x, 2, 1), 1: (stress_rest, 2, 0), 2: (stress_rest, 1, 0)}

    def step_plane(x, carry):
        for a in range(3):
            total = stress_x[a, x + 2] - stress_x[a, x]
            ref, number, shift = columns[a, 1]
            total = total + difference_rows(
                ref[number, x + shift], ghost_y[a, pl.ds(x, 1), :], ghost_y[3 + a, pl.ds(x, 1), :]
            )
            ref, number, shift = columns_z[a]
            total = total + (difference_z(ref[number, x + shift]) + ghost_z[a, x])
            out_ref[a, plane(x), :] = padded[a, x + 1] + (0.5 * macro_step) * total
        return carry

    lax.fori_loop(0, size_x, step_plane, 0, unroll=6)


def flow_step(flag_cell, position, velocity, viscosity, chunks, first, second, handed):
    size_x, size_y, size_z = viscosity.shape
    flags = flag_cell.shape[0]
    returned = chunks.shape[0] * back_rows
    row_count = size_x * size_y
    planes = (size_x, size_y, size_z)
    wide = (size_x + 2, size_y, size_z)
    return pl.pallas_call(
        functools.partial(flow_kernel, size_x, size_y, size_z, chunks.shape[0] // 2),
        out_shape=(
            jax.ShapeDtypeStruct((3, size_x * size_y, size_z), jnp.float32),
            jax.ShapeDtypeStruct((8, size_z), jnp.float32),
            jax.ShapeDtypeStruct((3, flags, size_z), jnp.float32),
            jax.ShapeDtypeStruct((flags, 4 * returned), jnp.bfloat16),
            jax.ShapeDtypeStruct((row_count, 3 * product_depth), jnp.bfloat16),
        ),
        in_specs=[SMEM] * 2 + [VMEM] * 6,
        out_specs=(VMEM,) * 5,
        scratch_shapes=[
            pltpu.VMEM((3, *wide), jnp.float32),
            pltpu.VMEM((3, *wide), jnp.float32),
            pltpu.VMEM((3, *planes), jnp.float32),
            pltpu.VMEM((item_count, *wide), jnp.float32),
            pltpu.VMEM((6, size_x, size_z), jnp.float32),
            pltpu.VMEM((3, *planes), jnp.float32),
            pltpu.VMEM((product_depth, -(-row_count // 128) * 128), jnp.float32),
            pltpu.VMEM((2, size_y, size_z), jnp.float32),
            pltpu.VMEM((2, size_x, size_z), jnp.float32),
            pltpu.VMEM(first.shape, jnp.float32),
            pltpu.VMEM(first.shape, jnp.float32),
        ],
        compiler_params=limit(12),
        cost_estimate=pl.CostEstimate(flops=4000000, bytes_accessed=3000000, transcendentals=0),
        name="flow_step",
    )(
        flag_cell, position,
        velocity.reshape(3, size_x * size_y, size_z),
        viscosity.reshape(size_x * size_y, size_z),
        chunks, first, second, handed,
    )


def pieces(value):
    high = value.astype(jnp.bfloat16)
    rest = value - high.astype(jnp.float32)
    middle = rest.astype(jnp.bfloat16)
    return high, middle, (rest - middle.astype(jnp.float32)).astype(jnp.bfloat16)


def polymer_kernel(
    size_x, size_y, size_z, macro_count, chunk_ref, viscous_ref, corner_ref, lines_ref, pick_ref,
    spread_ref, partial_ref, out_ref, flag_ref,
):
    flags = viscous_ref.shape[0]
    macro, core = place_of()
    chunks = chunk_ref[...]
    split = jnp.concatenate((*pieces(chunks), jnp.zeros(chunks.shape, jnp.bfloat16)), axis=0)
    values = jnp.dot(pick_ref[...], split, preferred_element_type=jnp.float32) * lines_ref[2]
    here, beside_z = lines_ref[0], lines_ref[1]
    lane = lanes_of((flags, 128))
    columns = [
        jnp.broadcast_to(
            jnp.sum(jnp.where((lane & 7) == k, values, 0.0), axis=1, keepdims=True), (flags, size_z)
        )
        for k in range(6)
    ]
    stress = viscous_ref[...]
    for k in range(6):
        stress = jnp.where(lane == k, stress + columns[k], stress)
    unused = jnp.zeros((product_depth - 3 * flags, size_z), jnp.float32)
    split = [
        pieces(
            jnp.concatenate(
                [
                    columns[pair_index(a, 0)] * here, columns[pair_index(a, 1)] * here,
                    columns[pair_index(a, 2)] * beside_z, unused,
                ],
                axis=0,
            )
        )
        for a in range(3)
    ]
    flag_ref[...] = stress.T[0:6, :]

    out_ref[...] = partial_ref[...]
    for s in range(2):
        inside = macro > 0 if s == 0 else macro < macro_count - 1
        beside = jnp.maximum(macro - 1, 0) if s == 0 else jnp.minimum(macro + 1, macro_count - 1)
        start = (2 * beside + core) * back_rows
        x = 0 if s == 0 else size_x - 1
        for u in range(2):
            at = x * size_y + (0 if u == 0 else size_y - 1)
            for a in range(2):
                number = 4 * s + 2 * u + a
                line = corner_ref[number : number + 1, :] * chunk_ref[pl.ds(start + 2 * u + a, 1), :]
                out_ref[1 - a, at : at + 1, :] += jnp.where(inside, line, 0.0)
    for a in range(3):
        out_ref[a] += jnp.dot(
            spread_ref[...], jnp.concatenate(split[a], axis=0), preferred_element_type=jnp.float32
        )


def add_polymer(chunks, viscous, corners, lines, pick, spread, partial, shape):
    flags = viscous.shape[0]
    size_x, size_y, size_z = shape
    return pl.pallas_call(
        functools.partial(polymer_kernel, size_x, size_y, size_z, chunks.shape[0] // 2),
        out_shape=(
            jax.ShapeDtypeStruct(partial.shape, jnp.float32),
            jax.ShapeDtypeStruct((6, flags), jnp.float32),
        ),
        in_specs=[VMEM] * 7,
        out_specs=(VMEM, VMEM),
        compiler_params=limit(8),
        cost_estimate=pl.CostEstimate(flops=400000, bytes_accessed=3000000, transcendentals=0),
        name="add_polymer",
    )(chunks.reshape(-1, 128), viscous, corners, lines, pick, spread, partial)


def shards(velocity, viscosity, flag_cell, flag_owner, conformations, increments):
    macro_count = lax.axis_size("macro")
    tile_count = lax.axis_size("tile")
    assert lax.axis_size("micro") == 2
    owner_count = 2 * macro_count
    capacity = conformations.shape[1] // owner_count
    size_x, size_y, size_z = viscosity.shape
    assert capacity <= slot_rows and capacity % 2 == 0 and size_y == 8 and size_z == 128 and size_x % 8 == 0 and size_x <= 48
    chunks, position, viscous, first, second, first_conform, first_noise = gather_rows(
        flag_cell, flag_owner.reshape(-1), velocity, viscosity, conformations, increments, capacity, owner_count
    )

    def exchange(rows):
        return lax.all_to_all(rows, ("macro", "micro"), split_axis=0, concat_axis=0, tiled=True)

    received = exchange(chunks.reshape(owner_count, -1, 128))
    swaps = []
    for start in range(2):
        pairs = [(i, i + 1) for i in range(start, tile_count - 1, 2)]
        swaps.append(pairs + [(high, low) for low, high in pairs])
    first = lax.ppermute(first, "tile", swaps[0])
    second = lax.ppermute(second, "tile", swaps[1])
    last_state, polymer = advance(
        conformations, increments, received, first_conform, first_noise, capacity
    )
    polymer, handed = add_lines(polymer, received, first, second)
    returned = exchange(polymer)
    handed = lax.ppermute(handed, "micro", [(0, 1), (1, 0)])
    partial, corners, lines, pick, spread = flow_step(
        flag_cell, position, velocity, viscosity, received, first, second, handed
    )
    velocity_next, flag_stress = add_polymer(
        returned, viscous, corners, lines, pick, spread, partial, viscosity.shape
    )
    return (velocity_next.reshape(velocity.shape), last_state, flag_stress)


def solution(mesh):
    in_specs = (
        P(None, "macro", "tile", "micro"),
        P("macro", "tile", "micro"),
        P(("macro", "tile", "micro")),
        P(("macro", "tile", "micro"), None),
        P(None, ("macro", "tile", "micro"), None),
        P(None, None, ("macro", "tile", "micro"), None),
    )
    out_specs = (
        P(None, "macro", "tile", "micro"),
        P(None, ("macro", "tile", "micro"), None),
        P(None, ("macro", "tile", "micro")),
    )
    return jax.shard_map(shards, mesh=mesh, in_specs=in_specs, out_specs=out_specs, check_vma=False)
```

```python
import functools

import jax
import jax.numpy as jnp
from jax import lax
from jax.experimental import pallas as pl
from jax.experimental.pallas import tpu as pltpu
from jax.sharding import PartitionSpec as P

stress_pairs = ((0, 0), (1, 1), (2, 2), (0, 1), (0, 2), (1, 2))
macro_step = 0.1
micro_step = 0.01
noise_weight = 0.1
relax_rate = 0.5
fene_extent = 30.0
spring_floor = 0.1
polymer_weight = 0.25

SMEM = pl.BlockSpec(memory_space=pltpu.SMEM)
VMEM = pl.BlockSpec(memory_space=pltpu.VMEM)


def pair_index(left_axis, right_axis):
    return stress_pairs.index((min(left_axis, right_axis), max(left_axis, right_axis)))


def lanes_of(shape):
    return lax.broadcasted_iota(jnp.int32, shape, len(shape) - 1)


slot_rows = 8
chunk_rows = 32
half_face = 28
handed_rows = 48
item_count = 7
back_rows = 8
polymer_row = 4


block_slots = 32
first_share = 2


def limit(mebibytes):
    return pltpu.CompilerParams(vmem_limit_bytes=mebibytes * 1024 * 1024)


def far(value):
    return pltpu.with_memory_space_constraint(value, pltpu.HBM)


def place_of():
    return lax.axis_index("macro"), lax.axis_index("micro")


def neighbour(index, side, count):
    return jnp.maximum(index - 1, 0) if side == 0 else jnp.minimum(index + 1, count - 1)


def rolled(value, amount):
    size = value.shape[-1]
    if isinstance(amount, int):
        return pltpu.roll(value, amount % size, value.ndim - 1)
    return pltpu.roll(value, lax.rem(amount + 2 * size, size), value.ndim - 1)


def gather_kernel(
    capacity, size_x, size_y, size_z, macro_count, cell_in, owner_in, velocity_in, viscosity_in,
    conform_in, noise_in, chunk_ref, position_ref, viscous_ref, first_ref, second_ref, conform_ref, noise_ref,
    cell_ref, owner_ref, velocity_ref, viscosity_ref, masked, gradients, paired, target, count, sems,
):
    flags = cell_ref.shape[0]
    copies = [
        pltpu.make_async_copy(source, into, sems.at[number])
        for number, (source, into) in enumerate(
            (
                (cell_in, cell_ref), (owner_in, owner_ref), (velocity_in, velocity_ref),
                (viscosity_in, viscosity_ref), (conform_in.at[:, 0:block_slots, :], conform_ref),
                (noise_in.at[0 : noise_ref.shape[0], :, 0:block_slots, :], noise_ref),
            )
        )
    ]
    for copy in copies:
        copy.start()
    paired_rows = paired.shape[0] // 2
    macro, core = place_of()
    lane = lanes_of((1, size_z))

    for owner in range(count.shape[0]):
        count[owner] = 0
    paired[...] = jnp.zeros_like(paired)
    for copy in copies[:2]:
        copy.wait()
    for j in range(flags):
        owner = owner_ref[j]
        rank = count[owner]
        count[owner] = rank + 1
        target[j] = (rank & 1) * paired_rows + owner * (slot_rows // 2) + lax.shift_right_logical(rank, 1)
        position_ref[j] = owner * slot_rows + rank
    for copy in copies[2:4]:
        copy.wait()
    planes = velocity_ref.reshape(3, size_x, size_y, size_z)
    layers = viscosity_ref.reshape(size_x, size_y, size_z)
    for j in range(flags):
        cell = cell_ref[j]
        x = lax.shift_right_logical(cell, 10)
        y = lax.shift_right_logical(cell, 7) & (size_y - 1)
        z = cell & (size_z - 1)
        here = (lane == z).astype(jnp.float32)
        along_z = (lane == z + 1).astype(jnp.float32) - (lane == z - 1).astype(jnp.float32)
        at = pl.ds(y, 1)
        for a in range(3):
            along_x = planes[a, x + 1, at, :] - planes[a, x - 1, at, :]
            along_y = planes[a, x, pl.ds(y + 1, 1), :] - planes[a, x, pl.ds(y - 1, 1), :]
            masked[3 * a, j : j + 1, :] = along_x * here
            masked[3 * a + 1, j : j + 1, :] = along_y * here
            masked[3 * a + 2, j : j + 1, :] = planes[a, x, at, :] * along_z
        masked[9, j : j + 1, :] = layers[x, at, :] * here

    even = lax.axis_index("tile") & 1 == 0

    def put(number, ref, low, high):
        rows = [ref[pl.ds(y, size_x, stride=size_y), :] for y in (low, high)]
        first_ref[number] = jnp.where(even, rows[1], rows[0])
        second_ref[number] = jnp.where(even, rows[0], rows[1])

    for layer in range(2):
        for a in range(3):
            put(3 * layer + a, velocity_ref.at[a], layer, size_y - 1 - layer)
    put(6, viscosity_ref, 0, size_y - 1)

    for side in range(2):
        beside = neighbour(macro, side, macro_count)
        for layer, owner in enumerate((2 * beside + core, 2 * beside + 1 - core)):
            start = pl.multiple_of(owner * chunk_rows, 8)
            x = layer if side == 0 else size_x - 1 - layer
            for a in range(3):
                chunk_ref[pl.ds(start + a * size_y, size_y), :] = velocity_ref[a, x * size_y : (x + 1) * size_y, :]
            x = 0 if side == 0 else size_x - 1
            half = x * size_y + layer * (size_y // 2)
            chunk_ref[pl.ds(start + 3 * size_y, size_y // 2), :] = viscosity_ref[half : half + size_y // 2, :]

    group = size_z // 8
    lane2 = lanes_of((size_y, size_z))
    first = pl.multiple_of((2 * macro + 1 - core) * chunk_rows, 8)
    source = jnp.where(core == 0, size_z - 2, 0)
    for block in range(-(-size_x // group)):
        total = jnp.zeros((size_y, size_z), jnp.float32)
        for x in range(block * group, min(size_x, (block + 1) * group)):
            rows = slice(x * size_y, (x + 1) * size_y)
            for a in range(4):
                at = 8 * (x - block * group) + 2 * a
                value = viscosity_ref[rows, :] if a == 3 else velocity_ref[a, rows, :]
                total = jnp.where((lane2 == at) | (lane2 == at + 1), rolled(value, at - source), total)
        chunk_ref[pl.ds(first + block * size_y, size_y), :] = total

    columns = [0.5 * jnp.sum(masked[c], axis=1, keepdims=True) for c in range(9)]
    viscous = jnp.sum(masked[9], axis=1, keepdims=True)
    wide = lanes_of((flags, 128))
    packed = jnp.zeros((flags, 128), jnp.float32)
    for c in range(9):
        packed = jnp.where(wide == c, columns[c], packed)
    gradients[...] = packed
    stress = jnp.zeros((flags, 128), jnp.float32)
    for k, (a, b) in enumerate(stress_pairs):
        stress = jnp.where(wide == k, viscous * (columns[3 * a + b] + columns[3 * b + a]), stress)
    viscous_ref[...] = stress

    for j in range(flags):
        paired[pl.ds(target[j], 1), :] = gradients[j : j + 1, :]
    rows = paired[0:paired_rows, :] + rolled(paired[paired_rows:, :], 64)
    for owner in range(count.shape[0]):
        chunk_ref[owner * chunk_rows + half_face : (owner + 1) * chunk_rows, :] = rows[
            owner * (slot_rows // 2) : (owner + 1) * (slot_rows // 2)
        ]
    for copy in copies[4:]:
        copy.wait()


def gather_rows(flag_cell, owner, velocity, viscosity, conformations, increments, capacity, owner_count):
    size_x, size_y, size_z = viscosity.shape
    flags = flag_cell.shape[0]
    face = jax.ShapeDtypeStruct((item_count, size_x, size_z), jnp.float32)
    steps, _, _, dumbbells = increments.shape
    return pl.pallas_call(
        functools.partial(gather_kernel, capacity, size_x, size_y, size_z, owner_count // 2),
        out_shape=(
            jax.ShapeDtypeStruct((owner_count * chunk_rows, 128), jnp.float32),
            jax.ShapeDtypeStruct((flags,), jnp.int32),
            jax.ShapeDtypeStruct((flags, 128), jnp.float32),
            face,
            face,
            pltpu.VMEM((3, block_slots, dumbbells), jnp.float32),
            pltpu.VMEM((steps // first_share, 3, block_slots, dumbbells), jnp.bfloat16),
        ),
        in_specs=[pl.BlockSpec(memory_space=pltpu.HBM)] * 6,
        out_specs=(VMEM, SMEM, VMEM, VMEM, VMEM, VMEM, VMEM),
        scratch_shapes=[
            pltpu.SMEM((flags,), jnp.int32),
            pltpu.SMEM((flags,), jnp.int32),
            pltpu.VMEM((3, size_x * size_y, size_z), jnp.float32),
            pltpu.VMEM((size_x * size_y, size_z), jnp.float32),
            pltpu.VMEM((10, flags, size_z), jnp.float32),
            pltpu.VMEM((flags, 128), jnp.float32),
            pltpu.VMEM((owner_count * slot_rows, 128), jnp.float32),
            pltpu.SMEM((flags,), jnp.int32),
            pltpu.SMEM((owner_count,), jnp.int32),
            pltpu.SemaphoreType.DMA((6,)),
        ],
        compiler_params=limit(8),
        cost_estimate=pl.CostEstimate(flops=400000, bytes_accessed=3000000, transcendentals=0),
        name="gather_rows",
    )(
        far(flag_cell),
        far(owner),
        far(velocity.reshape(3, size_x * size_y, size_z)),
        far(viscosity.reshape(size_x * size_y, size_z)),
        far(conformations),
        far(increments),
    )


def micro_kernel(
    capacity, parts, rows, groups, conform_ref, noise_ref, rate_ref, first_conform_ref, first_noise_ref,
    next_ref, chunk_ref, conform, noise, rate, rate_wide, sums_ref, read_sem, noise_sem,
):
    steps, _, slots, dumbbells = noise_ref.shape
    blocks = slots // rows
    span = steps // groups
    width = dumbbells // parts
    owners = slots // capacity
    scale = 1.0 / noise_weight
    extent = fene_extent * scale * scale

    def block_rows(block):
        return pl.ds(pl.multiple_of(block * rows, rows), rows)

    def read(block):
        at = block_rows(block)
        return pltpu.make_async_copy(conform_ref.at[:, at, :], conform.at[:, at, :], read_sem.at[block])

    def read_noise(block, group):
        at, when = block_rows(block), pl.ds(group * span, span)
        return pltpu.make_async_copy(
            noise_ref.at[when, :, at, :], noise.at[when, :, at, :], noise_sem.at[block, group]
        )

    pieces = [
        (half, slice(part * width, (part + 1) * width)) for half in range(rows // 16) for part in range(parts)
    ]
    assert len(pieces) == 8
    early = groups // first_share
    for block in range(blocks):
        if block > 0:
            read(block).start()
        for group in range(early if block == 0 else 0, groups):
            read_noise(block, group).start()
    for owner in range(owners):
        packed = rate_ref[owner, half_face : half_face + capacity // 2, :]
        rate[pl.ds(owner * capacity, capacity // 2, stride=2), :] = packed
        rate[pl.ds(owner * capacity + 1, capacity // 2, stride=2), :] = rolled(packed, 64)
        chunk_ref[owner] = jnp.zeros(chunk_ref.shape[1:], jnp.float32)
    for a in range(3):
        for b in range(3):
            column = micro_step * rate[:, 3 * a + b : 3 * a + b + 1] + (1.0 if a == b else 0.0)
            rate_wide[3 * a + b] = jnp.broadcast_to(column, (slots, width))

    def inverses(state, scale):
        rooms = []
        for piece in range(len(pieces)):
            q = state[3 * piece : 3 * piece + 3]
            room = (extent - q[0] * q[0]) - (q[1] * q[1] + q[2] * q[2])
            rooms.append(jnp.maximum(room, extent * spring_floor))
        levels = [rooms]
        while len(levels[-1]) > 1:
            levels.append([low * high for low, high in zip(levels[-1][0::2], levels[-1][1::2])])
        result = [scale * pl.reciprocal(levels[-1][0])]
        for level in reversed(levels[:-1]):
            result = [result[i // 2] * level[i ^ 1] for i in range(len(level))]
        return result

    def advance_block(block):
        ats = [pl.ds(block * rows + 16 * half, 16) for half in range(rows // 16)]
        ahead = [pl.ds(16 * half, 16) for half in range(rows // 16)]
        rates = [
            [[rate_wide.at[3 * a + b, at, :] for b in range(3)] for a in range(3)] for at in ats
        ]

        def substep(step, state):
            updated = []
            springs = inverses(state, micro_step * relax_rate * extent)
            for piece, (half, lanes) in enumerate(pieces):
                q = state[3 * piece : 3 * piece + 3]
                table = rates[half]
                for a in range(3):
                    b, c = [other for other in range(3) if other != a]
                    if block == 0 and step < steps // first_share:
                        kick = first_noise_ref[step, a, ahead[half], lanes]
                    else:
                        kick = noise[step, a, ats[half], lanes]
                    kick = kick.astype(jnp.float32)
                    rest = (table[a][b][...] * q[b] + table[a][c][...] * q[c]) + kick
                    updated.append((table[a][a][...] - springs[piece]) * q[a] + rest)
            return tuple(updated)

        def advance_group(group, state):
            if block > 0 or group >= early:
                read_noise(block, group).wait()
            for step in range(span):
                state = substep(group * span + step, state)
            return state

        if block > 0:
            read(block).wait()
            state = tuple(conform[a, ats[half], lanes] * scale for half, lanes in pieces for a in range(3))
        else:
            state = tuple(first_conform_ref[a, ahead[half], lanes] * scale for half, lanes in pieces for a in range(3))
        for group in range(groups):
            state = advance_group(group, state)
        inverse = inverses(state, 1.0)
        for half, at in enumerate(ats):
            sums = [None] * 6
            for piece, (other, lanes) in enumerate(pieces):
                if other != half:
                    continue
                q = state[3 * piece : 3 * piece + 3]
                for a in range(3):
                    next_ref[a, at, lanes] = q[a] * noise_weight
                for k, (a, b) in enumerate(stress_pairs):
                    term = (inverse[piece] * q[a]) * q[b]
                    sums[k] = term if sums[k] is None else sums[k] + term
            for k in range(6):
                sums_ref[k, at, :] = sums[k]

    for block in range(blocks):
        advance_block(block)
    lane = lanes_of((slots, 128))
    rank = lax.broadcasted_iota(jnp.int32, (slots, 128), 0) & (capacity - 1)
    packed = jnp.zeros((slots, 128), jnp.float32)
    weight = extent * noise_weight * noise_weight / dumbbells
    for k, (a, b) in enumerate(stress_pairs):
        mean = jnp.sum(sums_ref[k], axis=1, keepdims=True) * weight
        packed = jnp.where(lane == 8 * rank + k, polymer_weight * (mean - (1.0 if a == b else 0.0)), packed)
    for owner in range(owners):
        chunk_ref[owner, polymer_row : polymer_row + 1, :] = jnp.sum(
            packed[owner * capacity : (owner + 1) * capacity], axis=0, keepdims=True
        )


def advance(conformations, increments, chunks, first_conform, first_noise, capacity):
    slots, dumbbells = conformations.shape[1:]
    steps = increments.shape[0]
    owners = slots // capacity
    rows, parts, groups = block_slots, 4, 4
    blocks = slots // rows
    whole = pl.BlockSpec(memory_space=pltpu.HBM)
    return pl.pallas_call(
        functools.partial(micro_kernel, capacity, parts, rows, groups),
        out_shape=(
            pltpu.VMEM(conformations.shape, jnp.float32),
            jax.ShapeDtypeStruct((owners, back_rows, 128), jnp.float32),
        ),
        in_specs=[whole, whole, VMEM, VMEM, VMEM],
        out_specs=(VMEM, VMEM),
        scratch_shapes=[
            pltpu.VMEM(conformations.shape, jnp.float32),
            pltpu.VMEM(increments.shape, jnp.bfloat16),
            pltpu.VMEM((slots, 128), jnp.float32),
            pltpu.VMEM((9, slots, dumbbells // parts), jnp.float32),
            pltpu.VMEM((6, slots, dumbbells // parts), jnp.float32),
            pltpu.SemaphoreType.DMA((blocks,)),
            pltpu.SemaphoreType.DMA((blocks, groups)),
        ],
        compiler_params=limit(12),
        cost_estimate=pl.CostEstimate(flops=20000000, bytes_accessed=5000000, transcendentals=600000),
        name="advance",
    )(far(conformations), far(increments), chunks, first_conform, first_noise)


def lines_kernel(macro_count, chunk_ref, received_ref, first_ref, second_ref, out_ref, handed_ref):
    out_ref[...] = chunk_ref[...]
    macro, core = place_of()
    even = lax.axis_index("tile") & 1 == 0
    size_x = first_ref.shape[1]

    def side_of(u, item, at):
        first, second = first_ref[item, at, :], second_ref[item, at, :]
        return jnp.where(even, second, first) if u == 0 else jnp.where(even, first, second)

    for side in range(2):
        beside = neighbour(macro, side, macro_count)
        handed_ref[side, 0:chunk_rows, :] = received_ref[2 * beside + 1 - core]
        for number, a in enumerate((0, 2)):
            handed_ref[side, chunk_rows + number * 8 : chunk_rows + (number + 1) * 8, :] = received_ref[
                2 * beside + core, a * 8 : (a + 1) * 8, :
            ]
        x = 0 if side == 0 else size_x - 1
        for u in range(2):
            for a in range(2):
                at = 2 * u + a
                out_ref[2 * beside + core, at : at + 1, :] = side_of(u, a, slice(x, x + 1))
    for u in range(2):
        for number in range(2):
            start = handed_rows + number * size_x
            handed_ref[u, start : start + size_x, :] = side_of(u, 1 + number, slice(0, size_x))


def add_lines(chunks, received, first, second):
    return pl.pallas_call(
        functools.partial(lines_kernel, chunks.shape[0] // 2),
        out_shape=(
            jax.ShapeDtypeStruct(chunks.shape, jnp.float32),
            jax.ShapeDtypeStruct((2, handed_rows + 2 * first.shape[1], 128), jnp.float32),
        ),
        in_specs=[VMEM] * 4,
        out_specs=(VMEM,) * 2,
        compiler_params=limit(4),
        cost_estimate=pl.CostEstimate(flops=20000, bytes_accessed=400000, transcendentals=0),
        name="add_lines",
    )(chunks, received, first, second)


product_depth = 128


def one_hots(size_y, size_z, cell_ref, position_ref, lines_ref, pick_ref, spread_ref, rows):
    flags = cell_ref.shape[0]
    weight = 0.5 * macro_step
    row_count = spread_ref.shape[0]
    returned = pick_ref.shape[1] // 4
    lane = lanes_of((1, size_z))
    row_lane = lanes_of((1, rows.shape[1]))
    slot_lane = lanes_of((flags, returned))
    flag_row = lax.broadcasted_iota(jnp.int32, (flags, returned), 0)
    rows[3 * flags :, :] = jnp.zeros((product_depth - 3 * flags, rows.shape[1]), jnp.float32)
    slot = jnp.zeros((flags, returned), jnp.int32)
    group = lax.shift_right_logical(lane, 3)
    for j in range(flags):
        cell = cell_ref[j]
        row = lax.div(cell, size_z)
        z = cell - row * size_z
        lines_ref[0, j : j + 1, :] = jnp.where(lane == z, weight, 0.0)
        lines_ref[1, j : j + 1, :] = jnp.where(
            lane == z - 1, weight, jnp.where(lane == z + 1, -weight, 0.0)
        )
        for number, shift in enumerate((size_y, 1)):
            rows[number * flags + j : number * flags + j + 1, :] = jnp.where(
                row_lane == row - shift, 1.0, jnp.where(row_lane == row + shift, -1.0, 0.0)
            )
        rows[2 * flags + j : 2 * flags + j + 1, :] = jnp.where(row_lane == row, 1.0, 0.0)
        owner = lax.div(position_ref[j], slot_rows)
        rank = position_ref[j] - owner * slot_rows
        lines_ref[2, j : j + 1, :] = jnp.where(group == rank, 1.0, 0.0)
        slot = jnp.where(flag_row == j, owner * back_rows + polymer_row, slot)
    spread = rows[...].T[:row_count].astype(jnp.bfloat16)
    pick = jnp.where(slot_lane == slot, 1.0, 0.0).astype(jnp.bfloat16)
    for piece in range(3):
        spread_ref[:, piece * product_depth : (piece + 1) * product_depth] = spread
        pick_ref[:, piece * returned : (piece + 1) * returned] = pick
    pick_ref[:, 3 * returned :] = jnp.zeros((flags, returned), jnp.bfloat16)


def flow_kernel(
    size_x, size_y, size_z, macro_count, cell_ref, position_ref, velocity_ref, viscosity_ref, chunk_ref,
    first_ref, second_ref, handed_ref, out_ref, corner_ref, lines_ref, pick_ref, spread_ref,
    padded, stress_x, stress_rest, faces, ghost_y, ghost_z, rows, halves, beyond,
    y_low_ref, y_high_ref,
):
    macro, core = place_of()
    even = lax.axis_index("tile") & 1 == 0
    y_low_ref[...] = jnp.where(even, second_ref[...], first_ref[...])
    y_high_ref[...] = jnp.where(even, first_ref[...], second_ref[...])
    one_hots(size_y, size_z, cell_ref, position_ref, lines_ref, pick_ref, spread_ref, rows)
    inside = (macro > 0, macro < macro_count - 1)
    sign_z = jnp.where(core == 0, 1.0, -1.0)
    end = jnp.where(core == 0, size_z - 1, 0)
    shape = (size_y, size_z)
    lane, row = lanes_of(shape), lax.broadcasted_iota(jnp.int32, shape, 0)
    at_end = jnp.where(lane == end, sign_z, 0.0)

    def kept(value, condition):
        return jnp.where(condition, value, 0.0)

    def plane(x):
        return pl.ds(pl.multiple_of(x * size_y, 8), size_y)

    def difference_z(value):
        lane = lanes_of(value.shape)
        return jnp.where(lane == size_z - 1, 0.0, rolled(value, -1)) - jnp.where(
            lane == 0, 0.0, rolled(value, 1)
        )

    def difference_rows(value, low=0.0, high=0.0):
        count = value.shape[0]
        row = lax.broadcasted_iota(jnp.int32, value.shape, 0)
        return jnp.where(row == count - 1, high, pltpu.roll(value, count - 1, 0)) - jnp.where(
            row == 0, low, pltpu.roll(value, 1, 0)
        )

    x_faces, x_others = [], []
    half = size_y // 2
    for s in range(2):
        beside = neighbour(macro, s, macro_count)
        outer = chunk_ref[2 * beside + core]
        items = [outer[i * size_y : (i + 1) * size_y] for i in range(3)]
        items += [handed_ref[s, i * size_y : (i + 1) * size_y, :] for i in range(3)]
        halves[s, 0:half, :] = chunk_ref[2 * beside + core, 3 * size_y : 3 * size_y + half, :]
        halves[s, half:, :] = handed_ref[s, 3 * size_y : 3 * size_y + half, :]
        items.append(halves[s])
        x_faces.append([kept(item, inside[s]) for item in items])
        corners = [handed_ref[s, chunk_rows + i * size_y : chunk_rows + (i + 1) * size_y, :] for i in range(2)]
        x_others.append([kept(rolled(corner, 2 * end + 1), inside[s]) for corner in corners])

    y_others = []
    for u in range(2):
        start = handed_rows + size_x
        y_others.append(rolled(handed_ref[u, handed_rows:start, :], 2 * end + 1))
        beyond[u] = rolled(handed_ref[u, start : start + size_x, :], 2 * end + 1)

    group = size_z // 8
    packed = [
        chunk_ref[2 * macro + 1 - core, i * size_y : (i + 1) * size_y, :]
        for i in range(-(-size_x // group))
    ]
    for i, value in enumerate(packed):

        def unpack(x, carry):
            for q in range(item_count):
                a, layer = (q, 0) if q < 4 else (q - 4, 1)
                at = 8 * (x - i * group) + 2 * a + (core if layer == 0 else 1 - core)
                faces[q, x + 1] = rolled(value, end - at)
            return carry

        lax.fori_loop(i * group, min(size_x, (i + 1) * group), unpack, 0, unroll=8)
    faces[2, 0] = x_others[0][1]
    faces[2, size_x + 1] = x_others[1][1]

    for a in range(3):
        padded[a, 0] = x_faces[0][a]
        padded[a, size_x + 1] = x_faces[1][a]

    def fill(x, carry):
        for a in range(3):
            padded[a, x + 1] = velocity_ref[a, plane(x), :]
        return carry

    lax.fori_loop(0, size_x, fill, 0, unroll=True)

    rest = {(1, 1): 0, (2, 2): 1, (1, 2): 2}

    def stress_plane(x, carry):
        along_x, along_y, along_z, centre = [], [], [], []
        for a in range(3):
            value = padded[a, x + 1]
            centre.append(value)
            along_x.append(padded[a, x + 2] - padded[a, x])
            along_y.append(
                difference_rows(value, y_low_ref[a, pl.ds(x, 1), :], y_high_ref[a, pl.ds(x, 1), :])
            )
            along_z.append(difference_z(value) + faces[a, x + 1] * at_end)
        slopes = (along_x, along_y, along_z)
        half = 0.5 * viscosity_ref[plane(x), :]
        for a, b in stress_pairs:
            value = half * (slopes[b][a] + slopes[a][b])
            if a == 0:
                stress_x[b, x + 1] = value
            else:
                stress_rest[rest[a, b], x] = value
        weight = (0.5 * faces[3, x + 1]) * at_end
        normal = [(faces[4 + a, x + 1] - centre[a]) * sign_z for a in range(3)]
        ghost_z[0, x] = weight * (normal[0] + (faces[2, x + 2] - faces[2, x]))
        slope = difference_rows(faces[2, x + 1], beyond[0, pl.ds(x, 1), :], beyond[1, pl.ds(x, 1), :])
        ghost_z[1, x] = weight * (normal[1] + slope)
        ghost_z[2, x] = weight * (2.0 * normal[2])
        return carry

    lax.fori_loop(0, size_x, stress_plane, 0, unroll=6)

    for s in range(2):
        near, far, weight = x_faces[s][0:3], x_faces[s][3:6], 0.5 * x_faces[s][6]
        sign = -1.0 if s == 0 else 1.0
        normal = [(far[a] - padded[a, 1 if s == 0 else size_x]) * sign for a in range(3)]
        slope_y = difference_rows(near[0])
        slope_z = difference_z(near[0]) + x_others[s][0] * at_end
        at = 0 if s == 0 else size_x + 1
        stress_x[0, at] = weight * (2.0 * normal[0])
        stress_x[1, at] = weight * (normal[1] + slope_y)
        stress_x[2, at] = weight * (normal[2] + slope_z)
        for u in range(2):
            y, sign_y = (0, -1.0) if u == 0 else (size_y - 1, 1.0)
            number = 4 * s + 2 * u
            corner_ref[number : number + 1, :] = (0.5 * macro_step * sign * sign_y) * weight[y : y + 1, :]

    for u, ref in enumerate((y_low_ref, y_high_ref)):
        y, sign = (0, -1.0) if u == 0 else (size_y - 1, 1.0)
        weight = 0.5 * ref[6]
        normal = [
            (ref[3 + a] - velocity_ref[a, pl.ds(y, size_x, stride=size_y), :]) * sign for a in range(3)
        ]
        ghost_y[3 * u] = weight * (normal[0] + difference_rows(ref[1]))
        ghost_y[3 * u + 1] = weight * (2.0 * normal[1])
        wide = lanes_of((size_x, size_z))
        across = jnp.where(wide == end, y_others[u] * sign_z, 0.0)
        ghost_y[3 * u + 2] = weight * (normal[2] + (difference_z(ref[1]) + across))
        for s in range(2):
            x, sign_x = (0, -1.0) if s == 0 else (size_x - 1, 1.0)
            number = 4 * s + 2 * u + 1
            corner_ref[number : number + 1, :] = (0.5 * macro_step * sign * sign_x) * weight[x : x + 1, :]

    columns = {(0, 1): (stress_x, 1, 1), (1, 1): (stress_rest, 0, 0), (2, 1): (stress_rest, 2, 0)}
    columns_z = {0: (stress_x, 2, 1), 1: (stress_rest, 2, 0), 2: (stress_rest, 1, 0)}

    def step_plane(x, carry):
        for a in range(3):
            total = stress_x[a, x + 2] - stress_x[a, x]
            ref, number, shift = columns[a, 1]
            total = total + difference_rows(
                ref[number, x + shift], ghost_y[a, pl.ds(x, 1), :], ghost_y[3 + a, pl.ds(x, 1), :]
            )
            ref, number, shift = columns_z[a]
            total = total + (difference_z(ref[number, x + shift]) + ghost_z[a, x])
            out_ref[a, plane(x), :] = padded[a, x + 1] + (0.5 * macro_step) * total
        return carry

    lax.fori_loop(0, size_x, step_plane, 0, unroll=6)


def flow_step(flag_cell, position, velocity, viscosity, chunks, first, second, handed):
    size_x, size_y, size_z = viscosity.shape
    flags = flag_cell.shape[0]
    returned = chunks.shape[0] * back_rows
    row_count = size_x * size_y
    planes = (size_x, size_y, size_z)
    wide = (size_x + 2, size_y, size_z)
    return pl.pallas_call(
        functools.partial(flow_kernel, size_x, size_y, size_z, chunks.shape[0] // 2),
        out_shape=(
            jax.ShapeDtypeStruct((3, size_x * size_y, size_z), jnp.float32),
            jax.ShapeDtypeStruct((8, size_z), jnp.float32),
            jax.ShapeDtypeStruct((3, flags, size_z), jnp.float32),
            jax.ShapeDtypeStruct((flags, 4 * returned), jnp.bfloat16),
            jax.ShapeDtypeStruct((row_count, 3 * product_depth), jnp.bfloat16),
        ),
        in_specs=[SMEM] * 2 + [VMEM] * 6,
        out_specs=(VMEM,) * 5,
        scratch_shapes=[
            pltpu.VMEM((3, *wide), jnp.float32),
            pltpu.VMEM((3, *wide), jnp.float32),
            pltpu.VMEM((3, *planes), jnp.float32),
            pltpu.VMEM((item_count, *wide), jnp.float32),
            pltpu.VMEM((6, size_x, size_z), jnp.float32),
            pltpu.VMEM((3, *planes), jnp.float32),
            pltpu.VMEM((product_depth, -(-row_count // 128) * 128), jnp.float32),
            pltpu.VMEM((2, size_y, size_z), jnp.float32),
            pltpu.VMEM((2, size_x, size_z), jnp.float32),
            pltpu.VMEM(first.shape, jnp.float32),
            pltpu.VMEM(first.shape, jnp.float32),
        ],
        compiler_params=limit(12),
        cost_estimate=pl.CostEstimate(flops=4000000, bytes_accessed=3000000, transcendentals=0),
        name="flow_step",
    )(
        flag_cell, position,
        velocity.reshape(3, size_x * size_y, size_z),
        viscosity.reshape(size_x * size_y, size_z),
        chunks, first, second, handed,
    )


def pieces(value):
    high = value.astype(jnp.bfloat16)
    rest = value - high.astype(jnp.float32)
    middle = rest.astype(jnp.bfloat16)
    return high, middle, (rest - middle.astype(jnp.float32)).astype(jnp.bfloat16)


def polymer_kernel(
    size_x, size_y, size_z, macro_count, chunk_ref, viscous_ref, corner_ref, lines_ref, pick_ref,
    spread_ref, partial_ref, out_ref, flag_ref,
):
    flags = viscous_ref.shape[0]
    macro, core = place_of()
    chunks = chunk_ref[...]
    split = jnp.concatenate((*pieces(chunks), jnp.zeros(chunks.shape, jnp.bfloat16)), axis=0)
    values = jnp.dot(pick_ref[...], split, preferred_element_type=jnp.float32) * lines_ref[2]
    here, beside_z = lines_ref[0], lines_ref[1]
    lane = lanes_of((flags, 128))
    columns = [
        jnp.broadcast_to(
            jnp.sum(jnp.where((lane & 7) == k, values, 0.0), axis=1, keepdims=True), (flags, size_z)
        )
        for k in range(6)
    ]
    stress = viscous_ref[...]
    for k in range(6):
        stress = jnp.where(lane == k, stress + columns[k], stress)
    unused = jnp.zeros((product_depth - 3 * flags, size_z), jnp.float32)
    split = [
        pieces(
            jnp.concatenate(
                [
                    columns[pair_index(a, 0)] * here, columns[pair_index(a, 1)] * here,
                    columns[pair_index(a, 2)] * beside_z, unused,
                ],
                axis=0,
            )
        )
        for a in range(3)
    ]
    flag_ref[...] = stress.T[0:6, :]

    out_ref[...] = partial_ref[...]
    for s in range(2):
        inside = macro > 0 if s == 0 else macro < macro_count - 1
        beside = jnp.maximum(macro - 1, 0) if s == 0 else jnp.minimum(macro + 1, macro_count - 1)
        start = (2 * beside + core) * back_rows
        x = 0 if s == 0 else size_x - 1
        for u in range(2):
            at = x * size_y + (0 if u == 0 else size_y - 1)
            for a in range(2):
                number = 4 * s + 2 * u + a
                line = corner_ref[number : number + 1, :] * chunk_ref[pl.ds(start + 2 * u + a, 1), :]
                out_ref[1 - a, at : at + 1, :] += jnp.where(inside, line, 0.0)
    for a in range(3):
        out_ref[a] += jnp.dot(
            spread_ref[...], jnp.concatenate(split[a], axis=0), preferred_element_type=jnp.float32
        )


def add_polymer(chunks, viscous, corners, lines, pick, spread, partial, shape):
    flags = viscous.shape[0]
    size_x, size_y, size_z = shape
    return pl.pallas_call(
        functools.partial(polymer_kernel, size_x, size_y, size_z, chunks.shape[0] // 2),
        out_shape=(
            jax.ShapeDtypeStruct(partial.shape, jnp.float32),
            jax.ShapeDtypeStruct((6, flags), jnp.float32),
        ),
        in_specs=[VMEM] * 7,
        out_specs=(VMEM, VMEM),
        compiler_params=limit(8),
        cost_estimate=pl.CostEstimate(flops=400000, bytes_accessed=3000000, transcendentals=0),
        name="add_polymer",
    )(chunks.reshape(-1, 128), viscous, corners, lines, pick, spread, partial)


def shards(velocity, viscosity, flag_cell, flag_owner, conformations, increments):
    macro_count = lax.axis_size("macro")
    tile_count = lax.axis_size("tile")
    assert lax.axis_size("micro") == 2
    owner_count = 2 * macro_count
    capacity = conformations.shape[1] // owner_count
    size_x, size_y, size_z = viscosity.shape
    assert capacity <= slot_rows and capacity % 2 == 0 and size_y == 8 and size_z == 128 and size_x % 8 == 0 and size_x <= 48
    chunks, position, viscous, first, second, first_conform, first_noise = gather_rows(
        flag_cell, flag_owner.reshape(-1), velocity, viscosity, conformations, increments, capacity, owner_count
    )

    def exchange(rows):
        return lax.all_to_all(rows, ("macro", "micro"), split_axis=0, concat_axis=0, tiled=True)

    received = exchange(chunks.reshape(owner_count, -1, 128))
    swaps = []
    for start in range(2):
        pairs = [(i, i + 1) for i in range(start, tile_count - 1, 2)]
        swaps.append(pairs + [(high, low) for low, high in pairs])
    first = lax.ppermute(first, "tile", swaps[0])
    second = lax.ppermute(second, "tile", swaps[1])
    last_state, polymer = advance(
        conformations, increments, received, first_conform, first_noise, capacity
    )
    polymer, handed = add_lines(polymer, received, first, second)
    returned = exchange(polymer)
    handed = lax.ppermute(handed, "micro", [(0, 1), (1, 0)])
    partial, corners, lines, pick, spread = flow_step(
        flag_cell, position, velocity, viscosity, received, first, second, handed
    )
    velocity_next, flag_stress = add_polymer(
        returned, viscous, corners, lines, pick, spread, partial, viscosity.shape
    )
    return (velocity_next.reshape(velocity.shape), last_state, flag_stress)


def solution(mesh):
    in_specs = (
        P(None, "macro", "tile", "micro"),
        P("macro", "tile", "micro"),
        P(("macro", "tile", "micro")),
        P(("macro", "tile", "micro"), None),
        P(None, ("macro", "tile", "micro"), None),
        P(None, None, ("macro", "tile", "micro"), None),
    )
    out_specs = (
        P(None, "macro", "tile", "micro"),
        P(None, ("macro", "tile", "micro"), None),
        P(None, ("macro", "tile", "micro")),
    )
    return jax.shard_map(shards, mesh=mesh, in_specs=in_specs, out_specs=out_specs, check_vma=False)
```

```python
import functools

import jax
import jax.numpy as jnp
from jax import lax
from jax.experimental import pallas as pl
from jax.experimental.pallas import tpu as pltpu
from jax.sharding import PartitionSpec as P

stress_pairs = ((0, 0), (1, 1), (2, 2), (0, 1), (0, 2), (1, 2))
macro_step = 0.1
micro_step = 0.01
noise_weight = 0.1
relax_rate = 0.5
fene_extent = 30.0
spring_floor = 0.1
polymer_weight = 0.25

SMEM = pl.BlockSpec(memory_space=pltpu.SMEM)
VMEM = pl.BlockSpec(memory_space=pltpu.VMEM)


def pair_index(left_axis, right_axis):
    return stress_pairs.index((min(left_axis, right_axis), max(left_axis, right_axis)))


def lanes_of(shape):
    return lax.broadcasted_iota(jnp.int32, shape, len(shape) - 1)


slot_rows = 8
chunk_rows = 32
half_face = 28
handed_rows = 48
item_count = 7
back_rows = 8
polymer_row = 4


block_slots = 32
first_share = 2


def limit(mebibytes):
    return pltpu.CompilerParams(vmem_limit_bytes=mebibytes * 1024 * 1024)


def far(value):
    return pltpu.with_memory_space_constraint(value, pltpu.HBM)


def place_of():
    return lax.axis_index("macro"), lax.axis_index("micro")


def neighbour(index, side, count):
    return jnp.maximum(index - 1, 0) if side == 0 else jnp.minimum(index + 1, count - 1)


def rolled(value, amount):
    size = value.shape[-1]
    if isinstance(amount, int):
        return pltpu.roll(value, amount % size, value.ndim - 1)
    return pltpu.roll(value, lax.rem(amount + 2 * size, size), value.ndim - 1)


def gather_kernel(
    capacity, size_x, size_y, size_z, macro_count, cell_in, owner_in, velocity_in, viscosity_in,
    conform_in, noise_in, chunk_ref, position_ref, viscous_ref, first_ref, second_ref, conform_ref, noise_ref,
    cell_ref, owner_ref, velocity_ref, viscosity_ref, masked, gradients, paired, target, count, sems,
):
    flags = cell_ref.shape[0]
    copies = [
        pltpu.make_async_copy(source, into, sems.at[number])
        for number, (source, into) in enumerate(
            (
                (cell_in, cell_ref), (owner_in, owner_ref), (velocity_in, velocity_ref),
                (viscosity_in, viscosity_ref), (conform_in.at[:, 0:block_slots, :], conform_ref),
                (noise_in.at[0 : noise_ref.shape[0], :, 0:block_slots, :], noise_ref),
            )
        )
    ]
    for copy in copies:
        copy.start()
    paired_rows = paired.shape[0] // 2
    macro, core = place_of()
    lane = lanes_of((1, size_z))

    for owner in range(count.shape[0]):
        count[owner] = 0
    paired[...] = jnp.zeros_like(paired)
    for copy in copies[:2]:
        copy.wait()
    for j in range(flags):
        owner = owner_ref[j]
        rank = count[owner]
        count[owner] = rank + 1
        target[j] = (rank & 1) * paired_rows + owner * (slot_rows // 2) + lax.shift_right_logical(rank, 1)
        position_ref[j] = owner * slot_rows + rank
    for copy in copies[2:4]:
        copy.wait()
    planes = velocity_ref.reshape(3, size_x, size_y, size_z)
    layers = viscosity_ref.reshape(size_x, size_y, size_z)
    for j in range(flags):
        cell = cell_ref[j]
        x = lax.shift_right_logical(cell, 10)
        y = lax.shift_right_logical(cell, 7) & (size_y - 1)
        z = cell & (size_z - 1)
        here = (lane == z).astype(jnp.float32)
        along_z = (lane == z + 1).astype(jnp.float32) - (lane == z - 1).astype(jnp.float32)
        at = pl.ds(y, 1)
        for a in range(3):
            along_x = planes[a, x + 1, at, :] - planes[a, x - 1, at, :]
            along_y = planes[a, x, pl.ds(y + 1, 1), :] - planes[a, x, pl.ds(y - 1, 1), :]
            masked[3 * a, j : j + 1, :] = along_x * here
            masked[3 * a + 1, j : j + 1, :] = along_y * here
            masked[3 * a + 2, j : j + 1, :] = planes[a, x, at, :] * along_z
        masked[9, j : j + 1, :] = layers[x, at, :] * here

    even = lax.axis_index("tile") & 1 == 0

    def put(number, ref, low, high):
        rows = [ref[pl.ds(y, size_x, stride=size_y), :] for y in (low, high)]
        first_ref[number] = jnp.where(even, rows[1], rows[0])
        second_ref[number] = jnp.where(even, rows[0], rows[1])

    for layer in range(2):
        for a in range(3):
            put(3 * layer + a, velocity_ref.at[a], layer, size_y - 1 - layer)
    put(6, viscosity_ref, 0, size_y - 1)

    for side in range(2):
        beside = neighbour(macro, side, macro_count)
        for layer, owner in enumerate((2 * beside + core, 2 * beside + 1 - core)):
            start = pl.multiple_of(owner * chunk_rows, 8)
            x = layer if side == 0 else size_x - 1 - layer
            for a in range(3):
                chunk_ref[pl.ds(start + a * size_y, size_y), :] = velocity_ref[a, x * size_y : (x + 1) * size_y, :]
            x = 0 if side == 0 else size_x - 1
            half = x * size_y + layer * (size_y // 2)
            chunk_ref[pl.ds(start + 3 * size_y, size_y // 2), :] = viscosity_ref[half : half + size_y // 2, :]

    group = size_z // 8
    lane2 = lanes_of((size_y, size_z))
    first = pl.multiple_of((2 * macro + 1 - core) * chunk_rows, 8)
    source = jnp.where(core == 0, size_z - 2, 0)
    for block in range(-(-size_x // group)):
        total = jnp.zeros((size_y, size_z), jnp.float32)
        for x in range(block * group, min(size_x, (block + 1) * group)):
            rows = slice(x * size_y, (x + 1) * size_y)
            for a in range(4):
                at = 8 * (x - block * group) + 2 * a
                value = viscosity_ref[rows, :] if a == 3 else velocity_ref[a, rows, :]
                total = jnp.where((lane2 == at) | (lane2 == at + 1), rolled(value, at - source), total)
        chunk_ref[pl.ds(first + block * size_y, size_y), :] = total

    columns = [0.5 * jnp.sum(masked[c], axis=1, keepdims=True) for c in range(9)]
    viscous = jnp.sum(masked[9], axis=1, keepdims=True)
    wide = lanes_of((flags, 128))
    packed = jnp.zeros((flags, 128), jnp.float32)
    for c in range(9):
        packed = jnp.where(wide == c, columns[c], packed)
    gradients[...] = packed
    stress = jnp.zeros((flags, 128), jnp.float32)
    for k, (a, b) in enumerate(stress_pairs):
        stress = jnp.where(wide == k, viscous * (columns[3 * a + b] + columns[3 * b + a]), stress)
    viscous_ref[...] = stress

    for j in range(flags):
        paired[pl.ds(target[j], 1), :] = gradients[j : j + 1, :]
    rows = paired[0:paired_rows, :] + rolled(paired[paired_rows:, :], 64)
    for owner in range(count.shape[0]):
        chunk_ref[owner * chunk_rows + half_face : (owner + 1) * chunk_rows, :] = rows[
            owner * (slot_rows // 2) : (owner + 1) * (slot_rows // 2)
        ]
    for copy in copies[4:]:
        copy.wait()


def gather_rows(flag_cell, owner, velocity, viscosity, conformations, increments, capacity, owner_count):
    size_x, size_y, size_z = viscosity.shape
    flags = flag_cell.shape[0]
    face = jax.ShapeDtypeStruct((item_count, size_x, size_z), jnp.float32)
    steps, _, _, dumbbells = increments.shape
    return pl.pallas_call(
        functools.partial(gather_kernel, capacity, size_x, size_y, size_z, owner_count // 2),
        out_shape=(
            jax.ShapeDtypeStruct((owner_count * chunk_rows, 128), jnp.float32),
            jax.ShapeDtypeStruct((flags,), jnp.int32),
            jax.ShapeDtypeStruct((flags, 128), jnp.float32),
            face,
            face,
            pltpu.VMEM((3, block_slots, dumbbells), jnp.float32),
            pltpu.VMEM((steps // first_share, 3, block_slots, dumbbells), jnp.bfloat16),
        ),
        in_specs=[pl.BlockSpec(memory_space=pltpu.HBM)] * 6,
        out_specs=(VMEM, SMEM, VMEM, VMEM, VMEM, VMEM, VMEM),
        scratch_shapes=[
            pltpu.SMEM((flags,), jnp.int32),
            pltpu.SMEM((flags,), jnp.int32),
            pltpu.VMEM((3, size_x * size_y, size_z), jnp.float32),
            pltpu.VMEM((size_x * size_y, size_z), jnp.float32),
            pltpu.VMEM((10, flags, size_z), jnp.float32),
            pltpu.VMEM((flags, 128), jnp.float32),
            pltpu.VMEM((owner_count * slot_rows, 128), jnp.float32),
            pltpu.SMEM((flags,), jnp.int32),
            pltpu.SMEM((owner_count,), jnp.int32),
            pltpu.SemaphoreType.DMA((6,)),
        ],
        compiler_params=limit(8),
        cost_estimate=pl.CostEstimate(flops=400000, bytes_accessed=3000000, transcendentals=0),
        name="gather_rows",
    )(
        far(flag_cell),
        far(owner),
        far(velocity.reshape(3, size_x * size_y, size_z)),
        far(viscosity.reshape(size_x * size_y, size_z)),
        far(conformations),
        far(increments),
    )


def micro_kernel(
    capacity, parts, rows, groups, conform_ref, noise_ref, rate_ref, first_conform_ref, first_noise_ref,
    next_ref, chunk_ref, conform, noise, rate, rate_wide, sums_ref, read_sem, noise_sem,
):
    steps, _, slots, dumbbells = noise_ref.shape
    blocks = slots // rows
    span = steps // groups
    width = dumbbells // parts
    owners = slots // capacity
    scale = 1.0 / noise_weight
    extent = fene_extent * scale * scale

    def block_rows(block):
        return pl.ds(pl.multiple_of(block * rows, rows), rows)

    def read(block):
        at = block_rows(block)
        return pltpu.make_async_copy(conform_ref.at[:, at, :], conform.at[:, at, :], read_sem.at[block])

    def read_noise(block, group):
        at, when = block_rows(block), pl.ds(group * span, span)
        return pltpu.make_async_copy(
            noise_ref.at[when, :, at, :], noise.at[when, :, at, :], noise_sem.at[block, group]
        )

    pieces = [
        (half, slice(part * width, (part + 1) * width)) for half in range(rows // 16) for part in range(parts)
    ]
    assert len(pieces) == 8
    early = groups // first_share
    for block in range(blocks):
        if block > 0:
            read(block).start()
        for group in range(early if block == 0 else 0, groups):
            read_noise(block, group).start()
    conform[:, 0:rows, :] = first_conform_ref[...]
    for step in range(steps // first_share):
        noise[step, :, 0:rows, :] = first_noise_ref[step]
    for owner in range(owners):
        packed = rate_ref[owner, half_face : half_face + capacity // 2, :]
        rate[pl.ds(owner * capacity, capacity // 2, stride=2), :] = packed
        rate[pl.ds(owner * capacity + 1, capacity // 2, stride=2), :] = rolled(packed, 64)
        chunk_ref[owner] = jnp.zeros(chunk_ref.shape[1:], jnp.float32)
    for a in range(3):
        for b in range(3):
            column = micro_step * rate[:, 3 * a + b : 3 * a + b + 1] + (1.0 if a == b else 0.0)
            rate_wide[3 * a + b] = jnp.broadcast_to(column, (slots, width))

    def inverses(state, scale):
        rooms = []
        for piece in range(len(pieces)):
            q = state[3 * piece : 3 * piece + 3]
            room = (extent - q[0] * q[0]) - (q[1] * q[1] + q[2] * q[2])
            rooms.append(jnp.maximum(room, extent * spring_floor))
        levels = [rooms]
        while len(levels[-1]) > 1:
            levels.append([low * high for low, high in zip(levels[-1][0::2], levels[-1][1::2])])
        result = [scale * pl.reciprocal(levels[-1][0])]
        for level in reversed(levels[:-1]):
            result = [result[i // 2] * level[i ^ 1] for i in range(len(level))]
        return result

    def advance_block(block, carry):
        ats = [pl.ds(pl.multiple_of(block * rows + 16 * half, 16), 16) for half in range(rows // 16)]
        rates = [
            [[rate_wide.at[3 * a + b, at, :] for b in range(3)] for a in range(3)] for at in ats
        ]

        def substep(step, state):
            updated = []
            springs = inverses(state, micro_step * relax_rate * extent)
            for piece, (half, lanes) in enumerate(pieces):
                q = state[3 * piece : 3 * piece + 3]
                table = rates[half]
                for a in range(3):
                    b, c = [other for other in range(3) if other != a]
                    kick = noise[step, a, ats[half], lanes].astype(jnp.float32)
                    rest = (table[a][b][...] * q[b] + table[a][c][...] * q[c]) + kick
                    updated.append((table[a][a][...] - springs[piece]) * q[a] + rest)
            return tuple(updated)

        def advance_group(group, state):
            if group < early:

                @pl.when(block > 0)
                def _():
                    read_noise(block, group).wait()

            else:
                read_noise(block, group).wait()
            for step in range(span):
                state = substep(group * span + step, state)
            return state

        @pl.when(block > 0)
        def _():
            read(block).wait()

        state = tuple(conform[a, ats[half], lanes] * scale for half, lanes in pieces for a in range(3))
        for group in range(groups):
            state = advance_group(group, state)
        inverse = inverses(state, 1.0)
        for half, at in enumerate(ats):
            sums = [None] * 6
            for piece, (other, lanes) in enumerate(pieces):
                if other != half:
                    continue
                q = state[3 * piece : 3 * piece + 3]
                for a in range(3):
                    next_ref[a, at, lanes] = q[a] * noise_weight
                for k, (a, b) in enumerate(stress_pairs):
                    term = (inverse[piece] * q[a]) * q[b]
                    sums[k] = term if sums[k] is None else sums[k] + term
            for k in range(6):
                sums_ref[k, at, :] = sums[k]
        return carry

    lax.fori_loop(0, blocks, advance_block, 0)
    lane = lanes_of((slots, 128))
    rank = lax.broadcasted_iota(jnp.int32, (slots, 128), 0) & (capacity - 1)
    packed = jnp.zeros((slots, 128), jnp.float32)
    weight = extent * noise_weight * noise_weight / dumbbells
    for k, (a, b) in enumerate(stress_pairs):
        mean = jnp.sum(sums_ref[k], axis=1, keepdims=True) * weight
        packed = jnp.where(lane == 8 * rank + k, polymer_weight * (mean - (1.0 if a == b else 0.0)), packed)
    for owner in range(owners):
        chunk_ref[owner, polymer_row : polymer_row + 1, :] = jnp.sum(
            packed[owner * capacity : (owner + 1) * capacity], axis=0, keepdims=True
        )


def advance(conformations, increments, chunks, first_conform, first_noise, capacity):
    slots, dumbbells = conformations.shape[1:]
    steps = increments.shape[0]
    owners = slots // capacity
    rows, parts, groups = block_slots, 4, 4
    blocks = slots // rows
    whole = pl.BlockSpec(memory_space=pltpu.HBM)
    return pl.pallas_call(
        functools.partial(micro_kernel, capacity, parts, rows, groups),
        out_shape=(
            pltpu.VMEM(conformations.shape, jnp.float32),
            jax.ShapeDtypeStruct((owners, back_rows, 128), jnp.float32),
        ),
        in_specs=[whole, whole, VMEM, VMEM, VMEM],
        out_specs=(VMEM, VMEM),
        scratch_shapes=[
            pltpu.VMEM(conformations.shape, jnp.float32),
            pltpu.VMEM(increments.shape, jnp.bfloat16),
            pltpu.VMEM((slots, 128), jnp.float32),
            pltpu.VMEM((9, slots, dumbbells // parts), jnp.float32),
            pltpu.VMEM((6, slots, dumbbells // parts), jnp.float32),
            pltpu.SemaphoreType.DMA((blocks,)),
            pltpu.SemaphoreType.DMA((blocks, groups)),
        ],
        compiler_params=limit(12),
        cost_estimate=pl.CostEstimate(flops=20000000, bytes_accessed=5000000, transcendentals=600000),
        name="advance",
    )(far(conformations), far(increments), chunks, first_conform, first_noise)


def lines_kernel(macro_count, chunk_ref, received_ref, first_ref, second_ref, out_ref, handed_ref):
    out_ref[...] = chunk_ref[...]
    macro, core = place_of()
    even = lax.axis_index("tile") & 1 == 0
    size_x = first_ref.shape[1]

    def side_of(u, item, at):
        first, second = first_ref[item, at, :], second_ref[item, at, :]
        return jnp.where(even, second, first) if u == 0 else jnp.where(even, first, second)

    for side in range(2):
        beside = neighbour(macro, side, macro_count)
        handed_ref[side, 0:chunk_rows, :] = received_ref[2 * beside + 1 - core]
        for number, a in enumerate((0, 2)):
            handed_ref[side, chunk_rows + number * 8 : chunk_rows + (number + 1) * 8, :] = received_ref[
                2 * beside + core, a * 8 : (a + 1) * 8, :
            ]
        x = 0 if side == 0 else size_x - 1
        for u in range(2):
            for a in range(2):
                at = 2 * u + a
                out_ref[2 * beside + core, at : at + 1, :] = side_of(u, a, slice(x, x + 1))
    for u in range(2):
        for number in range(2):
            start = handed_rows + number * size_x
            handed_ref[u, start : start + size_x, :] = side_of(u, 1 + number, slice(0, size_x))


def add_lines(chunks, received, first, second):
    return pl.pallas_call(
        functools.partial(lines_kernel, chunks.shape[0] // 2),
        out_shape=(
            jax.ShapeDtypeStruct(chunks.shape, jnp.float32),
            jax.ShapeDtypeStruct((2, handed_rows + 2 * first.shape[1], 128), jnp.float32),
        ),
        in_specs=[VMEM] * 4,
        out_specs=(VMEM,) * 2,
        compiler_params=limit(4),
        cost_estimate=pl.CostEstimate(flops=20000, bytes_accessed=400000, transcendentals=0),
        name="add_lines",
    )(chunks, received, first, second)


product_depth = 128


def one_hots(size_y, size_z, cell_ref, position_ref, lines_ref, pick_ref, spread_ref, rows):
    flags = cell_ref.shape[0]
    weight = 0.5 * macro_step
    row_count = spread_ref.shape[0]
    returned = pick_ref.shape[1] // 4
    lane = lanes_of((1, size_z))
    row_lane = lanes_of((1, rows.shape[1]))
    slot_lane = lanes_of((flags, returned))
    flag_row = lax.broadcasted_iota(jnp.int32, (flags, returned), 0)
    rows[3 * flags :, :] = jnp.zeros((product_depth - 3 * flags, rows.shape[1]), jnp.float32)
    slot = jnp.zeros((flags, returned), jnp.int32)
    group = lax.shift_right_logical(lane, 3)
    for j in range(flags):
        cell = cell_ref[j]
        row = lax.div(cell, size_z)
        z = cell - row * size_z
        lines_ref[0, j : j + 1, :] = jnp.where(lane == z, weight, 0.0)
        lines_ref[1, j : j + 1, :] = jnp.where(
            lane == z - 1, weight, jnp.where(lane == z + 1, -weight, 0.0)
        )
        for number, shift in enumerate((size_y, 1)):
            rows[number * flags + j : number * flags + j + 1, :] = jnp.where(
                row_lane == row - shift, 1.0, jnp.where(row_lane == row + shift, -1.0, 0.0)
            )
        rows[2 * flags + j : 2 * flags + j + 1, :] = jnp.where(row_lane == row, 1.0, 0.0)
        owner = lax.div(position_ref[j], slot_rows)
        rank = position_ref[j] - owner * slot_rows
        lines_ref[2, j : j + 1, :] = jnp.where(group == rank, 1.0, 0.0)
        slot = jnp.where(flag_row == j, owner * back_rows + polymer_row, slot)
    spread = rows[...].T[:row_count].astype(jnp.bfloat16)
    pick = jnp.where(slot_lane == slot, 1.0, 0.0).astype(jnp.bfloat16)
    for piece in range(3):
        spread_ref[:, piece * product_depth : (piece + 1) * product_depth] = spread
        pick_ref[:, piece * returned : (piece + 1) * returned] = pick
    pick_ref[:, 3 * returned :] = jnp.zeros((flags, returned), jnp.bfloat16)


def flow_kernel(
    size_x, size_y, size_z, macro_count, cell_ref, position_ref, velocity_ref, viscosity_ref, chunk_ref,
    first_ref, second_ref, handed_ref, out_ref, corner_ref, lines_ref, pick_ref, spread_ref,
    padded, stress_x, stress_rest, faces, ghost_y, ghost_z, rows, halves, beyond,
    y_low_ref, y_high_ref,
):
    macro, core = place_of()
    even = lax.axis_index("tile") & 1 == 0
    y_low_ref[...] = jnp.where(even, second_ref[...], first_ref[...])
    y_high_ref[...] = jnp.where(even, first_ref[...], second_ref[...])
    one_hots(size_y, size_z, cell_ref, position_ref, lines_ref, pick_ref, spread_ref, rows)
    inside = (macro > 0, macro < macro_count - 1)
    sign_z = jnp.where(core == 0, 1.0, -1.0)
    end = jnp.where(core == 0, size_z - 1, 0)
    shape = (size_y, size_z)
    lane, row = lanes_of(shape), lax.broadcasted_iota(jnp.int32, shape, 0)
    at_end = jnp.where(lane == end, sign_z, 0.0)

    def kept(value, condition):
        return jnp.where(condition, value, 0.0)

    def plane(x):
        return pl.ds(pl.multiple_of(x * size_y, 8), size_y)

    def difference_z(value):
        lane = lanes_of(value.shape)
        return jnp.where(lane == size_z - 1, 0.0, rolled(value, -1)) - jnp.where(
            lane == 0, 0.0, rolled(value, 1)
        )

    def difference_rows(value, low=0.0, high=0.0):
        count = value.shape[0]
        row = lax.broadcasted_iota(jnp.int32, value.shape, 0)
        return jnp.where(row == count - 1, high, pltpu.roll(value, count - 1, 0)) - jnp.where(
            row == 0, low, pltpu.roll(value, 1, 0)
        )

    x_faces, x_others = [], []
    half = size_y // 2
    for s in range(2):
        beside = neighbour(macro, s, macro_count)
        outer = chunk_ref[2 * beside + core]
        items = [outer[i * size_y : (i + 1) * size_y] for i in range(3)]
        items += [handed_ref[s, i * size_y : (i + 1) * size_y, :] for i in range(3)]
        halves[s, 0:half, :] = chunk_ref[2 * beside + core, 3 * size_y : 3 * size_y + half, :]
        halves[s, half:, :] = handed_ref[s, 3 * size_y : 3 * size_y + half, :]
        items.append(halves[s])
        x_faces.append([kept(item, inside[s]) for item in items])
        corners = [handed_ref[s, chunk_rows + i * size_y : chunk_rows + (i + 1) * size_y, :] for i in range(2)]
        x_others.append([kept(rolled(corner, 2 * end + 1), inside[s]) for corner in corners])

    y_others = []
    for u in range(2):
        start = handed_rows + size_x
        y_others.append(rolled(handed_ref[u, handed_rows:start, :], 2 * end + 1))
        beyond[u] = rolled(handed_ref[u, start : start + size_x, :], 2 * end + 1)

    group = size_z // 8
    packed = [
        chunk_ref[2 * macro + 1 - core, i * size_y : (i + 1) * size_y, :]
        for i in range(-(-size_x // group))
    ]
    for i, value in enumerate(packed):

        def unpack(x, carry):
            for q in range(item_count):
                a, layer = (q, 0) if q < 4 else (q - 4, 1)
                at = 8 * (x - i * group) + 2 * a + (core if layer == 0 else 1 - core)
                faces[q, x + 1] = rolled(value, end - at)
            return carry

        lax.fori_loop(i * group, min(size_x, (i + 1) * group), unpack, 0, unroll=8)
    faces[2, 0] = x_others[0][1]
    faces[2, size_x + 1] = x_others[1][1]

    for a in range(3):
        padded[a, 0] = x_faces[0][a]
        padded[a, size_x + 1] = x_faces[1][a]

    def fill(x, carry):
        for a in range(3):
            padded[a, x + 1] = velocity_ref[a, plane(x), :]
        return carry

    lax.fori_loop(0, size_x, fill, 0, unroll=True)

    rest = {(1, 1): 0, (2, 2): 1, (1, 2): 2}

    def stress_plane(x, carry):
        along_x, along_y, along_z, centre = [], [], [], []
        for a in range(3):
            value = padded[a, x + 1]
            centre.append(value)
            along_x.append(padded[a, x + 2] - padded[a, x])
            along_y.append(
                difference_rows(value, y_low_ref[a, pl.ds(x, 1), :], y_high_ref[a, pl.ds(x, 1), :])
            )
            along_z.append(difference_z(value) + faces[a, x + 1] * at_end)
        slopes = (along_x, along_y, along_z)
        half = 0.5 * viscosity_ref[plane(x), :]
        for a, b in stress_pairs:
            value = half * (slopes[b][a] + slopes[a][b])
            if a == 0:
                stress_x[b, x + 1] = value
            else:
                stress_rest[rest[a, b], x] = value
        weight = (0.5 * faces[3, x + 1]) * at_end
        normal = [(faces[4 + a, x + 1] - centre[a]) * sign_z for a in range(3)]
        ghost_z[0, x] = weight * (normal[0] + (faces[2, x + 2] - faces[2, x]))
        slope = difference_rows(faces[2, x + 1], beyond[0, pl.ds(x, 1), :], beyond[1, pl.ds(x, 1), :])
        ghost_z[1, x] = weight * (normal[1] + slope)
        ghost_z[2, x] = weight * (2.0 * normal[2])
        return carry

    lax.fori_loop(0, size_x, stress_plane, 0, unroll=6)

    for s in range(2):
        near, far, weight = x_faces[s][0:3], x_faces[s][3:6], 0.5 * x_faces[s][6]
        sign = -1.0 if s == 0 else 1.0
        normal = [(far[a] - padded[a, 1 if s == 0 else size_x]) * sign for a in range(3)]
        slope_y = difference_rows(near[0])
        slope_z = difference_z(near[0]) + x_others[s][0] * at_end
        at = 0 if s == 0 else size_x + 1
        stress_x[0, at] = weight * (2.0 * normal[0])
        stress_x[1, at] = weight * (normal[1] + slope_y)
        stress_x[2, at] = weight * (normal[2] + slope_z)
        for u in range(2):
            y, sign_y = (0, -1.0) if u == 0 else (size_y - 1, 1.0)
            number = 4 * s + 2 * u
            corner_ref[number : number + 1, :] = (0.5 * macro_step * sign * sign_y) * weight[y : y + 1, :]

    for u, ref in enumerate((y_low_ref, y_high_ref)):
        y, sign = (0, -1.0) if u == 0 else (size_y - 1, 1.0)
        weight = 0.5 * ref[6]
        normal = [
            (ref[3 + a] - velocity_ref[a, pl.ds(y, size_x, stride=size_y), :]) * sign for a in range(3)
        ]
        ghost_y[3 * u] = weight * (normal[0] + difference_rows(ref[1]))
        ghost_y[3 * u + 1] = weight * (2.0 * normal[1])
        wide = lanes_of((size_x, size_z))
        across = jnp.where(wide == end, y_others[u] * sign_z, 0.0)
        ghost_y[3 * u + 2] = weight * (normal[2] + (difference_z(ref[1]) + across))
        for s in range(2):
            x, sign_x = (0, -1.0) if s == 0 else (size_x - 1, 1.0)
            number = 4 * s + 2 * u + 1
            corner_ref[number : number + 1, :] = (0.5 * macro_step * sign * sign_x) * weight[x : x + 1, :]

    columns = {(0, 1): (stress_x, 1, 1), (1, 1): (stress_rest, 0, 0), (2, 1): (stress_rest, 2, 0)}
    columns_z = {0: (stress_x, 2, 1), 1: (stress_rest, 2, 0), 2: (stress_rest, 1, 0)}

    def step_plane(x, carry):
        for a in range(3):
            total = stress_x[a, x + 2] - stress_x[a, x]
            ref, number, shift = columns[a, 1]
            total = total + difference_rows(
                ref[number, x + shift], ghost_y[a, pl.ds(x, 1), :], ghost_y[3 + a, pl.ds(x, 1), :]
            )
            ref, number, shift = columns_z[a]
            total = total + (difference_z(ref[number, x + shift]) + ghost_z[a, x])
            out_ref[a, plane(x), :] = padded[a, x + 1] + (0.5 * macro_step) * total
        return carry

    lax.fori_loop(0, size_x, step_plane, 0, unroll=6)


def flow_step(flag_cell, position, velocity, viscosity, chunks, first, second, handed):
    size_x, size_y, size_z = viscosity.shape
    flags = flag_cell.shape[0]
    returned = chunks.shape[0] * back_rows
    row_count = size_x * size_y
    planes = (size_x, size_y, size_z)
    wide = (size_x + 2, size_y, size_z)
    return pl.pallas_call(
        functools.partial(flow_kernel, size_x, size_y, size_z, chunks.shape[0] // 2),
        out_shape=(
            jax.ShapeDtypeStruct((3, size_x * size_y, size_z), jnp.float32),
            jax.ShapeDtypeStruct((8, size_z), jnp.float32),
            jax.ShapeDtypeStruct((3, flags, size_z), jnp.float32),
            jax.ShapeDtypeStruct((flags, 4 * returned), jnp.bfloat16),
            jax.ShapeDtypeStruct((row_count, 3 * product_depth), jnp.bfloat16),
        ),
        in_specs=[SMEM] * 2 + [VMEM] * 6,
        out_specs=(VMEM,) * 5,
        scratch_shapes=[
            pltpu.VMEM((3, *wide), jnp.float32),
            pltpu.VMEM((3, *wide), jnp.float32),
            pltpu.VMEM((3, *planes), jnp.float32),
            pltpu.VMEM((item_count, *wide), jnp.float32),
            pltpu.VMEM((6, size_x, size_z), jnp.float32),
            pltpu.VMEM((3, *planes), jnp.float32),
            pltpu.VMEM((product_depth, -(-row_count // 128) * 128), jnp.float32),
            pltpu.VMEM((2, size_y, size_z), jnp.float32),
            pltpu.VMEM((2, size_x, size_z), jnp.float32),
            pltpu.VMEM(first.shape, jnp.float32),
            pltpu.VMEM(first.shape, jnp.float32),
        ],
        compiler_params=limit(12),
        cost_estimate=pl.CostEstimate(flops=4000000, bytes_accessed=3000000, transcendentals=0),
        name="flow_step",
    )(
        flag_cell, position,
        velocity.reshape(3, size_x * size_y, size_z),
        viscosity.reshape(size_x * size_y, size_z),
        chunks, first, second, handed,
    )


def pieces(value):
    high = value.astype(jnp.bfloat16)
    rest = value - high.astype(jnp.float32)
    middle = rest.astype(jnp.bfloat16)
    return high, middle, (rest - middle.astype(jnp.float32)).astype(jnp.bfloat16)


def polymer_kernel(
    size_x, size_y, size_z, macro_count, chunk_ref, viscous_ref, corner_ref, lines_ref, pick_ref,
    spread_ref, partial_ref, out_ref, flag_ref,
):
    flags = viscous_ref.shape[0]
    macro, core = place_of()
    chunks = chunk_ref[...]
    split = jnp.concatenate((*pieces(chunks), jnp.zeros(chunks.shape, jnp.bfloat16)), axis=0)
    values = jnp.dot(pick_ref[...], split, preferred_element_type=jnp.float32) * lines_ref[2]
    here, beside_z = lines_ref[0], lines_ref[1]
    lane = lanes_of((flags, 128))
    columns = [
        jnp.broadcast_to(
            jnp.sum(jnp.where((lane & 7) == k, values, 0.0), axis=1, keepdims=True), (flags, size_z)
        )
        for k in range(6)
    ]
    stress = viscous_ref[...]
    for k in range(6):
        stress = jnp.where(lane == k, stress + columns[k], stress)
    unused = jnp.zeros((product_depth - 3 * flags, size_z), jnp.float32)
    split = [
        pieces(
            jnp.concatenate(
                [
                    columns[pair_index(a, 0)] * here, columns[pair_index(a, 1)] * here,
                    columns[pair_index(a, 2)] * beside_z, unused,
                ],
                axis=0,
            )
        )
        for a in range(3)
    ]
    flag_ref[...] = stress.T[0:6, :]

    for a in range(3):
        out_ref[a] = partial_ref[a] + jnp.dot(
            spread_ref[...], jnp.concatenate(split[a], axis=0), preferred_element_type=jnp.float32
        )

    for s in range(2):
        inside = macro > 0 if s == 0 else macro < macro_count - 1
        beside = jnp.maximum(macro - 1, 0) if s == 0 else jnp.minimum(macro + 1, macro_count - 1)
        start = (2 * beside + core) * back_rows
        x = 0 if s == 0 else size_x - 1
        for u in range(2):
            at = x * size_y + (0 if u == 0 else size_y - 1)
            for a in range(2):
                number = 4 * s + 2 * u + a
                line = corner_ref[number : number + 1, :] * chunk_ref[pl.ds(start + 2 * u + a, 1), :]
                out_ref[1 - a, at : at + 1, :] += jnp.where(inside, line, 0.0)


def add_polymer(chunks, viscous, corners, lines, pick, spread, partial, shape):
    flags = viscous.shape[0]
    size_x, size_y, size_z = shape
    return pl.pallas_call(
        functools.partial(polymer_kernel, size_x, size_y, size_z, chunks.shape[0] // 2),
        out_shape=(
            jax.ShapeDtypeStruct(partial.shape, jnp.float32),
            jax.ShapeDtypeStruct((6, flags), jnp.float32),
        ),
        in_specs=[VMEM] * 7,
        out_specs=(VMEM, VMEM),
        compiler_params=limit(8),
        cost_estimate=pl.CostEstimate(flops=400000, bytes_accessed=3000000, transcendentals=0),
        name="add_polymer",
    )(chunks.reshape(-1, 128), viscous, corners, lines, pick, spread, partial)


def shards(velocity, viscosity, flag_cell, flag_owner, conformations, increments):
    macro_count = lax.axis_size("macro")
    tile_count = lax.axis_size("tile")
    assert lax.axis_size("micro") == 2
    owner_count = 2 * macro_count
    capacity = conformations.shape[1] // owner_count
    size_x, size_y, size_z = viscosity.shape
    assert capacity <= slot_rows and capacity % 2 == 0 and size_y == 8 and size_z == 128 and size_x % 8 == 0 and size_x <= 48
    chunks, position, viscous, first, second, first_conform, first_noise = gather_rows(
        flag_cell, flag_owner.reshape(-1), velocity, viscosity, conformations, increments, capacity, owner_count
    )

    def exchange(rows):
        return lax.all_to_all(rows, ("macro", "micro"), split_axis=0, concat_axis=0, tiled=True)

    received = exchange(chunks.reshape(owner_count, -1, 128))
    swaps = []
    for start in range(2):
        pairs = [(i, i + 1) for i in range(start, tile_count - 1, 2)]
        swaps.append(pairs + [(high, low) for low, high in pairs])
    first = lax.ppermute(first, "tile", swaps[0])
    second = lax.ppermute(second, "tile", swaps[1])
    last_state, polymer = advance(
        conformations, increments, received, first_conform, first_noise, capacity
    )
    polymer, handed = add_lines(polymer, received, first, second)
    returned = exchange(polymer)
    handed = lax.ppermute(handed, "micro", [(0, 1), (1, 0)])
    partial, corners, lines, pick, spread = flow_step(
        flag_cell, position, velocity, viscosity, received, first, second, handed
    )
    velocity_next, flag_stress = add_polymer(
        returned, viscous, corners, lines, pick, spread, partial, viscosity.shape
    )
    return (velocity_next.reshape(velocity.shape), last_state, flag_stress)


def solution(mesh):
    in_specs = (
        P(None, "macro", "tile", "micro"),
        P("macro", "tile", "micro"),
        P(("macro", "tile", "micro")),
        P(("macro", "tile", "micro"), None),
        P(None, ("macro", "tile", "micro"), None),
        P(None, None, ("macro", "tile", "micro"), None),
    )
    out_specs = (
        P(None, "macro", "tile", "micro"),
        P(None, ("macro", "tile", "micro"), None),
        P(None, ("macro", "tile", "micro")),
    )
    return jax.shard_map(shards, mesh=mesh, in_specs=in_specs, out_specs=out_specs, check_vma=False)
```
